32 devices in a mesh: img: 8 (over y, x, core), ch: 4 (over z).
Axes of the slice: x: 2, y: 2, z: 4, core: 2. Of those that a mesh axis runs over, the one named last changes fastest.
Arguments:
- features: bfloat16 [64, 256, 256], P('img', 'ch'), may hold values from -8 to 8
- labels: int32 [64], P('img'), may hold values from 0 to 9
- groups: int32 [64], P('img'), may hold values from 0 to 3, as said below
- widths: int32 [4], replicated, may hold values from 1 to 4, as said below
- entry_conv: float32 [2304, 256], P('img', 'ch'), may hold values from -0.2625 to 0.2625
- entry_moment: float32 [2304, 256], P('img', 'ch'), may hold values from -48 to 48
- entry_square: float32 [2304, 256], P('img', 'ch'), may hold values from 5.89824 to 23.59296
- exit_conv: float32 [2304, 256], P('img', 'ch'), may hold values from -0.2625 to 0.2625
- exit_moment: float32 [2304, 256], P('img', 'ch'), may hold values from -64 to 64
- exit_square: float32 [2304, 256], P('img', 'ch'), may hold values from 10.48576 to 41.94304
- bypass_conv: float32 [256, 256], P('img', 'ch'), may hold values from -0.78125 to 0.78125
- bypass_moment: float32 [256, 256], P('img', 'ch'), may hold values from -192 to 192
- bypass_square: float32 [256, 256], P('img', 'ch'), may hold values from 95.0272 to 376.832
- norm_affine: float32 [23, 256], P(None, 'ch'), may hold values from -1.25 to 1.75
- norm_moment: float32 [23, 256], P(None, 'ch'), may hold values from -128 to 128
- norm_square: float32 [23, 256], P(None, 'ch'), may hold values from 0.32768 to 262.144
- cotangent: bfloat16 [64, 256, 1024], P('img', 'ch'), may hold values from -6 to 6
Outputs:
- block_output: bfloat16 [64, 256, 1024], P('img', 'ch')
- input_gradient: float32 [64, 256, 256], P('img', 'ch')
- entry_first: float32 [2304, 256], P('img', 'ch')
- entry_second: float32 [2304, 256], P('img', 'ch')
- entry_weight: float32 [2304, 256], P('img', 'ch')
- exit_first: float32 [2304, 256], P('img', 'ch')
- exit_second: float32 [2304, 256], P('img', 'ch')
- exit_weight: float32 [2304, 256], P('img', 'ch')
- bypass_first: float32 [256, 256], P('img', 'ch')
- bypass_second: float32 [256, 256], P('img', 'ch')
- bypass_weight: float32 [256, 256], P('img', 'ch')
- affine_first: float32 [23, 256], P(None, 'ch')
- affine_second: float32 [23, 256], P(None, 'ch')
- affine_values: float32 [23, 256], P(None, 'ch')
- trust_norms: float32 [3, 3], replicated
The draws below stay inside these ranges and needn't reach their ends.
Inputs may be any that keep to these rules, and one draw needn't show every extreme that they name: `groups`: each of the 4 micro-batches holds exactly 16 images. `widths`: every value from 1 to 4 occurs.
All inputs are finite; a program needn't handle non-finite values.
Results may differ from the reference program's by a relative error of at most 0.0075.
Values may be sent and summed in bfloat16 or wider, within the bound.
A program may use at most 128 MiB of HBM per device.

```python
import math
import jax
import jax.numpy as jnp
from jax import lax

C = 256
KCLASS = 10
LEVELS = 4
SIDE = 16
GROUPS = 4
STEP = 5
IMAGES = 64


def rising(count, top):
    return top ** (jnp.arange(count, dtype=jnp.float32) / max(count - 1, 1))


def conv_shape(noise, top, fan):
    rows = jnp.sqrt(rising(noise.shape[0], top))[:, None]
    cols = jnp.sqrt(rising(noise.shape[1], top))[None, :]
    return noise * rows * cols / jnp.sqrt(fan)


def affine_scale():
    small = 0.5 * (IMAGES * SIDE * SIDE / KCLASS) ** 0.5
    large = 0.5 * (4.0 * IMAGES * SIDE * SIDE) ** 0.5
    return jnp.concatenate([jnp.full((2 * KCLASS,), small, jnp.float32), jnp.full((2,), large, jnp.float32), jnp.full((1,), 2.0 * large, jnp.float32)])


def draw_features(key, part):
    key = jax.random.fold_in(key, 1)
    shape = (IMAGES, C, SIDE * SIDE)
    noise = jax.random.truncated_normal(key, -4.0, 4.0, shape, jnp.float32)
    scale = 0.6 * rising(IMAGES, 3.0)
    return (noise * scale[:, None, None]).astype(jnp.bfloat16)


def draw_groups(key, part):
    key = jax.random.fold_in(key, 2)
    return (jax.random.permutation(key, IMAGES) % GROUPS).astype(jnp.int32)


def draw_widths(key, part):
    key = jax.random.fold_in(key, 3)
    return (jax.random.permutation(key, GROUPS) % LEVELS + 1).astype(jnp.int32)


def draw_entry_conv(key, part):
    key = jax.random.fold_in(key, 4)
    shape = (9 * C, C)
    noise = jax.random.truncated_normal(key, -4.0, 4.0, shape, jnp.float32)
    top = 3.0
    return conv_shape(noise, top, 9.0 * C)


def draw_exit_conv(key, part):
    key = jax.random.fold_in(key, 5)
    shape = (9 * C, C)
    noise = jax.random.truncated_normal(key, -4.0, 4.0, shape, jnp.float32)
    top = 3.0
    return conv_shape(noise, top, 9.0 * C)


def draw_bypass_conv(key, part):
    key = jax.random.fold_in(key, 6)
    shape = (C, C)
    noise = jax.random.truncated_normal(key, -4.0, 4.0, shape, jnp.float32)
    top = 3.0
    return conv_shape(noise, top, 1.0 * C)


def draw_norm_affine(key, part):
    key = jax.random.fold_in(key, 7)
    shape = (2 * KCLASS + 3, C)
    noise = jax.random.truncated_normal(key, -2.5, 2.5, shape, jnp.float32)
    base = jnp.concatenate([jnp.ones((KCLASS,), jnp.float32), jnp.zeros((KCLASS,), jnp.float32), jnp.array([1.0, 0.0, 0.0], jnp.float32)])
    spread = jnp.concatenate([jnp.full((KCLASS,), 0.3, jnp.float32), jnp.full((KCLASS,), 0.5, jnp.float32), jnp.array([0.3, 0.5, 0.5], jnp.float32)])
    return base[:, None] + spread[:, None] * noise


def draw_norm_moment(key, part):
    key = jax.random.fold_in(key, 8)
    shape = (2 * KCLASS + 3, C)
    noise = jax.random.truncated_normal(key, -4.0, 4.0, shape, jnp.float32)
    return 0.11 * affine_scale()[:, None] * noise


def draw_norm_square(key, part):
    key = jax.random.fold_in(key, 9)
    shape = (2 * KCLASS + 3, C)
    factor = jnp.exp(jax.random.uniform(key, shape, jnp.float32, 0.0, 1.3863))
    scale = affine_scale()
    return 0.001 * (scale * scale)[:, None] * factor


def set_ends(values, own_key, least, high):
    spot = [jax.random.randint(jax.random.fold_in(own_key, axis), (), 0, length) for axis, length in enumerate(values.shape)]
    main_axis = values.shape.index(max(values.shape))
    beside = spot[:main_axis] + [(spot[main_axis] + 1) % values.shape[main_axis]] + spot[main_axis + 1:]
    return values.at[tuple(spot)].set(least).at[tuple(beside)].set(high)


def level_of(stream_key, shape, shards, least, largest):
    def one(position, parts):
        steps = jax.random.uniform(jax.random.fold_in(jax.random.fold_in(stream_key, 6), position), (parts,), jnp.float32, least / len(shards), largest / len(shards))
        return jnp.repeat(jnp.exp(steps), shape[position] // parts).reshape((-1,) + (1,) * (len(shape) - position - 1))

    factor_of = one(*shards[0])
    for cut in shards[1:]:
        factor_of = factor_of * one(*cut)
    return factor_of


def gaussian(key, dims, width, reach, shards=(), kind=jnp.bfloat16):
    factor_of = level_of(key, dims, shards, -0.22, 0.18) if shards else 1.0
    values = jax.random.normal(key, dims, jnp.float32) * width * factor_of
    return jnp.minimum(jnp.maximum(values, -reach), reach).astype(kind)


def setup_inputs(seed: int = 0) -> dict:
    key_list = jax.random.split(jax.random.key(seed), 18)
    return {
        "features": draw_features(jax.random.fold_in(key_list[17], 71), 0),
        "labels": set_ends(jax.random.randint(key_list[1], (IMAGES,), 0, KCLASS), jax.random.fold_in(key_list[1], 1), 0, KCLASS - 1).astype(jnp.int32),
        "groups": draw_groups(jax.random.fold_in(key_list[17], 71), 0),
        "widths": draw_widths(jax.random.fold_in(key_list[17], 71), 0),
        "entry_conv": draw_entry_conv(jax.random.fold_in(key_list[17], 71), 0),
        "entry_moment": gaussian(key_list[5], (9 * C, C), (0.033 * (4 * IMAGES * SIDE * SIDE) ** 0.5), 48.0, ((0, 8), (1, 4)), jnp.float32),
        "entry_square": jnp.clip(jnp.exp(math.log(23.59296) - 1.3862944 * jax.random.uniform(key_list[6], (9 * C, C), jnp.float32) ** level_of(key_list[6], (9 * C, C), ((0, 8), (1, 4)), -0.2, 0.2)), 5.89824, 23.59296),
        "exit_conv": draw_exit_conv(jax.random.fold_in(key_list[17], 71), 0),
        "exit_moment": gaussian(key_list[8], (9 * C, C), (0.044 * (4 * IMAGES * SIDE * SIDE) ** 0.5), 64.0, ((0, 8), (1, 4)), jnp.float32),
        "exit_square": jnp.clip(jnp.exp(math.log(41.94304) - 1.3862944 * jax.random.uniform(key_list[9], (9 * C, C), jnp.float32) ** level_of(key_list[9], (9 * C, C), ((0, 8), (1, 4)), -0.2, 0.2)), 10.48576, 41.94304),
        "bypass_conv": draw_bypass_conv(jax.random.fold_in(key_list[17], 71), 0),
        "bypass_moment": gaussian(key_list[11], (C, C), (0.13 * (4 * IMAGES * SIDE * SIDE) ** 0.5), 192.0, ((0, 8), (1, 4)), jnp.float32),
        "bypass_square": jnp.clip(jnp.exp(math.log(376.832) - 1.3776363 * jax.random.uniform(key_list[12], (C, C), jnp.float32) ** level_of(key_list[12], (C, C), ((0, 8), (1, 4)), -0.2, 0.2)), 95.0272, 376.832),
        "norm_affine": draw_norm_affine(jax.random.fold_in(key_list[17], 71), 0),
        "norm_moment": draw_norm_moment(jax.random.fold_in(key_list[17], 71), 0),
        "norm_square": draw_norm_square(jax.random.fold_in(key_list[17], 71), 0),
        "cotangent": gaussian(key_list[16], (IMAGES, C, 4 * SIDE * SIDE), 1.0, 6.0, ((0, 8), (1, 4))),
    }


HIGHEST = lax.Precision.HIGHEST
NORM_EPSILON = 1e-05
ADAM_EPSILON = 1e-06
MOMENT_DECAY = 0.9
SQUARE_DECAY = 0.999
WEIGHT_DECAY = 0.01
MATRIX_RATE = 0.3
AFFINE_RATE = 0.2

@jax.custom_vjp
def low(v):
    return lax.optimization_barrier(v.astype(jnp.bfloat16)).astype(jnp.float32)

@jax.custom_vjp
def low_back(v):
    return v

def low_keep(v):
    return (low(v), None)

def low_pass(kept, grad):
    return (grad,)

def back_keep(v):
    return (v, None)

def back_low(kept, grad):
    return (low(grad),)
low.defvjp(low_keep, low_pass)
low_back.defvjp(back_keep, back_low)

def to_grid(flat, side):
    return flat.reshape(flat.shape[0], flat.shape[1], side, side).transpose(0, 2, 3, 1)

def to_flat(grid):
    return grid.transpose(0, 3, 1, 2).reshape(grid.shape[0], grid.shape[3], grid.shape[1] * grid.shape[2])

def upsample(value):
    return jnp.repeat(jnp.repeat(value, 2, axis=1), 2, axis=2)

def convolve(value, weight):
    kernel = weight.reshape(3, 3, value.shape[3], weight.shape[1])
    return lax.conv_general_dilated(value, kernel, (1, 1), ((1, 1), (1, 1)), dimension_numbers=('NHWC', 'HWIO', 'NHWC'), precision=HIGHEST)

def normalize(value, member, count):
    totals = lax.optimization_barrier(jnp.sum(value, axis=(1, 2)))
    squares = lax.optimization_barrier(jnp.sum(value * value, axis=(1, 2)))
    mean = jnp.dot(member.T, totals, precision=HIGHEST) / count
    meansq = jnp.dot(member.T, squares, precision=HIGHEST) / count
    scale = lax.rsqrt(meansq - mean * mean + NORM_EPSILON)
    mean_rows = jnp.dot(member, mean, precision=HIGHEST)[:, None, None, :]
    scale_rows = jnp.dot(member, scale, precision=HIGHEST)[:, None, None, :]
    return (value - mean_rows) * scale_rows

def forward(flat_source, entry, exit_w, bypass, affine, member, label_hot, mask):
    source = to_grid(flat_source, SIDE)
    gamma = jnp.dot(label_hot, affine[:KCLASS], precision=HIGHEST)[:, None, None, :]
    beta = jnp.dot(label_hot, affine[KCLASS:2 * KCLASS], precision=HIGHEST)[:, None, None, :]
    count = IMAGES // GROUPS * SIDE * SIDE
    normal_in = normalize(source, member, count)
    hidden_in = low(jax.nn.silu(gamma * normal_in + beta))
    middle = low_back(convolve(upsample(hidden_in), low(entry)))
    normal_mid = normalize(middle, member, 4 * count)
    pre_mid = affine[2 * KCLASS] * normal_mid + affine[2 * KCLASS + 1]
    hidden_mid = low(jax.nn.silu(pre_mid) * mask[:, None, None, :])
    main = convolve(hidden_mid, low(exit_w))
    short = jnp.einsum('bhwi,io->bhwo', source, low(bypass), precision=HIGHEST)
    return to_flat(main + upsample(short) + affine[2 * KCLASS + 2])

def adam_update(weight, grad, moment, square):
    moment_new = MOMENT_DECAY * moment + (1.0 - MOMENT_DECAY) * grad
    square_new = SQUARE_DECAY * square + (1.0 - SQUARE_DECAY) * grad * grad
    direction = moment_new / (1.0 - MOMENT_DECAY ** STEP) / (jnp.sqrt(square_new / (1.0 - SQUARE_DECAY ** STEP)) + ADAM_EPSILON)
    return (moment_new, square_new, direction)

def lamb(weight, grad, moment, square):
    moment_new, square_new, direction = adam_update(weight, grad, moment, square)
    update = direction + WEIGHT_DECAY * weight
    weight_norm = jnp.sqrt(jnp.sum(weight * weight))
    update_norm = jnp.sqrt(jnp.sum(update * update))
    ratio = weight_norm / update_norm
    return (moment_new, square_new, weight - MATRIX_RATE * ratio * update, jnp.stack([weight_norm, update_norm, ratio]))

def reference(features, labels, groups, widths, entry_conv, entry_moment, entry_square, exit_conv, exit_moment, exit_square, bypass_conv, bypass_moment, bypass_square, norm_affine, norm_moment, norm_square, cotangent):
    member = (groups[:, None] == jnp.arange(GROUPS, dtype=jnp.int32)[None, :]).astype(jnp.float32)
    label_hot = (labels[:, None] == jnp.arange(KCLASS, dtype=jnp.int32)[None, :]).astype(jnp.float32)
    channel = jnp.arange(C, dtype=jnp.int32)
    keep = (channel[None, :] < widths[:, None] * (C // LEVELS)).astype(jnp.float32)
    mask = jnp.dot(member, keep, precision=HIGHEST)
    source = features.astype(jnp.float32)

    def apply(a, b, c, d, e):
        return forward(a, b, c, d, e, member, label_hot, mask)
    result, pull = jax.vjp(apply, source, entry_conv, exit_conv, bypass_conv, norm_affine)
    input_gradient, entry_grad, exit_grad, bypass_grad, affine_grad = pull(cotangent.astype(jnp.float32))
    entry_first, entry_second, entry_weight, entry_norms = lamb(entry_conv, entry_grad, entry_moment, entry_square)
    exit_first, exit_second, exit_weight, exit_norms = lamb(exit_conv, exit_grad, exit_moment, exit_square)
    bypass_first, bypass_second, bypass_weight, bypass_norms = lamb(bypass_conv, bypass_grad, bypass_moment, bypass_square)
    affine_first, affine_second, direction = adam_update(norm_affine, affine_grad, norm_moment, norm_square)
    affine_values = norm_affine - AFFINE_RATE * direction
    trust_norms = jnp.stack([entry_norms, exit_norms, bypass_norms])
    return (result.astype(jnp.bfloat16), input_gradient, entry_first, entry_second, entry_weight, exit_first, exit_second, exit_weight, bypass_first, bypass_second, bypass_weight, affine_first, affine_second, affine_values, trust_norms)
```

```python
import functools
import math
from types import SimpleNamespace

import jax
import jax.numpy as jnp
from jax import lax
from jax.experimental import pallas as pl
from jax.experimental.pallas import tpu as pltpu
from jax.sharding import PartitionSpec as P

LEVELS = 4
STEP = 5
NORM_EPSILON = 1e-05
ADAM_EPSILON = 1e-06
MOMENT_DECAY = 0.9
SQUARE_DECAY = 0.999
WEIGHT_DECAY = 0.01
MATRIX_RATE = 0.3
AFFINE_RATE = 0.2

OUTER = 8
VMEM_LIMIT = 56 * 1024 * 1024
BF16 = jnp.bfloat16
F32 = jnp.float32
MESH = pl.DeviceIdType.MESH
PARTS = ("s1", "r1", "s2", "r2", "s3", "r3", "s4", "r4", "acc")


def nn(left, right):
    return lax.dot_general(left, right, (((1,), (0,)), ((), ())), preferred_element_type=F32)


def nt(left, right):
    return lax.dot_general(left, right, (((1,), (1,)), ((), ())), preferred_element_type=F32)


def flip(index, mask):
    result = index
    for bit in range(3):
        if (mask >> bit) & 1:
            digit = lax.rem(lax.div(index, 1 << bit), 2)
            result = result + (1 - 2 * digit) * (1 << bit)
    return result


def sigmoid(value):
    return 0.5 * jnp.tanh(0.5 * value) + 0.5


def iota(shape, axis):
    return lax.broadcasted_iota(jnp.int32, shape, axis)


def to_bf16(condition):
    return jnp.where(condition, 1.0, 0.0).astype(BF16)


def pick_row(table, index):
    hit = iota(table.shape, 0) == index
    return jnp.sum(jnp.where(hit, table, 0.0), axis=0, keepdims=True)


def place_row(row, index, rows):
    hit = iota((rows, row.shape[1]), 0) == index
    return jnp.where(hit, row, 0.0)


def colsum(value):
    return jnp.sum(value, axis=0, keepdims=True)


def adam_update(grad, moment, square):
    moment_new = MOMENT_DECAY * moment + (1.0 - MOMENT_DECAY) * grad
    square_new = SQUARE_DECAY * square + (1.0 - SQUARE_DECAY) * grad * grad
    direction = (
        moment_new
        / (1.0 - MOMENT_DECAY**STEP)
        / (jnp.sqrt(square_new / (1.0 - SQUARE_DECAY**STEP)) + ADAM_EPSILON)
    )
    return (moment_new, square_new, direction)


def total(value):
    return jnp.sum(jnp.sum(value, axis=1, keepdims=True), axis=0, keepdims=True)


def main_kernel(cfg, *refs):
    r = SimpleNamespace(**dict(zip(cfg.names, refs)))
    inner, n_ch, batch, local = cfg.inner, cfg.n_ch, cfg.batch, cfg.local
    classes, count = cfg.classes, cfg.count
    per = batch // n_ch
    chans = local * n_ch
    rows = cfg.rows
    small = cfg.small
    send, recv, lsem = r.send, r.recv, r.lsem
    slots = SimpleNamespace(remote=0, local=0)

    img = lax.axis_index("img")
    me = lax.axis_index("ch")
    block = lax.div(img, inner)
    within = lax.rem(img, inner)
    core = lax.rem(block, 2)
    bit_x = lax.rem(lax.div(block, 2), 2)
    bit_y = lax.div(block, 4)

    def dev(block_id, within_id, ch_id):
        return (block_id * inner + within_id, ch_id)

    pending = []

    def post(src, dst, landed, peer):
        slot = slots.remote
        slots.remote = slot + 1
        copy = pltpu.make_async_remote_copy(
            src_ref=src,
            dst_ref=dst,
            send_sem=send.at[slot],
            recv_sem=recv.at[slot],
            device_id=peer,
            device_id_type=MESH,
        )
        copy.start()
        pending.append(copy.wait_send)
        arrival = pltpu.make_async_remote_copy(
            src_ref=landed,
            dst_ref=landed,
            send_sem=send.at[slot],
            recv_sem=recv.at[slot],
            device_id=peer,
            device_id_type=MESH,
        )
        return arrival.wait_recv

    def here(src, dst):
        slot = slots.local
        slots.local = slot + 1
        copy = pltpu.make_async_copy(src, dst, lsem.at[slot])
        copy.start()
        return copy.wait

    outer_peers = [(mask, flip(block, mask)) for mask in range(1, OUTER)]
    inner_peers = [(step, lax.rem(within + step, inner)) for step in range(1, inner)]
    inner_back = [(step, lax.rem(within + inner - step, inner)) for step in range(1, inner)]
    ch_peers = [(mask, flip(me, mask)) for mask in range(1, n_ch)]

    got_features = here(r.features, r.fown)
    own_features = here(r.features.at[pl.ds(per * me, per)], r.fbuf.at[me])
    states = (
        (r.entry, r.entry_m, r.entry_q),
        (r.exit, r.exit_m, r.exit_q),
        (r.bypass, r.bypass_m, r.bypass_q),
    ) if inner == 1 else ()
    held = [
        (master, here(m, getattr(r, v + "m")), here(q, getattr(r, v + "q")), v)
        for (master, m, q), v in zip(states, ("v1", "v2", "vs"))
    ]

    barrier = pltpu.get_barrier_semaphore()
    everyone = (
        [dev(peer, within, me) for _, peer in outer_peers]
        + [dev(block, peer, me) for _, peer in inner_peers]
        + [dev(block, within, peer) for _, peer in ch_peers]
    )
    for peer in everyone:
        pl.semaphore_signal(barrier, inc=1, device_id=peer, device_id_type=MESH)
    pl.semaphore_wait(barrier, len(everyone))

    feature_waits = [
        post(
            r.features.at[pl.ds(per * peer, per)],
            r.fbuf.at[me],
            r.fbuf.at[peer],
            dev(block, within, peer),
        )
        for _, peer in ch_peers
    ]

    lane = iota((512, 512), 0)
    column = iota((512, 512), 1)
    spot = 256 * ((lane >> 6) & 1) + 64 * (lane >> 7) + (lane & 63)
    r.unpack[...] = to_bf16(column == spot)
    e_row, e_col = iota((local, 128), 0), iota((local, 128), 1)
    low_half, high_half = to_bf16(e_col == e_row), to_bf16(e_col == e_row + local)

    def pack_own(value):
        half = value.shape[0] // 2
        return (nn(value[:half], low_half) + nn(value[half:], high_half)).astype(BF16)

    hw, hs = rows // 2, small // 2
    r.wz[me, 0:hw, :] = pack_own(r.entry[...].astype(BF16))
    r.wz[me, hw : 2 * hw, :] = pack_own(r.exit[...].astype(BF16))
    r.wz[me, 2 * hw : 2 * hw + hs, :] = pack_own(r.bypass[...].astype(BF16))
    r.aff_z[me] = jnp.zeros((24, 128), F32)
    r.aff_z[me, 0 : 2 * classes + 3, 0:local] = r.affine[...]
    weight_waits = []
    for _, peer in ch_peers:
        target = dev(block, within, peer)
        weight_waits.append(post(r.wz.at[me], r.wz.at[me], r.wz.at[peer], target))
        weight_waits.append(
            post(r.aff_z.at[me], r.aff_z.at[me], r.aff_z.at[peer], target)
        )

    got_features()
    member_rows = []
    values = []
    for b in range(batch):
        values.append(r.fown[b])
        member_rows.append((iota((16, 256), 0), r.groups[b]))
    flat = jnp.concatenate(values, axis=1)
    wide = flat.astype(F32)
    square = wide * wide
    square_hi = square.astype(BF16)
    square_lo = (square - square_hi.astype(F32)).astype(BF16)
    first_mask = jnp.concatenate([to_bf16(i == g) for i, g in member_rows], axis=1)
    second_mask = jnp.concatenate([to_bf16(i == g + 4) for i, g in member_rows], axis=1)
    sums = nt(first_mask, flat) + nt(second_mask, square_hi) + nt(second_mask, square_lo)

    def ordered_sum(ref, size):
        result = ref[0]
        for slot in range(1, size):
            result = result + ref[slot]
        return result

    class AllReduce:
        def __init__(self, number):
            self.over_outer, self.over_inner, self.over_ch = (
                getattr(r, axis + str(number), None) for axis in "abc"
            )

        def begin(self, value, masked=None):
            ref = self.over_outer
            if masked is None:
                ref[block] = value
            else:
                ref[block] = jnp.zeros(ref.shape[1:], F32)
                ref[block, :, 0:masked] = value
            self.waits = [
                post(ref.at[block], ref.at[block], ref.at[peer], dev(peer, within, me))
                for _, peer in outer_peers
            ]

        def middle(self):
            for wait in self.waits:
                wait()
            value = ordered_sum(self.over_outer, OUTER)
            if inner > 1:
                ref = self.over_inner
                ref[within] = value
                waits = [
                    post(ref.at[within], ref.at[within], ref.at[back], dev(block, peer, me))
                    for (_, peer), (_, back) in zip(inner_peers, inner_back)
                ]
                for wait in waits:
                    wait()
                value = ordered_sum(ref, inner)
            ref = self.over_ch
            ref[me] = value
            self.waits = [
                post(ref.at[me], ref.at[me], ref.at[peer], dev(block, within, peer))
                for _, peer in ch_peers
            ]

        def finish(self):
            for wait in self.waits:
                wait()
            return self.over_ch

        def end(self):
            return ordered_sum(self.finish(), n_ch)

    input_sums = AllReduce(1)
    input_sums.begin(sums[0:8], masked=local)

    ident = to_bf16(iota((256, 256), 0) == iota((256, 256), 1))
    r.ident[...] = ident
    q_out, q_in = iota((256, 256), 0), iota((256, 256), 1)
    r.shift[0] = to_bf16((q_in == q_out + 1) & ((q_out & 15) < 15))
    r.shift[1] = to_bf16((q_in == q_out - 1) & ((q_out & 15) > 0))
    rho, px = iota((512, 256), 0), iota((512, 256), 1)
    version, a, b_ = rho >> 8, (rho >> 7) & 1, (rho >> 6) & 1
    col = (rho & 15) + version * (1 - 2 * b_)
    target = (2 * ((rho & 63) >> 4) + a) * 32 + 2 * col + b_
    r.gridder[...] = to_bf16((px == target) & (col >= 0) & (col < 16))
    target = (
        (2 * ((lane & 127) >> 4) + (lane >> 8)) * 32 + 2 * (lane & 15) + ((lane >> 7) & 1)
    )
    r.flatter[...] = to_bf16(column == target)

    zeros = jnp.zeros((16, 256), BF16)
    for im in range(per):
        for ver in range(3):
            r.h1s[ver, im, 0:16, :] = zeros
            r.h1s[ver, im, 272:288, :] = zeros
        for ver in range(2):
            for ph in range(4):
                for ref in (r.h2s, r.dzs):
                    ref[ver, ph, im, 0:16, :] = zeros
                    ref[ver, ph, im, 272:288, :] = zeros

    for wait in weight_waits:
        wait()
    packed = jnp.concatenate([r.wz[c] for c in range(n_ch)], axis=1)
    full = nn(packed, r.unpack[...]).astype(BF16)

    def rows_of(ref, index):
        size = ref.shape[0] // OUTER
        return ref.at[pl.ds(pl.multiple_of(size * index, 16), size)]

    def spread(ref, first, half):
        own = rows_of(ref, block)
        own[0:half, :] = full[first : first + half, 0:256]
        own[half : 2 * half, :] = full[first : first + half, 256:512]
        return {
            mask: post(own, own, rows_of(ref, flip(block, mask)), dev(flip(block, mask), within, me))
            for mask in (2, 4, 6, 1)
        }

    gather1 = spread(r.w1, 0, hw)
    gather2 = spread(r.w2, hw, hw)
    gather3 = spread(r.ws, 2 * hw, hs)
    partner = flip(block, 1)

    def forward(ref, waits):
        rest = [waits[1]]
        for mask in (2, 4, 6):
            waits[mask]()
            mine = rows_of(ref, flip(block, mask))
            theirs = rows_of(ref, flip(partner, mask))
            rest.append(post(mine, mine, theirs, dev(partner, within, me)))
        return rest

    input_sums.middle()

    own_features()
    for wait in feature_waits:
        wait()
    own_cot = here(r.cotangent.at[pl.ds(per * me, per)], r.cbuf.at[me])
    cot_waits = [
        post(
            r.cotangent.at[pl.ds(per * peer, per)],
            r.cbuf.at[me],
            r.cbuf.at[peer],
            dev(block, within, peer),
        )
        for _, peer in ch_peers
    ]

    def channel_major(ref, im, lanes):
        return jnp.concatenate([ref[c, im, :, lanes] for c in range(n_ch)], axis=0)

    for im in range(per):
        r.fpm[256 * im : 256 * im + 256, :] = nt(
            ident, channel_major(r.fbuf, im, slice(0, 256))
        ).astype(BF16)

    def wide_lanes(ref):
        parts = [
            ref[c] + pltpu.roll(ref[c + 1], local, axis=1) for c in range(0, n_ch, 2)
        ]
        return jnp.concatenate(parts, axis=1)

    affine = wide_lanes(r.aff_z)
    stats = wide_lanes(input_sums.finish())
    mean1 = stats[0:4] / count
    inv1 = lax.rsqrt(stats[4:8] / count - mean1 * mean1 + NORM_EPSILON)
    gain = affine[2 * classes : 2 * classes + 1]
    shift = affine[2 * classes + 1 : 2 * classes + 2]
    out_bias = affine[2 * classes + 2 : 2 * classes + 3]
    group, label, mean1_b, inv1_b, gamma_b, beta_b, mask_b = [], [], [], [], [], [], []
    for im in range(per):
        group.append(r.groups[per * me + im])
        label.append(r.labels[per * me + im])
        mean1_b.append(pick_row(mean1, group[im]))
        inv1_b.append(pick_row(inv1, group[im]))
        gamma_b.append(pick_row(affine, label[im]))
        beta_b.append(pick_row(affine, label[im] + classes))
        width = r.widths[group[im]]
        mask_b.append(
            jnp.where(iota((1, chans), 1) < width * (chans // LEVELS), 1.0, 0.0)
        )

    for im in range(per):
        normal = (r.fpm[256 * im : 256 * im + 256, :].astype(F32) - mean1_b[im]) * inv1_b[im]
        pre = gamma_b[im] * normal + beta_b[im]
        hidden = (pre * sigmoid(pre)).astype(BF16)
        r.h1s[1, im, 16:272, :] = hidden
        r.h1s[0, im, 16:272, :] = nn(r.shift[1], hidden).astype(BF16)
        r.h1s[2, im, 16:272, :] = nn(r.shift[0], hidden).astype(BF16)
        r.h1cm[:, 256 * im : 256 * im + 256] = nt(ident, hidden).astype(BF16)

    for wait in forward(r.w1, gather1):
        wait()

    def taps():
        return [(dy, dx) for dy in range(3) for dx in range(3)]

    def stack(pieces):
        return jnp.concatenate(pieces, axis=0)

    def conv1(phase, carry):
        a, c = lax.div(phase, 2), lax.rem(phase, 2)
        parts = []
        for dy, dx in taps():
            first = pl.multiple_of(16 * lax.div(a + dy + 1, 2), 16)
            ver = lax.div(c + dx + 1, 2)
            parts.append(
                stack([r.h1s[ver, im, pl.ds(first, 256), :] for im in range(per)])
            )
        y = nn(jnp.concatenate(parts, axis=1), r.w1[...])
        r.y1[phase] = y
        out = []
        for im in range(per):
            piece = y[256 * im : 256 * im + 256]
            out.append(carry[2 * im] + colsum(piece))
            out.append(carry[2 * im + 1] + colsum(piece * piece))
        return tuple(out)

    nought = jnp.zeros((1, chans), F32)
    mid = lax.fori_loop(0, 4, conv1, (nought,) * (2 * per))
    payload = jnp.zeros((8, chans), F32)
    for im in range(per):
        payload = payload + place_row(mid[2 * im], group[im], 8)
        payload = payload + place_row(mid[2 * im + 1], group[im] + 4, 8)
    mid_sums = AllReduce(2)
    mid_sums.begin(payload)

    rest = forward(r.w2, gather2) + forward(r.ws, gather3)
    mid_sums.middle()
    for wait in rest:
        wait()

    def turn(src, dst):
        def one(tap, carry):
            first = pl.multiple_of(256 * tap, 256)
            dst[pl.ds(first, 256), :] = nt(r.ident[...], src[pl.ds(first, 256), :]).astype(
                BF16
            )
            return carry

        lax.fori_loop(0, 9, one, 0)

    turn(r.w2, r.w2t)
    turn(r.w1, r.w1t)
    r.short[...] = nn(r.fpm[...], r.ws[...]) + out_bias

    stats = mid_sums.end()
    mean2 = stats[0:4] / (4.0 * count)
    inv2 = lax.rsqrt(stats[4:8] / (4.0 * count) - mean2 * mean2 + NORM_EPSILON)
    mean2_b = [pick_row(mean2, group[im]) for im in range(per)]
    inv2_b = [pick_row(inv2, group[im]) for im in range(per)]

    def hidden2(phase, carry):
        c = lax.rem(phase, 2)
        for im in range(per):
            span = slice(256 * im, 256 * im + 256)
            normal = (r.y1[phase, span, :] - mean2_b[im]) * inv2_b[im]
            r.y1[phase, span, :] = normal
            pre = gain * normal + shift
            sig = sigmoid(pre)
            hidden = (pre * sig * mask_b[im]).astype(BF16)
            r.slope[phase, span, :] = sig * (1.0 + pre * (1.0 - sig)) * mask_b[im]
            r.h2s[0, phase, im, 16:272, :] = hidden
            r.h2s[1, phase, im, 16:272, :] = nn(r.shift[c], hidden).astype(BF16)
            lanes = pl.ds(pl.multiple_of(512 * phase + 256 * im, 256), 256)
            r.h2cm[:, lanes] = nt(r.ident[...], hidden).astype(BF16)
        return carry

    lax.fori_loop(0, 4, hidden2, 0)

    def tap_slice(ref, a, c, dy, dx, im):
        row, colm = a + dy + 1, c + dx + 1
        first = pl.multiple_of(16 * lax.div(row, 2), 16)
        ph = 2 * lax.rem(row, 2) + lax.rem(colm, 2)
        side_step = lax.div(colm, 2) - 1
        return ref[side_step * side_step, ph, im, pl.ds(first, 256), :]

    def conv2(phase, carry):
        a, c = lax.div(phase, 2), lax.rem(phase, 2)
        parts = [
            stack([tap_slice(r.h2s, a, c, dy, dx, im) for im in range(per)]) for dy, dx in taps()
        ]
        y = (nn(jnp.concatenate(parts, axis=1), r.w2[...]) + r.short[...]).astype(BF16)
        lanes = pl.ds(pl.multiple_of(256 * phase, 256), 256)
        for im in range(per):
            r.rc[im, :, lanes] = nt(r.ident[...], y[256 * im : 256 * im + 256]).astype(BF16)
        return carry

    lax.fori_loop(0, 4, conv2, 0)
    for im in range(per):
        for half in range(2):
            piece = jnp.concatenate(
                [r.rc[im, :, 256 * ph + 128 * half : 256 * ph + 128 * half + 128] for ph in range(4)],
                axis=1,
            )
            r.ocm[im, :, 512 * half : 512 * half + 512] = nn(piece, r.flatter[...]).astype(BF16)

    def own_channels(ref, index):
        return ref.at[:, pl.ds(pl.multiple_of(local * index, local), local), :]

    own_out = here(own_channels(r.ocm, me), r.out.at[pl.ds(per * me, per)])
    out_waits = [
        post(
            own_channels(r.ocm, peer),
            r.out.at[pl.ds(per * me, per)],
            r.out.at[pl.ds(per * peer, per)],
            dev(block, within, peer),
        )
        for _, peer in ch_peers
    ]

    own_cot()
    for wait in cot_waits:
        wait()

    for im in range(per):
        for n in range(4):
            piece = channel_major(r.cbuf, im, slice(256 * n, 256 * n + 256))
            grid = nt(r.gridder[...], piece).astype(BF16)
            for ver in range(2):
                for ph in range(4):
                    at = 256 * ver + 64 * ph
                    r.dzs[ver, ph, im, 16 + 64 * n : 80 + 64 * n, :] = grid[at : at + 64]

    coarse = jnp.zeros((256 * per, chans), F32)
    for ph in range(4):
        coarse = coarse + stack([r.dzs[0, ph, im, 16:272, :] for im in range(per)]).astype(F32)
    bias_sum = colsum(coarse)
    r.dzc[...] = coarse.astype(BF16)

    def back2(phase, carry):
        a, c = lax.div(phase, 2), lax.rem(phase, 2)
        parts = [
            stack([tap_slice(r.dzs, a, c, 2 - dy, 2 - dx, im) for im in range(per)])
            for dy, dx in taps()
        ]
        act = nn(jnp.concatenate(parts, axis=1), r.w2t[...]) * r.slope[phase]
        r.act[phase] = act
        both = act * r.y1[phase]
        out = []
        for im in range(per):
            out.append(carry[2 * im] + colsum(act[256 * im : 256 * im + 256]))
            out.append(carry[2 * im + 1] + colsum(both[256 * im : 256 * im + 256]))
        return tuple(out)

    mid = lax.fori_loop(0, 4, back2, (nought,) * (2 * per))
    payload = place_row(bias_sum, 8, 16)
    for im in range(per):
        payload = payload + place_row(mid[2 * im], group[im], 16)
        payload = payload + place_row(mid[2 * im + 1], group[im] + 4, 16)
    back_sums = AllReduce(3)
    back_sums.begin(payload)

    def grad2(tap, carry):
        dy, dx = lax.div(tap, 3), lax.rem(tap, 3)
        pieces = []
        for ph in range(4):
            a, c = ph // 2, ph % 2
            for im in range(per):
                pieces.append(tap_slice(r.dzs, a, c, 2 - dy, 2 - dx, im))
        first = pl.multiple_of(256 * tap, 256)
        r.dw2[pl.ds(first, 256), :] = nn(r.h2cm[...], stack(pieces))
        return carry

    lax.fori_loop(0, 9, grad2, 0)
    back_sums.middle()
    for im in range(per):
        piece = channel_major(r.fbuf, im, slice(0, 256))
        grad = nn(piece, r.dzc[256 * im : 256 * im + 256, :])
        if im == 0:
            r.dws[...] = grad
        else:
            r.dws[...] = r.dws[...] + grad
    r.dshort[...] = nt(r.dzc[...], r.ws[...])

    class GradSum:
        def __init__(self, number, size, fetch):
            self.size, self.fetch = size, fetch
            for part in PARTS:
                setattr(self, part, getattr(r, part + str(number)))

        def begin(self):
            for u in range(4):
                self.s1[u] = self.fetch(2 * u + 1 - core).astype(BF16)
            self.waits = [
                post(self.s1, self.r1, self.r1, dev(partner, within, me))
            ]

        def first(self):
            self.waits[0]()
            for u in range(4):
                self.acc[u] = self.fetch(2 * u + core) + self.r1[u].astype(F32)
            for v in range(2):
                self.s2[0, v] = self.acc[2 * v + 1 - bit_x, :, 0:128].astype(BF16)
                self.s2[1, v] = self.acc[2 * (1 - bit_y) + v, :, 128:256].astype(BF16)
            self.waits = [
                post(
                    self.s2.at[half],
                    self.r2.at[half],
                    self.r2.at[half],
                    dev(flip(block, mask), within, me),
                )
                for half, mask in ((0, 2), (1, 4))
            ]

        def second(self):
            for wait in self.waits:
                wait()
            acc, got = self.acc, self.r2
            self.s3[0] = (
                acc[2 * (1 - bit_y) + bit_x, :, 0:128] + got[0, 1 - bit_y].astype(F32)
            ).astype(BF16)
            self.s3[1] = (
                acc[2 * bit_y + 1 - bit_x, :, 128:256] + got[1, 1 - bit_x].astype(F32)
            ).astype(BF16)
            self.waits = [
                post(
                    self.s3.at[half],
                    self.r3.at[half],
                    self.r3.at[half],
                    dev(flip(block, mask), within, me),
                )
                for half, mask in ((0, 4), (1, 2))
            ]

        def third(self):
            for wait in self.waits:
                wait()
            acc, got, last = self.acc, self.r2, self.r3
            mine = 2 * bit_y + bit_x
            low = acc[mine, :, 0:128] + got[0, bit_y].astype(F32) + last[0].astype(F32)
            high = acc[mine, :, 128:256] + got[1, bit_x].astype(F32) + last[1].astype(F32)
            done = jnp.concatenate([low, high], axis=1).astype(BF16)
            half = self.size // 2
            packed = nt(
                jnp.concatenate([done[:half], done[half:]], axis=1), r.unpack[...]
            ).astype(BF16)
            for c in range(n_ch):
                self.s4[c] = packed[:, 128 * c : 128 * c + 128]
            self.r4[me] = self.s4[me]
            self.waits = [
                post(
                    self.s4.at[peer],
                    self.r4.at[me],
                    self.r4.at[peer],
                    dev(block, within, peer),
                )
                for _, peer in ch_peers
            ]

        def end(self, out):
            for wait in self.waits:
                wait()
            done = self.r4[0].astype(F32)
            for c in range(1, n_ch):
                done = done + self.r4[c].astype(F32)
            half = self.size // 2
            out[0:half, :] = done[:, 0:local]
            out[half : 2 * half, :] = pltpu.roll(done, local, axis=1)[:, 0:local]

    def block_rows(ref, size, index):
        return ref[pl.ds(pl.multiple_of(size * index, 8), size), :]

    second = GradSum(
        2,
        rows + small,
        lambda k: jnp.concatenate([block_rows(r.dw2, rows, k), block_rows(r.dws, small, k)], axis=0),
    )
    second.begin()

    stats = back_sums.end()
    affine_grad2 = stats
    p1_b = [pick_row(stats[0:4], group[im]) / (4.0 * count) for im in range(per)]
    p2_b = [pick_row(stats[4:8], group[im]) / (4.0 * count) for im in range(per)]

    for im in range(per):
        span = slice(256 * im, 256 * im + 256)
        scale = gain * inv2_b[im]
        combos = []
        for a in range(2):
            grads = []
            for c in range(2):
                ph = 2 * a + c
                d = scale * (r.act[ph, span, :] - (p1_b[im] + r.y1[ph, span, :] * p2_b[im]))
                grads.append(d.astype(BF16))
            right = nn(r.shift[0], grads[0])
            left = nn(r.shift[1], grads[1])
            even, odd = grads[0].astype(F32), grads[1].astype(F32)
            combos.append((odd + right, even + odd, left + even))
        gap = jnp.zeros((16, chans), F32)
        for dx in range(3):
            upper, lower = combos[0][dx], combos[1][dx]
            r.field[dx, im] = (lower + jnp.concatenate([upper[16:], gap], axis=0)).astype(BF16)
            r.field[3 + dx, im] = (upper + lower).astype(BF16)
            r.field[6 + dx, im] = (jnp.concatenate([gap, lower[:-16]], axis=0) + upper).astype(BF16)

    def grad1(tap, carry):
        first = pl.multiple_of(256 * tap, 256)
        r.dw1[pl.ds(first, 256), :] = nn(
            r.h1cm[...], stack([r.field[tap, im] for im in range(per)])
        )
        return carry

    lax.fori_loop(0, 9, grad1, 0)
    entry = GradSum(1, rows, lambda k: block_rows(r.dw1, rows, k))
    entry.begin()
    second.first()

    parts = [stack([r.field[tap, im] for im in range(per)]) for tap in range(9)]
    dh1 = nn(jnp.concatenate(parts, axis=1), r.w1t[...])
    payload = jnp.zeros((32, chans), F32)
    for im in range(per):
        span = slice(256 * im, 256 * im + 256)
        normal = (r.fpm[span, :].astype(F32) - mean1_b[im]) * inv1_b[im]
        pre = gamma_b[im] * normal + beta_b[im]
        sig = sigmoid(pre)
        act = dh1[span] * (sig * (1.0 + pre * (1.0 - sig)))
        r.act1[span, :] = act
        q1, q2 = colsum(act), colsum(act * normal)
        payload = payload + place_row(q2, label[im], 32)
        payload = payload + place_row(q1, label[im] + classes, 32)
        payload = payload + place_row(gamma_b[im] * q1, group[im] + 24, 32)
        payload = payload + place_row(gamma_b[im] * q2, group[im] + 28, 32)
    last_sums = AllReduce(4)
    last_sums.begin(payload)
    entry.first()
    second.second()
    last_sums.middle()
    entry.second()
    second.third()
    entry.third()

    stats = last_sums.end()
    for im in range(per):
        span = slice(256 * im, 256 * im + 256)
        normal = (r.fpm[span, :].astype(F32) - mean1_b[im]) * inv1_b[im]
        r1 = pick_row(stats[24:28], group[im]) / count
        r2 = pick_row(stats[28:32], group[im]) / count
        grad = inv1_b[im] * (gamma_b[im] * r.act1[span, :] - (r1 + normal * r2))
        grad = (grad + r.dshort[span, :]).astype(BF16)
        r.dcm[im] = nt(r.ident[...], grad).astype(BF16)
    own_dx = here(own_channels(r.dcm, me), r.dx.at[pl.ds(per * me, per)])
    dx_waits = [
        post(
            own_channels(r.dcm, peer),
            r.dx.at[pl.ds(per * me, per)],
            r.dx.at[pl.ds(per * peer, per)],
            dev(block, within, peer),
        )
        for _, peer in ch_peers
    ]

    table = jnp.zeros((24, chans), F32)
    table = table + jnp.where(iota((24, chans), 0) < 2 * classes, stats[0:24], 0.0)
    table = table + place_row(colsum(affine_grad2[4:8]), 2 * classes, 24)
    table = table + place_row(colsum(affine_grad2[0:4]), 2 * classes + 1, 24)
    table = table + place_row(affine_grad2[8:9], 2 * classes + 2, 24)
    mine = jnp.zeros((24, 128), F32)
    for c in range(n_ch):
        piece = table[:, 128 * (c // 2) : 128 * (c // 2) + 128]
        if c % 2:
            piece = pltpu.roll(piece, local, axis=1)
        mine = mine + jnp.where(me == c, piece, 0.0)
    r.affine_grad[...] = mine

    second.end(r.grad2)
    entry.end(r.grad1)

    if inner == 1:
        squares = []
        updates = []
        grads = (r.grad1[...], r.grad2[0:rows, :], r.grad2[rows : rows + small, :])
        for (weight, got_m, got_q, v), grad in zip(held, grads):
            got_m()
            got_q()
            master = weight[...]
            _, _, direction = adam_update(
                grad, getattr(r, v + "m")[...], getattr(r, v + "q")[...]
            )
            update = direction + WEIGHT_DECAY * master
            squares.append(total(master * master))
            updates.append(total(update * update))
        norms = jnp.zeros((8, 128), F32)
        row = iota((8, 128), 0)
        for index, value in enumerate(squares + updates):
            norms = norms + jnp.where(row == index, value, 0.0)
        norm_sums = AllReduce(5)
        norm_sums.begin(norms)
        norm_sums.middle()
        r.norms[...] = norm_sums.end()
    else:
        r.norms[...] = jnp.zeros((8, 128), F32)

    own_out()
    own_dx()
    for wait in out_waits + dx_waits:
        wait()
    for wait in pending:
        wait()
    cfg.used.append(slots.remote)


def final_kernel(cfg, *refs):
    r = SimpleNamespace(**dict(zip(cfg.names, refs)))
    classes = cfg.classes
    local = cfg.local
    r.block_output[...] = r.out[...]
    r.input_gradient[...] = r.dx[...].astype(F32)
    norms = jnp.sqrt(r.norms[...])
    weight_norm, update_norm = norms[0:3, 0:1], norms[3:6, 0:1]
    ratio = weight_norm / update_norm
    at = iota((3, 3), 1)
    r.trust_norms[...] = jnp.where(
        at == 0, weight_norm, jnp.where(at == 1, update_norm, ratio)
    )
    sets = (
        (r.entry, r.entry_m, r.entry_q, r.entry_g, r.entry_1, r.entry_2, r.entry_w),
        (r.exit, r.exit_m, r.exit_q, r.exit_g, r.exit_1, r.exit_2, r.exit_w),
        (r.bypass, r.bypass_m, r.bypass_q, r.bypass_g, r.bypass_1, r.bypass_2, r.bypass_w),
    )
    for index, (weight, m, q, g, first, second, result) in enumerate(sets):
        master = weight[...]
        moment, square, direction = adam_update(g[...], m[...], q[...])
        update = direction + WEIGHT_DECAY * master
        first[...] = moment
        second[...] = square
        result[...] = master - MATRIX_RATE * ratio[index : index + 1] * update
    grad = r.affine_grad[0 : 2 * classes + 3, 0:local]
    moment, square, direction = adam_update(grad, r.affine_m[...], r.affine_q[...])
    r.affine_1[...] = moment
    r.affine_2[...] = square
    r.affine_w[...] = r.affine[...] - AFFINE_RATE * direction


def per_device(
    features,
    labels,
    groups,
    widths,
    entry_conv,
    entry_moment,
    entry_square,
    exit_conv,
    exit_moment,
    exit_square,
    bypass_conv,
    bypass_moment,
    bypass_square,
    norm_affine,
    norm_moment,
    norm_square,
    cotangent,
):
    n_img, n_ch = lax.axis_size("img"), lax.axis_size("ch")
    batch, local, pixels = features.shape
    chans = local * n_ch
    side = math.isqrt(pixels)
    inner = n_img // OUTER
    classes = (norm_affine.shape[0] - 3) // 2
    per = batch // n_ch
    assert (side, chans, n_ch, local, batch % n_ch) == (16, 256, 4, 64, 0)
    rows, small = entry_conv.shape[0] * inner, bypass_conv.shape[0] * inner
    masters = (entry_conv, exit_conv, bypass_conv)
    if inner == 1:
        blocks = masters
    else:
        sets = [[o * inner + i for i in range(inner)] for o in range(OUTER)]
        blocks = tuple(
            lax.all_gather(w.astype(BF16), "img", axis=0, tiled=True, axis_index_groups=sets)
            for w in masters
        )

    vmem = pl.BlockSpec(memory_space=pltpu.VMEM)
    smem = pl.BlockSpec(memory_space=pltpu.SMEM)
    anywhere = pl.BlockSpec(memory_space=pl.ANY)
    states = dict(
        entry_m=entry_moment,
        entry_q=entry_square,
        exit_m=exit_moment,
        exit_q=exit_square,
        bypass_m=bypass_moment,
        bypass_q=bypass_square,
    )
    inputs = dict(
        labels=(labels, smem),
        groups=(groups, smem),
        widths=(widths, smem),
        features=(features, anywhere),
        cotangent=(cotangent, anywhere),
        entry=(blocks[0], vmem),
        exit=(blocks[1], vmem),
        bypass=(blocks[2], vmem),
        affine=(norm_affine, vmem),
    )
    if inner == 1:
        inputs.update({name: (value, anywhere) for name, value in states.items()})
    sds = jax.ShapeDtypeStruct
    outputs = dict(
        out=(sds(cotangent.shape, BF16), anywhere),
        dx=(sds(features.shape, BF16), anywhere),
        grad1=(sds((rows, local), F32), vmem),
        grad2=(sds((rows + small, local), F32), vmem),
        affine_grad=(sds((24, 128), F32), vmem),
        norms=(sds((8, 128), F32), vmem),
    )
    pix = pixels * per
    taps9 = 9 * chans
    held = lambda shape, dtype=BF16: pltpu.VMEM(shape, dtype)
    scratch = dict(
        fown=held((batch, local, pixels)),
        fbuf=held((n_ch, per, local, pixels)),
        cbuf=held((n_ch, per, local, 4 * pixels)),
        wz=held((n_ch, rows + small // 2, 128)),
        aff_z=held((n_ch, 24, 128), F32),
        w1=held((taps9, chans)),
        w2=held((taps9, chans)),
        ws=held((chans, chans)),
        w1t=held((taps9, chans)),
        w2t=held((taps9, chans)),
        unpack=held((512, 512)),
        ident=held((256, 256)),
        shift=held((2, 256, 256)),
        gridder=held((512, 256)),
        flatter=held((512, 512)),
        fpm=held((pix, chans)),
        h1s=held((3, per, pixels + 32, chans)),
        h1cm=held((chans, pix)),
        y1=held((4, pix, chans), F32),
        slope=held((4, pix, chans), F32),
        act=held((4, pix, chans), F32),
        h2s=held((2, 4, per, pixels + 32, chans)),
        dzs=held((2, 4, per, pixels + 32, chans)),
        h2cm=held((chans, 4 * pix)),
        short=held((pix, chans), F32),
        dshort=held((pix, chans), F32),
        dzc=held((pix, chans)),
        act1=held((pix, chans), F32),
        rc=held((per, chans, 4 * pixels)),
        ocm=held((per, chans, 4 * pixels)),
        dcm=held((per, chans, pixels)),
        field=held((9, per, pixels, chans)),
        dw1=held((taps9, chans), F32),
        dw2=held((taps9, chans), F32),
        dws=held((chans, chans), F32),
    )
    for number, size in ((1, rows), (2, rows + small)):
        shapes = (
            (4, size, chans),
            (4, size, chans),
            (2, 2, size, 128),
            (2, 2, size, 128),
            (2, size, 128),
            (2, size, 128),
            (n_ch, size // 2, 128),
            (n_ch, size // 2, 128),
        )
        for part, shape in zip(PARTS, shapes):
            scratch[part + str(number)] = held(shape)
        scratch[PARTS[-1] + str(number)] = held((4, size, chans), F32)
    exchanges = [(8, 128), (8, chans), (16, chans), (32, chans)]
    if inner == 1:
        exchanges.append((8, 128))
        for v, weight in zip(("v1", "v2", "vs"), masters):
            scratch[v + "m"] = held(weight.shape, F32)
            scratch[v + "q"] = held(weight.shape, F32)
    for number, shape in enumerate(exchanges, 1):
        for axis, size in zip("abc", (OUTER, inner, n_ch)):
            if size > 1:
                scratch[axis + str(number)] = held((size,) + shape, F32)
    remote_count = 3 + 6 + 3 * 7 + 3 + 6 + 2 * (1 + 2 + 2 + 3)
    remote_count += len(exchanges) * (7 + 3 + inner - 1)
    scratch.update(
        send=pltpu.SemaphoreType.DMA((remote_count,)),
        recv=pltpu.SemaphoreType.DMA((remote_count,)),
        lsem=pltpu.SemaphoreType.DMA((16,)),
    )
    cfg = SimpleNamespace(
        names=[*inputs, *outputs, *scratch],
        inner=inner,
        n_ch=n_ch,
        batch=batch,
        local=local,
        classes=classes,
        count=float(batch * n_img // widths.shape[0] * pixels),
        rows=rows,
        small=small,
        used=[],
    )
    out, dx, grad1, grad2, affine_grad, norms = pl.pallas_call(
        functools.partial(main_kernel, cfg),
        out_shape=[s for s, _ in outputs.values()],
        in_specs=[s for _, s in inputs.values()],
        out_specs=[s for _, s in outputs.values()],
        scratch_shapes=list(scratch.values()),
        compiler_params=pltpu.CompilerParams(
            collective_id=0, has_side_effects=True, vmem_limit_bytes=VMEM_LIMIT
        ),
        name="block_step",
    )(*[v for v, _ in inputs.values()])
    assert max(cfg.used) <= remote_count

    grads = [grad1, grad2[:rows], grad2[rows:]]
    if inner > 1:
        grads = [
            lax.psum_scatter(g, "img", scatter_dimension=0, axis_index_groups=sets, tiled=True)
            for g in grads
        ]
        updates = []
        for w, g, m, s in zip(
            masters,
            grads,
            (entry_moment, exit_moment, bypass_moment),
            (entry_square, exit_square, bypass_square),
        ):
            updates.append(adam_update(g, m, s)[2] + WEIGHT_DECAY * w)
        sums = lax.psum(
            jnp.stack([jnp.sum(w * w) for w in masters] + [jnp.sum(u * u) for u in updates]),
            ("img", "ch"),
        )
        norms = jnp.broadcast_to(jnp.pad(sums, (0, 2))[:, None], (8, 128))

    args = dict(
        out=out,
        dx=dx,
        norms=norms,
        affine_grad=affine_grad,
        entry_g=grads[0],
        exit_g=grads[1],
        bypass_g=grads[2],
        entry=entry_conv,
        exit=exit_conv,
        bypass=bypass_conv,
        **states,
        affine=norm_affine,
        affine_m=norm_moment,
        affine_q=norm_square,
    )
    tall, short, wide = (sds(w.shape, F32) for w in (entry_conv, bypass_conv, norm_affine))
    results = dict(
        block_output=sds(cotangent.shape, BF16),
        input_gradient=sds(features.shape, F32),
        entry_1=tall,
        entry_2=tall,
        entry_w=tall,
        exit_1=tall,
        exit_2=tall,
        exit_w=tall,
        bypass_1=short,
        bypass_2=short,
        bypass_w=short,
        affine_1=wide,
        affine_2=wide,
        affine_w=wide,
        trust_norms=sds((3, 3), F32),
    )
    end_cfg = SimpleNamespace(names=[*args, *results], classes=classes, local=local)
    return tuple(
        pl.pallas_call(
            functools.partial(final_kernel, end_cfg),
            out_shape=list(results.values()),
            in_specs=[vmem] * len(args),
            out_specs=[vmem] * len(results),
            compiler_params=pltpu.CompilerParams(vmem_limit_bytes=VMEM_LIMIT),
            name="finish",
        )(*args.values())
    )


def solution(mesh):
    wide = P("img", "ch")
    deep = P("img", "ch", None)
    table = P(None, "ch")
    return jax.shard_map(
        per_device,
        mesh=mesh,
        in_specs=(deep, P("img"), P("img"), P()) + (wide,) * 9 + (table,) * 3 + (deep,),
        out_specs=(deep, deep) + (wide,) * 9 + (table,) * 3 + (P(),),
        check_vma=False,
    )
```

```python
import functools
import math
from types import SimpleNamespace

import jax
import jax.numpy as jnp
from jax import lax
from jax.experimental import pallas as pl
from jax.experimental.pallas import tpu as pltpu
from jax.sharding import PartitionSpec as P

LEVELS = 4
STEP = 5
NORM_EPSILON = 1e-05
ADAM_EPSILON = 1e-06
MOMENT_DECAY = 0.9
SQUARE_DECAY = 0.999
WEIGHT_DECAY = 0.01
MATRIX_RATE = 0.3
AFFINE_RATE = 0.2

OUTER = 8
VMEM_LIMIT = 56 * 1024 * 1024
BF16 = jnp.bfloat16
F32 = jnp.float32
MESH = pl.DeviceIdType.MESH
PARTS = ("s1", "r1", "s2", "r2")


def nn(left, right):
    return lax.dot_general(left, right, (((1,), (0,)), ((), ())), preferred_element_type=F32)


def nt(left, right):
    return lax.dot_general(left, right, (((1,), (1,)), ((), ())), preferred_element_type=F32)


def flip(index, mask):
    result = index
    for bit in range(3):
        if (mask >> bit) & 1:
            digit = lax.rem(lax.div(index, 1 << bit), 2)
            result = result + (1 - 2 * digit) * (1 << bit)
    return result


def sigmoid(value):
    return 0.5 * jnp.tanh(0.5 * value) + 0.5


def iota(shape, axis):
    return lax.broadcasted_iota(jnp.int32, shape, axis)


def to_bf16(condition):
    return jnp.where(condition, 1.0, 0.0).astype(BF16)


def pick_row(table, index):
    hit = iota(table.shape, 0) == index
    return jnp.sum(jnp.where(hit, table, 0.0), axis=0, keepdims=True)


def place_row(row, index, rows):
    hit = iota((rows, row.shape[1]), 0) == index
    return jnp.where(hit, row, 0.0)


def colsum(value):
    return jnp.sum(value, axis=0, keepdims=True)


def adam_update(grad, moment, square):
    moment_new = MOMENT_DECAY * moment + (1.0 - MOMENT_DECAY) * grad
    square_new = SQUARE_DECAY * square + (1.0 - SQUARE_DECAY) * grad * grad
    direction = (
        moment_new
        / (1.0 - MOMENT_DECAY**STEP)
        / (jnp.sqrt(square_new / (1.0 - SQUARE_DECAY**STEP)) + ADAM_EPSILON)
    )
    return (moment_new, square_new, direction)


def total(value):
    return jnp.sum(jnp.sum(value, axis=1, keepdims=True), axis=0, keepdims=True)


def main_kernel(cfg, *refs):
    r = SimpleNamespace(**dict(zip(cfg.names, refs)))
    inner, n_ch, batch, local = cfg.inner, cfg.n_ch, cfg.batch, cfg.local
    classes, count = cfg.classes, cfg.count
    per = batch // n_ch
    chans = local * n_ch
    rows, small = cfg.rows, cfg.small
    tail = (rows - 256) // 2
    hw, hs = rows // 2, small // 2
    slots = SimpleNamespace(remote=0, local=0)

    img = lax.axis_index("img")
    me = lax.axis_index("ch")
    block = lax.div(img, inner)
    within = lax.rem(img, inner)
    core = lax.rem(block, 2)
    plane = lax.div(block, 2)
    partner = flip(block, 1)

    def dev(block_id, within_id, ch_id):
        return (block_id * inner + within_id, ch_id)

    pending = []

    def post(src, dst, landed, peer):
        slot = slots.remote
        slots.remote = slot + 1
        copy = pltpu.make_async_remote_copy(
            src_ref=src,
            dst_ref=dst,
            send_sem=r.send.at[slot],
            recv_sem=r.recv.at[slot],
            device_id=peer,
            device_id_type=MESH,
        )
        copy.start()
        pending.append(copy.wait_send)
        arrival = pltpu.make_async_remote_copy(
            src_ref=landed,
            dst_ref=landed,
            send_sem=r.send.at[slot],
            recv_sem=r.recv.at[slot],
            device_id=peer,
            device_id_type=MESH,
        )
        return arrival.wait_recv

    def here(src, dst):
        slot = slots.local
        slots.local = slot + 1
        copy = pltpu.make_async_copy(src, dst, r.lsem.at[slot])
        copy.start()
        return copy.wait

    outer_peers = [flip(block, mask) for mask in range(1, OUTER)]
    ch_peers = [flip(me, mask) for mask in range(1, n_ch)]
    inner_pairs = [
        (lax.rem(within + step, inner), lax.rem(within + inner - step, inner))
        for step in range(1, inner)
    ]
    all_peers = [
        (flip(block, mask), flip(me, turn))
        for mask in range(OUTER)
        for turn in range(n_ch)
        if mask or turn
    ]

    barrier = pltpu.get_barrier_semaphore()
    everyone = [dev(b, within, c) for b, c in all_peers]
    everyone += [dev(block, peer, me) for peer, _ in inner_pairs]
    for peer in everyone:
        pl.semaphore_signal(barrier, inc=1, device_id=peer, device_id_type=MESH)

    got_entry = here(r.entry, r.entry_v)
    got_features = here(r.features, r.fown)
    got_exit = here(r.exit, r.exit_v)
    got_bypass = here(r.bypass, r.bypass_v)
    got_affine = here(r.affine, r.affine_v)
    own_features = here(r.features.at[pl.ds(per * me, per)], r.fbuf.at[me])
    own_cot = here(r.cotangent.at[pl.ds(per * me, per)], r.cbuf.at[me])
    states = ((r.entry_m, r.entry_q), (r.exit_m, r.exit_q), (r.bypass_m, r.bypass_q)) if inner == 1 else ()
    held = [
        (here(m, getattr(r, v + "m")), here(q, getattr(r, v + "q")))
        for (m, q), v in zip(states, ("v1", "v2", "vs"))
    ]

    s_row, s_col = iota((hw, 384), 0), iota((hw, 384), 1)
    pick_first = to_bf16(s_col == jnp.where(s_row < 128, s_row, s_row + 128))
    pick_second = to_bf16(s_col == jnp.where(s_row < 128, s_row + 128, s_row + 128 + tail))
    r.padded[...] = jnp.zeros(r.padded.shape, BF16)

    def pack_own(value):
        r.padded[local : 2 * local, 0:rows] = value.astype(BF16)
        packed = nt(pick_first, r.padded[local : 3 * local, :])
        return (packed + nt(pick_second, r.padded[0 : 2 * local, :])).astype(BF16)

    got_entry()
    r.wz1[me] = pack_own(r.entry_v[...])
    pl.semaphore_wait(barrier, len(everyone))

    def to_channels(buffer):
        return [
            post(buffer.at[me], buffer.at[me], buffer.at[peer], dev(block, within, peer))
            for peer in ch_peers
        ]

    entry_waits = to_channels(r.wz1)
    feature_waits = [
        post(
            r.features.at[pl.ds(per * peer, per)],
            r.fbuf.at[me],
            r.fbuf.at[peer],
            dev(block, within, peer),
        )
        for peer in ch_peers
    ]
    got_affine()
    r.aff_z[me] = jnp.zeros((24, 128), F32)
    r.aff_z[me, 0 : 2 * classes + 3, 0:local] = r.affine_v[...]
    affine_waits = to_channels(r.aff_z)

    lane = iota((512, 512), 0)
    column = iota((512, 512), 1)
    spot = 256 * ((lane >> 6) & 1) + 64 * (lane >> 7) + (lane & 63)
    r.unpack[...] = to_bf16(column == spot)

    got_features()
    flat = jnp.concatenate([r.fown[b] for b in range(batch)], axis=1)
    wide = flat.astype(F32)
    square = wide * wide
    square_hi = square.astype(BF16)
    square_lo = (square - square_hi.astype(F32)).astype(BF16)
    level = iota((16, 256), 0)
    first_mask = jnp.concatenate([to_bf16(level == r.groups[b]) for b in range(batch)], axis=1)
    second_mask = jnp.concatenate([to_bf16(level == r.groups[b] + 4) for b in range(batch)], axis=1)
    sums = nt(first_mask, flat) + nt(second_mask, square_hi) + nt(second_mask, square_lo)

    def ordered_sum(ref, size):
        result = ref[0]
        for slot in range(1, size):
            result = result + ref[slot]
        return result

    class AllReduce:
        def __init__(self, number):
            self.over_outer, self.over_inner, self.over_ch = (
                getattr(r, axis + str(number), None) for axis in "abc"
            )

        def begin(self, value, masked=None):
            ref = self.over_outer
            if masked is None:
                ref[block] = value
            else:
                ref[block] = jnp.zeros(ref.shape[1:], F32)
                ref[block, :, 0:masked] = value
            self.waits = [
                post(ref.at[block], ref.at[block], ref.at[peer], dev(peer, within, me))
                for peer in outer_peers
            ]

        def middle(self):
            for wait in self.waits:
                wait()
            value = ordered_sum(self.over_outer, OUTER)
            if inner > 1:
                ref = self.over_inner
                ref[within] = value
                waits = [
                    post(ref.at[within], ref.at[within], ref.at[back], dev(block, peer, me))
                    for peer, back in inner_pairs
                ]
                for wait in waits:
                    wait()
                value = ordered_sum(ref, inner)
            self.over_ch[me] = value
            self.waits = to_channels(self.over_ch)

        def finish(self):
            for wait in self.waits:
                wait()
            return self.over_ch

        def end(self):
            return ordered_sum(self.finish(), n_ch)

    input_sums = AllReduce(1)
    input_sums.begin(sums[0:8], masked=local)

    got_exit()
    got_bypass()
    r.wz2[me, 0:hw, :] = pack_own(r.exit_v[...])
    e_row, e_col = iota((local, 128), 0), iota((local, 128), 1)
    value = r.bypass_v[...].astype(BF16)
    r.wz2[me, hw : hw + hs, :] = (
        nn(value[:hs], to_bf16(e_col == e_row)) + nn(value[hs:], to_bf16(e_col == e_row + local))
    ).astype(BF16)

    def rows_of(ref, index):
        size = ref.shape[0] // OUTER
        return ref.at[pl.ds(pl.multiple_of(size * index, 16), size)]

    def unpack_own(ref, full):
        own = rows_of(ref, block)
        if full.shape[0] == hw:
            own[0:128, :] = full[0:128, 0:256]
            own[128:256, :] = full[0:128, 256:512]
            own[256 : 256 + tail, :] = full[128:, 0:256]
            own[256 + tail :, :] = full[128:, 256:512]
        else:
            own[0:hs, :] = full[:, 0:256]
            own[hs:, :] = full[:, 256:512]

    def spread(ref):
        own = rows_of(ref, block)
        return {
            mask: post(own, own, rows_of(ref, flip(block, mask)), dev(flip(block, mask), within, me))
            for mask in (2, 4, 6, 1)
        }

    def forward(ref, waits):
        rest = [waits[1]]
        for mask in (2, 4, 6):
            waits[mask]()
            mine = rows_of(ref, flip(block, mask))
            theirs = rows_of(ref, flip(partner, mask))
            rest.append(post(mine, mine, theirs, dev(partner, within, me)))
        return rest

    def widen(buffer):
        packed = jnp.concatenate([buffer[c] for c in range(n_ch)], axis=1)
        return nn(packed, r.unpack[...]).astype(BF16)

    for wait in entry_waits:
        wait()
    unpack_own(r.w1, widen(r.wz1))
    gather1 = spread(r.w1)
    exit_waits = to_channels(r.wz2)

    ident = to_bf16(iota((256, 256), 0) == iota((256, 256), 1))
    r.ident[...] = ident
    q_out, q_in = iota((256, 256), 0), iota((256, 256), 1)
    r.shift[0] = to_bf16((q_in == q_out + 1) & ((q_out & 15) < 15))
    r.shift[1] = to_bf16((q_in == q_out - 1) & ((q_out & 15) > 0))

    input_sums.middle()
    cot_waits = [
        post(
            r.cotangent.at[pl.ds(per * peer, per)],
            r.cbuf.at[me],
            r.cbuf.at[peer],
            dev(block, within, peer),
        )
        for peer in ch_peers
    ]

    rho, px = iota((512, 256), 0), iota((512, 256), 1)
    version, a, b_ = rho >> 8, (rho >> 7) & 1, (rho >> 6) & 1
    col = (rho & 15) + version * (1 - 2 * b_)
    target = (2 * ((rho & 63) >> 4) + a) * 32 + 2 * col + b_
    r.gridder[...] = to_bf16((px == target) & (col >= 0) & (col < 16))
    target = (
        (2 * ((lane & 127) >> 4) + (lane >> 8)) * 32 + 2 * (lane & 15) + ((lane >> 7) & 1)
    )
    r.flatter[...] = to_bf16(column == target)
    zeros = jnp.zeros((16, 256), BF16)
    for im in range(per):
        for ver in range(3):
            r.h1s[ver, im, 0:16, :] = zeros
            r.h1s[ver, im, 272:288, :] = zeros
        for ver in range(2):
            for ph in range(4):
                for ref in (r.h2s, r.dzs):
                    ref[ver, ph, im, 0:16, :] = zeros
                    ref[ver, ph, im, 272:288, :] = zeros

    def channel_major(ref, im, lanes):
        return jnp.concatenate([ref[c, im, :, lanes] for c in range(n_ch)], axis=0)

    own_features()
    for wait in feature_waits:
        wait()
    for im in range(per):
        r.fpm[256 * im : 256 * im + 256, :] = nt(
            ident, channel_major(r.fbuf, im, slice(0, 256))
        ).astype(BF16)

    def wide_lanes(ref):
        parts = [
            ref[c] + pltpu.roll(ref[c + 1], local, axis=1) for c in range(0, n_ch, 2)
        ]
        return jnp.concatenate(parts, axis=1)

    for wait in affine_waits:
        wait()
    affine = wide_lanes(r.aff_z)
    stats = wide_lanes(input_sums.finish())
    mean1 = stats[0:4] / count
    inv1 = lax.rsqrt(stats[4:8] / count - mean1 * mean1 + NORM_EPSILON)
    gain = affine[2 * classes : 2 * classes + 1]
    shift = affine[2 * classes + 1 : 2 * classes + 2]
    out_bias = affine[2 * classes + 2 : 2 * classes + 3]
    group, label, mean1_b, inv1_b, gamma_b, beta_b, mask_b = [], [], [], [], [], [], []
    for im in range(per):
        group.append(r.groups[per * me + im])
        label.append(r.labels[per * me + im])
        mean1_b.append(pick_row(mean1, group[im]))
        inv1_b.append(pick_row(inv1, group[im]))
        gamma_b.append(pick_row(affine, label[im]))
        beta_b.append(pick_row(affine, label[im] + classes))
        width = r.widths[group[im]]
        mask_b.append(
            jnp.where(iota((1, chans), 1) < width * (chans // LEVELS), 1.0, 0.0)
        )

    for im in range(per):
        normal = (r.fpm[256 * im : 256 * im + 256, :].astype(F32) - mean1_b[im]) * inv1_b[im]
        pre = gamma_b[im] * normal + beta_b[im]
        hidden = (pre * sigmoid(pre)).astype(BF16)
        r.h1s[1, im, 16:272, :] = hidden
        r.h1s[0, im, 16:272, :] = nn(r.shift[1], hidden).astype(BF16)
        r.h1s[2, im, 16:272, :] = nn(r.shift[0], hidden).astype(BF16)
        r.h1cm[:, 256 * im : 256 * im + 256] = nt(ident, hidden).astype(BF16)

    for wait in exit_waits:
        wait()
    full = widen(r.wz2)
    unpack_own(r.w2, full[0:hw])
    unpack_own(r.ws, full[hw:])
    rest = forward(r.w1, gather1)
    gather2 = spread(r.w2)
    gather3 = spread(r.ws)
    for wait in rest:
        wait()

    def taps():
        return [(dy, dx) for dy in range(3) for dx in range(3)]

    def stack(pieces):
        return jnp.concatenate(pieces, axis=0)

    def conv1(phase, carry):
        a, c = lax.div(phase, 2), lax.rem(phase, 2)
        parts = []
        for dy, dx in taps():
            first = pl.multiple_of(16 * lax.div(a + dy + 1, 2), 16)
            ver = lax.div(c + dx + 1, 2)
            parts.append(
                stack([r.h1s[ver, im, pl.ds(first, 256), :] for im in range(per)])
            )
        y = nn(jnp.concatenate(parts, axis=1), r.w1[...])
        r.y1[phase] = y
        out = []
        for im in range(per):
            piece = y[256 * im : 256 * im + 256]
            out.append(carry[2 * im] + colsum(piece))
            out.append(carry[2 * im + 1] + colsum(piece * piece))
        return tuple(out)

    nought = jnp.zeros((1, chans), F32)
    mid = lax.fori_loop(0, 4, conv1, (nought,) * (2 * per))
    payload = jnp.zeros((8, chans), F32)
    for im in range(per):
        payload = payload + place_row(mid[2 * im], group[im], 8)
        payload = payload + place_row(mid[2 * im + 1], group[im] + 4, 8)
    mid_sums = AllReduce(2)
    mid_sums.begin(payload)

    def turn(src, dst):
        def one(tap, carry):
            first = pl.multiple_of(256 * tap, 256)
            dst[pl.ds(first, 256), :] = nt(r.ident[...], src[pl.ds(first, 256), :]).astype(BF16)
            return carry

        lax.fori_loop(0, 9, one, 0)

    turn(r.w1, r.w1t)
    rest = forward(r.w2, gather2) + forward(r.ws, gather3)
    mid_sums.middle()

    own_cot()
    for wait in cot_waits:
        wait()
    for im in range(per):
        for n in range(4):
            piece = channel_major(r.cbuf, im, slice(256 * n, 256 * n + 256))
            grid = nt(r.gridder[...], piece).astype(BF16)
            for ver in range(2):
                for ph in range(4):
                    at = 256 * ver + 64 * ph
                    r.dzs[ver, ph, im, 16 + 64 * n : 80 + 64 * n, :] = grid[at : at + 64]

    coarse = jnp.zeros((256 * per, chans), F32)
    for ph in range(4):
        coarse = coarse + stack([r.dzs[0, ph, im, 16:272, :] for im in range(per)]).astype(F32)
    bias_sum = colsum(coarse)
    r.dzc[...] = coarse.astype(BF16)

    def tap_slice(ref, a, c, dy, dx, im):
        row, colm = a + dy + 1, c + dx + 1
        first = pl.multiple_of(16 * lax.div(row, 2), 16)
        ph = 2 * lax.rem(row, 2) + lax.rem(colm, 2)
        side_step = lax.div(colm, 2) - 1
        return ref[side_step * side_step, ph, im, pl.ds(first, 256), :]

    for wait in rest:
        wait()
    turn(r.w2, r.w2t)

    def back2(phase, carry):
        a, c = lax.div(phase, 2), lax.rem(phase, 2)
        parts = [
            stack([tap_slice(r.dzs, a, c, 2 - dy, 2 - dx, im) for im in range(per)])
            for dy, dx in taps()
        ]
        r.act[phase] = nn(jnp.concatenate(parts, axis=1), r.w2t[...])
        return carry

    lax.fori_loop(0, 4, back2, 0)

    stats = mid_sums.end()
    mean2 = stats[0:4] / (4.0 * count)
    inv2 = lax.rsqrt(stats[4:8] / (4.0 * count) - mean2 * mean2 + NORM_EPSILON)
    mean2_b = [pick_row(mean2, group[im]) for im in range(per)]
    inv2_b = [pick_row(inv2, group[im]) for im in range(per)]

    def hidden2(phase, carry):
        c = lax.rem(phase, 2)
        out = []
        for im in range(per):
            span = slice(256 * im, 256 * im + 256)
            normal = (r.y1[phase, span, :] - mean2_b[im]) * inv2_b[im]
            r.y1[phase, span, :] = normal
            pre = gain * normal + shift
            sig = sigmoid(pre)
            hidden = (pre * sig * mask_b[im]).astype(BF16)
            act = r.act[phase, span, :] * (sig * (1.0 + pre * (1.0 - sig)) * mask_b[im])
            r.act[phase, span, :] = act
            out.append(carry[2 * im] + colsum(act))
            out.append(carry[2 * im + 1] + colsum(act * normal))
            r.h2s[0, phase, im, 16:272, :] = hidden
            r.h2s[1, phase, im, 16:272, :] = nn(r.shift[c], hidden).astype(BF16)
            lanes = pl.ds(pl.multiple_of(512 * phase + 256 * im, 256), 256)
            r.h2cm[:, lanes] = nt(r.ident[...], hidden).astype(BF16)
        return tuple(out)

    mid = lax.fori_loop(0, 4, hidden2, (nought,) * (2 * per))
    payload = place_row(bias_sum, 8, 16)
    for im in range(per):
        payload = payload + place_row(mid[2 * im], group[im], 16)
        payload = payload + place_row(mid[2 * im + 1], group[im] + 4, 16)
    back_sums = AllReduce(3)
    back_sums.begin(payload)

    def grad2(tap, carry):
        dy, dx = lax.div(tap, 3), lax.rem(tap, 3)
        pieces = []
        for ph in range(4):
            a, c = ph // 2, ph % 2
            for im in range(per):
                pieces.append(tap_slice(r.dzs, a, c, 2 - dy, 2 - dx, im))
        first = pl.multiple_of(256 * tap, 256)
        r.dw2[pl.ds(first, 256), :] = nn(r.h2cm[...], stack(pieces))
        return carry

    lax.fori_loop(0, 9, grad2, 0)
    back_sums.middle()
    for im in range(per):
        piece = channel_major(r.fbuf, im, slice(0, 256))
        grad = nn(piece, r.dzc[256 * im : 256 * im + 256, :])
        if im == 0:
            r.dws[...] = grad
        else:
            r.dws[...] = r.dws[...] + grad

    class GradSum:
        def __init__(self, number, fetch):
            self.fetch = fetch
            for part in PARTS:
                setattr(self, part, getattr(r, part + str(number)))

        def begin(self):
            for u in range(4):
                self.s1[u] = self.fetch(2 * u + 1 - core).astype(BF16)
            self.wait = post(self.s1, self.r1, self.r1, dev(partner, within, me))

        def first(self):
            self.wait()
            for u in range(4):
                value = (self.fetch(2 * u + core) + self.r1[u].astype(F32)).astype(BF16)
                left = [value[0:128], value[256 : 256 + tail]]
                right = [value[128:256], value[256 + tail : rows]]
                if value.shape[0] > rows:
                    left.append(value[rows : rows + hs])
                    right.append(value[rows + hs :])
                pair = jnp.concatenate([stack(left), stack(right)], axis=1)
                packed = nt(pair, r.unpack[...]).astype(BF16)
                for c in range(n_ch):
                    self.s2[u, c] = packed[:, 128 * c : 128 * c + 128]
            self.r2[plane, me] = self.s2[plane, me]
            self.waits = [
                post(
                    self.s2.at[lax.div(b, 2), c],
                    self.r2.at[plane, me],
                    self.r2.at[lax.div(b, 2), c],
                    dev(b, within, c),
                )
                for b, c in [
                    (flip(block, mask), flip(me, turn))
                    for turn in range(n_ch)
                    for mask in (0, 2, 4, 6)
                    if mask or turn
                ]
            ]

        def end(self, out, out_small=None):
            for wait in self.waits:
                wait()
            done = None
            for u in range(4):
                for c in range(n_ch):
                    piece = self.r2[u, c].astype(F32)
                    done = piece if done is None else done + piece
            turned = done[0:128].T
            out[:, 0:128] = turned[0:local]
            out[:, 128:256] = turned[local:]
            gap = jnp.zeros((128 - tail, 128), F32)
            turned = stack([done[128 : 128 + tail], gap]).T
            ends = turned[0:local] + pltpu.roll(turned[local:], tail, axis=1)
            out[:, 256:rows] = ends[:, 0 : rows - 256]
            if out_small is not None:
                last = done[hw:]
                out_small[0:hs, :] = last[:, 0:local]
                out_small[hs:, :] = pltpu.roll(last, local, axis=1)[:, 0:local]

    def block_rows(ref, size, index):
        return ref[pl.ds(pl.multiple_of(size * index, 8), size), :]

    second = GradSum(2, lambda k: stack([block_rows(r.dw2, rows, k), block_rows(r.dws, small, k)]))
    entry = GradSum(1, lambda k: block_rows(r.dw1, rows, k))
    second.begin()
    r.short[...] = nn(r.fpm[...], r.ws[...]) + out_bias
    r.dshort[...] = nt(r.dzc[...], r.ws[...])

    def conv2(phase, carry):
        a, c = lax.div(phase, 2), lax.rem(phase, 2)
        parts = [
            stack([tap_slice(r.h2s, a, c, dy, dx, im) for im in range(per)]) for dy, dx in taps()
        ]
        y = (nn(jnp.concatenate(parts, axis=1), r.w2[...]) + r.short[...]).astype(BF16)
        lanes = pl.ds(pl.multiple_of(256 * phase, 256), 256)
        for im in range(per):
            r.rc[im, :, lanes] = nt(r.ident[...], y[256 * im : 256 * im + 256]).astype(BF16)
        return carry

    lax.fori_loop(0, 4, conv2, 0)
    for im in range(per):
        for half in range(2):
            piece = jnp.concatenate(
                [r.rc[im, :, 256 * ph + 128 * half : 256 * ph + 128 * half + 128] for ph in range(4)],
                axis=1,
            )
            r.ocm[im, :, 512 * half : 512 * half + 512] = nn(piece, r.flatter[...]).astype(BF16)

    def own_channels(ref, index):
        return ref.at[:, pl.ds(pl.multiple_of(local * index, local), local), :]

    def give_back(ref, out):
        waits = [here(own_channels(ref, me), out.at[pl.ds(per * me, per)])]
        return waits + [
            post(
                own_channels(ref, peer),
                out.at[pl.ds(per * me, per)],
                out.at[pl.ds(per * peer, per)],
                dev(block, within, peer),
            )
            for peer in ch_peers
        ]

    out_waits = give_back(r.ocm, r.out)

    stats = back_sums.end()
    affine_grad2 = stats
    p1_b = [pick_row(stats[0:4], group[im]) / (4.0 * count) for im in range(per)]
    p2_b = [pick_row(stats[4:8], group[im]) / (4.0 * count) for im in range(per)]

    for im in range(per):
        span = slice(256 * im, 256 * im + 256)
        scale = gain * inv2_b[im]
        combos = []
        for a in range(2):
            grads = []
            for c in range(2):
                ph = 2 * a + c
                d = scale * (r.act[ph, span, :] - (p1_b[im] + r.y1[ph, span, :] * p2_b[im]))
                grads.append(d.astype(BF16))
            right = nn(r.shift[0], grads[0])
            left = nn(r.shift[1], grads[1])
            even, odd = grads[0].astype(F32), grads[1].astype(F32)
            combos.append((odd + right, even + odd, left + even))
        gap = jnp.zeros((16, chans), F32)
        for dx in range(3):
            upper, lower = combos[0][dx], combos[1][dx]
            r.field[dx, im] = (lower + stack([upper[16:], gap])).astype(BF16)
            r.field[3 + dx, im] = (upper + lower).astype(BF16)
            r.field[6 + dx, im] = (stack([gap, lower[:-16]]) + upper).astype(BF16)

    def grad1(tap, carry):
        first = pl.multiple_of(256 * tap, 256)
        r.dw1[pl.ds(first, 256), :] = nn(
            r.h1cm[...], stack([r.field[tap, im] for im in range(per)])
        )
        return carry

    lax.fori_loop(0, 9, grad1, 0)
    entry.begin()
    second.first()

    parts = [stack([r.field[tap, im] for im in range(per)]) for tap in range(9)]
    dh1 = nn(jnp.concatenate(parts, axis=1), r.w1t[...])
    payload = jnp.zeros((32, chans), F32)
    for im in range(per):
        span = slice(256 * im, 256 * im + 256)
        normal = (r.fpm[span, :].astype(F32) - mean1_b[im]) * inv1_b[im]
        pre = gamma_b[im] * normal + beta_b[im]
        sig = sigmoid(pre)
        act = dh1[span] * (sig * (1.0 + pre * (1.0 - sig)))
        r.act1[span, :] = act
        q1, q2 = colsum(act), colsum(act * normal)
        payload = payload + place_row(q2, label[im], 32)
        payload = payload + place_row(q1, label[im] + classes, 32)
        payload = payload + place_row(gamma_b[im] * q1, group[im] + 24, 32)
        payload = payload + place_row(gamma_b[im] * q2, group[im] + 28, 32)
    last_sums = AllReduce(4)
    last_sums.begin(payload)
    entry.first()
    last_sums.middle()
    second.end(r.grad2, r.grad3)

    stats = last_sums.end()
    for im in range(per):
        span = slice(256 * im, 256 * im + 256)
        normal = (r.fpm[span, :].astype(F32) - mean1_b[im]) * inv1_b[im]
        r1 = pick_row(stats[24:28], group[im]) / count
        r2 = pick_row(stats[28:32], group[im]) / count
        grad = inv1_b[im] * (gamma_b[im] * r.act1[span, :] - (r1 + normal * r2))
        grad = (grad + r.dshort[span, :]).astype(BF16)
        r.dcm[im] = nt(r.ident[...], grad).astype(BF16)
    out_waits += give_back(r.dcm, r.dx)

    table = jnp.zeros((24, chans), F32)
    table = table + jnp.where(iota((24, chans), 0) < 2 * classes, stats[0:24], 0.0)
    table = table + place_row(colsum(affine_grad2[4:8]), 2 * classes, 24)
    table = table + place_row(colsum(affine_grad2[0:4]), 2 * classes + 1, 24)
    table = table + place_row(affine_grad2[8:9], 2 * classes + 2, 24)
    mine = jnp.zeros((24, 128), F32)
    for c in range(n_ch):
        piece = table[:, 128 * (c // 2) : 128 * (c // 2) + 128]
        if c % 2:
            piece = pltpu.roll(piece, local, axis=1)
        mine = mine + jnp.where(me == c, piece, 0.0)
    r.affine_grad[...] = mine

    if inner == 1:
        row = iota((8, 128), 0)

        def norm_rows(index, weight, grad, v):
            for wait in held[index]:
                wait()
            master = weight[...]
            _, _, direction = adam_update(
                grad[...], getattr(r, v + "m")[...], getattr(r, v + "q")[...]
            )
            update = direction + WEIGHT_DECAY * master
            rows_w = jnp.where(row == index, total(master * master), 0.0)
            return rows_w + jnp.where(row == index + 3, total(update * update), 0.0)

        norms = norm_rows(1, r.exit_v, r.grad2, "v2") + norm_rows(2, r.bypass_v, r.grad3, "vs")
        entry.end(r.grad1)
        norms = norms + norm_rows(0, r.entry_v, r.grad1, "v1")
        r.every[block, me] = norms
        waits = [
            post(r.every.at[block, me], r.every.at[block, me], r.every.at[b, c], dev(b, within, c))
            for b, c in all_peers
        ]
        for wait in waits:
            wait()
        norms = jnp.zeros((8, 128), F32)
        for b in range(OUTER):
            norms = norms + ordered_sum(r.every.at[b], n_ch)
        r.norms[...] = norms
    else:
        entry.end(r.grad1)
        r.norms[...] = jnp.zeros((8, 128), F32)

    for wait in out_waits + pending:
        wait()
    cfg.used.append((slots.remote, slots.local))


def final_kernel(cfg, *refs):
    r = SimpleNamespace(**dict(zip(cfg.names, refs)))
    classes = cfg.classes
    local = cfg.local
    move = pltpu.make_async_copy(r.out, r.block_output, r.sem)
    move.start()
    r.input_gradient[...] = r.dx[...].astype(F32)
    norms = jnp.sqrt(r.norms[...])
    weight_norm, update_norm = norms[0:3, 0:1], norms[3:6, 0:1]
    ratio = weight_norm / update_norm
    at = iota((3, 3), 1)
    r.trust_norms[...] = jnp.where(
        at == 0, weight_norm, jnp.where(at == 1, update_norm, ratio)
    )
    sets = (
        (r.entry, r.entry_m, r.entry_q, r.entry_g, r.entry_1, r.entry_2, r.entry_w),
        (r.exit, r.exit_m, r.exit_q, r.exit_g, r.exit_1, r.exit_2, r.exit_w),
        (r.bypass, r.bypass_m, r.bypass_q, r.bypass_g, r.bypass_1, r.bypass_2, r.bypass_w),
    )
    for index, (weight, m, q, g, first, second, result) in enumerate(sets):
        master = weight[...]
        moment, square, direction = adam_update(g[...], m[...], q[...])
        update = direction + WEIGHT_DECAY * master
        first[...] = moment
        second[...] = square
        result[...] = master - MATRIX_RATE * ratio[index : index + 1] * update
    grad = r.affine_grad[0 : 2 * classes + 3, 0:local]
    moment, square, direction = adam_update(grad, r.affine_m[...], r.affine_q[...])
    r.affine_1[...] = moment
    r.affine_2[...] = square
    r.affine_w[...] = r.affine[...] - AFFINE_RATE * direction
    move.wait()


def per_device(
    features,
    labels,
    groups,
    widths,
    entry_conv,
    entry_moment,
    entry_square,
    exit_conv,
    exit_moment,
    exit_square,
    bypass_conv,
    bypass_moment,
    bypass_square,
    norm_affine,
    norm_moment,
    norm_square,
    cotangent,
):
    n_img, n_ch = lax.axis_size("img"), lax.axis_size("ch")
    batch, local, pixels = features.shape
    chans = local * n_ch
    side = math.isqrt(pixels)
    inner = n_img // OUTER
    classes = (norm_affine.shape[0] - 3) // 2
    per = batch // n_ch
    assert (side, chans, n_ch, local, batch % n_ch) == (16, 256, 4, 64, 0)
    rows, small = entry_conv.shape[0] * inner, bypass_conv.shape[0] * inner
    masters = (entry_conv, exit_conv, bypass_conv)
    if inner == 1:
        blocks = masters
    else:
        sets = [[o * inner + i for i in range(inner)] for o in range(OUTER)]
        blocks = tuple(
            lax.all_gather(w.astype(BF16), "img", axis=0, tiled=True, axis_index_groups=sets)
            for w in masters
        )

    vmem = pl.BlockSpec(memory_space=pltpu.VMEM)
    smem = pl.BlockSpec(memory_space=pltpu.SMEM)
    anywhere = pl.BlockSpec(memory_space=pl.ANY)
    states = dict(
        entry_m=entry_moment.T,
        entry_q=entry_square.T,
        exit_m=exit_moment.T,
        exit_q=exit_square.T,
        bypass_m=bypass_moment,
        bypass_q=bypass_square,
    )
    inputs = dict(
        labels=(labels, smem),
        groups=(groups, smem),
        widths=(widths, smem),
        features=(features, anywhere),
        cotangent=(cotangent, anywhere),
        entry=(blocks[0].T, anywhere),
        exit=(blocks[1].T, anywhere),
        bypass=(blocks[2], anywhere),
        affine=(norm_affine, anywhere),
    )
    if inner == 1:
        inputs.update({name: (value, anywhere) for name, value in states.items()})
    sds = jax.ShapeDtypeStruct
    outputs = dict(
        out=(sds(cotangent.shape, BF16), anywhere),
        dx=(sds(features.shape, BF16), anywhere),
        grad1=(sds((local, rows), F32), vmem),
        grad2=(sds((local, rows), F32), vmem),
        grad3=(sds((small, local), F32), vmem),
        affine_grad=(sds((24, 128), F32), vmem),
        norms=(sds((8, 128), F32), vmem),
    )
    pix = pixels * per
    taps9 = 9 * chans
    held = lambda shape, dtype=BF16: pltpu.VMEM(shape, dtype)
    scratch = dict(
        fown=held((batch, local, pixels)),
        fbuf=held((n_ch, per, local, pixels)),
        cbuf=held((n_ch, per, local, 4 * pixels)),
        entry_v=held((local, rows), blocks[0].dtype),
        exit_v=held((local, rows), blocks[1].dtype),
        bypass_v=held((small, local), blocks[2].dtype),
        affine_v=held(norm_affine.shape, F32),
        padded=held((3 * local, 384)),
        wz1=held((n_ch, rows // 2, 128)),
        wz2=held((n_ch, (rows + small) // 2, 128)),
        aff_z=held((n_ch, 24, 128), F32),
        w1=held((taps9, chans)),
        w2=held((taps9, chans)),
        ws=held((chans, chans)),
        w1t=held((taps9, chans)),
        w2t=held((taps9, chans)),
        unpack=held((512, 512)),
        ident=held((256, 256)),
        shift=held((2, 256, 256)),
        gridder=held((512, 256)),
        flatter=held((512, 512)),
        fpm=held((pix, chans)),
        h1s=held((3, per, pixels + 32, chans)),
        h1cm=held((chans, pix)),
        y1=held((4, pix, chans), F32),
        act=held((4, pix, chans), F32),
        h2s=held((2, 4, per, pixels + 32, chans)),
        dzs=held((2, 4, per, pixels + 32, chans)),
        h2cm=held((chans, 4 * pix)),
        short=held((pix, chans), F32),
        dshort=held((pix, chans), F32),
        dzc=held((pix, chans)),
        act1=held((pix, chans), F32),
        rc=held((per, chans, 4 * pixels)),
        ocm=held((per, chans, 4 * pixels)),
        dcm=held((per, chans, pixels)),
        field=held((9, per, pixels, chans)),
        dw1=held((taps9, chans), F32),
        dw2=held((taps9, chans), F32),
        dws=held((chans, chans), F32),
    )
    for number, size in ((1, rows), (2, rows + small)):
        shapes = ((4, size, chans),) * 2 + ((4, n_ch, size // 2, 128),) * 2
        for part, shape in zip(PARTS, shapes):
            scratch[part + str(number)] = held(shape)
    exchanges = [(8, 128), (8, chans), (16, chans), (32, chans)]
    if inner == 1:
        scratch.update(every=held((OUTER, n_ch, 8, 128), F32))
        for v, shape in (("v1", (local, rows)), ("v2", (local, rows)), ("vs", (small, local))):
            scratch[v + "m"] = held(shape, F32)
            scratch[v + "q"] = held(shape, F32)
    for number, shape in enumerate(exchanges, 1):
        for axis, size in zip("abc", (OUTER, inner, n_ch)):
            if size > 1:
                scratch[axis + str(number)] = held((size,) + shape, F32)
    remote_count = 7 * 3 + 3 * 7 + 2 * 16 + len(exchanges) * (7 + 3 + inner - 1)
    remote_count += 31 if inner == 1 else 0
    scratch.update(
        send=pltpu.SemaphoreType.DMA((remote_count,)),
        recv=pltpu.SemaphoreType.DMA((remote_count,)),
        lsem=pltpu.SemaphoreType.DMA((20,)),
    )
    cfg = SimpleNamespace(
        names=[*inputs, *outputs, *scratch],
        inner=inner,
        n_ch=n_ch,
        batch=batch,
        local=local,
        classes=classes,
        count=float(batch * n_img // widths.shape[0] * pixels),
        rows=rows,
        small=small,
        used=[],
    )
    out, dx, grad1, grad2, grad3, affine_grad, norms = pl.pallas_call(
        functools.partial(main_kernel, cfg),
        out_shape=[s for s, _ in outputs.values()],
        in_specs=[s for _, s in inputs.values()],
        out_specs=[s for _, s in outputs.values()],
        scratch_shapes=list(scratch.values()),
        compiler_params=pltpu.CompilerParams(
            collective_id=0, has_side_effects=True, vmem_limit_bytes=VMEM_LIMIT
        ),
        name="block_step",
    )(*[v for v, _ in inputs.values()])
    assert max(n for n, _ in cfg.used) <= remote_count and max(n for _, n in cfg.used) <= 20

    grads = [grad1, grad2, grad3]
    if inner > 1:
        grads = [
            lax.psum_scatter(g, "img", scatter_dimension=0, axis_index_groups=sets, tiled=True)
            for g in (grad1.T, grad2.T, grad3)
        ]
        updates = []
        for w, g, m, s in zip(
            masters,
            grads,
            (entry_moment, exit_moment, bypass_moment),
            (entry_square, exit_square, bypass_square),
        ):
            updates.append(adam_update(g, m, s)[2] + WEIGHT_DECAY * w)
        sums = lax.psum(
            jnp.stack([jnp.sum(w * w) for w in masters] + [jnp.sum(u * u) for u in updates]),
            ("img", "ch"),
        )
        norms = jnp.broadcast_to(jnp.pad(sums, (0, 2))[:, None], (8, 128))
        grads = [grads[0].T, grads[1].T, grads[2]]

    args = dict(
        out=out,
        dx=dx,
        norms=norms,
        affine_grad=affine_grad,
        entry_g=grads[0],
        exit_g=grads[1],
        bypass_g=grads[2],
        entry=entry_conv.T,
        exit=exit_conv.T,
        bypass=bypass_conv,
        **states,
        affine=norm_affine,
        affine_m=norm_moment,
        affine_q=norm_square,
    )
    tall = sds(entry_conv.shape[::-1], F32)
    short, wide = (sds(w.shape, F32) for w in (bypass_conv, norm_affine))
    results = dict(
        block_output=sds(cotangent.shape, BF16),
        input_gradient=sds(features.shape, F32),
        entry_1=tall,
        entry_2=tall,
        entry_w=tall,
        exit_1=tall,
        exit_2=tall,
        exit_w=tall,
        bypass_1=short,
        bypass_2=short,
        bypass_w=short,
        affine_1=wide,
        affine_2=wide,
        affine_w=wide,
        trust_norms=sds((3, 3), F32),
    )
    end_cfg = SimpleNamespace(names=[*args, *results], classes=classes, local=local)
    end_cfg.names.append("sem")
    final = pl.pallas_call(
        functools.partial(final_kernel, end_cfg),
        out_shape=list(results.values()),
        in_specs=[anywhere] + [vmem] * (len(args) - 1),
        out_specs=[anywhere] + [vmem] * (len(results) - 1),
        scratch_shapes=[pltpu.SemaphoreType.DMA],
        compiler_params=pltpu.CompilerParams(vmem_limit_bytes=VMEM_LIMIT),
        name="finish",
    )(*args.values())
    return tuple(v.T if s is tall else v for v, s in zip(final, results.values()))


def solution(mesh):
    wide = P("img", "ch")
    deep = P("img", "ch", None)
    table = P(None, "ch")
    return jax.shard_map(
        per_device,
        mesh=mesh,
        in_specs=(deep, P("img"), P("img"), P()) + (wide,) * 9 + (table,) * 3 + (deep,),
        out_specs=(deep, deep) + (wide,) * 9 + (table,) * 3 + (P(),),
        check_vma=False,
    )
```

```python
import functools
import math
from types import SimpleNamespace

import jax
import jax.numpy as jnp
from jax import lax
from jax.experimental import pallas as pl
from jax.experimental.pallas import tpu as pltpu
from jax.sharding import PartitionSpec as P

LEVELS = 4
STEP = 5
NORM_EPSILON = 1e-05
ADAM_EPSILON = 1e-06
MOMENT_DECAY = 0.9
SQUARE_DECAY = 0.999
WEIGHT_DECAY = 0.01
MATRIX_RATE = 0.3
AFFINE_RATE = 0.2

OUTER = 8
VMEM_LIMIT = 56 * 1024 * 1024
BF16 = jnp.bfloat16
F32 = jnp.float32
MESH = pl.DeviceIdType.MESH
PARTS = ("s1", "r1", "s2", "r2")


def nn(left, right):
    return lax.dot_general(left, right, (((1,), (0,)), ((), ())), preferred_element_type=F32)


def nt(left, right):
    return lax.dot_general(left, right, (((1,), (1,)), ((), ())), preferred_element_type=F32)


def flip(index, mask):
    result = index
    for bit in range(3):
        if (mask >> bit) & 1:
            digit = lax.rem(lax.div(index, 1 << bit), 2)
            result = result + (1 - 2 * digit) * (1 << bit)
    return result


def sigmoid(value):
    return 0.5 * jnp.tanh(0.5 * value) + 0.5


def iota(shape, axis):
    return lax.broadcasted_iota(jnp.int32, shape, axis)


def to_bf16(condition):
    return jnp.where(condition, 1.0, 0.0).astype(BF16)


def pick_row(table, index):
    hit = iota(table.shape, 0) == index
    return jnp.sum(jnp.where(hit, table, 0.0), axis=0, keepdims=True)


def place_row(row, index, rows):
    hit = iota((rows, row.shape[1]), 0) == index
    return jnp.where(hit, row, 0.0)


def colsum(value):
    return jnp.sum(value, axis=0, keepdims=True)


def adam_update(grad, moment, square):
    moment_new = MOMENT_DECAY * moment + (1.0 - MOMENT_DECAY) * grad
    square_new = SQUARE_DECAY * square + (1.0 - SQUARE_DECAY) * grad * grad
    direction = (
        moment_new
        / (1.0 - MOMENT_DECAY**STEP)
        / (jnp.sqrt(square_new / (1.0 - SQUARE_DECAY**STEP)) + ADAM_EPSILON)
    )
    return (moment_new, square_new, direction)


def total(value):
    return jnp.sum(jnp.sum(value, axis=1, keepdims=True), axis=0, keepdims=True)


def main_kernel(cfg, *refs):
    r = SimpleNamespace(**dict(zip(cfg.names, refs)))
    inner, n_ch, batch, local = cfg.inner, cfg.n_ch, cfg.batch, cfg.local
    classes, count = cfg.classes, cfg.count
    per = batch // n_ch
    chans = local * n_ch
    rows, small = cfg.rows, cfg.small
    tail = (rows - 256) // 2
    hw, hs = rows // 2, small // 2
    slots = SimpleNamespace(remote=0, local=0)

    img = lax.axis_index("img")
    me = lax.axis_index("ch")
    block = lax.div(img, inner)
    within = lax.rem(img, inner)
    core = lax.rem(block, 2)
    plane = lax.div(block, 2)
    partner = flip(block, 1)

    def dev(block_id, within_id, ch_id):
        return (block_id * inner + within_id, ch_id)

    pending = []

    def post(src, dst, landed, peer):
        slot = slots.remote
        slots.remote = slot + 1
        copy = pltpu.make_async_remote_copy(
            src_ref=src,
            dst_ref=dst,
            send_sem=r.send.at[slot],
            recv_sem=r.recv.at[slot],
            device_id=peer,
            device_id_type=MESH,
        )
        copy.start()
        pending.append(copy.wait_send)
        arrival = pltpu.make_async_remote_copy(
            src_ref=landed,
            dst_ref=landed,
            send_sem=r.send.at[slot],
            recv_sem=r.recv.at[slot],
            device_id=peer,
            device_id_type=MESH,
        )
        return arrival.wait_recv

    def here(src, dst):
        slot = slots.local
        slots.local = slot + 1
        copy = pltpu.make_async_copy(src, dst, r.lsem.at[slot])
        copy.start()
        return copy.wait

    outer_peers = [flip(block, mask) for mask in range(1, OUTER)]
    ch_peers = [flip(me, mask) for mask in range(1, n_ch)]
    inner_pairs = [
        (lax.rem(within + step, inner), lax.rem(within + inner - step, inner))
        for step in range(1, inner)
    ]
    all_peers = [
        (flip(block, mask), flip(me, turn))
        for mask in range(OUTER)
        for turn in range(n_ch)
        if mask or turn
    ]

    barrier = pltpu.get_barrier_semaphore()
    everyone = [dev(b, within, c) for b, c in all_peers]
    everyone += [dev(block, peer, me) for peer, _ in inner_pairs]
    for peer in everyone:
        pl.semaphore_signal(barrier, inc=1, device_id=peer, device_id_type=MESH)

    got_entry = here(r.entry, r.entry_v)
    got_features = here(r.features, r.fown)
    got_exit = here(r.exit, r.exit_v)
    got_bypass = here(r.bypass, r.bypass_v)
    got_affine = here(r.affine, r.affine_v)
    got_cot = here(r.cotangent, r.cown)
    states = ((r.entry_m, r.entry_q), (r.exit_m, r.exit_q), (r.bypass_m, r.bypass_q)) if inner == 1 else ()
    held = [
        (here(m, getattr(r, v + "m")), here(q, getattr(r, v + "q")))
        for (m, q), v in zip(states, ("v1", "v2", "vs"))
    ]

    s_row, s_col = iota((hw, 384), 0), iota((hw, 384), 1)
    pick_first = to_bf16(s_col == jnp.where(s_row < 128, s_row, s_row + 128))
    pick_second = to_bf16(s_col == jnp.where(s_row < 128, s_row + 128, s_row + 128 + tail))
    r.padded[...] = jnp.zeros(r.padded.shape, BF16)

    def pack_own(value):
        r.padded[local : 2 * local, 0:rows] = value.astype(BF16)
        packed = nt(pick_first, r.padded[local : 3 * local, :])
        return (packed + nt(pick_second, r.padded[0 : 2 * local, :])).astype(BF16)

    got_entry()
    r.wz1[me] = pack_own(r.entry_v[...])
    pl.semaphore_wait(barrier, len(everyone))

    def to_channels(buffer):
        return [
            post(buffer.at[me], buffer.at[me], buffer.at[peer], dev(block, within, peer))
            for peer in ch_peers
        ]

    entry_waits = to_channels(r.wz1)
    got_features()
    feature_waits = [
        post(
            r.fown.at[pl.ds(per * peer, per)],
            r.fbuf.at[me],
            r.fbuf.at[peer],
            dev(block, within, peer),
        )
        for peer in ch_peers
    ]
    got_affine()
    r.aff_z[me] = jnp.zeros((24, 128), F32)
    r.aff_z[me, 0 : 2 * classes + 3, 0:local] = r.affine_v[...]
    affine_waits = to_channels(r.aff_z)

    lane = iota((512, 512), 0)
    column = iota((512, 512), 1)
    spot = 256 * ((lane >> 6) & 1) + 64 * (lane >> 7) + (lane & 63)
    r.unpack[...] = to_bf16(column == spot)

    r.fbuf[me] = r.fown[pl.ds(per * me, per)]
    flat = jnp.concatenate([r.fown[b] for b in range(batch)], axis=1)
    wide = flat.astype(F32)
    square = wide * wide
    square_hi = square.astype(BF16)
    square_lo = (square - square_hi.astype(F32)).astype(BF16)
    level = iota((16, 256), 0)
    first_mask = jnp.concatenate([to_bf16(level == r.groups[b]) for b in range(batch)], axis=1)
    second_mask = jnp.concatenate([to_bf16(level == r.groups[b] + 4) for b in range(batch)], axis=1)
    sums = nt(first_mask, flat) + nt(second_mask, square_hi) + nt(second_mask, square_lo)

    def ordered_sum(ref, size):
        result = ref[0]
        for slot in range(1, size):
            result = result + ref[slot]
        return result

    class AllReduce:
        def __init__(self, number):
            self.over_outer, self.over_inner, self.over_ch = (
                getattr(r, axis + str(number), None) for axis in "abc"
            )

        def begin(self, value, masked=None):
            ref = self.over_outer
            if masked is None:
                ref[block] = value
            else:
                ref[block] = jnp.zeros(ref.shape[1:], F32)
                ref[block, :, 0:masked] = value
            self.waits = [
                post(ref.at[block], ref.at[block], ref.at[peer], dev(peer, within, me))
                for peer in outer_peers
            ]

        def middle(self):
            for wait in self.waits:
                wait()
            value = ordered_sum(self.over_outer, OUTER)
            if inner > 1:
                ref = self.over_inner
                ref[within] = value
                waits = [
                    post(ref.at[within], ref.at[within], ref.at[back], dev(block, peer, me))
                    for peer, back in inner_pairs
                ]
                for wait in waits:
                    wait()
                value = ordered_sum(ref, inner)
            self.over_ch[me] = value
            self.waits = to_channels(self.over_ch)

        def finish(self):
            for wait in self.waits:
                wait()
            return self.over_ch

        def end(self):
            return ordered_sum(self.finish(), n_ch)

    input_sums = AllReduce(1)
    input_sums.begin(sums[0:8], masked=local)

    got_exit()
    got_bypass()
    r.wz2[me, 0:hw, :] = pack_own(r.exit_v[...])
    e_row, e_col = iota((local, 128), 0), iota((local, 128), 1)
    value = r.bypass_v[...].astype(BF16)
    r.wz2[me, hw : hw + hs, :] = (
        nn(value[:hs], to_bf16(e_col == e_row)) + nn(value[hs:], to_bf16(e_col == e_row + local))
    ).astype(BF16)

    def rows_of(ref, index):
        size = ref.shape[0] // OUTER
        return ref.at[pl.ds(pl.multiple_of(size * index, 16), size)]

    def unpack_own(ref, full):
        own = rows_of(ref, block)
        if full.shape[0] == hw:
            own[0:128, :] = full[0:128, 0:256]
            own[128:256, :] = full[0:128, 256:512]
            own[256 : 256 + tail, :] = full[128:, 0:256]
            own[256 + tail :, :] = full[128:, 256:512]
        else:
            own[0:hs, :] = full[:, 0:256]
            own[hs:, :] = full[:, 256:512]

    def spread(ref):
        own = rows_of(ref, block)
        return {
            mask: post(own, own, rows_of(ref, flip(block, mask)), dev(flip(block, mask), within, me))
            for mask in (2, 4, 6, 1)
        }

    def forward(ref, waits):
        rest = [waits[1]]
        for mask in (2, 4, 6):
            waits[mask]()
            mine = rows_of(ref, flip(block, mask))
            theirs = rows_of(ref, flip(partner, mask))
            rest.append(post(mine, mine, theirs, dev(partner, within, me)))
        return rest

    def widen(buffer):
        packed = jnp.concatenate([buffer[c] for c in range(n_ch)], axis=1)
        return nn(packed, r.unpack[...]).astype(BF16)

    for wait in entry_waits:
        wait()
    unpack_own(r.w1, widen(r.wz1))
    gather1 = spread(r.w1)
    exit_waits = to_channels(r.wz2)

    ident = to_bf16(iota((256, 256), 0) == iota((256, 256), 1))
    r.ident[...] = ident
    q_out, q_in = iota((256, 256), 0), iota((256, 256), 1)
    r.shift[0] = to_bf16((q_in == q_out + 1) & ((q_out & 15) < 15))
    r.shift[1] = to_bf16((q_in == q_out - 1) & ((q_out & 15) > 0))

    input_sums.middle()
    got_cot()
    cot_waits = [
        post(
            r.cown.at[pl.ds(per * peer, per)],
            r.cbuf.at[me],
            r.cbuf.at[peer],
            dev(block, within, peer),
        )
        for peer in ch_peers
    ]

    rho, px = iota((512, 256), 0), iota((512, 256), 1)
    version, a, b_ = rho >> 8, (rho >> 7) & 1, (rho >> 6) & 1
    col = (rho & 15) + version * (1 - 2 * b_)
    target = (2 * ((rho & 63) >> 4) + a) * 32 + 2 * col + b_
    r.gridder[...] = to_bf16((px == target) & (col >= 0) & (col < 16))
    target = (
        (2 * ((lane & 127) >> 4) + (lane >> 8)) * 32 + 2 * (lane & 15) + ((lane >> 7) & 1)
    )
    r.flatter[...] = to_bf16(column == target)
    zeros = jnp.zeros((16, 256), BF16)
    for im in range(per):
        for ver in range(3):
            r.h1s[ver, im, 0:16, :] = zeros
            r.h1s[ver, im, 272:288, :] = zeros
        for ver in range(2):
            for ph in range(4):
                for ref in (r.h2s, r.dzs):
                    ref[ver, ph, im, 0:16, :] = zeros
                    ref[ver, ph, im, 272:288, :] = zeros

    def channel_major(ref, im, lanes):
        return jnp.concatenate([ref[c, im, :, lanes] for c in range(n_ch)], axis=0)

    for wait in feature_waits:
        wait()
    for im in range(per):
        r.fpm[256 * im : 256 * im + 256, :] = nt(
            ident, channel_major(r.fbuf, im, slice(0, 256))
        ).astype(BF16)

    def wide_lanes(ref):
        parts = [
            ref[c] + pltpu.roll(ref[c + 1], local, axis=1) for c in range(0, n_ch, 2)
        ]
        return jnp.concatenate(parts, axis=1)

    for wait in affine_waits:
        wait()
    affine = wide_lanes(r.aff_z)
    stats = wide_lanes(input_sums.finish())
    mean1 = stats[0:4] / count
    inv1 = lax.rsqrt(stats[4:8] / count - mean1 * mean1 + NORM_EPSILON)
    gain = affine[2 * classes : 2 * classes + 1]
    shift = affine[2 * classes + 1 : 2 * classes + 2]
    out_bias = affine[2 * classes + 2 : 2 * classes + 3]
    group, label, mean1_b, inv1_b, gamma_b, beta_b, mask_b = [], [], [], [], [], [], []
    for im in range(per):
        group.append(r.groups[per * me + im])
        label.append(r.labels[per * me + im])
        mean1_b.append(pick_row(mean1, group[im]))
        inv1_b.append(pick_row(inv1, group[im]))
        gamma_b.append(pick_row(affine, label[im]))
        beta_b.append(pick_row(affine, label[im] + classes))
        width = r.widths[group[im]]
        mask_b.append(
            jnp.where(iota((1, chans), 1) < width * (chans // LEVELS), 1.0, 0.0)
        )

    for im in range(per):
        normal = (r.fpm[256 * im : 256 * im + 256, :].astype(F32) - mean1_b[im]) * inv1_b[im]
        pre = gamma_b[im] * normal + beta_b[im]
        hidden = (pre * sigmoid(pre)).astype(BF16)
        r.h1s[1, im, 16:272, :] = hidden
        r.h1s[0, im, 16:272, :] = nn(r.shift[1], hidden).astype(BF16)
        r.h1s[2, im, 16:272, :] = nn(r.shift[0], hidden).astype(BF16)
        r.h1cm[:, 256 * im : 256 * im + 256] = nt(ident, hidden).astype(BF16)

    for wait in exit_waits:
        wait()
    full = widen(r.wz2)
    unpack_own(r.w2, full[0:hw])
    unpack_own(r.ws, full[hw:])
    rest = forward(r.w1, gather1)
    gather2 = spread(r.w2)
    gather3 = spread(r.ws)
    for wait in rest:
        wait()

    def taps():
        return [(dy, dx) for dy in range(3) for dx in range(3)]

    def stack(pieces):
        return jnp.concatenate(pieces, axis=0)

    def conv1(phase, carry):
        a, c = lax.div(phase, 2), lax.rem(phase, 2)
        parts = []
        for dy, dx in taps():
            first = pl.multiple_of(16 * lax.div(a + dy + 1, 2), 16)
            ver = lax.div(c + dx + 1, 2)
            parts.append(
                stack([r.h1s[ver, im, pl.ds(first, 256), :] for im in range(per)])
            )
        y = nn(jnp.concatenate(parts, axis=1), r.w1[...])
        r.y1[phase] = y
        out = []
        for im in range(per):
            piece = y[256 * im : 256 * im + 256]
            out.append(carry[2 * im] + colsum(piece))
            out.append(carry[2 * im + 1] + colsum(piece * piece))
        return tuple(out)

    nought = jnp.zeros((1, chans), F32)
    mid = lax.fori_loop(0, 4, conv1, (nought,) * (2 * per))
    payload = jnp.zeros((8, chans), F32)
    for im in range(per):
        payload = payload + place_row(mid[2 * im], group[im], 8)
        payload = payload + place_row(mid[2 * im + 1], group[im] + 4, 8)
    mid_sums = AllReduce(2)
    mid_sums.begin(payload)

    def turn(src, dst):
        def one(tap, carry):
            first = pl.multiple_of(256 * tap, 256)
            dst[pl.ds(first, 256), :] = nt(r.ident[...], src[pl.ds(first, 256), :]).astype(BF16)
            return carry

        lax.fori_loop(0, 9, one, 0)

    turn(r.w1, r.w1t)
    rest = forward(r.w2, gather2) + forward(r.ws, gather3)
    mid_sums.middle()

    r.cbuf[me] = r.cown[pl.ds(per * me, per)]
    for wait in cot_waits:
        wait()
    for im in range(per):
        for n in range(4):
            piece = channel_major(r.cbuf, im, slice(256 * n, 256 * n + 256))
            grid = nt(r.gridder[...], piece).astype(BF16)
            for ver in range(2):
                for ph in range(4):
                    at = 256 * ver + 64 * ph
                    r.dzs[ver, ph, im, 16 + 64 * n : 80 + 64 * n, :] = grid[at : at + 64]

    coarse = jnp.zeros((256 * per, chans), F32)
    for ph in range(4):
        coarse = coarse + stack([r.dzs[0, ph, im, 16:272, :] for im in range(per)]).astype(F32)
    bias_sum = colsum(coarse)
    r.dzc[...] = coarse.astype(BF16)

    def tap_slice(ref, a, c, dy, dx, im):
        row, colm = a + dy + 1, c + dx + 1
        first = pl.multiple_of(16 * lax.div(row, 2), 16)
        ph = 2 * lax.rem(row, 2) + lax.rem(colm, 2)
        side_step = lax.div(colm, 2) - 1
        return ref[side_step * side_step, ph, im, pl.ds(first, 256), :]

    for wait in rest:
        wait()
    turn(r.w2, r.w2t)

    def back2(phase, carry):
        a, c = lax.div(phase, 2), lax.rem(phase, 2)
        parts = [
            stack([tap_slice(r.dzs, a, c, 2 - dy, 2 - dx, im) for im in range(per)])
            for dy, dx in taps()
        ]
        r.act[phase] = nn(jnp.concatenate(parts, axis=1), r.w2t[...])
        return carry

    lax.fori_loop(0, 4, back2, 0)

    stats = mid_sums.end()
    mean2 = stats[0:4] / (4.0 * count)
    inv2 = lax.rsqrt(stats[4:8] / (4.0 * count) - mean2 * mean2 + NORM_EPSILON)
    mean2_b = [pick_row(mean2, group[im]) for im in range(per)]
    inv2_b = [pick_row(inv2, group[im]) for im in range(per)]

    def hidden2(phase, carry):
        c = lax.rem(phase, 2)
        out = []
        for im in range(per):
            span = slice(256 * im, 256 * im + 256)
            normal = (r.y1[phase, span, :] - mean2_b[im]) * inv2_b[im]
            r.y1[phase, span, :] = normal
            pre = gain * normal + shift
            sig = sigmoid(pre)
            hidden = (pre * sig * mask_b[im]).astype(BF16)
            act = r.act[phase, span, :] * (sig * (1.0 + pre * (1.0 - sig)) * mask_b[im])
            r.act[phase, span, :] = act
            out.append(carry[2 * im] + colsum(act))
            out.append(carry[2 * im + 1] + colsum(act * normal))
            r.h2s[0, phase, im, 16:272, :] = hidden
            r.h2s[1, phase, im, 16:272, :] = nn(r.shift[c], hidden).astype(BF16)
            lanes = pl.ds(pl.multiple_of(512 * phase + 256 * im, 256), 256)
            r.h2cm[:, lanes] = nt(r.ident[...], hidden).astype(BF16)
        return tuple(out)

    mid = lax.fori_loop(0, 4, hidden2, (nought,) * (2 * per))
    payload = place_row(bias_sum, 8, 16)
    for im in range(per):
        payload = payload + place_row(mid[2 * im], group[im], 16)
        payload = payload + place_row(mid[2 * im + 1], group[im] + 4, 16)
    back_sums = AllReduce(3)
    back_sums.begin(payload)

    def grad2(tap, carry):
        dy, dx = lax.div(tap, 3), lax.rem(tap, 3)
        pieces = []
        for ph in range(4):
            a, c = ph // 2, ph % 2
            for im in range(per):
                pieces.append(tap_slice(r.dzs, a, c, 2 - dy, 2 - dx, im))
        first = pl.multiple_of(256 * tap, 256)
        r.dw2[pl.ds(first, 256), :] = nn(r.h2cm[...], stack(pieces))
        return carry

    lax.fori_loop(0, 9, grad2, 0)
    back_sums.middle()
    for im in range(per):
        piece = channel_major(r.fbuf, im, slice(0, 256))
        grad = nn(piece, r.dzc[256 * im : 256 * im + 256, :])
        if im == 0:
            r.dws[...] = grad
        else:
            r.dws[...] = r.dws[...] + grad

    class GradSum:
        def __init__(self, number, fetch):
            self.fetch = fetch
            for part in PARTS:
                setattr(self, part, getattr(r, part + str(number)))

        def begin(self):
            for u in range(4):
                self.s1[u] = self.fetch(2 * u + 1 - core).astype(BF16)
            self.wait = post(self.s1, self.r1, self.r1, dev(partner, within, me))

        def first(self):
            self.wait()
            for u in range(4):
                value = (self.fetch(2 * u + core) + self.r1[u].astype(F32)).astype(BF16)
                left = [value[0:128], value[256 : 256 + tail]]
                right = [value[128:256], value[256 + tail : rows]]
                if value.shape[0] > rows:
                    left.append(value[rows : rows + hs])
                    right.append(value[rows + hs :])
                pair = jnp.concatenate([stack(left), stack(right)], axis=1)
                packed = nt(pair, r.unpack[...]).astype(BF16)
                for c in range(n_ch):
                    self.s2[u, c] = packed[:, 128 * c : 128 * c + 128]
            self.r2[plane, me] = self.s2[plane, me]
            self.waits = [
                post(
                    self.s2.at[lax.div(b, 2), c],
                    self.r2.at[plane, me],
                    self.r2.at[lax.div(b, 2), c],
                    dev(b, within, c),
                )
                for b, c in [
                    (flip(block, mask), flip(me, turn))
                    for turn in range(n_ch)
                    for mask in (0, 2, 4, 6)
                    if mask or turn
                ]
            ]

        def end(self, out, out_small=None):
            for wait in self.waits:
                wait()
            done = None
            for u in range(4):
                for c in range(n_ch):
                    piece = self.r2[u, c].astype(F32)
                    done = piece if done is None else done + piece
            turned = done[0:128].T
            out[:, 0:128] = turned[0:local]
            out[:, 128:256] = turned[local:]
            gap = jnp.zeros((128 - tail, 128), F32)
            turned = stack([done[128 : 128 + tail], gap]).T
            ends = turned[0:local] + pltpu.roll(turned[local:], tail, axis=1)
            out[:, 256:rows] = ends[:, 0 : rows - 256]
            if out_small is not None:
                last = done[hw:]
                out_small[0:hs, :] = last[:, 0:local]
                out_small[hs:, :] = pltpu.roll(last, local, axis=1)[:, 0:local]

    def block_rows(ref, size, index):
        return ref[pl.ds(pl.multiple_of(size * index, 8), size), :]

    second = GradSum(2, lambda k: stack([block_rows(r.dw2, rows, k), block_rows(r.dws, small, k)]))
    entry = GradSum(1, lambda k: block_rows(r.dw1, rows, k))
    second.begin()
    r.short[...] = nn(r.fpm[...], r.ws[...]) + out_bias
    r.dshort[...] = nt(r.dzc[...], r.ws[...])

    def conv2(phase, carry):
        a, c = lax.div(phase, 2), lax.rem(phase, 2)
        parts = [
            stack([tap_slice(r.h2s, a, c, dy, dx, im) for im in range(per)]) for dy, dx in taps()
        ]
        y = (nn(jnp.concatenate(parts, axis=1), r.w2[...]) + r.short[...]).astype(BF16)
        lanes = pl.ds(pl.multiple_of(256 * phase, 256), 256)
        for im in range(per):
            r.rc[im, :, lanes] = nt(r.ident[...], y[256 * im : 256 * im + 256]).astype(BF16)
        return carry

    lax.fori_loop(0, 4, conv2, 0)
    for im in range(per):
        for half in range(2):
            piece = jnp.concatenate(
                [r.rc[im, :, 256 * ph + 128 * half : 256 * ph + 128 * half + 128] for ph in range(4)],
                axis=1,
            )
            r.ocm[im, :, 512 * half : 512 * half + 512] = nn(piece, r.flatter[...]).astype(BF16)

    def own_channels(ref, index):
        return ref.at[:, pl.ds(pl.multiple_of(local * index, local), local), :]

    def give_back(ref, out):
        waits = [here(own_channels(ref, me), out.at[pl.ds(per * me, per)])]
        return waits + [
            post(
                own_channels(ref, peer),
                out.at[pl.ds(per * me, per)],
                out.at[pl.ds(per * peer, per)],
                dev(block, within, peer),
            )
            for peer in ch_peers
        ]

    out_waits = give_back(r.ocm, r.out)

    stats = back_sums.end()
    affine_grad2 = stats
    p1_b = [pick_row(stats[0:4], group[im]) / (4.0 * count) for im in range(per)]
    p2_b = [pick_row(stats[4:8], group[im]) / (4.0 * count) for im in range(per)]

    for im in range(per):
        span = slice(256 * im, 256 * im + 256)
        scale = gain * inv2_b[im]
        combos = []
        for a in range(2):
            grads = []
            for c in range(2):
                ph = 2 * a + c
                d = scale * (r.act[ph, span, :] - (p1_b[im] + r.y1[ph, span, :] * p2_b[im]))
                grads.append(d.astype(BF16))
            right = nn(r.shift[0], grads[0])
            left = nn(r.shift[1], grads[1])
            even, odd = grads[0].astype(F32), grads[1].astype(F32)
            combos.append((odd + right, even + odd, left + even))
        gap = jnp.zeros((16, chans), F32)
        for dx in range(3):
            upper, lower = combos[0][dx], combos[1][dx]
            r.field[dx, im] = (lower + stack([upper[16:], gap])).astype(BF16)
            r.field[3 + dx, im] = (upper + lower).astype(BF16)
            r.field[6 + dx, im] = (stack([gap, lower[:-16]]) + upper).astype(BF16)

    def grad1(tap, carry):
        first = pl.multiple_of(256 * tap, 256)
        r.dw1[pl.ds(first, 256), :] = nn(
            r.h1cm[...], stack([r.field[tap, im] for im in range(per)])
        )
        return carry

    lax.fori_loop(0, 9, grad1, 0)
    entry.begin()
    second.first()

    parts = [stack([r.field[tap, im] for im in range(per)]) for tap in range(9)]
    dh1 = nn(jnp.concatenate(parts, axis=1), r.w1t[...])
    payload = jnp.zeros((32, chans), F32)
    for im in range(per):
        span = slice(256 * im, 256 * im + 256)
        normal = (r.fpm[span, :].astype(F32) - mean1_b[im]) * inv1_b[im]
        pre = gamma_b[im] * normal + beta_b[im]
        sig = sigmoid(pre)
        act = dh1[span] * (sig * (1.0 + pre * (1.0 - sig)))
        r.act1[span, :] = act
        q1, q2 = colsum(act), colsum(act * normal)
        payload = payload + place_row(q2, label[im], 32)
        payload = payload + place_row(q1, label[im] + classes, 32)
        payload = payload + place_row(gamma_b[im] * q1, group[im] + 24, 32)
        payload = payload + place_row(gamma_b[im] * q2, group[im] + 28, 32)
    last_sums = AllReduce(4)
    last_sums.begin(payload)
    entry.first()
    last_sums.middle()
    second.end(r.grad2, r.grad3)

    stats = last_sums.end()
    for im in range(per):
        span = slice(256 * im, 256 * im + 256)
        normal = (r.fpm[span, :].astype(F32) - mean1_b[im]) * inv1_b[im]
        r1 = pick_row(stats[24:28], group[im]) / count
        r2 = pick_row(stats[28:32], group[im]) / count
        grad = inv1_b[im] * (gamma_b[im] * r.act1[span, :] - (r1 + normal * r2))
        grad = (grad + r.dshort[span, :]).astype(BF16)
        r.dcm[im] = nt(r.ident[...], grad).astype(BF16)
    out_waits += give_back(r.dcm, r.dx)

    table = jnp.zeros((24, chans), F32)
    table = table + jnp.where(iota((24, chans), 0) < 2 * classes, stats[0:24], 0.0)
    table = table + place_row(colsum(affine_grad2[4:8]), 2 * classes, 24)
    table = table + place_row(colsum(affine_grad2[0:4]), 2 * classes + 1, 24)
    table = table + place_row(affine_grad2[8:9], 2 * classes + 2, 24)
    mine = jnp.zeros((24, 128), F32)
    for c in range(n_ch):
        piece = table[:, 128 * (c // 2) : 128 * (c // 2) + 128]
        if c % 2:
            piece = pltpu.roll(piece, local, axis=1)
        mine = mine + jnp.where(me == c, piece, 0.0)
    r.affine_grad[...] = mine

    if inner == 1:
        row = iota((8, 128), 0)

        def norm_rows(index, weight, grad, v):
            for wait in held[index]:
                wait()
            master = weight[...]
            _, _, direction = adam_update(
                grad[...], getattr(r, v + "m")[...], getattr(r, v + "q")[...]
            )
            update = direction + WEIGHT_DECAY * master
            rows_w = jnp.where(row == index, total(master * master), 0.0)
            return rows_w + jnp.where(row == index + 3, total(update * update), 0.0)

        norms = norm_rows(1, r.exit_v, r.grad2, "v2") + norm_rows(2, r.bypass_v, r.grad3, "vs")
        entry.end(r.grad1)
        norms = norms + norm_rows(0, r.entry_v, r.grad1, "v1")
        r.every[block, me] = norms
        waits = [
            post(r.every.at[block, me], r.every.at[block, me], r.every.at[b, c], dev(b, within, c))
            for b, c in all_peers
        ]
        for wait in waits:
            wait()
        norms = jnp.zeros((8, 128), F32)
        for b in range(OUTER):
            norms = norms + ordered_sum(r.every.at[b], n_ch)
        r.norms[...] = norms
    else:
        entry.end(r.grad1)
        r.norms[...] = jnp.zeros((8, 128), F32)

    for wait in out_waits + pending:
        wait()
    cfg.used.append((slots.remote, slots.local))


def final_kernel(cfg, *refs):
    r = SimpleNamespace(**dict(zip(cfg.names, refs)))
    classes = cfg.classes
    local = cfg.local
    r.block_output[...] = r.out[...]
    r.input_gradient[...] = r.dx[...].astype(F32)
    norms = jnp.sqrt(r.norms[...])
    weight_norm, update_norm = norms[0:3, 0:1], norms[3:6, 0:1]
    ratio = weight_norm / update_norm
    at = iota((3, 3), 1)
    r.trust_norms[...] = jnp.where(
        at == 0, weight_norm, jnp.where(at == 1, update_norm, ratio)
    )
    sets = (
        (r.entry, r.entry_m, r.entry_q, r.entry_g, r.entry_1, r.entry_2, r.entry_w),
        (r.exit, r.exit_m, r.exit_q, r.exit_g, r.exit_1, r.exit_2, r.exit_w),
        (r.bypass, r.bypass_m, r.bypass_q, r.bypass_g, r.bypass_1, r.bypass_2, r.bypass_w),
    )
    for index, (weight, m, q, g, first, second, result) in enumerate(sets):
        master = weight[...]
        moment, square, direction = adam_update(g[...], m[...], q[...])
        update = direction + WEIGHT_DECAY * master
        first[...] = moment
        second[...] = square
        result[...] = master - MATRIX_RATE * ratio[index : index + 1] * update
    grad = r.affine_grad[0 : 2 * classes + 3, 0:local]
    moment, square, direction = adam_update(grad, r.affine_m[...], r.affine_q[...])
    r.affine_1[...] = moment
    r.affine_2[...] = square
    r.affine_w[...] = r.affine[...] - AFFINE_RATE * direction


def per_device(
    features,
    labels,
    groups,
    widths,
    entry_conv,
    entry_moment,
    entry_square,
    exit_conv,
    exit_moment,
    exit_square,
    bypass_conv,
    bypass_moment,
    bypass_square,
    norm_affine,
    norm_moment,
    norm_square,
    cotangent,
):
    n_img, n_ch = lax.axis_size("img"), lax.axis_size("ch")
    batch, local, pixels = features.shape
    chans = local * n_ch
    side = math.isqrt(pixels)
    inner = n_img // OUTER
    classes = (norm_affine.shape[0] - 3) // 2
    per = batch // n_ch
    assert (side, chans, n_ch, local, batch % n_ch) == (16, 256, 4, 64, 0)
    rows, small = entry_conv.shape[0] * inner, bypass_conv.shape[0] * inner
    masters = (entry_conv, exit_conv, bypass_conv)
    if inner == 1:
        blocks = masters
    else:
        sets = [[o * inner + i for i in range(inner)] for o in range(OUTER)]
        blocks = tuple(
            lax.all_gather(w.astype(BF16), "img", axis=0, tiled=True, axis_index_groups=sets)
            for w in masters
        )

    vmem = pl.BlockSpec(memory_space=pltpu.VMEM)
    smem = pl.BlockSpec(memory_space=pltpu.SMEM)
    anywhere = pl.BlockSpec(memory_space=pl.ANY)
    states = dict(
        entry_m=entry_moment.T,
        entry_q=entry_square.T,
        exit_m=exit_moment.T,
        exit_q=exit_square.T,
        bypass_m=bypass_moment,
        bypass_q=bypass_square,
    )
    inputs = dict(
        labels=(labels, smem),
        groups=(groups, smem),
        widths=(widths, smem),
        features=(features, anywhere),
        cotangent=(cotangent, anywhere),
        entry=(blocks[0].T, anywhere),
        exit=(blocks[1].T, anywhere),
        bypass=(blocks[2], anywhere),
        affine=(norm_affine, anywhere),
    )
    if inner == 1:
        inputs.update({name: (value, anywhere) for name, value in states.items()})
    sds = jax.ShapeDtypeStruct
    outputs = dict(
        out=(sds(cotangent.shape, BF16), vmem),
        dx=(sds(features.shape, BF16), vmem),
        grad1=(sds((local, rows), F32), vmem),
        grad2=(sds((local, rows), F32), vmem),
        grad3=(sds((small, local), F32), vmem),
        affine_grad=(sds((24, 128), F32), vmem),
        norms=(sds((8, 128), F32), vmem),
    )
    pix = pixels * per
    taps9 = 9 * chans
    held = lambda shape, dtype=BF16: pltpu.VMEM(shape, dtype)
    scratch = dict(
        fown=held((batch, local, pixels)),
        cown=held((batch, local, 4 * pixels)),
        fbuf=held((n_ch, per, local, pixels)),
        cbuf=held((n_ch, per, local, 4 * pixels)),
        entry_v=held((local, rows), blocks[0].dtype),
        exit_v=held((local, rows), blocks[1].dtype),
        bypass_v=held((small, local), blocks[2].dtype),
        affine_v=held(norm_affine.shape, F32),
        padded=held((3 * local, 384)),
        wz1=held((n_ch, rows // 2, 128)),
        wz2=held((n_ch, (rows + small) // 2, 128)),
        aff_z=held((n_ch, 24, 128), F32),
        w1=held((taps9, chans)),
        w2=held((taps9, chans)),
        ws=held((chans, chans)),
        w1t=held((taps9, chans)),
        w2t=held((taps9, chans)),
        unpack=held((512, 512)),
        ident=held((256, 256)),
        shift=held((2, 256, 256)),
        gridder=held((512, 256)),
        flatter=held((512, 512)),
        fpm=held((pix, chans)),
        h1s=held((3, per, pixels + 32, chans)),
        h1cm=held((chans, pix)),
        y1=held((4, pix, chans), F32),
        act=held((4, pix, chans), F32),
        h2s=held((2, 4, per, pixels + 32, chans)),
        dzs=held((2, 4, per, pixels + 32, chans)),
        h2cm=held((chans, 4 * pix)),
        short=held((pix, chans), F32),
        dshort=held((pix, chans), F32),
        dzc=held((pix, chans)),
        act1=held((pix, chans), F32),
        rc=held((per, chans, 4 * pixels)),
        ocm=held((per, chans, 4 * pixels)),
        dcm=held((per, chans, pixels)),
        field=held((9, per, pixels, chans)),
        dw1=held((taps9, chans), F32),
        dw2=held((taps9, chans), F32),
        dws=held((chans, chans), F32),
    )
    for number, size in ((1, rows), (2, rows + small)):
        shapes = ((4, size, chans),) * 2 + ((4, n_ch, size // 2, 128),) * 2
        for part, shape in zip(PARTS, shapes):
            scratch[part + str(number)] = held(shape)
    exchanges = [(8, 128), (8, chans), (16, chans), (32, chans)]
    if inner == 1:
        scratch.update(every=held((OUTER, n_ch, 8, 128), F32))
        for v, shape in (("v1", (local, rows)), ("v2", (local, rows)), ("vs", (small, local))):
            scratch[v + "m"] = held(shape, F32)
            scratch[v + "q"] = held(shape, F32)
    for number, shape in enumerate(exchanges, 1):
        for axis, size in zip("abc", (OUTER, inner, n_ch)):
            if size > 1:
                scratch[axis + str(number)] = held((size,) + shape, F32)
    remote_count = 7 * 3 + 3 * 7 + 2 * 16 + len(exchanges) * (7 + 3 + inner - 1)
    remote_count += 31 if inner == 1 else 0
    scratch.update(
        send=pltpu.SemaphoreType.DMA((remote_count,)),
        recv=pltpu.SemaphoreType.DMA((remote_count,)),
        lsem=pltpu.SemaphoreType.DMA((20,)),
    )
    cfg = SimpleNamespace(
        names=[*inputs, *outputs, *scratch],
        inner=inner,
        n_ch=n_ch,
        batch=batch,
        local=local,
        classes=classes,
        count=float(batch * n_img // widths.shape[0] * pixels),
        rows=rows,
        small=small,
        used=[],
    )
    out, dx, grad1, grad2, grad3, affine_grad, norms = pl.pallas_call(
        functools.partial(main_kernel, cfg),
        out_shape=[s for s, _ in outputs.values()],
        in_specs=[s for _, s in inputs.values()],
        out_specs=[s for _, s in outputs.values()],
        scratch_shapes=list(scratch.values()),
        compiler_params=pltpu.CompilerParams(
            collective_id=0, has_side_effects=True, vmem_limit_bytes=VMEM_LIMIT
        ),
        name="block_step",
    )(*[v for v, _ in inputs.values()])
    assert max(n for n, _ in cfg.used) <= remote_count and max(n for _, n in cfg.used) <= 20

    grads = [grad1, grad2, grad3]
    if inner > 1:
        grads = [
            lax.psum_scatter(g, "img", scatter_dimension=0, axis_index_groups=sets, tiled=True)
            for g in (grad1.T, grad2.T, grad3)
        ]
        updates = []
        for w, g, m, s in zip(
            masters,
            grads,
            (entry_moment, exit_moment, bypass_moment),
            (entry_square, exit_square, bypass_square),
        ):
            updates.append(adam_update(g, m, s)[2] + WEIGHT_DECAY * w)
        sums = lax.psum(
            jnp.stack([jnp.sum(w * w) for w in masters] + [jnp.sum(u * u) for u in updates]),
            ("img", "ch"),
        )
        norms = jnp.broadcast_to(jnp.pad(sums, (0, 2))[:, None], (8, 128))
        grads = [grads[0].T, grads[1].T, grads[2]]

    args = dict(
        out=out,
        dx=dx,
        norms=norms,
        affine_grad=affine_grad,
        entry_g=grads[0],
        exit_g=grads[1],
        bypass_g=grads[2],
        entry=entry_conv.T,
        exit=exit_conv.T,
        bypass=bypass_conv,
        **states,
        affine=norm_affine,
        affine_m=norm_moment,
        affine_q=norm_square,
    )
    tall = sds(entry_conv.shape[::-1], F32)
    short, wide = (sds(w.shape, F32) for w in (bypass_conv, norm_affine))
    results = dict(
        block_output=sds(cotangent.shape, BF16),
        input_gradient=sds(features.shape, F32),
        entry_1=tall,
        entry_2=tall,
        entry_w=tall,
        exit_1=tall,
        exit_2=tall,
        exit_w=tall,
        bypass_1=short,
        bypass_2=short,
        bypass_w=short,
        affine_1=wide,
        affine_2=wide,
        affine_w=wide,
        trust_norms=sds((3, 3), F32),
    )
    end_cfg = SimpleNamespace(names=[*args, *results], classes=classes, local=local)
    final = pl.pallas_call(
        functools.partial(final_kernel, end_cfg),
        out_shape=list(results.values()),
        in_specs=[vmem] * len(args),
        out_specs=[vmem] * len(results),
        compiler_params=pltpu.CompilerParams(vmem_limit_bytes=VMEM_LIMIT),
        name="finish",
    )(*args.values())
    return tuple(v.T if s is tall else v for v, s in zip(final, results.values()))


def solution(mesh):
    wide = P("img", "ch")
    deep = P("img", "ch", None)
    table = P(None, "ch")
    return jax.shard_map(
        per_device,
        mesh=mesh,
        in_specs=(deep, P("img"), P("img"), P()) + (wide,) * 9 + (table,) * 3 + (deep,),
        out_specs=(deep, deep) + (wide,) * 9 + (table,) * 3 + (P(),),
        check_vma=False,
    )
```

```python
import functools
import math
from types import SimpleNamespace

import jax
import jax.numpy as jnp
from jax import lax
from jax.experimental import pallas as pl
from jax.experimental.pallas import tpu as pltpu
from jax.sharding import PartitionSpec as P

LEVELS = 4
STEP = 5
NORM_EPSILON = 1e-05
ADAM_EPSILON = 1e-06
MOMENT_DECAY = 0.9
SQUARE_DECAY = 0.999
WEIGHT_DECAY = 0.01
MATRIX_RATE = 0.3
AFFINE_RATE = 0.2

OUTER = 8
VMEM_LIMIT = 56 * 1024 * 1024
BF16 = jnp.bfloat16
F32 = jnp.float32
MESH = pl.DeviceIdType.MESH
PARTS = ("s1", "r1", "s2", "r2", "s3", "r3", "s4", "r4", "acc")


def nn(left, right):
    return lax.dot_general(left, right, (((1,), (0,)), ((), ())), preferred_element_type=F32)


def nt(left, right):
    return lax.dot_general(left, right, (((1,), (1,)), ((), ())), preferred_element_type=F32)


def flip(index, mask):
    result = index
    for bit in range(3):
        if (mask >> bit) & 1:
            digit = lax.rem(lax.div(index, 1 << bit), 2)
            result = result + (1 - 2 * digit) * (1 << bit)
    return result


def sigmoid(value):
    return 0.5 * jnp.tanh(0.5 * value) + 0.5


def iota(shape, axis):
    return lax.broadcasted_iota(jnp.int32, shape, axis)


def to_bf16(condition):
    return jnp.where(condition, 1.0, 0.0).astype(BF16)


def pick_row(table, index):
    hit = iota(table.shape, 0) == index
    return jnp.sum(jnp.where(hit, table, 0.0), axis=0, keepdims=True)


def place_row(row, index, rows):
    hit = iota((rows, row.shape[1]), 0) == index
    return jnp.where(hit, row, 0.0)


def colsum(value):
    return jnp.sum(value, axis=0, keepdims=True)


def adam_update(grad, moment, square):
    moment_new = MOMENT_DECAY * moment + (1.0 - MOMENT_DECAY) * grad
    square_new = SQUARE_DECAY * square + (1.0 - SQUARE_DECAY) * grad * grad
    direction = (
        moment_new
        / (1.0 - MOMENT_DECAY**STEP)
        / (jnp.sqrt(square_new / (1.0 - SQUARE_DECAY**STEP)) + ADAM_EPSILON)
    )
    return (moment_new, square_new, direction)


def total(value):
    return jnp.sum(jnp.sum(value, axis=1, keepdims=True), axis=0, keepdims=True)


def main_kernel(cfg, *refs):
    r = SimpleNamespace(**dict(zip(cfg.names, refs)))
    inner, n_ch, batch, local = cfg.inner, cfg.n_ch, cfg.batch, cfg.local
    classes, count = cfg.classes, cfg.count
    per = batch // n_ch
    chans = local * n_ch
    rows, small = cfg.rows, cfg.small
    tail = (rows - 256) // 2
    hw, hs = rows // 2, small // 2
    slots = SimpleNamespace(remote=0, local=0)

    img = lax.axis_index("img")
    me = lax.axis_index("ch")
    block = lax.div(img, inner)
    within = lax.rem(img, inner)
    core = lax.rem(block, 2)
    plane = lax.div(block, 2)
    bit_x, bit_y = lax.rem(plane, 2), lax.div(plane, 2)
    partner = flip(block, 1)

    def dev(block_id, within_id, ch_id):
        return (block_id * inner + within_id, ch_id)

    pending = []

    def post(src, dst, landed, peer):
        slot = slots.remote
        slots.remote = slot + 1
        copy = pltpu.make_async_remote_copy(
            src_ref=src,
            dst_ref=dst,
            send_sem=r.send.at[slot],
            recv_sem=r.recv.at[slot],
            device_id=peer,
            device_id_type=MESH,
        )
        copy.start()
        pending.append(copy.wait_send)
        arrival = pltpu.make_async_remote_copy(
            src_ref=landed,
            dst_ref=landed,
            send_sem=r.send.at[slot],
            recv_sem=r.recv.at[slot],
            device_id=peer,
            device_id_type=MESH,
        )
        return arrival.wait_recv

    def here(src, dst):
        slot = slots.local
        slots.local = slot + 1
        copy = pltpu.make_async_copy(src, dst, r.lsem.at[slot])
        copy.start()
        return copy.wait

    outer_peers = [flip(block, mask) for mask in range(1, OUTER)]
    ch_peers = [flip(me, mask) for mask in range(1, n_ch)]
    inner_pairs = [
        (lax.rem(within + step, inner), lax.rem(within + inner - step, inner))
        for step in range(1, inner)
    ]
    barrier = pltpu.get_barrier_semaphore()
    everyone = [dev(peer, within, me) for peer in outer_peers]
    everyone += [dev(block, within, peer) for peer in ch_peers]
    everyone += [dev(block, peer, me) for peer, _ in inner_pairs]
    for peer in everyone:
        pl.semaphore_signal(barrier, inc=1, device_id=peer, device_id_type=MESH)

    got_entry = here(r.entry, r.entry_v)
    got_features = here(r.features, r.fown)
    got_exit = here(r.exit, r.exit_v)
    got_bypass = here(r.bypass, r.bypass_v)
    got_affine = here(r.affine, r.affine_v)
    got_cot = here(r.cotangent, r.cown)
    states = ((r.entry_m, r.entry_q), (r.exit_m, r.exit_q), (r.bypass_m, r.bypass_q)) if inner == 1 else ()
    held = [
        (here(m, getattr(r, v + "m")), here(q, getattr(r, v + "q")))
        for (m, q), v in zip(states, ("v1", "v2", "vs"))
    ]

    s_row, s_col = iota((hw, 384), 0), iota((hw, 384), 1)
    pick_first = to_bf16(s_col == jnp.where(s_row < 128, s_row, s_row + 128))
    pick_second = to_bf16(s_col == jnp.where(s_row < 128, s_row + 128, s_row + 128 + tail))
    r.padded[...] = jnp.zeros(r.padded.shape, BF16)

    def pack_own(value):
        r.padded[local : 2 * local, 0:rows] = value.astype(BF16)
        packed = nt(pick_first, r.padded[local : 3 * local, :])
        return (packed + nt(pick_second, r.padded[0 : 2 * local, :])).astype(BF16)

    got_entry()
    r.wz1[me] = pack_own(r.entry_v[...])
    pl.semaphore_wait(barrier, len(everyone))

    def to_channels(buffer):
        return [
            post(buffer.at[me], buffer.at[me], buffer.at[peer], dev(block, within, peer))
            for peer in ch_peers
        ]

    entry_waits = to_channels(r.wz1)
    got_features()
    feature_waits = [
        post(
            r.fown.at[pl.ds(per * peer, per)],
            r.fbuf.at[me],
            r.fbuf.at[peer],
            dev(block, within, peer),
        )
        for peer in ch_peers
    ]
    got_affine()
    r.aff_z[me] = jnp.zeros((24, 128), F32)
    r.aff_z[me, 0 : 2 * classes + 3, 0:local] = r.affine_v[...]
    affine_waits = to_channels(r.aff_z)

    lane = iota((512, 512), 0)
    column = iota((512, 512), 1)
    spot = 256 * ((lane >> 6) & 1) + 64 * (lane >> 7) + (lane & 63)
    r.unpack[...] = to_bf16(column == spot)

    r.fbuf[me] = r.fown[pl.ds(per * me, per)]
    flat = jnp.concatenate([r.fown[b] for b in range(batch)], axis=1)
    wide = flat.astype(F32)
    square = wide * wide
    square_hi = square.astype(BF16)
    square_lo = (square - square_hi.astype(F32)).astype(BF16)
    level = iota((16, 256), 0)
    first_mask = jnp.concatenate([to_bf16(level == r.groups[b]) for b in range(batch)], axis=1)
    second_mask = jnp.concatenate([to_bf16(level == r.groups[b] + 4) for b in range(batch)], axis=1)
    sums = nt(first_mask, flat) + nt(second_mask, square_hi) + nt(second_mask, square_lo)

    def ordered_sum(ref, size):
        result = ref[0]
        for slot in range(1, size):
            result = result + ref[slot]
        return result

    class AllReduce:
        def __init__(self, number):
            self.over_outer, self.over_inner, self.over_ch = (
                getattr(r, axis + str(number), None) for axis in "abc"
            )

        def begin(self, value, masked=None):
            ref = self.over_outer
            if masked is None:
                ref[block] = value
            else:
                ref[block] = jnp.zeros(ref.shape[1:], F32)
                ref[block, :, 0:masked] = value
            self.waits = [
                post(ref.at[block], ref.at[block], ref.at[peer], dev(peer, within, me))
                for peer in outer_peers
            ]

        def middle(self):
            for wait in self.waits:
                wait()
            value = ordered_sum(self.over_outer, OUTER)
            if inner > 1:
                ref = self.over_inner
                ref[within] = value
                waits = [
                    post(ref.at[within], ref.at[within], ref.at[back], dev(block, peer, me))
                    for peer, back in inner_pairs
                ]
                for wait in waits:
                    wait()
                value = ordered_sum(ref, inner)
            self.over_ch[me] = value
            self.waits = to_channels(self.over_ch)

        def finish(self):
            for wait in self.waits:
                wait()
            return self.over_ch

        def end(self):
            return ordered_sum(self.finish(), n_ch)

    input_sums = AllReduce(1)
    input_sums.begin(sums[0:8], masked=local)

    got_exit()
    got_bypass()
    r.wz2[me, 0:hw, :] = pack_own(r.exit_v[...])
    e_row, e_col = iota((local, 128), 0), iota((local, 128), 1)
    value = r.bypass_v[...].astype(BF16)
    r.wz2[me, hw : hw + hs, :] = (
        nn(value[:hs], to_bf16(e_col == e_row)) + nn(value[hs:], to_bf16(e_col == e_row + local))
    ).astype(BF16)

    def rows_of(ref, index):
        size = ref.shape[0] // OUTER
        return ref.at[pl.ds(pl.multiple_of(size * index, 16), size)]

    def unpack_own(ref, full):
        own = rows_of(ref, block)
        if full.shape[0] == hw:
            own[0:128, :] = full[0:128, 0:256]
            own[128:256, :] = full[0:128, 256:512]
            own[256 : 256 + tail, :] = full[128:, 0:256]
            own[256 + tail :, :] = full[128:, 256:512]
        else:
            own[0:hs, :] = full[:, 0:256]
            own[hs:, :] = full[:, 256:512]

    def spread(ref):
        own = rows_of(ref, block)
        return {
            mask: post(own, own, rows_of(ref, flip(block, mask)), dev(flip(block, mask), within, me))
            for mask in (2, 4, 6, 1)
        }

    def forward(ref, waits):
        rest = [waits[1]]
        for mask in (2, 4, 6):
            waits[mask]()
            mine = rows_of(ref, flip(block, mask))
            theirs = rows_of(ref, flip(partner, mask))
            rest.append(post(mine, mine, theirs, dev(partner, within, me)))
        return rest

    def widen(buffer):
        packed = jnp.concatenate([buffer[c] for c in range(n_ch)], axis=1)
        return nn(packed, r.unpack[...]).astype(BF16)

    for wait in entry_waits:
        wait()
    unpack_own(r.w1, widen(r.wz1))
    gather1 = spread(r.w1)
    exit_waits = to_channels(r.wz2)

    ident = to_bf16(iota((256, 256), 0) == iota((256, 256), 1))
    r.ident[...] = ident
    q_out, q_in = iota((256, 256), 0), iota((256, 256), 1)
    r.shift[0] = to_bf16((q_in == q_out + 1) & ((q_out & 15) < 15))
    r.shift[1] = to_bf16((q_in == q_out - 1) & ((q_out & 15) > 0))

    input_sums.middle()
    got_cot()
    cot_waits = [
        post(
            r.cown.at[pl.ds(per * peer, per)],
            r.cbuf.at[me],
            r.cbuf.at[peer],
            dev(block, within, peer),
        )
        for peer in ch_peers
    ]

    rho, px = iota((512, 256), 0), iota((512, 256), 1)
    version, a, b_ = rho >> 8, (rho >> 7) & 1, (rho >> 6) & 1
    col = (rho & 15) + version * (1 - 2 * b_)
    target = (2 * ((rho & 63) >> 4) + a) * 32 + 2 * col + b_
    r.gridder[...] = to_bf16((px == target) & (col >= 0) & (col < 16))
    target = (
        (2 * ((lane & 127) >> 4) + (lane >> 8)) * 32 + 2 * (lane & 15) + ((lane >> 7) & 1)
    )
    r.flatter[...] = to_bf16(column == target)
    zeros = jnp.zeros((16, 256), BF16)
    for im in range(per):
        for ver in range(3):
            r.h1s[ver, im, 0:16, :] = zeros
            r.h1s[ver, im, 272:288, :] = zeros
        for ver in range(2):
            for ph in range(4):
                for ref in (r.h2s, r.dzs):
                    ref[ver, ph, im, 0:16, :] = zeros
                    ref[ver, ph, im, 272:288, :] = zeros

    def channel_major(ref, im, lanes):
        return jnp.concatenate([ref[c, im, :, lanes] for c in range(n_ch)], axis=0)

    for wait in feature_waits:
        wait()
    for im in range(per):
        r.fpm[256 * im : 256 * im + 256, :] = nt(
            ident, channel_major(r.fbuf, im, slice(0, 256))
        ).astype(BF16)

    def wide_lanes(ref):
        parts = [
            ref[c] + pltpu.roll(ref[c + 1], local, axis=1) for c in range(0, n_ch, 2)
        ]
        return jnp.concatenate(parts, axis=1)

    for wait in affine_waits:
        wait()
    affine = wide_lanes(r.aff_z)
    stats = wide_lanes(input_sums.finish())
    mean1 = stats[0:4] / count
    inv1 = lax.rsqrt(stats[4:8] / count - mean1 * mean1 + NORM_EPSILON)
    gain = affine[2 * classes : 2 * classes + 1]
    shift = affine[2 * classes + 1 : 2 * classes + 2]
    out_bias = affine[2 * classes + 2 : 2 * classes + 3]
    group, label, mean1_b, inv1_b, gamma_b, beta_b, mask_b = [], [], [], [], [], [], []
    for im in range(per):
        group.append(r.groups[per * me + im])
        label.append(r.labels[per * me + im])
        mean1_b.append(pick_row(mean1, group[im]))
        inv1_b.append(pick_row(inv1, group[im]))
        gamma_b.append(pick_row(affine, label[im]))
        beta_b.append(pick_row(affine, label[im] + classes))
        width = r.widths[group[im]]
        mask_b.append(
            jnp.where(iota((1, chans), 1) < width * (chans // LEVELS), 1.0, 0.0)
        )

    for im in range(per):
        normal = (r.fpm[256 * im : 256 * im + 256, :].astype(F32) - mean1_b[im]) * inv1_b[im]
        pre = gamma_b[im] * normal + beta_b[im]
        hidden = (pre * sigmoid(pre)).astype(BF16)
        r.h1s[1, im, 16:272, :] = hidden
        r.h1s[0, im, 16:272, :] = nn(r.shift[1], hidden).astype(BF16)
        r.h1s[2, im, 16:272, :] = nn(r.shift[0], hidden).astype(BF16)
        r.h1cm[:, 256 * im : 256 * im + 256] = nt(ident, hidden).astype(BF16)

    for wait in exit_waits:
        wait()
    full = widen(r.wz2)
    unpack_own(r.w2, full[0:hw])
    unpack_own(r.ws, full[hw:])
    rest = forward(r.w1, gather1)
    gather2 = spread(r.w2)
    gather3 = spread(r.ws)
    for wait in rest:
        wait()

    def taps():
        return [(dy, dx) for dy in range(3) for dx in range(3)]

    def stack(pieces):
        return jnp.concatenate(pieces, axis=0)

    def conv1(phase, carry):
        a, c = lax.div(phase, 2), lax.rem(phase, 2)
        parts = []
        for dy, dx in taps():
            first = pl.multiple_of(16 * lax.div(a + dy + 1, 2), 16)
            ver = lax.div(c + dx + 1, 2)
            parts.append(
                stack([r.h1s[ver, im, pl.ds(first, 256), :] for im in range(per)])
            )
        y = nn(jnp.concatenate(parts, axis=1), r.w1[...])
        r.y1[phase] = y
        out = []
        for im in range(per):
            piece = y[256 * im : 256 * im + 256]
            out.append(carry[2 * im] + colsum(piece))
            out.append(carry[2 * im + 1] + colsum(piece * piece))
        return tuple(out)

    nought = jnp.zeros((1, chans), F32)
    mid = lax.fori_loop(0, 4, conv1, (nought,) * (2 * per))
    payload = jnp.zeros((8, chans), F32)
    for im in range(per):
        payload = payload + place_row(mid[2 * im], group[im], 8)
        payload = payload + place_row(mid[2 * im + 1], group[im] + 4, 8)
    mid_sums = AllReduce(2)
    mid_sums.begin(payload)

    def turn(src, dst):
        def one(tap, carry):
            first = pl.multiple_of(256 * tap, 256)
            dst[pl.ds(first, 256), :] = nt(r.ident[...], src[pl.ds(first, 256), :]).astype(BF16)
            return carry

        lax.fori_loop(0, 9, one, 0)

    turn(r.w1, r.w1t)
    rest = forward(r.w2, gather2) + forward(r.ws, gather3)
    mid_sums.middle()

    r.cbuf[me] = r.cown[pl.ds(per * me, per)]
    for wait in cot_waits:
        wait()
    for im in range(per):
        for n in range(4):
            piece = channel_major(r.cbuf, im, slice(256 * n, 256 * n + 256))
            grid = nt(r.gridder[...], piece).astype(BF16)
            for ver in range(2):
                for ph in range(4):
                    at = 256 * ver + 64 * ph
                    r.dzs[ver, ph, im, 16 + 64 * n : 80 + 64 * n, :] = grid[at : at + 64]

    coarse = jnp.zeros((256 * per, chans), F32)
    for ph in range(4):
        coarse = coarse + stack([r.dzs[0, ph, im, 16:272, :] for im in range(per)]).astype(F32)
    bias_sum = colsum(coarse)
    r.dzc[...] = coarse.astype(BF16)

    def tap_slice(ref, a, c, dy, dx, im):
        row, colm = a + dy + 1, c + dx + 1
        first = pl.multiple_of(16 * lax.div(row, 2), 16)
        ph = 2 * lax.rem(row, 2) + lax.rem(colm, 2)
        side_step = lax.div(colm, 2) - 1
        return ref[side_step * side_step, ph, im, pl.ds(first, 256), :]

    for wait in rest:
        wait()
    turn(r.w2, r.w2t)

    def back2(phase, carry):
        a, c = lax.div(phase, 2), lax.rem(phase, 2)
        parts = [
            stack([tap_slice(r.dzs, a, c, 2 - dy, 2 - dx, im) for im in range(per)])
            for dy, dx in taps()
        ]
        r.act[phase] = nn(jnp.concatenate(parts, axis=1), r.w2t[...])
        return carry

    lax.fori_loop(0, 4, back2, 0)

    stats = mid_sums.end()
    mean2 = stats[0:4] / (4.0 * count)
    inv2 = lax.rsqrt(stats[4:8] / (4.0 * count) - mean2 * mean2 + NORM_EPSILON)
    mean2_b = [pick_row(mean2, group[im]) for im in range(per)]
    inv2_b = [pick_row(inv2, group[im]) for im in range(per)]

    def hidden2(phase, carry):
        c = lax.rem(phase, 2)
        out = []
        for im in range(per):
            span = slice(256 * im, 256 * im + 256)
            normal = (r.y1[phase, span, :] - mean2_b[im]) * inv2_b[im]
            r.y1[phase, span, :] = normal
            pre = gain * normal + shift
            sig = sigmoid(pre)
            hidden = (pre * sig * mask_b[im]).astype(BF16)
            act = r.act[phase, span, :] * (sig * (1.0 + pre * (1.0 - sig)) * mask_b[im])
            r.act[phase, span, :] = act
            out.append(carry[2 * im] + colsum(act))
            out.append(carry[2 * im + 1] + colsum(act * normal))
            r.h2s[0, phase, im, 16:272, :] = hidden
            r.h2s[1, phase, im, 16:272, :] = nn(r.shift[c], hidden).astype(BF16)
            lanes = pl.ds(pl.multiple_of(512 * phase + 256 * im, 256), 256)
            r.h2cm[:, lanes] = nt(r.ident[...], hidden).astype(BF16)
        return tuple(out)

    mid = lax.fori_loop(0, 4, hidden2, (nought,) * (2 * per))
    payload = place_row(bias_sum, 8, 16)
    for im in range(per):
        payload = payload + place_row(mid[2 * im], group[im], 16)
        payload = payload + place_row(mid[2 * im + 1], group[im] + 4, 16)
    back_sums = AllReduce(3)
    back_sums.begin(payload)

    def grad2(tap, carry):
        dy, dx = lax.div(tap, 3), lax.rem(tap, 3)
        pieces = []
        for ph in range(4):
            a, c = ph // 2, ph % 2
            for im in range(per):
                pieces.append(tap_slice(r.dzs, a, c, 2 - dy, 2 - dx, im))
        first = pl.multiple_of(256 * tap, 256)
        r.dw2[pl.ds(first, 256), :] = nn(r.h2cm[...], stack(pieces))
        return carry

    lax.fori_loop(0, 9, grad2, 0)
    back_sums.middle()
    for im in range(per):
        piece = channel_major(r.fbuf, im, slice(0, 256))
        grad = nn(piece, r.dzc[256 * im : 256 * im + 256, :])
        if im == 0:
            r.dws[...] = grad
        else:
            r.dws[...] = r.dws[...] + grad

    class GradSum:
        def __init__(self, number, fetch):
            self.fetch = fetch
            for part in PARTS:
                setattr(self, part, getattr(r, part + str(number)))

        def begin(self):
            for u in range(4):
                self.s1[u] = self.fetch(2 * u + 1 - core).astype(BF16)
            self.waits = [post(self.s1, self.r1, self.r1, dev(partner, within, me))]

        def settle(self):
            for wait in self.waits:
                wait()

        def across(self, send, got, masks):
            self.waits = [
                post(send.at[h], got.at[h], got.at[h], dev(flip(block, masks[h]), within, me))
                for h in range(2)
            ]

        def first(self):
            self.settle()
            for u in range(4):
                self.acc[u] = self.fetch(2 * u + core) + self.r1[u].astype(F32)
            for v in range(2):
                self.s2[0, v] = self.acc[2 * v + 1 - bit_x, :, 0:128].astype(BF16)
                self.s2[1, v] = self.acc[2 * (1 - bit_y) + v, :, 128:256].astype(BF16)
            self.across(self.s2, self.r2, (2, 4))

        def second(self):
            self.settle()
            low = self.acc[2 * (1 - bit_y) + bit_x, :, 0:128] + self.r2[0, 1 - bit_y].astype(F32)
            high = self.acc[2 * bit_y + 1 - bit_x, :, 128:256] + self.r2[1, 1 - bit_x].astype(F32)
            self.s3[0] = low.astype(BF16)
            self.s3[1] = high.astype(BF16)
            self.across(self.s3, self.r3, (4, 2))

        def third(self):
            self.settle()
            low = self.acc[plane, :, 0:128] + self.r2[0, bit_y].astype(F32)
            high = self.acc[plane, :, 128:256] + self.r2[1, bit_x].astype(F32)
            low, high = low + self.r3[0].astype(F32), high + self.r3[1].astype(F32)
            value = jnp.concatenate([low, high], axis=1).astype(BF16)
            left = [value[0:128], value[256 : 256 + tail]]
            right = [value[128:256], value[256 + tail : rows]]
            if value.shape[0] > rows:
                left.append(value[rows : rows + hs])
                right.append(value[rows + hs :])
            pair = jnp.concatenate([stack(left), stack(right)], axis=1)
            packed = nt(pair, r.unpack[...]).astype(BF16)
            for c in range(n_ch):
                self.s4[c] = packed[:, 128 * c : 128 * c + 128]
            self.r4[me] = self.s4[me]
            self.waits = [
                post(self.s4.at[peer], self.r4.at[me], self.r4.at[peer], dev(block, within, peer))
                for peer in ch_peers
            ]

        def end(self, out, out_small=None):
            self.settle()
            done = self.r4[0].astype(F32)
            for c in range(1, n_ch):
                done = done + self.r4[c].astype(F32)
            turned = done[0:128].T
            out[:, 0:128] = turned[0:local]
            out[:, 128:256] = turned[local:]
            gap = jnp.zeros((128 - tail, 128), F32)
            turned = stack([done[128 : 128 + tail], gap]).T
            ends = turned[0:local] + pltpu.roll(turned[local:], tail, axis=1)
            out[:, 256:rows] = ends[:, 0 : rows - 256]
            if out_small is not None:
                last = done[hw:]
                out_small[0:hs, :] = last[:, 0:local]
                out_small[hs:, :] = pltpu.roll(last, local, axis=1)[:, 0:local]

    def block_rows(ref, size, index):
        return ref[pl.ds(pl.multiple_of(size * index, 8), size), :]

    second = GradSum(2, lambda k: stack([block_rows(r.dw2, rows, k), block_rows(r.dws, small, k)]))
    entry = GradSum(1, lambda k: block_rows(r.dw1, rows, k))
    second.begin()
    r.short[...] = nn(r.fpm[...], r.ws[...]) + out_bias
    r.dshort[...] = nt(r.dzc[...], r.ws[...])

    def conv2(phase, carry):
        a, c = lax.div(phase, 2), lax.rem(phase, 2)
        parts = [
            stack([tap_slice(r.h2s, a, c, dy, dx, im) for im in range(per)]) for dy, dx in taps()
        ]
        y = (nn(jnp.concatenate(parts, axis=1), r.w2[...]) + r.short[...]).astype(BF16)
        lanes = pl.ds(pl.multiple_of(256 * phase, 256), 256)
        for im in range(per):
            r.rc[im, :, lanes] = nt(r.ident[...], y[256 * im : 256 * im + 256]).astype(BF16)
        return carry

    lax.fori_loop(0, 4, conv2, 0)
    for im in range(per):
        for half in range(2):
            piece = jnp.concatenate(
                [r.rc[im, :, 256 * ph + 128 * half : 256 * ph + 128 * half + 128] for ph in range(4)],
                axis=1,
            )
            r.ocm[im, :, 512 * half : 512 * half + 512] = nn(piece, r.flatter[...]).astype(BF16)

    def own_channels(ref, index):
        return ref.at[:, pl.ds(pl.multiple_of(local * index, local), local), :]

    def give_back(ref, out):
        waits = [here(own_channels(ref, me), out.at[pl.ds(per * me, per)])]
        return waits + [
            post(
                own_channels(ref, peer),
                out.at[pl.ds(per * me, per)],
                out.at[pl.ds(per * peer, per)],
                dev(block, within, peer),
            )
            for peer in ch_peers
        ]

    out_waits = give_back(r.ocm, r.out)

    stats = back_sums.end()
    affine_grad2 = stats
    p1_b = [pick_row(stats[0:4], group[im]) / (4.0 * count) for im in range(per)]
    p2_b = [pick_row(stats[4:8], group[im]) / (4.0 * count) for im in range(per)]

    for im in range(per):
        span = slice(256 * im, 256 * im + 256)
        scale = gain * inv2_b[im]
        combos = []
        for a in range(2):
            grads = []
            for c in range(2):
                ph = 2 * a + c
                d = scale * (r.act[ph, span, :] - (p1_b[im] + r.y1[ph, span, :] * p2_b[im]))
                grads.append(d.astype(BF16))
            right = nn(r.shift[0], grads[0])
            left = nn(r.shift[1], grads[1])
            even, odd = grads[0].astype(F32), grads[1].astype(F32)
            combos.append((odd + right, even + odd, left + even))
        gap = jnp.zeros((16, chans), F32)
        for dx in range(3):
            upper, lower = combos[0][dx], combos[1][dx]
            r.field[dx, im] = (lower + stack([upper[16:], gap])).astype(BF16)
            r.field[3 + dx, im] = (upper + lower).astype(BF16)
            r.field[6 + dx, im] = (stack([gap, lower[:-16]]) + upper).astype(BF16)

    def grad1(tap, carry):
        first = pl.multiple_of(256 * tap, 256)
        r.dw1[pl.ds(first, 256), :] = nn(
            r.h1cm[...], stack([r.field[tap, im] for im in range(per)])
        )
        return carry

    lax.fori_loop(0, 9, grad1, 0)
    entry.begin()
    second.first()

    parts = [stack([r.field[tap, im] for im in range(per)]) for tap in range(9)]
    dh1 = nn(jnp.concatenate(parts, axis=1), r.w1t[...])
    payload = jnp.zeros((32, chans), F32)
    for im in range(per):
        span = slice(256 * im, 256 * im + 256)
        normal = (r.fpm[span, :].astype(F32) - mean1_b[im]) * inv1_b[im]
        pre = gamma_b[im] * normal + beta_b[im]
        sig = sigmoid(pre)
        act = dh1[span] * (sig * (1.0 + pre * (1.0 - sig)))
        r.act1[span, :] = act
        q1, q2 = colsum(act), colsum(act * normal)
        payload = payload + place_row(q2, label[im], 32)
        payload = payload + place_row(q1, label[im] + classes, 32)
        payload = payload + place_row(gamma_b[im] * q1, group[im] + 24, 32)
        payload = payload + place_row(gamma_b[im] * q2, group[im] + 28, 32)
    last_sums = AllReduce(4)
    last_sums.begin(payload)
    second.second()
    entry.first()
    last_sums.middle()
    second.third()
    entry.second()

    stats = last_sums.end()
    for im in range(per):
        span = slice(256 * im, 256 * im + 256)
        normal = (r.fpm[span, :].astype(F32) - mean1_b[im]) * inv1_b[im]
        r1 = pick_row(stats[24:28], group[im]) / count
        r2 = pick_row(stats[28:32], group[im]) / count
        grad = inv1_b[im] * (gamma_b[im] * r.act1[span, :] - (r1 + normal * r2))
        grad = (grad + r.dshort[span, :]).astype(BF16)
        r.dcm[im] = nt(r.ident[...], grad).astype(BF16)
    out_waits += give_back(r.dcm, r.dx)
    entry.third()
    second.end(r.grad2, r.grad3)

    table = jnp.zeros((24, chans), F32)
    table = table + jnp.where(iota((24, chans), 0) < 2 * classes, stats[0:24], 0.0)
    table = table + place_row(colsum(affine_grad2[4:8]), 2 * classes, 24)
    table = table + place_row(colsum(affine_grad2[0:4]), 2 * classes + 1, 24)
    table = table + place_row(affine_grad2[8:9], 2 * classes + 2, 24)
    mine = jnp.zeros((24, 128), F32)
    for c in range(n_ch):
        piece = table[:, 128 * (c // 2) : 128 * (c // 2) + 128]
        if c % 2:
            piece = pltpu.roll(piece, local, axis=1)
        mine = mine + jnp.where(me == c, piece, 0.0)
    r.affine_grad[...] = mine

    if inner == 1:
        row = iota((8, 128), 0)

        def norm_rows(index, weight, grad, v):
            for wait in held[index]:
                wait()
            master = weight[...]
            _, _, direction = adam_update(
                grad[...], getattr(r, v + "m")[...], getattr(r, v + "q")[...]
            )
            update = direction + WEIGHT_DECAY * master
            rows_w = jnp.where(row == index, total(master * master), 0.0)
            return rows_w + jnp.where(row == index + 3, total(update * update), 0.0)

        norms = norm_rows(1, r.exit_v, r.grad2, "v2") + norm_rows(2, r.bypass_v, r.grad3, "vs")
        entry.end(r.grad1)
        norms = norms + norm_rows(0, r.entry_v, r.grad1, "v1")
        norm_sums = AllReduce(5)
        norm_sums.begin(norms)
        norm_sums.middle()
        r.norms[...] = norm_sums.end()
    else:
        entry.end(r.grad1)
        r.norms[...] = jnp.zeros((8, 128), F32)

    for wait in out_waits + pending:
        wait()
    cfg.used.append((slots.remote, slots.local))


def final_kernel(cfg, *refs):
    r = SimpleNamespace(**dict(zip(cfg.names, refs)))
    classes = cfg.classes
    local = cfg.local
    r.block_output[...] = r.out[...]
    r.input_gradient[...] = r.dx[...].astype(F32)
    norms = jnp.sqrt(r.norms[...])
    weight_norm, update_norm = norms[0:3, 0:1], norms[3:6, 0:1]
    ratio = weight_norm / update_norm
    at = iota((3, 3), 1)
    r.trust_norms[...] = jnp.where(
        at == 0, weight_norm, jnp.where(at == 1, update_norm, ratio)
    )
    sets = (
        (r.entry, r.entry_m, r.entry_q, r.entry_g, r.entry_1, r.entry_2, r.entry_w),
        (r.exit, r.exit_m, r.exit_q, r.exit_g, r.exit_1, r.exit_2, r.exit_w),
        (r.bypass, r.bypass_m, r.bypass_q, r.bypass_g, r.bypass_1, r.bypass_2, r.bypass_w),
    )
    for index, (weight, m, q, g, first, second, result) in enumerate(sets):
        master = weight[...]
        moment, square, direction = adam_update(g[...], m[...], q[...])
        update = direction + WEIGHT_DECAY * master
        first[...] = moment
        second[...] = square
        result[...] = master - MATRIX_RATE * ratio[index : index + 1] * update
    grad = r.affine_grad[0 : 2 * classes + 3, 0:local]
    moment, square, direction = adam_update(grad, r.affine_m[...], r.affine_q[...])
    r.affine_1[...] = moment
    r.affine_2[...] = square
    r.affine_w[...] = r.affine[...] - AFFINE_RATE * direction


def per_device(
    features,
    labels,
    groups,
    widths,
    entry_conv,
    entry_moment,
    entry_square,
    exit_conv,
    exit_moment,
    exit_square,
    bypass_conv,
    bypass_moment,
    bypass_square,
    norm_affine,
    norm_moment,
    norm_square,
    cotangent,
):
    n_img, n_ch = lax.axis_size("img"), lax.axis_size("ch")
    batch, local, pixels = features.shape
    chans = local * n_ch
    side = math.isqrt(pixels)
    inner = n_img // OUTER
    classes = (norm_affine.shape[0] - 3) // 2
    per = batch // n_ch
    assert (side, chans, n_ch, local, batch % n_ch) == (16, 256, 4, 64, 0)
    rows, small = entry_conv.shape[0] * inner, bypass_conv.shape[0] * inner
    masters = (entry_conv, exit_conv, bypass_conv)
    if inner == 1:
        blocks = masters
    else:
        sets = [[o * inner + i for i in range(inner)] for o in range(OUTER)]
        blocks = tuple(
            lax.all_gather(w.astype(BF16), "img", axis=0, tiled=True, axis_index_groups=sets)
            for w in masters
        )

    vmem = pl.BlockSpec(memory_space=pltpu.VMEM)
    smem = pl.BlockSpec(memory_space=pltpu.SMEM)
    anywhere = pl.BlockSpec(memory_space=pl.ANY)
    states = dict(
        entry_m=entry_moment.T,
        entry_q=entry_square.T,
        exit_m=exit_moment.T,
        exit_q=exit_square.T,
        bypass_m=bypass_moment,
        bypass_q=bypass_square,
    )
    inputs = dict(
        labels=(labels, smem),
        groups=(groups, smem),
        widths=(widths, smem),
        features=(features, anywhere),
        cotangent=(cotangent, anywhere),
        entry=(blocks[0].T, anywhere),
        exit=(blocks[1].T, anywhere),
        bypass=(blocks[2], anywhere),
        affine=(norm_affine, anywhere),
    )
    if inner == 1:
        inputs.update({name: (value, anywhere) for name, value in states.items()})
    sds = jax.ShapeDtypeStruct
    outputs = dict(
        out=(sds(cotangent.shape, BF16), vmem),
        dx=(sds(features.shape, BF16), vmem),
        grad1=(sds((local, rows), F32), vmem),
        grad2=(sds((local, rows), F32), vmem),
        grad3=(sds((small, local), F32), vmem),
        affine_grad=(sds((24, 128), F32), vmem),
        norms=(sds((8, 128), F32), vmem),
    )
    pix = pixels * per
    taps9 = 9 * chans
    held = lambda shape, dtype=BF16: pltpu.VMEM(shape, dtype)
    scratch = dict(
        fown=held((batch, local, pixels)),
        cown=held((batch, local, 4 * pixels)),
        fbuf=held((n_ch, per, local, pixels)),
        cbuf=held((n_ch, per, local, 4 * pixels)),
        entry_v=held((local, rows), blocks[0].dtype),
        exit_v=held((local, rows), blocks[1].dtype),
        bypass_v=held((small, local), blocks[2].dtype),
        affine_v=held(norm_affine.shape, F32),
        padded=held((3 * local, 384)),
        wz1=held((n_ch, rows // 2, 128)),
        wz2=held((n_ch, (rows + small) // 2, 128)),
        aff_z=held((n_ch, 24, 128), F32),
        w1=held((taps9, chans)),
        w2=held((taps9, chans)),
        ws=held((chans, chans)),
        w1t=held((taps9, chans)),
        w2t=held((taps9, chans)),
        unpack=held((512, 512)),
        ident=held((256, 256)),
        shift=held((2, 256, 256)),
        gridder=held((512, 256)),
        flatter=held((512, 512)),
        fpm=held((pix, chans)),
        h1s=held((3, per, pixels + 32, chans)),
        h1cm=held((chans, pix)),
        y1=held((4, pix, chans), F32),
        act=held((4, pix, chans), F32),
        h2s=held((2, 4, per, pixels + 32, chans)),
        dzs=held((2, 4, per, pixels + 32, chans)),
        h2cm=held((chans, 4 * pix)),
        short=held((pix, chans), F32),
        dshort=held((pix, chans), F32),
        dzc=held((pix, chans)),
        act1=held((pix, chans), F32),
        rc=held((per, chans, 4 * pixels)),
        ocm=held((per, chans, 4 * pixels)),
        dcm=held((per, chans, pixels)),
        field=held((9, per, pixels, chans)),
        dw1=held((taps9, chans), F32),
        dw2=held((taps9, chans), F32),
        dws=held((chans, chans), F32),
    )
    for number, size in ((1, rows), (2, rows + small)):
        shapes = ((4, size, chans),) * 2 + ((2, 2, size, 128),) * 2 + ((2, size, 128),) * 2
        shapes += ((n_ch, size // 2, 128),) * 2
        for part, shape in zip(PARTS, shapes):
            scratch[part + str(number)] = held(shape)
        scratch[PARTS[-1] + str(number)] = held((4, size, chans), F32)
    exchanges = [(8, 128), (8, chans), (16, chans), (32, chans)]
    if inner == 1:
        exchanges.append((8, 128))
        for v, shape in (("v1", (local, rows)), ("v2", (local, rows)), ("vs", (small, local))):
            scratch[v + "m"] = held(shape, F32)
            scratch[v + "q"] = held(shape, F32)
    for number, shape in enumerate(exchanges, 1):
        for axis, size in zip("abc", (OUTER, inner, n_ch)):
            if size > 1:
                scratch[axis + str(number)] = held((size,) + shape, F32)
    remote_count = 7 * 3 + 3 * 7 + 2 * 8 + len(exchanges) * (7 + 3 + inner - 1)
    scratch.update(
        send=pltpu.SemaphoreType.DMA((remote_count,)),
        recv=pltpu.SemaphoreType.DMA((remote_count,)),
        lsem=pltpu.SemaphoreType.DMA((20,)),
    )
    cfg = SimpleNamespace(
        names=[*inputs, *outputs, *scratch],
        inner=inner,
        n_ch=n_ch,
        batch=batch,
        local=local,
        classes=classes,
        count=float(batch * n_img // widths.shape[0] * pixels),
        rows=rows,
        small=small,
        used=[],
    )
    out, dx, grad1, grad2, grad3, affine_grad, norms = pl.pallas_call(
        functools.partial(main_kernel, cfg),
        out_shape=[s for s, _ in outputs.values()],
        in_specs=[s for _, s in inputs.values()],
        out_specs=[s for _, s in outputs.values()],
        scratch_shapes=list(scratch.values()),
        compiler_params=pltpu.CompilerParams(
            collective_id=0, has_side_effects=True, vmem_limit_bytes=VMEM_LIMIT
        ),
        name="block_step",
    )(*[v for v, _ in inputs.values()])
    assert max(n for n, _ in cfg.used) <= remote_count and max(n for _, n in cfg.used) <= 20

    grads = [grad1, grad2, grad3]
    if inner > 1:
        grads = [
            lax.psum_scatter(g, "img", scatter_dimension=0, axis_index_groups=sets, tiled=True)
            for g in (grad1.T, grad2.T, grad3)
        ]
        updates = []
        for w, g, m, s in zip(
            masters,
            grads,
            (entry_moment, exit_moment, bypass_moment),
            (entry_square, exit_square, bypass_square),
        ):
            updates.append(adam_update(g, m, s)[2] + WEIGHT_DECAY * w)
        sums = lax.psum(
            jnp.stack([jnp.sum(w * w) for w in masters] + [jnp.sum(u * u) for u in updates]),
            ("img", "ch"),
        )
        norms = jnp.broadcast_to(jnp.pad(sums, (0, 2))[:, None], (8, 128))
        grads = [grads[0].T, grads[1].T, grads[2]]

    args = dict(
        out=out,
        dx=dx,
        norms=norms,
        affine_grad=affine_grad,
        entry_g=grads[0],
        exit_g=grads[1],
        bypass_g=grads[2],
        entry=entry_conv.T,
        exit=exit_conv.T,
        bypass=bypass_conv,
        **states,
        affine=norm_affine,
        affine_m=norm_moment,
        affine_q=norm_square,
    )
    tall = sds(entry_conv.shape[::-1], F32)
    short, wide = (sds(w.shape, F32) for w in (bypass_conv, norm_affine))
    results = dict(
        block_output=sds(cotangent.shape, BF16),
        input_gradient=sds(features.shape, F32),
        entry_1=tall,
        entry_2=tall,
        entry_w=tall,
        exit_1=tall,
        exit_2=tall,
        exit_w=tall,
        bypass_1=short,
        bypass_2=short,
        bypass_w=short,
        affine_1=wide,
        affine_2=wide,
        affine_w=wide,
        trust_norms=sds((3, 3), F32),
    )
    end_cfg = SimpleNamespace(names=[*args, *results], classes=classes, local=local)
    final = pl.pallas_call(
        functools.partial(final_kernel, end_cfg),
        out_shape=list(results.values()),
        in_specs=[vmem] * len(args),
        out_specs=[vmem] * len(results),
        compiler_params=pltpu.CompilerParams(vmem_limit_bytes=VMEM_LIMIT),
        name="finish",
    )(*args.values())
    return tuple(v.T if s is tall else v for v, s in zip(final, results.values()))


def solution(mesh):
    wide = P("img", "ch")
    deep = P("img", "ch", None)
    table = P(None, "ch")
    return jax.shard_map(
        per_device,
        mesh=mesh,
        in_specs=(deep, P("img"), P("img"), P()) + (wide,) * 9 + (table,) * 3 + (deep,),
        out_specs=(deep, deep) + (wide,) * 9 + (table,) * 3 + (P(),),
        check_vma=False,
    )
```

```python
import functools
import math
from types import SimpleNamespace

import jax
import jax.numpy as jnp
from jax import lax
from jax.experimental import pallas as pl
from jax.experimental.pallas import tpu as pltpu
from jax.sharding import PartitionSpec as P

LEVELS = 4
STEP = 5
NORM_EPSILON = 1e-05
ADAM_EPSILON = 1e-06
MOMENT_DECAY = 0.9
SQUARE_DECAY = 0.999
WEIGHT_DECAY = 0.01
MATRIX_RATE = 0.3
AFFINE_RATE = 0.2

OUTER = 8
VMEM_LIMIT = 56 * 1024 * 1024
BF16 = jnp.bfloat16
F32 = jnp.float32
MESH = pl.DeviceIdType.MESH
PARTS = ("s1", "r1", "s2", "r2", "s3", "r3", "s4", "r4", "acc")


def nn(left, right):
    return lax.dot_general(left, right, (((1,), (0,)), ((), ())), preferred_element_type=F32)


def nt(left, right):
    return lax.dot_general(left, right, (((1,), (1,)), ((), ())), preferred_element_type=F32)


def flip(index, mask):
    result = index
    for bit in range(3):
        if (mask >> bit) & 1:
            digit = lax.rem(lax.div(index, 1 << bit), 2)
            result = result + (1 - 2 * digit) * (1 << bit)
    return result


def sigmoid(value):
    return 0.5 * jnp.tanh(0.5 * value) + 0.5


def iota(shape, axis):
    return lax.broadcasted_iota(jnp.int32, shape, axis)


def to_bf16(condition):
    return jnp.where(condition, 1.0, 0.0).astype(BF16)


def pick_row(table, index):
    hit = iota(table.shape, 0) == index
    return jnp.sum(jnp.where(hit, table, 0.0), axis=0, keepdims=True)


def place_row(row, index, rows):
    hit = iota((rows, row.shape[1]), 0) == index
    return jnp.where(hit, row, 0.0)


def colsum(value):
    return jnp.sum(value, axis=0, keepdims=True)


def adam_update(grad, moment, square):
    moment_new = MOMENT_DECAY * moment + (1.0 - MOMENT_DECAY) * grad
    square_new = SQUARE_DECAY * square + (1.0 - SQUARE_DECAY) * grad * grad
    direction = (
        moment_new
        / (1.0 - MOMENT_DECAY**STEP)
        / (jnp.sqrt(square_new / (1.0 - SQUARE_DECAY**STEP)) + ADAM_EPSILON)
    )
    return (moment_new, square_new, direction)


def total(value):
    return jnp.sum(jnp.sum(value, axis=1, keepdims=True), axis=0, keepdims=True)


def main_kernel(cfg, *refs):
    r = SimpleNamespace(**dict(zip(cfg.names, refs)))
    inner, n_ch, batch, local = cfg.inner, cfg.n_ch, cfg.batch, cfg.local
    classes, count = cfg.classes, cfg.count
    per = batch // n_ch
    chans = local * n_ch
    rows, small = cfg.rows, cfg.small
    tail = (rows - 256) // 2
    hw, hs = rows // 2, small // 2
    slots = SimpleNamespace(remote=0, local=0)

    img = lax.axis_index("img")
    me = lax.axis_index("ch")
    block = lax.div(img, inner)
    within = lax.rem(img, inner)
    core = lax.rem(block, 2)
    plane = lax.div(block, 2)
    bit_x, bit_y = lax.rem(plane, 2), lax.div(plane, 2)

    def dev(block_id, within_id, ch_id):
        return (block_id * inner + within_id, ch_id)

    pending = []

    def post(src, dst, landed, peer):
        slot = slots.remote
        slots.remote = slot + 1
        copy = pltpu.make_async_remote_copy(
            src_ref=src,
            dst_ref=dst,
            send_sem=r.send.at[slot],
            recv_sem=r.recv.at[slot],
            device_id=peer,
            device_id_type=MESH,
        )
        copy.start()
        pending.append(copy.wait_send)
        arrival = pltpu.make_async_remote_copy(
            src_ref=landed,
            dst_ref=landed,
            send_sem=r.send.at[slot],
            recv_sem=r.recv.at[slot],
            device_id=peer,
            device_id_type=MESH,
        )
        return arrival.wait_recv

    def here(src, dst):
        slot = slots.local
        slots.local = slot + 1
        copy = pltpu.make_async_copy(src, dst, r.lsem.at[slot])
        copy.start()
        return copy.wait

    near = [(flip(block, mask), me) for mask in (1, 2, 4)] + [(block, flip(me, mask)) for mask in (1, 2)]
    core_peer, x_peer, y_peer = (dev(b, within, c) for b, c in near[:3])
    ch_peers = [flip(me, mask) for mask in range(1, n_ch)]
    inner_pairs = [
        (lax.rem(within + step, inner), lax.rem(within + inner - step, inner))
        for step in range(1, inner)
    ]
    barrier = pltpu.get_barrier_semaphore()
    everyone = [core_peer, x_peer, y_peer]
    everyone += [dev(block, within, peer) for peer in ch_peers]
    everyone += [dev(block, peer, me) for peer, _ in inner_pairs]
    for peer in everyone:
        pl.semaphore_signal(barrier, inc=1, device_id=peer, device_id_type=MESH)

    got_entry = here(r.entry, r.entry_v)
    got_features = here(r.features, r.fown)
    got_exit = here(r.exit, r.exit_v)
    got_bypass = here(r.bypass, r.bypass_v)
    got_affine = here(r.affine, r.affine_v)
    got_cot = here(r.cotangent, r.cown)
    states = ((r.entry_m, r.entry_q), (r.exit_m, r.exit_q), (r.bypass_m, r.bypass_q)) if inner == 1 else ()
    held = [
        (here(m, getattr(r, v + "m")), here(q, getattr(r, v + "q")))
        for (m, q), v in zip(states, ("v1", "v2", "vs"))
    ]

    s_row, s_col = iota((hw, 384), 0), iota((hw, 384), 1)
    pick_first = to_bf16(s_col == jnp.where(s_row < 128, s_row, s_row + 128))
    pick_second = to_bf16(s_col == jnp.where(s_row < 128, s_row + 128, s_row + 128 + tail))
    r.padded[...] = jnp.zeros(r.padded.shape, BF16)

    def pack_own(value):
        r.padded[local : 2 * local, 0:rows] = value.astype(BF16)
        packed = nt(pick_first, r.padded[local : 3 * local, :])
        return (packed + nt(pick_second, r.padded[0 : 2 * local, :])).astype(BF16)

    got_entry()
    r.wz[me, 0:hw, :] = pack_own(r.entry_v[...])
    got_exit()
    r.wz[me, hw : 2 * hw, :] = pack_own(r.exit_v[...])
    got_bypass()
    e_row, e_col = iota((local, 128), 0), iota((local, 128), 1)
    value = r.bypass_v[...].astype(BF16)
    r.wz[me, 2 * hw :, :] = (
        nn(value[:hs], to_bf16(e_col == e_row)) + nn(value[hs:], to_bf16(e_col == e_row + local))
    ).astype(BF16)
    pl.semaphore_wait(barrier, len(everyone))

    def to_channels(buffer):
        return [
            post(buffer.at[me], buffer.at[me], buffer.at[peer], dev(block, within, peer))
            for peer in ch_peers
        ]

    weight_waits = to_channels(r.wz)
    got_features()
    feature_waits = [
        post(
            r.fown.at[pl.ds(per * peer, per)],
            r.fbuf.at[me],
            r.fbuf.at[peer],
            dev(block, within, peer),
        )
        for peer in ch_peers
    ]
    lane = iota((512, 512), 0)
    column = iota((512, 512), 1)
    spot = 256 * ((lane >> 6) & 1) + 64 * (lane >> 7) + (lane & 63)
    r.unpack[...] = to_bf16(column == spot)

    r.fbuf[me] = r.fown[pl.ds(per * me, per)]
    flat = jnp.concatenate([r.fown[b] for b in range(batch)], axis=1)
    wide = flat.astype(F32)
    square = wide * wide
    square_hi = square.astype(BF16)
    square_lo = (square - square_hi.astype(F32)).astype(BF16)
    level = iota((16, 256), 0)
    first_mask = jnp.concatenate([to_bf16(level == r.groups[b]) for b in range(batch)], axis=1)
    second_mask = jnp.concatenate([to_bf16(level == r.groups[b] + 4) for b in range(batch)], axis=1)
    sums = nt(first_mask, flat) + nt(second_mask, square_hi) + nt(second_mask, square_lo)

    def ordered_sum(ref, size):
        result = ref[0]
        for slot in range(1, size):
            result = result + ref[slot]
        return result

    class AllReduce:
        def __init__(self, number, stages=5):
            self.send, self.got, self.over_inner = (
                getattr(r, part + str(number), None) for part in "abc"
            )
            self.stages = stages

        def begin(self, value):
            self.stage = 0
            self.send[0] = value
            self.start()

        def start(self):
            at, (b, c) = self.stage, near[self.stage]
            self.wait = post(
                self.send.at[at], self.got.at[at], self.got.at[at], dev(b, within, c)
            )

        def advance(self):
            self.wait()
            value = self.send[self.stage] + self.got[self.stage]
            if self.stage == 2 and inner > 1:
                ref = self.over_inner
                ref[within] = value
                waits = [
                    post(ref.at[within], ref.at[within], ref.at[back], dev(block, peer, me))
                    for peer, back in inner_pairs
                ]
                for wait in waits:
                    wait()
                value = ordered_sum(ref, inner)
            self.stage += 1
            if self.stage < self.stages:
                self.send[self.stage] = value
                self.start()
            return value

        def end(self):
            while self.stage < self.stages:
                value = self.advance()
            return value

    input_sums = AllReduce(1, 3)
    r.padsum[...] = jnp.zeros((8, 128), F32)
    r.padsum[:, 0:local] = sums[0:8]
    input_sums.begin(r.padsum[...])

    def unpack_own(own, full):
        own[0:128, :] = full[0:128, 0:256]
        own[128:256, :] = full[0:128, 256:512]
        own[256 : 256 + tail, :] = full[128:hw, 0:256]
        own[256 + tail : rows, :] = full[128:hw, 256:512]
        if full.shape[0] > hw:
            own[rows : rows + hs, :] = full[hw:, 0:256]
            own[rows + hs :, :] = full[hw:, 256:512]

    class Gather:
        def __init__(self, ref):
            self.ref = ref

        def near(self):
            own = [self.ref.at[core, bit_y, bit_x, :, pl.ds(128 * h, 128)] for h in range(2)]
            far_x = self.ref.at[core, bit_y, 1 - bit_x, :, pl.ds(0, 128)]
            far_y = self.ref.at[core, 1 - bit_y, bit_x, :, pl.ds(128, 128)]
            self.waits = [post(own[0], own[0], far_x, x_peer), post(own[1], own[1], far_y, y_peer)]

        def settle(self):
            for wait in self.waits:
                wait()

        def far(self):
            self.settle()
            own = self.ref.at[core, bit_y, :, :, pl.ds(0, 128)]
            got = self.ref.at[core, 1 - bit_y, :, :, pl.ds(0, 128)]
            low = post(own, own, got, y_peer)
            own = self.ref.at[core, :, bit_x, :, pl.ds(128, 128)]
            got = self.ref.at[core, :, 1 - bit_x, :, pl.ds(128, 128)]
            self.waits = [low, post(own, own, got, x_peer)]

        def pair(self):
            self.settle()
            own, got = self.ref.at[core], self.ref.at[1 - core]
            self.waits = [post(own, own, got, core_peer)]

        def finish(self, out, out_small=None):
            self.settle()
            for k in range(OUTER):
                at = self.ref.at[k % 2, k // 4, k // 2 % 2]
                out[rows * k : rows * k + rows, :] = at[0:rows, :]
                if out_small is not None:
                    out_small[small * k : small * k + small, :] = at[rows:, :]

    ident = to_bf16(iota((256, 256), 0) == iota((256, 256), 1))
    r.ident[...] = ident
    q_out, q_in = iota((256, 256), 0), iota((256, 256), 1)
    r.shift[0] = to_bf16((q_in == q_out + 1) & ((q_out & 15) < 15))
    r.shift[1] = to_bf16((q_in == q_out - 1) & ((q_out & 15) > 0))

    input_sums.advance()
    for wait in weight_waits:
        wait()
    packed = jnp.concatenate([r.wz[c] for c in range(n_ch)], axis=1)
    full = nn(packed, r.unpack[...]).astype(BF16)
    gather1, gather2 = Gather(r.g1), Gather(r.g2)
    unpack_own(r.g1.at[core, bit_y, bit_x], full[0:hw])
    gather1.near()
    input_sums.advance()
    unpack_own(r.g2.at[core, bit_y, bit_x], full[hw:])
    got_affine()
    r.aff_z[me] = jnp.zeros((32, 128), F32)
    r.aff_z[me, 0 : 2 * classes + 3, 0:local] = r.affine_v[...]
    gather1.far()
    r.aff_z[me, 24:32, :] = input_sums.advance()
    affine_waits = to_channels(r.aff_z)
    got_cot()
    cot_waits = [
        post(
            r.cown.at[pl.ds(per * peer, per)],
            r.cbuf.at[me],
            r.cbuf.at[peer],
            dev(block, within, peer),
        )
        for peer in ch_peers
    ]

    rho, px = iota((512, 256), 0), iota((512, 256), 1)
    version, a, b_ = rho >> 8, (rho >> 7) & 1, (rho >> 6) & 1
    col = (rho & 15) + version * (1 - 2 * b_)
    target = (2 * ((rho & 63) >> 4) + a) * 32 + 2 * col + b_
    r.gridder[...] = to_bf16((px == target) & (col >= 0) & (col < 16))
    target = (
        (2 * ((lane & 127) >> 4) + (lane >> 8)) * 32 + 2 * (lane & 15) + ((lane >> 7) & 1)
    )
    r.flatter[...] = to_bf16(column == target)
    zeros = jnp.zeros((16, 256), BF16)
    for im in range(per):
        for ver in range(3):
            r.h1s[ver, im, 0:16, :] = zeros
            r.h1s[ver, im, 272:288, :] = zeros
        for ver in range(2):
            for ph in range(4):
                for ref in (r.h2s, r.dzs):
                    ref[ver, ph, im, 0:16, :] = zeros
                    ref[ver, ph, im, 272:288, :] = zeros

    def channel_major(ref, im, lanes):
        return jnp.concatenate([ref[c, im, :, lanes] for c in range(n_ch)], axis=0)

    gather1.pair()
    gather2.near()
    for wait in feature_waits:
        wait()
    for im in range(per):
        r.fpm[256 * im : 256 * im + 256, :] = nt(
            ident, channel_major(r.fbuf, im, slice(0, 256))
        ).astype(BF16)

    def wide_lanes(ref):
        parts = [
            ref[c] + pltpu.roll(ref[c + 1], local, axis=1) for c in range(0, n_ch, 2)
        ]
        return jnp.concatenate(parts, axis=1)

    for wait in affine_waits:
        wait()
    affine = wide_lanes(r.aff_z)
    stats = affine[24:32]
    mean1 = stats[0:4] / count
    inv1 = lax.rsqrt(stats[4:8] / count - mean1 * mean1 + NORM_EPSILON)
    gain = affine[2 * classes : 2 * classes + 1]
    shift = affine[2 * classes + 1 : 2 * classes + 2]
    out_bias = affine[2 * classes + 2 : 2 * classes + 3]
    group, label, mean1_b, inv1_b, gamma_b, beta_b, mask_b = [], [], [], [], [], [], []
    for im in range(per):
        group.append(r.groups[per * me + im])
        label.append(r.labels[per * me + im])
        mean1_b.append(pick_row(mean1, group[im]))
        inv1_b.append(pick_row(inv1, group[im]))
        gamma_b.append(pick_row(affine, label[im]))
        beta_b.append(pick_row(affine, label[im] + classes))
        width = r.widths[group[im]]
        mask_b.append(
            jnp.where(iota((1, chans), 1) < width * (chans // LEVELS), 1.0, 0.0)
        )

    for im in range(per):
        normal = (r.fpm[256 * im : 256 * im + 256, :].astype(F32) - mean1_b[im]) * inv1_b[im]
        pre = gamma_b[im] * normal + beta_b[im]
        hidden = (pre * sigmoid(pre)).astype(BF16)
        r.h1s[1, im, 16:272, :] = hidden
        r.h1s[0, im, 16:272, :] = nn(r.shift[1], hidden).astype(BF16)
        r.h1s[2, im, 16:272, :] = nn(r.shift[0], hidden).astype(BF16)
        r.h1cm[:, 256 * im : 256 * im + 256] = nt(ident, hidden).astype(BF16)

    gather1.finish(r.w1)
    gather2.far()

    def taps():
        return [(dy, dx) for dy in range(3) for dx in range(3)]

    def stack(pieces):
        return jnp.concatenate(pieces, axis=0)

    def conv1(phase, carry):
        a, c = lax.div(phase, 2), lax.rem(phase, 2)
        parts = []
        for dy, dx in taps():
            first = pl.multiple_of(16 * lax.div(a + dy + 1, 2), 16)
            ver = lax.div(c + dx + 1, 2)
            parts.append(
                stack([r.h1s[ver, im, pl.ds(first, 256), :] for im in range(per)])
            )
        y = nn(jnp.concatenate(parts, axis=1), r.w1[...])
        r.y1[phase] = y
        out = []
        for im in range(per):
            piece = y[256 * im : 256 * im + 256]
            out.append(carry[2 * im] + colsum(piece))
            out.append(carry[2 * im + 1] + colsum(piece * piece))
        return tuple(out)

    nought = jnp.zeros((1, chans), F32)
    mid = lax.fori_loop(0, 4, conv1, (nought,) * (2 * per))
    payload = jnp.zeros((8, chans), F32)
    for im in range(per):
        payload = payload + place_row(mid[2 * im], group[im], 8)
        payload = payload + place_row(mid[2 * im + 1], group[im] + 4, 8)
    mid_sums = AllReduce(2)
    mid_sums.begin(payload)

    def turn(src, dst):
        def one(tap, carry):
            first = pl.multiple_of(256 * tap, 256)
            dst[pl.ds(first, 256), :] = nt(r.ident[...], src[pl.ds(first, 256), :]).astype(BF16)
            return carry

        lax.fori_loop(0, 9, one, 0)

    gather2.pair()
    turn(r.w1, r.w1t)
    mid_sums.advance()

    r.cbuf[me] = r.cown[pl.ds(per * me, per)]
    for wait in cot_waits:
        wait()
    for im in range(per):
        for n in range(4):
            piece = channel_major(r.cbuf, im, slice(256 * n, 256 * n + 256))
            grid = nt(r.gridder[...], piece).astype(BF16)
            for ver in range(2):
                for ph in range(4):
                    at = 256 * ver + 64 * ph
                    r.dzs[ver, ph, im, 16 + 64 * n : 80 + 64 * n, :] = grid[at : at + 64]

    coarse = jnp.zeros((256 * per, chans), F32)
    for ph in range(4):
        coarse = coarse + stack([r.dzs[0, ph, im, 16:272, :] for im in range(per)]).astype(F32)
    bias_sum = colsum(coarse)
    r.dzc[...] = coarse.astype(BF16)

    def tap_slice(ref, a, c, dy, dx, im):
        row, colm = a + dy + 1, c + dx + 1
        first = pl.multiple_of(16 * lax.div(row, 2), 16)
        ph = 2 * lax.rem(row, 2) + lax.rem(colm, 2)
        side_step = lax.div(colm, 2) - 1
        return ref[side_step * side_step, ph, im, pl.ds(first, 256), :]

    mid_sums.advance()
    gather2.finish(r.w2, r.ws)
    turn(r.w2, r.w2t)
    mid_sums.advance()

    def back2(phase, carry):
        a, c = lax.div(phase, 2), lax.rem(phase, 2)
        parts = [
            stack([tap_slice(r.dzs, a, c, 2 - dy, 2 - dx, im) for im in range(per)])
            for dy, dx in taps()
        ]
        r.act[phase] = nn(jnp.concatenate(parts, axis=1), r.w2t[...])
        return carry

    lax.fori_loop(0, 2, back2, 0)
    mid_sums.advance()
    lax.fori_loop(2, 4, back2, 0)

    stats = mid_sums.end()
    mean2 = stats[0:4] / (4.0 * count)
    inv2 = lax.rsqrt(stats[4:8] / (4.0 * count) - mean2 * mean2 + NORM_EPSILON)
    mean2_b = [pick_row(mean2, group[im]) for im in range(per)]
    inv2_b = [pick_row(inv2, group[im]) for im in range(per)]

    def hidden2(phase, carry):
        c = lax.rem(phase, 2)
        out = []
        for im in range(per):
            span = slice(256 * im, 256 * im + 256)
            normal = (r.y1[phase, span, :] - mean2_b[im]) * inv2_b[im]
            r.y1[phase, span, :] = normal
            pre = gain * normal + shift
            sig = sigmoid(pre)
            hidden = (pre * sig * mask_b[im]).astype(BF16)
            act = r.act[phase, span, :] * (sig * (1.0 + pre * (1.0 - sig)) * mask_b[im])
            r.act[phase, span, :] = act
            out.append(carry[2 * im] + colsum(act))
            out.append(carry[2 * im + 1] + colsum(act * normal))
            r.h2s[0, phase, im, 16:272, :] = hidden
            r.h2s[1, phase, im, 16:272, :] = nn(r.shift[c], hidden).astype(BF16)
            lanes = pl.ds(pl.multiple_of(512 * phase + 256 * im, 256), 256)
            r.h2cm[:, lanes] = nt(r.ident[...], hidden).astype(BF16)
        return tuple(out)

    mid = lax.fori_loop(0, 4, hidden2, (nought,) * (2 * per))
    payload = place_row(bias_sum, 8, 16)
    for im in range(per):
        payload = payload + place_row(mid[2 * im], group[im], 16)
        payload = payload + place_row(mid[2 * im + 1], group[im] + 4, 16)
    back_sums = AllReduce(3)
    back_sums.begin(payload)

    def grad2(tap, carry):
        dy, dx = lax.div(tap, 3), lax.rem(tap, 3)
        pieces = []
        for ph in range(4):
            a, c = ph // 2, ph % 2
            for im in range(per):
                pieces.append(tap_slice(r.dzs, a, c, 2 - dy, 2 - dx, im))
        first = pl.multiple_of(256 * tap, 256)
        r.dw2[pl.ds(first, 256), :] = nn(r.h2cm[...], stack(pieces))
        return carry

    for first in (0, 3, 6):
        lax.fori_loop(first, first + 3, grad2, 0)
        back_sums.advance()
    for im in range(per):
        piece = channel_major(r.fbuf, im, slice(0, 256))
        grad = nn(piece, r.dzc[256 * im : 256 * im + 256, :])
        if im == 0:
            r.dws[...] = grad
        else:
            r.dws[...] = r.dws[...] + grad

    class GradSum:
        def __init__(self, number, fetch):
            self.fetch = fetch
            for part in PARTS:
                setattr(self, part, getattr(r, part + str(number)))

        def begin(self):
            for u in range(4):
                self.s1[u] = self.fetch(2 * u + 1 - core).astype(BF16)
            self.waits = [post(self.s1, self.r1, self.r1, core_peer)]

        def settle(self):
            for wait in self.waits:
                wait()

        def across(self, send, got, peers):
            self.waits = [
                post(send.at[h], got.at[h], got.at[h], peers[h]) for h in range(2)
            ]

        def first(self):
            self.settle()
            for u in range(4):
                self.acc[u] = self.fetch(2 * u + core) + self.r1[u].astype(F32)
            for v in range(2):
                self.s2[0, v] = self.acc[2 * v + 1 - bit_x, :, 0:128].astype(BF16)
                self.s2[1, v] = self.acc[2 * (1 - bit_y) + v, :, 128:256].astype(BF16)
            self.across(self.s2, self.r2, (x_peer, y_peer))

        def second(self):
            self.settle()
            low = self.acc[2 * (1 - bit_y) + bit_x, :, 0:128] + self.r2[0, 1 - bit_y].astype(F32)
            high = self.acc[2 * bit_y + 1 - bit_x, :, 128:256] + self.r2[1, 1 - bit_x].astype(F32)
            self.s3[0] = low.astype(BF16)
            self.s3[1] = high.astype(BF16)
            self.across(self.s3, self.r3, (y_peer, x_peer))

        def third(self):
            self.settle()
            low = self.acc[plane, :, 0:128] + self.r2[0, bit_y].astype(F32)
            high = self.acc[plane, :, 128:256] + self.r2[1, bit_x].astype(F32)
            low, high = low + self.r3[0].astype(F32), high + self.r3[1].astype(F32)
            value = jnp.concatenate([low, high], axis=1).astype(BF16)
            left = [value[0:128], value[256 : 256 + tail]]
            right = [value[128:256], value[256 + tail : rows]]
            if value.shape[0] > rows:
                left.append(value[rows : rows + hs])
                right.append(value[rows + hs :])
            pair = jnp.concatenate([stack(left), stack(right)], axis=1)
            packed = nt(pair, r.unpack[...]).astype(BF16)
            for c in range(n_ch):
                self.s4[c] = packed[:, 128 * c : 128 * c + 128]
            self.r4[me] = self.s4[me]
            self.waits = [
                post(self.s4.at[peer], self.r4.at[me], self.r4.at[peer], dev(block, within, peer))
                for peer in ch_peers
            ]

        def end(self, out, out_small=None):
            self.settle()
            done = self.r4[0].astype(F32)
            for c in range(1, n_ch):
                done = done + self.r4[c].astype(F32)
            turned = done[0:128].T
            out[:, 0:128] = turned[0:local]
            out[:, 128:256] = turned[local:]
            gap = jnp.zeros((128 - tail, 128), F32)
            turned = stack([done[128 : 128 + tail], gap]).T
            ends = turned[0:local] + pltpu.roll(turned[local:], tail, axis=1)
            out[:, 256:rows] = ends[:, 0 : rows - 256]
            if out_small is not None:
                last = done[hw:]
                out_small[0:hs, :] = last[:, 0:local]
                out_small[hs:, :] = pltpu.roll(last, local, axis=1)[:, 0:local]

    def block_rows(ref, size, index):
        return ref[pl.ds(pl.multiple_of(size * index, 8), size), :]

    second = GradSum(2, lambda k: stack([block_rows(r.dw2, rows, k), block_rows(r.dws, small, k)]))
    entry = GradSum(1, lambda k: block_rows(r.dw1, rows, k))
    second.begin()
    back_sums.advance()
    r.short[...] = nn(r.fpm[...], r.ws[...]) + out_bias
    r.dshort[...] = nt(r.dzc[...], r.ws[...])

    def conv2(phase, carry):
        a, c = lax.div(phase, 2), lax.rem(phase, 2)
        parts = [
            stack([tap_slice(r.h2s, a, c, dy, dx, im) for im in range(per)]) for dy, dx in taps()
        ]
        y = (nn(jnp.concatenate(parts, axis=1), r.w2[...]) + r.short[...]).astype(BF16)
        lanes = pl.ds(pl.multiple_of(256 * phase, 256), 256)
        for im in range(per):
            r.rc[im, :, lanes] = nt(r.ident[...], y[256 * im : 256 * im + 256]).astype(BF16)
        return carry

    lax.fori_loop(0, 4, conv2, 0)
    for im in range(per):
        for half in range(2):
            piece = jnp.concatenate(
                [r.rc[im, :, 256 * ph + 128 * half : 256 * ph + 128 * half + 128] for ph in range(4)],
                axis=1,
            )
            r.ocm[im, :, 512 * half : 512 * half + 512] = nn(piece, r.flatter[...]).astype(BF16)

    def own_channels(ref, index):
        return ref.at[:, pl.ds(pl.multiple_of(local * index, local), local), :]

    def give_back(ref, out):
        waits = [here(own_channels(ref, me), out.at[pl.ds(per * me, per)])]
        return waits + [
            post(
                own_channels(ref, peer),
                out.at[pl.ds(per * me, per)],
                out.at[pl.ds(per * peer, per)],
                dev(block, within, peer),
            )
            for peer in ch_peers
        ]

    out_waits = give_back(r.ocm, r.out)

    stats = back_sums.end()
    affine_grad2 = stats
    p1_b = [pick_row(stats[0:4], group[im]) / (4.0 * count) for im in range(per)]
    p2_b = [pick_row(stats[4:8], group[im]) / (4.0 * count) for im in range(per)]

    for im in range(per):
        span = slice(256 * im, 256 * im + 256)
        scale = gain * inv2_b[im]
        combos = []
        for a in range(2):
            grads = []
            for c in range(2):
                ph = 2 * a + c
                d = scale * (r.act[ph, span, :] - (p1_b[im] + r.y1[ph, span, :] * p2_b[im]))
                grads.append(d.astype(BF16))
            right = nn(r.shift[0], grads[0])
            left = nn(r.shift[1], grads[1])
            even, odd = grads[0].astype(F32), grads[1].astype(F32)
            combos.append((odd + right, even + odd, left + even))
        gap = jnp.zeros((16, chans), F32)
        for dx in range(3):
            upper, lower = combos[0][dx], combos[1][dx]
            r.field[dx, im] = (lower + stack([upper[16:], gap])).astype(BF16)
            r.field[3 + dx, im] = (upper + lower).astype(BF16)
            r.field[6 + dx, im] = (stack([gap, lower[:-16]]) + upper).astype(BF16)

    def grad1(tap, carry):
        first = pl.multiple_of(256 * tap, 256)
        r.dw1[pl.ds(first, 256), :] = nn(
            r.h1cm[...], stack([r.field[tap, im] for im in range(per)])
        )
        return carry

    lax.fori_loop(0, 9, grad1, 0)
    entry.begin()
    second.first()

    parts = [stack([r.field[tap, im] for im in range(per)]) for tap in range(9)]
    dh1 = nn(jnp.concatenate(parts, axis=1), r.w1t[...])
    payload = jnp.zeros((32, chans), F32)
    for im in range(per):
        span = slice(256 * im, 256 * im + 256)
        normal = (r.fpm[span, :].astype(F32) - mean1_b[im]) * inv1_b[im]
        pre = gamma_b[im] * normal + beta_b[im]
        sig = sigmoid(pre)
        act = dh1[span] * (sig * (1.0 + pre * (1.0 - sig)))
        r.act1[span, :] = act
        q1, q2 = colsum(act), colsum(act * normal)
        payload = payload + place_row(q2, label[im], 32)
        payload = payload + place_row(q1, label[im] + classes, 32)
        payload = payload + place_row(gamma_b[im] * q1, group[im] + 24, 32)
        payload = payload + place_row(gamma_b[im] * q2, group[im] + 28, 32)
    last_sums = AllReduce(4)
    last_sums.begin(payload)
    second.second()
    entry.first()
    last_sums.advance()
    second.third()
    last_sums.advance()
    entry.second()

    stats = last_sums.end()
    for im in range(per):
        span = slice(256 * im, 256 * im + 256)
        normal = (r.fpm[span, :].astype(F32) - mean1_b[im]) * inv1_b[im]
        r1 = pick_row(stats[24:28], group[im]) / count
        r2 = pick_row(stats[28:32], group[im]) / count
        grad = inv1_b[im] * (gamma_b[im] * r.act1[span, :] - (r1 + normal * r2))
        grad = (grad + r.dshort[span, :]).astype(BF16)
        r.dcm[im] = nt(r.ident[...], grad).astype(BF16)
    out_waits += give_back(r.dcm, r.dx)
    entry.third()
    second.end(r.grad2, r.grad3)

    table = jnp.zeros((24, chans), F32)
    table = table + jnp.where(iota((24, chans), 0) < 2 * classes, stats[0:24], 0.0)
    table = table + place_row(colsum(affine_grad2[4:8]), 2 * classes, 24)
    table = table + place_row(colsum(affine_grad2[0:4]), 2 * classes + 1, 24)
    table = table + place_row(affine_grad2[8:9], 2 * classes + 2, 24)
    mine = jnp.zeros((24, 128), F32)
    for c in range(n_ch):
        piece = table[:, 128 * (c // 2) : 128 * (c // 2) + 128]
        if c % 2:
            piece = pltpu.roll(piece, local, axis=1)
        mine = mine + jnp.where(me == c, piece, 0.0)
    r.affine_grad[...] = mine

    if inner == 1:
        row = iota((8, 128), 0)

        def norm_rows(index, weight, grad, v):
            for wait in held[index]:
                wait()
            master = weight[...]
            _, _, direction = adam_update(
                grad[...], getattr(r, v + "m")[...], getattr(r, v + "q")[...]
            )
            update = direction + WEIGHT_DECAY * master
            rows_w = jnp.where(row == index, total(master * master), 0.0)
            return rows_w + jnp.where(row == index + 3, total(update * update), 0.0)

        norms = norm_rows(1, r.exit_v, r.grad2, "v2") + norm_rows(2, r.bypass_v, r.grad3, "vs")
        entry.end(r.grad1)
        norms = norms + norm_rows(0, r.entry_v, r.grad1, "v1")
        norm_sums = AllReduce(5)
        norm_sums.begin(norms)
        r.norms[...] = norm_sums.end()
    else:
        entry.end(r.grad1)
        r.norms[...] = jnp.zeros((8, 128), F32)

    for wait in out_waits + pending:
        wait()
    cfg.used.append((slots.remote, slots.local))


def final_kernel(cfg, *refs):
    r = SimpleNamespace(**dict(zip(cfg.names, refs)))
    classes = cfg.classes
    local = cfg.local
    r.block_output[...] = r.out[...]
    r.input_gradient[...] = r.dx[...].astype(F32)
    norms = jnp.sqrt(r.norms[...])
    weight_norm, update_norm = norms[0:3, 0:1], norms[3:6, 0:1]
    ratio = weight_norm / update_norm
    at = iota((3, 3), 1)
    r.trust_norms[...] = jnp.where(
        at == 0, weight_norm, jnp.where(at == 1, update_norm, ratio)
    )
    sets = (
        (r.entry, r.entry_m, r.entry_q, r.entry_g, r.entry_1, r.entry_2, r.entry_w),
        (r.exit, r.exit_m, r.exit_q, r.exit_g, r.exit_1, r.exit_2, r.exit_w),
        (r.bypass, r.bypass_m, r.bypass_q, r.bypass_g, r.bypass_1, r.bypass_2, r.bypass_w),
    )
    for index, (weight, m, q, g, first, second, result) in enumerate(sets):
        master = weight[...]
        moment, square, direction = adam_update(g[...], m[...], q[...])
        update = direction + WEIGHT_DECAY * master
        first[...] = moment
        second[...] = square
        result[...] = master - MATRIX_RATE * ratio[index : index + 1] * update
    grad = r.affine_grad[0 : 2 * classes + 3, 0:local]
    moment, square, direction = adam_update(grad, r.affine_m[...], r.affine_q[...])
    r.affine_1[...] = moment
    r.affine_2[...] = square
    r.affine_w[...] = r.affine[...] - AFFINE_RATE * direction


def per_device(
    features,
    labels,
    groups,
    widths,
    entry_conv,
    entry_moment,
    entry_square,
    exit_conv,
    exit_moment,
    exit_square,
    bypass_conv,
    bypass_moment,
    bypass_square,
    norm_affine,
    norm_moment,
    norm_square,
    cotangent,
):
    n_img, n_ch = lax.axis_size("img"), lax.axis_size("ch")
    batch, local, pixels = features.shape
    chans = local * n_ch
    side = math.isqrt(pixels)
    inner = n_img // OUTER
    classes = (norm_affine.shape[0] - 3) // 2
    per = batch // n_ch
    assert (side, chans, n_ch, local, batch % n_ch) == (16, 256, 4, 64, 0)
    rows, small = entry_conv.shape[0] * inner, bypass_conv.shape[0] * inner
    masters = (entry_conv, exit_conv, bypass_conv)
    if inner == 1:
        blocks = masters
    else:
        sets = [[o * inner + i for i in range(inner)] for o in range(OUTER)]
        blocks = tuple(
            lax.all_gather(w.astype(BF16), "img", axis=0, tiled=True, axis_index_groups=sets)
            for w in masters
        )

    vmem = pl.BlockSpec(memory_space=pltpu.VMEM)
    smem = pl.BlockSpec(memory_space=pltpu.SMEM)
    anywhere = pl.BlockSpec(memory_space=pl.ANY)
    states = dict(
        entry_m=entry_moment.T,
        entry_q=entry_square.T,
        exit_m=exit_moment.T,
        exit_q=exit_square.T,
        bypass_m=bypass_moment,
        bypass_q=bypass_square,
    )
    inputs = dict(
        labels=(labels, smem),
        groups=(groups, smem),
        widths=(widths, smem),
        features=(features, anywhere),
        cotangent=(cotangent, anywhere),
        entry=(blocks[0].T, anywhere),
        exit=(blocks[1].T, anywhere),
        bypass=(blocks[2], anywhere),
        affine=(norm_affine, anywhere),
    )
    if inner == 1:
        inputs.update({name: (value, anywhere) for name, value in states.items()})
    sds = jax.ShapeDtypeStruct
    outputs = dict(
        out=(sds(cotangent.shape, BF16), vmem),
        dx=(sds(features.shape, BF16), vmem),
        grad1=(sds((local, rows), F32), vmem),
        grad2=(sds((local, rows), F32), vmem),
        grad3=(sds((small, local), F32), vmem),
        affine_grad=(sds((24, 128), F32), vmem),
        norms=(sds((8, 128), F32), vmem),
    )
    pix = pixels * per
    taps9 = 9 * chans
    held = lambda shape, dtype=BF16: pltpu.VMEM(shape, dtype)
    scratch = dict(
        fown=held((batch, local, pixels)),
        cown=held((batch, local, 4 * pixels)),
        fbuf=held((n_ch, per, local, pixels)),
        cbuf=held((n_ch, per, local, 4 * pixels)),
        entry_v=held((local, rows), blocks[0].dtype),
        exit_v=held((local, rows), blocks[1].dtype),
        bypass_v=held((small, local), blocks[2].dtype),
        affine_v=held(norm_affine.shape, F32),
        padded=held((3 * local, 384)),
        wz=held((n_ch, rows + small // 2, 128)),
        g1=held((2, 2, 2, rows, chans)),
        g2=held((2, 2, 2, rows + small, chans)),
        aff_z=held((n_ch, 32, 128), F32),
        padsum=held((8, 128), F32),
        w1=held((taps9, chans)),
        w2=held((taps9, chans)),
        ws=held((chans, chans)),
        w1t=held((taps9, chans)),
        w2t=held((taps9, chans)),
        unpack=held((512, 512)),
        ident=held((256, 256)),
        shift=held((2, 256, 256)),
        gridder=held((512, 256)),
        flatter=held((512, 512)),
        fpm=held((pix, chans)),
        h1s=held((3, per, pixels + 32, chans)),
        h1cm=held((chans, pix)),
        y1=held((4, pix, chans), F32),
        act=held((4, pix, chans), F32),
        h2s=held((2, 4, per, pixels + 32, chans)),
        dzs=held((2, 4, per, pixels + 32, chans)),
        h2cm=held((chans, 4 * pix)),
        short=held((pix, chans), F32),
        dshort=held((pix, chans), F32),
        dzc=held((pix, chans)),
        act1=held((pix, chans), F32),
        rc=held((per, chans, 4 * pixels)),
        ocm=held((per, chans, 4 * pixels)),
        dcm=held((per, chans, pixels)),
        field=held((9, per, pixels, chans)),
        dw1=held((taps9, chans), F32),
        dw2=held((taps9, chans), F32),
        dws=held((chans, chans), F32),
    )
    for number, size in ((1, rows), (2, rows + small)):
        shapes = ((4, size, chans),) * 2 + ((2, 2, size, 128),) * 2 + ((2, size, 128),) * 2
        shapes += ((n_ch, size // 2, 128),) * 2
        for part, shape in zip(PARTS, shapes):
            scratch[part + str(number)] = held(shape)
        scratch[PARTS[-1] + str(number)] = held((4, size, chans), F32)
    exchanges = [(8, 128), (8, chans), (16, chans), (32, chans)]
    if inner == 1:
        exchanges.append((8, 128))
        for v, shape in (("v1", (local, rows)), ("v2", (local, rows)), ("vs", (small, local))):
            scratch[v + "m"] = held(shape, F32)
            scratch[v + "q"] = held(shape, F32)
    for number, shape in enumerate(exchanges, 1):
        for part, size in zip("abc", (5, 5, inner)):
            scratch[part + str(number)] = held((size,) + shape, F32)
    remote_count = 6 * 3 + 2 * 5 + 2 * 8 + len(exchanges) * (5 + inner - 1)
    scratch.update(
        send=pltpu.SemaphoreType.DMA((remote_count,)),
        recv=pltpu.SemaphoreType.DMA((remote_count,)),
        lsem=pltpu.SemaphoreType.DMA((20,)),
    )
    cfg = SimpleNamespace(
        names=[*inputs, *outputs, *scratch],
        inner=inner,
        n_ch=n_ch,
        batch=batch,
        local=local,
        classes=classes,
        count=float(batch * n_img // widths.shape[0] * pixels),
        rows=rows,
        small=small,
        used=[],
    )
    out, dx, grad1, grad2, grad3, affine_grad, norms = pl.pallas_call(
        functools.partial(main_kernel, cfg),
        out_shape=[s for s, _ in outputs.values()],
        in_specs=[s for _, s in inputs.values()],
        out_specs=[s for _, s in outputs.values()],
        scratch_shapes=list(scratch.values()),
        compiler_params=pltpu.CompilerParams(
            collective_id=0, has_side_effects=True, vmem_limit_bytes=VMEM_LIMIT
        ),
        name="block_step",
    )(*[v for v, _ in inputs.values()])
    assert max(n for n, _ in cfg.used) <= remote_count and max(n for _, n in cfg.used) <= 20

    grads = [grad1, grad2, grad3]
    if inner > 1:
        grads = [
            lax.psum_scatter(g, "img", scatter_dimension=0, axis_index_groups=sets, tiled=True)
            for g in (grad1.T, grad2.T, grad3)
        ]
        updates = []
        for w, g, m, s in zip(
            masters,
            grads,
            (entry_moment, exit_moment, bypass_moment),
            (entry_square, exit_square, bypass_square),
        ):
            updates.append(adam_update(g, m, s)[2] + WEIGHT_DECAY * w)
        sums = lax.psum(
            jnp.stack([jnp.sum(w * w) for w in masters] + [jnp.sum(u * u) for u in updates]),
            ("img", "ch"),
        )
        norms = jnp.broadcast_to(jnp.pad(sums, (0, 2))[:, None], (8, 128))
        grads = [grads[0].T, grads[1].T, grads[2]]

    args = dict(
        out=out,
        dx=dx,
        norms=norms,
        affine_grad=affine_grad,
        entry_g=grads[0],
        exit_g=grads[1],
        bypass_g=grads[2],
        entry=entry_conv.T,
        exit=exit_conv.T,
        bypass=bypass_conv,
        **states,
        affine=norm_affine,
        affine_m=norm_moment,
        affine_q=norm_square,
    )
    tall = sds(entry_conv.shape[::-1], F32)
    short, wide = (sds(w.shape, F32) for w in (bypass_conv, norm_affine))
    results = dict(
        block_output=sds(cotangent.shape, BF16),
        input_gradient=sds(features.shape, F32),
        entry_1=tall,
        entry_2=tall,
        entry_w=tall,
        exit_1=tall,
        exit_2=tall,
        exit_w=tall,
        bypass_1=short,
        bypass_2=short,
        bypass_w=short,
        affine_1=wide,
        affine_2=wide,
        affine_w=wide,
        trust_norms=sds((3, 3), F32),
    )
    end_cfg = SimpleNamespace(names=[*args, *results], classes=classes, local=local)
    final = pl.pallas_call(
        functools.partial(final_kernel, end_cfg),
        out_shape=list(results.values()),
        in_specs=[vmem] * len(args),
        out_specs=[vmem] * len(results),
        compiler_params=pltpu.CompilerParams(vmem_limit_bytes=VMEM_LIMIT),
        name="finish",
    )(*args.values())
    return tuple(v.T if s is tall else v for v, s in zip(final, results.values()))


def solution(mesh):
    wide = P("img", "ch")
    deep = P("img", "ch", None)
    table = P(None, "ch")
    return jax.shard_map(
        per_device,
        mesh=mesh,
        in_specs=(deep, P("img"), P("img"), P()) + (wide,) * 9 + (table,) * 3 + (deep,),
        out_specs=(deep, deep) + (wide,) * 9 + (table,) * 3 + (P(),),
        check_vma=False,
    )
```

```python
import functools
import math
from types import SimpleNamespace

import jax
import jax.numpy as jnp
from jax import lax
from jax.experimental import pallas as pl
from jax.experimental.pallas import tpu as pltpu
from jax.sharding import PartitionSpec as P

LEVELS = 4
STEP = 5
NORM_EPSILON = 1e-05
ADAM_EPSILON = 1e-06
MOMENT_DECAY = 0.9
SQUARE_DECAY = 0.999
WEIGHT_DECAY = 0.01
MATRIX_RATE = 0.3
AFFINE_RATE = 0.2

OUTER = 8
VMEM_LIMIT = 56 * 1024 * 1024
BF16 = jnp.bfloat16
F32 = jnp.float32
MESH = pl.DeviceIdType.MESH
PARTS = ("s1", "r1", "s2", "r2", "s3", "r3", "s4", "r4", "acc")


def nn(left, right):
    return lax.dot_general(left, right, (((1,), (0,)), ((), ())), preferred_element_type=F32)


def nt(left, right):
    return lax.dot_general(left, right, (((1,), (1,)), ((), ())), preferred_element_type=F32)


def flip(index, mask):
    result = index
    for bit in range(3):
        if (mask >> bit) & 1:
            digit = lax.rem(lax.div(index, 1 << bit), 2)
            result = result + (1 - 2 * digit) * (1 << bit)
    return result


def sigmoid(value):
    return 0.5 * jnp.tanh(0.5 * value) + 0.5


def iota(shape, axis):
    return lax.broadcasted_iota(jnp.int32, shape, axis)


def to_bf16(condition):
    return jnp.where(condition, 1.0, 0.0).astype(BF16)


def pick_row(table, index):
    hit = iota(table.shape, 0) == index
    return jnp.sum(jnp.where(hit, table, 0.0), axis=0, keepdims=True)


def place_row(row, index, rows):
    hit = iota((rows, row.shape[1]), 0) == index
    return jnp.where(hit, row, 0.0)


def colsum(value):
    return jnp.sum(value, axis=0, keepdims=True)


def adam_update(grad, moment, square):
    moment_new = MOMENT_DECAY * moment + (1.0 - MOMENT_DECAY) * grad
    square_new = SQUARE_DECAY * square + (1.0 - SQUARE_DECAY) * grad * grad
    direction = (
        moment_new
        / (1.0 - MOMENT_DECAY**STEP)
        / (jnp.sqrt(square_new / (1.0 - SQUARE_DECAY**STEP)) + ADAM_EPSILON)
    )
    return (moment_new, square_new, direction)


def total(value):
    return jnp.sum(jnp.sum(value, axis=1, keepdims=True), axis=0, keepdims=True)


def main_kernel(cfg, *refs):
    r = SimpleNamespace(**dict(zip(cfg.names, refs)))
    inner, n_ch, batch, local = cfg.inner, cfg.n_ch, cfg.batch, cfg.local
    classes, count = cfg.classes, cfg.count
    per = batch // n_ch
    chans = local * n_ch
    rows, small = cfg.rows, cfg.small
    tail = (rows - 256) // 2
    hw, hs = rows // 2, small // 2
    slots = SimpleNamespace(remote=0, local=0)

    img = lax.axis_index("img")
    me = lax.axis_index("ch")
    block = lax.div(img, inner)
    within = lax.rem(img, inner)
    core = lax.rem(block, 2)
    plane = lax.div(block, 2)
    bit_x, bit_y = lax.rem(plane, 2), lax.div(plane, 2)
    partner = flip(block, 1)

    def dev(block_id, within_id, ch_id):
        return (block_id * inner + within_id, ch_id)

    pending = []

    def post(src, dst, landed, peer):
        slot = slots.remote
        slots.remote = slot + 1
        copy = pltpu.make_async_remote_copy(
            src_ref=src,
            dst_ref=dst,
            send_sem=r.send.at[slot],
            recv_sem=r.recv.at[slot],
            device_id=peer,
            device_id_type=MESH,
        )
        copy.start()
        pending.append(copy.wait_send)
        arrival = pltpu.make_async_remote_copy(
            src_ref=landed,
            dst_ref=landed,
            send_sem=r.send.at[slot],
            recv_sem=r.recv.at[slot],
            device_id=peer,
            device_id_type=MESH,
        )
        return arrival.wait_recv

    def here(src, dst):
        slot = slots.local
        slots.local = slot + 1
        copy = pltpu.make_async_copy(src, dst, r.lsem.at[slot])
        copy.start()
        return copy.wait

    outer_peers = [flip(block, mask) for mask in range(1, OUTER)]
    ch_peers = [flip(me, mask) for mask in range(1, n_ch)]
    inner_pairs = [
        (lax.rem(within + step, inner), lax.rem(within + inner - step, inner))
        for step in range(1, inner)
    ]
    barrier = pltpu.get_barrier_semaphore()
    everyone = [dev(peer, within, me) for peer in outer_peers]
    everyone += [dev(block, within, peer) for peer in ch_peers]
    everyone += [dev(block, peer, me) for peer, _ in inner_pairs]
    for peer in everyone:
        pl.semaphore_signal(barrier, inc=1, device_id=peer, device_id_type=MESH)

    got_entry = here(r.entry, r.entry_v)
    got_features = here(r.features, r.fown)
    got_exit = here(r.exit, r.exit_v)
    got_bypass = here(r.bypass, r.bypass_v)
    got_affine = here(r.affine, r.affine_v)
    got_cot = here(r.cotangent, r.cown)
    states = ((r.entry_m, r.entry_q), (r.exit_m, r.exit_q), (r.bypass_m, r.bypass_q)) if inner == 1 else ()
    held = [
        (here(m, getattr(r, v + "m")), here(q, getattr(r, v + "q")))
        for (m, q), v in zip(states, ("v1", "v2", "vs"))
    ]

    s_row, s_col = iota((hw, 384), 0), iota((hw, 384), 1)
    pick_first = to_bf16(s_col == jnp.where(s_row < 128, s_row, s_row + 128))
    pick_second = to_bf16(s_col == jnp.where(s_row < 128, s_row + 128, s_row + 128 + tail))
    r.padded[...] = jnp.zeros(r.padded.shape, BF16)

    def pack_own(value):
        r.padded[local : 2 * local, 0:rows] = value.astype(BF16)
        packed = nt(pick_first, r.padded[local : 3 * local, :])
        return (packed + nt(pick_second, r.padded[0 : 2 * local, :])).astype(BF16)

    got_entry()
    r.wz1[me] = pack_own(r.entry_v[...])
    pl.semaphore_wait(barrier, len(everyone))

    def to_channels(buffer):
        return [
            post(buffer.at[me], buffer.at[me], buffer.at[peer], dev(block, within, peer))
            for peer in ch_peers
        ]

    entry_waits = to_channels(r.wz1)
    got_features()
    feature_waits = [
        post(
            r.fown.at[pl.ds(per * peer, per)],
            r.fbuf.at[me],
            r.fbuf.at[peer],
            dev(block, within, peer),
        )
        for peer in ch_peers
    ]
    got_affine()
    r.aff_z[me] = jnp.zeros((24, 128), F32)
    r.aff_z[me, 0 : 2 * classes + 3, 0:local] = r.affine_v[...]
    affine_waits = to_channels(r.aff_z)

    lane = iota((512, 512), 0)
    column = iota((512, 512), 1)
    spot = 256 * ((lane >> 6) & 1) + 64 * (lane >> 7) + (lane & 63)
    r.unpack[...] = to_bf16(column == spot)

    r.fbuf[me] = r.fown[pl.ds(per * me, per)]
    flat = jnp.concatenate([r.fown[b] for b in range(batch)], axis=1)
    wide = flat.astype(F32)
    square = wide * wide
    square_hi = square.astype(BF16)
    square_lo = (square - square_hi.astype(F32)).astype(BF16)
    level = iota((16, 256), 0)
    first_mask = jnp.concatenate([to_bf16(level == r.groups[b]) for b in range(batch)], axis=1)
    second_mask = jnp.concatenate([to_bf16(level == r.groups[b] + 4) for b in range(batch)], axis=1)
    sums = nt(first_mask, flat) + nt(second_mask, square_hi) + nt(second_mask, square_lo)

    def ordered_sum(ref, size):
        result = ref[0]
        for slot in range(1, size):
            result = result + ref[slot]
        return result

    class AllReduce:
        def __init__(self, number):
            self.over_outer, self.over_inner, self.over_ch = (
                getattr(r, axis + str(number), None) for axis in "abc"
            )

        def begin(self, value, masked=None):
            ref = self.over_outer
            if masked is None:
                ref[block] = value
            else:
                ref[block] = jnp.zeros(ref.shape[1:], F32)
                ref[block, :, 0:masked] = value
            self.waits = [
                post(ref.at[block], ref.at[block], ref.at[peer], dev(peer, within, me))
                for peer in outer_peers
            ]

        def middle(self):
            for wait in self.waits:
                wait()
            value = ordered_sum(self.over_outer, OUTER)
            if inner > 1:
                ref = self.over_inner
                ref[within] = value
                waits = [
                    post(ref.at[within], ref.at[within], ref.at[back], dev(block, peer, me))
                    for peer, back in inner_pairs
                ]
                for wait in waits:
                    wait()
                value = ordered_sum(ref, inner)
            self.over_ch[me] = value
            self.waits = to_channels(self.over_ch)

        def finish(self):
            for wait in self.waits:
                wait()
            return self.over_ch

        def end(self):
            return ordered_sum(self.finish(), n_ch)

    input_sums = AllReduce(1)
    input_sums.begin(sums[0:8], masked=local)

    got_exit()
    got_bypass()
    r.wz2[me, 0:hw, :] = pack_own(r.exit_v[...])
    e_row, e_col = iota((local, 128), 0), iota((local, 128), 1)
    value = r.bypass_v[...].astype(BF16)
    r.wz2[me, hw : hw + hs, :] = (
        nn(value[:hs], to_bf16(e_col == e_row)) + nn(value[hs:], to_bf16(e_col == e_row + local))
    ).astype(BF16)

    def rows_of(ref, index):
        size = ref.shape[0] // OUTER
        return ref.at[pl.ds(pl.multiple_of(size * index, 16), size)]

    def unpack_own(ref, full):
        own = rows_of(ref, block)
        if full.shape[0] == hw:
            own[0:128, :] = full[0:128, 0:256]
            own[128:256, :] = full[0:128, 256:512]
            own[256 : 256 + tail, :] = full[128:, 0:256]
            own[256 + tail :, :] = full[128:, 256:512]
        else:
            own[0:hs, :] = full[:, 0:256]
            own[hs:, :] = full[:, 256:512]

    def spread(ref):
        own = rows_of(ref, block)
        return {
            mask: post(own, own, rows_of(ref, flip(block, mask)), dev(flip(block, mask), within, me))
            for mask in (2, 4, 6, 1)
        }

    def forward(ref, waits):
        rest = [waits[1]]
        for mask in (2, 4, 6):
            waits[mask]()
            mine = rows_of(ref, flip(block, mask))
            theirs = rows_of(ref, flip(partner, mask))
            rest.append(post(mine, mine, theirs, dev(partner, within, me)))
        return rest

    def widen(buffer):
        packed = jnp.concatenate([buffer[c] for c in range(n_ch)], axis=1)
        return nn(packed, r.unpack[...]).astype(BF16)

    for wait in entry_waits:
        wait()
    unpack_own(r.w1, widen(r.wz1))
    gather1 = spread(r.w1)
    exit_waits = to_channels(r.wz2)

    ident = to_bf16(iota((256, 256), 0) == iota((256, 256), 1))
    r.ident[...] = ident
    q_out, q_in = iota((256, 256), 0), iota((256, 256), 1)
    r.shift[0] = to_bf16((q_in == q_out + 1) & ((q_out & 15) < 15))
    r.shift[1] = to_bf16((q_in == q_out - 1) & ((q_out & 15) > 0))

    input_sums.middle()
    got_cot()
    cot_waits = [
        post(
            r.cown.at[per * peer + im],
            r.cbuf.at[me, im],
            r.cbuf.at[peer, im],
            dev(block, within, peer),
        )
        for im in range(per)
        for peer in ch_peers
    ]

    rho, px = iota((512, 256), 0), iota((512, 256), 1)
    version, a, b_ = rho >> 8, (rho >> 7) & 1, (rho >> 6) & 1
    col = (rho & 15) + version * (1 - 2 * b_)
    target = (2 * ((rho & 63) >> 4) + a) * 32 + 2 * col + b_
    r.gridder[...] = to_bf16((px == target) & (col >= 0) & (col < 16))
    target = (
        (2 * ((lane & 127) >> 4) + (lane >> 8)) * 32 + 2 * (lane & 15) + ((lane >> 7) & 1)
    )
    r.flatter[...] = to_bf16(column == target)
    zeros = jnp.zeros((16, 256), BF16)
    for im in range(per):
        for ver in range(3):
            r.h1s[ver, im, 0:16, :] = zeros
            r.h1s[ver, im, 272:288, :] = zeros
        for ver in range(2):
            for ph in range(4):
                for ref in (r.h2s, r.dzs):
                    ref[ver, ph, im, 0:16, :] = zeros
                    ref[ver, ph, im, 272:288, :] = zeros

    def channel_major(ref, im, lanes):
        return jnp.concatenate([ref[c, im, :, lanes] for c in range(n_ch)], axis=0)

    for wait in feature_waits:
        wait()
    for im in range(per):
        r.fpm[256 * im : 256 * im + 256, :] = nt(
            ident, channel_major(r.fbuf, im, slice(0, 256))
        ).astype(BF16)

    def wide_lanes(ref):
        parts = [
            ref[c] + pltpu.roll(ref[c + 1], local, axis=1) for c in range(0, n_ch, 2)
        ]
        return jnp.concatenate(parts, axis=1)

    for wait in affine_waits:
        wait()
    affine = wide_lanes(r.aff_z)
    stats = wide_lanes(input_sums.finish())
    mean1 = stats[0:4] / count
    inv1 = lax.rsqrt(stats[4:8] / count - mean1 * mean1 + NORM_EPSILON)
    gain = affine[2 * classes : 2 * classes + 1]
    shift = affine[2 * classes + 1 : 2 * classes + 2]
    out_bias = affine[2 * classes + 2 : 2 * classes + 3]
    group, label, mean1_b, inv1_b, gamma_b, beta_b, mask_b = [], [], [], [], [], [], []
    for im in range(per):
        group.append(r.groups[per * me + im])
        label.append(r.labels[per * me + im])
        mean1_b.append(pick_row(mean1, group[im]))
        inv1_b.append(pick_row(inv1, group[im]))
        gamma_b.append(pick_row(affine, label[im]))
        beta_b.append(pick_row(affine, label[im] + classes))
        width = r.widths[group[im]]
        mask_b.append(
            jnp.where(iota((1, chans), 1) < width * (chans // LEVELS), 1.0, 0.0)
        )

    for im in range(per):
        normal = (r.fpm[256 * im : 256 * im + 256, :].astype(F32) - mean1_b[im]) * inv1_b[im]
        pre = gamma_b[im] * normal + beta_b[im]
        hidden = (pre * sigmoid(pre)).astype(BF16)
        r.h1s[1, im, 16:272, :] = hidden
        r.h1s[0, im, 16:272, :] = nn(r.shift[1], hidden).astype(BF16)
        r.h1s[2, im, 16:272, :] = nn(r.shift[0], hidden).astype(BF16)
        r.h1cm[:, 256 * im : 256 * im + 256] = nt(ident, hidden).astype(BF16)

    for wait in exit_waits:
        wait()
    full = widen(r.wz2)
    unpack_own(r.w2, full[0:hw])
    unpack_own(r.ws, full[hw:])
    rest = forward(r.w1, gather1)
    gather2 = spread(r.w2)
    gather3 = spread(r.ws)
    for wait in rest:
        wait()

    def taps():
        return [(dy, dx) for dy in range(3) for dx in range(3)]

    def stack(pieces):
        return jnp.concatenate(pieces, axis=0)

    def conv1(phase, carry):
        a, c = lax.div(phase, 2), lax.rem(phase, 2)
        parts = []
        for dy, dx in taps():
            first = pl.multiple_of(16 * lax.div(a + dy + 1, 2), 16)
            ver = lax.div(c + dx + 1, 2)
            parts.append(
                stack([r.h1s[ver, im, pl.ds(first, 256), :] for im in range(per)])
            )
        y = nn(jnp.concatenate(parts, axis=1), r.w1[...])
        r.y1[phase] = y
        out = []
        for im in range(per):
            piece = y[256 * im : 256 * im + 256]
            out.append(carry[2 * im] + colsum(piece))
            out.append(carry[2 * im + 1] + colsum(piece * piece))
        return tuple(out)

    nought = jnp.zeros((1, chans), F32)
    mid = lax.fori_loop(0, 4, conv1, (nought,) * (2 * per))
    payload = jnp.zeros((8, chans), F32)
    for im in range(per):
        payload = payload + place_row(mid[2 * im], group[im], 8)
        payload = payload + place_row(mid[2 * im + 1], group[im] + 4, 8)
    mid_sums = AllReduce(2)
    mid_sums.begin(payload)

    def turn(src, dst):
        def one(tap, carry):
            first = pl.multiple_of(256 * tap, 256)
            dst[pl.ds(first, 256), :] = nt(r.ident[...], src[pl.ds(first, 256), :]).astype(BF16)
            return carry

        lax.fori_loop(0, 9, one, 0)

    turn(r.w1, r.w1t)
    rest = forward(r.w2, gather2) + forward(r.ws, gather3)
    mid_sums.middle()

    r.cbuf[me] = r.cown[pl.ds(per * me, per)]
    for wait in cot_waits:
        wait()
    for im in range(per):
        for n in range(4):
            piece = channel_major(r.cbuf, im, slice(256 * n, 256 * n + 256))
            grid = nt(r.gridder[...], piece).astype(BF16)
            for ver in range(2):
                for ph in range(4):
                    at = 256 * ver + 64 * ph
                    r.dzs[ver, ph, im, 16 + 64 * n : 80 + 64 * n, :] = grid[at : at + 64]

    coarse = jnp.zeros((256 * per, chans), F32)
    for ph in range(4):
        coarse = coarse + stack([r.dzs[0, ph, im, 16:272, :] for im in range(per)]).astype(F32)
    bias_sum = colsum(coarse)
    r.dzc[...] = coarse.astype(BF16)

    def tap_slice(ref, a, c, dy, dx, im):
        row, colm = a + dy + 1, c + dx + 1
        first = pl.multiple_of(16 * lax.div(row, 2), 16)
        ph = 2 * lax.rem(row, 2) + lax.rem(colm, 2)
        side_step = lax.div(colm, 2) - 1
        return ref[side_step * side_step, ph, im, pl.ds(first, 256), :]

    for wait in rest:
        wait()
    turn(r.w2, r.w2t)

    def back2(phase, carry):
        a, c = lax.div(phase, 2), lax.rem(phase, 2)
        parts = [
            stack([tap_slice(r.dzs, a, c, 2 - dy, 2 - dx, im) for im in range(per)])
            for dy, dx in taps()
        ]
        r.act[phase] = nn(jnp.concatenate(parts, axis=1), r.w2t[...])
        return carry

    lax.fori_loop(0, 4, back2, 0)

    stats = mid_sums.end()
    mean2 = stats[0:4] / (4.0 * count)
    inv2 = lax.rsqrt(stats[4:8] / (4.0 * count) - mean2 * mean2 + NORM_EPSILON)
    mean2_b = [pick_row(mean2, group[im]) for im in range(per)]
    inv2_b = [pick_row(inv2, group[im]) for im in range(per)]

    def hidden2(phase, carry):
        c = lax.rem(phase, 2)
        out = []
        for im in range(per):
            span = slice(256 * im, 256 * im + 256)
            normal = (r.y1[phase, span, :] - mean2_b[im]) * inv2_b[im]
            r.y1[phase, span, :] = normal
            pre = gain * normal + shift
            sig = sigmoid(pre)
            hidden = (pre * sig * mask_b[im]).astype(BF16)
            act = r.act[phase, span, :] * (sig * (1.0 + pre * (1.0 - sig)) * mask_b[im])
            r.act[phase, span, :] = act
            out.append(carry[2 * im] + colsum(act))
            out.append(carry[2 * im + 1] + colsum(act * normal))
            r.h2s[0, phase, im, 16:272, :] = hidden
            r.h2s[1, phase, im, 16:272, :] = nn(r.shift[c], hidden).astype(BF16)
            lanes = pl.ds(pl.multiple_of(512 * phase + 256 * im, 256), 256)
            r.h2cm[:, lanes] = nt(r.ident[...], hidden).astype(BF16)
        return tuple(out)

    mid = lax.fori_loop(0, 4, hidden2, (nought,) * (2 * per))
    payload = place_row(bias_sum, 8, 16)
    for im in range(per):
        payload = payload + place_row(mid[2 * im], group[im], 16)
        payload = payload + place_row(mid[2 * im + 1], group[im] + 4, 16)
    back_sums = AllReduce(3)
    back_sums.begin(payload)

    def grad2(tap, carry):
        dy, dx = lax.div(tap, 3), lax.rem(tap, 3)
        pieces = []
        for ph in range(4):
            a, c = ph // 2, ph % 2
            for im in range(per):
                pieces.append(tap_slice(r.dzs, a, c, 2 - dy, 2 - dx, im))
        first = pl.multiple_of(256 * tap, 256)
        r.dw2[pl.ds(first, 256), :] = nn(r.h2cm[...], stack(pieces))
        return carry

    lax.fori_loop(0, 9, grad2, 0)
    back_sums.middle()
    for im in range(per):
        piece = channel_major(r.fbuf, im, slice(0, 256))
        grad = nn(piece, r.dzc[256 * im : 256 * im + 256, :])
        if im == 0:
            r.dws[...] = grad
        else:
            r.dws[...] = r.dws[...] + grad

    class GradSum:
        def __init__(self, number, fetch):
            self.fetch = fetch
            for part in PARTS:
                setattr(self, part, getattr(r, part + str(number)))

        def begin(self):
            self.waits = []
            for u in range(4):
                self.s1[u] = self.fetch(2 * u + 1 - core).astype(BF16)
                self.waits.append(
                    post(self.s1.at[u], self.r1.at[u], self.r1.at[u], dev(partner, within, me))
                )

        def settle(self):
            for wait in self.waits:
                wait()

        def across(self, send, got, masks):
            parts = [(h, v) for v in range(2) for h in range(2)] if len(send.shape) == 4 else [(0,), (1,)]
            self.waits = [
                post(send.at[p], got.at[p], got.at[p], dev(flip(block, masks[p[0]]), within, me))
                for p in parts
            ]

        def first(self):
            for u in range(4):
                self.waits[u]()
                self.acc[u] = self.fetch(2 * u + core) + self.r1[u].astype(F32)
            for v in range(2):
                self.s2[0, v] = self.acc[2 * v + 1 - bit_x, :, 0:128].astype(BF16)
                self.s2[1, v] = self.acc[2 * (1 - bit_y) + v, :, 128:256].astype(BF16)
            self.across(self.s2, self.r2, (2, 4))

        def second(self):
            self.settle()
            low = self.acc[2 * (1 - bit_y) + bit_x, :, 0:128] + self.r2[0, 1 - bit_y].astype(F32)
            high = self.acc[2 * bit_y + 1 - bit_x, :, 128:256] + self.r2[1, 1 - bit_x].astype(F32)
            self.s3[0] = low.astype(BF16)
            self.s3[1] = high.astype(BF16)
            self.across(self.s3, self.r3, (4, 2))

        def third(self):
            self.settle()
            low = self.acc[plane, :, 0:128] + self.r2[0, bit_y].astype(F32)
            high = self.acc[plane, :, 128:256] + self.r2[1, bit_x].astype(F32)
            low, high = low + self.r3[0].astype(F32), high + self.r3[1].astype(F32)
            value = jnp.concatenate([low, high], axis=1).astype(BF16)
            left = [value[0:128], value[256 : 256 + tail]]
            right = [value[128:256], value[256 + tail : rows]]
            if value.shape[0] > rows:
                left.append(value[rows : rows + hs])
                right.append(value[rows + hs :])
            pair = jnp.concatenate([stack(left), stack(right)], axis=1)
            packed = nt(pair, r.unpack[...]).astype(BF16)
            for c in range(n_ch):
                self.s4[c] = packed[:, 128 * c : 128 * c + 128]
            self.r4[me] = self.s4[me]
            self.waits = [
                post(self.s4.at[peer], self.r4.at[me], self.r4.at[peer], dev(block, within, peer))
                for peer in ch_peers
            ]

        def end(self, out, out_small=None):
            self.settle()
            done = self.r4[0].astype(F32)
            for c in range(1, n_ch):
                done = done + self.r4[c].astype(F32)
            turned = done[0:128].T
            out[:, 0:128] = turned[0:local]
            out[:, 128:256] = turned[local:]
            gap = jnp.zeros((128 - tail, 128), F32)
            turned = stack([done[128 : 128 + tail], gap]).T
            ends = turned[0:local] + pltpu.roll(turned[local:], tail, axis=1)
            out[:, 256:rows] = ends[:, 0 : rows - 256]
            if out_small is not None:
                last = done[hw:]
                out_small[0:hs, :] = last[:, 0:local]
                out_small[hs:, :] = pltpu.roll(last, local, axis=1)[:, 0:local]

    def block_rows(ref, size, index):
        return ref[pl.ds(pl.multiple_of(size * index, 8), size), :]

    second = GradSum(2, lambda k: stack([block_rows(r.dw2, rows, k), block_rows(r.dws, small, k)]))
    entry = GradSum(1, lambda k: block_rows(r.dw1, rows, k))
    second.begin()
    r.short[...] = nn(r.fpm[...], r.ws[...]) + out_bias
    r.dshort[...] = nt(r.dzc[...], r.ws[...])

    def conv2(phase, carry):
        a, c = lax.div(phase, 2), lax.rem(phase, 2)
        parts = [
            stack([tap_slice(r.h2s, a, c, dy, dx, im) for im in range(per)]) for dy, dx in taps()
        ]
        y = (nn(jnp.concatenate(parts, axis=1), r.w2[...]) + r.short[...]).astype(BF16)
        lanes = pl.ds(pl.multiple_of(256 * phase, 256), 256)
        for im in range(per):
            r.rc[im, :, lanes] = nt(r.ident[...], y[256 * im : 256 * im + 256]).astype(BF16)
        return carry

    lax.fori_loop(0, 4, conv2, 0)
    for im in range(per):
        for half in range(2):
            piece = jnp.concatenate(
                [r.rc[im, :, 256 * ph + 128 * half : 256 * ph + 128 * half + 128] for ph in range(4)],
                axis=1,
            )
            r.ocm[im, :, 512 * half : 512 * half + 512] = nn(piece, r.flatter[...]).astype(BF16)

    def own_channels(ref, index, im):
        return ref.at[im, pl.ds(pl.multiple_of(local * index, local), local), :]

    def give_back(ref, out):
        waits = [here(own_channels(ref, me, im), out.at[per * me + im]) for im in range(per)]
        return waits + [
            post(
                own_channels(ref, peer, im),
                out.at[per * me + im],
                out.at[per * peer + im],
                dev(block, within, peer),
            )
            for im in range(per)
            for peer in ch_peers
        ]

    out_waits = give_back(r.ocm, r.out)

    stats = back_sums.end()
    affine_grad2 = stats
    p1_b = [pick_row(stats[0:4], group[im]) / (4.0 * count) for im in range(per)]
    p2_b = [pick_row(stats[4:8], group[im]) / (4.0 * count) for im in range(per)]

    for im in range(per):
        span = slice(256 * im, 256 * im + 256)
        scale = gain * inv2_b[im]
        combos = []
        for a in range(2):
            grads = []
            for c in range(2):
                ph = 2 * a + c
                d = scale * (r.act[ph, span, :] - (p1_b[im] + r.y1[ph, span, :] * p2_b[im]))
                grads.append(d.astype(BF16))
            right = nn(r.shift[0], grads[0])
            left = nn(r.shift[1], grads[1])
            even, odd = grads[0].astype(F32), grads[1].astype(F32)
            combos.append((odd + right, even + odd, left + even))
        gap = jnp.zeros((16, chans), F32)
        for dx in range(3):
            upper, lower = combos[0][dx], combos[1][dx]
            r.field[dx, im] = (lower + stack([upper[16:], gap])).astype(BF16)
            r.field[3 + dx, im] = (upper + lower).astype(BF16)
            r.field[6 + dx, im] = (stack([gap, lower[:-16]]) + upper).astype(BF16)

    def grad1(tap, carry):
        first = pl.multiple_of(256 * tap, 256)
        r.dw1[pl.ds(first, 256), :] = nn(
            r.h1cm[...], stack([r.field[tap, im] for im in range(per)])
        )
        return carry

    lax.fori_loop(0, 9, grad1, 0)
    entry.begin()
    second.first()

    parts = [stack([r.field[tap, im] for im in range(per)]) for tap in range(9)]
    dh1 = nn(jnp.concatenate(parts, axis=1), r.w1t[...])
    payload = jnp.zeros((32, chans), F32)
    for im in range(per):
        span = slice(256 * im, 256 * im + 256)
        normal = (r.fpm[span, :].astype(F32) - mean1_b[im]) * inv1_b[im]
        pre = gamma_b[im] * normal + beta_b[im]
        sig = sigmoid(pre)
        act = dh1[span] * (sig * (1.0 + pre * (1.0 - sig)))
        r.act1[span, :] = act
        q1, q2 = colsum(act), colsum(act * normal)
        payload = payload + place_row(q2, label[im], 32)
        payload = payload + place_row(q1, label[im] + classes, 32)
        payload = payload + place_row(gamma_b[im] * q1, group[im] + 24, 32)
        payload = payload + place_row(gamma_b[im] * q2, group[im] + 28, 32)
    last_sums = AllReduce(4)
    last_sums.begin(payload)
    second.second()
    entry.first()
    last_sums.middle()
    second.third()
    entry.second()

    stats = last_sums.end()
    for im in range(per):
        span = slice(256 * im, 256 * im + 256)
        normal = (r.fpm[span, :].astype(F32) - mean1_b[im]) * inv1_b[im]
        r1 = pick_row(stats[24:28], group[im]) / count
        r2 = pick_row(stats[28:32], group[im]) / count
        grad = inv1_b[im] * (gamma_b[im] * r.act1[span, :] - (r1 + normal * r2))
        grad = (grad + r.dshort[span, :]).astype(BF16)
        r.dcm[im] = nt(r.ident[...], grad).astype(BF16)
    out_waits += give_back(r.dcm, r.dx)
    entry.third()
    second.end(r.grad2, r.grad3)

    table = jnp.zeros((24, chans), F32)
    table = table + jnp.where(iota((24, chans), 0) < 2 * classes, stats[0:24], 0.0)
    table = table + place_row(colsum(affine_grad2[4:8]), 2 * classes, 24)
    table = table + place_row(colsum(affine_grad2[0:4]), 2 * classes + 1, 24)
    table = table + place_row(affine_grad2[8:9], 2 * classes + 2, 24)
    mine = jnp.zeros((24, 128), F32)
    for c in range(n_ch):
        piece = table[:, 128 * (c // 2) : 128 * (c // 2) + 128]
        if c % 2:
            piece = pltpu.roll(piece, local, axis=1)
        mine = mine + jnp.where(me == c, piece, 0.0)
    r.affine_grad[...] = mine

    if inner == 1:
        row = iota((8, 128), 0)

        def norm_rows(index, weight, grad, v):
            for wait in held[index]:
                wait()
            master = weight[...]
            _, _, direction = adam_update(
                grad[...], getattr(r, v + "m")[...], getattr(r, v + "q")[...]
            )
            update = direction + WEIGHT_DECAY * master
            rows_w = jnp.where(row == index, total(master * master), 0.0)
            return rows_w + jnp.where(row == index + 3, total(update * update), 0.0)

        norms = norm_rows(1, r.exit_v, r.grad2, "v2") + norm_rows(2, r.bypass_v, r.grad3, "vs")
        entry.end(r.grad1)
        norms = norms + norm_rows(0, r.entry_v, r.grad1, "v1")
        norm_sums = AllReduce(5)
        norm_sums.begin(norms)
        norm_sums.middle()
        r.norms[...] = norm_sums.end()
    else:
        entry.end(r.grad1)
        r.norms[...] = jnp.zeros((8, 128), F32)

    for wait in out_waits + pending:
        wait()
    cfg.used.append((slots.remote, slots.local))


def final_kernel(cfg, *refs):
    r = SimpleNamespace(**dict(zip(cfg.names, refs)))
    classes = cfg.classes
    local = cfg.local
    r.block_output[...] = r.out[...]
    r.input_gradient[...] = r.dx[...].astype(F32)
    norms = jnp.sqrt(r.norms[...])
    weight_norm, update_norm = norms[0:3, 0:1], norms[3:6, 0:1]
    ratio = weight_norm / update_norm
    at = iota((3, 3), 1)
    r.trust_norms[...] = jnp.where(
        at == 0, weight_norm, jnp.where(at == 1, update_norm, ratio)
    )
    sets = (
        (r.entry, r.entry_m, r.entry_q, r.entry_g, r.entry_1, r.entry_2, r.entry_w),
        (r.exit, r.exit_m, r.exit_q, r.exit_g, r.exit_1, r.exit_2, r.exit_w),
        (r.bypass, r.bypass_m, r.bypass_q, r.bypass_g, r.bypass_1, r.bypass_2, r.bypass_w),
    )
    for index, (weight, m, q, g, first, second, result) in enumerate(sets):
        master = weight[...]
        moment, square, direction = adam_update(g[...], m[...], q[...])
        update = direction + WEIGHT_DECAY * master
        first[...] = moment
        second[...] = square
        result[...] = master - MATRIX_RATE * ratio[index : index + 1] * update
    grad = r.affine_grad[0 : 2 * classes + 3, 0:local]
    moment, square, direction = adam_update(grad, r.affine_m[...], r.affine_q[...])
    r.affine_1[...] = moment
    r.affine_2[...] = square
    r.affine_w[...] = r.affine[...] - AFFINE_RATE * direction


def per_device(
    features,
    labels,
    groups,
    widths,
    entry_conv,
    entry_moment,
    entry_square,
    exit_conv,
    exit_moment,
    exit_square,
    bypass_conv,
    bypass_moment,
    bypass_square,
    norm_affine,
    norm_moment,
    norm_square,
    cotangent,
):
    n_img, n_ch = lax.axis_size("img"), lax.axis_size("ch")
    batch, local, pixels = features.shape
    chans = local * n_ch
    side = math.isqrt(pixels)
    inner = n_img // OUTER
    classes = (norm_affine.shape[0] - 3) // 2
    per = batch // n_ch
    assert (side, chans, n_ch, local, batch % n_ch) == (16, 256, 4, 64, 0)
    rows, small = entry_conv.shape[0] * inner, bypass_conv.shape[0] * inner
    masters = (entry_conv, exit_conv, bypass_conv)
    if inner == 1:
        blocks = masters
    else:
        sets = [[o * inner + i for i in range(inner)] for o in range(OUTER)]
        blocks = tuple(
            lax.all_gather(w.astype(BF16), "img", axis=0, tiled=True, axis_index_groups=sets)
            for w in masters
        )

    vmem = pl.BlockSpec(memory_space=pltpu.VMEM)
    smem = pl.BlockSpec(memory_space=pltpu.SMEM)
    anywhere = pl.BlockSpec(memory_space=pl.ANY)
    states = dict(
        entry_m=entry_moment.T,
        entry_q=entry_square.T,
        exit_m=exit_moment.T,
        exit_q=exit_square.T,
        bypass_m=bypass_moment,
        bypass_q=bypass_square,
    )
    inputs = dict(
        labels=(labels, smem),
        groups=(groups, smem),
        widths=(widths, smem),
        features=(features, anywhere),
        cotangent=(cotangent, anywhere),
        entry=(blocks[0].T, anywhere),
        exit=(blocks[1].T, anywhere),
        bypass=(blocks[2], anywhere),
        affine=(norm_affine, anywhere),
    )
    if inner == 1:
        inputs.update({name: (value, anywhere) for name, value in states.items()})
    sds = jax.ShapeDtypeStruct
    outputs = dict(
        out=(sds(cotangent.shape, BF16), vmem),
        dx=(sds(features.shape, BF16), vmem),
        grad1=(sds((local, rows), F32), vmem),
        grad2=(sds((local, rows), F32), vmem),
        grad3=(sds((small, local), F32), vmem),
        affine_grad=(sds((24, 128), F32), vmem),
        norms=(sds((8, 128), F32), vmem),
    )
    pix = pixels * per
    taps9 = 9 * chans
    held = lambda shape, dtype=BF16: pltpu.VMEM(shape, dtype)
    scratch = dict(
        fown=held((batch, local, pixels)),
        cown=held((batch, local, 4 * pixels)),
        fbuf=held((n_ch, per, local, pixels)),
        cbuf=held((n_ch, per, local, 4 * pixels)),
        entry_v=held((local, rows), blocks[0].dtype),
        exit_v=held((local, rows), blocks[1].dtype),
        bypass_v=held((small, local), blocks[2].dtype),
        affine_v=held(norm_affine.shape, F32),
        padded=held((3 * local, 384)),
        wz1=held((n_ch, rows // 2, 128)),
        wz2=held((n_ch, (rows + small) // 2, 128)),
        aff_z=held((n_ch, 24, 128), F32),
        w1=held((taps9, chans)),
        w2=held((taps9, chans)),
        ws=held((chans, chans)),
        w1t=held((taps9, chans)),
        w2t=held((taps9, chans)),
        unpack=held((512, 512)),
        ident=held((256, 256)),
        shift=held((2, 256, 256)),
        gridder=held((512, 256)),
        flatter=held((512, 512)),
        fpm=held((pix, chans)),
        h1s=held((3, per, pixels + 32, chans)),
        h1cm=held((chans, pix)),
        y1=held((4, pix, chans), F32),
        act=held((4, pix, chans), F32),
        h2s=held((2, 4, per, pixels + 32, chans)),
        dzs=held((2, 4, per, pixels + 32, chans)),
        h2cm=held((chans, 4 * pix)),
        short=held((pix, chans), F32),
        dshort=held((pix, chans), F32),
        dzc=held((pix, chans)),
        act1=held((pix, chans), F32),
        rc=held((per, chans, 4 * pixels)),
        ocm=held((per, chans, 4 * pixels)),
        dcm=held((per, chans, pixels)),
        field=held((9, per, pixels, chans)),
        dw1=held((taps9, chans), F32),
        dw2=held((taps9, chans), F32),
        dws=held((chans, chans), F32),
    )
    for number, size in ((1, rows), (2, rows + small)):
        shapes = ((4, size, chans),) * 2 + ((2, 2, size, 128),) * 2 + ((2, size, 128),) * 2
        shapes += ((n_ch, size // 2, 128),) * 2
        for part, shape in zip(PARTS, shapes):
            scratch[part + str(number)] = held(shape)
        scratch[PARTS[-1] + str(number)] = held((4, size, chans), F32)
    exchanges = [(8, 128), (8, chans), (16, chans), (32, chans)]
    if inner == 1:
        exchanges.append((8, 128))
        for v, shape in (("v1", (local, rows)), ("v2", (local, rows)), ("vs", (small, local))):
            scratch[v + "m"] = held(shape, F32)
            scratch[v + "q"] = held(shape, F32)
    for number, shape in enumerate(exchanges, 1):
        for axis, size in zip("abc", (OUTER, inner, n_ch)):
            if size > 1:
                scratch[axis + str(number)] = held((size,) + shape, F32)
    remote_count = 4 * 3 + 3 * 3 * per + 3 * 7 + 2 * 13 + len(exchanges) * (7 + 3 + inner - 1)
    scratch.update(
        send=pltpu.SemaphoreType.DMA((remote_count,)),
        recv=pltpu.SemaphoreType.DMA((remote_count,)),
        lsem=pltpu.SemaphoreType.DMA((20,)),
    )
    cfg = SimpleNamespace(
        names=[*inputs, *outputs, *scratch],
        inner=inner,
        n_ch=n_ch,
        batch=batch,
        local=local,
        classes=classes,
        count=float(batch * n_img // widths.shape[0] * pixels),
        rows=rows,
        small=small,
        used=[],
    )
    out, dx, grad1, grad2, grad3, affine_grad, norms = pl.pallas_call(
        functools.partial(main_kernel, cfg),
        out_shape=[s for s, _ in outputs.values()],
        in_specs=[s for _, s in inputs.values()],
        out_specs=[s for _, s in outputs.values()],
        scratch_shapes=list(scratch.values()),
        compiler_params=pltpu.CompilerParams(
            collective_id=0, has_side_effects=True, vmem_limit_bytes=VMEM_LIMIT
        ),
        name="block_step",
    )(*[v for v, _ in inputs.values()])
    assert max(n for n, _ in cfg.used) <= remote_count and max(n for _, n in cfg.used) <= 20

    grads = [grad1, grad2, grad3]
    if inner > 1:
        grads = [
            lax.psum_scatter(g, "img", scatter_dimension=0, axis_index_groups=sets, tiled=True)
            for g in (grad1.T, grad2.T, grad3)
        ]
        updates = []
        for w, g, m, s in zip(
            masters,
            grads,
            (entry_moment, exit_moment, bypass_moment),
            (entry_square, exit_square, bypass_square),
        ):
            updates.append(adam_update(g, m, s)[2] + WEIGHT_DECAY * w)
        sums = lax.psum(
            jnp.stack([jnp.sum(w * w) for w in masters] + [jnp.sum(u * u) for u in updates]),
            ("img", "ch"),
        )
        norms = jnp.broadcast_to(jnp.pad(sums, (0, 2))[:, None], (8, 128))
        grads = [grads[0].T, grads[1].T, grads[2]]

    args = dict(
        out=out,
        dx=dx,
        norms=norms,
        affine_grad=affine_grad,
        entry_g=grads[0],
        exit_g=grads[1],
        bypass_g=grads[2],
        entry=entry_conv.T,
        exit=exit_conv.T,
        bypass=bypass_conv,
        **states,
        affine=norm_affine,
        affine_m=norm_moment,
        affine_q=norm_square,
    )
    tall = sds(entry_conv.shape[::-1], F32)
    short, wide = (sds(w.shape, F32) for w in (bypass_conv, norm_affine))
    results = dict(
        block_output=sds(cotangent.shape, BF16),
        input_gradient=sds(features.shape, F32),
        entry_1=tall,
        entry_2=tall,
        entry_w=tall,
        exit_1=tall,
        exit_2=tall,
        exit_w=tall,
        bypass_1=short,
        bypass_2=short,
        bypass_w=short,
        affine_1=wide,
        affine_2=wide,
        affine_w=wide,
        trust_norms=sds((3, 3), F32),
    )
    end_cfg = SimpleNamespace(names=[*args, *results], classes=classes, local=local)
    final = pl.pallas_call(
        functools.partial(final_kernel, end_cfg),
        out_shape=list(results.values()),
        in_specs=[vmem] * len(args),
        out_specs=[vmem] * len(results),
        compiler_params=pltpu.CompilerParams(vmem_limit_bytes=VMEM_LIMIT),
        name="finish",
    )(*args.values())
    return tuple(v.T if s is tall else v for v, s in zip(final, results.values()))


def solution(mesh):
    wide = P("img", "ch")
    deep = P("img", "ch", None)
    table = P(None, "ch")
    return jax.shard_map(
        per_device,
        mesh=mesh,
        in_specs=(deep, P("img"), P("img"), P()) + (wide,) * 9 + (table,) * 3 + (deep,),
        out_specs=(deep, deep) + (wide,) * 9 + (table,) * 3 + (P(),),
        check_vma=False,
    )
```

```python
import functools
import math
from types import SimpleNamespace

import jax
import jax.numpy as jnp
from jax import lax
from jax.experimental import pallas as pl
from jax.experimental.pallas import tpu as pltpu
from jax.sharding import PartitionSpec as P

LEVELS = 4
STEP = 5
NORM_EPSILON = 1e-05
ADAM_EPSILON = 1e-06
MOMENT_DECAY = 0.9
SQUARE_DECAY = 0.999
WEIGHT_DECAY = 0.01
MATRIX_RATE = 0.3
AFFINE_RATE = 0.2

OUTER = 8
VMEM_LIMIT = 56 * 1024 * 1024
BF16 = jnp.bfloat16
F32 = jnp.float32
MESH = pl.DeviceIdType.MESH
PARTS = ("s1", "r1", "s2", "r2", "s3", "r3", "s4", "r4", "acc")


def nn(left, right):
    return lax.dot_general(left, right, (((1,), (0,)), ((), ())), preferred_element_type=F32)


def nt(left, right):
    return lax.dot_general(left, right, (((1,), (1,)), ((), ())), preferred_element_type=F32)


def flip(index, mask):
    result = index
    for bit in range(3):
        if (mask >> bit) & 1:
            digit = lax.rem(lax.div(index, 1 << bit), 2)
            result = result + (1 - 2 * digit) * (1 << bit)
    return result


def sigmoid(value):
    return 0.5 * jnp.tanh(0.5 * value) + 0.5


def iota(shape, axis):
    return lax.broadcasted_iota(jnp.int32, shape, axis)


def to_bf16(condition):
    return jnp.where(condition, 1.0, 0.0).astype(BF16)


def pick_row(table, index):
    hit = iota(table.shape, 0) == index
    return jnp.sum(jnp.where(hit, table, 0.0), axis=0, keepdims=True)


def place_row(row, index, rows):
    hit = iota((rows, row.shape[1]), 0) == index
    return jnp.where(hit, row, 0.0)


def colsum(value):
    return jnp.sum(value, axis=0, keepdims=True)


def adam_update(grad, moment, square):
    moment_new = MOMENT_DECAY * moment + (1.0 - MOMENT_DECAY) * grad
    square_new = SQUARE_DECAY * square + (1.0 - SQUARE_DECAY) * grad * grad
    direction = (
        moment_new
        / (1.0 - MOMENT_DECAY**STEP)
        / (jnp.sqrt(square_new / (1.0 - SQUARE_DECAY**STEP)) + ADAM_EPSILON)
    )
    return (moment_new, square_new, direction)


def total(value):
    return jnp.sum(jnp.sum(value, axis=1, keepdims=True), axis=0, keepdims=True)


def main_kernel(cfg, *refs):
    r = SimpleNamespace(**dict(zip(cfg.names, refs)))
    inner, n_ch, batch, local = cfg.inner, cfg.n_ch, cfg.batch, cfg.local
    classes, count = cfg.classes, cfg.count
    per = batch // n_ch
    chans = local * n_ch
    rows, small = cfg.rows, cfg.small
    tail = (rows - 256) // 2
    hw, hs = rows // 2, small // 2
    slots = SimpleNamespace(remote=0, local=0)

    img = lax.axis_index("img")
    me = lax.axis_index("ch")
    block = lax.div(img, inner)
    within = lax.rem(img, inner)
    core = lax.rem(block, 2)
    plane = lax.div(block, 2)
    bit_x, bit_y = lax.rem(plane, 2), lax.div(plane, 2)
    partner = flip(block, 1)

    def dev(block_id, within_id, ch_id):
        return (block_id * inner + within_id, ch_id)

    pending = []

    def post(src, dst, landed, peer):
        slot = slots.remote
        slots.remote = slot + 1
        copy = pltpu.make_async_remote_copy(
            src_ref=src,
            dst_ref=dst,
            send_sem=r.send.at[slot],
            recv_sem=r.recv.at[slot],
            device_id=peer,
            device_id_type=MESH,
        )
        copy.start()
        pending.append(copy.wait_send)
        arrival = pltpu.make_async_remote_copy(
            src_ref=landed,
            dst_ref=landed,
            send_sem=r.send.at[slot],
            recv_sem=r.recv.at[slot],
            device_id=peer,
            device_id_type=MESH,
        )
        return arrival.wait_recv

    def here(src, dst):
        slot = slots.local
        slots.local = slot + 1
        copy = pltpu.make_async_copy(src, dst, r.lsem.at[slot])
        copy.start()
        return copy.wait

    outer_peers = [flip(block, mask) for mask in range(1, OUTER)]
    ch_peers = [flip(me, mask) for mask in range(1, n_ch)]
    inner_pairs = [
        (lax.rem(within + step, inner), lax.rem(within + inner - step, inner))
        for step in range(1, inner)
    ]
    barrier = pltpu.get_barrier_semaphore()
    everyone = [dev(peer, within, me) for peer in outer_peers]
    everyone += [dev(block, within, peer) for peer in ch_peers]
    everyone += [dev(block, peer, me) for peer, _ in inner_pairs]
    for peer in everyone:
        pl.semaphore_signal(barrier, inc=1, device_id=peer, device_id_type=MESH)

    got_entry = here(r.entry, r.entry_v)
    got_features = here(r.features, r.fown)
    got_exit = here(r.exit, r.exit_v)
    got_bypass = here(r.bypass, r.bypass_v)
    got_affine = here(r.affine, r.affine_v)
    got_cot = here(r.cotangent, r.cown)
    states = ((r.entry_m, r.entry_q), (r.exit_m, r.exit_q), (r.bypass_m, r.bypass_q)) if inner == 1 else ()
    held = [
        (here(m, getattr(r, v + "m")), here(q, getattr(r, v + "q")))
        for (m, q), v in zip(states, ("v1", "v2", "vs"))
    ]

    s_row, s_col = iota((hw, 384), 0), iota((hw, 384), 1)
    pick_first = to_bf16(s_col == jnp.where(s_row < 128, s_row, s_row + 128))
    pick_second = to_bf16(s_col == jnp.where(s_row < 128, s_row + 128, s_row + 128 + tail))
    r.padded[...] = jnp.zeros(r.padded.shape, BF16)

    def pack_own(value):
        r.padded[local : 2 * local, 0:rows] = value.astype(BF16)
        packed = nt(pick_first, r.padded[local : 3 * local, :])
        return (packed + nt(pick_second, r.padded[0 : 2 * local, :])).astype(BF16)

    got_entry()
    r.wz1[me] = pack_own(r.entry_v[...])
    pl.semaphore_wait(barrier, len(everyone))

    def to_channels(buffer):
        return [
            post(buffer.at[me], buffer.at[me], buffer.at[peer], dev(block, within, peer))
            for peer in ch_peers
        ]

    entry_waits = to_channels(r.wz1)
    got_features()
    feature_waits = [
        post(
            r.fown.at[pl.ds(per * peer, per)],
            r.fbuf.at[me],
            r.fbuf.at[peer],
            dev(block, within, peer),
        )
        for peer in ch_peers
    ]
    got_affine()
    r.aff_z[me] = jnp.zeros((24, 128), F32)
    r.aff_z[me, 0 : 2 * classes + 3, 0:local] = r.affine_v[...]
    affine_waits = to_channels(r.aff_z)

    lane = iota((512, 512), 0)
    column = iota((512, 512), 1)
    spot = 256 * ((lane >> 6) & 1) + 64 * (lane >> 7) + (lane & 63)
    r.unpack[...] = to_bf16(column == spot)

    r.fbuf[me] = r.fown[pl.ds(per * me, per)]
    flat = jnp.concatenate([r.fown[b] for b in range(batch)], axis=1)
    wide = flat.astype(F32)
    square = wide * wide
    square_hi = square.astype(BF16)
    square_lo = (square - square_hi.astype(F32)).astype(BF16)
    level = iota((16, 256), 0)
    first_mask = jnp.concatenate([to_bf16(level == r.groups[b]) for b in range(batch)], axis=1)
    second_mask = jnp.concatenate([to_bf16(level == r.groups[b] + 4) for b in range(batch)], axis=1)
    sums = nt(first_mask, flat) + nt(second_mask, square_hi) + nt(second_mask, square_lo)

    def ordered_sum(ref, size):
        result = ref[0]
        for slot in range(1, size):
            result = result + ref[slot]
        return result

    class AllReduce:
        def __init__(self, number):
            self.over_outer, self.over_inner, self.over_ch = (
                getattr(r, axis + str(number), None) for axis in "abc"
            )

        def begin(self, value, masked=None):
            ref = self.over_outer
            if masked is None:
                ref[block] = value
            else:
                ref[block] = jnp.zeros(ref.shape[1:], F32)
                ref[block, :, 0:masked] = value
            self.waits = [
                post(ref.at[block], ref.at[block], ref.at[peer], dev(peer, within, me))
                for peer in outer_peers
            ]

        def middle(self):
            for wait in self.waits:
                wait()
            value = ordered_sum(self.over_outer, OUTER)
            if inner > 1:
                ref = self.over_inner
                ref[within] = value
                waits = [
                    post(ref.at[within], ref.at[within], ref.at[back], dev(block, peer, me))
                    for peer, back in inner_pairs
                ]
                for wait in waits:
                    wait()
                value = ordered_sum(ref, inner)
            self.over_ch[me] = value
            self.waits = to_channels(self.over_ch)

        def finish(self):
            for wait in self.waits:
                wait()
            return self.over_ch

        def end(self):
            return ordered_sum(self.finish(), n_ch)

    input_sums = AllReduce(1)
    input_sums.begin(sums[0:8], masked=local)

    got_exit()
    got_bypass()
    r.wz2[me, 0:hw, :] = pack_own(r.exit_v[...])
    e_row, e_col = iota((local, 128), 0), iota((local, 128), 1)
    value = r.bypass_v[...].astype(BF16)
    r.wz2[me, hw : hw + hs, :] = (
        nn(value[:hs], to_bf16(e_col == e_row)) + nn(value[hs:], to_bf16(e_col == e_row + local))
    ).astype(BF16)

    def rows_of(ref, index):
        size = ref.shape[0] // OUTER
        return ref.at[pl.ds(pl.multiple_of(size * index, 16), size)]

    def unpack_own(ref, full):
        own = rows_of(ref, block)
        if full.shape[0] == hw:
            own[0:128, :] = full[0:128, 0:256]
            own[128:256, :] = full[0:128, 256:512]
            own[256 : 256 + tail, :] = full[128:, 0:256]
            own[256 + tail :, :] = full[128:, 256:512]
        else:
            own[0:hs, :] = full[:, 0:256]
            own[hs:, :] = full[:, 256:512]

    def spread(ref):
        own = rows_of(ref, block)
        return {
            mask: post(own, own, rows_of(ref, flip(block, mask)), dev(flip(block, mask), within, me))
            for mask in (2, 4, 6, 1)
        }

    def forward(ref, waits):
        rest = [waits[1]]
        for mask in (2, 4, 6):
            waits[mask]()
            mine = rows_of(ref, flip(block, mask))
            theirs = rows_of(ref, flip(partner, mask))
            rest.append(post(mine, mine, theirs, dev(partner, within, me)))
        return rest

    def widen(buffer):
        packed = jnp.concatenate([buffer[c] for c in range(n_ch)], axis=1)
        return nn(packed, r.unpack[...]).astype(BF16)

    for wait in entry_waits:
        wait()
    unpack_own(r.w1, widen(r.wz1))
    gather1 = spread(r.w1)
    exit_waits = to_channels(r.wz2)

    ident = to_bf16(iota((256, 256), 0) == iota((256, 256), 1))
    r.ident[...] = ident
    q_out, q_in = iota((256, 256), 0), iota((256, 256), 1)
    r.shift[0] = to_bf16((q_in == q_out + 1) & ((q_out & 15) < 15))
    r.shift[1] = to_bf16((q_in == q_out - 1) & ((q_out & 15) > 0))

    input_sums.middle()
    got_cot()
    cot_waits = [
        post(
            r.cown.at[per * peer + im],
            r.cbuf.at[me, im],
            r.cbuf.at[peer, im],
            dev(block, within, peer),
        )
        for im in range(per)
        for peer in ch_peers
    ]

    rho, px = iota((512, 256), 0), iota((512, 256), 1)
    version, a, b_ = rho >> 8, (rho >> 7) & 1, (rho >> 6) & 1
    col = (rho & 15) + version * (1 - 2 * b_)
    target = (2 * ((rho & 63) >> 4) + a) * 32 + 2 * col + b_
    r.gridder[...] = to_bf16((px == target) & (col >= 0) & (col < 16))
    target = (
        (2 * ((lane & 127) >> 4) + (lane >> 8)) * 32 + 2 * (lane & 15) + ((lane >> 7) & 1)
    )
    r.flatter[...] = to_bf16(column == target)
    zeros = jnp.zeros((16, 256), BF16)
    for im in range(per):
        for ver in range(3):
            r.h1s[ver, im, 0:16, :] = zeros
            r.h1s[ver, im, 272:288, :] = zeros
        for ver in range(2):
            for ph in range(4):
                for ref in (r.h2s, r.dzs):
                    ref[ver, ph, im, 0:16, :] = zeros
                    ref[ver, ph, im, 272:288, :] = zeros

    def channel_major(ref, im, lanes):
        return jnp.concatenate([ref[c, im, :, lanes] for c in range(n_ch)], axis=0)

    for wait in feature_waits:
        wait()
    for im in range(per):
        r.fpm[256 * im : 256 * im + 256, :] = nt(
            ident, channel_major(r.fbuf, im, slice(0, 256))
        ).astype(BF16)

    def wide_lanes(ref):
        parts = [
            ref[c] + pltpu.roll(ref[c + 1], local, axis=1) for c in range(0, n_ch, 2)
        ]
        return jnp.concatenate(parts, axis=1)

    for wait in affine_waits:
        wait()
    affine = wide_lanes(r.aff_z)
    stats = wide_lanes(input_sums.finish())
    mean1 = stats[0:4] / count
    inv1 = lax.rsqrt(stats[4:8] / count - mean1 * mean1 + NORM_EPSILON)
    gain = affine[2 * classes : 2 * classes + 1]
    shift = affine[2 * classes + 1 : 2 * classes + 2]
    out_bias = affine[2 * classes + 2 : 2 * classes + 3]
    group, label, mean1_b, inv1_b, gamma_b, beta_b, mask_b = [], [], [], [], [], [], []
    for im in range(per):
        group.append(r.groups[per * me + im])
        label.append(r.labels[per * me + im])
        mean1_b.append(pick_row(mean1, group[im]))
        inv1_b.append(pick_row(inv1, group[im]))
        gamma_b.append(pick_row(affine, label[im]))
        beta_b.append(pick_row(affine, label[im] + classes))
        width = r.widths[group[im]]
        mask_b.append(
            jnp.where(iota((1, chans), 1) < width * (chans // LEVELS), 1.0, 0.0)
        )

    for im in range(per):
        normal = (r.fpm[256 * im : 256 * im + 256, :].astype(F32) - mean1_b[im]) * inv1_b[im]
        pre = gamma_b[im] * normal + beta_b[im]
        hidden = (pre * sigmoid(pre)).astype(BF16)
        r.h1s[1, im, 16:272, :] = hidden
        r.h1s[0, im, 16:272, :] = nn(r.shift[1], hidden).astype(BF16)
        r.h1s[2, im, 16:272, :] = nn(r.shift[0], hidden).astype(BF16)
        r.h1cm[:, 256 * im : 256 * im + 256] = nt(ident, hidden).astype(BF16)

    for wait in exit_waits:
        wait()
    full = widen(r.wz2)
    unpack_own(r.w2, full[0:hw])
    unpack_own(r.ws, full[hw:])
    rest = forward(r.w1, gather1)
    gather2 = spread(r.w2)
    gather3 = spread(r.ws)
    for wait in rest:
        wait()

    def taps():
        return [(dy, dx) for dy in range(3) for dx in range(3)]

    def stack(pieces):
        return jnp.concatenate(pieces, axis=0)

    def conv1(phase, carry):
        a, c = lax.div(phase, 2), lax.rem(phase, 2)
        parts = []
        for dy, dx in taps():
            first = pl.multiple_of(16 * lax.div(a + dy + 1, 2), 16)
            ver = lax.div(c + dx + 1, 2)
            parts.append(
                stack([r.h1s[ver, im, pl.ds(first, 256), :] for im in range(per)])
            )
        y = nn(jnp.concatenate(parts, axis=1), r.w1[...])
        r.y1[phase] = y
        out = []
        for im in range(per):
            piece = y[256 * im : 256 * im + 256]
            out.append(carry[2 * im] + colsum(piece))
            out.append(carry[2 * im + 1] + colsum(piece * piece))
        return tuple(out)

    nought = jnp.zeros((1, chans), F32)
    mid = lax.fori_loop(0, 4, conv1, (nought,) * (2 * per))
    payload = jnp.zeros((8, chans), F32)
    for im in range(per):
        payload = payload + place_row(mid[2 * im], group[im], 8)
        payload = payload + place_row(mid[2 * im + 1], group[im] + 4, 8)
    mid_sums = AllReduce(2)
    mid_sums.begin(payload)

    def turn(src, dst):
        def one(tap, carry):
            first = pl.multiple_of(256 * tap, 256)
            dst[pl.ds(first, 256), :] = nt(r.ident[...], src[pl.ds(first, 256), :]).astype(BF16)
            return carry

        lax.fori_loop(0, 9, one, 0)

    turn(r.w1, r.w1t)
    rest = forward(r.w2, gather2) + forward(r.ws, gather3)
    mid_sums.middle()

    r.cbuf[me] = r.cown[pl.ds(per * me, per)]
    for wait in cot_waits:
        wait()
    for im in range(per):
        for n in range(4):
            piece = channel_major(r.cbuf, im, slice(256 * n, 256 * n + 256))
            grid = nt(r.gridder[...], piece).astype(BF16)
            for ver in range(2):
                for ph in range(4):
                    at = 256 * ver + 64 * ph
                    r.dzs[ver, ph, im, 16 + 64 * n : 80 + 64 * n, :] = grid[at : at + 64]

    coarse = jnp.zeros((256 * per, chans), F32)
    for ph in range(4):
        coarse = coarse + stack([r.dzs[0, ph, im, 16:272, :] for im in range(per)]).astype(F32)
    bias_sum = colsum(coarse)
    r.dzc[...] = coarse.astype(BF16)

    def tap_slice(ref, a, c, dy, dx, im):
        row, colm = a + dy + 1, c + dx + 1
        first = pl.multiple_of(16 * lax.div(row, 2), 16)
        ph = 2 * lax.rem(row, 2) + lax.rem(colm, 2)
        side_step = lax.div(colm, 2) - 1
        return ref[side_step * side_step, ph, im, pl.ds(first, 256), :]

    for wait in rest:
        wait()
    turn(r.w2, r.w2t)

    def back2(phase, carry):
        a, c = lax.div(phase, 2), lax.rem(phase, 2)
        parts = [
            stack([tap_slice(r.dzs, a, c, 2 - dy, 2 - dx, im) for im in range(per)])
            for dy, dx in taps()
        ]
        r.act[phase] = nn(jnp.concatenate(parts, axis=1), r.w2t[...])
        return carry

    lax.fori_loop(0, 4, back2, 0)

    stats = mid_sums.end()
    mean2 = stats[0:4] / (4.0 * count)
    inv2 = lax.rsqrt(stats[4:8] / (4.0 * count) - mean2 * mean2 + NORM_EPSILON)
    mean2_b = [pick_row(mean2, group[im]) for im in range(per)]
    inv2_b = [pick_row(inv2, group[im]) for im in range(per)]

    def hidden2(phase, carry):
        c = lax.rem(phase, 2)
        out = []
        for im in range(per):
            span = slice(256 * im, 256 * im + 256)
            normal = (r.y1[phase, span, :] - mean2_b[im]) * inv2_b[im]
            r.y1[phase, span, :] = normal
            pre = gain * normal + shift
            sig = sigmoid(pre)
            hidden = (pre * sig * mask_b[im]).astype(BF16)
            act = r.act[phase, span, :] * (sig * (1.0 + pre * (1.0 - sig)) * mask_b[im])
            r.act[phase, span, :] = act
            out.append(carry[2 * im] + colsum(act))
            out.append(carry[2 * im + 1] + colsum(act * normal))
            r.h2s[0, phase, im, 16:272, :] = hidden
            r.h2s[1, phase, im, 16:272, :] = nn(r.shift[c], hidden).astype(BF16)
            lanes = pl.ds(pl.multiple_of(512 * phase + 256 * im, 256), 256)
            r.h2cm[:, lanes] = nt(r.ident[...], hidden).astype(BF16)
        return tuple(out)

    mid = lax.fori_loop(0, 4, hidden2, (nought,) * (2 * per))
    payload = place_row(bias_sum, 8, 16)
    for im in range(per):
        payload = payload + place_row(mid[2 * im], group[im], 16)
        payload = payload + place_row(mid[2 * im + 1], group[im] + 4, 16)
    back_sums = AllReduce(3)
    back_sums.begin(payload)

    def grad2(tap, carry):
        dy, dx = lax.div(tap, 3), lax.rem(tap, 3)
        pieces = []
        for ph in range(4):
            a, c = ph // 2, ph % 2
            for im in range(per):
                pieces.append(tap_slice(r.dzs, a, c, 2 - dy, 2 - dx, im))
        first = pl.multiple_of(256 * tap, 256)
        r.dw2[pl.ds(first, 256), :] = nn(r.h2cm[...], stack(pieces))
        return carry

    lax.fori_loop(0, 9, grad2, 0)
    back_sums.middle()
    for im in range(per):
        piece = channel_major(r.fbuf, im, slice(0, 256))
        grad = nn(piece, r.dzc[256 * im : 256 * im + 256, :])
        if im == 0:
            r.dws[...] = grad
        else:
            r.dws[...] = r.dws[...] + grad

    class GradSum:
        def __init__(self, number, fetch):
            self.fetch = fetch
            for part in PARTS:
                setattr(self, part, getattr(r, part + str(number)))

        def begin(self):
            self.waits = []
            for u in range(4):
                self.s1[u] = self.fetch(2 * u + 1 - core).astype(BF16)
                self.waits.append(
                    post(self.s1.at[u], self.r1.at[u], self.r1.at[u], dev(partner, within, me))
                )

        def settle(self):
            for wait in self.waits:
                wait()

        def across(self, send, got, masks):
            parts = [(h, v) for v in range(2) for h in range(2)] if len(send.shape) == 4 else [(0,), (1,)]
            self.waits = [
                post(send.at[p], got.at[p], got.at[p], dev(flip(block, masks[p[0]]), within, me))
                for p in parts
            ]

        def first(self):
            for u in range(4):
                self.waits[u]()
                self.acc[u] = self.fetch(2 * u + core) + self.r1[u].astype(F32)
            for v in range(2):
                self.s2[0, v] = self.acc[2 * v + 1 - bit_x, :, 0:128].astype(BF16)
                self.s2[1, v] = self.acc[2 * (1 - bit_y) + v, :, 128:256].astype(BF16)
            self.across(self.s2, self.r2, (2, 4))

        def second(self):
            self.settle()
            low = self.acc[2 * (1 - bit_y) + bit_x, :, 0:128] + self.r2[0, 1 - bit_y].astype(F32)
            high = self.acc[2 * bit_y + 1 - bit_x, :, 128:256] + self.r2[1, 1 - bit_x].astype(F32)
            self.s3[0] = low.astype(BF16)
            self.s3[1] = high.astype(BF16)
            self.across(self.s3, self.r3, (4, 2))

        def third(self):
            self.settle()
            low = self.acc[plane, :, 0:128] + self.r2[0, bit_y].astype(F32)
            high = self.acc[plane, :, 128:256] + self.r2[1, bit_x].astype(F32)
            low, high = low + self.r3[0].astype(F32), high + self.r3[1].astype(F32)
            value = jnp.concatenate([low, high], axis=1).astype(BF16)
            left = [value[0:128], value[256 : 256 + tail]]
            right = [value[128:256], value[256 + tail : rows]]
            if value.shape[0] > rows:
                left.append(value[rows : rows + hs])
                right.append(value[rows + hs :])
            pair = jnp.concatenate([stack(left), stack(right)], axis=1)
            packed = nt(pair, r.unpack[...]).astype(BF16)
            for c in range(n_ch):
                self.s4[c] = packed[:, 128 * c : 128 * c + 128]
            self.r4[me] = self.s4[me]
            self.waits = [
                post(self.s4.at[peer], self.r4.at[me], self.r4.at[peer], dev(block, within, peer))
                for peer in ch_peers
            ]

        def end(self, out, out_small=None):
            self.settle()
            done = self.r4[0].astype(F32)
            for c in range(1, n_ch):
                done = done + self.r4[c].astype(F32)
            turned = done[0:128].T
            out[:, 0:128] = turned[0:local]
            out[:, 128:256] = turned[local:]
            gap = jnp.zeros((128 - tail, 128), F32)
            turned = stack([done[128 : 128 + tail], gap]).T
            ends = turned[0:local] + pltpu.roll(turned[local:], tail, axis=1)
            out[:, 256:rows] = ends[:, 0 : rows - 256]
            if out_small is not None:
                last = done[hw:]
                out_small[0:hs, :] = last[:, 0:local]
                out_small[hs:, :] = pltpu.roll(last, local, axis=1)[:, 0:local]

    def block_rows(ref, size, index):
        return ref[pl.ds(pl.multiple_of(size * index, 8), size), :]

    second = GradSum(2, lambda k: stack([block_rows(r.dw2, rows, k), block_rows(r.dws, small, k)]))
    entry = GradSum(1, lambda k: block_rows(r.dw1, rows, k))
    second.begin()
    r.short[...] = nn(r.fpm[...], r.ws[...]) + out_bias
    r.dshort[...] = nt(r.dzc[...], r.ws[...])

    stats = back_sums.end()
    affine_grad2 = stats
    p1_b = [pick_row(stats[0:4], group[im]) / (4.0 * count) for im in range(per)]
    p2_b = [pick_row(stats[4:8], group[im]) / (4.0 * count) for im in range(per)]

    for im in range(per):
        span = slice(256 * im, 256 * im + 256)
        scale = gain * inv2_b[im]
        combos = []
        for a in range(2):
            grads = []
            for c in range(2):
                ph = 2 * a + c
                d = scale * (r.act[ph, span, :] - (p1_b[im] + r.y1[ph, span, :] * p2_b[im]))
                grads.append(d.astype(BF16))
            right = nn(r.shift[0], grads[0])
            left = nn(r.shift[1], grads[1])
            even, odd = grads[0].astype(F32), grads[1].astype(F32)
            combos.append((odd + right, even + odd, left + even))
        gap = jnp.zeros((16, chans), F32)
        for dx in range(3):
            upper, lower = combos[0][dx], combos[1][dx]
            r.field[dx, im] = (lower + stack([upper[16:], gap])).astype(BF16)
            r.field[3 + dx, im] = (upper + lower).astype(BF16)
            r.field[6 + dx, im] = (stack([gap, lower[:-16]]) + upper).astype(BF16)

    def grad1(tap, carry):
        first = pl.multiple_of(256 * tap, 256)
        r.dw1[pl.ds(first, 256), :] = nn(
            r.h1cm[...], stack([r.field[tap, im] for im in range(per)])
        )
        return carry

    lax.fori_loop(0, 9, grad1, 0)
    entry.begin()

    def conv2(phase, carry):
        a, c = lax.div(phase, 2), lax.rem(phase, 2)
        parts = [
            stack([tap_slice(r.h2s, a, c, dy, dx, im) for im in range(per)]) for dy, dx in taps()
        ]
        y = (nn(jnp.concatenate(parts, axis=1), r.w2[...]) + r.short[...]).astype(BF16)
        lanes = pl.ds(pl.multiple_of(256 * phase, 256), 256)
        for im in range(per):
            r.rc[im, :, lanes] = nt(r.ident[...], y[256 * im : 256 * im + 256]).astype(BF16)
        return carry

    parts = [stack([r.field[tap, im] for im in range(per)]) for tap in range(9)]
    dh1 = nn(jnp.concatenate(parts, axis=1), r.w1t[...])
    payload = jnp.zeros((32, chans), F32)
    for im in range(per):
        span = slice(256 * im, 256 * im + 256)
        normal = (r.fpm[span, :].astype(F32) - mean1_b[im]) * inv1_b[im]
        pre = gamma_b[im] * normal + beta_b[im]
        sig = sigmoid(pre)
        act = dh1[span] * (sig * (1.0 + pre * (1.0 - sig)))
        r.act1[span, :] = act
        q1, q2 = colsum(act), colsum(act * normal)
        payload = payload + place_row(q2, label[im], 32)
        payload = payload + place_row(q1, label[im] + classes, 32)
        payload = payload + place_row(gamma_b[im] * q1, group[im] + 24, 32)
        payload = payload + place_row(gamma_b[im] * q2, group[im] + 28, 32)
    last_sums = AllReduce(4)
    last_sums.begin(payload)
    entry.first()
    lax.fori_loop(0, 2, conv2, 0)
    last_sums.middle()
    entry.second()
    second.first()
    lax.fori_loop(2, 4, conv2, 0)
    entry.third()
    second.second()
    for im in range(per):
        for half in range(2):
            piece = jnp.concatenate(
                [r.rc[im, :, 256 * ph + 128 * half : 256 * ph + 128 * half + 128] for ph in range(4)],
                axis=1,
            )
            r.ocm[im, :, 512 * half : 512 * half + 512] = nn(piece, r.flatter[...]).astype(BF16)

    def own_channels(ref, index, im):
        return ref.at[im, pl.ds(pl.multiple_of(local * index, local), local), :]

    def give_back(ref, out):
        waits = [here(own_channels(ref, me, im), out.at[per * me + im]) for im in range(per)]
        return waits + [
            post(
                own_channels(ref, peer, im),
                out.at[per * me + im],
                out.at[per * peer + im],
                dev(block, within, peer),
            )
            for im in range(per)
            for peer in ch_peers
        ]

    out_waits = give_back(r.ocm, r.out)
    second.third()

    stats = last_sums.end()
    for im in range(per):
        span = slice(256 * im, 256 * im + 256)
        normal = (r.fpm[span, :].astype(F32) - mean1_b[im]) * inv1_b[im]
        r1 = pick_row(stats[24:28], group[im]) / count
        r2 = pick_row(stats[28:32], group[im]) / count
        grad = inv1_b[im] * (gamma_b[im] * r.act1[span, :] - (r1 + normal * r2))
        grad = (grad + r.dshort[span, :]).astype(BF16)
        r.dcm[im] = nt(r.ident[...], grad).astype(BF16)
    out_waits += give_back(r.dcm, r.dx)
    second.end(r.grad2, r.grad3)

    table = jnp.zeros((24, chans), F32)
    table = table + jnp.where(iota((24, chans), 0) < 2 * classes, stats[0:24], 0.0)
    table = table + place_row(colsum(affine_grad2[4:8]), 2 * classes, 24)
    table = table + place_row(colsum(affine_grad2[0:4]), 2 * classes + 1, 24)
    table = table + place_row(affine_grad2[8:9], 2 * classes + 2, 24)
    mine = jnp.zeros((24, 128), F32)
    for c in range(n_ch):
        piece = table[:, 128 * (c // 2) : 128 * (c // 2) + 128]
        if c % 2:
            piece = pltpu.roll(piece, local, axis=1)
        mine = mine + jnp.where(me == c, piece, 0.0)
    r.affine_grad[...] = mine

    if inner == 1:
        row = iota((8, 128), 0)

        def norm_rows(index, weight, grad, v):
            for wait in held[index]:
                wait()
            master = weight[...]
            _, _, direction = adam_update(
                grad[...], getattr(r, v + "m")[...], getattr(r, v + "q")[...]
            )
            update = direction + WEIGHT_DECAY * master
            rows_w = jnp.where(row == index, total(master * master), 0.0)
            return rows_w + jnp.where(row == index + 3, total(update * update), 0.0)

        norms = norm_rows(1, r.exit_v, r.grad2, "v2") + norm_rows(2, r.bypass_v, r.grad3, "vs")
        entry.end(r.grad1)
        norms = norms + norm_rows(0, r.entry_v, r.grad1, "v1")
        norm_sums = AllReduce(5)
        norm_sums.begin(norms)
        norm_sums.middle()
        r.norms[...] = norm_sums.end()
    else:
        entry.end(r.grad1)
        r.norms[...] = jnp.zeros((8, 128), F32)

    for wait in out_waits + pending:
        wait()
    cfg.used.append((slots.remote, slots.local))


def final_kernel(cfg, *refs):
    r = SimpleNamespace(**dict(zip(cfg.names, refs)))
    classes = cfg.classes
    local = cfg.local
    r.block_output[...] = r.out[...]
    r.input_gradient[...] = r.dx[...].astype(F32)
    norms = jnp.sqrt(r.norms[...])
    weight_norm, update_norm = norms[0:3, 0:1], norms[3:6, 0:1]
    ratio = weight_norm / update_norm
    at = iota((3, 3), 1)
    r.trust_norms[...] = jnp.where(
        at == 0, weight_norm, jnp.where(at == 1, update_norm, ratio)
    )
    sets = (
        (r.entry, r.entry_m, r.entry_q, r.entry_g, r.entry_1, r.entry_2, r.entry_w),
        (r.exit, r.exit_m, r.exit_q, r.exit_g, r.exit_1, r.exit_2, r.exit_w),
        (r.bypass, r.bypass_m, r.bypass_q, r.bypass_g, r.bypass_1, r.bypass_2, r.bypass_w),
    )
    for index, (weight, m, q, g, first, second, result) in enumerate(sets):
        master = weight[...]
        moment, square, direction = adam_update(g[...], m[...], q[...])
        update = direction + WEIGHT_DECAY * master
        first[...] = moment
        second[...] = square
        result[...] = master - MATRIX_RATE * ratio[index : index + 1] * update
    grad = r.affine_grad[0 : 2 * classes + 3, 0:local]
    moment, square, direction = adam_update(grad, r.affine_m[...], r.affine_q[...])
    r.affine_1[...] = moment
    r.affine_2[...] = square
    r.affine_w[...] = r.affine[...] - AFFINE_RATE * direction


def per_device(
    features,
    labels,
    groups,
    widths,
    entry_conv,
    entry_moment,
    entry_square,
    exit_conv,
    exit_moment,
    exit_square,
    bypass_conv,
    bypass_moment,
    bypass_square,
    norm_affine,
    norm_moment,
    norm_square,
    cotangent,
):
    n_img, n_ch = lax.axis_size("img"), lax.axis_size("ch")
    batch, local, pixels = features.shape
    chans = local * n_ch
    side = math.isqrt(pixels)
    inner = n_img // OUTER
    classes = (norm_affine.shape[0] - 3) // 2
    per = batch // n_ch
    assert (side, chans, n_ch, local, batch % n_ch) == (16, 256, 4, 64, 0)
    rows, small = entry_conv.shape[0] * inner, bypass_conv.shape[0] * inner
    masters = (entry_conv, exit_conv, bypass_conv)
    if inner == 1:
        blocks = masters
    else:
        sets = [[o * inner + i for i in range(inner)] for o in range(OUTER)]
        blocks = tuple(
            lax.all_gather(w.astype(BF16), "img", axis=0, tiled=True, axis_index_groups=sets)
            for w in masters
        )

    vmem = pl.BlockSpec(memory_space=pltpu.VMEM)
    smem = pl.BlockSpec(memory_space=pltpu.SMEM)
    anywhere = pl.BlockSpec(memory_space=pl.ANY)
    states = dict(
        entry_m=entry_moment.T,
        entry_q=entry_square.T,
        exit_m=exit_moment.T,
        exit_q=exit_square.T,
        bypass_m=bypass_moment,
        bypass_q=bypass_square,
    )
    inputs = dict(
        labels=(labels, smem),
        groups=(groups, smem),
        widths=(widths, smem),
        features=(features, anywhere),
        cotangent=(cotangent, anywhere),
        entry=(blocks[0].T, anywhere),
        exit=(blocks[1].T, anywhere),
        bypass=(blocks[2], anywhere),
        affine=(norm_affine, anywhere),
    )
    if inner == 1:
        inputs.update({name: (value, anywhere) for name, value in states.items()})
    sds = jax.ShapeDtypeStruct
    outputs = dict(
        out=(sds(cotangent.shape, BF16), vmem),
        dx=(sds(features.shape, BF16), vmem),
        grad1=(sds((local, rows), F32), vmem),
        grad2=(sds((local, rows), F32), vmem),
        grad3=(sds((small, local), F32), vmem),
        affine_grad=(sds((24, 128), F32), vmem),
        norms=(sds((8, 128), F32), vmem),
    )
    pix = pixels * per
    taps9 = 9 * chans
    held = lambda shape, dtype=BF16: pltpu.VMEM(shape, dtype)
    scratch = dict(
        fown=held((batch, local, pixels)),
        cown=held((batch, local, 4 * pixels)),
        fbuf=held((n_ch, per, local, pixels)),
        cbuf=held((n_ch, per, local, 4 * pixels)),
        entry_v=held((local, rows), blocks[0].dtype),
        exit_v=held((local, rows), blocks[1].dtype),
        bypass_v=held((small, local), blocks[2].dtype),
        affine_v=held(norm_affine.shape, F32),
        padded=held((3 * local, 384)),
        wz1=held((n_ch, rows // 2, 128)),
        wz2=held((n_ch, (rows + small) // 2, 128)),
        aff_z=held((n_ch, 24, 128), F32),
        w1=held((taps9, chans)),
        w2=held((taps9, chans)),
        ws=held((chans, chans)),
        w1t=held((taps9, chans)),
        w2t=held((taps9, chans)),
        unpack=held((512, 512)),
        ident=held((256, 256)),
        shift=held((2, 256, 256)),
        gridder=held((512, 256)),
        flatter=held((512, 512)),
        fpm=held((pix, chans)),
        h1s=held((3, per, pixels + 32, chans)),
        h1cm=held((chans, pix)),
        y1=held((4, pix, chans), F32),
        act=held((4, pix, chans), F32),
        h2s=held((2, 4, per, pixels + 32, chans)),
        dzs=held((2, 4, per, pixels + 32, chans)),
        h2cm=held((chans, 4 * pix)),
        short=held((pix, chans), F32),
        dshort=held((pix, chans), F32),
        dzc=held((pix, chans)),
        act1=held((pix, chans), F32),
        rc=held((per, chans, 4 * pixels)),
        ocm=held((per, chans, 4 * pixels)),
        dcm=held((per, chans, pixels)),
        field=held((9, per, pixels, chans)),
        dw1=held((taps9, chans), F32),
        dw2=held((taps9, chans), F32),
        dws=held((chans, chans), F32),
    )
    for number, size in ((1, rows), (2, rows + small)):
        shapes = ((4, size, chans),) * 2 + ((2, 2, size, 128),) * 2 + ((2, size, 128),) * 2
        shapes += ((n_ch, size // 2, 128),) * 2
        for part, shape in zip(PARTS, shapes):
            scratch[part + str(number)] = held(shape)
        scratch[PARTS[-1] + str(number)] = held((4, size, chans), F32)
    exchanges = [(8, 128), (8, chans), (16, chans), (32, chans)]
    if inner == 1:
        exchanges.append((8, 128))
        for v, shape in (("v1", (local, rows)), ("v2", (local, rows)), ("vs", (small, local))):
            scratch[v + "m"] = held(shape, F32)
            scratch[v + "q"] = held(shape, F32)
    for number, shape in enumerate(exchanges, 1):
        for axis, size in zip("abc", (OUTER, inner, n_ch)):
            if size > 1:
                scratch[axis + str(number)] = held((size,) + shape, F32)
    remote_count = 4 * 3 + 3 * 3 * per + 3 * 7 + 2 * 13 + len(exchanges) * (7 + 3 + inner - 1)
    scratch.update(
        send=pltpu.SemaphoreType.DMA((remote_count,)),
        recv=pltpu.SemaphoreType.DMA((remote_count,)),
        lsem=pltpu.SemaphoreType.DMA((20,)),
    )
    cfg = SimpleNamespace(
        names=[*inputs, *outputs, *scratch],
        inner=inner,
        n_ch=n_ch,
        batch=batch,
        local=local,
        classes=classes,
        count=float(batch * n_img // widths.shape[0] * pixels),
        rows=rows,
        small=small,
        used=[],
    )
    out, dx, grad1, grad2, grad3, affine_grad, norms = pl.pallas_call(
        functools.partial(main_kernel, cfg),
        out_shape=[s for s, _ in outputs.values()],
        in_specs=[s for _, s in inputs.values()],
        out_specs=[s for _, s in outputs.values()],
        scratch_shapes=list(scratch.values()),
        compiler_params=pltpu.CompilerParams(
            collective_id=0, has_side_effects=True, vmem_limit_bytes=VMEM_LIMIT
        ),
        name="block_step",
    )(*[v for v, _ in inputs.values()])
    assert max(n for n, _ in cfg.used) <= remote_count and max(n for _, n in cfg.used) <= 20

    grads = [grad1, grad2, grad3]
    if inner > 1:
        grads = [
            lax.psum_scatter(g, "img", scatter_dimension=0, axis_index_groups=sets, tiled=True)
            for g in (grad1.T, grad2.T, grad3)
        ]
        updates = []
        for w, g, m, s in zip(
            masters,
            grads,
            (entry_moment, exit_moment, bypass_moment),
            (entry_square, exit_square, bypass_square),
        ):
            updates.append(adam_update(g, m, s)[2] + WEIGHT_DECAY * w)
        sums = lax.psum(
            jnp.stack([jnp.sum(w * w) for w in masters] + [jnp.sum(u * u) for u in updates]),
            ("img", "ch"),
        )
        norms = jnp.broadcast_to(jnp.pad(sums, (0, 2))[:, None], (8, 128))
        grads = [grads[0].T, grads[1].T, grads[2]]

    args = dict(
        out=out,
        dx=dx,
        norms=norms,
        affine_grad=affine_grad,
        entry_g=grads[0],
        exit_g=grads[1],
        bypass_g=grads[2],
        entry=entry_conv.T,
        exit=exit_conv.T,
        bypass=bypass_conv,
        **states,
        affine=norm_affine,
        affine_m=norm_moment,
        affine_q=norm_square,
    )
    tall = sds(entry_conv.shape[::-1], F32)
    short, wide = (sds(w.shape, F32) for w in (bypass_conv, norm_affine))
    results = dict(
        block_output=sds(cotangent.shape, BF16),
        input_gradient=sds(features.shape, F32),
        entry_1=tall,
        entry_2=tall,
        entry_w=tall,
        exit_1=tall,
        exit_2=tall,
        exit_w=tall,
        bypass_1=short,
        bypass_2=short,
        bypass_w=short,
        affine_1=wide,
        affine_2=wide,
        affine_w=wide,
        trust_norms=sds((3, 3), F32),
    )
    end_cfg = SimpleNamespace(names=[*args, *results], classes=classes, local=local)
    final = pl.pallas_call(
        functools.partial(final_kernel, end_cfg),
        out_shape=list(results.values()),
        in_specs=[vmem] * len(args),
        out_specs=[vmem] * len(results),
        compiler_params=pltpu.CompilerParams(vmem_limit_bytes=VMEM_LIMIT),
        name="finish",
    )(*args.values())
    return tuple(v.T if s is tall else v for v, s in zip(final, results.values()))


def solution(mesh):
    wide = P("img", "ch")
    deep = P("img", "ch", None)
    table = P(None, "ch")
    return jax.shard_map(
        per_device,
        mesh=mesh,
        in_specs=(deep, P("img"), P("img"), P()) + (wide,) * 9 + (table,) * 3 + (deep,),
        out_specs=(deep, deep) + (wide,) * 9 + (table,) * 3 + (P(),),
        check_vma=False,
    )
```

```python
import functools
import math
from types import SimpleNamespace

import jax
import jax.numpy as jnp
from jax import lax
from jax.experimental import pallas as pl
from jax.experimental.pallas import tpu as pltpu
from jax.sharding import PartitionSpec as P

LEVELS = 4
STEP = 5
NORM_EPSILON = 1e-05
ADAM_EPSILON = 1e-06
MOMENT_DECAY = 0.9
SQUARE_DECAY = 0.999
WEIGHT_DECAY = 0.01
MATRIX_RATE = 0.3
AFFINE_RATE = 0.2

OUTER = 8
VMEM_LIMIT = 56 * 1024 * 1024
BF16 = jnp.bfloat16
F32 = jnp.float32
MESH = pl.DeviceIdType.MESH
PARTS = ("s1", "r1", "s2", "r2", "s3", "r3", "s4", "r4", "acc")


def nn(left, right):
    return lax.dot_general(left, right, (((1,), (0,)), ((), ())), preferred_element_type=F32)


def nt(left, right):
    return lax.dot_general(left, right, (((1,), (1,)), ((), ())), preferred_element_type=F32)


def flip(index, mask):
    result = index
    for bit in range(3):
        if (mask >> bit) & 1:
            digit = lax.rem(lax.div(index, 1 << bit), 2)
            result = result + (1 - 2 * digit) * (1 << bit)
    return result


def sigmoid(value):
    return 0.5 * jnp.tanh(0.5 * value) + 0.5


def iota(shape, axis):
    return lax.broadcasted_iota(jnp.int32, shape, axis)


def to_bf16(condition):
    return jnp.where(condition, 1.0, 0.0).astype(BF16)


def pick_row(table, index):
    hit = iota(table.shape, 0) == index
    return jnp.sum(jnp.where(hit, table, 0.0), axis=0, keepdims=True)


def place_row(row, index, rows):
    hit = iota((rows, row.shape[1]), 0) == index
    return jnp.where(hit, row, 0.0)


def colsum(value):
    return jnp.sum(value, axis=0, keepdims=True)


def adam_update(grad, moment, square):
    moment_new = MOMENT_DECAY * moment + (1.0 - MOMENT_DECAY) * grad
    square_new = SQUARE_DECAY * square + (1.0 - SQUARE_DECAY) * grad * grad
    direction = (
        moment_new
        / (1.0 - MOMENT_DECAY**STEP)
        / (jnp.sqrt(square_new / (1.0 - SQUARE_DECAY**STEP)) + ADAM_EPSILON)
    )
    return (moment_new, square_new, direction)


def total(value):
    return jnp.sum(jnp.sum(value, axis=1, keepdims=True), axis=0, keepdims=True)


def main_kernel(cfg, *refs):
    r = SimpleNamespace(**dict(zip(cfg.names, refs)))
    inner, n_ch, batch, local = cfg.inner, cfg.n_ch, cfg.batch, cfg.local
    classes, count = cfg.classes, cfg.count
    per = batch // n_ch
    chans = local * n_ch
    rows, small = cfg.rows, cfg.small
    tail = (rows - 256) // 2
    hw, hs = rows // 2, small // 2
    slots = SimpleNamespace(remote=0, local=0)

    img = lax.axis_index("img")
    me = lax.axis_index("ch")
    block = lax.div(img, inner)
    within = lax.rem(img, inner)
    core = lax.rem(block, 2)
    plane = lax.div(block, 2)
    bit_x, bit_y = lax.rem(plane, 2), lax.div(plane, 2)
    partner = flip(block, 1)

    def dev(block_id, within_id, ch_id):
        return (block_id * inner + within_id, ch_id)

    pending = []

    def post(src, dst, landed, peer):
        slot = slots.remote
        slots.remote = slot + 1
        copy = pltpu.make_async_remote_copy(
            src_ref=src,
            dst_ref=dst,
            send_sem=r.send.at[slot],
            recv_sem=r.recv.at[slot],
            device_id=peer,
            device_id_type=MESH,
        )
        copy.start()
        pending.append(copy.wait_send)
        arrival = pltpu.make_async_remote_copy(
            src_ref=landed,
            dst_ref=landed,
            send_sem=r.send.at[slot],
            recv_sem=r.recv.at[slot],
            device_id=peer,
            device_id_type=MESH,
        )
        return arrival.wait_recv

    def here(src, dst):
        slot = slots.local
        slots.local = slot + 1
        copy = pltpu.make_async_copy(src, dst, r.lsem.at[slot])
        copy.start()
        return copy.wait

    outer_peers = [flip(block, mask) for mask in range(1, OUTER)]
    ch_peers = [flip(me, mask) for mask in range(1, n_ch)]
    inner_pairs = [
        (lax.rem(within + step, inner), lax.rem(within + inner - step, inner))
        for step in range(1, inner)
    ]
    up, down, far = (lax.rem(me + step, n_ch) for step in (1, 3, 2))
    up_peer, down_peer = dev(block, within, up), dev(block, within, down)

    class Ring:
        def __init__(self, source, target, passing):
            self.target, self.passing = target, passing
            self.waits = []
            self.early = [
                post(source(far, 0), passing.at[0], passing.at[0], up_peer),
                post(source(far, 1), passing.at[1], passing.at[1], down_peer),
            ]
            for im in range(per):
                self.waits += [
                    post(source(up, im), target(me, im), target(down, im), up_peer),
                    post(source(down, im), target(me, im), target(up, im), down_peer),
                ]

        def forward(self):
            self.early[0]()
            self.waits.append(
                post(self.passing.at[0], self.target(down, 0), self.target(far, 0), up_peer)
            )
            self.early[1]()
            self.waits.append(
                post(self.passing.at[1], self.target(up, 1), self.target(far, 1), down_peer)
            )

        def settle(self):
            for wait in self.waits:
                wait()

    barrier = pltpu.get_barrier_semaphore()
    everyone = [dev(peer, within, me) for peer in outer_peers]
    everyone += [dev(block, within, peer) for peer in ch_peers]
    everyone += [dev(block, peer, me) for peer, _ in inner_pairs]
    for peer in everyone:
        pl.semaphore_signal(barrier, inc=1, device_id=peer, device_id_type=MESH)

    got_entry = here(r.entry, r.entry_v)
    got_features = here(r.features, r.fown)
    got_exit = here(r.exit, r.exit_v)
    got_bypass = here(r.bypass, r.bypass_v)
    got_affine = here(r.affine, r.affine_v)
    got_cot = here(r.cotangent, r.cown)
    states = ((r.entry_m, r.entry_q), (r.exit_m, r.exit_q), (r.bypass_m, r.bypass_q)) if inner == 1 else ()
    held = [
        (here(m, getattr(r, v + "m")), here(q, getattr(r, v + "q")))
        for (m, q), v in zip(states, ("v1", "v2", "vs"))
    ]

    s_row, s_col = iota((hw, 384), 0), iota((hw, 384), 1)
    pick_first = to_bf16(s_col == jnp.where(s_row < 128, s_row, s_row + 128))
    pick_second = to_bf16(s_col == jnp.where(s_row < 128, s_row + 128, s_row + 128 + tail))
    r.padded[...] = jnp.zeros(r.padded.shape, BF16)

    def pack_own(value):
        r.padded[local : 2 * local, 0:rows] = value.astype(BF16)
        packed = nt(pick_first, r.padded[local : 3 * local, :])
        return (packed + nt(pick_second, r.padded[0 : 2 * local, :])).astype(BF16)

    got_entry()
    r.wz1[me] = pack_own(r.entry_v[...])
    pl.semaphore_wait(barrier, len(everyone))

    def to_channels(buffer):
        return [
            post(buffer.at[me], buffer.at[me], buffer.at[peer], dev(block, within, peer))
            for peer in ch_peers
        ]

    entry_waits = to_channels(r.wz1)
    got_features()
    features = Ring(
        lambda c, im: r.fown.at[per * c + im], lambda c, im: r.fbuf.at[c, im], r.pass_f
    )
    got_affine()
    r.aff_z[me] = jnp.zeros((24, 128), F32)
    r.aff_z[me, 0 : 2 * classes + 3, 0:local] = r.affine_v[...]
    affine_waits = to_channels(r.aff_z)

    lane = iota((512, 512), 0)
    column = iota((512, 512), 1)
    spot = 256 * ((lane >> 6) & 1) + 64 * (lane >> 7) + (lane & 63)
    r.unpack[...] = to_bf16(column == spot)

    r.fbuf[me] = r.fown[pl.ds(per * me, per)]
    flat = jnp.concatenate([r.fown[b] for b in range(batch)], axis=1)
    wide = flat.astype(F32)
    square = wide * wide
    square_hi = square.astype(BF16)
    square_lo = (square - square_hi.astype(F32)).astype(BF16)
    level = iota((16, 256), 0)
    first_mask = jnp.concatenate([to_bf16(level == r.groups[b]) for b in range(batch)], axis=1)
    second_mask = jnp.concatenate([to_bf16(level == r.groups[b] + 4) for b in range(batch)], axis=1)
    sums = nt(first_mask, flat) + nt(second_mask, square_hi) + nt(second_mask, square_lo)

    def ordered_sum(ref, size):
        result = ref[0]
        for slot in range(1, size):
            result = result + ref[slot]
        return result

    class AllReduce:
        def __init__(self, number):
            self.over_outer, self.over_inner, self.over_ch = (
                getattr(r, axis + str(number), None) for axis in "abc"
            )

        def begin(self, value, masked=None):
            ref = self.over_outer
            if masked is None:
                ref[block] = value
            else:
                ref[block] = jnp.zeros(ref.shape[1:], F32)
                ref[block, :, 0:masked] = value
            self.waits = [
                post(ref.at[block], ref.at[block], ref.at[peer], dev(peer, within, me))
                for peer in outer_peers
            ]

        def middle(self):
            for wait in self.waits:
                wait()
            value = ordered_sum(self.over_outer, OUTER)
            if inner > 1:
                ref = self.over_inner
                ref[within] = value
                waits = [
                    post(ref.at[within], ref.at[within], ref.at[back], dev(block, peer, me))
                    for peer, back in inner_pairs
                ]
                for wait in waits:
                    wait()
                value = ordered_sum(ref, inner)
            self.over_ch[me] = value
            self.waits = to_channels(self.over_ch)

        def finish(self):
            for wait in self.waits:
                wait()
            return self.over_ch

        def end(self):
            return ordered_sum(self.finish(), n_ch)

    input_sums = AllReduce(1)
    input_sums.begin(sums[0:8], masked=local)

    got_exit()
    got_bypass()
    r.wz2[me, 0:hw, :] = pack_own(r.exit_v[...])
    e_row, e_col = iota((local, 128), 0), iota((local, 128), 1)
    value = r.bypass_v[...].astype(BF16)
    r.wz2[me, hw : hw + hs, :] = (
        nn(value[:hs], to_bf16(e_col == e_row)) + nn(value[hs:], to_bf16(e_col == e_row + local))
    ).astype(BF16)

    def rows_of(ref, index):
        size = ref.shape[0] // OUTER
        return ref.at[pl.ds(pl.multiple_of(size * index, 16), size)]

    def unpack_own(ref, full):
        own = rows_of(ref, block)
        if full.shape[0] == hw:
            own[0:128, :] = full[0:128, 0:256]
            own[128:256, :] = full[0:128, 256:512]
            own[256 : 256 + tail, :] = full[128:, 0:256]
            own[256 + tail :, :] = full[128:, 256:512]
        else:
            own[0:hs, :] = full[:, 0:256]
            own[hs:, :] = full[:, 256:512]

    def spread(ref):
        own = rows_of(ref, block)
        return {
            mask: post(own, own, rows_of(ref, flip(block, mask)), dev(flip(block, mask), within, me))
            for mask in (2, 4, 6, 1)
        }

    def forward(ref, waits):
        rest = [waits[1]]
        for mask in (2, 4, 6):
            waits[mask]()
            mine = rows_of(ref, flip(block, mask))
            theirs = rows_of(ref, flip(partner, mask))
            rest.append(post(mine, mine, theirs, dev(partner, within, me)))
        return rest

    def widen(buffer):
        packed = jnp.concatenate([buffer[c] for c in range(n_ch)], axis=1)
        return nn(packed, r.unpack[...]).astype(BF16)

    for wait in entry_waits:
        wait()
    unpack_own(r.w1, widen(r.wz1))
    gather1 = spread(r.w1)
    exit_waits = to_channels(r.wz2)

    ident = to_bf16(iota((256, 256), 0) == iota((256, 256), 1))
    r.ident[...] = ident
    q_out, q_in = iota((256, 256), 0), iota((256, 256), 1)
    r.shift[0] = to_bf16((q_in == q_out + 1) & ((q_out & 15) < 15))
    r.shift[1] = to_bf16((q_in == q_out - 1) & ((q_out & 15) > 0))

    input_sums.middle()
    got_cot()
    features.forward()
    cotangent = Ring(
        lambda c, im: r.cown.at[per * c + im], lambda c, im: r.cbuf.at[c, im], r.pass_c
    )

    rho, px = iota((512, 256), 0), iota((512, 256), 1)
    version, a, b_ = rho >> 8, (rho >> 7) & 1, (rho >> 6) & 1
    col = (rho & 15) + version * (1 - 2 * b_)
    target = (2 * ((rho & 63) >> 4) + a) * 32 + 2 * col + b_
    r.gridder[...] = to_bf16((px == target) & (col >= 0) & (col < 16))
    target = (
        (2 * ((lane & 127) >> 4) + (lane >> 8)) * 32 + 2 * (lane & 15) + ((lane >> 7) & 1)
    )
    r.flatter[...] = to_bf16(column == target)
    zeros = jnp.zeros((16, 256), BF16)
    for im in range(per):
        for ver in range(3):
            r.h1s[ver, im, 0:16, :] = zeros
            r.h1s[ver, im, 272:288, :] = zeros
        for ver in range(2):
            for ph in range(4):
                for ref in (r.h2s, r.dzs):
                    ref[ver, ph, im, 0:16, :] = zeros
                    ref[ver, ph, im, 272:288, :] = zeros

    def channel_major(ref, im, lanes):
        return jnp.concatenate([ref[c, im, :, lanes] for c in range(n_ch)], axis=0)

    features.settle()
    for im in range(per):
        r.fpm[256 * im : 256 * im + 256, :] = nt(
            ident, channel_major(r.fbuf, im, slice(0, 256))
        ).astype(BF16)

    def wide_lanes(ref):
        parts = [
            ref[c] + pltpu.roll(ref[c + 1], local, axis=1) for c in range(0, n_ch, 2)
        ]
        return jnp.concatenate(parts, axis=1)

    for wait in affine_waits:
        wait()
    affine = wide_lanes(r.aff_z)
    stats = wide_lanes(input_sums.finish())
    mean1 = stats[0:4] / count
    inv1 = lax.rsqrt(stats[4:8] / count - mean1 * mean1 + NORM_EPSILON)
    gain = affine[2 * classes : 2 * classes + 1]
    shift = affine[2 * classes + 1 : 2 * classes + 2]
    out_bias = affine[2 * classes + 2 : 2 * classes + 3]
    group, label, mean1_b, inv1_b, gamma_b, beta_b, mask_b = [], [], [], [], [], [], []
    for im in range(per):
        group.append(r.groups[per * me + im])
        label.append(r.labels[per * me + im])
        mean1_b.append(pick_row(mean1, group[im]))
        inv1_b.append(pick_row(inv1, group[im]))
        gamma_b.append(pick_row(affine, label[im]))
        beta_b.append(pick_row(affine, label[im] + classes))
        width = r.widths[group[im]]
        mask_b.append(
            jnp.where(iota((1, chans), 1) < width * (chans // LEVELS), 1.0, 0.0)
        )

    for im in range(per):
        normal = (r.fpm[256 * im : 256 * im + 256, :].astype(F32) - mean1_b[im]) * inv1_b[im]
        pre = gamma_b[im] * normal + beta_b[im]
        hidden = (pre * sigmoid(pre)).astype(BF16)
        r.h1s[1, im, 16:272, :] = hidden
        r.h1s[0, im, 16:272, :] = nn(r.shift[1], hidden).astype(BF16)
        r.h1s[2, im, 16:272, :] = nn(r.shift[0], hidden).astype(BF16)
        r.h1cm[:, 256 * im : 256 * im + 256] = nt(ident, hidden).astype(BF16)

    for wait in exit_waits:
        wait()
    full = widen(r.wz2)
    unpack_own(r.w2, full[0:hw])
    unpack_own(r.ws, full[hw:])
    rest = forward(r.w1, gather1)
    gather2 = spread(r.w2)
    gather3 = spread(r.ws)
    for wait in rest:
        wait()

    def taps():
        return [(dy, dx) for dy in range(3) for dx in range(3)]

    def stack(pieces):
        return jnp.concatenate(pieces, axis=0)

    def conv1(phase, carry):
        a, c = lax.div(phase, 2), lax.rem(phase, 2)
        parts = []
        for dy, dx in taps():
            first = pl.multiple_of(16 * lax.div(a + dy + 1, 2), 16)
            ver = lax.div(c + dx + 1, 2)
            parts.append(
                stack([r.h1s[ver, im, pl.ds(first, 256), :] for im in range(per)])
            )
        y = nn(jnp.concatenate(parts, axis=1), r.w1[...])
        r.y1[phase] = y
        out = []
        for im in range(per):
            piece = y[256 * im : 256 * im + 256]
            out.append(carry[2 * im] + colsum(piece))
            out.append(carry[2 * im + 1] + colsum(piece * piece))
        return tuple(out)

    nought = jnp.zeros((1, chans), F32)
    mid = lax.fori_loop(0, 4, conv1, (nought,) * (2 * per))
    payload = jnp.zeros((8, chans), F32)
    for im in range(per):
        payload = payload + place_row(mid[2 * im], group[im], 8)
        payload = payload + place_row(mid[2 * im + 1], group[im] + 4, 8)
    mid_sums = AllReduce(2)
    mid_sums.begin(payload)

    def turn(src, dst):
        def one(tap, carry):
            first = pl.multiple_of(256 * tap, 256)
            dst[pl.ds(first, 256), :] = nt(r.ident[...], src[pl.ds(first, 256), :]).astype(BF16)
            return carry

        lax.fori_loop(0, 9, one, 0)

    cotangent.forward()
    turn(r.w1, r.w1t)
    rest = forward(r.w2, gather2) + forward(r.ws, gather3)
    mid_sums.middle()

    r.cbuf[me] = r.cown[pl.ds(per * me, per)]
    cotangent.settle()
    for im in range(per):
        for n in range(4):
            piece = channel_major(r.cbuf, im, slice(256 * n, 256 * n + 256))
            grid = nt(r.gridder[...], piece).astype(BF16)
            for ver in range(2):
                for ph in range(4):
                    at = 256 * ver + 64 * ph
                    r.dzs[ver, ph, im, 16 + 64 * n : 80 + 64 * n, :] = grid[at : at + 64]

    coarse = jnp.zeros((256 * per, chans), F32)
    for ph in range(4):
        coarse = coarse + stack([r.dzs[0, ph, im, 16:272, :] for im in range(per)]).astype(F32)
    bias_sum = colsum(coarse)
    r.dzc[...] = coarse.astype(BF16)

    def tap_slice(ref, a, c, dy, dx, im):
        row, colm = a + dy + 1, c + dx + 1
        first = pl.multiple_of(16 * lax.div(row, 2), 16)
        ph = 2 * lax.rem(row, 2) + lax.rem(colm, 2)
        side_step = lax.div(colm, 2) - 1
        return ref[side_step * side_step, ph, im, pl.ds(first, 256), :]

    for wait in rest:
        wait()
    turn(r.w2, r.w2t)

    def back2(phase, carry):
        a, c = lax.div(phase, 2), lax.rem(phase, 2)
        parts = [
            stack([tap_slice(r.dzs, a, c, 2 - dy, 2 - dx, im) for im in range(per)])
            for dy, dx in taps()
        ]
        r.act[phase] = nn(jnp.concatenate(parts, axis=1), r.w2t[...])
        return carry

    lax.fori_loop(0, 4, back2, 0)

    stats = mid_sums.end()
    mean2 = stats[0:4] / (4.0 * count)
    inv2 = lax.rsqrt(stats[4:8] / (4.0 * count) - mean2 * mean2 + NORM_EPSILON)
    mean2_b = [pick_row(mean2, group[im]) for im in range(per)]
    inv2_b = [pick_row(inv2, group[im]) for im in range(per)]

    def hidden2(phase, carry):
        c = lax.rem(phase, 2)
        out = []
        for im in range(per):
            span = slice(256 * im, 256 * im + 256)
            normal = (r.y1[phase, span, :] - mean2_b[im]) * inv2_b[im]
            r.y1[phase, span, :] = normal
            pre = gain * normal + shift
            sig = sigmoid(pre)
            hidden = (pre * sig * mask_b[im]).astype(BF16)
            act = r.act[phase, span, :] * (sig * (1.0 + pre * (1.0 - sig)) * mask_b[im])
            r.act[phase, span, :] = act
            out.append(carry[2 * im] + colsum(act))
            out.append(carry[2 * im + 1] + colsum(act * normal))
            r.h2s[0, phase, im, 16:272, :] = hidden
            r.h2s[1, phase, im, 16:272, :] = nn(r.shift[c], hidden).astype(BF16)
            lanes = pl.ds(pl.multiple_of(512 * phase + 256 * im, 256), 256)
            r.h2cm[:, lanes] = nt(r.ident[...], hidden).astype(BF16)
        return tuple(out)

    mid = lax.fori_loop(0, 4, hidden2, (nought,) * (2 * per))
    payload = place_row(bias_sum, 8, 16)
    for im in range(per):
        payload = payload + place_row(mid[2 * im], group[im], 16)
        payload = payload + place_row(mid[2 * im + 1], group[im] + 4, 16)
    back_sums = AllReduce(3)
    back_sums.begin(payload)

    r.short[...] = nn(r.fpm[...], r.ws[...]) + out_bias
    def conv2(phase, carry):
        a, c = lax.div(phase, 2), lax.rem(phase, 2)
        parts = [
            stack([tap_slice(r.h2s, a, c, dy, dx, im) for im in range(per)]) for dy, dx in taps()
        ]
        y = (nn(jnp.concatenate(parts, axis=1), r.w2[...]) + r.short[...]).astype(BF16)
        lanes = pl.ds(pl.multiple_of(256 * phase, 256), 256)
        for im in range(per):
            r.rc[im, :, lanes] = nt(r.ident[...], y[256 * im : 256 * im + 256]).astype(BF16)
        return carry

    lax.fori_loop(0, 4, conv2, 0)
    for im in range(per):
        for half in range(2):
            piece = jnp.concatenate(
                [r.rc[im, :, 256 * ph + 128 * half : 256 * ph + 128 * half + 128] for ph in range(4)],
                axis=1,
            )
            r.ocm[im, :, 512 * half : 512 * half + 512] = nn(piece, r.flatter[...]).astype(BF16)

    def own_channels(ref, index, im):
        return ref.at[im, pl.ds(pl.multiple_of(local * index, local), local), :]

    def give_back(ref, out, passing):
        for im in range(per):
            out[per * me + im] = own_channels(ref, me, im)[...]
        return Ring(
            lambda c, im: own_channels(ref, c, im), lambda c, im: out.at[per * c + im], passing
        )

    block_output = give_back(r.ocm, r.out, r.pass_o)

    def grad2(tap, carry):
        dy, dx = lax.div(tap, 3), lax.rem(tap, 3)
        pieces = []
        for ph in range(4):
            a, c = ph // 2, ph % 2
            for im in range(per):
                pieces.append(tap_slice(r.dzs, a, c, 2 - dy, 2 - dx, im))
        first = pl.multiple_of(256 * tap, 256)
        r.dw2[pl.ds(first, 256), :] = nn(r.h2cm[...], stack(pieces))
        return carry

    back_sums.middle()
    lax.fori_loop(0, 9, grad2, 0)
    for im in range(per):
        piece = channel_major(r.fbuf, im, slice(0, 256))
        grad = nn(piece, r.dzc[256 * im : 256 * im + 256, :])
        if im == 0:
            r.dws[...] = grad
        else:
            r.dws[...] = r.dws[...] + grad

    class GradSum:
        def __init__(self, number, fetch):
            self.fetch = fetch
            for part in PARTS:
                setattr(self, part, getattr(r, part + str(number)))

        def begin(self):
            self.waits = []
            for u in range(4):
                self.s1[u] = self.fetch(2 * u + 1 - core).astype(BF16)
                self.waits.append(
                    post(self.s1.at[u], self.r1.at[u], self.r1.at[u], dev(partner, within, me))
                )

        def settle(self):
            for wait in self.waits:
                wait()

        def across(self, send, got, masks):
            parts = [(h, v) for v in range(2) for h in range(2)] if len(send.shape) == 4 else [(0,), (1,)]
            self.waits = [
                post(send.at[p], got.at[p], got.at[p], dev(flip(block, masks[p[0]]), within, me))
                for p in parts
            ]

        def first(self):
            for u in range(4):
                self.waits[u]()
                self.acc[u] = self.fetch(2 * u + core) + self.r1[u].astype(F32)
            for v in range(2):
                self.s2[0, v] = self.acc[2 * v + 1 - bit_x, :, 0:128].astype(BF16)
                self.s2[1, v] = self.acc[2 * (1 - bit_y) + v, :, 128:256].astype(BF16)
            self.across(self.s2, self.r2, (2, 4))

        def second(self):
            self.settle()
            low = self.acc[2 * (1 - bit_y) + bit_x, :, 0:128] + self.r2[0, 1 - bit_y].astype(F32)
            high = self.acc[2 * bit_y + 1 - bit_x, :, 128:256] + self.r2[1, 1 - bit_x].astype(F32)
            self.s3[0] = low.astype(BF16)
            self.s3[1] = high.astype(BF16)
            self.across(self.s3, self.r3, (4, 2))

        def third(self):
            self.settle()
            low = self.acc[plane, :, 0:128] + self.r2[0, bit_y].astype(F32)
            high = self.acc[plane, :, 128:256] + self.r2[1, bit_x].astype(F32)
            low, high = low + self.r3[0].astype(F32), high + self.r3[1].astype(F32)
            value = jnp.concatenate([low, high], axis=1).astype(BF16)
            left = [value[0:128], value[256 : 256 + tail]]
            right = [value[128:256], value[256 + tail : rows]]
            if value.shape[0] > rows:
                left.append(value[rows : rows + hs])
                right.append(value[rows + hs :])
            pair = jnp.concatenate([stack(left), stack(right)], axis=1)
            packed = nt(pair, r.unpack[...]).astype(BF16)
            for c in range(n_ch):
                self.s4[c] = packed[:, 128 * c : 128 * c + 128]
            self.r4[me] = self.s4[me]
            self.waits = [
                post(self.s4.at[peer], self.r4.at[me], self.r4.at[peer], dev(block, within, peer))
                for peer in ch_peers
            ]

        def end(self, out, out_small=None):
            self.settle()
            done = self.r4[0].astype(F32)
            for c in range(1, n_ch):
                done = done + self.r4[c].astype(F32)
            turned = done[0:128].T
            out[:, 0:128] = turned[0:local]
            out[:, 128:256] = turned[local:]
            gap = jnp.zeros((128 - tail, 128), F32)
            turned = stack([done[128 : 128 + tail], gap]).T
            ends = turned[0:local] + pltpu.roll(turned[local:], tail, axis=1)
            out[:, 256:rows] = ends[:, 0 : rows - 256]
            if out_small is not None:
                last = done[hw:]
                out_small[0:hs, :] = last[:, 0:local]
                out_small[hs:, :] = pltpu.roll(last, local, axis=1)[:, 0:local]

    def block_rows(ref, size, index):
        return ref[pl.ds(pl.multiple_of(size * index, 8), size), :]

    second = GradSum(2, lambda k: stack([block_rows(r.dw2, rows, k), block_rows(r.dws, small, k)]))
    entry = GradSum(1, lambda k: block_rows(r.dw1, rows, k))
    second.begin()
    r.dshort[...] = nt(r.dzc[...], r.ws[...])

    stats = back_sums.end()
    affine_grad2 = stats
    p1_b = [pick_row(stats[0:4], group[im]) / (4.0 * count) for im in range(per)]
    p2_b = [pick_row(stats[4:8], group[im]) / (4.0 * count) for im in range(per)]

    for im in range(per):
        span = slice(256 * im, 256 * im + 256)
        scale = gain * inv2_b[im]
        combos = []
        for a in range(2):
            grads = []
            for c in range(2):
                ph = 2 * a + c
                d = scale * (r.act[ph, span, :] - (p1_b[im] + r.y1[ph, span, :] * p2_b[im]))
                grads.append(d.astype(BF16))
            right = nn(r.shift[0], grads[0])
            left = nn(r.shift[1], grads[1])
            even, odd = grads[0].astype(F32), grads[1].astype(F32)
            combos.append((odd + right, even + odd, left + even))
        gap = jnp.zeros((16, chans), F32)
        for dx in range(3):
            upper, lower = combos[0][dx], combos[1][dx]
            r.field[dx, im] = (lower + stack([upper[16:], gap])).astype(BF16)
            r.field[3 + dx, im] = (upper + lower).astype(BF16)
            r.field[6 + dx, im] = (stack([gap, lower[:-16]]) + upper).astype(BF16)

    block_output.forward()

    def grad1(tap, carry):
        first = pl.multiple_of(256 * tap, 256)
        r.dw1[pl.ds(first, 256), :] = nn(
            r.h1cm[...], stack([r.field[tap, im] for im in range(per)])
        )
        return carry

    lax.fori_loop(0, 9, grad1, 0)
    entry.begin()
    second.first()

    parts = [stack([r.field[tap, im] for im in range(per)]) for tap in range(9)]
    dh1 = nn(jnp.concatenate(parts, axis=1), r.w1t[...])
    payload = jnp.zeros((32, chans), F32)
    for im in range(per):
        span = slice(256 * im, 256 * im + 256)
        normal = (r.fpm[span, :].astype(F32) - mean1_b[im]) * inv1_b[im]
        pre = gamma_b[im] * normal + beta_b[im]
        sig = sigmoid(pre)
        act = dh1[span] * (sig * (1.0 + pre * (1.0 - sig)))
        r.act1[span, :] = act
        q1, q2 = colsum(act), colsum(act * normal)
        payload = payload + place_row(q2, label[im], 32)
        payload = payload + place_row(q1, label[im] + classes, 32)
        payload = payload + place_row(gamma_b[im] * q1, group[im] + 24, 32)
        payload = payload + place_row(gamma_b[im] * q2, group[im] + 28, 32)
    last_sums = AllReduce(4)
    last_sums.begin(payload)
    second.second()
    entry.first()
    last_sums.middle()
    second.third()
    entry.second()

    stats = last_sums.end()
    for im in range(per):
        span = slice(256 * im, 256 * im + 256)
        normal = (r.fpm[span, :].astype(F32) - mean1_b[im]) * inv1_b[im]
        r1 = pick_row(stats[24:28], group[im]) / count
        r2 = pick_row(stats[28:32], group[im]) / count
        grad = inv1_b[im] * (gamma_b[im] * r.act1[span, :] - (r1 + normal * r2))
        grad = (grad + r.dshort[span, :]).astype(BF16)
        r.dcm[im] = nt(r.ident[...], grad).astype(BF16)
    input_gradient = give_back(r.dcm, r.dx, r.pass_x)
    entry.third()
    second.end(r.grad2, r.grad3)
    input_gradient.forward()

    table = jnp.zeros((24, chans), F32)
    table = table + jnp.where(iota((24, chans), 0) < 2 * classes, stats[0:24], 0.0)
    table = table + place_row(colsum(affine_grad2[4:8]), 2 * classes, 24)
    table = table + place_row(colsum(affine_grad2[0:4]), 2 * classes + 1, 24)
    table = table + place_row(affine_grad2[8:9], 2 * classes + 2, 24)
    mine = jnp.zeros((24, 128), F32)
    for c in range(n_ch):
        piece = table[:, 128 * (c // 2) : 128 * (c // 2) + 128]
        if c % 2:
            piece = pltpu.roll(piece, local, axis=1)
        mine = mine + jnp.where(me == c, piece, 0.0)
    r.affine_grad[...] = mine

    if inner == 1:
        row = iota((8, 128), 0)

        def norm_rows(index, weight, grad, v):
            for wait in held[index]:
                wait()
            master = weight[...]
            _, _, direction = adam_update(
                grad[...], getattr(r, v + "m")[...], getattr(r, v + "q")[...]
            )
            update = direction + WEIGHT_DECAY * master
            rows_w = jnp.where(row == index, total(master * master), 0.0)
            return rows_w + jnp.where(row == index + 3, total(update * update), 0.0)

        norms = norm_rows(1, r.exit_v, r.grad2, "v2") + norm_rows(2, r.bypass_v, r.grad3, "vs")
        entry.end(r.grad1)
        norms = norms + norm_rows(0, r.entry_v, r.grad1, "v1")
        norm_sums = AllReduce(5)
        norm_sums.begin(norms)
        norm_sums.middle()
        r.norms[...] = norm_sums.end()
    else:
        entry.end(r.grad1)
        r.norms[...] = jnp.zeros((8, 128), F32)

    block_output.settle()
    input_gradient.settle()
    for wait in pending:
        wait()
    cfg.used.append((slots.remote, slots.local))


def final_kernel(cfg, *refs):
    r = SimpleNamespace(**dict(zip(cfg.names, refs)))
    classes = cfg.classes
    local = cfg.local
    r.block_output[...] = r.out[...]
    r.input_gradient[...] = r.dx[...].astype(F32)
    norms = jnp.sqrt(r.norms[...])
    weight_norm, update_norm = norms[0:3, 0:1], norms[3:6, 0:1]
    ratio = weight_norm / update_norm
    at = iota((3, 3), 1)
    r.trust_norms[...] = jnp.where(
        at == 0, weight_norm, jnp.where(at == 1, update_norm, ratio)
    )
    sets = (
        (r.entry, r.entry_m, r.entry_q, r.entry_g, r.entry_1, r.entry_2, r.entry_w),
        (r.exit, r.exit_m, r.exit_q, r.exit_g, r.exit_1, r.exit_2, r.exit_w),
        (r.bypass, r.bypass_m, r.bypass_q, r.bypass_g, r.bypass_1, r.bypass_2, r.bypass_w),
    )
    for index, (weight, m, q, g, first, second, result) in enumerate(sets):
        master = weight[...]
        moment, square, direction = adam_update(g[...], m[...], q[...])
        update = direction + WEIGHT_DECAY * master
        first[...] = moment
        second[...] = square
        result[...] = master - MATRIX_RATE * ratio[index : index + 1] * update
    grad = r.affine_grad[0 : 2 * classes + 3, 0:local]
    moment, square, direction = adam_update(grad, r.affine_m[...], r.affine_q[...])
    r.affine_1[...] = moment
    r.affine_2[...] = square
    r.affine_w[...] = r.affine[...] - AFFINE_RATE * direction


def per_device(
    features,
    labels,
    groups,
    widths,
    entry_conv,
    entry_moment,
    entry_square,
    exit_conv,
    exit_moment,
    exit_square,
    bypass_conv,
    bypass_moment,
    bypass_square,
    norm_affine,
    norm_moment,
    norm_square,
    cotangent,
):
    n_img, n_ch = lax.axis_size("img"), lax.axis_size("ch")
    batch, local, pixels = features.shape
    chans = local * n_ch
    side = math.isqrt(pixels)
    inner = n_img // OUTER
    classes = (norm_affine.shape[0] - 3) // 2
    per = batch // n_ch
    assert (side, chans, n_ch, local, batch % n_ch) == (16, 256, 4, 64, 0) and per == 2
    rows, small = entry_conv.shape[0] * inner, bypass_conv.shape[0] * inner
    masters = (entry_conv, exit_conv, bypass_conv)
    if inner == 1:
        blocks = masters
    else:
        sets = [[o * inner + i for i in range(inner)] for o in range(OUTER)]
        blocks = tuple(
            lax.all_gather(w.astype(BF16), "img", axis=0, tiled=True, axis_index_groups=sets)
            for w in masters
        )

    vmem = pl.BlockSpec(memory_space=pltpu.VMEM)
    smem = pl.BlockSpec(memory_space=pltpu.SMEM)
    anywhere = pl.BlockSpec(memory_space=pl.ANY)
    states = dict(
        entry_m=entry_moment.T,
        entry_q=entry_square.T,
        exit_m=exit_moment.T,
        exit_q=exit_square.T,
        bypass_m=bypass_moment,
        bypass_q=bypass_square,
    )
    inputs = dict(
        labels=(labels, smem),
        groups=(groups, smem),
        widths=(widths, smem),
        features=(features, anywhere),
        cotangent=(cotangent, anywhere),
        entry=(blocks[0].T, anywhere),
        exit=(blocks[1].T, anywhere),
        bypass=(blocks[2], anywhere),
        affine=(norm_affine, anywhere),
    )
    if inner == 1:
        inputs.update({name: (value, anywhere) for name, value in states.items()})
    sds = jax.ShapeDtypeStruct
    outputs = dict(
        out=(sds(cotangent.shape, BF16), vmem),
        dx=(sds(features.shape, BF16), vmem),
        grad1=(sds((local, rows), F32), vmem),
        grad2=(sds((local, rows), F32), vmem),
        grad3=(sds((small, local), F32), vmem),
        affine_grad=(sds((24, 128), F32), vmem),
        norms=(sds((8, 128), F32), vmem),
    )
    pix = pixels * per
    taps9 = 9 * chans
    held = lambda shape, dtype=BF16: pltpu.VMEM(shape, dtype)
    scratch = dict(
        fown=held((batch, local, pixels)),
        cown=held((batch, local, 4 * pixels)),
        pass_f=held((2, local, pixels)),
        pass_c=held((2, local, 4 * pixels)),
        pass_o=held((2, local, 4 * pixels)),
        pass_x=held((2, local, pixels)),
        fbuf=held((n_ch, per, local, pixels)),
        cbuf=held((n_ch, per, local, 4 * pixels)),
        entry_v=held((local, rows), blocks[0].dtype),
        exit_v=held((local, rows), blocks[1].dtype),
        bypass_v=held((small, local), blocks[2].dtype),
        affine_v=held(norm_affine.shape, F32),
        padded=held((3 * local, 384)),
        wz1=held((n_ch, rows // 2, 128)),
        wz2=held((n_ch, (rows + small) // 2, 128)),
        aff_z=held((n_ch, 24, 128), F32),
        w1=held((taps9, chans)),
        w2=held((taps9, chans)),
        ws=held((chans, chans)),
        w1t=held((taps9, chans)),
        w2t=held((taps9, chans)),
        unpack=held((512, 512)),
        ident=held((256, 256)),
        shift=held((2, 256, 256)),
        gridder=held((512, 256)),
        flatter=held((512, 512)),
        fpm=held((pix, chans)),
        h1s=held((3, per, pixels + 32, chans)),
        h1cm=held((chans, pix)),
        y1=held((4, pix, chans), F32),
        act=held((4, pix, chans), F32),
        h2s=held((2, 4, per, pixels + 32, chans)),
        dzs=held((2, 4, per, pixels + 32, chans)),
        h2cm=held((chans, 4 * pix)),
        short=held((pix, chans), F32),
        dshort=held((pix, chans), F32),
        dzc=held((pix, chans)),
        act1=held((pix, chans), F32),
        rc=held((per, chans, 4 * pixels)),
        ocm=held((per, chans, 4 * pixels)),
        dcm=held((per, chans, pixels)),
        field=held((9, per, pixels, chans)),
        dw1=held((taps9, chans), F32),
        dw2=held((taps9, chans), F32),
        dws=held((chans, chans), F32),
    )
    for number, size in ((1, rows), (2, rows + small)):
        shapes = ((4, size, chans),) * 2 + ((2, 2, size, 128),) * 2 + ((2, size, 128),) * 2
        shapes += ((n_ch, size // 2, 128),) * 2
        for part, shape in zip(PARTS, shapes):
            scratch[part + str(number)] = held(shape)
        scratch[PARTS[-1] + str(number)] = held((4, size, chans), F32)
    exchanges = [(8, 128), (8, chans), (16, chans), (32, chans)]
    if inner == 1:
        exchanges.append((8, 128))
        for v, shape in (("v1", (local, rows)), ("v2", (local, rows)), ("vs", (small, local))):
            scratch[v + "m"] = held(shape, F32)
            scratch[v + "q"] = held(shape, F32)
    for number, shape in enumerate(exchanges, 1):
        for axis, size in zip("abc", (OUTER, inner, n_ch)):
            if size > 1:
                scratch[axis + str(number)] = held((size,) + shape, F32)
    remote_count = 3 * 3 + 4 * 4 * per + 3 * 7 + 2 * 13 + len(exchanges) * (7 + 3 + inner - 1)
    scratch.update(
        send=pltpu.SemaphoreType.DMA((remote_count,)),
        recv=pltpu.SemaphoreType.DMA((remote_count,)),
        lsem=pltpu.SemaphoreType.DMA((20,)),
    )
    cfg = SimpleNamespace(
        names=[*inputs, *outputs, *scratch],
        inner=inner,
        n_ch=n_ch,
        batch=batch,
        local=local,
        classes=classes,
        count=float(batch * n_img // widths.shape[0] * pixels),
        rows=rows,
        small=small,
        used=[],
    )
    out, dx, grad1, grad2, grad3, affine_grad, norms = pl.pallas_call(
        functools.partial(main_kernel, cfg),
        out_shape=[s for s, _ in outputs.values()],
        in_specs=[s for _, s in inputs.values()],
        out_specs=[s for _, s in outputs.values()],
        scratch_shapes=list(scratch.values()),
        compiler_params=pltpu.CompilerParams(
            collective_id=0, has_side_effects=True, vmem_limit_bytes=VMEM_LIMIT
        ),
        name="block_step",
    )(*[v for v, _ in inputs.values()])
    assert max(n for n, _ in cfg.used) <= remote_count and max(n for _, n in cfg.used) <= 20

    grads = [grad1, grad2, grad3]
    if inner > 1:
        grads = [
            lax.psum_scatter(g, "img", scatter_dimension=0, axis_index_groups=sets, tiled=True)
            for g in (grad1.T, grad2.T, grad3)
        ]
        updates = []
        for w, g, m, s in zip(
            masters,
            grads,
            (entry_moment, exit_moment, bypass_moment),
            (entry_square, exit_square, bypass_square),
        ):
            updates.append(adam_update(g, m, s)[2] + WEIGHT_DECAY * w)
        sums = lax.psum(
            jnp.stack([jnp.sum(w * w) for w in masters] + [jnp.sum(u * u) for u in updates]),
            ("img", "ch"),
        )
        norms = jnp.broadcast_to(jnp.pad(sums, (0, 2))[:, None], (8, 128))
        grads = [grads[0].T, grads[1].T, grads[2]]

    args = dict(
        out=out,
        dx=dx,
        norms=norms,
        affine_grad=affine_grad,
        entry_g=grads[0],
        exit_g=grads[1],
        bypass_g=grads[2],
        entry=entry_conv.T,
        exit=exit_conv.T,
        bypass=bypass_conv,
        **states,
        affine=norm_affine,
        affine_m=norm_moment,
        affine_q=norm_square,
    )
    tall = sds(entry_conv.shape[::-1], F32)
    short, wide = (sds(w.shape, F32) for w in (bypass_conv, norm_affine))
    results = dict(
        block_output=sds(cotangent.shape, BF16),
        input_gradient=sds(features.shape, F32),
        entry_1=tall,
        entry_2=tall,
        entry_w=tall,
        exit_1=tall,
        exit_2=tall,
        exit_w=tall,
        bypass_1=short,
        bypass_2=short,
        bypass_w=short,
        affine_1=wide,
        affine_2=wide,
        affine_w=wide,
        trust_norms=sds((3, 3), F32),
    )
    end_cfg = SimpleNamespace(names=[*args, *results], classes=classes, local=local)
    final = pl.pallas_call(
        functools.partial(final_kernel, end_cfg),
        out_shape=list(results.values()),
        in_specs=[vmem] * len(args),
        out_specs=[vmem] * len(results),
        compiler_params=pltpu.CompilerParams(vmem_limit_bytes=VMEM_LIMIT),
        name="finish",
    )(*args.values())
    return tuple(v.T if s is tall else v for v, s in zip(final, results.values()))


def solution(mesh):
    wide = P("img", "ch")
    deep = P("img", "ch", None)
    table = P(None, "ch")
    return jax.shard_map(
        per_device,
        mesh=mesh,
        in_specs=(deep, P("img"), P("img"), P()) + (wide,) * 9 + (table,) * 3 + (deep,),
        out_specs=(deep, deep) + (wide,) * 9 + (table,) * 3 + (P(),),
        check_vma=False,
    )
```

```python
import functools
import math
from types import SimpleNamespace

import jax
import jax.numpy as jnp
from jax import lax
from jax.experimental import pallas as pl
from jax.experimental.pallas import tpu as pltpu
from jax.sharding import PartitionSpec as P

LEVELS = 4
STEP = 5
NORM_EPSILON = 1e-05
ADAM_EPSILON = 1e-06
MOMENT_DECAY = 0.9
SQUARE_DECAY = 0.999
WEIGHT_DECAY = 0.01
MATRIX_RATE = 0.3
AFFINE_RATE = 0.2

OUTER = 8
VMEM_LIMIT = 56 * 1024 * 1024
BF16 = jnp.bfloat16
F32 = jnp.float32
MESH = pl.DeviceIdType.MESH
PARTS = ("s1", "r1", "s2", "r2", "s3", "r3", "s4", "r4", "acc")


def nn(left, right):
    return lax.dot_general(left, right, (((1,), (0,)), ((), ())), preferred_element_type=F32)


def nt(left, right):
    return lax.dot_general(left, right, (((1,), (1,)), ((), ())), preferred_element_type=F32)


def flip(index, mask):
    result = index
    for bit in range(3):
        if (mask >> bit) & 1:
            digit = lax.rem(lax.div(index, 1 << bit), 2)
            result = result + (1 - 2 * digit) * (1 << bit)
    return result


def sigmoid(value):
    return 0.5 * jnp.tanh(0.5 * value) + 0.5


def iota(shape, axis):
    return lax.broadcasted_iota(jnp.int32, shape, axis)


def to_bf16(condition):
    return jnp.where(condition, 1.0, 0.0).astype(BF16)


def pick_row(table, index):
    hit = iota(table.shape, 0) == index
    return jnp.sum(jnp.where(hit, table, 0.0), axis=0, keepdims=True)


def place_row(row, index, rows):
    hit = iota((rows, row.shape[1]), 0) == index
    return jnp.where(hit, row, 0.0)


def colsum(value):
    return jnp.sum(value, axis=0, keepdims=True)


def adam_update(grad, moment, square):
    moment_new = MOMENT_DECAY * moment + (1.0 - MOMENT_DECAY) * grad
    square_new = SQUARE_DECAY * square + (1.0 - SQUARE_DECAY) * grad * grad
    direction = (
        moment_new
        / (1.0 - MOMENT_DECAY**STEP)
        / (jnp.sqrt(square_new / (1.0 - SQUARE_DECAY**STEP)) + ADAM_EPSILON)
    )
    return (moment_new, square_new, direction)


def total(value):
    return jnp.sum(jnp.sum(value, axis=1, keepdims=True), axis=0, keepdims=True)


def main_kernel(cfg, *refs):
    r = SimpleNamespace(**dict(zip(cfg.names, refs)))
    inner, n_ch, batch, local = cfg.inner, cfg.n_ch, cfg.batch, cfg.local
    classes, count = cfg.classes, cfg.count
    per = batch // n_ch
    chans = local * n_ch
    rows, small = cfg.rows, cfg.small
    tail = (rows - 256) // 2
    hw, hs = rows // 2, small // 2
    slots = SimpleNamespace(remote=0, local=0)

    img = lax.axis_index("img")
    me = lax.axis_index("ch")
    block = lax.div(img, inner)
    within = lax.rem(img, inner)
    core = lax.rem(block, 2)
    plane = lax.div(block, 2)
    bit_x, bit_y = lax.rem(plane, 2), lax.div(plane, 2)
    partner = flip(block, 1)

    def dev(block_id, within_id, ch_id):
        return (block_id * inner + within_id, ch_id)

    pending = []
    scopes = []

    def scope(name):
        if scopes:
            scopes.pop().__exit__(None, None, None)
        if name:
            scopes.append(jax.named_scope(name))
            scopes[-1].__enter__()


    def post(src, dst, landed, peer):
        slot = slots.remote
        slots.remote = slot + 1
        copy = pltpu.make_async_remote_copy(
            src_ref=src,
            dst_ref=dst,
            send_sem=r.send.at[slot],
            recv_sem=r.recv.at[slot],
            device_id=peer,
            device_id_type=MESH,
        )
        copy.start()
        pending.append(copy.wait_send)
        arrival = pltpu.make_async_remote_copy(
            src_ref=landed,
            dst_ref=landed,
            send_sem=r.send.at[slot],
            recv_sem=r.recv.at[slot],
            device_id=peer,
            device_id_type=MESH,
        )
        return arrival.wait_recv

    def here(src, dst):
        slot = slots.local
        slots.local = slot + 1
        copy = pltpu.make_async_copy(src, dst, r.lsem.at[slot])
        copy.start()
        return copy.wait

    outer_peers = [flip(block, mask) for mask in range(1, OUTER)]
    ch_peers = [flip(me, mask) for mask in range(1, n_ch)]
    inner_pairs = [
        (lax.rem(within + step, inner), lax.rem(within + inner - step, inner))
        for step in range(1, inner)
    ]
    barrier = pltpu.get_barrier_semaphore()
    everyone = [dev(peer, within, me) for peer in outer_peers]
    everyone += [dev(block, within, peer) for peer in ch_peers]
    everyone += [dev(block, peer, me) for peer, _ in inner_pairs]
    for peer in everyone:
        pl.semaphore_signal(barrier, inc=1, device_id=peer, device_id_type=MESH)

    scope("setup")
    got_entry = here(r.entry, r.entry_v)
    got_features = here(r.features, r.fown)
    got_exit = here(r.exit, r.exit_v)
    got_bypass = here(r.bypass, r.bypass_v)
    got_affine = here(r.affine, r.affine_v)
    got_cot = here(r.cotangent, r.cown)
    states = ((r.entry_m, r.entry_q), (r.exit_m, r.exit_q), (r.bypass_m, r.bypass_q)) if inner == 1 else ()
    held = [
        (here(m, getattr(r, v + "m")), here(q, getattr(r, v + "q")))
        for (m, q), v in zip(states, ("v1", "v2", "vs"))
    ]

    s_row, s_col = iota((hw, 384), 0), iota((hw, 384), 1)
    pick_first = to_bf16(s_col == jnp.where(s_row < 128, s_row, s_row + 128))
    pick_second = to_bf16(s_col == jnp.where(s_row < 128, s_row + 128, s_row + 128 + tail))
    r.padded[...] = jnp.zeros(r.padded.shape, BF16)

    def pack_own(value):
        r.padded[local : 2 * local, 0:rows] = value.astype(BF16)
        packed = nt(pick_first, r.padded[local : 3 * local, :])
        return (packed + nt(pick_second, r.padded[0 : 2 * local, :])).astype(BF16)

    got_entry()
    r.wz1[me] = pack_own(r.entry_v[...])
    scope("barrier")
    pl.semaphore_wait(barrier, len(everyone))

    def to_channels(buffer):
        return [
            post(buffer.at[me], buffer.at[me], buffer.at[peer], dev(block, within, peer))
            for peer in ch_peers
        ]

    scope("stats")
    entry_waits = to_channels(r.wz1)
    got_features()
    feature_waits = [
        post(
            r.fown.at[pl.ds(per * peer, per)],
            r.fbuf.at[me],
            r.fbuf.at[peer],
            dev(block, within, peer),
        )
        for peer in ch_peers
    ]
    got_affine()
    r.aff_z[me] = jnp.zeros((24, 128), F32)
    r.aff_z[me, 0 : 2 * classes + 3, 0:local] = r.affine_v[...]
    affine_waits = to_channels(r.aff_z)

    lane = iota((512, 512), 0)
    column = iota((512, 512), 1)
    spot = 256 * ((lane >> 6) & 1) + 64 * (lane >> 7) + (lane & 63)
    r.unpack[...] = to_bf16(column == spot)

    r.fbuf[me] = r.fown[pl.ds(per * me, per)]
    flat = jnp.concatenate([r.fown[b] for b in range(batch)], axis=1)
    wide = flat.astype(F32)
    square = wide * wide
    square_hi = square.astype(BF16)
    square_lo = (square - square_hi.astype(F32)).astype(BF16)
    level = iota((16, 256), 0)
    first_mask = jnp.concatenate([to_bf16(level == r.groups[b]) for b in range(batch)], axis=1)
    second_mask = jnp.concatenate([to_bf16(level == r.groups[b] + 4) for b in range(batch)], axis=1)
    sums = nt(first_mask, flat) + nt(second_mask, square_hi) + nt(second_mask, square_lo)

    def ordered_sum(ref, size):
        result = ref[0]
        for slot in range(1, size):
            result = result + ref[slot]
        return result

    class AllReduce:
        def __init__(self, number):
            self.over_outer, self.over_inner, self.over_ch = (
                getattr(r, axis + str(number), None) for axis in "abc"
            )

        def begin(self, value, masked=None):
            ref = self.over_outer
            if masked is None:
                ref[block] = value
            else:
                ref[block] = jnp.zeros(ref.shape[1:], F32)
                ref[block, :, 0:masked] = value
            self.waits = [
                post(ref.at[block], ref.at[block], ref.at[peer], dev(peer, within, me))
                for peer in outer_peers
            ]

        def middle(self):
            for wait in self.waits:
                wait()
            value = ordered_sum(self.over_outer, OUTER)
            if inner > 1:
                ref = self.over_inner
                ref[within] = value
                waits = [
                    post(ref.at[within], ref.at[within], ref.at[back], dev(block, peer, me))
                    for peer, back in inner_pairs
                ]
                for wait in waits:
                    wait()
                value = ordered_sum(ref, inner)
            self.over_ch[me] = value
            self.waits = to_channels(self.over_ch)

        def finish(self):
            for wait in self.waits:
                wait()
            return self.over_ch

        def end(self):
            return ordered_sum(self.finish(), n_ch)

    input_sums = AllReduce(1)
    input_sums.begin(sums[0:8], masked=local)

    got_exit()
    got_bypass()
    r.wz2[me, 0:hw, :] = pack_own(r.exit_v[...])
    e_row, e_col = iota((local, 128), 0), iota((local, 128), 1)
    value = r.bypass_v[...].astype(BF16)
    r.wz2[me, hw : hw + hs, :] = (
        nn(value[:hs], to_bf16(e_col == e_row)) + nn(value[hs:], to_bf16(e_col == e_row + local))
    ).astype(BF16)

    def rows_of(ref, index):
        size = ref.shape[0] // OUTER
        return ref.at[pl.ds(pl.multiple_of(size * index, 16), size)]

    def unpack_own(ref, full):
        own = rows_of(ref, block)
        if full.shape[0] == hw:
            own[0:128, :] = full[0:128, 0:256]
            own[128:256, :] = full[0:128, 256:512]
            own[256 : 256 + tail, :] = full[128:, 0:256]
            own[256 + tail :, :] = full[128:, 256:512]
        else:
            own[0:hs, :] = full[:, 0:256]
            own[hs:, :] = full[:, 256:512]

    def spread(ref):
        own = rows_of(ref, block)
        return {
            mask: post(own, own, rows_of(ref, flip(block, mask)), dev(flip(block, mask), within, me))
            for mask in (2, 4, 6, 1)
        }

    def forward(ref, waits):
        rest = [waits[1]]
        for mask in (2, 4, 6):
            waits[mask]()
            mine = rows_of(ref, flip(block, mask))
            theirs = rows_of(ref, flip(partner, mask))
            rest.append(post(mine, mine, theirs, dev(partner, within, me)))
        return rest

    def widen(buffer):
        packed = jnp.concatenate([buffer[c] for c in range(n_ch)], axis=1)
        return nn(packed, r.unpack[...]).astype(BF16)

    scope("wz")
    for wait in entry_waits:
        wait()
    unpack_own(r.w1, widen(r.wz1))
    gather1 = spread(r.w1)
    exit_waits = to_channels(r.wz2)

    scope("const")
    ident = to_bf16(iota((256, 256), 0) == iota((256, 256), 1))
    r.ident[...] = ident
    q_out, q_in = iota((256, 256), 0), iota((256, 256), 1)
    r.shift[0] = to_bf16((q_in == q_out + 1) & ((q_out & 15) < 15))
    r.shift[1] = to_bf16((q_in == q_out - 1) & ((q_out & 15) > 0))

    scope("statmid")
    input_sums.middle()
    scope("cotpost")
    got_cot()
    cot_waits = [
        post(
            r.cown.at[per * peer + im],
            r.cbuf.at[me, im],
            r.cbuf.at[peer, im],
            dev(block, within, peer),
        )
        for im in range(per)
        for peer in ch_peers
    ]

    rho, px = iota((512, 256), 0), iota((512, 256), 1)
    version, a, b_ = rho >> 8, (rho >> 7) & 1, (rho >> 6) & 1
    col = (rho & 15) + version * (1 - 2 * b_)
    target = (2 * ((rho & 63) >> 4) + a) * 32 + 2 * col + b_
    r.gridder[...] = to_bf16((px == target) & (col >= 0) & (col < 16))
    target = (
        (2 * ((lane & 127) >> 4) + (lane >> 8)) * 32 + 2 * (lane & 15) + ((lane >> 7) & 1)
    )
    r.flatter[...] = to_bf16(column == target)
    zeros = jnp.zeros((16, 256), BF16)
    for im in range(per):
        for ver in range(3):
            r.h1s[ver, im, 0:16, :] = zeros
            r.h1s[ver, im, 272:288, :] = zeros
        for ver in range(2):
            for ph in range(4):
                for ref in (r.h2s, r.dzs):
                    ref[ver, ph, im, 0:16, :] = zeros
                    ref[ver, ph, im, 272:288, :] = zeros

    def channel_major(ref, im, lanes):
        return jnp.concatenate([ref[c, im, :, lanes] for c in range(n_ch)], axis=0)

    scope("feat")
    for wait in feature_waits:
        wait()
    for im in range(per):
        r.fpm[256 * im : 256 * im + 256, :] = nt(
            ident, channel_major(r.fbuf, im, slice(0, 256))
        ).astype(BF16)

    def wide_lanes(ref):
        parts = [
            ref[c] + pltpu.roll(ref[c + 1], local, axis=1) for c in range(0, n_ch, 2)
        ]
        return jnp.concatenate(parts, axis=1)

    scope("statz")
    for wait in affine_waits:
        wait()
    affine = wide_lanes(r.aff_z)
    stats = wide_lanes(input_sums.finish())
    mean1 = stats[0:4] / count
    inv1 = lax.rsqrt(stats[4:8] / count - mean1 * mean1 + NORM_EPSILON)
    gain = affine[2 * classes : 2 * classes + 1]
    shift = affine[2 * classes + 1 : 2 * classes + 2]
    out_bias = affine[2 * classes + 2 : 2 * classes + 3]
    group, label, mean1_b, inv1_b, gamma_b, beta_b, mask_b = [], [], [], [], [], [], []
    for im in range(per):
        group.append(r.groups[per * me + im])
        label.append(r.labels[per * me + im])
        mean1_b.append(pick_row(mean1, group[im]))
        inv1_b.append(pick_row(inv1, group[im]))
        gamma_b.append(pick_row(affine, label[im]))
        beta_b.append(pick_row(affine, label[im] + classes))
        width = r.widths[group[im]]
        mask_b.append(
            jnp.where(iota((1, chans), 1) < width * (chans // LEVELS), 1.0, 0.0)
        )

    scope("h1")
    for im in range(per):
        normal = (r.fpm[256 * im : 256 * im + 256, :].astype(F32) - mean1_b[im]) * inv1_b[im]
        pre = gamma_b[im] * normal + beta_b[im]
        hidden = (pre * sigmoid(pre)).astype(BF16)
        r.h1s[1, im, 16:272, :] = hidden
        r.h1s[0, im, 16:272, :] = nn(r.shift[1], hidden).astype(BF16)
        r.h1s[2, im, 16:272, :] = nn(r.shift[0], hidden).astype(BF16)
        r.h1cm[:, 256 * im : 256 * im + 256] = nt(ident, hidden).astype(BF16)

    scope("w2own")
    for wait in exit_waits:
        wait()
    full = widen(r.wz2)
    unpack_own(r.w2, full[0:hw])
    unpack_own(r.ws, full[hw:])
    scope("w1wait")
    rest = forward(r.w1, gather1)
    gather2 = spread(r.w2)
    gather3 = spread(r.ws)
    for wait in rest:
        wait()

    def taps():
        return [(dy, dx) for dy in range(3) for dx in range(3)]

    def stack(pieces):
        return jnp.concatenate(pieces, axis=0)

    def conv1(phase, carry):
        a, c = lax.div(phase, 2), lax.rem(phase, 2)
        parts = []
        for dy, dx in taps():
            first = pl.multiple_of(16 * lax.div(a + dy + 1, 2), 16)
            ver = lax.div(c + dx + 1, 2)
            parts.append(
                stack([r.h1s[ver, im, pl.ds(first, 256), :] for im in range(per)])
            )
        y = nn(jnp.concatenate(parts, axis=1), r.w1[...])
        r.y1[phase] = y
        out = []
        for im in range(per):
            piece = y[256 * im : 256 * im + 256]
            out.append(carry[2 * im] + colsum(piece))
            out.append(carry[2 * im + 1] + colsum(piece * piece))
        return tuple(out)

    nought = jnp.zeros((1, chans), F32)
    scope("conv1")
    mid = lax.fori_loop(0, 4, conv1, (nought,) * (2 * per))
    scope("s2")
    payload = jnp.zeros((8, chans), F32)
    for im in range(per):
        payload = payload + place_row(mid[2 * im], group[im], 8)
        payload = payload + place_row(mid[2 * im + 1], group[im] + 4, 8)
    mid_sums = AllReduce(2)
    mid_sums.begin(payload)

    def turn(src, dst):
        def one(tap, carry):
            first = pl.multiple_of(256 * tap, 256)
            dst[pl.ds(first, 256), :] = nt(r.ident[...], src[pl.ds(first, 256), :]).astype(BF16)
            return carry

        lax.fori_loop(0, 9, one, 0)

    scope("w1t")
    turn(r.w1, r.w1t)
    scope("w2fwd")
    rest = forward(r.w2, gather2) + forward(r.ws, gather3)
    scope("s2mid")
    mid_sums.middle()

    scope("cotwait")
    r.cbuf[me] = r.cown[pl.ds(per * me, per)]
    for wait in cot_waits:
        wait()
    scope("dz")
    for im in range(per):
        for n in range(4):
            piece = channel_major(r.cbuf, im, slice(256 * n, 256 * n + 256))
            grid = nt(r.gridder[...], piece).astype(BF16)
            for ver in range(2):
                for ph in range(4):
                    at = 256 * ver + 64 * ph
                    r.dzs[ver, ph, im, 16 + 64 * n : 80 + 64 * n, :] = grid[at : at + 64]

    coarse = jnp.zeros((256 * per, chans), F32)
    for ph in range(4):
        coarse = coarse + stack([r.dzs[0, ph, im, 16:272, :] for im in range(per)]).astype(F32)
    bias_sum = colsum(coarse)
    r.dzc[...] = coarse.astype(BF16)

    def tap_slice(ref, a, c, dy, dx, im):
        row, colm = a + dy + 1, c + dx + 1
        first = pl.multiple_of(16 * lax.div(row, 2), 16)
        ph = 2 * lax.rem(row, 2) + lax.rem(colm, 2)
        side_step = lax.div(colm, 2) - 1
        return ref[side_step * side_step, ph, im, pl.ds(first, 256), :]

    scope("w2wait")
    for wait in rest:
        wait()
    scope("w2t")
    turn(r.w2, r.w2t)

    def back2(phase, carry):
        a, c = lax.div(phase, 2), lax.rem(phase, 2)
        parts = [
            stack([tap_slice(r.dzs, a, c, 2 - dy, 2 - dx, im) for im in range(per)])
            for dy, dx in taps()
        ]
        r.act[phase] = nn(jnp.concatenate(parts, axis=1), r.w2t[...])
        return carry

    scope("dh2")
    lax.fori_loop(0, 4, back2, 0)

    scope("s2end")
    stats = mid_sums.end()
    mean2 = stats[0:4] / (4.0 * count)
    inv2 = lax.rsqrt(stats[4:8] / (4.0 * count) - mean2 * mean2 + NORM_EPSILON)
    mean2_b = [pick_row(mean2, group[im]) for im in range(per)]
    inv2_b = [pick_row(inv2, group[im]) for im in range(per)]

    def hidden2(phase, carry):
        c = lax.rem(phase, 2)
        out = []
        for im in range(per):
            span = slice(256 * im, 256 * im + 256)
            normal = (r.y1[phase, span, :] - mean2_b[im]) * inv2_b[im]
            r.y1[phase, span, :] = normal
            pre = gain * normal + shift
            sig = sigmoid(pre)
            hidden = (pre * sig * mask_b[im]).astype(BF16)
            act = r.act[phase, span, :] * (sig * (1.0 + pre * (1.0 - sig)) * mask_b[im])
            r.act[phase, span, :] = act
            out.append(carry[2 * im] + colsum(act))
            out.append(carry[2 * im + 1] + colsum(act * normal))
            r.h2s[0, phase, im, 16:272, :] = hidden
            r.h2s[1, phase, im, 16:272, :] = nn(r.shift[c], hidden).astype(BF16)
            lanes = pl.ds(pl.multiple_of(512 * phase + 256 * im, 256), 256)
            r.h2cm[:, lanes] = nt(r.ident[...], hidden).astype(BF16)
        return tuple(out)

    scope("h2")
    mid = lax.fori_loop(0, 4, hidden2, (nought,) * (2 * per))
    scope("s3")
    payload = place_row(bias_sum, 8, 16)
    for im in range(per):
        payload = payload + place_row(mid[2 * im], group[im], 16)
        payload = payload + place_row(mid[2 * im + 1], group[im] + 4, 16)
    back_sums = AllReduce(3)
    back_sums.begin(payload)

    r.short[...] = nn(r.fpm[...], r.ws[...]) + out_bias
    def conv2(phase, carry):
        a, c = lax.div(phase, 2), lax.rem(phase, 2)
        parts = [
            stack([tap_slice(r.h2s, a, c, dy, dx, im) for im in range(per)]) for dy, dx in taps()
        ]
        y = (nn(jnp.concatenate(parts, axis=1), r.w2[...]) + r.short[...]).astype(BF16)
        lanes = pl.ds(pl.multiple_of(256 * phase, 256), 256)
        for im in range(per):
            r.rc[im, :, lanes] = nt(r.ident[...], y[256 * im : 256 * im + 256]).astype(BF16)
        return carry

    scope("conv2")
    lax.fori_loop(0, 4, conv2, 0)
    scope("order")
    for im in range(per):
        for half in range(2):
            piece = jnp.concatenate(
                [r.rc[im, :, 256 * ph + 128 * half : 256 * ph + 128 * half + 128] for ph in range(4)],
                axis=1,
            )
            r.ocm[im, :, 512 * half : 512 * half + 512] = nn(piece, r.flatter[...]).astype(BF16)

    def own_channels(ref, index, im):
        return ref.at[im, pl.ds(pl.multiple_of(local * index, local), local), :]

    def give_back(ref, out):
        waits = [here(own_channels(ref, me, im), out.at[per * me + im]) for im in range(per)]
        return waits + [
            post(
                own_channels(ref, peer, im),
                out.at[per * me + im],
                out.at[per * peer + im],
                dev(block, within, peer),
            )
            for im in range(per)
            for peer in ch_peers
        ]

    scope("outpost")
    out_waits = give_back(r.ocm, r.out)

    def grad2(tap, carry):
        dy, dx = lax.div(tap, 3), lax.rem(tap, 3)
        pieces = []
        for ph in range(4):
            a, c = ph // 2, ph % 2
            for im in range(per):
                pieces.append(tap_slice(r.dzs, a, c, 2 - dy, 2 - dx, im))
        first = pl.multiple_of(256 * tap, 256)
        r.dw2[pl.ds(first, 256), :] = nn(r.h2cm[...], stack(pieces))
        return carry

    scope("s3mid")
    back_sums.middle()
    scope("dw2")
    lax.fori_loop(0, 9, grad2, 0)
    scope("dws")
    for im in range(per):
        piece = channel_major(r.fbuf, im, slice(0, 256))
        grad = nn(piece, r.dzc[256 * im : 256 * im + 256, :])
        if im == 0:
            r.dws[...] = grad
        else:
            r.dws[...] = r.dws[...] + grad

    class GradSum:
        def __init__(self, number, fetch):
            self.fetch = fetch
            for part in PARTS:
                setattr(self, part, getattr(r, part + str(number)))

        def begin(self):
            self.waits = []
            for u in range(4):
                self.s1[u] = self.fetch(2 * u + 1 - core).astype(BF16)
                self.waits.append(
                    post(self.s1.at[u], self.r1.at[u], self.r1.at[u], dev(partner, within, me))
                )

        def settle(self):
            for wait in self.waits:
                wait()

        def across(self, send, got, masks):
            parts = [(h, v) for v in range(2) for h in range(2)] if len(send.shape) == 4 else [(0,), (1,)]
            self.waits = [
                post(send.at[p], got.at[p], got.at[p], dev(flip(block, masks[p[0]]), within, me))
                for p in parts
            ]

        def first(self):
            for u in range(4):
                self.waits[u]()
                self.acc[u] = self.fetch(2 * u + core) + self.r1[u].astype(F32)
            for v in range(2):
                self.s2[0, v] = self.acc[2 * v + 1 - bit_x, :, 0:128].astype(BF16)
                self.s2[1, v] = self.acc[2 * (1 - bit_y) + v, :, 128:256].astype(BF16)
            self.across(self.s2, self.r2, (2, 4))

        def second(self):
            self.settle()
            low = self.acc[2 * (1 - bit_y) + bit_x, :, 0:128] + self.r2[0, 1 - bit_y].astype(F32)
            high = self.acc[2 * bit_y + 1 - bit_x, :, 128:256] + self.r2[1, 1 - bit_x].astype(F32)
            self.s3[0] = low.astype(BF16)
            self.s3[1] = high.astype(BF16)
            self.across(self.s3, self.r3, (4, 2))

        def third(self):
            self.settle()
            low = self.acc[plane, :, 0:128] + self.r2[0, bit_y].astype(F32)
            high = self.acc[plane, :, 128:256] + self.r2[1, bit_x].astype(F32)
            low, high = low + self.r3[0].astype(F32), high + self.r3[1].astype(F32)
            value = jnp.concatenate([low, high], axis=1).astype(BF16)
            left = [value[0:128], value[256 : 256 + tail]]
            right = [value[128:256], value[256 + tail : rows]]
            if value.shape[0] > rows:
                left.append(value[rows : rows + hs])
                right.append(value[rows + hs :])
            pair = jnp.concatenate([stack(left), stack(right)], axis=1)
            packed = nt(pair, r.unpack[...]).astype(BF16)
            for c in range(n_ch):
                self.s4[c] = packed[:, 128 * c : 128 * c + 128]
            self.r4[me] = self.s4[me]
            self.waits = [
                post(self.s4.at[peer], self.r4.at[me], self.r4.at[peer], dev(block, within, peer))
                for peer in ch_peers
            ]

        def end(self, out, out_small=None):
            self.settle()
            done = self.r4[0].astype(F32)
            for c in range(1, n_ch):
                done = done + self.r4[c].astype(F32)
            turned = done[0:128].T
            out[:, 0:128] = turned[0:local]
            out[:, 128:256] = turned[local:]
            gap = jnp.zeros((128 - tail, 128), F32)
            turned = stack([done[128 : 128 + tail], gap]).T
            ends = turned[0:local] + pltpu.roll(turned[local:], tail, axis=1)
            out[:, 256:rows] = ends[:, 0 : rows - 256]
            if out_small is not None:
                last = done[hw:]
                out_small[0:hs, :] = last[:, 0:local]
                out_small[hs:, :] = pltpu.roll(last, local, axis=1)[:, 0:local]

    def block_rows(ref, size, index):
        return ref[pl.ds(pl.multiple_of(size * index, 8), size), :]

    second = GradSum(2, lambda k: stack([block_rows(r.dw2, rows, k), block_rows(r.dws, small, k)]))
    entry = GradSum(1, lambda k: block_rows(r.dw1, rows, k))
    scope("g2a")
    second.begin()
    r.dshort[...] = nt(r.dzc[...], r.ws[...])

    scope("s3end")
    stats = back_sums.end()
    affine_grad2 = stats
    p1_b = [pick_row(stats[0:4], group[im]) / (4.0 * count) for im in range(per)]
    p2_b = [pick_row(stats[4:8], group[im]) / (4.0 * count) for im in range(per)]

    scope("dy1")
    for im in range(per):
        span = slice(256 * im, 256 * im + 256)
        scale = gain * inv2_b[im]
        combos = []
        for a in range(2):
            grads = []
            for c in range(2):
                ph = 2 * a + c
                d = scale * (r.act[ph, span, :] - (p1_b[im] + r.y1[ph, span, :] * p2_b[im]))
                grads.append(d.astype(BF16))
            right = nn(r.shift[0], grads[0])
            left = nn(r.shift[1], grads[1])
            even, odd = grads[0].astype(F32), grads[1].astype(F32)
            combos.append((odd + right, even + odd, left + even))
        gap = jnp.zeros((16, chans), F32)
        for dx in range(3):
            upper, lower = combos[0][dx], combos[1][dx]
            r.field[dx, im] = (lower + stack([upper[16:], gap])).astype(BF16)
            r.field[3 + dx, im] = (upper + lower).astype(BF16)
            r.field[6 + dx, im] = (stack([gap, lower[:-16]]) + upper).astype(BF16)

    def grad1(tap, carry):
        first = pl.multiple_of(256 * tap, 256)
        r.dw1[pl.ds(first, 256), :] = nn(
            r.h1cm[...], stack([r.field[tap, im] for im in range(per)])
        )
        return carry

    scope("dw1")
    lax.fori_loop(0, 9, grad1, 0)
    scope("g1a")
    entry.begin()
    scope("g2b")
    second.first()

    scope("dh1")
    parts = [stack([r.field[tap, im] for im in range(per)]) for tap in range(9)]
    dh1 = nn(jnp.concatenate(parts, axis=1), r.w1t[...])
    payload = jnp.zeros((32, chans), F32)
    for im in range(per):
        span = slice(256 * im, 256 * im + 256)
        normal = (r.fpm[span, :].astype(F32) - mean1_b[im]) * inv1_b[im]
        pre = gamma_b[im] * normal + beta_b[im]
        sig = sigmoid(pre)
        act = dh1[span] * (sig * (1.0 + pre * (1.0 - sig)))
        r.act1[span, :] = act
        q1, q2 = colsum(act), colsum(act * normal)
        payload = payload + place_row(q2, label[im], 32)
        payload = payload + place_row(q1, label[im] + classes, 32)
        payload = payload + place_row(gamma_b[im] * q1, group[im] + 24, 32)
        payload = payload + place_row(gamma_b[im] * q2, group[im] + 28, 32)
    scope("s4")
    last_sums = AllReduce(4)
    last_sums.begin(payload)
    scope("g2c")
    second.second()
    scope("g1b")
    entry.first()
    scope("s4mid")
    last_sums.middle()
    scope("g2d")
    second.third()
    scope("g1c")
    entry.second()

    scope("s4end")
    stats = last_sums.end()
    scope("dx")
    for im in range(per):
        span = slice(256 * im, 256 * im + 256)
        normal = (r.fpm[span, :].astype(F32) - mean1_b[im]) * inv1_b[im]
        r1 = pick_row(stats[24:28], group[im]) / count
        r2 = pick_row(stats[28:32], group[im]) / count
        grad = inv1_b[im] * (gamma_b[im] * r.act1[span, :] - (r1 + normal * r2))
        grad = (grad + r.dshort[span, :]).astype(BF16)
        r.dcm[im] = nt(r.ident[...], grad).astype(BF16)
    out_waits += give_back(r.dcm, r.dx)
    scope("g1d")
    entry.third()
    scope("g2end")
    second.end(r.grad2, r.grad3)

    scope("affine")
    table = jnp.zeros((24, chans), F32)
    table = table + jnp.where(iota((24, chans), 0) < 2 * classes, stats[0:24], 0.0)
    table = table + place_row(colsum(affine_grad2[4:8]), 2 * classes, 24)
    table = table + place_row(colsum(affine_grad2[0:4]), 2 * classes + 1, 24)
    table = table + place_row(affine_grad2[8:9], 2 * classes + 2, 24)
    mine = jnp.zeros((24, 128), F32)
    for c in range(n_ch):
        piece = table[:, 128 * (c // 2) : 128 * (c // 2) + 128]
        if c % 2:
            piece = pltpu.roll(piece, local, axis=1)
        mine = mine + jnp.where(me == c, piece, 0.0)
    r.affine_grad[...] = mine

    scope("norms")
    if inner == 1:
        row = iota((8, 128), 0)

        def norm_rows(index, weight, grad, v):
            for wait in held[index]:
                wait()
            master = weight[...]
            _, _, direction = adam_update(
                grad[...], getattr(r, v + "m")[...], getattr(r, v + "q")[...]
            )
            update = direction + WEIGHT_DECAY * master
            rows_w = jnp.where(row == index, total(master * master), 0.0)
            return rows_w + jnp.where(row == index + 3, total(update * update), 0.0)

        norms = norm_rows(1, r.exit_v, r.grad2, "v2") + norm_rows(2, r.bypass_v, r.grad3, "vs")
        entry.end(r.grad1)
        norms = norms + norm_rows(0, r.entry_v, r.grad1, "v1")
        norm_sums = AllReduce(5)
        norm_sums.begin(norms)
        norm_sums.middle()
        r.norms[...] = norm_sums.end()
    else:
        entry.end(r.grad1)
        r.norms[...] = jnp.zeros((8, 128), F32)

    scope("ends")
    for wait in out_waits + pending:
        wait()
    scope(None)
    cfg.used.append((slots.remote, slots.local))


def final_kernel(cfg, *refs):
    r = SimpleNamespace(**dict(zip(cfg.names, refs)))
    classes = cfg.classes
    local = cfg.local
    r.block_output[...] = r.out[...]
    r.input_gradient[...] = r.dx[...].astype(F32)
    norms = jnp.sqrt(r.norms[...])
    weight_norm, update_norm = norms[0:3, 0:1], norms[3:6, 0:1]
    ratio = weight_norm / update_norm
    at = iota((3, 3), 1)
    r.trust_norms[...] = jnp.where(
        at == 0, weight_norm, jnp.where(at == 1, update_norm, ratio)
    )
    sets = (
        (r.entry, r.entry_m, r.entry_q, r.entry_g, r.entry_1, r.entry_2, r.entry_w),
        (r.exit, r.exit_m, r.exit_q, r.exit_g, r.exit_1, r.exit_2, r.exit_w),
        (r.bypass, r.bypass_m, r.bypass_q, r.bypass_g, r.bypass_1, r.bypass_2, r.bypass_w),
    )
    for index, (weight, m, q, g, first, second, result) in enumerate(sets):
        master = weight[...]
        moment, square, direction = adam_update(g[...], m[...], q[...])
        update = direction + WEIGHT_DECAY * master
        first[...] = moment
        second[...] = square
        result[...] = master - MATRIX_RATE * ratio[index : index + 1] * update
    grad = r.affine_grad[0 : 2 * classes + 3, 0:local]
    moment, square, direction = adam_update(grad, r.affine_m[...], r.affine_q[...])
    r.affine_1[...] = moment
    r.affine_2[...] = square
    r.affine_w[...] = r.affine[...] - AFFINE_RATE * direction


def per_device(
    features,
    labels,
    groups,
    widths,
    entry_conv,
    entry_moment,
    entry_square,
    exit_conv,
    exit_moment,
    exit_square,
    bypass_conv,
    bypass_moment,
    bypass_square,
    norm_affine,
    norm_moment,
    norm_square,
    cotangent,
):
    n_img, n_ch = lax.axis_size("img"), lax.axis_size("ch")
    batch, local, pixels = features.shape
    chans = local * n_ch
    side = math.isqrt(pixels)
    inner = n_img // OUTER
    classes = (norm_affine.shape[0] - 3) // 2
    per = batch // n_ch
    assert (side, chans, n_ch, local, batch % n_ch) == (16, 256, 4, 64, 0)
    rows, small = entry_conv.shape[0] * inner, bypass_conv.shape[0] * inner
    masters = (entry_conv, exit_conv, bypass_conv)
    if inner == 1:
        blocks = masters
    else:
        sets = [[o * inner + i for i in range(inner)] for o in range(OUTER)]
        blocks = tuple(
            lax.all_gather(w.astype(BF16), "img", axis=0, tiled=True, axis_index_groups=sets)
            for w in masters
        )

    vmem = pl.BlockSpec(memory_space=pltpu.VMEM)
    smem = pl.BlockSpec(memory_space=pltpu.SMEM)
    anywhere = pl.BlockSpec(memory_space=pl.ANY)
    states = dict(
        entry_m=entry_moment.T,
        entry_q=entry_square.T,
        exit_m=exit_moment.T,
        exit_q=exit_square.T,
        bypass_m=bypass_moment,
        bypass_q=bypass_square,
    )
    inputs = dict(
        labels=(labels, smem),
        groups=(groups, smem),
        widths=(widths, smem),
        features=(features, anywhere),
        cotangent=(cotangent, anywhere),
        entry=(blocks[0].T, anywhere),
        exit=(blocks[1].T, anywhere),
        bypass=(blocks[2], anywhere),
        affine=(norm_affine, anywhere),
    )
    if inner == 1:
        inputs.update({name: (value, anywhere) for name, value in states.items()})
    sds = jax.ShapeDtypeStruct
    outputs = dict(
        out=(sds(cotangent.shape, BF16), vmem),
        dx=(sds(features.shape, BF16), vmem),
        grad1=(sds((local, rows), F32), vmem),
        grad2=(sds((local, rows), F32), vmem),
        grad3=(sds((small, local), F32), vmem),
        affine_grad=(sds((24, 128), F32), vmem),
        norms=(sds((8, 128), F32), vmem),
    )
    pix = pixels * per
    taps9 = 9 * chans
    held = lambda shape, dtype=BF16: pltpu.VMEM(shape, dtype)
    scratch = dict(
        fown=held((batch, local, pixels)),
        cown=held((batch, local, 4 * pixels)),
        fbuf=held((n_ch, per, local, pixels)),
        cbuf=held((n_ch, per, local, 4 * pixels)),
        entry_v=held((local, rows), blocks[0].dtype),
        exit_v=held((local, rows), blocks[1].dtype),
        bypass_v=held((small, local), blocks[2].dtype),
        affine_v=held(norm_affine.shape, F32),
        padded=held((3 * local, 384)),
        wz1=held((n_ch, rows // 2, 128)),
        wz2=held((n_ch, (rows + small) // 2, 128)),
        aff_z=held((n_ch, 24, 128), F32),
        w1=held((taps9, chans)),
        w2=held((taps9, chans)),
        ws=held((chans, chans)),
        w1t=held((taps9, chans)),
        w2t=held((taps9, chans)),
        unpack=held((512, 512)),
        ident=held((256, 256)),
        shift=held((2, 256, 256)),
        gridder=held((512, 256)),
        flatter=held((512, 512)),
        fpm=held((pix, chans)),
        h1s=held((3, per, pixels + 32, chans)),
        h1cm=held((chans, pix)),
        y1=held((4, pix, chans), F32),
        act=held((4, pix, chans), F32),
        h2s=held((2, 4, per, pixels + 32, chans)),
        dzs=held((2, 4, per, pixels + 32, chans)),
        h2cm=held((chans, 4 * pix)),
        short=held((pix, chans), F32),
        dshort=held((pix, chans), F32),
        dzc=held((pix, chans)),
        act1=held((pix, chans), F32),
        rc=held((per, chans, 4 * pixels)),
        ocm=held((per, chans, 4 * pixels)),
        dcm=held((per, chans, pixels)),
        field=held((9, per, pixels, chans)),
        dw1=held((taps9, chans), F32),
        dw2=held((taps9, chans), F32),
        dws=held((chans, chans), F32),
    )
    for number, size in ((1, rows), (2, rows + small)):
        shapes = ((4, size, chans),) * 2 + ((2, 2, size, 128),) * 2 + ((2, size, 128),) * 2
        shapes += ((n_ch, size // 2, 128),) * 2
        for part, shape in zip(PARTS, shapes):
            scratch[part + str(number)] = held(shape)
        scratch[PARTS[-1] + str(number)] = held((4, size, chans), F32)
    exchanges = [(8, 128), (8, chans), (16, chans), (32, chans)]
    if inner == 1:
        exchanges.append((8, 128))
        for v, shape in (("v1", (local, rows)), ("v2", (local, rows)), ("vs", (small, local))):
            scratch[v + "m"] = held(shape, F32)
            scratch[v + "q"] = held(shape, F32)
    for number, shape in enumerate(exchanges, 1):
        for axis, size in zip("abc", (OUTER, inner, n_ch)):
            if size > 1:
                scratch[axis + str(number)] = held((size,) + shape, F32)
    remote_count = 4 * 3 + 3 * 3 * per + 3 * 7 + 2 * 13 + len(exchanges) * (7 + 3 + inner - 1)
    scratch.update(
        send=pltpu.SemaphoreType.DMA((remote_count,)),
        recv=pltpu.SemaphoreType.DMA((remote_count,)),
        lsem=pltpu.SemaphoreType.DMA((20,)),
    )
    cfg = SimpleNamespace(
        names=[*inputs, *outputs, *scratch],
        inner=inner,
        n_ch=n_ch,
        batch=batch,
        local=local,
        classes=classes,
        count=float(batch * n_img // widths.shape[0] * pixels),
        rows=rows,
        small=small,
        used=[],
    )
    out, dx, grad1, grad2, grad3, affine_grad, norms = pl.pallas_call(
        functools.partial(main_kernel, cfg),
        out_shape=[s for s, _ in outputs.values()],
        in_specs=[s for _, s in inputs.values()],
        out_specs=[s for _, s in outputs.values()],
        scratch_shapes=list(scratch.values()),
        compiler_params=pltpu.CompilerParams(
            collective_id=0, has_side_effects=True, vmem_limit_bytes=VMEM_LIMIT
        ),
        name="block_step",
    )(*[v for v, _ in inputs.values()])
    assert max(n for n, _ in cfg.used) <= remote_count and max(n for _, n in cfg.used) <= 20

    grads = [grad1, grad2, grad3]
    if inner > 1:
        grads = [
            lax.psum_scatter(g, "img", scatter_dimension=0, axis_index_groups=sets, tiled=True)
            for g in (grad1.T, grad2.T, grad3)
        ]
        updates = []
        for w, g, m, s in zip(
            masters,
            grads,
            (entry_moment, exit_moment, bypass_moment),
            (entry_square, exit_square, bypass_square),
        ):
            updates.append(adam_update(g, m, s)[2] + WEIGHT_DECAY * w)
        sums = lax.psum(
            jnp.stack([jnp.sum(w * w) for w in masters] + [jnp.sum(u * u) for u in updates]),
            ("img", "ch"),
        )
        norms = jnp.broadcast_to(jnp.pad(sums, (0, 2))[:, None], (8, 128))
        grads = [grads[0].T, grads[1].T, grads[2]]

    args = dict(
        out=out,
        dx=dx,
        norms=norms,
        affine_grad=affine_grad,
        entry_g=grads[0],
        exit_g=grads[1],
        bypass_g=grads[2],
        entry=entry_conv.T,
        exit=exit_conv.T,
        bypass=bypass_conv,
        **states,
        affine=norm_affine,
        affine_m=norm_moment,
        affine_q=norm_square,
    )
    tall = sds(entry_conv.shape[::-1], F32)
    short, wide = (sds(w.shape, F32) for w in (bypass_conv, norm_affine))
    results = dict(
        block_output=sds(cotangent.shape, BF16),
        input_gradient=sds(features.shape, F32),
        entry_1=tall,
        entry_2=tall,
        entry_w=tall,
        exit_1=tall,
        exit_2=tall,
        exit_w=tall,
        bypass_1=short,
        bypass_2=short,
        bypass_w=short,
        affine_1=wide,
        affine_2=wide,
        affine_w=wide,
        trust_norms=sds((3, 3), F32),
    )
    end_cfg = SimpleNamespace(names=[*args, *results], classes=classes, local=local)
    final = pl.pallas_call(
        functools.partial(final_kernel, end_cfg),
        out_shape=list(results.values()),
        in_specs=[vmem] * len(args),
        out_specs=[vmem] * len(results),
        compiler_params=pltpu.CompilerParams(vmem_limit_bytes=VMEM_LIMIT),
        name="finish",
    )(*args.values())
    return tuple(v.T if s is tall else v for v, s in zip(final, results.values()))


def solution(mesh):
    wide = P("img", "ch")
    deep = P("img", "ch", None)
    table = P(None, "ch")
    return jax.shard_map(
        per_device,
        mesh=mesh,
        in_specs=(deep, P("img"), P("img"), P()) + (wide,) * 9 + (table,) * 3 + (deep,),
        out_specs=(deep, deep) + (wide,) * 9 + (table,) * 3 + (P(),),
        check_vma=False,
    )
```

```python
import functools
import math
from types import SimpleNamespace

import jax
import jax.numpy as jnp
from jax import lax
from jax.experimental import pallas as pl
from jax.experimental.pallas import tpu as pltpu
from jax.sharding import PartitionSpec as P

LEVELS = 4
STEP = 5
NORM_EPSILON = 1e-05
ADAM_EPSILON = 1e-06
MOMENT_DECAY = 0.9
SQUARE_DECAY = 0.999
WEIGHT_DECAY = 0.01
MATRIX_RATE = 0.3
AFFINE_RATE = 0.2

OUTER = 8
VMEM_LIMIT = 56 * 1024 * 1024
BF16 = jnp.bfloat16
F32 = jnp.float32
MESH = pl.DeviceIdType.MESH
PARTS = ("s1", "r1", "s2", "r2", "s3", "r3", "s4", "r4", "acc")


def nn(left, right):
    return lax.dot_general(left, right, (((1,), (0,)), ((), ())), preferred_element_type=F32)


def nt(left, right):
    return lax.dot_general(left, right, (((1,), (1,)), ((), ())), preferred_element_type=F32)


def flip(index, mask):
    result = index
    for bit in range(3):
        if (mask >> bit) & 1:
            digit = lax.rem(lax.div(index, 1 << bit), 2)
            result = result + (1 - 2 * digit) * (1 << bit)
    return result


def sigmoid(value):
    return 0.5 * jnp.tanh(0.5 * value) + 0.5


def iota(shape, axis):
    return lax.broadcasted_iota(jnp.int32, shape, axis)


def to_bf16(condition):
    return jnp.where(condition, 1.0, 0.0).astype(BF16)


def pick_row(table, index):
    hit = iota(table.shape, 0) == index
    return jnp.sum(jnp.where(hit, table, 0.0), axis=0, keepdims=True)


def place_row(row, index, rows):
    hit = iota((rows, row.shape[1]), 0) == index
    return jnp.where(hit, row, 0.0)


def colsum(value):
    return jnp.sum(value, axis=0, keepdims=True)


def adam_update(grad, moment, square):
    moment_new = MOMENT_DECAY * moment + (1.0 - MOMENT_DECAY) * grad
    square_new = SQUARE_DECAY * square + (1.0 - SQUARE_DECAY) * grad * grad
    direction = (
        moment_new
        / (1.0 - MOMENT_DECAY**STEP)
        / (jnp.sqrt(square_new / (1.0 - SQUARE_DECAY**STEP)) + ADAM_EPSILON)
    )
    return (moment_new, square_new, direction)


def total(value):
    return jnp.sum(jnp.sum(value, axis=1, keepdims=True), axis=0, keepdims=True)


def main_kernel(cfg, *refs):
    r = SimpleNamespace(**dict(zip(cfg.names, refs)))
    inner, n_ch, batch, local = cfg.inner, cfg.n_ch, cfg.batch, cfg.local
    classes, count = cfg.classes, cfg.count
    per = batch // n_ch
    chans = local * n_ch
    rows, small = cfg.rows, cfg.small
    tail = (rows - 256) // 2
    hw, hs = rows // 2, small // 2
    slots = SimpleNamespace(remote=0, local=0)

    img = lax.axis_index("img")
    me = lax.axis_index("ch")
    block = lax.div(img, inner)
    within = lax.rem(img, inner)
    core = lax.rem(block, 2)
    plane = lax.div(block, 2)
    bit_x, bit_y = lax.rem(plane, 2), lax.div(plane, 2)
    partner = flip(block, 1)

    def dev(block_id, within_id, ch_id):
        return (block_id * inner + within_id, ch_id)

    pending = []

    def post(src, dst, landed, peer):
        slot = slots.remote
        slots.remote = slot + 1
        copy = pltpu.make_async_remote_copy(
            src_ref=src,
            dst_ref=dst,
            send_sem=r.send.at[slot],
            recv_sem=r.recv.at[slot],
            device_id=peer,
            device_id_type=MESH,
        )
        copy.start()
        pending.append(copy.wait_send)
        arrival = pltpu.make_async_remote_copy(
            src_ref=landed,
            dst_ref=landed,
            send_sem=r.send.at[slot],
            recv_sem=r.recv.at[slot],
            device_id=peer,
            device_id_type=MESH,
        )
        return arrival.wait_recv

    def here(src, dst):
        slot = slots.local
        slots.local = slot + 1
        copy = pltpu.make_async_copy(src, dst, r.lsem.at[slot])
        copy.start()
        return copy.wait

    outer_peers = [flip(block, mask) for mask in range(1, OUTER)]
    ch_peers = [flip(me, mask) for mask in range(1, n_ch)]
    inner_pairs = [
        (lax.rem(within + step, inner), lax.rem(within + inner - step, inner))
        for step in range(1, inner)
    ]
    up, down, far = (lax.rem(me + step, n_ch) for step in (1, 3, 2))
    up_peer, down_peer = dev(block, within, up), dev(block, within, down)

    class Ring:
        def __init__(self, source, target, passing):
            self.target, self.passing = target, passing
            self.waits = []
            self.early = [
                post(source(far, 0), passing.at[0], passing.at[0], up_peer),
                post(source(far, 1), passing.at[1], passing.at[1], down_peer),
            ]
            for im in range(per):
                self.waits += [
                    post(source(up, im), target(me, im), target(down, im), up_peer),
                    post(source(down, im), target(me, im), target(up, im), down_peer),
                ]

        def forward(self):
            self.early[0]()
            self.waits.append(
                post(self.passing.at[0], self.target(down, 0), self.target(far, 0), up_peer)
            )
            self.early[1]()
            self.waits.append(
                post(self.passing.at[1], self.target(up, 1), self.target(far, 1), down_peer)
            )

        def settle(self):
            for wait in self.waits:
                wait()

    barrier = pltpu.get_barrier_semaphore()
    everyone = [dev(peer, within, me) for peer in outer_peers]
    everyone += [dev(block, within, peer) for peer in ch_peers]
    everyone += [dev(block, peer, me) for peer, _ in inner_pairs]
    for peer in everyone:
        pl.semaphore_signal(barrier, inc=1, device_id=peer, device_id_type=MESH)

    got_entry = here(r.entry, r.entry_v)
    got_features = here(r.features, r.fown)
    got_exit = here(r.exit, r.exit_v)
    got_bypass = here(r.bypass, r.bypass_v)
    got_affine = here(r.affine, r.affine_v)
    got_cot = here(r.cotangent, r.cown)
    states = ((r.entry_m, r.entry_q), (r.exit_m, r.exit_q), (r.bypass_m, r.bypass_q)) if inner == 1 else ()
    held = [
        (here(m, getattr(r, v + "m")), here(q, getattr(r, v + "q")))
        for (m, q), v in zip(states, ("v1", "v2", "vs"))
    ]

    s_row, s_col = iota((hw, 384), 0), iota((hw, 384), 1)
    pick_first = to_bf16(s_col == jnp.where(s_row < 128, s_row, s_row + 128))
    pick_second = to_bf16(s_col == jnp.where(s_row < 128, s_row + 128, s_row + 128 + tail))
    r.padded[...] = jnp.zeros(r.padded.shape, BF16)

    def pack_own(value):
        r.padded[local : 2 * local, 0:rows] = value.astype(BF16)
        packed = nt(pick_first, r.padded[local : 3 * local, :])
        return (packed + nt(pick_second, r.padded[0 : 2 * local, :])).astype(BF16)

    got_entry()
    r.wz1[me] = pack_own(r.entry_v[...])
    pl.semaphore_wait(barrier, len(everyone))

    def to_channels(buffer):
        return [
            post(buffer.at[me], buffer.at[me], buffer.at[peer], dev(block, within, peer))
            for peer in ch_peers
        ]

    entry_waits = to_channels(r.wz1)
    got_features()
    features = Ring(
        lambda c, im: r.fown.at[per * c + im], lambda c, im: r.fbuf.at[c, im], r.pass_f
    )
    got_affine()
    r.aff_z[me] = jnp.zeros((24, 128), F32)
    r.aff_z[me, 0 : 2 * classes + 3, 0:local] = r.affine_v[...]
    affine_waits = to_channels(r.aff_z)

    lane = iota((512, 512), 0)
    column = iota((512, 512), 1)
    spot = 256 * ((lane >> 6) & 1) + 64 * (lane >> 7) + (lane & 63)
    r.unpack[...] = to_bf16(column == spot)

    r.fbuf[me] = r.fown[pl.ds(per * me, per)]
    flat = jnp.concatenate([r.fown[b] for b in range(batch)], axis=1)
    wide = flat.astype(F32)
    square = wide * wide
    square_hi = square.astype(BF16)
    square_lo = (square - square_hi.astype(F32)).astype(BF16)
    level = iota((16, 256), 0)
    first_mask = jnp.concatenate([to_bf16(level == r.groups[b]) for b in range(batch)], axis=1)
    second_mask = jnp.concatenate([to_bf16(level == r.groups[b] + 4) for b in range(batch)], axis=1)
    sums = nt(first_mask, flat) + nt(second_mask, square_hi) + nt(second_mask, square_lo)

    def ordered_sum(ref, size):
        result = ref[0]
        for slot in range(1, size):
            result = result + ref[slot]
        return result

    class AllReduce:
        def __init__(self, number):
            self.over_outer, self.over_inner, self.over_ch = (
                getattr(r, axis + str(number), None) for axis in "abc"
            )

        def begin(self, value, masked=None):
            ref = self.over_outer
            if masked is None:
                ref[block] = value
            else:
                ref[block] = jnp.zeros(ref.shape[1:], F32)
                ref[block, :, 0:masked] = value
            self.waits = [
                post(ref.at[block], ref.at[block], ref.at[peer], dev(peer, within, me))
                for peer in outer_peers
            ]

        def middle(self):
            for wait in self.waits:
                wait()
            value = ordered_sum(self.over_outer, OUTER)
            if inner > 1:
                ref = self.over_inner
                ref[within] = value
                waits = [
                    post(ref.at[within], ref.at[within], ref.at[back], dev(block, peer, me))
                    for peer, back in inner_pairs
                ]
                for wait in waits:
                    wait()
                value = ordered_sum(ref, inner)
            self.over_ch[me] = value
            self.waits = to_channels(self.over_ch)

        def finish(self):
            for wait in self.waits:
                wait()
            return self.over_ch

        def end(self):
            return ordered_sum(self.finish(), n_ch)

    input_sums = AllReduce(1)
    input_sums.begin(sums[0:8], masked=local)

    got_exit()
    got_bypass()
    r.wz2[me, 0:hw, :] = pack_own(r.exit_v[...])
    e_row, e_col = iota((local, 128), 0), iota((local, 128), 1)
    value = r.bypass_v[...].astype(BF16)
    r.wz2[me, hw : hw + hs, :] = (
        nn(value[:hs], to_bf16(e_col == e_row)) + nn(value[hs:], to_bf16(e_col == e_row + local))
    ).astype(BF16)

    def rows_of(ref, index):
        size = ref.shape[0] // OUTER
        return ref.at[pl.ds(pl.multiple_of(size * index, 16), size)]

    def unpack_own(ref, full):
        own = rows_of(ref, block)
        if full.shape[0] == hw:
            own[0:128, :] = full[0:128, 0:256]
            own[128:256, :] = full[0:128, 256:512]
            own[256 : 256 + tail, :] = full[128:, 0:256]
            own[256 + tail :, :] = full[128:, 256:512]
        else:
            own[0:hs, :] = full[:, 0:256]
            own[hs:, :] = full[:, 256:512]

    def spread(ref):
        own = rows_of(ref, block)
        return {
            mask: post(own, own, rows_of(ref, flip(block, mask)), dev(flip(block, mask), within, me))
            for mask in (2, 4, 6, 1)
        }

    def forward(ref, waits):
        rest = [waits[1]]
        for mask in (2, 4, 6):
            waits[mask]()
            mine = rows_of(ref, flip(block, mask))
            theirs = rows_of(ref, flip(partner, mask))
            rest.append(post(mine, mine, theirs, dev(partner, within, me)))
        return rest

    def widen(buffer):
        packed = jnp.concatenate([buffer[c] for c in range(n_ch)], axis=1)
        return nn(packed, r.unpack[...]).astype(BF16)

    for wait in entry_waits:
        wait()
    unpack_own(r.w1, widen(r.wz1))
    gather1 = spread(r.w1)
    exit_waits = to_channels(r.wz2)

    ident = to_bf16(iota((256, 256), 0) == iota((256, 256), 1))
    r.ident[...] = ident
    q_out, q_in = iota((256, 256), 0), iota((256, 256), 1)
    r.shift[0] = to_bf16((q_in == q_out + 1) & ((q_out & 15) < 15))
    r.shift[1] = to_bf16((q_in == q_out - 1) & ((q_out & 15) > 0))

    input_sums.middle()
    features.forward()
    rho, px = iota((512, 256), 0), iota((512, 256), 1)
    version, a, b_ = rho >> 8, (rho >> 7) & 1, (rho >> 6) & 1
    col = (rho & 15) + version * (1 - 2 * b_)
    target = (2 * ((rho & 63) >> 4) + a) * 32 + 2 * col + b_
    r.gridder[...] = to_bf16((px == target) & (col >= 0) & (col < 16))
    target = (
        (2 * ((lane & 127) >> 4) + (lane >> 8)) * 32 + 2 * (lane & 15) + ((lane >> 7) & 1)
    )
    r.flatter[...] = to_bf16(column == target)
    zeros = jnp.zeros((16, 256), BF16)
    for im in range(per):
        for ver in range(3):
            r.h1s[ver, im, 0:16, :] = zeros
            r.h1s[ver, im, 272:288, :] = zeros
        for ver in range(2):
            for ph in range(4):
                for ref in (r.h2s, r.dzs):
                    ref[ver, ph, im, 0:16, :] = zeros
                    ref[ver, ph, im, 272:288, :] = zeros

    def channel_major(ref, im, lanes):
        return jnp.concatenate([ref[c, im, :, lanes] for c in range(n_ch)], axis=0)

    features.settle()
    for im in range(per):
        r.fpm[256 * im : 256 * im + 256, :] = nt(
            ident, channel_major(r.fbuf, im, slice(0, 256))
        ).astype(BF16)

    def wide_lanes(ref):
        parts = [
            ref[c] + pltpu.roll(ref[c + 1], local, axis=1) for c in range(0, n_ch, 2)
        ]
        return jnp.concatenate(parts, axis=1)

    for wait in affine_waits:
        wait()
    affine = wide_lanes(r.aff_z)
    stats = wide_lanes(input_sums.finish())
    mean1 = stats[0:4] / count
    inv1 = lax.rsqrt(stats[4:8] / count - mean1 * mean1 + NORM_EPSILON)
    gain = affine[2 * classes : 2 * classes + 1]
    shift = affine[2 * classes + 1 : 2 * classes + 2]
    out_bias = affine[2 * classes + 2 : 2 * classes + 3]
    group, label, mean1_b, inv1_b, gamma_b, beta_b, mask_b = [], [], [], [], [], [], []
    for im in range(per):
        group.append(r.groups[per * me + im])
        label.append(r.labels[per * me + im])
        mean1_b.append(pick_row(mean1, group[im]))
        inv1_b.append(pick_row(inv1, group[im]))
        gamma_b.append(pick_row(affine, label[im]))
        beta_b.append(pick_row(affine, label[im] + classes))
        width = r.widths[group[im]]
        mask_b.append(
            jnp.where(iota((1, chans), 1) < width * (chans // LEVELS), 1.0, 0.0)
        )

    for im in range(per):
        normal = (r.fpm[256 * im : 256 * im + 256, :].astype(F32) - mean1_b[im]) * inv1_b[im]
        pre = gamma_b[im] * normal + beta_b[im]
        hidden = (pre * sigmoid(pre)).astype(BF16)
        r.h1s[1, im, 16:272, :] = hidden
        r.h1s[0, im, 16:272, :] = nn(r.shift[1], hidden).astype(BF16)
        r.h1s[2, im, 16:272, :] = nn(r.shift[0], hidden).astype(BF16)
        r.h1cm[:, 256 * im : 256 * im + 256] = nt(ident, hidden).astype(BF16)

    for wait in exit_waits:
        wait()
    full = widen(r.wz2)
    unpack_own(r.w2, full[0:hw])
    unpack_own(r.ws, full[hw:])
    rest = forward(r.w1, gather1)
    gather2 = spread(r.w2)
    gather3 = spread(r.ws)
    got_cot()
    cotangent = Ring(
        lambda c, im: r.cown.at[per * c + im], lambda c, im: r.cbuf.at[c, im], r.pass_c
    )

    for wait in rest:
        wait()

    def taps():
        return [(dy, dx) for dy in range(3) for dx in range(3)]

    def stack(pieces):
        return jnp.concatenate(pieces, axis=0)

    def conv1(phase, carry):
        a, c = lax.div(phase, 2), lax.rem(phase, 2)
        parts = []
        for dy, dx in taps():
            first = pl.multiple_of(16 * lax.div(a + dy + 1, 2), 16)
            ver = lax.div(c + dx + 1, 2)
            parts.append(
                stack([r.h1s[ver, im, pl.ds(first, 256), :] for im in range(per)])
            )
        y = nn(jnp.concatenate(parts, axis=1), r.w1[...])
        r.y1[phase] = y
        out = []
        for im in range(per):
            piece = y[256 * im : 256 * im + 256]
            out.append(carry[2 * im] + colsum(piece))
            out.append(carry[2 * im + 1] + colsum(piece * piece))
        return tuple(out)

    nought = jnp.zeros((1, chans), F32)
    mid = lax.fori_loop(0, 4, conv1, (nought,) * (2 * per))
    payload = jnp.zeros((8, chans), F32)
    for im in range(per):
        payload = payload + place_row(mid[2 * im], group[im], 8)
        payload = payload + place_row(mid[2 * im + 1], group[im] + 4, 8)
    mid_sums = AllReduce(2)
    mid_sums.begin(payload)

    def turn(src, dst):
        def one(tap, carry):
            first = pl.multiple_of(256 * tap, 256)
            dst[pl.ds(first, 256), :] = nt(r.ident[...], src[pl.ds(first, 256), :]).astype(BF16)
            return carry

        lax.fori_loop(0, 9, one, 0)

    cotangent.forward()
    turn(r.w1, r.w1t)
    rest = forward(r.w2, gather2) + forward(r.ws, gather3)
    mid_sums.middle()

    r.cbuf[me] = r.cown[pl.ds(per * me, per)]
    cotangent.settle()
    for im in range(per):
        for n in range(4):
            piece = channel_major(r.cbuf, im, slice(256 * n, 256 * n + 256))
            grid = nt(r.gridder[...], piece).astype(BF16)
            for ver in range(2):
                for ph in range(4):
                    at = 256 * ver + 64 * ph
                    r.dzs[ver, ph, im, 16 + 64 * n : 80 + 64 * n, :] = grid[at : at + 64]

    coarse = jnp.zeros((256 * per, chans), F32)
    for ph in range(4):
        coarse = coarse + stack([r.dzs[0, ph, im, 16:272, :] for im in range(per)]).astype(F32)
    bias_sum = colsum(coarse)
    r.dzc[...] = coarse.astype(BF16)

    def tap_slice(ref, a, c, dy, dx, im):
        row, colm = a + dy + 1, c + dx + 1
        first = pl.multiple_of(16 * lax.div(row, 2), 16)
        ph = 2 * lax.rem(row, 2) + lax.rem(colm, 2)
        side_step = lax.div(colm, 2) - 1
        return ref[side_step * side_step, ph, im, pl.ds(first, 256), :]

    for wait in rest:
        wait()
    turn(r.w2, r.w2t)

    def back2(phase, carry):
        a, c = lax.div(phase, 2), lax.rem(phase, 2)
        parts = [
            stack([tap_slice(r.dzs, a, c, 2 - dy, 2 - dx, im) for im in range(per)])
            for dy, dx in taps()
        ]
        r.act[phase] = nn(jnp.concatenate(parts, axis=1), r.w2t[...])
        return carry

    lax.fori_loop(0, 4, back2, 0)

    stats = mid_sums.end()
    mean2 = stats[0:4] / (4.0 * count)
    inv2 = lax.rsqrt(stats[4:8] / (4.0 * count) - mean2 * mean2 + NORM_EPSILON)
    mean2_b = [pick_row(mean2, group[im]) for im in range(per)]
    inv2_b = [pick_row(inv2, group[im]) for im in range(per)]

    def hidden2(phase, carry):
        c = lax.rem(phase, 2)
        out = []
        for im in range(per):
            span = slice(256 * im, 256 * im + 256)
            normal = (r.y1[phase, span, :] - mean2_b[im]) * inv2_b[im]
            r.y1[phase, span, :] = normal
            pre = gain * normal + shift
            sig = sigmoid(pre)
            hidden = (pre * sig * mask_b[im]).astype(BF16)
            act = r.act[phase, span, :] * (sig * (1.0 + pre * (1.0 - sig)) * mask_b[im])
            r.act[phase, span, :] = act
            out.append(carry[2 * im] + colsum(act))
            out.append(carry[2 * im + 1] + colsum(act * normal))
            r.h2s[0, phase, im, 16:272, :] = hidden
            r.h2s[1, phase, im, 16:272, :] = nn(r.shift[c], hidden).astype(BF16)
            lanes = pl.ds(pl.multiple_of(512 * phase + 256 * im, 256), 256)
            r.h2cm[:, lanes] = nt(r.ident[...], hidden).astype(BF16)
        return tuple(out)

    mid = lax.fori_loop(0, 4, hidden2, (nought,) * (2 * per))
    payload = place_row(bias_sum, 8, 16)
    for im in range(per):
        payload = payload + place_row(mid[2 * im], group[im], 16)
        payload = payload + place_row(mid[2 * im + 1], group[im] + 4, 16)
    back_sums = AllReduce(3)
    back_sums.begin(payload)

    r.short[...] = nn(r.fpm[...], r.ws[...]) + out_bias
    def conv2(phase, carry):
        a, c = lax.div(phase, 2), lax.rem(phase, 2)
        parts = [
            stack([tap_slice(r.h2s, a, c, dy, dx, im) for im in range(per)]) for dy, dx in taps()
        ]
        y = (nn(jnp.concatenate(parts, axis=1), r.w2[...]) + r.short[...]).astype(BF16)
        lanes = pl.ds(pl.multiple_of(256 * phase, 256), 256)
        for im in range(per):
            r.rc[im, :, lanes] = nt(r.ident[...], y[256 * im : 256 * im + 256]).astype(BF16)
        return carry

    lax.fori_loop(0, 4, conv2, 0)
    for im in range(per):
        for half in range(2):
            piece = jnp.concatenate(
                [r.rc[im, :, 256 * ph + 128 * half : 256 * ph + 128 * half + 128] for ph in range(4)],
                axis=1,
            )
            r.ocm[im, :, 512 * half : 512 * half + 512] = nn(piece, r.flatter[...]).astype(BF16)

    def own_channels(ref, index, im):
        return ref.at[im, pl.ds(pl.multiple_of(local * index, local), local), :]

    def give_back(ref, out, passing):
        for im in range(per):
            out[per * me + im] = own_channels(ref, me, im)[...]
        return Ring(
            lambda c, im: own_channels(ref, c, im), lambda c, im: out.at[per * c + im], passing
        )

    back_sums.middle()
    block_output = give_back(r.ocm, r.out, r.pass_o)

    def grad2(tap, carry):
        dy, dx = lax.div(tap, 3), lax.rem(tap, 3)
        pieces = []
        for ph in range(4):
            a, c = ph // 2, ph % 2
            for im in range(per):
                pieces.append(tap_slice(r.dzs, a, c, 2 - dy, 2 - dx, im))
        first = pl.multiple_of(256 * tap, 256)
        r.dw2[pl.ds(first, 256), :] = nn(r.h2cm[...], stack(pieces))
        return carry

    lax.fori_loop(0, 9, grad2, 0)
    for im in range(per):
        piece = channel_major(r.fbuf, im, slice(0, 256))
        grad = nn(piece, r.dzc[256 * im : 256 * im + 256, :])
        if im == 0:
            r.dws[...] = grad
        else:
            r.dws[...] = r.dws[...] + grad

    class GradSum:
        def __init__(self, number, fetch):
            self.fetch = fetch
            for part in PARTS:
                setattr(self, part, getattr(r, part + str(number)))

        def begin(self):
            self.waits = []
            for u in range(4):
                self.s1[u] = self.fetch(2 * u + 1 - core).astype(BF16)
                self.waits.append(
                    post(self.s1.at[u], self.r1.at[u], self.r1.at[u], dev(partner, within, me))
                )

        def settle(self):
            for wait in self.waits:
                wait()

        def across(self, send, got, masks):
            parts = [(h, v) for v in range(2) for h in range(2)] if len(send.shape) == 4 else [(0,), (1,)]
            self.waits = [
                post(send.at[p], got.at[p], got.at[p], dev(flip(block, masks[p[0]]), within, me))
                for p in parts
            ]

        def first(self):
            for u in range(4):
                self.waits[u]()
                self.acc[u] = self.fetch(2 * u + core) + self.r1[u].astype(F32)
            for v in range(2):
                self.s2[0, v] = self.acc[2 * v + 1 - bit_x, :, 0:128].astype(BF16)
                self.s2[1, v] = self.acc[2 * (1 - bit_y) + v, :, 128:256].astype(BF16)
            self.across(self.s2, self.r2, (2, 4))

        def second(self):
            self.settle()
            low = self.acc[2 * (1 - bit_y) + bit_x, :, 0:128] + self.r2[0, 1 - bit_y].astype(F32)
            high = self.acc[2 * bit_y + 1 - bit_x, :, 128:256] + self.r2[1, 1 - bit_x].astype(F32)
            self.s3[0] = low.astype(BF16)
            self.s3[1] = high.astype(BF16)
            self.across(self.s3, self.r3, (4, 2))

        def third(self):
            self.settle()
            low = self.acc[plane, :, 0:128] + self.r2[0, bit_y].astype(F32)
            high = self.acc[plane, :, 128:256] + self.r2[1, bit_x].astype(F32)
            low, high = low + self.r3[0].astype(F32), high + self.r3[1].astype(F32)
            value = jnp.concatenate([low, high], axis=1).astype(BF16)
            left = [value[0:128], value[256 : 256 + tail]]
            right = [value[128:256], value[256 + tail : rows]]
            if value.shape[0] > rows:
                left.append(value[rows : rows + hs])
                right.append(value[rows + hs :])
            pair = jnp.concatenate([stack(left), stack(right)], axis=1)
            packed = nt(pair, r.unpack[...]).astype(BF16)
            for c in range(n_ch):
                self.s4[c] = packed[:, 128 * c : 128 * c + 128]
            self.r4[me] = self.s4[me]
            self.waits = [
                post(self.s4.at[peer], self.r4.at[me], self.r4.at[peer], dev(block, within, peer))
                for peer in ch_peers
            ]

        def end(self, out, out_small=None):
            self.settle()
            done = self.r4[0].astype(F32)
            for c in range(1, n_ch):
                done = done + self.r4[c].astype(F32)
            turned = done[0:128].T
            out[:, 0:128] = turned[0:local]
            out[:, 128:256] = turned[local:]
            gap = jnp.zeros((128 - tail, 128), F32)
            turned = stack([done[128 : 128 + tail], gap]).T
            ends = turned[0:local] + pltpu.roll(turned[local:], tail, axis=1)
            out[:, 256:rows] = ends[:, 0 : rows - 256]
            if out_small is not None:
                last = done[hw:]
                out_small[0:hs, :] = last[:, 0:local]
                out_small[hs:, :] = pltpu.roll(last, local, axis=1)[:, 0:local]

    def block_rows(ref, size, index):
        return ref[pl.ds(pl.multiple_of(size * index, 8), size), :]

    second = GradSum(2, lambda k: stack([block_rows(r.dw2, rows, k), block_rows(r.dws, small, k)]))
    entry = GradSum(1, lambda k: block_rows(r.dw1, rows, k))
    second.begin()
    r.dshort[...] = nt(r.dzc[...], r.ws[...])

    stats = back_sums.end()
    affine_grad2 = stats
    p1_b = [pick_row(stats[0:4], group[im]) / (4.0 * count) for im in range(per)]
    p2_b = [pick_row(stats[4:8], group[im]) / (4.0 * count) for im in range(per)]

    for im in range(per):
        span = slice(256 * im, 256 * im + 256)
        scale = gain * inv2_b[im]
        combos = []
        for a in range(2):
            grads = []
            for c in range(2):
                ph = 2 * a + c
                d = scale * (r.act[ph, span, :] - (p1_b[im] + r.y1[ph, span, :] * p2_b[im]))
                grads.append(d.astype(BF16))
            right = nn(r.shift[0], grads[0])
            left = nn(r.shift[1], grads[1])
            even, odd = grads[0].astype(F32), grads[1].astype(F32)
            combos.append((odd + right, even + odd, left + even))
        gap = jnp.zeros((16, chans), F32)
        for dx in range(3):
            upper, lower = combos[0][dx], combos[1][dx]
            r.field[dx, im] = (lower + stack([upper[16:], gap])).astype(BF16)
            r.field[3 + dx, im] = (upper + lower).astype(BF16)
            r.field[6 + dx, im] = (stack([gap, lower[:-16]]) + upper).astype(BF16)

    block_output.forward()

    def grad1(tap, carry):
        first = pl.multiple_of(256 * tap, 256)
        r.dw1[pl.ds(first, 256), :] = nn(
            r.h1cm[...], stack([r.field[tap, im] for im in range(per)])
        )
        return carry

    lax.fori_loop(0, 9, grad1, 0)
    entry.begin()
    second.first()

    parts = [stack([r.field[tap, im] for im in range(per)]) for tap in range(9)]
    dh1 = nn(jnp.concatenate(parts, axis=1), r.w1t[...])
    payload = jnp.zeros((32, chans), F32)
    for im in range(per):
        span = slice(256 * im, 256 * im + 256)
        normal = (r.fpm[span, :].astype(F32) - mean1_b[im]) * inv1_b[im]
        pre = gamma_b[im] * normal + beta_b[im]
        sig = sigmoid(pre)
        act = dh1[span] * (sig * (1.0 + pre * (1.0 - sig)))
        r.act1[span, :] = act
        q1, q2 = colsum(act), colsum(act * normal)
        payload = payload + place_row(q2, label[im], 32)
        payload = payload + place_row(q1, label[im] + classes, 32)
        payload = payload + place_row(gamma_b[im] * q1, group[im] + 24, 32)
        payload = payload + place_row(gamma_b[im] * q2, group[im] + 28, 32)
    last_sums = AllReduce(4)
    last_sums.begin(payload)
    second.second()
    entry.first()
    last_sums.middle()
    second.third()
    entry.second()

    stats = last_sums.end()
    for im in range(per):
        span = slice(256 * im, 256 * im + 256)
        normal = (r.fpm[span, :].astype(F32) - mean1_b[im]) * inv1_b[im]
        r1 = pick_row(stats[24:28], group[im]) / count
        r2 = pick_row(stats[28:32], group[im]) / count
        grad = inv1_b[im] * (gamma_b[im] * r.act1[span, :] - (r1 + normal * r2))
        grad = (grad + r.dshort[span, :]).astype(BF16)
        r.dcm[im] = nt(r.ident[...], grad).astype(BF16)
    input_gradient = give_back(r.dcm, r.dx, r.pass_x)
    entry.third()
    second.end(r.grad2, r.grad3)
    input_gradient.forward()

    table = jnp.zeros((24, chans), F32)
    table = table + jnp.where(iota((24, chans), 0) < 2 * classes, stats[0:24], 0.0)
    table = table + place_row(colsum(affine_grad2[4:8]), 2 * classes, 24)
    table = table + place_row(colsum(affine_grad2[0:4]), 2 * classes + 1, 24)
    table = table + place_row(affine_grad2[8:9], 2 * classes + 2, 24)
    mine = jnp.zeros((24, 128), F32)
    for c in range(n_ch):
        piece = table[:, 128 * (c // 2) : 128 * (c // 2) + 128]
        if c % 2:
            piece = pltpu.roll(piece, local, axis=1)
        mine = mine + jnp.where(me == c, piece, 0.0)
    r.affine_grad[...] = mine

    if inner == 1:
        row = iota((8, 128), 0)

        def norm_rows(index, weight, grad, v):
            for wait in held[index]:
                wait()
            master = weight[...]
            _, _, direction = adam_update(
                grad[...], getattr(r, v + "m")[...], getattr(r, v + "q")[...]
            )
            update = direction + WEIGHT_DECAY * master
            rows_w = jnp.where(row == index, total(master * master), 0.0)
            return rows_w + jnp.where(row == index + 3, total(update * update), 0.0)

        norms = norm_rows(1, r.exit_v, r.grad2, "v2") + norm_rows(2, r.bypass_v, r.grad3, "vs")
        entry.end(r.grad1)
        norms = norms + norm_rows(0, r.entry_v, r.grad1, "v1")
        norm_sums = AllReduce(5)
        norm_sums.begin(norms)
        norm_sums.middle()
        r.norms[...] = norm_sums.end()
    else:
        entry.end(r.grad1)
        r.norms[...] = jnp.zeros((8, 128), F32)

    block_output.settle()
    input_gradient.settle()
    for wait in pending:
        wait()
    cfg.used.append((slots.remote, slots.local))


def final_kernel(cfg, *refs):
    r = SimpleNamespace(**dict(zip(cfg.names, refs)))
    classes = cfg.classes
    local = cfg.local
    r.block_output[...] = r.out[...]
    r.input_gradient[...] = r.dx[...].astype(F32)
    norms = jnp.sqrt(r.norms[...])
    weight_norm, update_norm = norms[0:3, 0:1], norms[3:6, 0:1]
    ratio = weight_norm / update_norm
    at = iota((3, 3), 1)
    r.trust_norms[...] = jnp.where(
        at == 0, weight_norm, jnp.where(at == 1, update_norm, ratio)
    )
    sets = (
        (r.entry, r.entry_m, r.entry_q, r.entry_g, r.entry_1, r.entry_2, r.entry_w),
        (r.exit, r.exit_m, r.exit_q, r.exit_g, r.exit_1, r.exit_2, r.exit_w),
        (r.bypass, r.bypass_m, r.bypass_q, r.bypass_g, r.bypass_1, r.bypass_2, r.bypass_w),
    )
    for index, (weight, m, q, g, first, second, result) in enumerate(sets):
        master = weight[...]
        moment, square, direction = adam_update(g[...], m[...], q[...])
        update = direction + WEIGHT_DECAY * master
        first[...] = moment
        second[...] = square
        result[...] = master - MATRIX_RATE * ratio[index : index + 1] * update
    grad = r.affine_grad[0 : 2 * classes + 3, 0:local]
    moment, square, direction = adam_update(grad, r.affine_m[...], r.affine_q[...])
    r.affine_1[...] = moment
    r.affine_2[...] = square
    r.affine_w[...] = r.affine[...] - AFFINE_RATE * direction


def per_device(
    features,
    labels,
    groups,
    widths,
    entry_conv,
    entry_moment,
    entry_square,
    exit_conv,
    exit_moment,
    exit_square,
    bypass_conv,
    bypass_moment,
    bypass_square,
    norm_affine,
    norm_moment,
    norm_square,
    cotangent,
):
    n_img, n_ch = lax.axis_size("img"), lax.axis_size("ch")
    batch, local, pixels = features.shape
    chans = local * n_ch
    side = math.isqrt(pixels)
    inner = n_img // OUTER
    classes = (norm_affine.shape[0] - 3) // 2
    per = batch // n_ch
    assert (side, chans, n_ch, local, batch % n_ch) == (16, 256, 4, 64, 0) and per == 2
    rows, small = entry_conv.shape[0] * inner, bypass_conv.shape[0] * inner
    masters = (entry_conv, exit_conv, bypass_conv)
    if inner == 1:
        blocks = masters
    else:
        sets = [[o * inner + i for i in range(inner)] for o in range(OUTER)]
        blocks = tuple(
            lax.all_gather(w.astype(BF16), "img", axis=0, tiled=True, axis_index_groups=sets)
            for w in masters
        )

    vmem = pl.BlockSpec(memory_space=pltpu.VMEM)
    smem = pl.BlockSpec(memory_space=pltpu.SMEM)
    anywhere = pl.BlockSpec(memory_space=pl.ANY)
    states = dict(
        entry_m=entry_moment.T,
        entry_q=entry_square.T,
        exit_m=exit_moment.T,
        exit_q=exit_square.T,
        bypass_m=bypass_moment,
        bypass_q=bypass_square,
    )
    inputs = dict(
        labels=(labels, smem),
        groups=(groups, smem),
        widths=(widths, smem),
        features=(features, anywhere),
        cotangent=(cotangent, anywhere),
        entry=(blocks[0].T, anywhere),
        exit=(blocks[1].T, anywhere),
        bypass=(blocks[2], anywhere),
        affine=(norm_affine, anywhere),
    )
    if inner == 1:
        inputs.update({name: (value, anywhere) for name, value in states.items()})
    sds = jax.ShapeDtypeStruct
    outputs = dict(
        out=(sds(cotangent.shape, BF16), vmem),
        dx=(sds(features.shape, BF16), vmem),
        grad1=(sds((local, rows), F32), vmem),
        grad2=(sds((local, rows), F32), vmem),
        grad3=(sds((small, local), F32), vmem),
        affine_grad=(sds((24, 128), F32), vmem),
        norms=(sds((8, 128), F32), vmem),
    )
    pix = pixels * per
    taps9 = 9 * chans
    held = lambda shape, dtype=BF16: pltpu.VMEM(shape, dtype)
    scratch = dict(
        fown=held((batch, local, pixels)),
        cown=held((batch, local, 4 * pixels)),
        pass_f=held((2, local, pixels)),
        pass_c=held((2, local, 4 * pixels)),
        pass_o=held((2, local, 4 * pixels)),
        pass_x=held((2, local, pixels)),
        fbuf=held((n_ch, per, local, pixels)),
        cbuf=held((n_ch, per, local, 4 * pixels)),
        entry_v=held((local, rows), blocks[0].dtype),
        exit_v=held((local, rows), blocks[1].dtype),
        bypass_v=held((small, local), blocks[2].dtype),
        affine_v=held(norm_affine.shape, F32),
        padded=held((3 * local, 384)),
        wz1=held((n_ch, rows // 2, 128)),
        wz2=held((n_ch, (rows + small) // 2, 128)),
        aff_z=held((n_ch, 24, 128), F32),
        w1=held((taps9, chans)),
        w2=held((taps9, chans)),
        ws=held((chans, chans)),
        w1t=held((taps9, chans)),
        w2t=held((taps9, chans)),
        unpack=held((512, 512)),
        ident=held((256, 256)),
        shift=held((2, 256, 256)),
        gridder=held((512, 256)),
        flatter=held((512, 512)),
        fpm=held((pix, chans)),
        h1s=held((3, per, pixels + 32, chans)),
        h1cm=held((chans, pix)),
        y1=held((4, pix, chans), F32),
        act=held((4, pix, chans), F32),
        h2s=held((2, 4, per, pixels + 32, chans)),
        dzs=held((2, 4, per, pixels + 32, chans)),
        h2cm=held((chans, 4 * pix)),
        short=held((pix, chans), F32),
        dshort=held((pix, chans), F32),
        dzc=held((pix, chans)),
        act1=held((pix, chans), F32),
        rc=held((per, chans, 4 * pixels)),
        ocm=held((per, chans, 4 * pixels)),
        dcm=held((per, chans, pixels)),
        field=held((9, per, pixels, chans)),
        dw1=held((taps9, chans), F32),
        dw2=held((taps9, chans), F32),
        dws=held((chans, chans), F32),
    )
    for number, size in ((1, rows), (2, rows + small)):
        shapes = ((4, size, chans),) * 2 + ((2, 2, size, 128),) * 2 + ((2, size, 128),) * 2
        shapes += ((n_ch, size // 2, 128),) * 2
        for part, shape in zip(PARTS, shapes):
            scratch[part + str(number)] = held(shape)
        scratch[PARTS[-1] + str(number)] = held((4, size, chans), F32)
    exchanges = [(8, 128), (8, chans), (16, chans), (32, chans)]
    if inner == 1:
        exchanges.append((8, 128))
        for v, shape in (("v1", (local, rows)), ("v2", (local, rows)), ("vs", (small, local))):
            scratch[v + "m"] = held(shape, F32)
            scratch[v + "q"] = held(shape, F32)
    for number, shape in enumerate(exchanges, 1):
        for axis, size in zip("abc", (OUTER, inner, n_ch)):
            if size > 1:
                scratch[axis + str(number)] = held((size,) + shape, F32)
    remote_count = 3 * 3 + 4 * 4 * per + 3 * 7 + 2 * 13 + len(exchanges) * (7 + 3 + inner - 1)
    scratch.update(
        send=pltpu.SemaphoreType.DMA((remote_count,)),
        recv=pltpu.SemaphoreType.DMA((remote_count,)),
        lsem=pltpu.SemaphoreType.DMA((20,)),
    )
    cfg = SimpleNamespace(
        names=[*inputs, *outputs, *scratch],
        inner=inner,
        n_ch=n_ch,
        batch=batch,
        local=local,
        classes=classes,
        count=float(batch * n_img // widths.shape[0] * pixels),
        rows=rows,
        small=small,
        used=[],
    )
    out, dx, grad1, grad2, grad3, affine_grad, norms = pl.pallas_call(
        functools.partial(main_kernel, cfg),
        out_shape=[s for s, _ in outputs.values()],
        in_specs=[s for _, s in inputs.values()],
        out_specs=[s for _, s in outputs.values()],
        scratch_shapes=list(scratch.values()),
        compiler_params=pltpu.CompilerParams(
            collective_id=0, has_side_effects=True, vmem_limit_bytes=VMEM_LIMIT
        ),
        name="block_step",
    )(*[v for v, _ in inputs.values()])
    assert max(n for n, _ in cfg.used) <= remote_count and max(n for _, n in cfg.used) <= 20

    grads = [grad1, grad2, grad3]
    if inner > 1:
        grads = [
            lax.psum_scatter(g, "img", scatter_dimension=0, axis_index_groups=sets, tiled=True)
            for g in (grad1.T, grad2.T, grad3)
        ]
        updates = []
        for w, g, m, s in zip(
            masters,
            grads,
            (entry_moment, exit_moment, bypass_moment),
            (entry_square, exit_square, bypass_square),
        ):
            updates.append(adam_update(g, m, s)[2] + WEIGHT_DECAY * w)
        sums = lax.psum(
            jnp.stack([jnp.sum(w * w) for w in masters] + [jnp.sum(u * u) for u in updates]),
            ("img", "ch"),
        )
        norms = jnp.broadcast_to(jnp.pad(sums, (0, 2))[:, None], (8, 128))
        grads = [grads[0].T, grads[1].T, grads[2]]

    args = dict(
        out=out,
        dx=dx,
        norms=norms,
        affine_grad=affine_grad,
        entry_g=grads[0],
        exit_g=grads[1],
        bypass_g=grads[2],
        entry=entry_conv.T,
        exit=exit_conv.T,
        bypass=bypass_conv,
        **states,
        affine=norm_affine,
        affine_m=norm_moment,
        affine_q=norm_square,
    )
    tall = sds(entry_conv.shape[::-1], F32)
    short, wide = (sds(w.shape, F32) for w in (bypass_conv, norm_affine))
    results = dict(
        block_output=sds(cotangent.shape, BF16),
        input_gradient=sds(features.shape, F32),
        entry_1=tall,
        entry_2=tall,
        entry_w=tall,
        exit_1=tall,
        exit_2=tall,
        exit_w=tall,
        bypass_1=short,
        bypass_2=short,
        bypass_w=short,
        affine_1=wide,
        affine_2=wide,
        affine_w=wide,
        trust_norms=sds((3, 3), F32),
    )
    end_cfg = SimpleNamespace(names=[*args, *results], classes=classes, local=local)
    final = pl.pallas_call(
        functools.partial(final_kernel, end_cfg),
        out_shape=list(results.values()),
        in_specs=[vmem] * len(args),
        out_specs=[vmem] * len(results),
        compiler_params=pltpu.CompilerParams(vmem_limit_bytes=VMEM_LIMIT),
        name="finish",
    )(*args.values())
    return tuple(v.T if s is tall else v for v, s in zip(final, results.values()))


def solution(mesh):
    wide = P("img", "ch")
    deep = P("img", "ch", None)
    table = P(None, "ch")
    return jax.shard_map(
        per_device,
        mesh=mesh,
        in_specs=(deep, P("img"), P("img"), P()) + (wide,) * 9 + (table,) * 3 + (deep,),
        out_specs=(deep, deep) + (wide,) * 9 + (table,) * 3 + (P(),),
        check_vma=False,
    )
```

```python
import functools
import math
from types import SimpleNamespace

import jax
import jax.numpy as jnp
from jax import lax
from jax.experimental import pallas as pl
from jax.experimental.pallas import tpu as pltpu
from jax.sharding import PartitionSpec as P

LEVELS = 4
STEP = 5
NORM_EPSILON = 1e-05
ADAM_EPSILON = 1e-06
MOMENT_DECAY = 0.9
SQUARE_DECAY = 0.999
WEIGHT_DECAY = 0.01
MATRIX_RATE = 0.3
AFFINE_RATE = 0.2

OUTER = 8
VMEM_LIMIT = 56 * 1024 * 1024
BF16 = jnp.bfloat16
F32 = jnp.float32
MESH = pl.DeviceIdType.MESH
PARTS = ("s1", "r1", "s2", "r2", "s3", "r3", "s4", "r4", "acc")


def nn(left, right):
    return lax.dot_general(left, right, (((1,), (0,)), ((), ())), preferred_element_type=F32)


def nt(left, right):
    return lax.dot_general(left, right, (((1,), (1,)), ((), ())), preferred_element_type=F32)


def flip(index, mask):
    result = index
    for bit in range(3):
        if (mask >> bit) & 1:
            digit = lax.rem(lax.div(index, 1 << bit), 2)
            result = result + (1 - 2 * digit) * (1 << bit)
    return result


def sigmoid(value):
    return 0.5 * jnp.tanh(0.5 * value) + 0.5


def iota(shape, axis):
    return lax.broadcasted_iota(jnp.int32, shape, axis)


def to_bf16(condition):
    return jnp.where(condition, 1.0, 0.0).astype(BF16)


def pick_row(table, index):
    hit = iota(table.shape, 0) == index
    return jnp.sum(jnp.where(hit, table, 0.0), axis=0, keepdims=True)


def place_row(row, index, rows):
    hit = iota((rows, row.shape[1]), 0) == index
    return jnp.where(hit, row, 0.0)


def colsum(value):
    return jnp.sum(value, axis=0, keepdims=True)


def adam_update(grad, moment, square):
    moment_new = MOMENT_DECAY * moment + (1.0 - MOMENT_DECAY) * grad
    square_new = SQUARE_DECAY * square + (1.0 - SQUARE_DECAY) * grad * grad
    direction = (
        moment_new
        / (1.0 - MOMENT_DECAY**STEP)
        / (jnp.sqrt(square_new / (1.0 - SQUARE_DECAY**STEP)) + ADAM_EPSILON)
    )
    return (moment_new, square_new, direction)


def total(value):
    return jnp.sum(jnp.sum(value, axis=1, keepdims=True), axis=0, keepdims=True)


def main_kernel(cfg, *refs):
    r = SimpleNamespace(**dict(zip(cfg.names, refs)))
    inner, n_ch, batch, local = cfg.inner, cfg.n_ch, cfg.batch, cfg.local
    classes, count = cfg.classes, cfg.count
    per = batch // n_ch
    chans = local * n_ch
    rows, small = cfg.rows, cfg.small
    tail = (rows - 256) // 2
    hw, hs = rows // 2, small // 2
    slots = SimpleNamespace(remote=0, local=0)

    img = lax.axis_index("img")
    me = lax.axis_index("ch")
    block = lax.div(img, inner)
    within = lax.rem(img, inner)
    core = lax.rem(block, 2)
    plane = lax.div(block, 2)
    bit_x, bit_y = lax.rem(plane, 2), lax.div(plane, 2)
    partner = flip(block, 1)

    def dev(block_id, within_id, ch_id):
        return (block_id * inner + within_id, ch_id)

    pending = []

    def post(src, dst, landed, peer):
        slot = slots.remote
        slots.remote = slot + 1
        copy = pltpu.make_async_remote_copy(
            src_ref=src,
            dst_ref=dst,
            send_sem=r.send.at[slot],
            recv_sem=r.recv.at[slot],
            device_id=peer,
            device_id_type=MESH,
        )
        copy.start()
        pending.append(copy.wait_send)
        arrival = pltpu.make_async_remote_copy(
            src_ref=landed,
            dst_ref=landed,
            send_sem=r.send.at[slot],
            recv_sem=r.recv.at[slot],
            device_id=peer,
            device_id_type=MESH,
        )
        return arrival.wait_recv

    def here(src, dst):
        slot = slots.local
        slots.local = slot + 1
        copy = pltpu.make_async_copy(src, dst, r.lsem.at[slot])
        copy.start()
        return copy.wait

    outer_peers = [flip(block, mask) for mask in range(1, OUTER)]
    ch_peers = [flip(me, mask) for mask in range(1, n_ch)]
    inner_pairs = [
        (lax.rem(within + step, inner), lax.rem(within + inner - step, inner))
        for step in range(1, inner)
    ]
    up, down, far = (lax.rem(me + step, n_ch) for step in (1, 3, 2))
    up_peer, down_peer = dev(block, within, up), dev(block, within, down)

    class Ring:
        def __init__(self, source, target, passing):
            self.target, self.passing = target, passing
            self.waits = []
            self.early = [
                post(source(far, 0), passing.at[0], passing.at[0], up_peer),
                post(source(far, 1), passing.at[1], passing.at[1], down_peer),
            ]
            for im in range(per):
                self.waits += [
                    post(source(up, im), target(me, im), target(down, im), up_peer),
                    post(source(down, im), target(me, im), target(up, im), down_peer),
                ]

        def forward(self):
            self.early[0]()
            self.waits.append(
                post(self.passing.at[0], self.target(down, 0), self.target(far, 0), up_peer)
            )
            self.early[1]()
            self.waits.append(
                post(self.passing.at[1], self.target(up, 1), self.target(far, 1), down_peer)
            )

        def settle(self):
            for wait in self.waits:
                wait()

    barrier = pltpu.get_barrier_semaphore()
    everyone = [dev(peer, within, me) for peer in outer_peers]
    everyone += [dev(block, within, peer) for peer in ch_peers]
    everyone += [dev(block, peer, me) for peer, _ in inner_pairs]
    for peer in everyone:
        pl.semaphore_signal(barrier, inc=1, device_id=peer, device_id_type=MESH)

    got_entry = here(r.entry, r.entry_v)
    got_features = here(r.features, r.fown)
    got_exit = here(r.exit, r.exit_v)
    got_bypass = here(r.bypass, r.bypass_v)
    got_affine = here(r.affine, r.affine_v)
    got_cot = here(r.cotangent, r.cown)
    states = ((r.entry_m, r.entry_q), (r.exit_m, r.exit_q), (r.bypass_m, r.bypass_q)) if inner == 1 else ()
    held = [
        (here(m, getattr(r, v + "m")), here(q, getattr(r, v + "q")))
        for (m, q), v in zip(states, ("v1", "v2", "vs"))
    ]

    s_row, s_col = iota((hw, 384), 0), iota((hw, 384), 1)
    pick_first = to_bf16(s_col == jnp.where(s_row < 128, s_row, s_row + 128))
    pick_second = to_bf16(s_col == jnp.where(s_row < 128, s_row + 128, s_row + 128 + tail))
    r.padded[...] = jnp.zeros(r.padded.shape, BF16)

    def pack_own(value):
        r.padded[local : 2 * local, 0:rows] = value.astype(BF16)
        packed = nt(pick_first, r.padded[local : 3 * local, :])
        return (packed + nt(pick_second, r.padded[0 : 2 * local, :])).astype(BF16)

    got_entry()
    r.wz1[me] = pack_own(r.entry_v[...])
    pl.semaphore_wait(barrier, len(everyone))

    def to_channels(buffer):
        return [
            post(buffer.at[me], buffer.at[me], buffer.at[peer], dev(block, within, peer))
            for peer in ch_peers
        ]

    entry_waits = to_channels(r.wz1)
    got_features()
    features = Ring(
        lambda c, im: r.fown.at[per * c + im], lambda c, im: r.fbuf.at[c, im], r.pass_f
    )
    got_affine()
    r.aff_z[me] = jnp.zeros((24, 128), F32)
    r.aff_z[me, 0 : 2 * classes + 3, 0:local] = r.affine_v[...]
    affine_waits = to_channels(r.aff_z)

    lane = iota((512, 512), 0)
    column = iota((512, 512), 1)
    spot = 256 * ((lane >> 6) & 1) + 64 * (lane >> 7) + (lane & 63)
    r.unpack[...] = to_bf16(column == spot)

    r.fbuf[me] = r.fown[pl.ds(per * me, per)]
    flat = jnp.concatenate([r.fown[b] for b in range(batch)], axis=1)
    wide = flat.astype(F32)
    square = wide * wide
    square_hi = square.astype(BF16)
    square_lo = (square - square_hi.astype(F32)).astype(BF16)
    level = iota((16, 256), 0)
    first_mask = jnp.concatenate([to_bf16(level == r.groups[b]) for b in range(batch)], axis=1)
    second_mask = jnp.concatenate([to_bf16(level == r.groups[b] + 4) for b in range(batch)], axis=1)
    sums = nt(first_mask, flat) + nt(second_mask, square_hi) + nt(second_mask, square_lo)

    def ordered_sum(ref, size):
        result = ref[0]
        for slot in range(1, size):
            result = result + ref[slot]
        return result

    class AllReduce:
        def __init__(self, number):
            self.over_outer, self.over_inner, self.over_ch = (
                getattr(r, axis + str(number), None) for axis in "abc"
            )

        def begin(self, value, masked=None):
            ref = self.over_outer
            if masked is None:
                ref[block] = value
            else:
                ref[block] = jnp.zeros(ref.shape[1:], F32)
                ref[block, :, 0:masked] = value
            self.waits = [
                post(ref.at[block], ref.at[block], ref.at[peer], dev(peer, within, me))
                for peer in outer_peers
            ]

        def middle(self):
            for wait in self.waits:
                wait()
            value = ordered_sum(self.over_outer, OUTER)
            if inner > 1:
                ref = self.over_inner
                ref[within] = value
                waits = [
                    post(ref.at[within], ref.at[within], ref.at[back], dev(block, peer, me))
                    for peer, back in inner_pairs
                ]
                for wait in waits:
                    wait()
                value = ordered_sum(ref, inner)
            self.over_ch[me] = value
            self.waits = to_channels(self.over_ch)

        def finish(self):
            for wait in self.waits:
                wait()
            return self.over_ch

        def end(self):
            return ordered_sum(self.finish(), n_ch)

    input_sums = AllReduce(1)
    input_sums.begin(sums[0:8], masked=local)

    got_exit()
    got_bypass()
    r.wz2[me, 0:hw, :] = pack_own(r.exit_v[...])
    e_row, e_col = iota((local, 128), 0), iota((local, 128), 1)
    value = r.bypass_v[...].astype(BF16)
    r.wz2[me, hw : hw + hs, :] = (
        nn(value[:hs], to_bf16(e_col == e_row)) + nn(value[hs:], to_bf16(e_col == e_row + local))
    ).astype(BF16)

    def rows_of(ref, index):
        size = ref.shape[0] // OUTER
        return ref.at[pl.ds(pl.multiple_of(size * index, 16), size)]

    def unpack_own(ref, full):
        own = rows_of(ref, block)
        if full.shape[0] == hw:
            own[0:128, :] = full[0:128, 0:256]
            own[128:256, :] = full[0:128, 256:512]
            own[256 : 256 + tail, :] = full[128:, 0:256]
            own[256 + tail :, :] = full[128:, 256:512]
        else:
            own[0:hs, :] = full[:, 0:256]
            own[hs:, :] = full[:, 256:512]

    def spread(ref):
        own = rows_of(ref, block)
        return {
            mask: post(own, own, rows_of(ref, flip(block, mask)), dev(flip(block, mask), within, me))
            for mask in (2, 4, 6, 1)
        }

    def forward(ref, waits):
        rest = [waits[1]]
        for mask in (2, 4, 6):
            waits[mask]()
            mine = rows_of(ref, flip(block, mask))
            theirs = rows_of(ref, flip(partner, mask))
            rest.append(post(mine, mine, theirs, dev(partner, within, me)))
        return rest

    def widen(buffer):
        packed = jnp.concatenate([buffer[c] for c in range(n_ch)], axis=1)
        return nn(packed, r.unpack[...]).astype(BF16)

    for wait in entry_waits:
        wait()
    unpack_own(r.w1, widen(r.wz1))
    gather1 = spread(r.w1)
    exit_waits = to_channels(r.wz2)

    ident = to_bf16(iota((256, 256), 0) == iota((256, 256), 1))
    r.ident[...] = ident
    q_out, q_in = iota((256, 256), 0), iota((256, 256), 1)
    r.shift[0] = to_bf16((q_in == q_out + 1) & ((q_out & 15) < 15))
    r.shift[1] = to_bf16((q_in == q_out - 1) & ((q_out & 15) > 0))

    input_sums.middle()
    features.forward()
    got_cot()
    cotangent = Ring(
        lambda c, im: r.cown.at[per * c + im], lambda c, im: r.cbuf.at[c, im], r.pass_c
    )

    rho, px = iota((512, 256), 0), iota((512, 256), 1)
    version, a, b_ = rho >> 8, (rho >> 7) & 1, (rho >> 6) & 1
    col = (rho & 15) + version * (1 - 2 * b_)
    target = (2 * ((rho & 63) >> 4) + a) * 32 + 2 * col + b_
    r.gridder[...] = to_bf16((px == target) & (col >= 0) & (col < 16))
    target = (
        (2 * ((lane & 127) >> 4) + (lane >> 8)) * 32 + 2 * (lane & 15) + ((lane >> 7) & 1)
    )
    r.flatter[...] = to_bf16(column == target)
    zeros = jnp.zeros((16, 256), BF16)
    for im in range(per):
        for ver in range(3):
            r.h1s[ver, im, 0:16, :] = zeros
            r.h1s[ver, im, 272:288, :] = zeros
        for ver in range(2):
            for ph in range(4):
                for ref in (r.h2s, r.dzs):
                    ref[ver, ph, im, 0:16, :] = zeros
                    ref[ver, ph, im, 272:288, :] = zeros

    def channel_major(ref, im, lanes):
        return jnp.concatenate([ref[c, im, :, lanes] for c in range(n_ch)], axis=0)

    features.settle()
    for im in range(per):
        r.fpm[256 * im : 256 * im + 256, :] = nt(
            ident, channel_major(r.fbuf, im, slice(0, 256))
        ).astype(BF16)

    def wide_lanes(ref):
        parts = [
            ref[c] + pltpu.roll(ref[c + 1], local, axis=1) for c in range(0, n_ch, 2)
        ]
        return jnp.concatenate(parts, axis=1)

    for wait in affine_waits:
        wait()
    affine = wide_lanes(r.aff_z)
    stats = wide_lanes(input_sums.finish())
    mean1 = stats[0:4] / count
    inv1 = lax.rsqrt(stats[4:8] / count - mean1 * mean1 + NORM_EPSILON)
    gain = affine[2 * classes : 2 * classes + 1]
    shift = affine[2 * classes + 1 : 2 * classes + 2]
    out_bias = affine[2 * classes + 2 : 2 * classes + 3]
    group, label, mean1_b, inv1_b, gamma_b, beta_b, mask_b = [], [], [], [], [], [], []
    for im in range(per):
        group.append(r.groups[per * me + im])
        label.append(r.labels[per * me + im])
        mean1_b.append(pick_row(mean1, group[im]))
        inv1_b.append(pick_row(inv1, group[im]))
        gamma_b.append(pick_row(affine, label[im]))
        beta_b.append(pick_row(affine, label[im] + classes))
        width = r.widths[group[im]]
        mask_b.append(
            jnp.where(iota((1, chans), 1) < width * (chans // LEVELS), 1.0, 0.0)
        )

    for im in range(per):
        normal = (r.fpm[256 * im : 256 * im + 256, :].astype(F32) - mean1_b[im]) * inv1_b[im]
        pre = gamma_b[im] * normal + beta_b[im]
        hidden = (pre * sigmoid(pre)).astype(BF16)
        r.h1s[1, im, 16:272, :] = hidden
        r.h1s[0, im, 16:272, :] = nn(r.shift[1], hidden).astype(BF16)
        r.h1s[2, im, 16:272, :] = nn(r.shift[0], hidden).astype(BF16)
        r.h1cm[:, 256 * im : 256 * im + 256] = nt(ident, hidden).astype(BF16)

    for wait in exit_waits:
        wait()
    full = widen(r.wz2)
    unpack_own(r.w2, full[0:hw])
    unpack_own(r.ws, full[hw:])
    rest = forward(r.w1, gather1)
    gather2 = spread(r.w2)
    gather3 = spread(r.ws)
    for wait in rest:
        wait()

    def taps():
        return [(dy, dx) for dy in range(3) for dx in range(3)]

    def stack(pieces):
        return jnp.concatenate(pieces, axis=0)

    def conv1(phase, carry):
        a, c = lax.div(phase, 2), lax.rem(phase, 2)
        parts = []
        for dy, dx in taps():
            first = pl.multiple_of(16 * lax.div(a + dy + 1, 2), 16)
            ver = lax.div(c + dx + 1, 2)
            parts.append(
                stack([r.h1s[ver, im, pl.ds(first, 256), :] for im in range(per)])
            )
        y = nn(jnp.concatenate(parts, axis=1), r.w1[...])
        r.y1[phase] = y
        out = []
        for im in range(per):
            piece = y[256 * im : 256 * im + 256]
            out.append(carry[2 * im] + colsum(piece))
            out.append(carry[2 * im + 1] + colsum(piece * piece))
        return tuple(out)

    nought = jnp.zeros((1, chans), F32)
    mid = lax.fori_loop(0, 4, conv1, (nought,) * (2 * per))
    payload = jnp.zeros((8, chans), F32)
    for im in range(per):
        payload = payload + place_row(mid[2 * im], group[im], 8)
        payload = payload + place_row(mid[2 * im + 1], group[im] + 4, 8)
    mid_sums = AllReduce(2)
    mid_sums.begin(payload)

    def turn(src, dst):
        def one(tap, carry):
            first = pl.multiple_of(256 * tap, 256)
            dst[pl.ds(first, 256), :] = nt(r.ident[...], src[pl.ds(first, 256), :]).astype(BF16)
            return carry

        lax.fori_loop(0, 9, one, 0)

    cotangent.forward()
    turn(r.w1, r.w1t)
    rest = forward(r.w2, gather2) + forward(r.ws, gather3)
    mid_sums.middle()

    r.cbuf[me] = r.cown[pl.ds(per * me, per)]
    cotangent.settle()
    for im in range(per):
        for n in range(4):
            piece = channel_major(r.cbuf, im, slice(256 * n, 256 * n + 256))
            grid = nt(r.gridder[...], piece).astype(BF16)
            for ver in range(2):
                for ph in range(4):
                    at = 256 * ver + 64 * ph
                    r.dzs[ver, ph, im, 16 + 64 * n : 80 + 64 * n, :] = grid[at : at + 64]

    coarse = jnp.zeros((256 * per, chans), F32)
    for ph in range(4):
        coarse = coarse + stack([r.dzs[0, ph, im, 16:272, :] for im in range(per)]).astype(F32)
    bias_sum = colsum(coarse)
    r.dzc[...] = coarse.astype(BF16)

    def tap_slice(ref, a, c, dy, dx, im):
        row, colm = a + dy + 1, c + dx + 1
        first = pl.multiple_of(16 * lax.div(row, 2), 16)
        ph = 2 * lax.rem(row, 2) + lax.rem(colm, 2)
        side_step = lax.div(colm, 2) - 1
        return ref[side_step * side_step, ph, im, pl.ds(first, 256), :]

    for wait in rest:
        wait()
    turn(r.w2, r.w2t)

    def back2(phase, carry):
        a, c = lax.div(phase, 2), lax.rem(phase, 2)
        parts = [
            stack([tap_slice(r.dzs, a, c, 2 - dy, 2 - dx, im) for im in range(per)])
            for dy, dx in taps()
        ]
        r.act[phase] = nn(jnp.concatenate(parts, axis=1), r.w2t[...])
        return carry

    lax.fori_loop(0, 4, back2, 0)

    stats = mid_sums.end()
    mean2 = stats[0:4] / (4.0 * count)
    inv2 = lax.rsqrt(stats[4:8] / (4.0 * count) - mean2 * mean2 + NORM_EPSILON)
    mean2_b = [pick_row(mean2, group[im]) for im in range(per)]
    inv2_b = [pick_row(inv2, group[im]) for im in range(per)]

    def hidden2(phase, carry):
        c = lax.rem(phase, 2)
        out = []
        for im in range(per):
            span = slice(256 * im, 256 * im + 256)
            normal = (r.y1[phase, span, :] - mean2_b[im]) * inv2_b[im]
            r.y1[phase, span, :] = normal
            pre = gain * normal + shift
            sig = sigmoid(pre)
            hidden = (pre * sig * mask_b[im]).astype(BF16)
            act = r.act[phase, span, :] * (sig * (1.0 + pre * (1.0 - sig)) * mask_b[im])
            r.act[phase, span, :] = act
            out.append(carry[2 * im] + colsum(act))
            out.append(carry[2 * im + 1] + colsum(act * normal))
            r.h2s[0, phase, im, 16:272, :] = hidden
            r.h2s[1, phase, im, 16:272, :] = nn(r.shift[c], hidden).astype(BF16)
            lanes = pl.ds(pl.multiple_of(512 * phase + 256 * im, 256), 256)
            r.h2cm[:, lanes] = nt(r.ident[...], hidden).astype(BF16)
        return tuple(out)

    mid = lax.fori_loop(0, 4, hidden2, (nought,) * (2 * per))
    payload = place_row(bias_sum, 8, 16)
    for im in range(per):
        payload = payload + place_row(mid[2 * im], group[im], 16)
        payload = payload + place_row(mid[2 * im + 1], group[im] + 4, 16)
    back_sums = AllReduce(3)
    back_sums.begin(payload)

    r.short[...] = nn(r.fpm[...], r.ws[...]) + out_bias
    def conv2(phase, carry):
        a, c = lax.div(phase, 2), lax.rem(phase, 2)
        parts = [
            stack([tap_slice(r.h2s, a, c, dy, dx, im) for im in range(per)]) for dy, dx in taps()
        ]
        y = (nn(jnp.concatenate(parts, axis=1), r.w2[...]) + r.short[...]).astype(BF16)
        lanes = pl.ds(pl.multiple_of(256 * phase, 256), 256)
        for im in range(per):
            r.rc[im, :, lanes] = nt(r.ident[...], y[256 * im : 256 * im + 256]).astype(BF16)
        return carry

    lax.fori_loop(0, 4, conv2, 0)
    for im in range(per):
        for half in range(2):
            piece = jnp.concatenate(
                [r.rc[im, :, 256 * ph + 128 * half : 256 * ph + 128 * half + 128] for ph in range(4)],
                axis=1,
            )
            r.ocm[im, :, 512 * half : 512 * half + 512] = nn(piece, r.flatter[...]).astype(BF16)

    def own_channels(ref, index, im):
        return ref.at[im, pl.ds(pl.multiple_of(local * index, local), local), :]

    def give_back(ref, out, passing):
        for im in range(per):
            out[per * me + im] = own_channels(ref, me, im)[...]
        return Ring(
            lambda c, im: own_channels(ref, c, im), lambda c, im: out.at[per * c + im], passing
        )

    back_sums.middle()
    block_output = give_back(r.ocm, r.out, r.pass_o)

    def grad2(tap, carry):
        dy, dx = lax.div(tap, 3), lax.rem(tap, 3)
        pieces = []
        for ph in range(4):
            a, c = ph // 2, ph % 2
            for im in range(per):
                pieces.append(tap_slice(r.dzs, a, c, 2 - dy, 2 - dx, im))
        first = pl.multiple_of(256 * tap, 256)
        r.dw2[pl.ds(first, 256), :] = nn(r.h2cm[...], stack(pieces))
        return carry

    lax.fori_loop(0, 9, grad2, 0)
    for im in range(per):
        piece = channel_major(r.fbuf, im, slice(0, 256))
        grad = nn(piece, r.dzc[256 * im : 256 * im + 256, :])
        if im == 0:
            r.dws[...] = grad
        else:
            r.dws[...] = r.dws[...] + grad

    class GradSum:
        def __init__(self, number, fetch):
            self.fetch = fetch
            for part in PARTS:
                setattr(self, part, getattr(r, part + str(number)))

        def begin(self):
            self.waits = []
            for u in range(4):
                self.s1[u] = self.fetch(2 * u + 1 - core).astype(BF16)
                self.waits.append(
                    post(self.s1.at[u], self.r1.at[u], self.r1.at[u], dev(partner, within, me))
                )

        def settle(self):
            for wait in self.waits:
                wait()

        def across(self, send, got, masks):
            parts = [(h, v) for v in range(2) for h in range(2)] if len(send.shape) == 4 else [(0,), (1,)]
            self.waits = [
                post(send.at[p], got.at[p], got.at[p], dev(flip(block, masks[p[0]]), within, me))
                for p in parts
            ]

        def first(self):
            for u in range(4):
                self.waits[u]()
                self.acc[u] = self.fetch(2 * u + core) + self.r1[u].astype(F32)
            for v in range(2):
                self.s2[0, v] = self.acc[2 * v + 1 - bit_x, :, 0:128].astype(BF16)
                self.s2[1, v] = self.acc[2 * (1 - bit_y) + v, :, 128:256].astype(BF16)
            self.across(self.s2, self.r2, (2, 4))

        def second(self):
            self.settle()
            low = self.acc[2 * (1 - bit_y) + bit_x, :, 0:128] + self.r2[0, 1 - bit_y].astype(F32)
            high = self.acc[2 * bit_y + 1 - bit_x, :, 128:256] + self.r2[1, 1 - bit_x].astype(F32)
            self.s3[0] = low.astype(BF16)
            self.s3[1] = high.astype(BF16)
            self.across(self.s3, self.r3, (4, 2))

        def third(self):
            self.settle()
            low = self.acc[plane, :, 0:128] + self.r2[0, bit_y].astype(F32)
            high = self.acc[plane, :, 128:256] + self.r2[1, bit_x].astype(F32)
            low, high = low + self.r3[0].astype(F32), high + self.r3[1].astype(F32)
            value = jnp.concatenate([low, high], axis=1).astype(BF16)
            left = [value[0:128], value[256 : 256 + tail]]
            right = [value[128:256], value[256 + tail : rows]]
            if value.shape[0] > rows:
                left.append(value[rows : rows + hs])
                right.append(value[rows + hs :])
            pair = jnp.concatenate([stack(left), stack(right)], axis=1)
            packed = nt(pair, r.unpack[...]).astype(BF16)
            for c in range(n_ch):
                self.s4[c] = packed[:, 128 * c : 128 * c + 128]
            self.r4[me] = self.s4[me]
            self.waits = [
                post(self.s4.at[peer], self.r4.at[me], self.r4.at[peer], dev(block, within, peer))
                for peer in ch_peers
            ]

        def end(self, out, out_small=None):
            self.settle()
            done = self.r4[0].astype(F32)
            for c in range(1, n_ch):
                done = done + self.r4[c].astype(F32)
            turned = done[0:128].T
            out[:, 0:128] = turned[0:local]
            out[:, 128:256] = turned[local:]
            gap = jnp.zeros((128 - tail, 128), F32)
            turned = stack([done[128 : 128 + tail], gap]).T
            ends = turned[0:local] + pltpu.roll(turned[local:], tail, axis=1)
            out[:, 256:rows] = ends[:, 0 : rows - 256]
            if out_small is not None:
                last = done[hw:]
                out_small[0:hs, :] = last[:, 0:local]
                out_small[hs:, :] = pltpu.roll(last, local, axis=1)[:, 0:local]

    def block_rows(ref, size, index):
        return ref[pl.ds(pl.multiple_of(size * index, 8), size), :]

    second = GradSum(2, lambda k: stack([block_rows(r.dw2, rows, k), block_rows(r.dws, small, k)]))
    entry = GradSum(1, lambda k: block_rows(r.dw1, rows, k))
    second.begin()
    r.dshort[...] = nt(r.dzc[...], r.ws[...])

    stats = back_sums.end()
    affine_grad2 = stats
    p1_b = [pick_row(stats[0:4], group[im]) / (4.0 * count) for im in range(per)]
    p2_b = [pick_row(stats[4:8], group[im]) / (4.0 * count) for im in range(per)]

    for im in range(per):
        span = slice(256 * im, 256 * im + 256)
        scale = gain * inv2_b[im]
        combos = []
        for a in range(2):
            grads = []
            for c in range(2):
                ph = 2 * a + c
                d = scale * (r.act[ph, span, :] - (p1_b[im] + r.y1[ph, span, :] * p2_b[im]))
                grads.append(d.astype(BF16))
            right = nn(r.shift[0], grads[0])
            left = nn(r.shift[1], grads[1])
            even, odd = grads[0].astype(F32), grads[1].astype(F32)
            combos.append((odd + right, even + odd, left + even))
        gap = jnp.zeros((16, chans), F32)
        for dx in range(3):
            upper, lower = combos[0][dx], combos[1][dx]
            r.field[dx, im] = (lower + stack([upper[16:], gap])).astype(BF16)
            r.field[3 + dx, im] = (upper + lower).astype(BF16)
            r.field[6 + dx, im] = (stack([gap, lower[:-16]]) + upper).astype(BF16)

    block_output.forward()

    def grad1(tap, carry):
        first = pl.multiple_of(256 * tap, 256)
        r.dw1[pl.ds(first, 256), :] = nn(
            r.h1cm[...], stack([r.field[tap, im] for im in range(per)])
        )
        return carry

    lax.fori_loop(0, 9, grad1, 0)
    entry.begin()
    second.first()

    parts = [stack([r.field[tap, im] for im in range(per)]) for tap in range(9)]
    dh1 = nn(jnp.concatenate(parts, axis=1), r.w1t[...])
    payload = jnp.zeros((32, chans), F32)
    for im in range(per):
        span = slice(256 * im, 256 * im + 256)
        normal = (r.fpm[span, :].astype(F32) - mean1_b[im]) * inv1_b[im]
        pre = gamma_b[im] * normal + beta_b[im]
        sig = sigmoid(pre)
        act = dh1[span] * (sig * (1.0 + pre * (1.0 - sig)))
        r.act1[span, :] = act
        q1, q2 = colsum(act), colsum(act * normal)
        payload = payload + place_row(q2, label[im], 32)
        payload = payload + place_row(q1, label[im] + classes, 32)
        payload = payload + place_row(gamma_b[im] * q1, group[im] + 24, 32)
        payload = payload + place_row(gamma_b[im] * q2, group[im] + 28, 32)
    last_sums = AllReduce(4)
    last_sums.begin(payload)
    second.second()
    entry.first()
    last_sums.middle()
    second.third()
    entry.second()

    stats = last_sums.end()
    for im in range(per):
        span = slice(256 * im, 256 * im + 256)
        normal = (r.fpm[span, :].astype(F32) - mean1_b[im]) * inv1_b[im]
        r1 = pick_row(stats[24:28], group[im]) / count
        r2 = pick_row(stats[28:32], group[im]) / count
        grad = inv1_b[im] * (gamma_b[im] * r.act1[span, :] - (r1 + normal * r2))
        grad = (grad + r.dshort[span, :]).astype(BF16)
        r.dcm[im] = nt(r.ident[...], grad).astype(BF16)
    input_gradient = give_back(r.dcm, r.dx, r.pass_x)
    entry.third()
    second.end(r.grad2, r.grad3)
    input_gradient.forward()

    table = jnp.zeros((24, chans), F32)
    table = table + jnp.where(iota((24, chans), 0) < 2 * classes, stats[0:24], 0.0)
    table = table + place_row(colsum(affine_grad2[4:8]), 2 * classes, 24)
    table = table + place_row(colsum(affine_grad2[0:4]), 2 * classes + 1, 24)
    table = table + place_row(affine_grad2[8:9], 2 * classes + 2, 24)
    mine = jnp.zeros((24, 128), F32)
    for c in range(n_ch):
        piece = table[:, 128 * (c // 2) : 128 * (c // 2) + 128]
        if c % 2:
            piece = pltpu.roll(piece, local, axis=1)
        mine = mine + jnp.where(me == c, piece, 0.0)
    r.affine_grad[...] = mine

    if inner == 1:
        row = iota((8, 128), 0)

        def norm_rows(index, weight, grad, v):
            for wait in held[index]:
                wait()
            master = weight[...]
            _, _, direction = adam_update(
                grad[...], getattr(r, v + "m")[...], getattr(r, v + "q")[...]
            )
            update = direction + WEIGHT_DECAY * master
            rows_w = jnp.where(row == index, total(master * master), 0.0)
            return rows_w + jnp.where(row == index + 3, total(update * update), 0.0)

        norms = norm_rows(1, r.exit_v, r.grad2, "v2") + norm_rows(2, r.bypass_v, r.grad3, "vs")
        entry.end(r.grad1)
        norms = norms + norm_rows(0, r.entry_v, r.grad1, "v1")
        norm_sums = AllReduce(5)
        norm_sums.begin(norms)
        norm_sums.middle()
        r.norms[...] = norm_sums.end()
    else:
        entry.end(r.grad1)
        r.norms[...] = jnp.zeros((8, 128), F32)

    block_output.settle()
    input_gradient.settle()
    for wait in pending:
        wait()
    cfg.used.append((slots.remote, slots.local))


def final_kernel(cfg, *refs):
    r = SimpleNamespace(**dict(zip(cfg.names, refs)))
    classes = cfg.classes
    local = cfg.local
    r.block_output[...] = r.out[...]
    r.input_gradient[...] = r.dx[...].astype(F32)
    norms = jnp.sqrt(r.norms[...])
    weight_norm, update_norm = norms[0:3, 0:1], norms[3:6, 0:1]
    ratio = weight_norm / update_norm
    at = iota((3, 3), 1)
    r.trust_norms[...] = jnp.where(
        at == 0, weight_norm, jnp.where(at == 1, update_norm, ratio)
    )
    sets = (
        (r.entry, r.entry_m, r.entry_q, r.entry_g, r.entry_1, r.entry_2, r.entry_w),
        (r.exit, r.exit_m, r.exit_q, r.exit_g, r.exit_1, r.exit_2, r.exit_w),
        (r.bypass, r.bypass_m, r.bypass_q, r.bypass_g, r.bypass_1, r.bypass_2, r.bypass_w),
    )
    for index, (weight, m, q, g, first, second, result) in enumerate(sets):
        master = weight[...]
        moment, square, direction = adam_update(g[...], m[...], q[...])
        update = direction + WEIGHT_DECAY * master
        first[...] = moment
        second[...] = square
        result[...] = master - MATRIX_RATE * ratio[index : index + 1] * update
    grad = r.affine_grad[0 : 2 * classes + 3, 0:local]
    moment, square, direction = adam_update(grad, r.affine_m[...], r.affine_q[...])
    r.affine_1[...] = moment
    r.affine_2[...] = square
    r.affine_w[...] = r.affine[...] - AFFINE_RATE * direction


def per_device(
    features,
    labels,
    groups,
    widths,
    entry_conv,
    entry_moment,
    entry_square,
    exit_conv,
    exit_moment,
    exit_square,
    bypass_conv,
    bypass_moment,
    bypass_square,
    norm_affine,
    norm_moment,
    norm_square,
    cotangent,
):
    n_img, n_ch = lax.axis_size("img"), lax.axis_size("ch")
    batch, local, pixels = features.shape
    chans = local * n_ch
    side = math.isqrt(pixels)
    inner = n_img // OUTER
    classes = (norm_affine.shape[0] - 3) // 2
    per = batch // n_ch
    assert (side, chans, n_ch, local, batch % n_ch) == (16, 256, 4, 64, 0) and per == 2
    rows, small = entry_conv.shape[0] * inner, bypass_conv.shape[0] * inner
    masters = (entry_conv, exit_conv, bypass_conv)
    if inner == 1:
        blocks = masters
    else:
        sets = [[o * inner + i for i in range(inner)] for o in range(OUTER)]
        blocks = tuple(
            lax.all_gather(w.astype(BF16), "img", axis=0, tiled=True, axis_index_groups=sets)
            for w in masters
        )

    vmem = pl.BlockSpec(memory_space=pltpu.VMEM)
    smem = pl.BlockSpec(memory_space=pltpu.SMEM)
    anywhere = pl.BlockSpec(memory_space=pl.ANY)
    states = dict(
        entry_m=entry_moment.T,
        entry_q=entry_square.T,
        exit_m=exit_moment.T,
        exit_q=exit_square.T,
        bypass_m=bypass_moment,
        bypass_q=bypass_square,
    )
    inputs = dict(
        labels=(labels, smem),
        groups=(groups, smem),
        widths=(widths, smem),
        features=(features, anywhere),
        cotangent=(cotangent, anywhere),
        entry=(blocks[0].T, anywhere),
        exit=(blocks[1].T, anywhere),
        bypass=(blocks[2], anywhere),
        affine=(norm_affine, anywhere),
    )
    if inner == 1:
        inputs.update({name: (value, anywhere) for name, value in states.items()})
    sds = jax.ShapeDtypeStruct
    outputs = dict(
        out=(sds(cotangent.shape, BF16), vmem),
        dx=(sds(features.shape, BF16), vmem),
        grad1=(sds((local, rows), F32), vmem),
        grad2=(sds((local, rows), F32), vmem),
        grad3=(sds((small, local), F32), vmem),
        affine_grad=(sds((24, 128), F32), vmem),
        norms=(sds((8, 128), F32), vmem),
    )
    pix = pixels * per
    taps9 = 9 * chans
    held = lambda shape, dtype=BF16: pltpu.VMEM(shape, dtype)
    scratch = dict(
        fown=held((batch, local, pixels)),
        cown=held((batch, local, 4 * pixels)),
        pass_f=held((2, local, pixels)),
        pass_c=held((2, local, 4 * pixels)),
        pass_o=held((2, local, 4 * pixels)),
        pass_x=held((2, local, pixels)),
        fbuf=held((n_ch, per, local, pixels)),
        cbuf=held((n_ch, per, local, 4 * pixels)),
        entry_v=held((local, rows), blocks[0].dtype),
        exit_v=held((local, rows), blocks[1].dtype),
        bypass_v=held((small, local), blocks[2].dtype),
        affine_v=held(norm_affine.shape, F32),
        padded=held((3 * local, 384)),
        wz1=held((n_ch, rows // 2, 128)),
        wz2=held((n_ch, (rows + small) // 2, 128)),
        aff_z=held((n_ch, 24, 128), F32),
        w1=held((taps9, chans)),
        w2=held((taps9, chans)),
        ws=held((chans, chans)),
        w1t=held((taps9, chans)),
        w2t=held((taps9, chans)),
        unpack=held((512, 512)),
        ident=held((256, 256)),
        shift=held((2, 256, 256)),
        gridder=held((512, 256)),
        flatter=held((512, 512)),
        fpm=held((pix, chans)),
        h1s=held((3, per, pixels + 32, chans)),
        h1cm=held((chans, pix)),
        y1=held((4, pix, chans), F32),
        act=held((4, pix, chans), F32),
        h2s=held((2, 4, per, pixels + 32, chans)),
        dzs=held((2, 4, per, pixels + 32, chans)),
        h2cm=held((chans, 4 * pix)),
        short=held((pix, chans), F32),
        dshort=held((pix, chans), F32),
        dzc=held((pix, chans)),
        act1=held((pix, chans), F32),
        rc=held((per, chans, 4 * pixels)),
        ocm=held((per, chans, 4 * pixels)),
        dcm=held((per, chans, pixels)),
        field=held((9, per, pixels, chans)),
        dw1=held((taps9, chans), F32),
        dw2=held((taps9, chans), F32),
        dws=held((chans, chans), F32),
    )
    for number, size in ((1, rows), (2, rows + small)):
        shapes = ((4, size, chans),) * 2 + ((2, 2, size, 128),) * 2 + ((2, size, 128),) * 2
        shapes += ((n_ch, size // 2, 128),) * 2
        for part, shape in zip(PARTS, shapes):
            scratch[part + str(number)] = held(shape)
        scratch[PARTS[-1] + str(number)] = held((4, size, chans), F32)
    exchanges = [(8, 128), (8, chans), (16, chans), (32, chans)]
    if inner == 1:
        exchanges.append((8, 128))
        for v, shape in (("v1", (local, rows)), ("v2", (local, rows)), ("vs", (small, local))):
            scratch[v + "m"] = held(shape, F32)
            scratch[v + "q"] = held(shape, F32)
    for number, shape in enumerate(exchanges, 1):
        for axis, size in zip("abc", (OUTER, inner, n_ch)):
            if size > 1:
                scratch[axis + str(number)] = held((size,) + shape, F32)
    remote_count = 3 * 3 + 4 * 4 * per + 3 * 7 + 2 * 13 + len(exchanges) * (7 + 3 + inner - 1)
    scratch.update(
        send=pltpu.SemaphoreType.DMA((remote_count,)),
        recv=pltpu.SemaphoreType.DMA((remote_count,)),
        lsem=pltpu.SemaphoreType.DMA((20,)),
    )
    cfg = SimpleNamespace(
        names=[*inputs, *outputs, *scratch],
        inner=inner,
        n_ch=n_ch,
        batch=batch,
        local=local,
        classes=classes,
        count=float(batch * n_img // widths.shape[0] * pixels),
        rows=rows,
        small=small,
        used=[],
    )
    out, dx, grad1, grad2, grad3, affine_grad, norms = pl.pallas_call(
        functools.partial(main_kernel, cfg),
        out_shape=[s for s, _ in outputs.values()],
        in_specs=[s for _, s in inputs.values()],
        out_specs=[s for _, s in outputs.values()],
        scratch_shapes=list(scratch.values()),
        compiler_params=pltpu.CompilerParams(
            collective_id=0, has_side_effects=True, vmem_limit_bytes=VMEM_LIMIT
        ),
        name="block_step",
    )(*[v for v, _ in inputs.values()])
    assert max(n for n, _ in cfg.used) <= remote_count and max(n for _, n in cfg.used) <= 20

    grads = [grad1, grad2, grad3]
    if inner > 1:
        grads = [
            lax.psum_scatter(g, "img", scatter_dimension=0, axis_index_groups=sets, tiled=True)
            for g in (grad1.T, grad2.T, grad3)
        ]
        updates = []
        for w, g, m, s in zip(
            masters,
            grads,
            (entry_moment, exit_moment, bypass_moment),
            (entry_square, exit_square, bypass_square),
        ):
            updates.append(adam_update(g, m, s)[2] + WEIGHT_DECAY * w)
        sums = lax.psum(
            jnp.stack([jnp.sum(w * w) for w in masters] + [jnp.sum(u * u) for u in updates]),
            ("img", "ch"),
        )
        norms = jnp.broadcast_to(jnp.pad(sums, (0, 2))[:, None], (8, 128))
        grads = [grads[0].T, grads[1].T, grads[2]]

    args = dict(
        out=out,
        dx=dx,
        norms=norms,
        affine_grad=affine_grad,
        entry_g=grads[0],
        exit_g=grads[1],
        bypass_g=grads[2],
        entry=entry_conv.T,
        exit=exit_conv.T,
        bypass=bypass_conv,
        **states,
        affine=norm_affine,
        affine_m=norm_moment,
        affine_q=norm_square,
    )
    tall = sds(entry_conv.shape[::-1], F32)
    short, wide = (sds(w.shape, F32) for w in (bypass_conv, norm_affine))
    results = dict(
        block_output=sds(cotangent.shape, BF16),
        input_gradient=sds(features.shape, F32),
        entry_1=tall,
        entry_2=tall,
        entry_w=tall,
        exit_1=tall,
        exit_2=tall,
        exit_w=tall,
        bypass_1=short,
        bypass_2=short,
        bypass_w=short,
        affine_1=wide,
        affine_2=wide,
        affine_w=wide,
        trust_norms=sds((3, 3), F32),
    )
    end_cfg = SimpleNamespace(names=[*args, *results], classes=classes, local=local)
    final = pl.pallas_call(
        functools.partial(final_kernel, end_cfg),
        out_shape=list(results.values()),
        in_specs=[vmem] * len(args),
        out_specs=[vmem] * len(results),
        compiler_params=pltpu.CompilerParams(vmem_limit_bytes=VMEM_LIMIT),
        name="finish",
    )(*args.values())
    return tuple(v.T if s is tall else v for v, s in zip(final, results.values()))


def solution(mesh):
    wide = P("img", "ch")
    deep = P("img", "ch", None)
    table = P(None, "ch")
    return jax.shard_map(
        per_device,
        mesh=mesh,
        in_specs=(deep, P("img"), P("img"), P()) + (wide,) * 9 + (table,) * 3 + (deep,),
        out_specs=(deep, deep) + (wide,) * 9 + (table,) * 3 + (P(),),
        check_vma=False,
    )
```

```python
import functools
import math
from types import SimpleNamespace

import jax
import jax.numpy as jnp
from jax import lax
from jax.experimental import pallas as pl
from jax.experimental.pallas import tpu as pltpu
from jax.sharding import PartitionSpec as P

LEVELS = 4
STEP = 5
NORM_EPSILON = 1e-05
ADAM_EPSILON = 1e-06
MOMENT_DECAY = 0.9
SQUARE_DECAY = 0.999
WEIGHT_DECAY = 0.01
MATRIX_RATE = 0.3
AFFINE_RATE = 0.2

OUTER = 8
VMEM_LIMIT = 56 * 1024 * 1024
BF16 = jnp.bfloat16
F32 = jnp.float32
MESH = pl.DeviceIdType.MESH
PARTS = ("s1", "r1", "s2", "r2", "s3", "r3", "s4", "r4", "acc")


def nn(left, right):
    return lax.dot_general(left, right, (((1,), (0,)), ((), ())), preferred_element_type=F32)


def nt(left, right):
    return lax.dot_general(left, right, (((1,), (1,)), ((), ())), preferred_element_type=F32)


def tn(left, right):
    return lax.dot_general(left, right, (((0,), (0,)), ((), ())), preferred_element_type=F32)


def flip(index, mask):
    result = index
    for bit in range(3):
        if (mask >> bit) & 1:
            digit = lax.rem(lax.div(index, 1 << bit), 2)
            result = result + (1 - 2 * digit) * (1 << bit)
    return result


def sigmoid(value):
    return 0.5 * jnp.tanh(0.5 * value) + 0.5


def iota(shape, axis):
    return lax.broadcasted_iota(jnp.int32, shape, axis)


def to_bf16(condition):
    return jnp.where(condition, 1.0, 0.0).astype(BF16)


def pick_row(table, index):
    hit = iota(table.shape, 0) == index
    return jnp.sum(jnp.where(hit, table, 0.0), axis=0, keepdims=True)


def place_row(row, index, rows):
    hit = iota((rows, row.shape[1]), 0) == index
    return jnp.where(hit, row, 0.0)


def colsum(value):
    return jnp.sum(value, axis=0, keepdims=True)


def adam_update(grad, moment, square):
    moment_new = MOMENT_DECAY * moment + (1.0 - MOMENT_DECAY) * grad
    square_new = SQUARE_DECAY * square + (1.0 - SQUARE_DECAY) * grad * grad
    direction = (
        moment_new
        / (1.0 - MOMENT_DECAY**STEP)
        / (jnp.sqrt(square_new / (1.0 - SQUARE_DECAY**STEP)) + ADAM_EPSILON)
    )
    return (moment_new, square_new, direction)


def total(value):
    return jnp.sum(jnp.sum(value, axis=1, keepdims=True), axis=0, keepdims=True)


def main_kernel(cfg, *refs):
    r = SimpleNamespace(**dict(zip(cfg.names, refs)))
    inner, n_ch, batch, local = cfg.inner, cfg.n_ch, cfg.batch, cfg.local
    classes, count = cfg.classes, cfg.count
    per = batch // n_ch
    chans = local * n_ch
    rows, small = cfg.rows, cfg.small
    tail = (rows - 256) // 2
    hw, hs = rows // 2, small // 2
    slots = SimpleNamespace(remote=0, local=0)

    img = lax.axis_index("img")
    me = lax.axis_index("ch")
    block = lax.div(img, inner)
    within = lax.rem(img, inner)
    core = lax.rem(block, 2)
    plane = lax.div(block, 2)
    bit_x, bit_y = lax.rem(plane, 2), lax.div(plane, 2)
    partner = flip(block, 1)

    def dev(block_id, within_id, ch_id):
        return (block_id * inner + within_id, ch_id)

    pending = []

    def post(src, dst, landed, peer):
        slot = slots.remote
        slots.remote = slot + 1
        copy = pltpu.make_async_remote_copy(
            src_ref=src,
            dst_ref=dst,
            send_sem=r.send.at[slot],
            recv_sem=r.recv.at[slot],
            device_id=peer,
            device_id_type=MESH,
        )
        copy.start()
        pending.append(copy.wait_send)
        arrival = pltpu.make_async_remote_copy(
            src_ref=landed,
            dst_ref=landed,
            send_sem=r.send.at[slot],
            recv_sem=r.recv.at[slot],
            device_id=peer,
            device_id_type=MESH,
        )
        return arrival.wait_recv

    def here(src, dst):
        slot = slots.local
        slots.local = slot + 1
        copy = pltpu.make_async_copy(src, dst, r.lsem.at[slot])
        copy.start()
        return copy.wait

    outer_peers = [flip(block, mask) for mask in range(1, OUTER)]
    ch_peers = [flip(me, mask) for mask in range(1, n_ch)]
    inner_pairs = [
        (lax.rem(within + step, inner), lax.rem(within + inner - step, inner))
        for step in range(1, inner)
    ]
    up, down, far = (lax.rem(me + step, n_ch) for step in (1, 3, 2))
    up_peer, down_peer = dev(block, within, up), dev(block, within, down)

    class Ring:
        def __init__(self, source, target, passing):
            self.target, self.passing = target, passing
            self.waits = []
            self.early = [
                post(source(far, 0), passing.at[0], passing.at[0], up_peer),
                post(source(far, 1), passing.at[1], passing.at[1], down_peer),
            ]
            for im in range(per):
                self.waits += [
                    post(source(up, im), target(me, im), target(down, im), up_peer),
                    post(source(down, im), target(me, im), target(up, im), down_peer),
                ]

        def forward(self):
            self.early[0]()
            self.waits.append(
                post(self.passing.at[0], self.target(down, 0), self.target(far, 0), up_peer)
            )
            self.early[1]()
            self.waits.append(
                post(self.passing.at[1], self.target(up, 1), self.target(far, 1), down_peer)
            )

        def settle(self):
            for wait in self.waits:
                wait()

    barrier = pltpu.get_barrier_semaphore()
    everyone = [dev(peer, within, me) for peer in outer_peers]
    everyone += [dev(block, within, peer) for peer in ch_peers]
    everyone += [dev(block, peer, me) for peer, _ in inner_pairs]
    for peer in everyone:
        pl.semaphore_signal(barrier, inc=1, device_id=peer, device_id_type=MESH)

    got_entry = here(r.entry, r.entry_v)
    got_features = here(r.features, r.fown)
    got_exit = here(r.exit, r.exit_v)
    got_bypass = here(r.bypass, r.bypass_v)
    got_affine = here(r.affine, r.affine_v)
    got_cot = here(r.cotangent, r.cown)
    states = ((r.entry_m, r.entry_q), (r.exit_m, r.exit_q), (r.bypass_m, r.bypass_q)) if inner == 1 else ()
    held = [
        (here(m, getattr(r, v + "m")), here(q, getattr(r, v + "q")))
        for (m, q), v in zip(states, ("v1", "v2", "vs"))
    ]

    s_row, s_col = iota((hw, 384), 0), iota((hw, 384), 1)
    pick_first = to_bf16(s_col == jnp.where(s_row < 128, s_row, s_row + 128))
    pick_second = to_bf16(s_col == jnp.where(s_row < 128, s_row + 128, s_row + 128 + tail))
    r.padded[...] = jnp.zeros(r.padded.shape, BF16)

    def pack_own(value):
        r.padded[local : 2 * local, 0:rows] = value.astype(BF16)
        packed = nt(pick_first, r.padded[local : 3 * local, :])
        return (packed + nt(pick_second, r.padded[0 : 2 * local, :])).astype(BF16)

    got_entry()
    r.wz1[me] = pack_own(r.entry_v[...])
    pl.semaphore_wait(barrier, len(everyone))

    def to_channels(buffer):
        return [
            post(buffer.at[me], buffer.at[me], buffer.at[peer], dev(block, within, peer))
            for peer in ch_peers
        ]

    entry_waits = to_channels(r.wz1)
    got_features()
    features = Ring(
        lambda c, im: r.fown.at[per * c + im], lambda c, im: r.fbuf.at[c, im], r.pass_f
    )
    got_affine()
    r.aff_z[me] = jnp.zeros((24, 128), F32)
    r.aff_z[me, 0 : 2 * classes + 3, 0:local] = r.affine_v[...]
    affine_waits = to_channels(r.aff_z)

    lane = iota((512, 512), 0)
    column = iota((512, 512), 1)
    spot = 256 * ((lane >> 6) & 1) + 64 * (lane >> 7) + (lane & 63)
    r.unpack[...] = to_bf16(column == spot)

    r.fbuf[me] = r.fown[pl.ds(per * me, per)]
    flat = jnp.concatenate([r.fown[b] for b in range(batch)], axis=1)
    wide = flat.astype(F32)
    square = wide * wide
    square_hi = square.astype(BF16)
    square_lo = (square - square_hi.astype(F32)).astype(BF16)
    level = iota((16, 256), 0)
    first_mask = jnp.concatenate([to_bf16(level == r.groups[b]) for b in range(batch)], axis=1)
    second_mask = jnp.concatenate([to_bf16(level == r.groups[b] + 4) for b in range(batch)], axis=1)
    sums = nt(first_mask, flat) + nt(second_mask, square_hi) + nt(second_mask, square_lo)

    def ordered_sum(ref, size):
        result = ref[0]
        for slot in range(1, size):
            result = result + ref[slot]
        return result

    class AllReduce:
        def __init__(self, number):
            self.over_outer, self.over_inner, self.over_ch = (
                getattr(r, axis + str(number), None) for axis in "abc"
            )

        def begin(self, value, masked=None):
            ref = self.over_outer
            if masked is None:
                ref[block] = value
            else:
                ref[block] = jnp.zeros(ref.shape[1:], F32)
                ref[block, :, 0:masked] = value
            self.waits = [
                post(ref.at[block], ref.at[block], ref.at[peer], dev(peer, within, me))
                for peer in outer_peers
            ]

        def middle(self):
            for wait in self.waits:
                wait()
            value = ordered_sum(self.over_outer, OUTER)
            if inner > 1:
                ref = self.over_inner
                ref[within] = value
                waits = [
                    post(ref.at[within], ref.at[within], ref.at[back], dev(block, peer, me))
                    for peer, back in inner_pairs
                ]
                for wait in waits:
                    wait()
                value = ordered_sum(ref, inner)
            self.over_ch[me] = value
            self.waits = to_channels(self.over_ch)

        def finish(self):
            for wait in self.waits:
                wait()
            return self.over_ch

        def end(self):
            return ordered_sum(self.finish(), n_ch)

    input_sums = AllReduce(1)
    input_sums.begin(sums[0:8], masked=local)

    got_exit()
    got_bypass()
    r.wz2[me, 0:hw, :] = pack_own(r.exit_v[...])
    e_row, e_col = iota((local, 128), 0), iota((local, 128), 1)
    value = r.bypass_v[...].astype(BF16)
    r.wz2[me, hw : hw + hs, :] = (
        nn(value[:hs], to_bf16(e_col == e_row)) + nn(value[hs:], to_bf16(e_col == e_row + local))
    ).astype(BF16)

    def rows_of(ref, index):
        size = ref.shape[0] // OUTER
        return ref.at[pl.ds(pl.multiple_of(size * index, 16), size)]

    def unpack_own(ref, full):
        own = rows_of(ref, block)
        if full.shape[0] == hw:
            own[0:128, :] = full[0:128, 0:256]
            own[128:256, :] = full[0:128, 256:512]
            own[256 : 256 + tail, :] = full[128:, 0:256]
            own[256 + tail :, :] = full[128:, 256:512]
        else:
            own[0:hs, :] = full[:, 0:256]
            own[hs:, :] = full[:, 256:512]

    def spread(ref):
        own = rows_of(ref, block)
        return {
            mask: post(own, own, rows_of(ref, flip(block, mask)), dev(flip(block, mask), within, me))
            for mask in (2, 4, 6, 1)
        }

    def forward(ref, waits):
        rest = [waits[1]]
        for mask in (2, 4, 6):
            waits[mask]()
            mine = rows_of(ref, flip(block, mask))
            theirs = rows_of(ref, flip(partner, mask))
            rest.append(post(mine, mine, theirs, dev(partner, within, me)))
        return rest

    def widen(buffer):
        packed = jnp.concatenate([buffer[c] for c in range(n_ch)], axis=1)
        return nn(packed, r.unpack[...]).astype(BF16)

    for wait in entry_waits:
        wait()
    unpack_own(r.w1, widen(r.wz1))
    gather1 = spread(r.w1)
    exit_waits = to_channels(r.wz2)

    ident = to_bf16(iota((256, 256), 0) == iota((256, 256), 1))
    r.ident[...] = ident
    q_out, q_in = iota((256, 256), 0), iota((256, 256), 1)
    r.shift[0] = to_bf16((q_in == q_out + 1) & ((q_out & 15) < 15))
    r.shift[1] = to_bf16((q_in == q_out - 1) & ((q_out & 15) > 0))

    input_sums.middle()
    features.forward()
    got_cot()
    cotangent = Ring(
        lambda c, im: r.cown.at[per * c + im], lambda c, im: r.cbuf.at[c, im], r.pass_c
    )

    rho, px = iota((512, 256), 0), iota((512, 256), 1)
    version, a, b_ = rho >> 8, (rho >> 7) & 1, (rho >> 6) & 1
    col = (rho & 15) + version * (1 - 2 * b_)
    target = (2 * ((rho & 63) >> 4) + a) * 32 + 2 * col + b_
    r.gridder[...] = to_bf16((px == target) & (col >= 0) & (col < 16))
    zeros = jnp.zeros((16, 256), BF16)
    for im in range(per):
        for ver in range(3):
            r.h1s[ver, im, 0:16, :] = zeros
            r.h1s[ver, im, 272:288, :] = zeros
        for ver in range(2):
            for ph in range(4):
                for ref in (r.h2s, r.dzs):
                    ref[ver, ph, im, 0:16, :] = zeros
                    ref[ver, ph, im, 272:288, :] = zeros

    def channel_major(ref, im, lanes):
        return jnp.concatenate([ref[c, im, :, lanes] for c in range(n_ch)], axis=0)

    features.settle()
    for im in range(per):
        r.fpm[256 * im : 256 * im + 256, :] = nt(
            ident, channel_major(r.fbuf, im, slice(0, 256))
        ).astype(BF16)

    def wide_lanes(ref):
        parts = [
            ref[c] + pltpu.roll(ref[c + 1], local, axis=1) for c in range(0, n_ch, 2)
        ]
        return jnp.concatenate(parts, axis=1)

    for wait in affine_waits:
        wait()
    affine = wide_lanes(r.aff_z)
    stats = wide_lanes(input_sums.finish())
    mean1 = stats[0:4] / count
    inv1 = lax.rsqrt(stats[4:8] / count - mean1 * mean1 + NORM_EPSILON)
    gain = affine[2 * classes : 2 * classes + 1]
    shift = affine[2 * classes + 1 : 2 * classes + 2]
    out_bias = affine[2 * classes + 2 : 2 * classes + 3]
    group, label, mean1_b, inv1_b, gamma_b, beta_b, mask_b = [], [], [], [], [], [], []
    for im in range(per):
        group.append(r.groups[per * me + im])
        label.append(r.labels[per * me + im])
        mean1_b.append(pick_row(mean1, group[im]))
        inv1_b.append(pick_row(inv1, group[im]))
        gamma_b.append(pick_row(affine, label[im]))
        beta_b.append(pick_row(affine, label[im] + classes))
        width = r.widths[group[im]]
        mask_b.append(
            jnp.where(iota((1, chans), 1) < width * (chans // LEVELS), 1.0, 0.0)
        )

    for im in range(per):
        normal = (r.fpm[256 * im : 256 * im + 256, :].astype(F32) - mean1_b[im]) * inv1_b[im]
        pre = gamma_b[im] * normal + beta_b[im]
        hidden = (pre * sigmoid(pre)).astype(BF16)
        r.h1s[1, im, 16:272, :] = hidden
        r.h1s[0, im, 16:272, :] = nn(r.shift[1], hidden).astype(BF16)
        r.h1s[2, im, 16:272, :] = nn(r.shift[0], hidden).astype(BF16)
        r.h1cm[:, 256 * im : 256 * im + 256] = nt(ident, hidden).astype(BF16)

    for wait in exit_waits:
        wait()
    full = widen(r.wz2)
    unpack_own(r.w2, full[0:hw])
    unpack_own(r.ws, full[hw:])
    rest = forward(r.w1, gather1)
    gather2 = spread(r.w2)
    gather3 = spread(r.ws)
    for wait in rest:
        wait()

    def back_product(parts, ref):
        result = nt(parts[0], ref[0:256, :])
        for tap in range(1, 9):
            result = result + nt(parts[tap], ref[256 * tap : 256 * tap + 256, :])
        return result

    def taps():
        return [(dy, dx) for dy in range(3) for dx in range(3)]

    def stack(pieces):
        return jnp.concatenate(pieces, axis=0)

    def conv1(phase, carry):
        a, c = lax.div(phase, 2), lax.rem(phase, 2)
        parts = []
        for dy, dx in taps():
            first = pl.multiple_of(16 * lax.div(a + dy + 1, 2), 16)
            ver = lax.div(c + dx + 1, 2)
            parts.append(
                stack([r.h1s[ver, im, pl.ds(first, 256), :] for im in range(per)])
            )
        y = nn(jnp.concatenate(parts, axis=1), r.w1[...])
        r.y1[phase] = y
        out = []
        for im in range(per):
            piece = y[256 * im : 256 * im + 256]
            out.append(carry[2 * im] + colsum(piece))
            out.append(carry[2 * im + 1] + colsum(piece * piece))
        return tuple(out)

    nought = jnp.zeros((1, chans), F32)
    mid = lax.fori_loop(0, 4, conv1, (nought,) * (2 * per))
    payload = jnp.zeros((8, chans), F32)
    for im in range(per):
        payload = payload + place_row(mid[2 * im], group[im], 8)
        payload = payload + place_row(mid[2 * im + 1], group[im] + 4, 8)
    mid_sums = AllReduce(2)
    mid_sums.begin(payload)

    cotangent.forward()
    rest = forward(r.w2, gather2) + forward(r.ws, gather3)
    mid_sums.middle()

    r.cbuf[me] = r.cown[pl.ds(per * me, per)]
    cotangent.settle()
    for im in range(per):
        for n in range(4):
            piece = channel_major(r.cbuf, im, slice(256 * n, 256 * n + 256))
            grid = nt(r.gridder[...], piece).astype(BF16)
            for ver in range(2):
                for ph in range(4):
                    at = 256 * ver + 64 * ph
                    r.dzs[ver, ph, im, 16 + 64 * n : 80 + 64 * n, :] = grid[at : at + 64]

    coarse = jnp.zeros((256 * per, chans), F32)
    for ph in range(4):
        coarse = coarse + stack([r.dzs[0, ph, im, 16:272, :] for im in range(per)]).astype(F32)
    bias_sum = colsum(coarse)
    r.dzc[...] = coarse.astype(BF16)

    def tap_slice(ref, a, c, dy, dx, im):
        row, colm = a + dy + 1, c + dx + 1
        first = pl.multiple_of(16 * lax.div(row, 2), 16)
        ph = 2 * lax.rem(row, 2) + lax.rem(colm, 2)
        side_step = lax.div(colm, 2) - 1
        return ref[side_step * side_step, ph, im, pl.ds(first, 256), :]

    for wait in rest:
        wait()

    def back2(phase, carry):
        a, c = lax.div(phase, 2), lax.rem(phase, 2)
        parts = [
            stack([tap_slice(r.dzs, a, c, 2 - dy, 2 - dx, im) for im in range(per)])
            for dy, dx in taps()
        ]
        r.act[phase] = back_product(parts, r.w2)
        return carry

    lax.fori_loop(0, 4, back2, 0)

    stats = mid_sums.end()
    mean2 = stats[0:4] / (4.0 * count)
    inv2 = lax.rsqrt(stats[4:8] / (4.0 * count) - mean2 * mean2 + NORM_EPSILON)
    mean2_b = [pick_row(mean2, group[im]) for im in range(per)]
    inv2_b = [pick_row(inv2, group[im]) for im in range(per)]

    def hidden2(phase, carry):
        c = lax.rem(phase, 2)
        out = []
        for im in range(per):
            span = slice(256 * im, 256 * im + 256)
            normal = (r.y1[phase, span, :] - mean2_b[im]) * inv2_b[im]
            r.y1[phase, span, :] = normal
            pre = gain * normal + shift
            sig = sigmoid(pre)
            hidden = (pre * sig * mask_b[im]).astype(BF16)
            act = r.act[phase, span, :] * (sig * (1.0 + pre * (1.0 - sig)) * mask_b[im])
            r.act[phase, span, :] = act
            out.append(carry[2 * im] + colsum(act))
            out.append(carry[2 * im + 1] + colsum(act * normal))
            r.h2s[0, phase, im, 16:272, :] = hidden
            r.h2s[1, phase, im, 16:272, :] = nn(r.shift[c], hidden).astype(BF16)
            lanes = pl.ds(pl.multiple_of(512 * phase + 256 * im, 256), 256)
            r.h2cm[:, lanes] = nt(r.ident[...], hidden).astype(BF16)
        return tuple(out)

    mid = lax.fori_loop(0, 4, hidden2, (nought,) * (2 * per))
    payload = place_row(bias_sum, 8, 16)
    for im in range(per):
        payload = payload + place_row(mid[2 * im], group[im], 16)
        payload = payload + place_row(mid[2 * im + 1], group[im] + 4, 16)
    back_sums = AllReduce(3)
    back_sums.begin(payload)

    r.short[...] = nn(r.fpm[...], r.ws[...]) + out_bias
    def conv2(phase, carry):
        a, c = lax.div(phase, 2), lax.rem(phase, 2)
        parts = [
            stack([tap_slice(r.h2s, a, c, dy, dx, im) for im in range(per)]) for dy, dx in taps()
        ]
        y = nn(jnp.concatenate(parts, axis=1), r.w2[...]) + r.short[...]
        r.rc[phase] = y.astype(BF16)
        return carry

    lax.fori_loop(0, 4, conv2, 0)
    for im in range(per):
        for n in range(4):
            first = 256 * im + 64 * n
            piece = stack([r.rc[ph, first : first + 64, :] for ph in range(4)])
            r.ocm[im, :, 256 * n : 256 * n + 256] = tn(piece, r.gridder[0:256, :]).astype(BF16)

    def own_channels(ref, index, im):
        return ref.at[im, pl.ds(pl.multiple_of(local * index, local), local), :]

    def give_back(ref, out, passing):
        for im in range(per):
            out[per * me + im] = own_channels(ref, me, im)[...]
        return Ring(
            lambda c, im: own_channels(ref, c, im), lambda c, im: out.at[per * c + im], passing
        )

    back_sums.middle()
    block_output = give_back(r.ocm, r.out, r.pass_o)

    def grad2(tap, carry):
        dy, dx = lax.div(tap, 3), lax.rem(tap, 3)
        pieces = []
        for ph in range(4):
            a, c = ph // 2, ph % 2
            for im in range(per):
                pieces.append(tap_slice(r.dzs, a, c, 2 - dy, 2 - dx, im))
        first = pl.multiple_of(256 * tap, 256)
        r.dw2[pl.ds(first, 256), :] = nn(r.h2cm[...], stack(pieces))
        return carry

    lax.fori_loop(0, 9, grad2, 0)
    for im in range(per):
        piece = channel_major(r.fbuf, im, slice(0, 256))
        grad = nn(piece, r.dzc[256 * im : 256 * im + 256, :])
        if im == 0:
            r.dws[...] = grad
        else:
            r.dws[...] = r.dws[...] + grad

    class GradSum:
        def __init__(self, number, fetch):
            self.fetch = fetch
            for part in PARTS:
                setattr(self, part, getattr(r, part + str(number)))

        def begin(self):
            self.waits = []
            for u in range(4):
                self.s1[u] = self.fetch(2 * u + 1 - core).astype(BF16)
                self.waits.append(
                    post(self.s1.at[u], self.r1.at[u], self.r1.at[u], dev(partner, within, me))
                )

        def settle(self):
            for wait in self.waits:
                wait()

        def across(self, send, got, masks):
            parts = [(h, v) for v in range(2) for h in range(2)] if len(send.shape) == 4 else [(0,), (1,)]
            self.waits = [
                post(send.at[p], got.at[p], got.at[p], dev(flip(block, masks[p[0]]), within, me))
                for p in parts
            ]

        def first(self):
            for u in range(4):
                self.waits[u]()
                self.acc[u] = self.fetch(2 * u + core) + self.r1[u].astype(F32)
            for v in range(2):
                self.s2[0, v] = self.acc[2 * v + 1 - bit_x, :, 0:128].astype(BF16)
                self.s2[1, v] = self.acc[2 * (1 - bit_y) + v, :, 128:256].astype(BF16)
            self.across(self.s2, self.r2, (2, 4))

        def second(self):
            self.settle()
            low = self.acc[2 * (1 - bit_y) + bit_x, :, 0:128] + self.r2[0, 1 - bit_y].astype(F32)
            high = self.acc[2 * bit_y + 1 - bit_x, :, 128:256] + self.r2[1, 1 - bit_x].astype(F32)
            self.s3[0] = low.astype(BF16)
            self.s3[1] = high.astype(BF16)
            self.across(self.s3, self.r3, (4, 2))

        def third(self):
            self.settle()
            low = self.acc[plane, :, 0:128] + self.r2[0, bit_y].astype(F32)
            high = self.acc[plane, :, 128:256] + self.r2[1, bit_x].astype(F32)
            low, high = low + self.r3[0].astype(F32), high + self.r3[1].astype(F32)
            value = jnp.concatenate([low, high], axis=1).astype(BF16)
            left = [value[0:128], value[256 : 256 + tail]]
            right = [value[128:256], value[256 + tail : rows]]
            if value.shape[0] > rows:
                left.append(value[rows : rows + hs])
                right.append(value[rows + hs :])
            pair = jnp.concatenate([stack(left), stack(right)], axis=1)
            packed = nt(pair, r.unpack[...]).astype(BF16)
            for c in range(n_ch):
                self.s4[c] = packed[:, 128 * c : 128 * c + 128]
            self.r4[me] = self.s4[me]
            self.waits = [
                post(self.s4.at[peer], self.r4.at[me], self.r4.at[peer], dev(block, within, peer))
                for peer in ch_peers
            ]

        def end(self, out, out_small=None):
            self.settle()
            done = self.r4[0].astype(F32)
            for c in range(1, n_ch):
                done = done + self.r4[c].astype(F32)
            turned = done[0:128].T
            out[:, 0:128] = turned[0:local]
            out[:, 128:256] = turned[local:]
            gap = jnp.zeros((128 - tail, 128), F32)
            turned = stack([done[128 : 128 + tail], gap]).T
            ends = turned[0:local] + pltpu.roll(turned[local:], tail, axis=1)
            out[:, 256:rows] = ends[:, 0 : rows - 256]
            if out_small is not None:
                last = done[hw:]
                out_small[0:hs, :] = last[:, 0:local]
                out_small[hs:, :] = pltpu.roll(last, local, axis=1)[:, 0:local]

    def block_rows(ref, size, index):
        return ref[pl.ds(pl.multiple_of(size * index, 8), size), :]

    second = GradSum(2, lambda k: stack([block_rows(r.dw2, rows, k), block_rows(r.dws, small, k)]))
    entry = GradSum(1, lambda k: block_rows(r.dw1, rows, k))
    second.begin()
    r.dshort[...] = nt(r.dzc[...], r.ws[...])

    stats = back_sums.end()
    affine_grad2 = stats
    p1_b = [pick_row(stats[0:4], group[im]) / (4.0 * count) for im in range(per)]
    p2_b = [pick_row(stats[4:8], group[im]) / (4.0 * count) for im in range(per)]

    for im in range(per):
        span = slice(256 * im, 256 * im + 256)
        scale = gain * inv2_b[im]
        combos = []
        for a in range(2):
            grads = []
            for c in range(2):
                ph = 2 * a + c
                d = scale * (r.act[ph, span, :] - (p1_b[im] + r.y1[ph, span, :] * p2_b[im]))
                grads.append(d.astype(BF16))
            right = nn(r.shift[0], grads[0])
            left = nn(r.shift[1], grads[1])
            even, odd = grads[0].astype(F32), grads[1].astype(F32)
            combos.append((odd + right, even + odd, left + even))
        gap = jnp.zeros((16, chans), F32)
        if im == 0:
            second.first()
        for dx in range(3):
            upper, lower = combos[0][dx], combos[1][dx]
            r.field[dx, im] = (lower + stack([upper[16:], gap])).astype(BF16)
            r.field[3 + dx, im] = (upper + lower).astype(BF16)
            r.field[6 + dx, im] = (stack([gap, lower[:-16]]) + upper).astype(BF16)

    block_output.forward()

    def grad1(tap, carry):
        first = pl.multiple_of(256 * tap, 256)
        r.dw1[pl.ds(first, 256), :] = nn(
            r.h1cm[...], stack([r.field[tap, im] for im in range(per)])
        )
        return carry

    lax.fori_loop(0, 9, grad1, 0)
    entry.begin()
    second.second()

    parts = [stack([r.field[tap, im] for im in range(per)]) for tap in range(9)]
    dh1 = back_product(parts, r.w1)
    payload = jnp.zeros((32, chans), F32)
    for im in range(per):
        span = slice(256 * im, 256 * im + 256)
        normal = (r.fpm[span, :].astype(F32) - mean1_b[im]) * inv1_b[im]
        pre = gamma_b[im] * normal + beta_b[im]
        sig = sigmoid(pre)
        act = dh1[span] * (sig * (1.0 + pre * (1.0 - sig)))
        r.act1[span, :] = act
        q1, q2 = colsum(act), colsum(act * normal)
        payload = payload + place_row(q2, label[im], 32)
        payload = payload + place_row(q1, label[im] + classes, 32)
        payload = payload + place_row(gamma_b[im] * q1, group[im] + 24, 32)
        payload = payload + place_row(gamma_b[im] * q2, group[im] + 28, 32)
    last_sums = AllReduce(4)
    last_sums.begin(payload)
    entry.first()
    second.third()
    last_sums.middle()
    entry.second()

    stats = last_sums.end()
    for im in range(per):
        span = slice(256 * im, 256 * im + 256)
        normal = (r.fpm[span, :].astype(F32) - mean1_b[im]) * inv1_b[im]
        r1 = pick_row(stats[24:28], group[im]) / count
        r2 = pick_row(stats[28:32], group[im]) / count
        grad = inv1_b[im] * (gamma_b[im] * r.act1[span, :] - (r1 + normal * r2))
        grad = (grad + r.dshort[span, :]).astype(BF16)
        r.dcm[im] = nt(r.ident[...], grad).astype(BF16)
    entry.third()
    input_gradient = give_back(r.dcm, r.dx, r.pass_x)
    second.end(r.grad2, r.grad3)
    input_gradient.forward()

    table = jnp.zeros((24, chans), F32)
    table = table + jnp.where(iota((24, chans), 0) < 2 * classes, stats[0:24], 0.0)
    table = table + place_row(colsum(affine_grad2[4:8]), 2 * classes, 24)
    table = table + place_row(colsum(affine_grad2[0:4]), 2 * classes + 1, 24)
    table = table + place_row(affine_grad2[8:9], 2 * classes + 2, 24)
    mine = jnp.zeros((24, 128), F32)
    for c in range(n_ch):
        piece = table[:, 128 * (c // 2) : 128 * (c // 2) + 128]
        if c % 2:
            piece = pltpu.roll(piece, local, axis=1)
        mine = mine + jnp.where(me == c, piece, 0.0)
    r.affine_grad[...] = mine

    if inner == 1:
        row = iota((8, 128), 0)

        def norm_rows(index, weight, grad, v):
            for wait in held[index]:
                wait()
            master = weight[...]
            _, _, direction = adam_update(
                grad[...], getattr(r, v + "m")[...], getattr(r, v + "q")[...]
            )
            update = direction + WEIGHT_DECAY * master
            rows_w = jnp.where(row == index, total(master * master), 0.0)
            return rows_w + jnp.where(row == index + 3, total(update * update), 0.0)

        norms = norm_rows(1, r.exit_v, r.grad2, "v2") + norm_rows(2, r.bypass_v, r.grad3, "vs")
        entry.end(r.grad1)
        norms = norms + norm_rows(0, r.entry_v, r.grad1, "v1")
        norm_sums = AllReduce(5)
        norm_sums.begin(norms)
        norm_sums.middle()
        r.norms[...] = norm_sums.end()
    else:
        entry.end(r.grad1)
        r.norms[...] = jnp.zeros((8, 128), F32)

    block_output.settle()
    input_gradient.settle()
    for wait in pending:
        wait()
    cfg.used.append((slots.remote, slots.local))


def final_kernel(cfg, *refs):
    r = SimpleNamespace(**dict(zip(cfg.names, refs)))
    classes = cfg.classes
    local = cfg.local
    r.block_output[...] = r.out[...]
    r.input_gradient[...] = r.dx[...].astype(F32)
    norms = jnp.sqrt(r.norms[...])
    weight_norm, update_norm = norms[0:3, 0:1], norms[3:6, 0:1]
    ratio = weight_norm / update_norm
    at = iota((3, 3), 1)
    r.trust_norms[...] = jnp.where(
        at == 0, weight_norm, jnp.where(at == 1, update_norm, ratio)
    )
    sets = (
        (r.entry, r.entry_m, r.entry_q, r.entry_g, r.entry_1, r.entry_2, r.entry_w),
        (r.exit, r.exit_m, r.exit_q, r.exit_g, r.exit_1, r.exit_2, r.exit_w),
        (r.bypass, r.bypass_m, r.bypass_q, r.bypass_g, r.bypass_1, r.bypass_2, r.bypass_w),
    )
    for index, (weight, m, q, g, first, second, result) in enumerate(sets):
        master = weight[...]
        moment, square, direction = adam_update(g[...], m[...], q[...])
        update = direction + WEIGHT_DECAY * master
        first[...] = moment
        second[...] = square
        result[...] = master - MATRIX_RATE * ratio[index : index + 1] * update
    grad = r.affine_grad[0 : 2 * classes + 3, 0:local]
    moment, square, direction = adam_update(grad, r.affine_m[...], r.affine_q[...])
    r.affine_1[...] = moment
    r.affine_2[...] = square
    r.affine_w[...] = r.affine[...] - AFFINE_RATE * direction


def per_device(
    features,
    labels,
    groups,
    widths,
    entry_conv,
    entry_moment,
    entry_square,
    exit_conv,
    exit_moment,
    exit_square,
    bypass_conv,
    bypass_moment,
    bypass_square,
    norm_affine,
    norm_moment,
    norm_square,
    cotangent,
):
    n_img, n_ch = lax.axis_size("img"), lax.axis_size("ch")
    batch, local, pixels = features.shape
    chans = local * n_ch
    side = math.isqrt(pixels)
    inner = n_img // OUTER
    classes = (norm_affine.shape[0] - 3) // 2
    per = batch // n_ch
    assert (side, chans, n_ch, local, batch % n_ch) == (16, 256, 4, 64, 0) and per == 2
    rows, small = entry_conv.shape[0] * inner, bypass_conv.shape[0] * inner
    masters = (entry_conv, exit_conv, bypass_conv)
    if inner == 1:
        blocks = masters
    else:
        sets = [[o * inner + i for i in range(inner)] for o in range(OUTER)]
        blocks = tuple(
            lax.all_gather(w.astype(BF16), "img", axis=0, tiled=True, axis_index_groups=sets)
            for w in masters
        )

    vmem = pl.BlockSpec(memory_space=pltpu.VMEM)
    smem = pl.BlockSpec(memory_space=pltpu.SMEM)
    anywhere = pl.BlockSpec(memory_space=pl.ANY)
    states = dict(
        entry_m=entry_moment.T,
        entry_q=entry_square.T,
        exit_m=exit_moment.T,
        exit_q=exit_square.T,
        bypass_m=bypass_moment,
        bypass_q=bypass_square,
    )
    inputs = dict(
        labels=(labels, smem),
        groups=(groups, smem),
        widths=(widths, smem),
        features=(features, anywhere),
        cotangent=(cotangent, anywhere),
        entry=(blocks[0].T, anywhere),
        exit=(blocks[1].T, anywhere),
        bypass=(blocks[2], anywhere),
        affine=(norm_affine, anywhere),
    )
    if inner == 1:
        inputs.update({name: (value, anywhere) for name, value in states.items()})
    sds = jax.ShapeDtypeStruct
    outputs = dict(
        out=(sds(cotangent.shape, BF16), vmem),
        dx=(sds(features.shape, BF16), vmem),
        grad1=(sds((local, rows), F32), vmem),
        grad2=(sds((local, rows), F32), vmem),
        grad3=(sds((small, local), F32), vmem),
        affine_grad=(sds((24, 128), F32), vmem),
        norms=(sds((8, 128), F32), vmem),
    )
    pix = pixels * per
    taps9 = 9 * chans
    held = lambda shape, dtype=BF16: pltpu.VMEM(shape, dtype)
    scratch = dict(
        fown=held((batch, local, pixels)),
        cown=held((batch, local, 4 * pixels)),
        pass_f=held((2, local, pixels)),
        pass_c=held((2, local, 4 * pixels)),
        pass_o=held((2, local, 4 * pixels)),
        pass_x=held((2, local, pixels)),
        fbuf=held((n_ch, per, local, pixels)),
        cbuf=held((n_ch, per, local, 4 * pixels)),
        entry_v=held((local, rows), blocks[0].dtype),
        exit_v=held((local, rows), blocks[1].dtype),
        bypass_v=held((small, local), blocks[2].dtype),
        affine_v=held(norm_affine.shape, F32),
        padded=held((3 * local, 384)),
        wz1=held((n_ch, rows // 2, 128)),
        wz2=held((n_ch, (rows + small) // 2, 128)),
        aff_z=held((n_ch, 24, 128), F32),
        w1=held((taps9, chans)),
        w2=held((taps9, chans)),
        ws=held((chans, chans)),
        unpack=held((512, 512)),
        ident=held((256, 256)),
        shift=held((2, 256, 256)),
        gridder=held((512, 256)),
        fpm=held((pix, chans)),
        h1s=held((3, per, pixels + 32, chans)),
        h1cm=held((chans, pix)),
        y1=held((4, pix, chans), F32),
        act=held((4, pix, chans), F32),
        h2s=held((2, 4, per, pixels + 32, chans)),
        dzs=held((2, 4, per, pixels + 32, chans)),
        h2cm=held((chans, 4 * pix)),
        short=held((pix, chans), F32),
        dshort=held((pix, chans), F32),
        dzc=held((pix, chans)),
        act1=held((pix, chans), F32),
        rc=held((4, pix, chans)),
        ocm=held((per, chans, 4 * pixels)),
        dcm=held((per, chans, pixels)),
        field=held((9, per, pixels, chans)),
        dw1=held((taps9, chans), F32),
        dw2=held((taps9, chans), F32),
        dws=held((chans, chans), F32),
    )
    for number, size in ((1, rows), (2, rows + small)):
        shapes = ((4, size, chans),) * 2 + ((2, 2, size, 128),) * 2 + ((2, size, 128),) * 2
        shapes += ((n_ch, size // 2, 128),) * 2
        for part, shape in zip(PARTS, shapes):
            scratch[part + str(number)] = held(shape)
        scratch[PARTS[-1] + str(number)] = held((4, size, chans), F32)
    exchanges = [(8, 128), (8, chans), (16, chans), (32, chans)]
    if inner == 1:
        exchanges.append((8, 128))
        for v, shape in (("v1", (local, rows)), ("v2", (local, rows)), ("vs", (small, local))):
            scratch[v + "m"] = held(shape, F32)
            scratch[v + "q"] = held(shape, F32)
    for number, shape in enumerate(exchanges, 1):
        for axis, size in zip("abc", (OUTER, inner, n_ch)):
            if size > 1:
                scratch[axis + str(number)] = held((size,) + shape, F32)
    remote_count = 3 * 3 + 4 * 4 * per + 3 * 7 + 2 * 13 + len(exchanges) * (7 + 3 + inner - 1)
    scratch.update(
        send=pltpu.SemaphoreType.DMA((remote_count,)),
        recv=pltpu.SemaphoreType.DMA((remote_count,)),
        lsem=pltpu.SemaphoreType.DMA((20,)),
    )
    cfg = SimpleNamespace(
        names=[*inputs, *outputs, *scratch],
        inner=inner,
        n_ch=n_ch,
        batch=batch,
        local=local,
        classes=classes,
        count=float(batch * n_img // widths.shape[0] * pixels),
        rows=rows,
        small=small,
        used=[],
    )
    out, dx, grad1, grad2, grad3, affine_grad, norms = pl.pallas_call(
        functools.partial(main_kernel, cfg),
        out_shape=[s for s, _ in outputs.values()],
        in_specs=[s for _, s in inputs.values()],
        out_specs=[s for _, s in outputs.values()],
        scratch_shapes=list(scratch.values()),
        compiler_params=pltpu.CompilerParams(
            collective_id=0, has_side_effects=True, vmem_limit_bytes=VMEM_LIMIT
        ),
        name="block_step",
    )(*[v for v, _ in inputs.values()])
    assert max(n for n, _ in cfg.used) <= remote_count and max(n for _, n in cfg.used) <= 20

    grads = [grad1, grad2, grad3]
    if inner > 1:
        grads = [
            lax.psum_scatter(g, "img", scatter_dimension=0, axis_index_groups=sets, tiled=True)
            for g in (grad1.T, grad2.T, grad3)
        ]
        updates = []
        for w, g, m, s in zip(
            masters,
            grads,
            (entry_moment, exit_moment, bypass_moment),
            (entry_square, exit_square, bypass_square),
        ):
            updates.append(adam_update(g, m, s)[2] + WEIGHT_DECAY * w)
        sums = lax.psum(
            jnp.stack([jnp.sum(w * w) for w in masters] + [jnp.sum(u * u) for u in updates]),
            ("img", "ch"),
        )
        norms = jnp.broadcast_to(jnp.pad(sums, (0, 2))[:, None], (8, 128))
        grads = [grads[0].T, grads[1].T, grads[2]]

    args = dict(
        out=out,
        dx=dx,
        norms=norms,
        affine_grad=affine_grad,
        entry_g=grads[0],
        exit_g=grads[1],
        bypass_g=grads[2],
        entry=entry_conv.T,
        exit=exit_conv.T,
        bypass=bypass_conv,
        **states,
        affine=norm_affine,
        affine_m=norm_moment,
        affine_q=norm_square,
    )
    tall = sds(entry_conv.shape[::-1], F32)
    short, wide = (sds(w.shape, F32) for w in (bypass_conv, norm_affine))
    results = dict(
        block_output=sds(cotangent.shape, BF16),
        input_gradient=sds(features.shape, F32),
        entry_1=tall,
        entry_2=tall,
        entry_w=tall,
        exit_1=tall,
        exit_2=tall,
        exit_w=tall,
        bypass_1=short,
        bypass_2=short,
        bypass_w=short,
        affine_1=wide,
        affine_2=wide,
        affine_w=wide,
        trust_norms=sds((3, 3), F32),
    )
    end_cfg = SimpleNamespace(names=[*args, *results], classes=classes, local=local)
    final = pl.pallas_call(
        functools.partial(final_kernel, end_cfg),
        out_shape=list(results.values()),
        in_specs=[vmem] * len(args),
        out_specs=[vmem] * len(results),
        compiler_params=pltpu.CompilerParams(vmem_limit_bytes=VMEM_LIMIT),
        name="finish",
    )(*args.values())
    return tuple(v.T if s is tall else v for v, s in zip(final, results.values()))


def solution(mesh):
    wide = P("img", "ch")
    deep = P("img", "ch", None)
    table = P(None, "ch")
    return jax.shard_map(
        per_device,
        mesh=mesh,
        in_specs=(deep, P("img"), P("img"), P()) + (wide,) * 9 + (table,) * 3 + (deep,),
        out_specs=(deep, deep) + (wide,) * 9 + (table,) * 3 + (P(),),
        check_vma=False,
    )
```

```python
import functools
import math
from types import SimpleNamespace

import jax
import jax.numpy as jnp
from jax import lax
from jax.experimental import pallas as pl
from jax.experimental.pallas import tpu as pltpu
from jax.sharding import PartitionSpec as P

LEVELS = 4
STEP = 5
NORM_EPSILON = 1e-05
ADAM_EPSILON = 1e-06
MOMENT_DECAY = 0.9
SQUARE_DECAY = 0.999
WEIGHT_DECAY = 0.01
MATRIX_RATE = 0.3
AFFINE_RATE = 0.2

OUTER = 8
VMEM_LIMIT = 56 * 1024 * 1024
BF16 = jnp.bfloat16
F32 = jnp.float32
MESH = pl.DeviceIdType.MESH
PARTS = ("s1", "r1", "s2", "r2", "s3", "r3", "s4", "r4", "acc")


def nn(left, right):
    return lax.dot_general(left, right, (((1,), (0,)), ((), ())), preferred_element_type=F32)


def nt(left, right):
    return lax.dot_general(left, right, (((1,), (1,)), ((), ())), preferred_element_type=F32)


def tn(left, right):
    return lax.dot_general(left, right, (((0,), (0,)), ((), ())), preferred_element_type=F32)


def flip(index, mask):
    result = index
    for bit in range(3):
        if (mask >> bit) & 1:
            digit = lax.rem(lax.div(index, 1 << bit), 2)
            result = result + (1 - 2 * digit) * (1 << bit)
    return result


def sigmoid(value):
    return 0.5 * jnp.tanh(0.5 * value) + 0.5


def iota(shape, axis):
    return lax.broadcasted_iota(jnp.int32, shape, axis)


def to_bf16(condition):
    return jnp.where(condition, 1.0, 0.0).astype(BF16)


def pick_row(table, index):
    hit = iota(table.shape, 0) == index
    return jnp.sum(jnp.where(hit, table, 0.0), axis=0, keepdims=True)


def place_row(row, index, rows):
    hit = iota((rows, row.shape[1]), 0) == index
    return jnp.where(hit, row, 0.0)


def colsum(value):
    return jnp.sum(value, axis=0, keepdims=True)


def adam_update(grad, moment, square):
    moment_new = MOMENT_DECAY * moment + (1.0 - MOMENT_DECAY) * grad
    square_new = SQUARE_DECAY * square + (1.0 - SQUARE_DECAY) * grad * grad
    direction = (
        moment_new
        / (1.0 - MOMENT_DECAY**STEP)
        / (jnp.sqrt(square_new / (1.0 - SQUARE_DECAY**STEP)) + ADAM_EPSILON)
    )
    return (moment_new, square_new, direction)


def total(value):
    return jnp.sum(jnp.sum(value, axis=1, keepdims=True), axis=0, keepdims=True)


def main_kernel(cfg, *refs):
    r = SimpleNamespace(**dict(zip(cfg.names, refs)))
    inner, n_ch, batch, local = cfg.inner, cfg.n_ch, cfg.batch, cfg.local
    classes, count = cfg.classes, cfg.count
    per = batch // n_ch
    chans = local * n_ch
    rows, small = cfg.rows, cfg.small
    tail = (rows - 256) // 2
    hw, hs = rows // 2, small // 2
    slots = SimpleNamespace(remote=0, local=0)

    img = lax.axis_index("img")
    me = lax.axis_index("ch")
    block = lax.div(img, inner)
    within = lax.rem(img, inner)
    core = lax.rem(block, 2)
    plane = lax.div(block, 2)
    bit_x, bit_y = lax.rem(plane, 2), lax.div(plane, 2)
    partner = flip(block, 1)

    def dev(block_id, within_id, ch_id):
        return (block_id * inner + within_id, ch_id)

    pending = []

    def post(src, dst, landed, peer):
        slot = slots.remote
        slots.remote = slot + 1
        copy = pltpu.make_async_remote_copy(
            src_ref=src,
            dst_ref=dst,
            send_sem=r.send.at[slot],
            recv_sem=r.recv.at[slot],
            device_id=peer,
            device_id_type=MESH,
        )
        copy.start()
        pending.append(copy.wait_send)
        arrival = pltpu.make_async_remote_copy(
            src_ref=landed,
            dst_ref=landed,
            send_sem=r.send.at[slot],
            recv_sem=r.recv.at[slot],
            device_id=peer,
            device_id_type=MESH,
        )
        return arrival.wait_recv

    def here(src, dst):
        slot = slots.local
        slots.local = slot + 1
        copy = pltpu.make_async_copy(src, dst, r.lsem.at[slot])
        copy.start()
        return copy.wait

    outer_peers = [flip(block, mask) for mask in range(1, OUTER)]
    ch_peers = [flip(me, mask) for mask in range(1, n_ch)]
    inner_pairs = [
        (lax.rem(within + step, inner), lax.rem(within + inner - step, inner))
        for step in range(1, inner)
    ]
    up, down, far = (lax.rem(me + step, n_ch) for step in (1, 3, 2))
    up_peer, down_peer = dev(block, within, up), dev(block, within, down)

    class Ring:
        def __init__(self, source, target, passing):
            self.target, self.passing = target, passing
            self.waits = []
            self.early = [
                post(source(far, 0), passing.at[0], passing.at[0], up_peer),
                post(source(far, 1), passing.at[1], passing.at[1], down_peer),
            ]
            for im in range(per):
                self.waits += [
                    post(source(up, im), target(me, im), target(down, im), up_peer),
                    post(source(down, im), target(me, im), target(up, im), down_peer),
                ]

        def forward(self):
            self.early[0]()
            self.waits.append(
                post(self.passing.at[0], self.target(down, 0), self.target(far, 0), up_peer)
            )
            self.early[1]()
            self.waits.append(
                post(self.passing.at[1], self.target(up, 1), self.target(far, 1), down_peer)
            )

        def settle(self):
            for wait in self.waits:
                wait()

    barrier = pltpu.get_barrier_semaphore()
    everyone = [dev(peer, within, me) for peer in outer_peers]
    everyone += [dev(block, within, peer) for peer in ch_peers]
    everyone += [dev(block, peer, me) for peer, _ in inner_pairs]
    for peer in everyone:
        pl.semaphore_signal(barrier, inc=1, device_id=peer, device_id_type=MESH)

    got_entry = here(r.entry, r.entry_v)
    got_features = here(r.features, r.fown)
    got_exit = here(r.exit, r.exit_v)
    got_bypass = here(r.bypass, r.bypass_v)
    got_affine = here(r.affine, r.affine_v)
    got_cot = here(r.cotangent, r.cown)
    states = ((r.entry_m, r.entry_q), (r.exit_m, r.exit_q), (r.bypass_m, r.bypass_q)) if inner == 1 else ()
    held = [
        (here(m, getattr(r, v + "m")), here(q, getattr(r, v + "q")))
        for (m, q), v in zip(states, ("v1", "v2", "vs"))
    ]

    s_row, s_col = iota((hw, 384), 0), iota((hw, 384), 1)
    pick_first = to_bf16(s_col == jnp.where(s_row < 128, s_row, s_row + 128))
    pick_second = to_bf16(s_col == jnp.where(s_row < 128, s_row + 128, s_row + 128 + tail))
    r.padded[...] = jnp.zeros(r.padded.shape, BF16)

    def pack_own(value):
        r.padded[local : 2 * local, 0:rows] = value.astype(BF16)
        packed = nt(pick_first, r.padded[local : 3 * local, :])
        return (packed + nt(pick_second, r.padded[0 : 2 * local, :])).astype(BF16)

    got_entry()
    r.wz1[me] = pack_own(r.entry_v[...])
    pl.semaphore_wait(barrier, len(everyone))

    def to_channels(buffer):
        return [
            post(buffer.at[me], buffer.at[me], buffer.at[peer], dev(block, within, peer))
            for peer in ch_peers
        ]

    entry_waits = to_channels(r.wz1)
    got_features()
    feature_waits = [
        post(
            r.fown.at[pl.ds(per * peer, per)],
            r.fbuf.at[me],
            r.fbuf.at[peer],
            dev(block, within, peer),
        )
        for peer in ch_peers
    ]
    r.fbuf[me] = r.fown[pl.ds(per * me, per)]
    flat = jnp.concatenate([r.fown[b] for b in range(batch)], axis=1)
    wide = flat.astype(F32)
    square = wide * wide
    square_hi = square.astype(BF16)
    square_lo = (square - square_hi.astype(F32)).astype(BF16)
    level = iota((16, 256), 0)
    first_mask = jnp.concatenate([to_bf16(level == r.groups[b]) for b in range(batch)], axis=1)
    second_mask = jnp.concatenate([to_bf16(level == r.groups[b] + 4) for b in range(batch)], axis=1)
    sums = nt(first_mask, flat) + nt(second_mask, square_hi) + nt(second_mask, square_lo)

    got_affine()
    r.aff_z[me] = jnp.zeros((32, 128), F32)
    r.aff_z[me, 0 : 2 * classes + 3, 0:local] = r.affine_v[...]
    r.aff_z[me, 24:32, 0:local] = sums[0:8]
    affine_waits = to_channels(r.aff_z)

    got_exit()
    got_bypass()
    r.wz2[me, 0:hw, :] = pack_own(r.exit_v[...])
    e_row, e_col = iota((local, 128), 0), iota((local, 128), 1)
    value = r.bypass_v[...].astype(BF16)
    r.wz2[me, hw : hw + hs, :] = (
        nn(value[:hs], to_bf16(e_col == e_row)) + nn(value[hs:], to_bf16(e_col == e_row + local))
    ).astype(BF16)

    exit_waits = to_channels(r.wz2)
    got_cot()
    cotangent = Ring(
        lambda c, im: r.cown.at[per * c + im], lambda c, im: r.cbuf.at[c, im], r.pass_c
    )

    lane = iota((512, 512), 0)
    column = iota((512, 512), 1)
    spot = 256 * ((lane >> 6) & 1) + 64 * (lane >> 7) + (lane & 63)
    r.unpack[...] = to_bf16(column == spot)

    def ordered_sum(ref, size):
        result = ref[0]
        for slot in range(1, size):
            result = result + ref[slot]
        return result

    class AllReduce:
        def __init__(self, number):
            self.over_outer, self.over_inner, self.over_ch = (
                getattr(r, axis + str(number), None) for axis in "abc"
            )

        def begin(self, value):
            ref = self.over_outer
            ref[block] = value
            self.waits = [
                post(ref.at[block], ref.at[block], ref.at[peer], dev(peer, within, me))
                for peer in outer_peers
            ]

        def plane(self):
            for wait in self.waits:
                wait()
            value = ordered_sum(self.over_outer, OUTER)
            if inner > 1:
                ref = self.over_inner
                ref[within] = value
                waits = [
                    post(ref.at[within], ref.at[within], ref.at[back], dev(block, peer, me))
                    for peer, back in inner_pairs
                ]
                for wait in waits:
                    wait()
                value = ordered_sum(ref, inner)
            return value

        def middle(self):
            self.over_ch[me] = self.plane()
            self.waits = to_channels(self.over_ch)

        def end(self):
            for wait in self.waits:
                wait()
            return ordered_sum(self.over_ch, n_ch)

    def rows_of(ref, index):
        size = ref.shape[0] // OUTER
        return ref.at[pl.ds(pl.multiple_of(size * index, 16), size)]

    def unpack_own(ref, full):
        own = rows_of(ref, block)
        if full.shape[0] == hw:
            own[0:128, :] = full[0:128, 0:256]
            own[128:256, :] = full[0:128, 256:512]
            own[256 : 256 + tail, :] = full[128:, 0:256]
            own[256 + tail :, :] = full[128:, 256:512]
        else:
            own[0:hs, :] = full[:, 0:256]
            own[hs:, :] = full[:, 256:512]

    def spread(ref):
        own = rows_of(ref, block)
        return {
            mask: post(own, own, rows_of(ref, flip(block, mask)), dev(flip(block, mask), within, me))
            for mask in (2, 4, 6, 1)
        }

    def forward(ref, waits):
        rest = [waits[1]]
        for mask in (2, 4, 6):
            waits[mask]()
            mine = rows_of(ref, flip(block, mask))
            theirs = rows_of(ref, flip(partner, mask))
            rest.append(post(mine, mine, theirs, dev(partner, within, me)))
        return rest

    def widen(buffer):
        packed = jnp.concatenate([buffer[c] for c in range(n_ch)], axis=1)
        return nn(packed, r.unpack[...]).astype(BF16)

    def wide_lanes(ref):
        parts = [
            ref[c] + pltpu.roll(ref[c + 1], local, axis=1) for c in range(0, n_ch, 2)
        ]
        return jnp.concatenate(parts, axis=1)

    for wait in affine_waits:
        wait()
    affine = wide_lanes(r.aff_z)
    input_sums = AllReduce(1)
    input_sums.begin(affine[24:32])
    for wait in entry_waits:
        wait()
    unpack_own(r.w1, widen(r.wz1))
    gather1 = spread(r.w1)

    ident = to_bf16(iota((256, 256), 0) == iota((256, 256), 1))
    r.ident[...] = ident
    q_out, q_in = iota((256, 256), 0), iota((256, 256), 1)
    r.shift[0] = to_bf16((q_in == q_out + 1) & ((q_out & 15) < 15))
    r.shift[1] = to_bf16((q_in == q_out - 1) & ((q_out & 15) > 0))

    rho, px = iota((512, 256), 0), iota((512, 256), 1)
    version, a, b_ = rho >> 8, (rho >> 7) & 1, (rho >> 6) & 1
    col = (rho & 15) + version * (1 - 2 * b_)
    target = (2 * ((rho & 63) >> 4) + a) * 32 + 2 * col + b_
    r.gridder[...] = to_bf16((px == target) & (col >= 0) & (col < 16))
    zeros = jnp.zeros((16, 256), BF16)
    for im in range(per):
        for ver in range(3):
            r.h1s[ver, im, 0:16, :] = zeros
            r.h1s[ver, im, 272:288, :] = zeros
        for ver in range(2):
            for ph in range(4):
                for ref in (r.h2s, r.dzs):
                    ref[ver, ph, im, 0:16, :] = zeros
                    ref[ver, ph, im, 272:288, :] = zeros

    def channel_major(ref, im, lanes):
        return jnp.concatenate([ref[c, im, :, lanes] for c in range(n_ch)], axis=0)

    for wait in feature_waits:
        wait()
    for im in range(per):
        r.fpm[256 * im : 256 * im + 256, :] = nt(
            ident, channel_major(r.fbuf, im, slice(0, 256))
        ).astype(BF16)

    stats = input_sums.plane()
    mean1 = stats[0:4] / count
    inv1 = lax.rsqrt(stats[4:8] / count - mean1 * mean1 + NORM_EPSILON)
    gain = affine[2 * classes : 2 * classes + 1]
    shift = affine[2 * classes + 1 : 2 * classes + 2]
    out_bias = affine[2 * classes + 2 : 2 * classes + 3]
    group, label, mean1_b, inv1_b, gamma_b, beta_b, mask_b = [], [], [], [], [], [], []
    for im in range(per):
        group.append(r.groups[per * me + im])
        label.append(r.labels[per * me + im])
        mean1_b.append(pick_row(mean1, group[im]))
        inv1_b.append(pick_row(inv1, group[im]))
        gamma_b.append(pick_row(affine, label[im]))
        beta_b.append(pick_row(affine, label[im] + classes))
        width = r.widths[group[im]]
        mask_b.append(
            jnp.where(iota((1, chans), 1) < width * (chans // LEVELS), 1.0, 0.0)
        )

    for im in range(per):
        normal = (r.fpm[256 * im : 256 * im + 256, :].astype(F32) - mean1_b[im]) * inv1_b[im]
        pre = gamma_b[im] * normal + beta_b[im]
        hidden = (pre * sigmoid(pre)).astype(BF16)
        r.h1s[1, im, 16:272, :] = hidden
        r.h1s[0, im, 16:272, :] = nn(r.shift[1], hidden).astype(BF16)
        r.h1s[2, im, 16:272, :] = nn(r.shift[0], hidden).astype(BF16)
        r.h1cm[:, 256 * im : 256 * im + 256] = nt(ident, hidden).astype(BF16)

    for wait in exit_waits:
        wait()
    full = widen(r.wz2)
    unpack_own(r.w2, full[0:hw])
    unpack_own(r.ws, full[hw:])
    rest = forward(r.w1, gather1)
    gather2 = spread(r.w2)
    gather3 = spread(r.ws)
    cotangent.forward()
    for wait in rest:
        wait()

    def back_product(parts, ref):
        result = nt(parts[0], ref[0:256, :])
        for tap in range(1, 9):
            result = result + nt(parts[tap], ref[256 * tap : 256 * tap + 256, :])
        return result

    def taps():
        return [(dy, dx) for dy in range(3) for dx in range(3)]

    def stack(pieces):
        return jnp.concatenate(pieces, axis=0)

    def conv1(phase, carry):
        a, c = lax.div(phase, 2), lax.rem(phase, 2)
        parts = []
        for dy, dx in taps():
            first = pl.multiple_of(16 * lax.div(a + dy + 1, 2), 16)
            ver = lax.div(c + dx + 1, 2)
            parts.append(
                stack([r.h1s[ver, im, pl.ds(first, 256), :] for im in range(per)])
            )
        y = nn(jnp.concatenate(parts, axis=1), r.w1[...])
        r.y1[phase] = y
        out = []
        for im in range(per):
            piece = y[256 * im : 256 * im + 256]
            out.append(carry[2 * im] + colsum(piece))
            out.append(carry[2 * im + 1] + colsum(piece * piece))
        return tuple(out)

    nought = jnp.zeros((1, chans), F32)
    mid = lax.fori_loop(0, 4, conv1, (nought,) * (2 * per))
    payload = jnp.zeros((8, chans), F32)
    for im in range(per):
        payload = payload + place_row(mid[2 * im], group[im], 8)
        payload = payload + place_row(mid[2 * im + 1], group[im] + 4, 8)
    mid_sums = AllReduce(2)
    mid_sums.begin(payload)

    rest = forward(r.w2, gather2) + forward(r.ws, gather3)
    mid_sums.middle()

    r.cbuf[me] = r.cown[pl.ds(per * me, per)]
    cotangent.settle()
    for im in range(per):
        for n in range(4):
            piece = channel_major(r.cbuf, im, slice(256 * n, 256 * n + 256))
            grid = nt(r.gridder[...], piece).astype(BF16)
            for ver in range(2):
                for ph in range(4):
                    at = 256 * ver + 64 * ph
                    r.dzs[ver, ph, im, 16 + 64 * n : 80 + 64 * n, :] = grid[at : at + 64]

    coarse = jnp.zeros((256 * per, chans), F32)
    for ph in range(4):
        coarse = coarse + stack([r.dzs[0, ph, im, 16:272, :] for im in range(per)]).astype(F32)
    bias_sum = colsum(coarse)
    r.dzc[...] = coarse.astype(BF16)

    def tap_slice(ref, a, c, dy, dx, im):
        row, colm = a + dy + 1, c + dx + 1
        first = pl.multiple_of(16 * lax.div(row, 2), 16)
        ph = 2 * lax.rem(row, 2) + lax.rem(colm, 2)
        side_step = lax.div(colm, 2) - 1
        return ref[side_step * side_step, ph, im, pl.ds(first, 256), :]

    for wait in rest:
        wait()

    def back2(phase, carry):
        a, c = lax.div(phase, 2), lax.rem(phase, 2)
        parts = [
            stack([tap_slice(r.dzs, a, c, 2 - dy, 2 - dx, im) for im in range(per)])
            for dy, dx in taps()
        ]
        r.act[phase] = back_product(parts, r.w2)
        return carry

    lax.fori_loop(0, 4, back2, 0)

    stats = mid_sums.end()
    mean2 = stats[0:4] / (4.0 * count)
    inv2 = lax.rsqrt(stats[4:8] / (4.0 * count) - mean2 * mean2 + NORM_EPSILON)
    mean2_b = [pick_row(mean2, group[im]) for im in range(per)]
    inv2_b = [pick_row(inv2, group[im]) for im in range(per)]

    def hidden2(phase, carry):
        c = lax.rem(phase, 2)
        out = []
        for im in range(per):
            span = slice(256 * im, 256 * im + 256)
            normal = (r.y1[phase, span, :] - mean2_b[im]) * inv2_b[im]
            r.y1[phase, span, :] = normal
            pre = gain * normal + shift
            sig = sigmoid(pre)
            hidden = (pre * sig * mask_b[im]).astype(BF16)
            act = r.act[phase, span, :] * (sig * (1.0 + pre * (1.0 - sig)) * mask_b[im])
            r.act[phase, span, :] = act
            out.append(carry[2 * im] + colsum(act))
            out.append(carry[2 * im + 1] + colsum(act * normal))
            r.h2s[0, phase, im, 16:272, :] = hidden
            r.h2s[1, phase, im, 16:272, :] = nn(r.shift[c], hidden).astype(BF16)
            lanes = pl.ds(pl.multiple_of(512 * phase + 256 * im, 256), 256)
            r.h2cm[:, lanes] = nt(r.ident[...], hidden).astype(BF16)
        return tuple(out)

    mid = lax.fori_loop(0, 4, hidden2, (nought,) * (2 * per))
    payload = place_row(bias_sum, 8, 16)
    for im in range(per):
        payload = payload + place_row(mid[2 * im], group[im], 16)
        payload = payload + place_row(mid[2 * im + 1], group[im] + 4, 16)
    back_sums = AllReduce(3)
    back_sums.begin(payload)

    r.short[...] = nn(r.fpm[...], r.ws[...]) + out_bias
    def conv2(phase, carry):
        a, c = lax.div(phase, 2), lax.rem(phase, 2)
        parts = [
            stack([tap_slice(r.h2s, a, c, dy, dx, im) for im in range(per)]) for dy, dx in taps()
        ]
        y = nn(jnp.concatenate(parts, axis=1), r.w2[...]) + r.short[...]
        r.rc[phase] = y.astype(BF16)
        return carry

    lax.fori_loop(0, 4, conv2, 0)
    for im in range(per):
        for n in range(4):
            first = 256 * im + 64 * n
            piece = stack([r.rc[ph, first : first + 64, :] for ph in range(4)])
            r.ocm[im, :, 256 * n : 256 * n + 256] = tn(piece, r.gridder[0:256, :]).astype(BF16)

    def own_channels(ref, index, im):
        return ref.at[im, pl.ds(pl.multiple_of(local * index, local), local), :]

    def give_back(ref, out, passing):
        for im in range(per):
            out[per * me + im] = own_channels(ref, me, im)[...]
        return Ring(
            lambda c, im: own_channels(ref, c, im), lambda c, im: out.at[per * c + im], passing
        )

    back_sums.middle()
    block_output = give_back(r.ocm, r.out, r.pass_o)

    def grad2(tap, carry):
        dy, dx = lax.div(tap, 3), lax.rem(tap, 3)
        pieces = []
        for ph in range(4):
            a, c = ph // 2, ph % 2
            for im in range(per):
                pieces.append(tap_slice(r.dzs, a, c, 2 - dy, 2 - dx, im))
        first = pl.multiple_of(256 * tap, 256)
        r.dw2[pl.ds(first, 256), :] = nn(r.h2cm[...], stack(pieces))
        return carry

    lax.fori_loop(0, 9, grad2, 0)
    for im in range(per):
        piece = channel_major(r.fbuf, im, slice(0, 256))
        grad = nn(piece, r.dzc[256 * im : 256 * im + 256, :])
        if im == 0:
            r.dws[...] = grad
        else:
            r.dws[...] = r.dws[...] + grad

    class GradSum:
        def __init__(self, number, fetch):
            self.fetch = fetch
            for part in PARTS:
                setattr(self, part, getattr(r, part + str(number)))

        def begin(self):
            self.waits = []
            for u in range(4):
                self.s1[u] = self.fetch(2 * u + 1 - core).astype(BF16)
                self.waits.append(
                    post(self.s1.at[u], self.r1.at[u], self.r1.at[u], dev(partner, within, me))
                )

        def settle(self):
            for wait in self.waits:
                wait()

        def across(self, send, got, masks):
            parts = [(h, v) for v in range(2) for h in range(2)] if len(send.shape) == 4 else [(0,), (1,)]
            self.waits = [
                post(send.at[p], got.at[p], got.at[p], dev(flip(block, masks[p[0]]), within, me))
                for p in parts
            ]

        def first(self):
            for u in range(4):
                self.waits[u]()
                self.acc[u] = self.fetch(2 * u + core) + self.r1[u].astype(F32)
            for v in range(2):
                self.s2[0, v] = self.acc[2 * v + 1 - bit_x, :, 0:128].astype(BF16)
                self.s2[1, v] = self.acc[2 * (1 - bit_y) + v, :, 128:256].astype(BF16)
            self.across(self.s2, self.r2, (2, 4))

        def second(self):
            self.settle()
            low = self.acc[2 * (1 - bit_y) + bit_x, :, 0:128] + self.r2[0, 1 - bit_y].astype(F32)
            high = self.acc[2 * bit_y + 1 - bit_x, :, 128:256] + self.r2[1, 1 - bit_x].astype(F32)
            self.s3[0] = low.astype(BF16)
            self.s3[1] = high.astype(BF16)
            self.across(self.s3, self.r3, (4, 2))

        def third(self):
            self.settle()
            low = self.acc[plane, :, 0:128] + self.r2[0, bit_y].astype(F32)
            high = self.acc[plane, :, 128:256] + self.r2[1, bit_x].astype(F32)
            low, high = low + self.r3[0].astype(F32), high + self.r3[1].astype(F32)
            value = jnp.concatenate([low, high], axis=1).astype(BF16)
            left = [value[0:128], value[256 : 256 + tail]]
            right = [value[128:256], value[256 + tail : rows]]
            if value.shape[0] > rows:
                left.append(value[rows : rows + hs])
                right.append(value[rows + hs :])
            pair = jnp.concatenate([stack(left), stack(right)], axis=1)
            packed = nt(pair, r.unpack[...]).astype(BF16)
            for c in range(n_ch):
                self.s4[c] = packed[:, 128 * c : 128 * c + 128]
            self.r4[me] = self.s4[me]
            self.waits = [
                post(self.s4.at[peer], self.r4.at[me], self.r4.at[peer], dev(block, within, peer))
                for peer in ch_peers
            ]

        def end(self, out, out_small=None):
            self.settle()
            done = self.r4[0].astype(F32)
            for c in range(1, n_ch):
                done = done + self.r4[c].astype(F32)
            turned = done[0:128].T
            out[:, 0:128] = turned[0:local]
            out[:, 128:256] = turned[local:]
            gap = jnp.zeros((128 - tail, 128), F32)
            turned = stack([done[128 : 128 + tail], gap]).T
            ends = turned[0:local] + pltpu.roll(turned[local:], tail, axis=1)
            out[:, 256:rows] = ends[:, 0 : rows - 256]
            if out_small is not None:
                last = done[hw:]
                out_small[0:hs, :] = last[:, 0:local]
                out_small[hs:, :] = pltpu.roll(last, local, axis=1)[:, 0:local]

    def block_rows(ref, size, index):
        return ref[pl.ds(pl.multiple_of(size * index, 8), size), :]

    second = GradSum(2, lambda k: stack([block_rows(r.dw2, rows, k), block_rows(r.dws, small, k)]))
    entry = GradSum(1, lambda k: block_rows(r.dw1, rows, k))
    second.begin()
    r.dshort[...] = nt(r.dzc[...], r.ws[...])

    stats = back_sums.end()
    affine_grad2 = stats
    p1_b = [pick_row(stats[0:4], group[im]) / (4.0 * count) for im in range(per)]
    p2_b = [pick_row(stats[4:8], group[im]) / (4.0 * count) for im in range(per)]

    for im in range(per):
        span = slice(256 * im, 256 * im + 256)
        scale = gain * inv2_b[im]
        combos = []
        for a in range(2):
            grads = []
            for c in range(2):
                ph = 2 * a + c
                d = scale * (r.act[ph, span, :] - (p1_b[im] + r.y1[ph, span, :] * p2_b[im]))
                grads.append(d.astype(BF16))
            right = nn(r.shift[0], grads[0])
            left = nn(r.shift[1], grads[1])
            even, odd = grads[0].astype(F32), grads[1].astype(F32)
            combos.append((odd + right, even + odd, left + even))
        gap = jnp.zeros((16, chans), F32)
        if im == 0:
            second.first()
        for dx in range(3):
            upper, lower = combos[0][dx], combos[1][dx]
            r.field[dx, im] = (lower + stack([upper[16:], gap])).astype(BF16)
            r.field[3 + dx, im] = (upper + lower).astype(BF16)
            r.field[6 + dx, im] = (stack([gap, lower[:-16]]) + upper).astype(BF16)

    block_output.forward()

    def grad1(tap, carry):
        first = pl.multiple_of(256 * tap, 256)
        r.dw1[pl.ds(first, 256), :] = nn(
            r.h1cm[...], stack([r.field[tap, im] for im in range(per)])
        )
        return carry

    lax.fori_loop(0, 9, grad1, 0)
    entry.begin()
    second.second()

    parts = [stack([r.field[tap, im] for im in range(per)]) for tap in range(9)]
    dh1 = back_product(parts, r.w1)
    payload = jnp.zeros((32, chans), F32)
    for im in range(per):
        span = slice(256 * im, 256 * im + 256)
        normal = (r.fpm[span, :].astype(F32) - mean1_b[im]) * inv1_b[im]
        pre = gamma_b[im] * normal + beta_b[im]
        sig = sigmoid(pre)
        act = dh1[span] * (sig * (1.0 + pre * (1.0 - sig)))
        r.act1[span, :] = act
        q1, q2 = colsum(act), colsum(act * normal)
        payload = payload + place_row(q2, label[im], 32)
        payload = payload + place_row(q1, label[im] + classes, 32)
        payload = payload + place_row(gamma_b[im] * q1, group[im] + 24, 32)
        payload = payload + place_row(gamma_b[im] * q2, group[im] + 28, 32)
    last_sums = AllReduce(4)
    last_sums.begin(payload)
    entry.first()
    second.third()
    last_sums.middle()
    entry.second()

    stats = last_sums.end()
    for im in range(per):
        span = slice(256 * im, 256 * im + 256)
        normal = (r.fpm[span, :].astype(F32) - mean1_b[im]) * inv1_b[im]
        r1 = pick_row(stats[24:28], group[im]) / count
        r2 = pick_row(stats[28:32], group[im]) / count
        grad = inv1_b[im] * (gamma_b[im] * r.act1[span, :] - (r1 + normal * r2))
        grad = (grad + r.dshort[span, :]).astype(BF16)
        r.dcm[im] = nt(r.ident[...], grad).astype(BF16)
    entry.third()
    input_gradient = give_back(r.dcm, r.dx, r.pass_x)
    second.end(r.grad2, r.grad3)
    input_gradient.forward()

    table = jnp.zeros((24, chans), F32)
    table = table + jnp.where(iota((24, chans), 0) < 2 * classes, stats[0:24], 0.0)
    table = table + place_row(colsum(affine_grad2[4:8]), 2 * classes, 24)
    table = table + place_row(colsum(affine_grad2[0:4]), 2 * classes + 1, 24)
    table = table + place_row(affine_grad2[8:9], 2 * classes + 2, 24)
    mine = jnp.zeros((24, 128), F32)
    for c in range(n_ch):
        piece = table[:, 128 * (c // 2) : 128 * (c // 2) + 128]
        if c % 2:
            piece = pltpu.roll(piece, local, axis=1)
        mine = mine + jnp.where(me == c, piece, 0.0)
    r.affine_grad[...] = mine

    if inner == 1:
        row = iota((8, 128), 0)

        def norm_rows(index, weight, grad, v):
            for wait in held[index]:
                wait()
            master = weight[...]
            _, _, direction = adam_update(
                grad[...], getattr(r, v + "m")[...], getattr(r, v + "q")[...]
            )
            update = direction + WEIGHT_DECAY * master
            rows_w = jnp.where(row == index, total(master * master), 0.0)
            return rows_w + jnp.where(row == index + 3, total(update * update), 0.0)

        norms = norm_rows(1, r.exit_v, r.grad2, "v2") + norm_rows(2, r.bypass_v, r.grad3, "vs")
        entry.end(r.grad1)
        norms = norms + norm_rows(0, r.entry_v, r.grad1, "v1")
        norm_sums = AllReduce(5)
        norm_sums.begin(norms)
        norm_sums.middle()
        r.norms[...] = norm_sums.end()
    else:
        entry.end(r.grad1)
        r.norms[...] = jnp.zeros((8, 128), F32)

    block_output.settle()
    input_gradient.settle()
    for wait in pending:
        wait()
    cfg.used.append((slots.remote, slots.local))


def final_kernel(cfg, *refs):
    r = SimpleNamespace(**dict(zip(cfg.names, refs)))
    classes = cfg.classes
    local = cfg.local
    r.block_output[...] = r.out[...]
    r.input_gradient[...] = r.dx[...].astype(F32)
    norms = jnp.sqrt(r.norms[...])
    weight_norm, update_norm = norms[0:3, 0:1], norms[3:6, 0:1]
    ratio = weight_norm / update_norm
    at = iota((3, 3), 1)
    r.trust_norms[...] = jnp.where(
        at == 0, weight_norm, jnp.where(at == 1, update_norm, ratio)
    )
    sets = (
        (r.entry, r.entry_m, r.entry_q, r.entry_g, r.entry_1, r.entry_2, r.entry_w),
        (r.exit, r.exit_m, r.exit_q, r.exit_g, r.exit_1, r.exit_2, r.exit_w),
        (r.bypass, r.bypass_m, r.bypass_q, r.bypass_g, r.bypass_1, r.bypass_2, r.bypass_w),
    )
    for index, (weight, m, q, g, first, second, result) in enumerate(sets):
        master = weight[...]
        moment, square, direction = adam_update(g[...], m[...], q[...])
        update = direction + WEIGHT_DECAY * master
        first[...] = moment
        second[...] = square
        result[...] = master - MATRIX_RATE * ratio[index : index + 1] * update
    grad = r.affine_grad[0 : 2 * classes + 3, 0:local]
    moment, square, direction = adam_update(grad, r.affine_m[...], r.affine_q[...])
    r.affine_1[...] = moment
    r.affine_2[...] = square
    r.affine_w[...] = r.affine[...] - AFFINE_RATE * direction


def per_device(
    features,
    labels,
    groups,
    widths,
    entry_conv,
    entry_moment,
    entry_square,
    exit_conv,
    exit_moment,
    exit_square,
    bypass_conv,
    bypass_moment,
    bypass_square,
    norm_affine,
    norm_moment,
    norm_square,
    cotangent,
):
    n_img, n_ch = lax.axis_size("img"), lax.axis_size("ch")
    batch, local, pixels = features.shape
    chans = local * n_ch
    side = math.isqrt(pixels)
    inner = n_img // OUTER
    classes = (norm_affine.shape[0] - 3) // 2
    per = batch // n_ch
    assert (side, chans, n_ch, local, batch % n_ch) == (16, 256, 4, 64, 0) and per == 2
    rows, small = entry_conv.shape[0] * inner, bypass_conv.shape[0] * inner
    masters = (entry_conv, exit_conv, bypass_conv)
    if inner == 1:
        blocks = masters
    else:
        sets = [[o * inner + i for i in range(inner)] for o in range(OUTER)]
        blocks = tuple(
            lax.all_gather(w.astype(BF16), "img", axis=0, tiled=True, axis_index_groups=sets)
            for w in masters
        )

    vmem = pl.BlockSpec(memory_space=pltpu.VMEM)
    smem = pl.BlockSpec(memory_space=pltpu.SMEM)
    anywhere = pl.BlockSpec(memory_space=pl.ANY)
    states = dict(
        entry_m=entry_moment.T,
        entry_q=entry_square.T,
        exit_m=exit_moment.T,
        exit_q=exit_square.T,
        bypass_m=bypass_moment,
        bypass_q=bypass_square,
    )
    inputs = dict(
        labels=(labels, smem),
        groups=(groups, smem),
        widths=(widths, smem),
        features=(features, anywhere),
        cotangent=(cotangent, anywhere),
        entry=(blocks[0].T, anywhere),
        exit=(blocks[1].T, anywhere),
        bypass=(blocks[2], anywhere),
        affine=(norm_affine, anywhere),
    )
    if inner == 1:
        inputs.update({name: (value, anywhere) for name, value in states.items()})
    sds = jax.ShapeDtypeStruct
    outputs = dict(
        out=(sds(cotangent.shape, BF16), vmem),
        dx=(sds(features.shape, BF16), vmem),
        grad1=(sds((local, rows), F32), vmem),
        grad2=(sds((local, rows), F32), vmem),
        grad3=(sds((small, local), F32), vmem),
        affine_grad=(sds((24, 128), F32), vmem),
        norms=(sds((8, 128), F32), vmem),
    )
    pix = pixels * per
    taps9 = 9 * chans
    held = lambda shape, dtype=BF16: pltpu.VMEM(shape, dtype)
    scratch = dict(
        fown=held((batch, local, pixels)),
        cown=held((batch, local, 4 * pixels)),
        pass_c=held((2, local, 4 * pixels)),
        pass_o=held((2, local, 4 * pixels)),
        pass_x=held((2, local, pixels)),
        fbuf=held((n_ch, per, local, pixels)),
        cbuf=held((n_ch, per, local, 4 * pixels)),
        entry_v=held((local, rows), blocks[0].dtype),
        exit_v=held((local, rows), blocks[1].dtype),
        bypass_v=held((small, local), blocks[2].dtype),
        affine_v=held(norm_affine.shape, F32),
        padded=held((3 * local, 384)),
        wz1=held((n_ch, rows // 2, 128)),
        wz2=held((n_ch, (rows + small) // 2, 128)),
        aff_z=held((n_ch, 32, 128), F32),
        w1=held((taps9, chans)),
        w2=held((taps9, chans)),
        ws=held((chans, chans)),
        unpack=held((512, 512)),
        ident=held((256, 256)),
        shift=held((2, 256, 256)),
        gridder=held((512, 256)),
        fpm=held((pix, chans)),
        h1s=held((3, per, pixels + 32, chans)),
        h1cm=held((chans, pix)),
        y1=held((4, pix, chans), F32),
        act=held((4, pix, chans), F32),
        h2s=held((2, 4, per, pixels + 32, chans)),
        dzs=held((2, 4, per, pixels + 32, chans)),
        h2cm=held((chans, 4 * pix)),
        short=held((pix, chans), F32),
        dshort=held((pix, chans), F32),
        dzc=held((pix, chans)),
        act1=held((pix, chans), F32),
        rc=held((4, pix, chans)),
        ocm=held((per, chans, 4 * pixels)),
        dcm=held((per, chans, pixels)),
        field=held((9, per, pixels, chans)),
        dw1=held((taps9, chans), F32),
        dw2=held((taps9, chans), F32),
        dws=held((chans, chans), F32),
    )
    for number, size in ((1, rows), (2, rows + small)):
        shapes = ((4, size, chans),) * 2 + ((2, 2, size, 128),) * 2 + ((2, size, 128),) * 2
        shapes += ((n_ch, size // 2, 128),) * 2
        for part, shape in zip(PARTS, shapes):
            scratch[part + str(number)] = held(shape)
        scratch[PARTS[-1] + str(number)] = held((4, size, chans), F32)
    exchanges = [(8, chans), (8, chans), (16, chans), (32, chans)]
    if inner == 1:
        exchanges.append((8, 128))
        for v, shape in (("v1", (local, rows)), ("v2", (local, rows)), ("vs", (small, local))):
            scratch[v + "m"] = held(shape, F32)
            scratch[v + "q"] = held(shape, F32)
    for number, shape in enumerate(exchanges, 1):
        for axis, size in zip("abc", (OUTER, inner, n_ch)):
            if size > 1:
                scratch[axis + str(number)] = held((size,) + shape, F32)
    remote_count = 3 * 3 + 4 * 4 * per + 3 * 7 + 2 * 13 + len(exchanges) * (7 + 3 + inner - 1)
    scratch.update(
        send=pltpu.SemaphoreType.DMA((remote_count,)),
        recv=pltpu.SemaphoreType.DMA((remote_count,)),
        lsem=pltpu.SemaphoreType.DMA((20,)),
    )
    cfg = SimpleNamespace(
        names=[*inputs, *outputs, *scratch],
        inner=inner,
        n_ch=n_ch,
        batch=batch,
        local=local,
        classes=classes,
        count=float(batch * n_img // widths.shape[0] * pixels),
        rows=rows,
        small=small,
        used=[],
    )
    out, dx, grad1, grad2, grad3, affine_grad, norms = pl.pallas_call(
        functools.partial(main_kernel, cfg),
        out_shape=[s for s, _ in outputs.values()],
        in_specs=[s for _, s in inputs.values()],
        out_specs=[s for _, s in outputs.values()],
        scratch_shapes=list(scratch.values()),
        compiler_params=pltpu.CompilerParams(
            collective_id=0, has_side_effects=True, vmem_limit_bytes=VMEM_LIMIT
        ),
        name="block_step",
    )(*[v for v, _ in inputs.values()])
    assert max(n for n, _ in cfg.used) <= remote_count and max(n for _, n in cfg.used) <= 20

    grads = [grad1, grad2, grad3]
    if inner > 1:
        grads = [
            lax.psum_scatter(g, "img", scatter_dimension=0, axis_index_groups=sets, tiled=True)
            for g in (grad1.T, grad2.T, grad3)
        ]
        updates = []
        for w, g, m, s in zip(
            masters,
            grads,
            (entry_moment, exit_moment, bypass_moment),
            (entry_square, exit_square, bypass_square),
        ):
            updates.append(adam_update(g, m, s)[2] + WEIGHT_DECAY * w)
        sums = lax.psum(
            jnp.stack([jnp.sum(w * w) for w in masters] + [jnp.sum(u * u) for u in updates]),
            ("img", "ch"),
        )
        norms = jnp.broadcast_to(jnp.pad(sums, (0, 2))[:, None], (8, 128))
        grads = [grads[0].T, grads[1].T, grads[2]]

    args = dict(
        out=out,
        dx=dx,
        norms=norms,
        affine_grad=affine_grad,
        entry_g=grads[0],
        exit_g=grads[1],
        bypass_g=grads[2],
        entry=entry_conv.T,
        exit=exit_conv.T,
        bypass=bypass_conv,
        **states,
        affine=norm_affine,
        affine_m=norm_moment,
        affine_q=norm_square,
    )
    tall = sds(entry_conv.shape[::-1], F32)
    short, wide = (sds(w.shape, F32) for w in (bypass_conv, norm_affine))
    results = dict(
        block_output=sds(cotangent.shape, BF16),
        input_gradient=sds(features.shape, F32),
        entry_1=tall,
        entry_2=tall,
        entry_w=tall,
        exit_1=tall,
        exit_2=tall,
        exit_w=tall,
        bypass_1=short,
        bypass_2=short,
        bypass_w=short,
        affine_1=wide,
        affine_2=wide,
        affine_w=wide,
        trust_norms=sds((3, 3), F32),
    )
    end_cfg = SimpleNamespace(names=[*args, *results], classes=classes, local=local)
    final = pl.pallas_call(
        functools.partial(final_kernel, end_cfg),
        out_shape=list(results.values()),
        in_specs=[vmem] * len(args),
        out_specs=[vmem] * len(results),
        compiler_params=pltpu.CompilerParams(vmem_limit_bytes=VMEM_LIMIT),
        name="finish",
    )(*args.values())
    return tuple(v.T if s is tall else v for v, s in zip(final, results.values()))


def solution(mesh):
    wide = P("img", "ch")
    deep = P("img", "ch", None)
    table = P(None, "ch")
    return jax.shard_map(
        per_device,
        mesh=mesh,
        in_specs=(deep, P("img"), P("img"), P()) + (wide,) * 9 + (table,) * 3 + (deep,),
        out_specs=(deep, deep) + (wide,) * 9 + (table,) * 3 + (P(),),
        check_vma=False,
    )
```

```python
import functools
import math
from types import SimpleNamespace

import jax
import jax.numpy as jnp
from jax import lax
from jax.experimental import pallas as pl
from jax.experimental.pallas import tpu as pltpu
from jax.sharding import PartitionSpec as P

LEVELS = 4
STEP = 5
NORM_EPSILON = 1e-05
ADAM_EPSILON = 1e-06
MOMENT_DECAY = 0.9
SQUARE_DECAY = 0.999
WEIGHT_DECAY = 0.01
MATRIX_RATE = 0.3
AFFINE_RATE = 0.2

OUTER = 8
VMEM_LIMIT = 56 * 1024 * 1024
BF16 = jnp.bfloat16
F32 = jnp.float32
MESH = pl.DeviceIdType.MESH
PARTS = ("s1", "r1", "s2", "r2", "s3", "r3", "s4", "r4", "acc")


def nn(left, right):
    return lax.dot_general(left, right, (((1,), (0,)), ((), ())), preferred_element_type=F32)


def nt(left, right):
    return lax.dot_general(left, right, (((1,), (1,)), ((), ())), preferred_element_type=F32)


def tn(left, right):
    return lax.dot_general(left, right, (((0,), (0,)), ((), ())), preferred_element_type=F32)


def flip(index, mask):
    result = index
    for bit in range(3):
        if (mask >> bit) & 1:
            digit = lax.rem(lax.div(index, 1 << bit), 2)
            result = result + (1 - 2 * digit) * (1 << bit)
    return result


def sigmoid(value):
    return 0.5 * jnp.tanh(0.5 * value) + 0.5


def iota(shape, axis):
    return lax.broadcasted_iota(jnp.int32, shape, axis)


def to_bf16(condition):
    return jnp.where(condition, 1.0, 0.0).astype(BF16)


def pick_row(table, index):
    hit = iota(table.shape, 0) == index
    return jnp.sum(jnp.where(hit, table, 0.0), axis=0, keepdims=True)


def place_row(row, index, rows):
    hit = iota((rows, row.shape[1]), 0) == index
    return jnp.where(hit, row, 0.0)


def colsum(value):
    return jnp.sum(value, axis=0, keepdims=True)


def adam_update(grad, moment, square):
    moment_new = MOMENT_DECAY * moment + (1.0 - MOMENT_DECAY) * grad
    square_new = SQUARE_DECAY * square + (1.0 - SQUARE_DECAY) * grad * grad
    direction = (
        moment_new
        / (1.0 - MOMENT_DECAY**STEP)
        / (jnp.sqrt(square_new / (1.0 - SQUARE_DECAY**STEP)) + ADAM_EPSILON)
    )
    return (moment_new, square_new, direction)


def total(value):
    return jnp.sum(jnp.sum(value, axis=1, keepdims=True), axis=0, keepdims=True)


def main_kernel(cfg, *refs):
    r = SimpleNamespace(**dict(zip(cfg.names, refs)))
    inner, n_ch, batch, local = cfg.inner, cfg.n_ch, cfg.batch, cfg.local
    classes, count = cfg.classes, cfg.count
    per = batch // n_ch
    chans = local * n_ch
    rows, small = cfg.rows, cfg.small
    tail = (rows - 256) // 2
    hw, hs = rows // 2, small // 2
    slots = SimpleNamespace(remote=0, local=0)

    img = lax.axis_index("img")
    me = lax.axis_index("ch")
    block = lax.div(img, inner)
    within = lax.rem(img, inner)
    core = lax.rem(block, 2)
    plane = lax.div(block, 2)
    bit_x, bit_y = lax.rem(plane, 2), lax.div(plane, 2)
    partner = flip(block, 1)

    def dev(block_id, within_id, ch_id):
        return (block_id * inner + within_id, ch_id)

    pending = []

    def post(src, dst, landed, peer):
        slot = slots.remote
        slots.remote = slot + 1
        copy = pltpu.make_async_remote_copy(
            src_ref=src,
            dst_ref=dst,
            send_sem=r.send.at[slot],
            recv_sem=r.recv.at[slot],
            device_id=peer,
            device_id_type=MESH,
        )
        copy.start()
        pending.append(copy.wait_send)
        arrival = pltpu.make_async_remote_copy(
            src_ref=landed,
            dst_ref=landed,
            send_sem=r.send.at[slot],
            recv_sem=r.recv.at[slot],
            device_id=peer,
            device_id_type=MESH,
        )
        return arrival.wait_recv

    def here(src, dst):
        slot = slots.local
        slots.local = slot + 1
        copy = pltpu.make_async_copy(src, dst, r.lsem.at[slot])
        copy.start()
        return copy.wait

    outer_peers = [flip(block, mask) for mask in range(1, OUTER)]
    ch_peers = [flip(me, mask) for mask in range(1, n_ch)]
    inner_pairs = [
        (lax.rem(within + step, inner), lax.rem(within + inner - step, inner))
        for step in range(1, inner)
    ]
    up, down, far = (lax.rem(me + step, n_ch) for step in (1, 3, 2))
    up_peer, down_peer = dev(block, within, up), dev(block, within, down)

    class Ring:
        def __init__(self, source, target, passing):
            self.target, self.passing = target, passing
            self.waits = []
            self.early = [
                post(source(far, 0), passing.at[0], passing.at[0], up_peer),
                post(source(far, 1), passing.at[1], passing.at[1], down_peer),
            ]
            for im in range(per):
                self.waits += [
                    post(source(up, im), target(me, im), target(down, im), up_peer),
                    post(source(down, im), target(me, im), target(up, im), down_peer),
                ]

        def forward(self):
            self.early[0]()
            self.waits.append(
                post(self.passing.at[0], self.target(down, 0), self.target(far, 0), up_peer)
            )
            self.early[1]()
            self.waits.append(
                post(self.passing.at[1], self.target(up, 1), self.target(far, 1), down_peer)
            )

        def settle(self):
            for wait in self.waits:
                wait()

    barrier = pltpu.get_barrier_semaphore()
    everyone = [dev(peer, within, me) for peer in outer_peers]
    everyone += [dev(block, within, peer) for peer in ch_peers]
    everyone += [dev(block, peer, me) for peer, _ in inner_pairs]
    for peer in everyone:
        pl.semaphore_signal(barrier, inc=1, device_id=peer, device_id_type=MESH)

    got_entry = here(r.entry, r.entry_v)
    got_features = here(r.features, r.fown)
    got_exit = here(r.exit, r.exit_v)
    got_bypass = here(r.bypass, r.bypass_v)
    got_affine = here(r.affine, r.affine_v)
    got_cot = here(r.cotangent, r.cown)
    states = ((r.entry_m, r.entry_q), (r.exit_m, r.exit_q), (r.bypass_m, r.bypass_q)) if inner == 1 else ()
    held = [
        (here(m, getattr(r, v + "m")), here(q, getattr(r, v + "q")))
        for (m, q), v in zip(states, ("v1", "v2", "vs"))
    ]

    s_row, s_col = iota((hw, 384), 0), iota((hw, 384), 1)
    pick_first = to_bf16(s_col == jnp.where(s_row < 128, s_row, s_row + 128))
    pick_second = to_bf16(s_col == jnp.where(s_row < 128, s_row + 128, s_row + 128 + tail))
    r.padded[...] = jnp.zeros(r.padded.shape, BF16)

    def pack_own(value):
        r.padded[local : 2 * local, 0:rows] = value.astype(BF16)
        packed = nt(pick_first, r.padded[local : 3 * local, :])
        return (packed + nt(pick_second, r.padded[0 : 2 * local, :])).astype(BF16)

    got_entry()
    r.wz1[me] = pack_own(r.entry_v[...])
    pl.semaphore_wait(barrier, len(everyone))

    def to_channels(buffer):
        return [
            post(buffer.at[me], buffer.at[me], buffer.at[peer], dev(block, within, peer))
            for peer in ch_peers
        ]

    entry_waits = to_channels(r.wz1)
    got_features()
    feature_waits = [
        post(
            r.fown.at[pl.ds(per * peer, per)],
            r.fbuf.at[me],
            r.fbuf.at[peer],
            dev(block, within, peer),
        )
        for peer in ch_peers
    ]
    r.fbuf[me] = r.fown[pl.ds(per * me, per)]
    flat = jnp.concatenate([r.fown[b] for b in range(batch)], axis=1)
    wide = flat.astype(F32)
    square = wide * wide
    square_hi = square.astype(BF16)
    square_lo = (square - square_hi.astype(F32)).astype(BF16)
    level = iota((16, 256), 0)
    first_mask = jnp.concatenate([to_bf16(level == r.groups[b]) for b in range(batch)], axis=1)
    second_mask = jnp.concatenate([to_bf16(level == r.groups[b] + 4) for b in range(batch)], axis=1)
    sums = nt(first_mask, flat) + nt(second_mask, square_hi) + nt(second_mask, square_lo)

    got_affine()
    r.aff_z[me] = jnp.zeros((32, 128), F32)
    r.aff_z[me, 0 : 2 * classes + 3, 0:local] = r.affine_v[...]
    r.aff_z[me, 24:32, 0:local] = sums[0:8]
    affine_waits = to_channels(r.aff_z)

    got_exit()
    got_bypass()
    r.wz2[me, 0:hw, :] = pack_own(r.exit_v[...])
    e_row, e_col = iota((local, 128), 0), iota((local, 128), 1)
    value = r.bypass_v[...].astype(BF16)
    r.wz2[me, hw : hw + hs, :] = (
        nn(value[:hs], to_bf16(e_col == e_row)) + nn(value[hs:], to_bf16(e_col == e_row + local))
    ).astype(BF16)

    exit_waits = to_channels(r.wz2)
    got_cot()
    cotangent = Ring(
        lambda c, im: r.cown.at[per * c + im], lambda c, im: r.cbuf.at[c, im], r.pass_c
    )

    lane = iota((512, 512), 0)
    column = iota((512, 512), 1)
    spot = 256 * ((lane >> 6) & 1) + 64 * (lane >> 7) + (lane & 63)
    r.unpack[...] = to_bf16(column == spot)

    def ordered_sum(ref, size):
        result = ref[0]
        for slot in range(1, size):
            result = result + ref[slot]
        return result

    class AllReduce:
        def __init__(self, number):
            self.over_outer, self.over_inner, self.over_ch = (
                getattr(r, axis + str(number), None) for axis in "abc"
            )

        def begin(self, value):
            ref = self.over_outer
            ref[block] = value
            self.waits = [
                post(ref.at[block], ref.at[block], ref.at[peer], dev(peer, within, me))
                for peer in outer_peers
            ]

        def plane(self):
            for wait in self.waits:
                wait()
            value = ordered_sum(self.over_outer, OUTER)
            if inner > 1:
                ref = self.over_inner
                ref[within] = value
                waits = [
                    post(ref.at[within], ref.at[within], ref.at[back], dev(block, peer, me))
                    for peer, back in inner_pairs
                ]
                for wait in waits:
                    wait()
                value = ordered_sum(ref, inner)
            return value

        def middle(self):
            self.over_ch[me] = self.plane()
            self.waits = to_channels(self.over_ch)

        def end(self):
            for wait in self.waits:
                wait()
            return ordered_sum(self.over_ch, n_ch)

    def rows_of(ref, index):
        size = ref.shape[0] // OUTER
        return ref.at[pl.ds(pl.multiple_of(size * index, 16), size)]

    def unpack_own(ref, full):
        own = rows_of(ref, block)
        if full.shape[0] == hw:
            own[0:128, :] = full[0:128, 0:256]
            own[128:256, :] = full[0:128, 256:512]
            own[256 : 256 + tail, :] = full[128:, 0:256]
            own[256 + tail :, :] = full[128:, 256:512]
        else:
            own[0:hs, :] = full[:, 0:256]
            own[hs:, :] = full[:, 256:512]

    def spread(ref):
        own = rows_of(ref, block)
        return {
            mask: post(own, own, rows_of(ref, flip(block, mask)), dev(flip(block, mask), within, me))
            for mask in (2, 4, 6, 1)
        }

    def forward(ref, waits):
        rest = [waits[1]]
        for mask in (2, 4, 6):
            waits[mask]()
            mine = rows_of(ref, flip(block, mask))
            theirs = rows_of(ref, flip(partner, mask))
            rest.append(post(mine, mine, theirs, dev(partner, within, me)))
        return rest

    def widen(buffer):
        packed = jnp.concatenate([buffer[c] for c in range(n_ch)], axis=1)
        return nn(packed, r.unpack[...]).astype(BF16)

    def wide_lanes(ref):
        parts = [
            ref[c] + pltpu.roll(ref[c + 1], local, axis=1) for c in range(0, n_ch, 2)
        ]
        return jnp.concatenate(parts, axis=1)

    for wait in affine_waits:
        wait()
    affine = wide_lanes(r.aff_z)
    input_sums = AllReduce(1)
    input_sums.begin(affine[24:32])
    for wait in entry_waits:
        wait()
    unpack_own(r.w1, widen(r.wz1))
    gather1 = spread(r.w1)

    ident = to_bf16(iota((256, 256), 0) == iota((256, 256), 1))
    r.ident[...] = ident
    q_out, q_in = iota((256, 256), 0), iota((256, 256), 1)
    r.shift[0] = to_bf16((q_in == q_out + 1) & ((q_out & 15) < 15))
    r.shift[1] = to_bf16((q_in == q_out - 1) & ((q_out & 15) > 0))

    for wait in exit_waits:
        wait()
    full = widen(r.wz2)
    unpack_own(r.w2, full[0:hw])
    unpack_own(r.ws, full[hw:])
    gather2 = spread(r.w2)
    gather3 = spread(r.ws)

    rho, px = iota((512, 256), 0), iota((512, 256), 1)
    version, a, b_ = rho >> 8, (rho >> 7) & 1, (rho >> 6) & 1
    col = (rho & 15) + version * (1 - 2 * b_)
    target = (2 * ((rho & 63) >> 4) + a) * 32 + 2 * col + b_
    r.gridder[...] = to_bf16((px == target) & (col >= 0) & (col < 16))
    zeros = jnp.zeros((16, 256), BF16)
    for im in range(per):
        for ver in range(3):
            r.h1s[ver, im, 0:16, :] = zeros
            r.h1s[ver, im, 272:288, :] = zeros
        for ver in range(2):
            for ph in range(4):
                for ref in (r.h2s, r.dzs):
                    ref[ver, ph, im, 0:16, :] = zeros
                    ref[ver, ph, im, 272:288, :] = zeros

    def channel_major(ref, im, lanes):
        return jnp.concatenate([ref[c, im, :, lanes] for c in range(n_ch)], axis=0)

    for wait in feature_waits:
        wait()
    for im in range(per):
        r.fpm[256 * im : 256 * im + 256, :] = nt(
            ident, channel_major(r.fbuf, im, slice(0, 256))
        ).astype(BF16)

    stats = input_sums.plane()
    mean1 = stats[0:4] / count
    inv1 = lax.rsqrt(stats[4:8] / count - mean1 * mean1 + NORM_EPSILON)
    gain = affine[2 * classes : 2 * classes + 1]
    shift = affine[2 * classes + 1 : 2 * classes + 2]
    out_bias = affine[2 * classes + 2 : 2 * classes + 3]
    group, label, mean1_b, inv1_b, gamma_b, beta_b, mask_b = [], [], [], [], [], [], []
    for im in range(per):
        group.append(r.groups[per * me + im])
        label.append(r.labels[per * me + im])
        mean1_b.append(pick_row(mean1, group[im]))
        inv1_b.append(pick_row(inv1, group[im]))
        gamma_b.append(pick_row(affine, label[im]))
        beta_b.append(pick_row(affine, label[im] + classes))
        width = r.widths[group[im]]
        mask_b.append(
            jnp.where(iota((1, chans), 1) < width * (chans // LEVELS), 1.0, 0.0)
        )

    for im in range(per):
        normal = (r.fpm[256 * im : 256 * im + 256, :].astype(F32) - mean1_b[im]) * inv1_b[im]
        pre = gamma_b[im] * normal + beta_b[im]
        hidden = (pre * sigmoid(pre)).astype(BF16)
        r.h1s[1, im, 16:272, :] = hidden
        r.h1s[0, im, 16:272, :] = nn(r.shift[1], hidden).astype(BF16)
        r.h1s[2, im, 16:272, :] = nn(r.shift[0], hidden).astype(BF16)
        r.h1cm[:, 256 * im : 256 * im + 256] = nt(ident, hidden).astype(BF16)

    rest = forward(r.w1, gather1)
    cotangent.forward()
    for wait in rest:
        wait()

    def back_product(parts, ref):
        result = nt(parts[0], ref[0:256, :])
        for tap in range(1, 9):
            result = result + nt(parts[tap], ref[256 * tap : 256 * tap + 256, :])
        return result

    def taps():
        return [(dy, dx) for dy in range(3) for dx in range(3)]

    def stack(pieces):
        return jnp.concatenate(pieces, axis=0)

    def conv1(phase, carry):
        a, c = lax.div(phase, 2), lax.rem(phase, 2)
        parts = []
        for dy, dx in taps():
            first = pl.multiple_of(16 * lax.div(a + dy + 1, 2), 16)
            ver = lax.div(c + dx + 1, 2)
            parts.append(
                stack([r.h1s[ver, im, pl.ds(first, 256), :] for im in range(per)])
            )
        y = nn(jnp.concatenate(parts, axis=1), r.w1[...])
        r.y1[phase] = y
        out = []
        for im in range(per):
            piece = y[256 * im : 256 * im + 256]
            out.append(carry[2 * im] + colsum(piece))
            out.append(carry[2 * im + 1] + colsum(piece * piece))
        return tuple(out)

    nought = jnp.zeros((1, chans), F32)
    mid = lax.fori_loop(0, 4, conv1, (nought,) * (2 * per))
    payload = jnp.zeros((8, chans), F32)
    for im in range(per):
        payload = payload + place_row(mid[2 * im], group[im], 8)
        payload = payload + place_row(mid[2 * im + 1], group[im] + 4, 8)
    mid_sums = AllReduce(2)
    mid_sums.begin(payload)

    rest = forward(r.w2, gather2) + forward(r.ws, gather3)
    mid_sums.middle()

    r.cbuf[me] = r.cown[pl.ds(per * me, per)]
    cotangent.settle()
    for im in range(per):
        for n in range(4):
            piece = channel_major(r.cbuf, im, slice(256 * n, 256 * n + 256))
            grid = nt(r.gridder[...], piece).astype(BF16)
            for ver in range(2):
                for ph in range(4):
                    at = 256 * ver + 64 * ph
                    r.dzs[ver, ph, im, 16 + 64 * n : 80 + 64 * n, :] = grid[at : at + 64]

    coarse = jnp.zeros((256 * per, chans), F32)
    for ph in range(4):
        coarse = coarse + stack([r.dzs[0, ph, im, 16:272, :] for im in range(per)]).astype(F32)
    bias_sum = colsum(coarse)
    r.dzc[...] = coarse.astype(BF16)

    def tap_slice(ref, a, c, dy, dx, im):
        row, colm = a + dy + 1, c + dx + 1
        first = pl.multiple_of(16 * lax.div(row, 2), 16)
        ph = 2 * lax.rem(row, 2) + lax.rem(colm, 2)
        side_step = lax.div(colm, 2) - 1
        return ref[side_step * side_step, ph, im, pl.ds(first, 256), :]

    for wait in rest:
        wait()

    def back2(phase, carry):
        a, c = lax.div(phase, 2), lax.rem(phase, 2)
        parts = [
            stack([tap_slice(r.dzs, a, c, 2 - dy, 2 - dx, im) for im in range(per)])
            for dy, dx in taps()
        ]
        r.act[phase] = back_product(parts, r.w2)
        return carry

    lax.fori_loop(0, 4, back2, 0)

    stats = mid_sums.end()
    mean2 = stats[0:4] / (4.0 * count)
    inv2 = lax.rsqrt(stats[4:8] / (4.0 * count) - mean2 * mean2 + NORM_EPSILON)
    mean2_b = [pick_row(mean2, group[im]) for im in range(per)]
    inv2_b = [pick_row(inv2, group[im]) for im in range(per)]

    def hidden2(phase, carry):
        c = lax.rem(phase, 2)
        out = []
        for im in range(per):
            span = slice(256 * im, 256 * im + 256)
            normal = (r.y1[phase, span, :] - mean2_b[im]) * inv2_b[im]
            r.y1[phase, span, :] = normal
            pre = gain * normal + shift
            sig = sigmoid(pre)
            hidden = (pre * sig * mask_b[im]).astype(BF16)
            act = r.act[phase, span, :] * (sig * (1.0 + pre * (1.0 - sig)) * mask_b[im])
            r.act[phase, span, :] = act
            out.append(carry[2 * im] + colsum(act))
            out.append(carry[2 * im + 1] + colsum(act * normal))
            r.h2s[0, phase, im, 16:272, :] = hidden
            r.h2s[1, phase, im, 16:272, :] = nn(r.shift[c], hidden).astype(BF16)
            lanes = pl.ds(pl.multiple_of(512 * phase + 256 * im, 256), 256)
            r.h2cm[:, lanes] = nt(r.ident[...], hidden).astype(BF16)
        return tuple(out)

    mid = lax.fori_loop(0, 4, hidden2, (nought,) * (2 * per))
    payload = place_row(bias_sum, 8, 16)
    for im in range(per):
        payload = payload + place_row(mid[2 * im], group[im], 16)
        payload = payload + place_row(mid[2 * im + 1], group[im] + 4, 16)
    back_sums = AllReduce(3)
    back_sums.begin(payload)

    r.short[...] = nn(r.fpm[...], r.ws[...]) + out_bias
    def conv2(phase, carry):
        a, c = lax.div(phase, 2), lax.rem(phase, 2)
        parts = [
            stack([tap_slice(r.h2s, a, c, dy, dx, im) for im in range(per)]) for dy, dx in taps()
        ]
        y = nn(jnp.concatenate(parts, axis=1), r.w2[...]) + r.short[...]
        r.rc[phase] = y.astype(BF16)
        return carry

    lax.fori_loop(0, 4, conv2, 0)
    for im in range(per):
        for n in range(4):
            first = 256 * im + 64 * n
            piece = stack([r.rc[ph, first : first + 64, :] for ph in range(4)])
            r.ocm[im, :, 256 * n : 256 * n + 256] = tn(piece, r.gridder[0:256, :]).astype(BF16)

    def own_channels(ref, index, im):
        return ref.at[im, pl.ds(pl.multiple_of(local * index, local), local), :]

    def give_back(ref, out, passing):
        for im in range(per):
            out[per * me + im] = own_channels(ref, me, im)[...]
        return Ring(
            lambda c, im: own_channels(ref, c, im), lambda c, im: out.at[per * c + im], passing
        )

    back_sums.middle()
    block_output = give_back(r.ocm, r.out, r.pass_o)

    def grad2(tap, carry):
        dy, dx = lax.div(tap, 3), lax.rem(tap, 3)
        pieces = []
        for ph in range(4):
            a, c = ph // 2, ph % 2
            for im in range(per):
                pieces.append(tap_slice(r.dzs, a, c, 2 - dy, 2 - dx, im))
        first = pl.multiple_of(256 * tap, 256)
        r.dw2[pl.ds(first, 256), :] = nn(r.h2cm[...], stack(pieces))
        return carry

    lax.fori_loop(0, 9, grad2, 0)
    for im in range(per):
        piece = channel_major(r.fbuf, im, slice(0, 256))
        grad = nn(piece, r.dzc[256 * im : 256 * im + 256, :])
        if im == 0:
            r.dws[...] = grad
        else:
            r.dws[...] = r.dws[...] + grad

    class GradSum:
        def __init__(self, number, fetch):
            self.fetch = fetch
            for part in PARTS:
                setattr(self, part, getattr(r, part + str(number)))

        def begin(self):
            self.waits = []
            for u in range(4):
                self.s1[u] = self.fetch(2 * u + 1 - core).astype(BF16)
                self.waits.append(
                    post(self.s1.at[u], self.r1.at[u], self.r1.at[u], dev(partner, within, me))
                )

        def settle(self):
            for wait in self.waits:
                wait()

        def across(self, send, got, masks):
            parts = [(h, v) for v in range(2) for h in range(2)] if len(send.shape) == 4 else [(0,), (1,)]
            self.waits = [
                post(send.at[p], got.at[p], got.at[p], dev(flip(block, masks[p[0]]), within, me))
                for p in parts
            ]

        def first(self):
            for u in range(4):
                self.waits[u]()
                self.acc[u] = self.fetch(2 * u + core) + self.r1[u].astype(F32)
            for v in range(2):
                self.s2[0, v] = self.acc[2 * v + 1 - bit_x, :, 0:128].astype(BF16)
                self.s2[1, v] = self.acc[2 * (1 - bit_y) + v, :, 128:256].astype(BF16)
            self.across(self.s2, self.r2, (2, 4))

        def second(self):
            self.settle()
            low = self.acc[2 * (1 - bit_y) + bit_x, :, 0:128] + self.r2[0, 1 - bit_y].astype(F32)
            high = self.acc[2 * bit_y + 1 - bit_x, :, 128:256] + self.r2[1, 1 - bit_x].astype(F32)
            self.s3[0] = low.astype(BF16)
            self.s3[1] = high.astype(BF16)
            self.across(self.s3, self.r3, (4, 2))

        def third(self):
            self.settle()
            low = self.acc[plane, :, 0:128] + self.r2[0, bit_y].astype(F32)
            high = self.acc[plane, :, 128:256] + self.r2[1, bit_x].astype(F32)
            low, high = low + self.r3[0].astype(F32), high + self.r3[1].astype(F32)
            value = jnp.concatenate([low, high], axis=1).astype(BF16)
            left = [value[0:128], value[256 : 256 + tail]]
            right = [value[128:256], value[256 + tail : rows]]
            if value.shape[0] > rows:
                left.append(value[rows : rows + hs])
                right.append(value[rows + hs :])
            pair = jnp.concatenate([stack(left), stack(right)], axis=1)
            packed = nt(pair, r.unpack[...]).astype(BF16)
            for c in range(n_ch):
                self.s4[c] = packed[:, 128 * c : 128 * c + 128]
            self.r4[me] = self.s4[me]
            self.waits = [
                post(self.s4.at[peer], self.r4.at[me], self.r4.at[peer], dev(block, within, peer))
                for peer in ch_peers
            ]

        def end(self, out, out_small=None):
            self.settle()
            done = self.r4[0].astype(F32)
            for c in range(1, n_ch):
                done = done + self.r4[c].astype(F32)
            turned = done[0:128].T
            out[:, 0:128] = turned[0:local]
            out[:, 128:256] = turned[local:]
            gap = jnp.zeros((128 - tail, 128), F32)
            turned = stack([done[128 : 128 + tail], gap]).T
            ends = turned[0:local] + pltpu.roll(turned[local:], tail, axis=1)
            out[:, 256:rows] = ends[:, 0 : rows - 256]
            if out_small is not None:
                last = done[hw:]
                out_small[0:hs, :] = last[:, 0:local]
                out_small[hs:, :] = pltpu.roll(last, local, axis=1)[:, 0:local]

    def block_rows(ref, size, index):
        return ref[pl.ds(pl.multiple_of(size * index, 8), size), :]

    second = GradSum(2, lambda k: stack([block_rows(r.dw2, rows, k), block_rows(r.dws, small, k)]))
    entry = GradSum(1, lambda k: block_rows(r.dw1, rows, k))
    second.begin()
    r.dshort[...] = nt(r.dzc[...], r.ws[...])

    stats = back_sums.end()
    affine_grad2 = stats
    p1_b = [pick_row(stats[0:4], group[im]) / (4.0 * count) for im in range(per)]
    p2_b = [pick_row(stats[4:8], group[im]) / (4.0 * count) for im in range(per)]

    for im in range(per):
        span = slice(256 * im, 256 * im + 256)
        scale = gain * inv2_b[im]
        combos = []
        for a in range(2):
            grads = []
            for c in range(2):
                ph = 2 * a + c
                d = scale * (r.act[ph, span, :] - (p1_b[im] + r.y1[ph, span, :] * p2_b[im]))
                grads.append(d.astype(BF16))
            right = nn(r.shift[0], grads[0])
            left = nn(r.shift[1], grads[1])
            even, odd = grads[0].astype(F32), grads[1].astype(F32)
            combos.append((odd + right, even + odd, left + even))
        gap = jnp.zeros((16, chans), F32)
        if im == 0:
            second.first()
        for dx in range(3):
            upper, lower = combos[0][dx], combos[1][dx]
            r.field[dx, im] = (lower + stack([upper[16:], gap])).astype(BF16)
            r.field[3 + dx, im] = (upper + lower).astype(BF16)
            r.field[6 + dx, im] = (stack([gap, lower[:-16]]) + upper).astype(BF16)

    block_output.forward()

    def grad1(tap, carry):
        first = pl.multiple_of(256 * tap, 256)
        r.dw1[pl.ds(first, 256), :] = nn(
            r.h1cm[...], stack([r.field[tap, im] for im in range(per)])
        )
        return carry

    lax.fori_loop(0, 9, grad1, 0)
    entry.begin()
    second.second()

    parts = [stack([r.field[tap, im] for im in range(per)]) for tap in range(9)]
    dh1 = back_product(parts, r.w1)
    payload = jnp.zeros((32, chans), F32)
    for im in range(per):
        span = slice(256 * im, 256 * im + 256)
        normal = (r.fpm[span, :].astype(F32) - mean1_b[im]) * inv1_b[im]
        pre = gamma_b[im] * normal + beta_b[im]
        sig = sigmoid(pre)
        act = dh1[span] * (sig * (1.0 + pre * (1.0 - sig)))
        r.act1[span, :] = act
        q1, q2 = colsum(act), colsum(act * normal)
        payload = payload + place_row(q2, label[im], 32)
        payload = payload + place_row(q1, label[im] + classes, 32)
        payload = payload + place_row(gamma_b[im] * q1, group[im] + 24, 32)
        payload = payload + place_row(gamma_b[im] * q2, group[im] + 28, 32)
    last_sums = AllReduce(4)
    last_sums.begin(payload)
    entry.first()
    second.third()
    last_sums.middle()
    entry.second()

    stats = last_sums.end()
    for im in range(per):
        span = slice(256 * im, 256 * im + 256)
        normal = (r.fpm[span, :].astype(F32) - mean1_b[im]) * inv1_b[im]
        r1 = pick_row(stats[24:28], group[im]) / count
        r2 = pick_row(stats[28:32], group[im]) / count
        grad = inv1_b[im] * (gamma_b[im] * r.act1[span, :] - (r1 + normal * r2))
        grad = (grad + r.dshort[span, :]).astype(BF16)
        r.dcm[im] = nt(r.ident[...], grad).astype(BF16)
    entry.third()
    input_gradient = give_back(r.dcm, r.dx, r.pass_x)
    second.end(r.grad2, r.grad3)
    input_gradient.forward()

    table = jnp.zeros((24, chans), F32)
    table = table + jnp.where(iota((24, chans), 0) < 2 * classes, stats[0:24], 0.0)
    table = table + place_row(colsum(affine_grad2[4:8]), 2 * classes, 24)
    table = table + place_row(colsum(affine_grad2[0:4]), 2 * classes + 1, 24)
    table = table + place_row(affine_grad2[8:9], 2 * classes + 2, 24)
    mine = jnp.zeros((24, 128), F32)
    for c in range(n_ch):
        piece = table[:, 128 * (c // 2) : 128 * (c // 2) + 128]
        if c % 2:
            piece = pltpu.roll(piece, local, axis=1)
        mine = mine + jnp.where(me == c, piece, 0.0)
    r.affine_grad[...] = mine

    if inner == 1:
        row = iota((8, 128), 0)

        def norm_rows(index, weight, grad, v):
            for wait in held[index]:
                wait()
            master = weight[...]
            _, _, direction = adam_update(
                grad[...], getattr(r, v + "m")[...], getattr(r, v + "q")[...]
            )
            update = direction + WEIGHT_DECAY * master
            rows_w = jnp.where(row == index, total(master * master), 0.0)
            return rows_w + jnp.where(row == index + 3, total(update * update), 0.0)

        norms = norm_rows(1, r.exit_v, r.grad2, "v2") + norm_rows(2, r.bypass_v, r.grad3, "vs")
        entry.end(r.grad1)
        norms = norms + norm_rows(0, r.entry_v, r.grad1, "v1")
        norm_sums = AllReduce(5)
        norm_sums.begin(norms)
        norm_sums.middle()
        r.norms[...] = norm_sums.end()
    else:
        entry.end(r.grad1)
        r.norms[...] = jnp.zeros((8, 128), F32)

    block_output.settle()
    input_gradient.settle()
    for wait in pending:
        wait()
    cfg.used.append((slots.remote, slots.local))


def final_kernel(cfg, *refs):
    r = SimpleNamespace(**dict(zip(cfg.names, refs)))
    classes = cfg.classes
    local = cfg.local
    r.block_output[...] = r.out[...]
    r.input_gradient[...] = r.dx[...].astype(F32)
    norms = jnp.sqrt(r.norms[...])
    weight_norm, update_norm = norms[0:3, 0:1], norms[3:6, 0:1]
    ratio = weight_norm / update_norm
    at = iota((3, 3), 1)
    r.trust_norms[...] = jnp.where(
        at == 0, weight_norm, jnp.where(at == 1, update_norm, ratio)
    )
    sets = (
        (r.entry, r.entry_m, r.entry_q, r.entry_g, r.entry_1, r.entry_2, r.entry_w),
        (r.exit, r.exit_m, r.exit_q, r.exit_g, r.exit_1, r.exit_2, r.exit_w),
        (r.bypass, r.bypass_m, r.bypass_q, r.bypass_g, r.bypass_1, r.bypass_2, r.bypass_w),
    )
    for index, (weight, m, q, g, first, second, result) in enumerate(sets):
        master = weight[...]
        moment, square, direction = adam_update(g[...], m[...], q[...])
        update = direction + WEIGHT_DECAY * master
        first[...] = moment
        second[...] = square
        result[...] = master - MATRIX_RATE * ratio[index : index + 1] * update
    grad = r.affine_grad[0 : 2 * classes + 3, 0:local]
    moment, square, direction = adam_update(grad, r.affine_m[...], r.affine_q[...])
    r.affine_1[...] = moment
    r.affine_2[...] = square
    r.affine_w[...] = r.affine[...] - AFFINE_RATE * direction


def per_device(
    features,
    labels,
    groups,
    widths,
    entry_conv,
    entry_moment,
    entry_square,
    exit_conv,
    exit_moment,
    exit_square,
    bypass_conv,
    bypass_moment,
    bypass_square,
    norm_affine,
    norm_moment,
    norm_square,
    cotangent,
):
    n_img, n_ch = lax.axis_size("img"), lax.axis_size("ch")
    batch, local, pixels = features.shape
    chans = local * n_ch
    side = math.isqrt(pixels)
    inner = n_img // OUTER
    classes = (norm_affine.shape[0] - 3) // 2
    per = batch // n_ch
    assert (side, chans, n_ch, local, batch % n_ch) == (16, 256, 4, 64, 0) and per == 2
    rows, small = entry_conv.shape[0] * inner, bypass_conv.shape[0] * inner
    masters = (entry_conv, exit_conv, bypass_conv)
    if inner == 1:
        blocks = masters
    else:
        sets = [[o * inner + i for i in range(inner)] for o in range(OUTER)]
        blocks = tuple(
            lax.all_gather(w.astype(BF16), "img", axis=0, tiled=True, axis_index_groups=sets)
            for w in masters
        )

    vmem = pl.BlockSpec(memory_space=pltpu.VMEM)
    smem = pl.BlockSpec(memory_space=pltpu.SMEM)
    anywhere = pl.BlockSpec(memory_space=pl.ANY)
    states = dict(
        entry_m=entry_moment.T,
        entry_q=entry_square.T,
        exit_m=exit_moment.T,
        exit_q=exit_square.T,
        bypass_m=bypass_moment,
        bypass_q=bypass_square,
    )
    inputs = dict(
        labels=(labels, smem),
        groups=(groups, smem),
        widths=(widths, smem),
        features=(features, anywhere),
        cotangent=(cotangent, anywhere),
        entry=(blocks[0].T, anywhere),
        exit=(blocks[1].T, anywhere),
        bypass=(blocks[2], anywhere),
        affine=(norm_affine, anywhere),
    )
    if inner == 1:
        inputs.update({name: (value, anywhere) for name, value in states.items()})
    sds = jax.ShapeDtypeStruct
    outputs = dict(
        out=(sds(cotangent.shape, BF16), vmem),
        dx=(sds(features.shape, BF16), vmem),
        grad1=(sds((local, rows), F32), vmem),
        grad2=(sds((local, rows), F32), vmem),
        grad3=(sds((small, local), F32), vmem),
        affine_grad=(sds((24, 128), F32), vmem),
        norms=(sds((8, 128), F32), vmem),
    )
    pix = pixels * per
    taps9 = 9 * chans
    held = lambda shape, dtype=BF16: pltpu.VMEM(shape, dtype)
    scratch = dict(
        fown=held((batch, local, pixels)),
        cown=held((batch, local, 4 * pixels)),
        pass_c=held((2, local, 4 * pixels)),
        pass_o=held((2, local, 4 * pixels)),
        pass_x=held((2, local, pixels)),
        fbuf=held((n_ch, per, local, pixels)),
        cbuf=held((n_ch, per, local, 4 * pixels)),
        entry_v=held((local, rows), blocks[0].dtype),
        exit_v=held((local, rows), blocks[1].dtype),
        bypass_v=held((small, local), blocks[2].dtype),
        affine_v=held(norm_affine.shape, F32),
        padded=held((3 * local, 384)),
        wz1=held((n_ch, rows // 2, 128)),
        wz2=held((n_ch, (rows + small) // 2, 128)),
        aff_z=held((n_ch, 32, 128), F32),
        w1=held((taps9, chans)),
        w2=held((taps9, chans)),
        ws=held((chans, chans)),
        unpack=held((512, 512)),
        ident=held((256, 256)),
        shift=held((2, 256, 256)),
        gridder=held((512, 256)),
        fpm=held((pix, chans)),
        h1s=held((3, per, pixels + 32, chans)),
        h1cm=held((chans, pix)),
        y1=held((4, pix, chans), F32),
        act=held((4, pix, chans), F32),
        h2s=held((2, 4, per, pixels + 32, chans)),
        dzs=held((2, 4, per, pixels + 32, chans)),
        h2cm=held((chans, 4 * pix)),
        short=held((pix, chans), F32),
        dshort=held((pix, chans), F32),
        dzc=held((pix, chans)),
        act1=held((pix, chans), F32),
        rc=held((4, pix, chans)),
        ocm=held((per, chans, 4 * pixels)),
        dcm=held((per, chans, pixels)),
        field=held((9, per, pixels, chans)),
        dw1=held((taps9, chans), F32),
        dw2=held((taps9, chans), F32),
        dws=held((chans, chans), F32),
    )
    for number, size in ((1, rows), (2, rows + small)):
        shapes = ((4, size, chans),) * 2 + ((2, 2, size, 128),) * 2 + ((2, size, 128),) * 2
        shapes += ((n_ch, size // 2, 128),) * 2
        for part, shape in zip(PARTS, shapes):
            scratch[part + str(number)] = held(shape)
        scratch[PARTS[-1] + str(number)] = held((4, size, chans), F32)
    exchanges = [(8, chans), (8, chans), (16, chans), (32, chans)]
    if inner == 1:
        exchanges.append((8, 128))
        for v, shape in (("v1", (local, rows)), ("v2", (local, rows)), ("vs", (small, local))):
            scratch[v + "m"] = held(shape, F32)
            scratch[v + "q"] = held(shape, F32)
    for number, shape in enumerate(exchanges, 1):
        for axis, size in zip("abc", (OUTER, inner, n_ch)):
            if size > 1:
                scratch[axis + str(number)] = held((size,) + shape, F32)
    remote_count = 3 * 3 + 4 * 4 * per + 3 * 7 + 2 * 13 + len(exchanges) * (7 + 3 + inner - 1)
    scratch.update(
        send=pltpu.SemaphoreType.DMA((remote_count,)),
        recv=pltpu.SemaphoreType.DMA((remote_count,)),
        lsem=pltpu.SemaphoreType.DMA((20,)),
    )
    cfg = SimpleNamespace(
        names=[*inputs, *outputs, *scratch],
        inner=inner,
        n_ch=n_ch,
        batch=batch,
        local=local,
        classes=classes,
        count=float(batch * n_img // widths.shape[0] * pixels),
        rows=rows,
        small=small,
        used=[],
    )
    out, dx, grad1, grad2, grad3, affine_grad, norms = pl.pallas_call(
        functools.partial(main_kernel, cfg),
        out_shape=[s for s, _ in outputs.values()],
        in_specs=[s for _, s in inputs.values()],
        out_specs=[s for _, s in outputs.values()],
        scratch_shapes=list(scratch.values()),
        compiler_params=pltpu.CompilerParams(
            collective_id=0, has_side_effects=True, vmem_limit_bytes=VMEM_LIMIT
        ),
        name="block_step",
    )(*[v for v, _ in inputs.values()])
    assert max(n for n, _ in cfg.used) <= remote_count and max(n for _, n in cfg.used) <= 20

    grads = [grad1, grad2, grad3]
    if inner > 1:
        grads = [
            lax.psum_scatter(g, "img", scatter_dimension=0, axis_index_groups=sets, tiled=True)
            for g in (grad1.T, grad2.T, grad3)
        ]
        updates = []
        for w, g, m, s in zip(
            masters,
            grads,
            (entry_moment, exit_moment, bypass_moment),
            (entry_square, exit_square, bypass_square),
        ):
            updates.append(adam_update(g, m, s)[2] + WEIGHT_DECAY * w)
        sums = lax.psum(
            jnp.stack([jnp.sum(w * w) for w in masters] + [jnp.sum(u * u) for u in updates]),
            ("img", "ch"),
        )
        norms = jnp.broadcast_to(jnp.pad(sums, (0, 2))[:, None], (8, 128))
        grads = [grads[0].T, grads[1].T, grads[2]]

    args = dict(
        out=out,
        dx=dx,
        norms=norms,
        affine_grad=affine_grad,
        entry_g=grads[0],
        exit_g=grads[1],
        bypass_g=grads[2],
        entry=entry_conv.T,
        exit=exit_conv.T,
        bypass=bypass_conv,
        **states,
        affine=norm_affine,
        affine_m=norm_moment,
        affine_q=norm_square,
    )
    tall = sds(entry_conv.shape[::-1], F32)
    short, wide = (sds(w.shape, F32) for w in (bypass_conv, norm_affine))
    results = dict(
        block_output=sds(cotangent.shape, BF16),
        input_gradient=sds(features.shape, F32),
        entry_1=tall,
        entry_2=tall,
        entry_w=tall,
        exit_1=tall,
        exit_2=tall,
        exit_w=tall,
        bypass_1=short,
        bypass_2=short,
        bypass_w=short,
        affine_1=wide,
        affine_2=wide,
        affine_w=wide,
        trust_norms=sds((3, 3), F32),
    )
    end_cfg = SimpleNamespace(names=[*args, *results], classes=classes, local=local)
    final = pl.pallas_call(
        functools.partial(final_kernel, end_cfg),
        out_shape=list(results.values()),
        in_specs=[vmem] * len(args),
        out_specs=[vmem] * len(results),
        compiler_params=pltpu.CompilerParams(vmem_limit_bytes=VMEM_LIMIT),
        name="finish",
    )(*args.values())
    return tuple(v.T if s is tall else v for v, s in zip(final, results.values()))


def solution(mesh):
    wide = P("img", "ch")
    deep = P("img", "ch", None)
    table = P(None, "ch")
    return jax.shard_map(
        per_device,
        mesh=mesh,
        in_specs=(deep, P("img"), P("img"), P()) + (wide,) * 9 + (table,) * 3 + (deep,),
        out_specs=(deep, deep) + (wide,) * 9 + (table,) * 3 + (P(),),
        check_vma=False,
    )
```

```python
import functools
import math
from types import SimpleNamespace

import jax
import jax.numpy as jnp
from jax import lax
from jax.experimental import pallas as pl
from jax.experimental.pallas import tpu as pltpu
from jax.sharding import PartitionSpec as P

LEVELS = 4
STEP = 5
NORM_EPSILON = 1e-05
ADAM_EPSILON = 1e-06
MOMENT_DECAY = 0.9
SQUARE_DECAY = 0.999
WEIGHT_DECAY = 0.01
MATRIX_RATE = 0.3
AFFINE_RATE = 0.2

OUTER = 8
VMEM_LIMIT = 56 * 1024 * 1024
BF16 = jnp.bfloat16
F32 = jnp.float32
MESH = pl.DeviceIdType.MESH
PARTS = ("s1", "r1", "s2", "r2", "s3", "r3")


def nn(left, right):
    return lax.dot_general(left, right, (((1,), (0,)), ((), ())), preferred_element_type=F32)


def nt(left, right):
    return lax.dot_general(left, right, (((1,), (1,)), ((), ())), preferred_element_type=F32)


def tn(left, right):
    return lax.dot_general(left, right, (((0,), (0,)), ((), ())), preferred_element_type=F32)


def flip(index, mask):
    result = index
    for bit in range(3):
        if (mask >> bit) & 1:
            digit = lax.rem(lax.div(index, 1 << bit), 2)
            result = result + (1 - 2 * digit) * (1 << bit)
    return result


def sigmoid(value):
    return 0.5 * jnp.tanh(0.5 * value) + 0.5


def iota(shape, axis):
    return lax.broadcasted_iota(jnp.int32, shape, axis)


def to_bf16(condition):
    return jnp.where(condition, 1.0, 0.0).astype(BF16)


def pick_row(table, index):
    hit = iota(table.shape, 0) == index
    return jnp.sum(jnp.where(hit, table, 0.0), axis=0, keepdims=True)


def place_row(row, index, rows):
    hit = iota((rows, row.shape[1]), 0) == index
    return jnp.where(hit, row, 0.0)


def colsum(value):
    return jnp.sum(value, axis=0, keepdims=True)


def adam_update(grad, moment, square):
    moment_new = MOMENT_DECAY * moment + (1.0 - MOMENT_DECAY) * grad
    square_new = SQUARE_DECAY * square + (1.0 - SQUARE_DECAY) * grad * grad
    direction = (
        moment_new
        / (1.0 - MOMENT_DECAY**STEP)
        / (jnp.sqrt(square_new / (1.0 - SQUARE_DECAY**STEP)) + ADAM_EPSILON)
    )
    return (moment_new, square_new, direction)


def total(value):
    return jnp.sum(jnp.sum(value, axis=1, keepdims=True), axis=0, keepdims=True)


def main_kernel(cfg, *refs):
    r = SimpleNamespace(**dict(zip(cfg.names, refs)))
    inner, n_ch, batch, local = cfg.inner, cfg.n_ch, cfg.batch, cfg.local
    classes, count = cfg.classes, cfg.count
    per = batch // n_ch
    chans = local * n_ch
    rows, small = cfg.rows, cfg.small
    tail = (rows - 256) // 2
    hw, hs = rows // 2, small // 2
    slots = SimpleNamespace(remote=0, local=0)

    img = lax.axis_index("img")
    me = lax.axis_index("ch")
    block = lax.div(img, inner)
    within = lax.rem(img, inner)
    core = lax.rem(block, 2)
    plane = lax.div(block, 2)
    partner = flip(block, 1)

    def dev(block_id, within_id, ch_id):
        return (block_id * inner + within_id, ch_id)

    pending = []

    def post(src, dst, landed, peer):
        slot = slots.remote
        slots.remote = slot + 1
        copy = pltpu.make_async_remote_copy(
            src_ref=src,
            dst_ref=dst,
            send_sem=r.send.at[slot],
            recv_sem=r.recv.at[slot],
            device_id=peer,
            device_id_type=MESH,
        )
        copy.start()
        pending.append(copy.wait_send)
        arrival = pltpu.make_async_remote_copy(
            src_ref=landed,
            dst_ref=landed,
            send_sem=r.send.at[slot],
            recv_sem=r.recv.at[slot],
            device_id=peer,
            device_id_type=MESH,
        )
        return arrival.wait_recv

    def here(src, dst):
        slot = slots.local
        slots.local = slot + 1
        copy = pltpu.make_async_copy(src, dst, r.lsem.at[slot])
        copy.start()
        return copy.wait

    outer_peers = [flip(block, mask) for mask in range(1, OUTER)]
    ch_peers = [flip(me, mask) for mask in range(1, n_ch)]
    inner_pairs = [
        (lax.rem(within + step, inner), lax.rem(within + inner - step, inner))
        for step in range(1, inner)
    ]
    up, down, far = (lax.rem(me + step, n_ch) for step in (1, 3, 2))
    up_peer, down_peer = dev(block, within, up), dev(block, within, down)

    class Ring:
        def __init__(self, source, target, passing):
            self.target, self.passing = target, passing
            self.waits = []
            self.early = [
                post(source(far, 0), passing.at[0], passing.at[0], up_peer),
                post(source(far, 1), passing.at[1], passing.at[1], down_peer),
            ]
            for im in range(per):
                self.waits += [
                    post(source(up, im), target(me, im), target(down, im), up_peer),
                    post(source(down, im), target(me, im), target(up, im), down_peer),
                ]

        def forward(self):
            self.early[0]()
            self.waits.append(
                post(self.passing.at[0], self.target(down, 0), self.target(far, 0), up_peer)
            )
            self.early[1]()
            self.waits.append(
                post(self.passing.at[1], self.target(up, 1), self.target(far, 1), down_peer)
            )

        def settle(self):
            for wait in self.waits:
                wait()

    barrier = pltpu.get_barrier_semaphore()
    everyone = [dev(peer, within, me) for peer in outer_peers]
    everyone += [dev(block, within, peer) for peer in ch_peers]
    everyone += [dev(block, peer, me) for peer, _ in inner_pairs]
    for peer in everyone:
        pl.semaphore_signal(barrier, inc=1, device_id=peer, device_id_type=MESH)

    got_entry = here(r.entry, r.entry_v)
    got_features = here(r.features, r.fown)
    got_exit = here(r.exit, r.exit_v)
    got_bypass = here(r.bypass, r.bypass_v)
    got_affine = here(r.affine, r.affine_v)
    got_cot = here(r.cotangent, r.cown)
    states = ((r.entry_m, r.entry_q), (r.exit_m, r.exit_q), (r.bypass_m, r.bypass_q)) if inner == 1 else ()
    held = [
        (here(m, getattr(r, v + "m")), here(q, getattr(r, v + "q")))
        for (m, q), v in zip(states, ("v1", "v2", "vs"))
    ]

    s_row, s_col = iota((hw, 384), 0), iota((hw, 384), 1)
    pick_first = to_bf16(s_col == jnp.where(s_row < 128, s_row, s_row + 128))
    pick_second = to_bf16(s_col == jnp.where(s_row < 128, s_row + 128, s_row + 128 + tail))
    r.padded[...] = jnp.zeros(r.padded.shape, BF16)

    def pack_own(value):
        r.padded[local : 2 * local, 0:rows] = value.astype(BF16)
        packed = nt(pick_first, r.padded[local : 3 * local, :])
        return (packed + nt(pick_second, r.padded[0 : 2 * local, :])).astype(BF16)

    got_entry()
    r.wz1[me] = pack_own(r.entry_v[...])
    pl.semaphore_wait(barrier, len(everyone))

    def to_channels(buffer):
        return [
            post(buffer.at[me], buffer.at[me], buffer.at[peer], dev(block, within, peer))
            for peer in ch_peers
        ]

    entry_waits = to_channels(r.wz1)
    got_features()
    feature_waits = [
        post(
            r.fown.at[pl.ds(per * peer, per)],
            r.fbuf.at[me],
            r.fbuf.at[peer],
            dev(block, within, peer),
        )
        for peer in ch_peers
    ]
    r.fbuf[me] = r.fown[pl.ds(per * me, per)]
    flat = jnp.concatenate([r.fown[b] for b in range(batch)], axis=1)
    wide = flat.astype(F32)
    square = wide * wide
    square_hi = square.astype(BF16)
    square_lo = (square - square_hi.astype(F32)).astype(BF16)
    level = iota((16, 256), 0)
    first_mask = jnp.concatenate([to_bf16(level == r.groups[b]) for b in range(batch)], axis=1)
    second_mask = jnp.concatenate([to_bf16(level == r.groups[b] + 4) for b in range(batch)], axis=1)
    sums = nt(first_mask, flat) + nt(second_mask, square_hi) + nt(second_mask, square_lo)

    got_affine()
    r.aff_z[me] = jnp.zeros((32, 128), F32)
    r.aff_z[me, 0 : 2 * classes + 3, 0:local] = r.affine_v[...]
    r.aff_z[me, 24:32, 0:local] = sums[0:8]
    affine_waits = to_channels(r.aff_z)

    got_exit()
    got_bypass()
    r.wz2[me, 0:hw, :] = pack_own(r.exit_v[...])
    e_row, e_col = iota((local, 128), 0), iota((local, 128), 1)
    value = r.bypass_v[...].astype(BF16)
    r.wz2[me, hw : hw + hs, :] = (
        nn(value[:hs], to_bf16(e_col == e_row)) + nn(value[hs:], to_bf16(e_col == e_row + local))
    ).astype(BF16)

    exit_waits = to_channels(r.wz2)
    got_cot()
    cotangent = Ring(
        lambda c, im: r.cown.at[per * c + im], lambda c, im: r.cbuf.at[c, im], r.pass_c
    )

    lane = iota((512, 512), 0)
    column = iota((512, 512), 1)
    spot = 256 * ((lane >> 6) & 1) + 64 * (lane >> 7) + (lane & 63)
    r.unpack[...] = to_bf16(column == spot)

    def ordered_sum(ref, size):
        result = ref[0]
        for slot in range(1, size):
            result = result + ref[slot]
        return result

    class AllReduce:
        def __init__(self, number):
            self.over_outer, self.over_inner, self.over_ch = (
                getattr(r, axis + str(number), None) for axis in "abc"
            )

        def begin(self, value):
            ref = self.over_outer
            ref[block] = value
            self.waits = [
                post(ref.at[block], ref.at[block], ref.at[peer], dev(peer, within, me))
                for peer in outer_peers
            ]

        def plane(self):
            for wait in self.waits:
                wait()
            value = ordered_sum(self.over_outer, OUTER)
            if inner > 1:
                ref = self.over_inner
                ref[within] = value
                waits = [
                    post(ref.at[within], ref.at[within], ref.at[back], dev(block, peer, me))
                    for peer, back in inner_pairs
                ]
                for wait in waits:
                    wait()
                value = ordered_sum(ref, inner)
            return value

        def middle(self):
            self.over_ch[me] = self.plane()
            self.waits = to_channels(self.over_ch)

        def end(self):
            for wait in self.waits:
                wait()
            return ordered_sum(self.over_ch, n_ch)

    def rows_of(ref, index):
        size = ref.shape[0] // OUTER
        return ref.at[pl.ds(pl.multiple_of(size * index, 16), size)]

    def unpack_own(ref, full):
        own = rows_of(ref, block)
        if full.shape[0] == hw:
            own[0:128, :] = full[0:128, 0:256]
            own[128:256, :] = full[0:128, 256:512]
            own[256 : 256 + tail, :] = full[128:, 0:256]
            own[256 + tail :, :] = full[128:, 256:512]
        else:
            own[0:hs, :] = full[:, 0:256]
            own[hs:, :] = full[:, 256:512]

    def spread(ref):
        own = rows_of(ref, block)
        return {
            mask: post(own, own, rows_of(ref, flip(block, mask)), dev(flip(block, mask), within, me))
            for mask in (2, 4, 6, 1)
        }

    def forward(ref, waits):
        rest = [waits[1]]
        for mask in (2, 4, 6):
            waits[mask]()
            mine = rows_of(ref, flip(block, mask))
            theirs = rows_of(ref, flip(partner, mask))
            rest.append(post(mine, mine, theirs, dev(partner, within, me)))
        return rest

    def widen(buffer):
        packed = jnp.concatenate([buffer[c] for c in range(n_ch)], axis=1)
        return nn(packed, r.unpack[...]).astype(BF16)

    def wide_lanes(ref):
        parts = [
            ref[c] + pltpu.roll(ref[c + 1], local, axis=1) for c in range(0, n_ch, 2)
        ]
        return jnp.concatenate(parts, axis=1)

    for wait in affine_waits:
        wait()
    affine = wide_lanes(r.aff_z)
    input_sums = AllReduce(1)
    input_sums.begin(affine[24:32])
    for wait in entry_waits:
        wait()
    unpack_own(r.w1, widen(r.wz1))
    gather1 = spread(r.w1)

    ident = to_bf16(iota((256, 256), 0) == iota((256, 256), 1))
    r.ident[...] = ident
    q_out, q_in = iota((256, 256), 0), iota((256, 256), 1)
    r.shift[0] = to_bf16((q_in == q_out + 1) & ((q_out & 15) < 15))
    r.shift[1] = to_bf16((q_in == q_out - 1) & ((q_out & 15) > 0))

    for wait in exit_waits:
        wait()
    full = widen(r.wz2)
    unpack_own(r.w2, full[0:hw])
    unpack_own(r.ws, full[hw:])
    gather2 = spread(r.w2)
    gather3 = spread(r.ws)

    rho, px = iota((512, 256), 0), iota((512, 256), 1)
    version, a, b_ = rho >> 8, (rho >> 7) & 1, (rho >> 6) & 1
    col = (rho & 15) + version * (1 - 2 * b_)
    target = (2 * ((rho & 63) >> 4) + a) * 32 + 2 * col + b_
    r.gridder[...] = to_bf16((px == target) & (col >= 0) & (col < 16))
    zeros = jnp.zeros((16, 256), BF16)
    for im in range(per):
        for ver in range(3):
            r.h1s[ver, im, 0:16, :] = zeros
            r.h1s[ver, im, 272:288, :] = zeros
        for ver in range(2):
            for ph in range(4):
                for ref in (r.h2s, r.dzs):
                    ref[ver, ph, im, 0:16, :] = zeros
                    ref[ver, ph, im, 272:288, :] = zeros

    def channel_major(ref, im, lanes):
        return jnp.concatenate([ref[c, im, :, lanes] for c in range(n_ch)], axis=0)

    for wait in feature_waits:
        wait()
    for im in range(per):
        r.fpm[256 * im : 256 * im + 256, :] = nt(
            ident, channel_major(r.fbuf, im, slice(0, 256))
        ).astype(BF16)

    stats = input_sums.plane()
    mean1 = stats[0:4] / count
    inv1 = lax.rsqrt(stats[4:8] / count - mean1 * mean1 + NORM_EPSILON)
    gain = affine[2 * classes : 2 * classes + 1]
    shift = affine[2 * classes + 1 : 2 * classes + 2]
    out_bias = affine[2 * classes + 2 : 2 * classes + 3]
    group, label, mean1_b, inv1_b, gamma_b, beta_b, mask_b = [], [], [], [], [], [], []
    for im in range(per):
        group.append(r.groups[per * me + im])
        label.append(r.labels[per * me + im])
        mean1_b.append(pick_row(mean1, group[im]))
        inv1_b.append(pick_row(inv1, group[im]))
        gamma_b.append(pick_row(affine, label[im]))
        beta_b.append(pick_row(affine, label[im] + classes))
        width = r.widths[group[im]]
        mask_b.append(
            jnp.where(iota((1, chans), 1) < width * (chans // LEVELS), 1.0, 0.0)
        )

    for im in range(per):
        normal = (r.fpm[256 * im : 256 * im + 256, :].astype(F32) - mean1_b[im]) * inv1_b[im]
        pre = gamma_b[im] * normal + beta_b[im]
        hidden = (pre * sigmoid(pre)).astype(BF16)
        r.h1s[1, im, 16:272, :] = hidden
        r.h1s[0, im, 16:272, :] = nn(r.shift[1], hidden).astype(BF16)
        r.h1s[2, im, 16:272, :] = nn(r.shift[0], hidden).astype(BF16)
        r.h1cm[:, 256 * im : 256 * im + 256] = nt(ident, hidden).astype(BF16)

    rest = forward(r.w1, gather1)
    cotangent.forward()
    for wait in rest:
        wait()

    def back_product(parts, ref):
        result = nt(parts[0], ref[0:256, :])
        for tap in range(1, 9):
            result = result + nt(parts[tap], ref[256 * tap : 256 * tap + 256, :])
        return result

    def taps():
        return [(dy, dx) for dy in range(3) for dx in range(3)]

    def stack(pieces):
        return jnp.concatenate(pieces, axis=0)

    def conv1(phase, carry):
        a, c = lax.div(phase, 2), lax.rem(phase, 2)
        parts = []
        for dy, dx in taps():
            first = pl.multiple_of(16 * lax.div(a + dy + 1, 2), 16)
            ver = lax.div(c + dx + 1, 2)
            parts.append(
                stack([r.h1s[ver, im, pl.ds(first, 256), :] for im in range(per)])
            )
        y = nn(jnp.concatenate(parts, axis=1), r.w1[...])
        r.y1[phase] = y
        out = []
        for im in range(per):
            piece = y[256 * im : 256 * im + 256]
            out.append(carry[2 * im] + colsum(piece))
            out.append(carry[2 * im + 1] + colsum(piece * piece))
        return tuple(out)

    nought = jnp.zeros((1, chans), F32)
    mid = lax.fori_loop(0, 4, conv1, (nought,) * (2 * per))
    payload = jnp.zeros((8, chans), F32)
    for im in range(per):
        payload = payload + place_row(mid[2 * im], group[im], 8)
        payload = payload + place_row(mid[2 * im + 1], group[im] + 4, 8)
    mid_sums = AllReduce(2)
    mid_sums.begin(payload)

    rest = forward(r.w2, gather2) + forward(r.ws, gather3)
    mid_sums.middle()

    r.cbuf[me] = r.cown[pl.ds(per * me, per)]
    cotangent.settle()
    for im in range(per):
        for n in range(4):
            piece = channel_major(r.cbuf, im, slice(256 * n, 256 * n + 256))
            grid = nt(r.gridder[...], piece).astype(BF16)
            for ver in range(2):
                for ph in range(4):
                    at = 256 * ver + 64 * ph
                    r.dzs[ver, ph, im, 16 + 64 * n : 80 + 64 * n, :] = grid[at : at + 64]

    coarse = jnp.zeros((256 * per, chans), F32)
    for ph in range(4):
        coarse = coarse + stack([r.dzs[0, ph, im, 16:272, :] for im in range(per)]).astype(F32)
    bias_sum = colsum(coarse)
    r.dzc[...] = coarse.astype(BF16)

    def tap_slice(ref, a, c, dy, dx, im):
        row, colm = a + dy + 1, c + dx + 1
        first = pl.multiple_of(16 * lax.div(row, 2), 16)
        ph = 2 * lax.rem(row, 2) + lax.rem(colm, 2)
        side_step = lax.div(colm, 2) - 1
        return ref[side_step * side_step, ph, im, pl.ds(first, 256), :]

    for wait in rest:
        wait()

    def back2(phase, carry):
        a, c = lax.div(phase, 2), lax.rem(phase, 2)
        parts = [
            stack([tap_slice(r.dzs, a, c, 2 - dy, 2 - dx, im) for im in range(per)])
            for dy, dx in taps()
        ]
        r.act[phase] = back_product(parts, r.w2)
        return carry

    lax.fori_loop(0, 4, back2, 0)

    stats = mid_sums.end()
    mean2 = stats[0:4] / (4.0 * count)
    inv2 = lax.rsqrt(stats[4:8] / (4.0 * count) - mean2 * mean2 + NORM_EPSILON)
    mean2_b = [pick_row(mean2, group[im]) for im in range(per)]
    inv2_b = [pick_row(inv2, group[im]) for im in range(per)]

    def hidden2(phase, carry):
        c = lax.rem(phase, 2)
        out = []
        for im in range(per):
            span = slice(256 * im, 256 * im + 256)
            normal = (r.y1[phase, span, :] - mean2_b[im]) * inv2_b[im]
            r.y1[phase, span, :] = normal
            pre = gain * normal + shift
            sig = sigmoid(pre)
            hidden = (pre * sig * mask_b[im]).astype(BF16)
            act = r.act[phase, span, :] * (sig * (1.0 + pre * (1.0 - sig)) * mask_b[im])
            r.act[phase, span, :] = act
            out.append(carry[2 * im] + colsum(act))
            out.append(carry[2 * im + 1] + colsum(act * normal))
            r.h2s[0, phase, im, 16:272, :] = hidden
            r.h2s[1, phase, im, 16:272, :] = nn(r.shift[c], hidden).astype(BF16)
            lanes = pl.ds(pl.multiple_of(512 * phase + 256 * im, 256), 256)
            r.h2cm[:, lanes] = nt(r.ident[...], hidden).astype(BF16)
        return tuple(out)

    mid = lax.fori_loop(0, 4, hidden2, (nought,) * (2 * per))
    payload = place_row(bias_sum, 8, 16)
    for im in range(per):
        payload = payload + place_row(mid[2 * im], group[im], 16)
        payload = payload + place_row(mid[2 * im + 1], group[im] + 4, 16)
    back_sums = AllReduce(3)
    back_sums.begin(payload)

    r.short[...] = nn(r.fpm[...], r.ws[...]) + out_bias
    def conv2(phase, carry):
        a, c = lax.div(phase, 2), lax.rem(phase, 2)
        parts = [
            stack([tap_slice(r.h2s, a, c, dy, dx, im) for im in range(per)]) for dy, dx in taps()
        ]
        y = nn(jnp.concatenate(parts, axis=1), r.w2[...]) + r.short[...]
        r.rc[phase] = y.astype(BF16)
        return carry

    lax.fori_loop(0, 4, conv2, 0)
    for im in range(per):
        for n in range(4):
            first = 256 * im + 64 * n
            piece = stack([r.rc[ph, first : first + 64, :] for ph in range(4)])
            r.ocm[im, :, 256 * n : 256 * n + 256] = tn(piece, r.gridder[0:256, :]).astype(BF16)

    def own_channels(ref, index, im):
        return ref.at[im, pl.ds(pl.multiple_of(local * index, local), local), :]

    def give_back(ref, out, passing):
        for im in range(per):
            out[per * me + im] = own_channels(ref, me, im)[...]
        return Ring(
            lambda c, im: own_channels(ref, c, im), lambda c, im: out.at[per * c + im], passing
        )

    back_sums.middle()
    block_output = give_back(r.ocm, r.out, r.pass_o)

    def grad2(tap, carry):
        dy, dx = lax.div(tap, 3), lax.rem(tap, 3)
        pieces = []
        for ph in range(4):
            a, c = ph // 2, ph % 2
            for im in range(per):
                pieces.append(tap_slice(r.dzs, a, c, 2 - dy, 2 - dx, im))
        first = pl.multiple_of(256 * tap, 256)
        r.dw2[pl.ds(first, 256), :] = nn(r.h2cm[...], stack(pieces))
        return carry

    lax.fori_loop(0, 9, grad2, 0)
    for im in range(per):
        piece = channel_major(r.fbuf, im, slice(0, 256))
        grad = nn(piece, r.dzc[256 * im : 256 * im + 256, :])
        if im == 0:
            r.dws[...] = grad
        else:
            r.dws[...] = r.dws[...] + grad

    class GradSum:
        def __init__(self, number, fetch):
            self.fetch = fetch
            for part in PARTS:
                setattr(self, part, getattr(r, part + str(number)))

        def begin(self):
            self.waits = []
            for u in range(4):
                self.s1[u] = self.fetch(2 * u + 1 - core).astype(BF16)
                self.waits.append(
                    post(self.s1.at[u], self.r1.at[u], self.r1.at[u], dev(partner, within, me))
                )

        def settle(self):
            for wait in self.waits:
                wait()

        def first(self):
            for u in range(4):
                self.waits[u]()
                value = self.fetch(2 * u + core) + self.r1[u].astype(F32)
                self.s2[u] = value.astype(BF16)
            self.waits = [
                post(
                    self.s2.at[lax.div(flip(block, mask), 2)],
                    self.r2.at[plane],
                    self.r2.at[lax.div(flip(block, mask), 2)],
                    dev(flip(block, mask), within, me),
                )
                for mask in (2, 4, 6)
            ]
            self.r2[plane] = self.s2[plane]

        def second(self):
            self.settle()
            value = self.r2[0].astype(F32)
            for u in range(1, 4):
                value = value + self.r2[u].astype(F32)
            value = value.astype(BF16)
            left = [value[0:128], value[256 : 256 + tail]]
            right = [value[128:256], value[256 + tail : rows]]
            if value.shape[0] > rows:
                left.append(value[rows : rows + hs])
                right.append(value[rows + hs :])
            pair = jnp.concatenate([stack(left), stack(right)], axis=1)
            packed = nt(pair, r.unpack[...]).astype(BF16)
            for c in range(n_ch):
                self.s3[c] = packed[:, 128 * c : 128 * c + 128]
            self.r3[me] = self.s3[me]
            self.waits = [
                post(self.s3.at[peer], self.r3.at[me], self.r3.at[peer], dev(block, within, peer))
                for peer in ch_peers
            ]

        def end(self, out, out_small=None):
            self.settle()
            done = self.r3[0].astype(F32)
            for c in range(1, n_ch):
                done = done + self.r3[c].astype(F32)
            turned = done[0:128].T
            out[:, 0:128] = turned[0:local]
            out[:, 128:256] = turned[local:]
            gap = jnp.zeros((128 - tail, 128), F32)
            turned = stack([done[128 : 128 + tail], gap]).T
            ends = turned[0:local] + pltpu.roll(turned[local:], tail, axis=1)
            out[:, 256:rows] = ends[:, 0 : rows - 256]
            if out_small is not None:
                last = done[hw:]
                out_small[0:hs, :] = last[:, 0:local]
                out_small[hs:, :] = pltpu.roll(last, local, axis=1)[:, 0:local]

    def block_rows(ref, size, index):
        return ref[pl.ds(pl.multiple_of(size * index, 8), size), :]

    second = GradSum(2, lambda k: stack([block_rows(r.dw2, rows, k), block_rows(r.dws, small, k)]))
    entry = GradSum(1, lambda k: block_rows(r.dw1, rows, k))
    second.begin()
    r.dshort[...] = nt(r.dzc[...], r.ws[...])

    stats = back_sums.end()
    affine_grad2 = stats
    p1_b = [pick_row(stats[0:4], group[im]) / (4.0 * count) for im in range(per)]
    p2_b = [pick_row(stats[4:8], group[im]) / (4.0 * count) for im in range(per)]

    for im in range(per):
        span = slice(256 * im, 256 * im + 256)
        scale = gain * inv2_b[im]
        combos = []
        for a in range(2):
            grads = []
            for c in range(2):
                ph = 2 * a + c
                d = scale * (r.act[ph, span, :] - (p1_b[im] + r.y1[ph, span, :] * p2_b[im]))
                grads.append(d.astype(BF16))
            right = nn(r.shift[0], grads[0])
            left = nn(r.shift[1], grads[1])
            even, odd = grads[0].astype(F32), grads[1].astype(F32)
            combos.append((odd + right, even + odd, left + even))
        gap = jnp.zeros((16, chans), F32)
        if im == 0:
            second.first()
        for dx in range(3):
            upper, lower = combos[0][dx], combos[1][dx]
            r.field[dx, im] = (lower + stack([upper[16:], gap])).astype(BF16)
            r.field[3 + dx, im] = (upper + lower).astype(BF16)
            r.field[6 + dx, im] = (stack([gap, lower[:-16]]) + upper).astype(BF16)

    block_output.forward()

    def grad1(tap, carry):
        first = pl.multiple_of(256 * tap, 256)
        r.dw1[pl.ds(first, 256), :] = nn(
            r.h1cm[...], stack([r.field[tap, im] for im in range(per)])
        )
        return carry

    lax.fori_loop(0, 9, grad1, 0)
    entry.begin()
    second.second()

    parts = [stack([r.field[tap, im] for im in range(per)]) for tap in range(9)]
    dh1 = back_product(parts, r.w1)
    payload = jnp.zeros((32, chans), F32)
    for im in range(per):
        span = slice(256 * im, 256 * im + 256)
        normal = (r.fpm[span, :].astype(F32) - mean1_b[im]) * inv1_b[im]
        pre = gamma_b[im] * normal + beta_b[im]
        sig = sigmoid(pre)
        act = dh1[span] * (sig * (1.0 + pre * (1.0 - sig)))
        r.act1[span, :] = act
        q1, q2 = colsum(act), colsum(act * normal)
        payload = payload + place_row(q2, label[im], 32)
        payload = payload + place_row(q1, label[im] + classes, 32)
        payload = payload + place_row(gamma_b[im] * q1, group[im] + 24, 32)
        payload = payload + place_row(gamma_b[im] * q2, group[im] + 28, 32)
    last_sums = AllReduce(4)
    entry.first()
    last_sums.begin(payload)
    second.end(r.grad2, r.grad3)

    row = iota((8, 128), 0)

    def norm_rows(index, weight, grad, v):
        for wait in held[index]:
            wait()
        master = weight[...]
        _, _, direction = adam_update(
            grad[...], getattr(r, v + "m")[...], getattr(r, v + "q")[...]
        )
        update = direction + WEIGHT_DECAY * master
        rows_w = jnp.where(row == index, total(master * master), 0.0)
        return rows_w + jnp.where(row == index + 3, total(update * update), 0.0)

    if inner == 1:
        norms = norm_rows(1, r.exit_v, r.grad2, "v2") + norm_rows(2, r.bypass_v, r.grad3, "vs")
    entry.second()
    last_sums.middle()

    stats = last_sums.end()
    for im in range(per):
        span = slice(256 * im, 256 * im + 256)
        normal = (r.fpm[span, :].astype(F32) - mean1_b[im]) * inv1_b[im]
        r1 = pick_row(stats[24:28], group[im]) / count
        r2 = pick_row(stats[28:32], group[im]) / count
        grad = inv1_b[im] * (gamma_b[im] * r.act1[span, :] - (r1 + normal * r2))
        grad = (grad + r.dshort[span, :]).astype(BF16)
        r.dcm[im] = nt(r.ident[...], grad).astype(BF16)
    input_gradient = give_back(r.dcm, r.dx, r.pass_x)

    table = jnp.zeros((24, chans), F32)
    table = table + jnp.where(iota((24, chans), 0) < 2 * classes, stats[0:24], 0.0)
    table = table + place_row(colsum(affine_grad2[4:8]), 2 * classes, 24)
    table = table + place_row(colsum(affine_grad2[0:4]), 2 * classes + 1, 24)
    table = table + place_row(affine_grad2[8:9], 2 * classes + 2, 24)
    mine = jnp.zeros((24, 128), F32)
    for c in range(n_ch):
        piece = table[:, 128 * (c // 2) : 128 * (c // 2) + 128]
        if c % 2:
            piece = pltpu.roll(piece, local, axis=1)
        mine = mine + jnp.where(me == c, piece, 0.0)
    r.affine_grad[...] = mine

    if inner == 1:
        entry.end(r.grad1)
        norms = norms + norm_rows(0, r.entry_v, r.grad1, "v1")
        norm_sums = AllReduce(5)
        norm_sums.begin(norms)
        input_gradient.forward()
        norm_sums.middle()
        r.norms[...] = norm_sums.end()
    else:
        entry.end(r.grad1)
        input_gradient.forward()
        r.norms[...] = jnp.zeros((8, 128), F32)

    block_output.settle()
    input_gradient.settle()
    for wait in pending:
        wait()
    cfg.used.append((slots.remote, slots.local))


def final_kernel(cfg, *refs):
    r = SimpleNamespace(**dict(zip(cfg.names, refs)))
    classes = cfg.classes
    local = cfg.local
    r.block_output[...] = r.out[...]
    r.input_gradient[...] = r.dx[...].astype(F32)
    norms = jnp.sqrt(r.norms[...])
    weight_norm, update_norm = norms[0:3, 0:1], norms[3:6, 0:1]
    ratio = weight_norm / update_norm
    at = iota((3, 3), 1)
    r.trust_norms[...] = jnp.where(
        at == 0, weight_norm, jnp.where(at == 1, update_norm, ratio)
    )
    sets = (
        (r.entry, r.entry_m, r.entry_q, r.entry_g, r.entry_1, r.entry_2, r.entry_w),
        (r.exit, r.exit_m, r.exit_q, r.exit_g, r.exit_1, r.exit_2, r.exit_w),
        (r.bypass, r.bypass_m, r.bypass_q, r.bypass_g, r.bypass_1, r.bypass_2, r.bypass_w),
    )
    for index, (weight, m, q, g, first, second, result) in enumerate(sets):
        master = weight[...]
        moment, square, direction = adam_update(g[...], m[...], q[...])
        update = direction + WEIGHT_DECAY * master
        first[...] = moment
        second[...] = square
        result[...] = master - MATRIX_RATE * ratio[index : index + 1] * update
    grad = r.affine_grad[0 : 2 * classes + 3, 0:local]
    moment, square, direction = adam_update(grad, r.affine_m[...], r.affine_q[...])
    r.affine_1[...] = moment
    r.affine_2[...] = square
    r.affine_w[...] = r.affine[...] - AFFINE_RATE * direction


def per_device(
    features,
    labels,
    groups,
    widths,
    entry_conv,
    entry_moment,
    entry_square,
    exit_conv,
    exit_moment,
    exit_square,
    bypass_conv,
    bypass_moment,
    bypass_square,
    norm_affine,
    norm_moment,
    norm_square,
    cotangent,
):
    n_img, n_ch = lax.axis_size("img"), lax.axis_size("ch")
    batch, local, pixels = features.shape
    chans = local * n_ch
    side = math.isqrt(pixels)
    inner = n_img // OUTER
    classes = (norm_affine.shape[0] - 3) // 2
    per = batch // n_ch
    assert (side, chans, n_ch, local, batch % n_ch) == (16, 256, 4, 64, 0) and per == 2
    rows, small = entry_conv.shape[0] * inner, bypass_conv.shape[0] * inner
    masters = (entry_conv, exit_conv, bypass_conv)
    if inner == 1:
        blocks = masters
    else:
        sets = [[o * inner + i for i in range(inner)] for o in range(OUTER)]
        blocks = tuple(
            lax.all_gather(w.astype(BF16), "img", axis=0, tiled=True, axis_index_groups=sets)
            for w in masters
        )

    vmem = pl.BlockSpec(memory_space=pltpu.VMEM)
    smem = pl.BlockSpec(memory_space=pltpu.SMEM)
    anywhere = pl.BlockSpec(memory_space=pl.ANY)
    states = dict(
        entry_m=entry_moment.T,
        entry_q=entry_square.T,
        exit_m=exit_moment.T,
        exit_q=exit_square.T,
        bypass_m=bypass_moment,
        bypass_q=bypass_square,
    )
    inputs = dict(
        labels=(labels, smem),
        groups=(groups, smem),
        widths=(widths, smem),
        features=(features, anywhere),
        cotangent=(cotangent, anywhere),
        entry=(blocks[0].T, anywhere),
        exit=(blocks[1].T, anywhere),
        bypass=(blocks[2], anywhere),
        affine=(norm_affine, anywhere),
    )
    if inner == 1:
        inputs.update({name: (value, anywhere) for name, value in states.items()})
    sds = jax.ShapeDtypeStruct
    outputs = dict(
        out=(sds(cotangent.shape, BF16), vmem),
        dx=(sds(features.shape, BF16), vmem),
        grad1=(sds((local, rows), F32), vmem),
        grad2=(sds((local, rows), F32), vmem),
        grad3=(sds((small, local), F32), vmem),
        affine_grad=(sds((24, 128), F32), vmem),
        norms=(sds((8, 128), F32), vmem),
    )
    pix = pixels * per
    taps9 = 9 * chans
    held = lambda shape, dtype=BF16: pltpu.VMEM(shape, dtype)
    scratch = dict(
        fown=held((batch, local, pixels)),
        cown=held((batch, local, 4 * pixels)),
        pass_c=held((2, local, 4 * pixels)),
        pass_o=held((2, local, 4 * pixels)),
        pass_x=held((2, local, pixels)),
        fbuf=held((n_ch, per, local, pixels)),
        cbuf=held((n_ch, per, local, 4 * pixels)),
        entry_v=held((local, rows), blocks[0].dtype),
        exit_v=held((local, rows), blocks[1].dtype),
        bypass_v=held((small, local), blocks[2].dtype),
        affine_v=held(norm_affine.shape, F32),
        padded=held((3 * local, 384)),
        wz1=held((n_ch, rows // 2, 128)),
        wz2=held((n_ch, (rows + small) // 2, 128)),
        aff_z=held((n_ch, 32, 128), F32),
        w1=held((taps9, chans)),
        w2=held((taps9, chans)),
        ws=held((chans, chans)),
        unpack=held((512, 512)),
        ident=held((256, 256)),
        shift=held((2, 256, 256)),
        gridder=held((512, 256)),
        fpm=held((pix, chans)),
        h1s=held((3, per, pixels + 32, chans)),
        h1cm=held((chans, pix)),
        y1=held((4, pix, chans), F32),
        act=held((4, pix, chans), F32),
        h2s=held((2, 4, per, pixels + 32, chans)),
        dzs=held((2, 4, per, pixels + 32, chans)),
        h2cm=held((chans, 4 * pix)),
        short=held((pix, chans), F32),
        dshort=held((pix, chans), F32),
        dzc=held((pix, chans)),
        act1=held((pix, chans), F32),
        rc=held((4, pix, chans)),
        ocm=held((per, chans, 4 * pixels)),
        dcm=held((per, chans, pixels)),
        field=held((9, per, pixels, chans)),
        dw1=held((taps9, chans), F32),
        dw2=held((taps9, chans), F32),
        dws=held((chans, chans), F32),
    )
    for number, size in ((1, rows), (2, rows + small)):
        shapes = ((4, size, chans),) * 4 + ((n_ch, size // 2, 128),) * 2
        for part, shape in zip(PARTS, shapes):
            scratch[part + str(number)] = held(shape)
    exchanges = [(8, chans), (8, chans), (16, chans), (32, chans)]
    if inner == 1:
        exchanges.append((8, 128))
        for v, shape in (("v1", (local, rows)), ("v2", (local, rows)), ("vs", (small, local))):
            scratch[v + "m"] = held(shape, F32)
            scratch[v + "q"] = held(shape, F32)
    for number, shape in enumerate(exchanges, 1):
        for axis, size in zip("abc", (OUTER, inner, n_ch)):
            if size > 1:
                scratch[axis + str(number)] = held((size,) + shape, F32)
    remote_count = 3 * 3 + 4 * 4 * per + 3 * 7 + 2 * 13 + len(exchanges) * (7 + 3 + inner - 1)
    scratch.update(
        send=pltpu.SemaphoreType.DMA((remote_count,)),
        recv=pltpu.SemaphoreType.DMA((remote_count,)),
        lsem=pltpu.SemaphoreType.DMA((20,)),
    )
    cfg = SimpleNamespace(
        names=[*inputs, *outputs, *scratch],
        inner=inner,
        n_ch=n_ch,
        batch=batch,
        local=local,
        classes=classes,
        count=float(batch * n_img // widths.shape[0] * pixels),
        rows=rows,
        small=small,
        used=[],
    )
    out, dx, grad1, grad2, grad3, affine_grad, norms = pl.pallas_call(
        functools.partial(main_kernel, cfg),
        out_shape=[s for s, _ in outputs.values()],
        in_specs=[s for _, s in inputs.values()],
        out_specs=[s for _, s in outputs.values()],
        scratch_shapes=list(scratch.values()),
        compiler_params=pltpu.CompilerParams(
            collective_id=0, has_side_effects=True, vmem_limit_bytes=VMEM_LIMIT
        ),
        name="block_step",
    )(*[v for v, _ in inputs.values()])
    assert max(n for n, _ in cfg.used) <= remote_count and max(n for _, n in cfg.used) <= 20

    grads = [grad1, grad2, grad3]
    if inner > 1:
        grads = [
            lax.psum_scatter(g, "img", scatter_dimension=0, axis_index_groups=sets, tiled=True)
            for g in (grad1.T, grad2.T, grad3)
        ]
        updates = []
        for w, g, m, s in zip(
            masters,
            grads,
            (entry_moment, exit_moment, bypass_moment),
            (entry_square, exit_square, bypass_square),
        ):
            updates.append(adam_update(g, m, s)[2] + WEIGHT_DECAY * w)
        sums = lax.psum(
            jnp.stack([jnp.sum(w * w) for w in masters] + [jnp.sum(u * u) for u in updates]),
            ("img", "ch"),
        )
        norms = jnp.broadcast_to(jnp.pad(sums, (0, 2))[:, None], (8, 128))
        grads = [grads[0].T, grads[1].T, grads[2]]

    args = dict(
        out=out,
        dx=dx,
        norms=norms,
        affine_grad=affine_grad,
        entry_g=grads[0],
        exit_g=grads[1],
        bypass_g=grads[2],
        entry=entry_conv.T,
        exit=exit_conv.T,
        bypass=bypass_conv,
        **states,
        affine=norm_affine,
        affine_m=norm_moment,
        affine_q=norm_square,
    )
    tall = sds(entry_conv.shape[::-1], F32)
    short, wide = (sds(w.shape, F32) for w in (bypass_conv, norm_affine))
    results = dict(
        block_output=sds(cotangent.shape, BF16),
        input_gradient=sds(features.shape, F32),
        entry_1=tall,
        entry_2=tall,
        entry_w=tall,
        exit_1=tall,
        exit_2=tall,
        exit_w=tall,
        bypass_1=short,
        bypass_2=short,
        bypass_w=short,
        affine_1=wide,
        affine_2=wide,
        affine_w=wide,
        trust_norms=sds((3, 3), F32),
    )
    end_cfg = SimpleNamespace(names=[*args, *results], classes=classes, local=local)
    final = pl.pallas_call(
        functools.partial(final_kernel, end_cfg),
        out_shape=list(results.values()),
        in_specs=[vmem] * len(args),
        out_specs=[vmem] * len(results),
        compiler_params=pltpu.CompilerParams(vmem_limit_bytes=VMEM_LIMIT),
        name="finish",
    )(*args.values())
    return tuple(v.T if s is tall else v for v, s in zip(final, results.values()))


def solution(mesh):
    wide = P("img", "ch")
    deep = P("img", "ch", None)
    table = P(None, "ch")
    return jax.shard_map(
        per_device,
        mesh=mesh,
        in_specs=(deep, P("img"), P("img"), P()) + (wide,) * 9 + (table,) * 3 + (deep,),
        out_specs=(deep, deep) + (wide,) * 9 + (table,) * 3 + (P(),),
        check_vma=False,
    )
```

```python
import functools
import math
from types import SimpleNamespace

import jax
import jax.numpy as jnp
from jax import lax
from jax.experimental import pallas as pl
from jax.experimental.pallas import tpu as pltpu
from jax.sharding import PartitionSpec as P

LEVELS = 4
STEP = 5
NORM_EPSILON = 1e-05
ADAM_EPSILON = 1e-06
MOMENT_DECAY = 0.9
SQUARE_DECAY = 0.999
WEIGHT_DECAY = 0.01
MATRIX_RATE = 0.3
AFFINE_RATE = 0.2

OUTER = 8
VMEM_LIMIT = 56 * 1024 * 1024
BF16 = jnp.bfloat16
F32 = jnp.float32
MESH = pl.DeviceIdType.MESH
PARTS = ("s1", "r1", "s2", "r2")


def nn(left, right):
    return lax.dot_general(left, right, (((1,), (0,)), ((), ())), preferred_element_type=F32)


def nt(left, right):
    return lax.dot_general(left, right, (((1,), (1,)), ((), ())), preferred_element_type=F32)


def tn(left, right):
    return lax.dot_general(left, right, (((0,), (0,)), ((), ())), preferred_element_type=F32)


def flip(index, mask):
    result = index
    for bit in range(3):
        if (mask >> bit) & 1:
            digit = lax.rem(lax.div(index, 1 << bit), 2)
            result = result + (1 - 2 * digit) * (1 << bit)
    return result


def sigmoid(value):
    return 0.5 * jnp.tanh(0.5 * value) + 0.5


def iota(shape, axis):
    return lax.broadcasted_iota(jnp.int32, shape, axis)


def to_bf16(condition):
    return jnp.where(condition, 1.0, 0.0).astype(BF16)


def pick_row(table, index):
    hit = iota(table.shape, 0) == index
    return jnp.sum(jnp.where(hit, table, 0.0), axis=0, keepdims=True)


def place_row(row, index, rows):
    hit = iota((rows, row.shape[1]), 0) == index
    return jnp.where(hit, row, 0.0)


def colsum(value):
    return jnp.sum(value, axis=0, keepdims=True)


def adam_update(grad, moment, square):
    moment_new = MOMENT_DECAY * moment + (1.0 - MOMENT_DECAY) * grad
    square_new = SQUARE_DECAY * square + (1.0 - SQUARE_DECAY) * grad * grad
    direction = (
        moment_new
        / (1.0 - MOMENT_DECAY**STEP)
        / (jnp.sqrt(square_new / (1.0 - SQUARE_DECAY**STEP)) + ADAM_EPSILON)
    )
    return (moment_new, square_new, direction)


def total(value):
    return jnp.sum(jnp.sum(value, axis=1, keepdims=True), axis=0, keepdims=True)


def main_kernel(cfg, *refs):
    r = SimpleNamespace(**dict(zip(cfg.names, refs)))
    inner, n_ch, batch, local = cfg.inner, cfg.n_ch, cfg.batch, cfg.local
    classes, count = cfg.classes, cfg.count
    per = batch // n_ch
    chans = local * n_ch
    rows, small = cfg.rows, cfg.small
    tail = (rows - 256) // 2
    hw, hs = rows // 2, small // 2
    slots = SimpleNamespace(remote=0, local=0)

    img = lax.axis_index("img")
    me = lax.axis_index("ch")
    block = lax.div(img, inner)
    within = lax.rem(img, inner)

    def dev(block_id, within_id, ch_id):
        return (block_id * inner + within_id, ch_id)

    pending = []

    def post(src, dst, landed, peer):
        slot = slots.remote
        slots.remote = slot + 1
        copy = pltpu.make_async_remote_copy(
            src_ref=src,
            dst_ref=dst,
            send_sem=r.send.at[slot],
            recv_sem=r.recv.at[slot],
            device_id=peer,
            device_id_type=MESH,
        )
        copy.start()
        pending.append(copy.wait_send)
        arrival = pltpu.make_async_remote_copy(
            src_ref=landed,
            dst_ref=landed,
            send_sem=r.send.at[slot],
            recv_sem=r.recv.at[slot],
            device_id=peer,
            device_id_type=MESH,
        )
        return arrival.wait_recv

    def here(src, dst):
        slot = slots.local
        slots.local = slot + 1
        copy = pltpu.make_async_copy(src, dst, r.lsem.at[slot])
        copy.start()
        return copy.wait

    spread_peers = [flip(block, mask) for mask in (1, 6, 7, 2, 4, 3, 5)]
    outer_peers = [flip(block, mask) for mask in range(1, OUTER)]
    ch_peers = [flip(me, mask) for mask in range(1, n_ch)]
    inner_pairs = [
        (lax.rem(within + step, inner), lax.rem(within + inner - step, inner))
        for step in range(1, inner)
    ]
    up, down, far = (lax.rem(me + step, n_ch) for step in (1, 3, 2))
    up_peer, down_peer = dev(block, within, up), dev(block, within, down)

    class Ring:
        def __init__(self, source, target, passing):
            self.target, self.passing = target, passing
            self.waits = []
            self.early = [
                post(source(far, 0), passing.at[0], passing.at[0], up_peer),
                post(source(far, 1), passing.at[1], passing.at[1], down_peer),
            ]
            for im in range(per):
                self.waits += [
                    post(source(up, im), target(me, im), target(down, im), up_peer),
                    post(source(down, im), target(me, im), target(up, im), down_peer),
                ]

        def forward(self):
            self.early[0]()
            self.waits.append(
                post(self.passing.at[0], self.target(down, 0), self.target(far, 0), up_peer)
            )
            self.early[1]()
            self.waits.append(
                post(self.passing.at[1], self.target(up, 1), self.target(far, 1), down_peer)
            )

        def settle(self):
            for wait in self.waits:
                wait()

    barrier = pltpu.get_barrier_semaphore()
    everyone = [dev(peer, within, me) for peer in outer_peers]
    everyone += [dev(block, within, peer) for peer in ch_peers]
    everyone += [dev(block, peer, me) for peer, _ in inner_pairs]
    for peer in everyone:
        pl.semaphore_signal(barrier, inc=1, device_id=peer, device_id_type=MESH)

    got_entry = here(r.entry, r.entry_v)
    got_features = here(r.features, r.fown)
    got_exit = here(r.exit, r.exit_v)
    got_bypass = here(r.bypass, r.bypass_v)
    got_affine = here(r.affine, r.affine_v)
    got_cot = here(r.cotangent, r.cown)
    states = ((r.entry_m, r.entry_q), (r.exit_m, r.exit_q), (r.bypass_m, r.bypass_q)) if inner == 1 else ()
    held = [
        (here(m, getattr(r, v + "m")), here(q, getattr(r, v + "q")))
        for (m, q), v in zip(states, ("v1", "v2", "vs"))
    ]

    s_row, s_col = iota((hw, 384), 0), iota((hw, 384), 1)
    pick_first = to_bf16(s_col == jnp.where(s_row < 128, s_row, s_row + 128))
    pick_second = to_bf16(s_col == jnp.where(s_row < 128, s_row + 128, s_row + 128 + tail))
    r.padded[...] = jnp.zeros(r.padded.shape, BF16)

    def pack_own(value):
        r.padded[local : 2 * local, 0:rows] = value.astype(BF16)
        packed = nt(pick_first, r.padded[local : 3 * local, :])
        return (packed + nt(pick_second, r.padded[0 : 2 * local, :])).astype(BF16)

    got_entry()
    r.wz1[me] = pack_own(r.entry_v[...])
    pl.semaphore_wait(barrier, len(everyone))

    def to_channels(buffer):
        return [
            post(buffer.at[me], buffer.at[me], buffer.at[peer], dev(block, within, peer))
            for peer in ch_peers
        ]

    entry_waits = to_channels(r.wz1)
    got_features()
    feature_waits = [
        post(
            r.fown.at[pl.ds(per * peer, per)],
            r.fbuf.at[me],
            r.fbuf.at[peer],
            dev(block, within, peer),
        )
        for peer in ch_peers
    ]
    r.fbuf[me] = r.fown[pl.ds(per * me, per)]
    flat = jnp.concatenate([r.fown[b] for b in range(batch)], axis=1)
    wide = flat.astype(F32)
    square = wide * wide
    square_hi = square.astype(BF16)
    square_lo = (square - square_hi.astype(F32)).astype(BF16)
    level = iota((16, 256), 0)
    first_mask = jnp.concatenate([to_bf16(level == r.groups[b]) for b in range(batch)], axis=1)
    second_mask = jnp.concatenate([to_bf16(level == r.groups[b] + 4) for b in range(batch)], axis=1)
    sums = nt(first_mask, flat) + nt(second_mask, square_hi) + nt(second_mask, square_lo)

    got_affine()
    r.aff_z[me] = jnp.zeros((32, 128), F32)
    r.aff_z[me, 0 : 2 * classes + 3, 0:local] = r.affine_v[...]
    r.aff_z[me, 24:32, 0:local] = sums[0:8]
    affine_waits = to_channels(r.aff_z)

    got_exit()
    got_bypass()
    r.wz2[me, 0:hw, :] = pack_own(r.exit_v[...])
    e_row, e_col = iota((local, 128), 0), iota((local, 128), 1)
    value = r.bypass_v[...].astype(BF16)
    r.wz2[me, hw : hw + hs, :] = (
        nn(value[:hs], to_bf16(e_col == e_row)) + nn(value[hs:], to_bf16(e_col == e_row + local))
    ).astype(BF16)

    exit_waits = to_channels(r.wz2)
    got_cot()
    cotangent = Ring(
        lambda c, im: r.cown.at[per * c + im], lambda c, im: r.cbuf.at[c, im], r.pass_c
    )

    lane = iota((512, 512), 0)
    column = iota((512, 512), 1)
    spot = 256 * ((lane >> 6) & 1) + 64 * (lane >> 7) + (lane & 63)
    r.unpack[...] = to_bf16(column == spot)

    def ordered_sum(ref, size):
        result = ref[0]
        for slot in range(1, size):
            result = result + ref[slot]
        return result

    class AllReduce:
        def __init__(self, number):
            self.over_outer, self.over_inner, self.over_ch = (
                getattr(r, axis + str(number), None) for axis in "abc"
            )

        def begin(self, value):
            ref = self.over_outer
            ref[block] = value
            self.waits = [
                post(ref.at[block], ref.at[block], ref.at[peer], dev(peer, within, me))
                for peer in outer_peers
            ]

        def plane(self):
            for wait in self.waits:
                wait()
            value = ordered_sum(self.over_outer, OUTER)
            if inner > 1:
                ref = self.over_inner
                ref[within] = value
                waits = [
                    post(ref.at[within], ref.at[within], ref.at[back], dev(block, peer, me))
                    for peer, back in inner_pairs
                ]
                for wait in waits:
                    wait()
                value = ordered_sum(ref, inner)
            return value

        def middle(self):
            self.over_ch[me] = self.plane()
            self.waits = to_channels(self.over_ch)

        def end(self):
            for wait in self.waits:
                wait()
            return ordered_sum(self.over_ch, n_ch)

    def rows_of(ref, index):
        size = ref.shape[0] // OUTER
        return ref.at[pl.ds(pl.multiple_of(size * index, 16), size)]

    def unpack_own(ref, full):
        own = rows_of(ref, block)
        if full.shape[0] == hw:
            own[0:128, :] = full[0:128, 0:256]
            own[128:256, :] = full[0:128, 256:512]
            own[256 : 256 + tail, :] = full[128:, 0:256]
            own[256 + tail :, :] = full[128:, 256:512]
        else:
            own[0:hs, :] = full[:, 0:256]
            own[hs:, :] = full[:, 256:512]

    def spread(ref):
        own = rows_of(ref, block)
        return [
            post(own, own, rows_of(ref, peer), dev(peer, within, me)) for peer in spread_peers
        ]

    def widen(buffer):
        packed = jnp.concatenate([buffer[c] for c in range(n_ch)], axis=1)
        return nn(packed, r.unpack[...]).astype(BF16)

    def wide_lanes(ref):
        parts = [
            ref[c] + pltpu.roll(ref[c + 1], local, axis=1) for c in range(0, n_ch, 2)
        ]
        return jnp.concatenate(parts, axis=1)

    for wait in affine_waits:
        wait()
    affine = wide_lanes(r.aff_z)
    input_sums = AllReduce(1)
    input_sums.begin(affine[24:32])
    for wait in entry_waits:
        wait()
    unpack_own(r.w1, widen(r.wz1))
    gather1 = spread(r.w1)

    ident = to_bf16(iota((256, 256), 0) == iota((256, 256), 1))
    r.ident[...] = ident
    q_out, q_in = iota((256, 256), 0), iota((256, 256), 1)
    r.shift[0] = to_bf16((q_in == q_out + 1) & ((q_out & 15) < 15))
    r.shift[1] = to_bf16((q_in == q_out - 1) & ((q_out & 15) > 0))

    for wait in exit_waits:
        wait()
    full = widen(r.wz2)
    unpack_own(r.w2, full[0:hw])
    unpack_own(r.ws, full[hw:])
    gather2 = spread(r.w2)
    gather3 = spread(r.ws)

    rho, px = iota((512, 256), 0), iota((512, 256), 1)
    version, a, b_ = rho >> 8, (rho >> 7) & 1, (rho >> 6) & 1
    col = (rho & 15) + version * (1 - 2 * b_)
    target = (2 * ((rho & 63) >> 4) + a) * 32 + 2 * col + b_
    r.gridder[...] = to_bf16((px == target) & (col >= 0) & (col < 16))
    zeros = jnp.zeros((16, 256), BF16)
    for im in range(per):
        for ver in range(3):
            r.h1s[ver, im, 0:16, :] = zeros
            r.h1s[ver, im, 272:288, :] = zeros
        for ver in range(2):
            for ph in range(4):
                for ref in (r.h2s, r.dzs):
                    ref[ver, ph, im, 0:16, :] = zeros
                    ref[ver, ph, im, 272:288, :] = zeros

    def channel_major(ref, im, lanes):
        return jnp.concatenate([ref[c, im, :, lanes] for c in range(n_ch)], axis=0)

    for wait in feature_waits:
        wait()
    for im in range(per):
        r.fpm[256 * im : 256 * im + 256, :] = nt(
            ident, channel_major(r.fbuf, im, slice(0, 256))
        ).astype(BF16)

    stats = input_sums.plane()
    mean1 = stats[0:4] / count
    inv1 = lax.rsqrt(stats[4:8] / count - mean1 * mean1 + NORM_EPSILON)
    gain = affine[2 * classes : 2 * classes + 1]
    shift = affine[2 * classes + 1 : 2 * classes + 2]
    out_bias = affine[2 * classes + 2 : 2 * classes + 3]
    group, label, mean1_b, inv1_b, gamma_b, beta_b, mask_b = [], [], [], [], [], [], []
    for im in range(per):
        group.append(r.groups[per * me + im])
        label.append(r.labels[per * me + im])
        mean1_b.append(pick_row(mean1, group[im]))
        inv1_b.append(pick_row(inv1, group[im]))
        gamma_b.append(pick_row(affine, label[im]))
        beta_b.append(pick_row(affine, label[im] + classes))
        width = r.widths[group[im]]
        mask_b.append(
            jnp.where(iota((1, chans), 1) < width * (chans // LEVELS), 1.0, 0.0)
        )

    for im in range(per):
        normal = (r.fpm[256 * im : 256 * im + 256, :].astype(F32) - mean1_b[im]) * inv1_b[im]
        pre = gamma_b[im] * normal + beta_b[im]
        hidden = (pre * sigmoid(pre)).astype(BF16)
        r.h1s[1, im, 16:272, :] = hidden
        r.h1s[0, im, 16:272, :] = nn(r.shift[1], hidden).astype(BF16)
        r.h1s[2, im, 16:272, :] = nn(r.shift[0], hidden).astype(BF16)
        r.h1cm[:, 256 * im : 256 * im + 256] = nt(ident, hidden).astype(BF16)

    cotangent.forward()
    for wait in gather1:
        wait()

    def back_product(parts, ref):
        result = nt(parts[0], ref[0:256, :])
        for tap in range(1, 9):
            result = result + nt(parts[tap], ref[256 * tap : 256 * tap + 256, :])
        return result

    def taps():
        return [(dy, dx) for dy in range(3) for dx in range(3)]

    def stack(pieces):
        return jnp.concatenate(pieces, axis=0)

    def conv1(phase, carry):
        a, c = lax.div(phase, 2), lax.rem(phase, 2)
        parts = []
        for dy, dx in taps():
            first = pl.multiple_of(16 * lax.div(a + dy + 1, 2), 16)
            ver = lax.div(c + dx + 1, 2)
            parts.append(
                stack([r.h1s[ver, im, pl.ds(first, 256), :] for im in range(per)])
            )
        y = nn(jnp.concatenate(parts, axis=1), r.w1[...])
        r.y1[phase] = y
        out = []
        for im in range(per):
            piece = y[256 * im : 256 * im + 256]
            out.append(carry[2 * im] + colsum(piece))
            out.append(carry[2 * im + 1] + colsum(piece * piece))
        return tuple(out)

    nought = jnp.zeros((1, chans), F32)
    mid = lax.fori_loop(0, 4, conv1, (nought,) * (2 * per))
    payload = jnp.zeros((8, chans), F32)
    for im in range(per):
        payload = payload + place_row(mid[2 * im], group[im], 8)
        payload = payload + place_row(mid[2 * im + 1], group[im] + 4, 8)
    mid_sums = AllReduce(2)
    mid_sums.begin(payload)

    mid_sums.middle()

    r.cbuf[me] = r.cown[pl.ds(per * me, per)]
    cotangent.settle()
    for im in range(per):
        for n in range(4):
            piece = channel_major(r.cbuf, im, slice(256 * n, 256 * n + 256))
            grid = nt(r.gridder[...], piece).astype(BF16)
            for ver in range(2):
                for ph in range(4):
                    at = 256 * ver + 64 * ph
                    r.dzs[ver, ph, im, 16 + 64 * n : 80 + 64 * n, :] = grid[at : at + 64]

    coarse = jnp.zeros((256 * per, chans), F32)
    for ph in range(4):
        coarse = coarse + stack([r.dzs[0, ph, im, 16:272, :] for im in range(per)]).astype(F32)
    bias_sum = colsum(coarse)
    r.dzc[...] = coarse.astype(BF16)

    def tap_slice(ref, a, c, dy, dx, im):
        row, colm = a + dy + 1, c + dx + 1
        first = pl.multiple_of(16 * lax.div(row, 2), 16)
        ph = 2 * lax.rem(row, 2) + lax.rem(colm, 2)
        side_step = lax.div(colm, 2) - 1
        return ref[side_step * side_step, ph, im, pl.ds(first, 256), :]

    for wait in gather2 + gather3:
        wait()

    def back2(phase, carry):
        a, c = lax.div(phase, 2), lax.rem(phase, 2)
        parts = [
            stack([tap_slice(r.dzs, a, c, 2 - dy, 2 - dx, im) for im in range(per)])
            for dy, dx in taps()
        ]
        r.act[phase] = back_product(parts, r.w2)
        return carry

    lax.fori_loop(0, 4, back2, 0)

    stats = mid_sums.end()
    mean2 = stats[0:4] / (4.0 * count)
    inv2 = lax.rsqrt(stats[4:8] / (4.0 * count) - mean2 * mean2 + NORM_EPSILON)
    mean2_b = [pick_row(mean2, group[im]) for im in range(per)]
    inv2_b = [pick_row(inv2, group[im]) for im in range(per)]

    def hidden2(phase, carry):
        c = lax.rem(phase, 2)
        out = []
        for im in range(per):
            span = slice(256 * im, 256 * im + 256)
            normal = (r.y1[phase, span, :] - mean2_b[im]) * inv2_b[im]
            r.y1[phase, span, :] = normal
            pre = gain * normal + shift
            sig = sigmoid(pre)
            hidden = (pre * sig * mask_b[im]).astype(BF16)
            act = r.act[phase, span, :] * (sig * (1.0 + pre * (1.0 - sig)) * mask_b[im])
            r.act[phase, span, :] = act
            out.append(carry[2 * im] + colsum(act))
            out.append(carry[2 * im + 1] + colsum(act * normal))
            r.h2s[0, phase, im, 16:272, :] = hidden
            r.h2s[1, phase, im, 16:272, :] = nn(r.shift[c], hidden).astype(BF16)
            lanes = pl.ds(pl.multiple_of(512 * phase + 256 * im, 256), 256)
            r.h2cm[:, lanes] = nt(r.ident[...], hidden).astype(BF16)
        return tuple(out)

    mid = lax.fori_loop(0, 4, hidden2, (nought,) * (2 * per))
    payload = place_row(bias_sum, 8, 16)
    for im in range(per):
        payload = payload + place_row(mid[2 * im], group[im], 16)
        payload = payload + place_row(mid[2 * im + 1], group[im] + 4, 16)
    back_sums = AllReduce(3)
    back_sums.begin(payload)

    r.short[...] = nn(r.fpm[...], r.ws[...]) + out_bias
    def conv2(phase, carry):
        a, c = lax.div(phase, 2), lax.rem(phase, 2)
        parts = [
            stack([tap_slice(r.h2s, a, c, dy, dx, im) for im in range(per)]) for dy, dx in taps()
        ]
        y = nn(jnp.concatenate(parts, axis=1), r.w2[...]) + r.short[...]
        r.rc[phase] = y.astype(BF16)
        return carry

    lax.fori_loop(0, 4, conv2, 0)
    for im in range(per):
        for n in range(4):
            first = 256 * im + 64 * n
            piece = stack([r.rc[ph, first : first + 64, :] for ph in range(4)])
            r.ocm[im, :, 256 * n : 256 * n + 256] = tn(piece, r.gridder[0:256, :]).astype(BF16)

    def own_channels(ref, index, im):
        return ref.at[im, pl.ds(pl.multiple_of(local * index, local), local), :]

    def give_back(ref, out, passing):
        for im in range(per):
            out[per * me + im] = own_channels(ref, me, im)[...]
        return Ring(
            lambda c, im: own_channels(ref, c, im), lambda c, im: out.at[per * c + im], passing
        )

    back_sums.middle()
    block_output = give_back(r.ocm, r.out, r.pass_o)

    def grad2(tap, carry):
        dy, dx = lax.div(tap, 3), lax.rem(tap, 3)
        pieces = []
        for ph in range(4):
            a, c = ph // 2, ph % 2
            for im in range(per):
                pieces.append(tap_slice(r.dzs, a, c, 2 - dy, 2 - dx, im))
        first = pl.multiple_of(256 * tap, 256)
        r.dw2[pl.ds(first, 256), :] = nn(r.h2cm[...], stack(pieces))
        return carry

    lax.fori_loop(0, 9, grad2, 0)
    for im in range(per):
        piece = channel_major(r.fbuf, im, slice(0, 256))
        grad = nn(piece, r.dzc[256 * im : 256 * im + 256, :])
        if im == 0:
            r.dws[...] = grad
        else:
            r.dws[...] = r.dws[...] + grad

    class GradSum:
        def __init__(self, number, fetch):
            self.fetch = fetch
            for part in PARTS:
                setattr(self, part, getattr(r, part + str(number)))

        def begin(self):
            self.waits = []
            for peer in spread_peers:
                self.s1[peer] = self.fetch(peer).astype(BF16)
                self.waits.append(
                    post(self.s1.at[peer], self.r1.at[block], self.r1.at[peer], dev(peer, within, me))
                )

        def settle(self):
            for wait in self.waits:
                wait()

        def second(self):
            value = self.fetch(block)
            for wait, peer in zip(self.waits, spread_peers):
                wait()
                value = value + self.r1[peer].astype(F32)
            value = value.astype(BF16)
            left = [value[0:128], value[256 : 256 + tail]]
            right = [value[128:256], value[256 + tail : rows]]
            if value.shape[0] > rows:
                left.append(value[rows : rows + hs])
                right.append(value[rows + hs :])
            pair = jnp.concatenate([stack(left), stack(right)], axis=1)
            packed = nt(pair, r.unpack[...]).astype(BF16)
            for c in range(n_ch):
                self.s2[c] = packed[:, 128 * c : 128 * c + 128]
            self.r2[me] = self.s2[me]
            self.waits = [
                post(self.s2.at[peer], self.r2.at[me], self.r2.at[peer], dev(block, within, peer))
                for peer in ch_peers
            ]

        def end(self, out, out_small=None):
            self.settle()
            done = self.r2[0].astype(F32)
            for c in range(1, n_ch):
                done = done + self.r2[c].astype(F32)
            turned = done[0:128].T
            out[:, 0:128] = turned[0:local]
            out[:, 128:256] = turned[local:]
            gap = jnp.zeros((128 - tail, 128), F32)
            turned = stack([done[128 : 128 + tail], gap]).T
            ends = turned[0:local] + pltpu.roll(turned[local:], tail, axis=1)
            out[:, 256:rows] = ends[:, 0 : rows - 256]
            if out_small is not None:
                last = done[hw:]
                out_small[0:hs, :] = last[:, 0:local]
                out_small[hs:, :] = pltpu.roll(last, local, axis=1)[:, 0:local]

    def block_rows(ref, size, index):
        return ref[pl.ds(pl.multiple_of(size * index, 8), size), :]

    second = GradSum(2, lambda k: stack([block_rows(r.dw2, rows, k), block_rows(r.dws, small, k)]))
    entry = GradSum(1, lambda k: block_rows(r.dw1, rows, k))
    second.begin()
    r.dshort[...] = nt(r.dzc[...], r.ws[...])

    stats = back_sums.end()
    affine_grad2 = stats
    p1_b = [pick_row(stats[0:4], group[im]) / (4.0 * count) for im in range(per)]
    p2_b = [pick_row(stats[4:8], group[im]) / (4.0 * count) for im in range(per)]

    for im in range(per):
        span = slice(256 * im, 256 * im + 256)
        scale = gain * inv2_b[im]
        combos = []
        for a in range(2):
            grads = []
            for c in range(2):
                ph = 2 * a + c
                d = scale * (r.act[ph, span, :] - (p1_b[im] + r.y1[ph, span, :] * p2_b[im]))
                grads.append(d.astype(BF16))
            right = nn(r.shift[0], grads[0])
            left = nn(r.shift[1], grads[1])
            even, odd = grads[0].astype(F32), grads[1].astype(F32)
            combos.append((odd + right, even + odd, left + even))
        gap = jnp.zeros((16, chans), F32)
        for dx in range(3):
            upper, lower = combos[0][dx], combos[1][dx]
            r.field[dx, im] = (lower + stack([upper[16:], gap])).astype(BF16)
            r.field[3 + dx, im] = (upper + lower).astype(BF16)
            r.field[6 + dx, im] = (stack([gap, lower[:-16]]) + upper).astype(BF16)

    block_output.forward()

    def grad1(tap, carry):
        first = pl.multiple_of(256 * tap, 256)
        r.dw1[pl.ds(first, 256), :] = nn(
            r.h1cm[...], stack([r.field[tap, im] for im in range(per)])
        )
        return carry

    lax.fori_loop(0, 9, grad1, 0)
    entry.begin()
    second.second()

    parts = [stack([r.field[tap, im] for im in range(per)]) for tap in range(9)]
    dh1 = back_product(parts, r.w1)
    payload = jnp.zeros((32, chans), F32)
    for im in range(per):
        span = slice(256 * im, 256 * im + 256)
        normal = (r.fpm[span, :].astype(F32) - mean1_b[im]) * inv1_b[im]
        pre = gamma_b[im] * normal + beta_b[im]
        sig = sigmoid(pre)
        act = dh1[span] * (sig * (1.0 + pre * (1.0 - sig)))
        r.act1[span, :] = act
        q1, q2 = colsum(act), colsum(act * normal)
        payload = payload + place_row(q2, label[im], 32)
        payload = payload + place_row(q1, label[im] + classes, 32)
        payload = payload + place_row(gamma_b[im] * q1, group[im] + 24, 32)
        payload = payload + place_row(gamma_b[im] * q2, group[im] + 28, 32)
    last_sums = AllReduce(4)
    last_sums.begin(payload)
    second.end(r.grad2, r.grad3)

    row = iota((8, 128), 0)

    def norm_rows(index, weight, grad, v):
        for wait in held[index]:
            wait()
        master = weight[...]
        _, _, direction = adam_update(
            grad[...], getattr(r, v + "m")[...], getattr(r, v + "q")[...]
        )
        update = direction + WEIGHT_DECAY * master
        rows_w = jnp.where(row == index, total(master * master), 0.0)
        return rows_w + jnp.where(row == index + 3, total(update * update), 0.0)

    if inner == 1:
        norms = norm_rows(1, r.exit_v, r.grad2, "v2") + norm_rows(2, r.bypass_v, r.grad3, "vs")
    entry.second()
    last_sums.middle()

    stats = last_sums.end()
    for im in range(per):
        span = slice(256 * im, 256 * im + 256)
        normal = (r.fpm[span, :].astype(F32) - mean1_b[im]) * inv1_b[im]
        r1 = pick_row(stats[24:28], group[im]) / count
        r2 = pick_row(stats[28:32], group[im]) / count
        grad = inv1_b[im] * (gamma_b[im] * r.act1[span, :] - (r1 + normal * r2))
        grad = (grad + r.dshort[span, :]).astype(BF16)
        r.dcm[im] = nt(r.ident[...], grad).astype(BF16)
    input_gradient = give_back(r.dcm, r.dx, r.pass_x)

    table = jnp.zeros((24, chans), F32)
    table = table + jnp.where(iota((24, chans), 0) < 2 * classes, stats[0:24], 0.0)
    table = table + place_row(colsum(affine_grad2[4:8]), 2 * classes, 24)
    table = table + place_row(colsum(affine_grad2[0:4]), 2 * classes + 1, 24)
    table = table + place_row(affine_grad2[8:9], 2 * classes + 2, 24)
    mine = jnp.zeros((24, 128), F32)
    for c in range(n_ch):
        piece = table[:, 128 * (c // 2) : 128 * (c // 2) + 128]
        if c % 2:
            piece = pltpu.roll(piece, local, axis=1)
        mine = mine + jnp.where(me == c, piece, 0.0)
    r.affine_grad[...] = mine

    if inner == 1:
        entry.end(r.grad1)
        norms = norms + norm_rows(0, r.entry_v, r.grad1, "v1")
        norm_sums = AllReduce(5)
        norm_sums.begin(norms)
        input_gradient.forward()
        norm_sums.middle()
        r.norms[...] = norm_sums.end()
    else:
        entry.end(r.grad1)
        input_gradient.forward()
        r.norms[...] = jnp.zeros((8, 128), F32)

    block_output.settle()
    input_gradient.settle()
    for wait in pending:
        wait()
    cfg.used.append((slots.remote, slots.local))


def final_kernel(cfg, *refs):
    r = SimpleNamespace(**dict(zip(cfg.names, refs)))
    classes = cfg.classes
    local = cfg.local
    r.block_output[...] = r.out[...]
    r.input_gradient[...] = r.dx[...].astype(F32)
    norms = jnp.sqrt(r.norms[...])
    weight_norm, update_norm = norms[0:3, 0:1], norms[3:6, 0:1]
    ratio = weight_norm / update_norm
    at = iota((3, 3), 1)
    r.trust_norms[...] = jnp.where(
        at == 0, weight_norm, jnp.where(at == 1, update_norm, ratio)
    )
    sets = (
        (r.entry, r.entry_m, r.entry_q, r.entry_g, r.entry_1, r.entry_2, r.entry_w),
        (r.exit, r.exit_m, r.exit_q, r.exit_g, r.exit_1, r.exit_2, r.exit_w),
        (r.bypass, r.bypass_m, r.bypass_q, r.bypass_g, r.bypass_1, r.bypass_2, r.bypass_w),
    )
    for index, (weight, m, q, g, first, second, result) in enumerate(sets):
        master = weight[...]
        moment, square, direction = adam_update(g[...], m[...], q[...])
        update = direction + WEIGHT_DECAY * master
        first[...] = moment
        second[...] = square
        result[...] = master - MATRIX_RATE * ratio[index : index + 1] * update
    grad = r.affine_grad[0 : 2 * classes + 3, 0:local]
    moment, square, direction = adam_update(grad, r.affine_m[...], r.affine_q[...])
    r.affine_1[...] = moment
    r.affine_2[...] = square
    r.affine_w[...] = r.affine[...] - AFFINE_RATE * direction


def per_device(
    features,
    labels,
    groups,
    widths,
    entry_conv,
    entry_moment,
    entry_square,
    exit_conv,
    exit_moment,
    exit_square,
    bypass_conv,
    bypass_moment,
    bypass_square,
    norm_affine,
    norm_moment,
    norm_square,
    cotangent,
):
    n_img, n_ch = lax.axis_size("img"), lax.axis_size("ch")
    batch, local, pixels = features.shape
    chans = local * n_ch
    side = math.isqrt(pixels)
    inner = n_img // OUTER
    classes = (norm_affine.shape[0] - 3) // 2
    per = batch // n_ch
    assert (side, chans, n_ch, local, batch % n_ch) == (16, 256, 4, 64, 0) and per == 2
    rows, small = entry_conv.shape[0] * inner, bypass_conv.shape[0] * inner
    masters = (entry_conv, exit_conv, bypass_conv)
    if inner == 1:
        blocks = masters
    else:
        sets = [[o * inner + i for i in range(inner)] for o in range(OUTER)]
        blocks = tuple(
            lax.all_gather(w.astype(BF16), "img", axis=0, tiled=True, axis_index_groups=sets)
            for w in masters
        )

    vmem = pl.BlockSpec(memory_space=pltpu.VMEM)
    smem = pl.BlockSpec(memory_space=pltpu.SMEM)
    anywhere = pl.BlockSpec(memory_space=pl.ANY)
    states = dict(
        entry_m=entry_moment.T,
        entry_q=entry_square.T,
        exit_m=exit_moment.T,
        exit_q=exit_square.T,
        bypass_m=bypass_moment,
        bypass_q=bypass_square,
    )
    inputs = dict(
        labels=(labels, smem),
        groups=(groups, smem),
        widths=(widths, smem),
        features=(features, anywhere),
        cotangent=(cotangent, anywhere),
        entry=(blocks[0].T, anywhere),
        exit=(blocks[1].T, anywhere),
        bypass=(blocks[2], anywhere),
        affine=(norm_affine, anywhere),
    )
    if inner == 1:
        inputs.update({name: (value, anywhere) for name, value in states.items()})
    sds = jax.ShapeDtypeStruct
    outputs = dict(
        out=(sds(cotangent.shape, BF16), vmem),
        dx=(sds(features.shape, BF16), vmem),
        grad1=(sds((local, rows), F32), vmem),
        grad2=(sds((local, rows), F32), vmem),
        grad3=(sds((small, local), F32), vmem),
        affine_grad=(sds((24, 128), F32), vmem),
        norms=(sds((8, 128), F32), vmem),
    )
    pix = pixels * per
    taps9 = 9 * chans
    held = lambda shape, dtype=BF16: pltpu.VMEM(shape, dtype)
    scratch = dict(
        fown=held((batch, local, pixels)),
        cown=held((batch, local, 4 * pixels)),
        pass_c=held((2, local, 4 * pixels)),
        pass_o=held((2, local, 4 * pixels)),
        pass_x=held((2, local, pixels)),
        fbuf=held((n_ch, per, local, pixels)),
        cbuf=held((n_ch, per, local, 4 * pixels)),
        entry_v=held((local, rows), blocks[0].dtype),
        exit_v=held((local, rows), blocks[1].dtype),
        bypass_v=held((small, local), blocks[2].dtype),
        affine_v=held(norm_affine.shape, F32),
        padded=held((3 * local, 384)),
        wz1=held((n_ch, rows // 2, 128)),
        wz2=held((n_ch, (rows + small) // 2, 128)),
        aff_z=held((n_ch, 32, 128), F32),
        w1=held((taps9, chans)),
        w2=held((taps9, chans)),
        ws=held((chans, chans)),
        unpack=held((512, 512)),
        ident=held((256, 256)),
        shift=held((2, 256, 256)),
        gridder=held((512, 256)),
        fpm=held((pix, chans)),
        h1s=held((3, per, pixels + 32, chans)),
        h1cm=held((chans, pix)),
        y1=held((4, pix, chans), F32),
        act=held((4, pix, chans), F32),
        h2s=held((2, 4, per, pixels + 32, chans)),
        dzs=held((2, 4, per, pixels + 32, chans)),
        h2cm=held((chans, 4 * pix)),
        short=held((pix, chans), F32),
        dshort=held((pix, chans), F32),
        dzc=held((pix, chans)),
        act1=held((pix, chans), F32),
        rc=held((4, pix, chans)),
        ocm=held((per, chans, 4 * pixels)),
        dcm=held((per, chans, pixels)),
        field=held((9, per, pixels, chans)),
        dw1=held((taps9, chans), F32),
        dw2=held((taps9, chans), F32),
        dws=held((chans, chans), F32),
    )
    for number, size in ((1, rows), (2, rows + small)):
        shapes = ((OUTER, size, chans),) * 2 + ((n_ch, size // 2, 128),) * 2
        for part, shape in zip(PARTS, shapes):
            scratch[part + str(number)] = held(shape)
    exchanges = [(8, chans), (8, chans), (16, chans), (32, chans)]
    if inner == 1:
        exchanges.append((8, 128))
        for v, shape in (("v1", (local, rows)), ("v2", (local, rows)), ("vs", (small, local))):
            scratch[v + "m"] = held(shape, F32)
            scratch[v + "q"] = held(shape, F32)
    for number, shape in enumerate(exchanges, 1):
        for axis, size in zip("abc", (OUTER, inner, n_ch)):
            if size > 1:
                scratch[axis + str(number)] = held((size,) + shape, F32)
    remote_count = 3 * 3 + 4 * 4 * per + 3 * 7 + 2 * 13 + len(exchanges) * (7 + 3 + inner - 1)
    scratch.update(
        send=pltpu.SemaphoreType.DMA((remote_count,)),
        recv=pltpu.SemaphoreType.DMA((remote_count,)),
        lsem=pltpu.SemaphoreType.DMA((20,)),
    )
    cfg = SimpleNamespace(
        names=[*inputs, *outputs, *scratch],
        inner=inner,
        n_ch=n_ch,
        batch=batch,
        local=local,
        classes=classes,
        count=float(batch * n_img // widths.shape[0] * pixels),
        rows=rows,
        small=small,
        used=[],
    )
    out, dx, grad1, grad2, grad3, affine_grad, norms = pl.pallas_call(
        functools.partial(main_kernel, cfg),
        out_shape=[s for s, _ in outputs.values()],
        in_specs=[s for _, s in inputs.values()],
        out_specs=[s for _, s in outputs.values()],
        scratch_shapes=list(scratch.values()),
        compiler_params=pltpu.CompilerParams(
            collective_id=0, has_side_effects=True, vmem_limit_bytes=VMEM_LIMIT
        ),
        name="block_step",
    )(*[v for v, _ in inputs.values()])
    assert max(n for n, _ in cfg.used) <= remote_count and max(n for _, n in cfg.used) <= 20

    grads = [grad1, grad2, grad3]
    if inner > 1:
        grads = [
            lax.psum_scatter(g, "img", scatter_dimension=0, axis_index_groups=sets, tiled=True)
            for g in (grad1.T, grad2.T, grad3)
        ]
        updates = []
        for w, g, m, s in zip(
            masters,
            grads,
            (entry_moment, exit_moment, bypass_moment),
            (entry_square, exit_square, bypass_square),
        ):
            updates.append(adam_update(g, m, s)[2] + WEIGHT_DECAY * w)
        sums = lax.psum(
            jnp.stack([jnp.sum(w * w) for w in masters] + [jnp.sum(u * u) for u in updates]),
            ("img", "ch"),
        )
        norms = jnp.broadcast_to(jnp.pad(sums, (0, 2))[:, None], (8, 128))
        grads = [grads[0].T, grads[1].T, grads[2]]

    args = dict(
        out=out,
        dx=dx,
        norms=norms,
        affine_grad=affine_grad,
        entry_g=grads[0],
        exit_g=grads[1],
        bypass_g=grads[2],
        entry=entry_conv.T,
        exit=exit_conv.T,
        bypass=bypass_conv,
        **states,
        affine=norm_affine,
        affine_m=norm_moment,
        affine_q=norm_square,
    )
    tall = sds(entry_conv.shape[::-1], F32)
    short, wide = (sds(w.shape, F32) for w in (bypass_conv, norm_affine))
    results = dict(
        block_output=sds(cotangent.shape, BF16),
        input_gradient=sds(features.shape, F32),
        entry_1=tall,
        entry_2=tall,
        entry_w=tall,
        exit_1=tall,
        exit_2=tall,
        exit_w=tall,
        bypass_1=short,
        bypass_2=short,
        bypass_w=short,
        affine_1=wide,
        affine_2=wide,
        affine_w=wide,
        trust_norms=sds((3, 3), F32),
    )
    end_cfg = SimpleNamespace(names=[*args, *results], classes=classes, local=local)
    final = pl.pallas_call(
        functools.partial(final_kernel, end_cfg),
        out_shape=list(results.values()),
        in_specs=[vmem] * len(args),
        out_specs=[vmem] * len(results),
        compiler_params=pltpu.CompilerParams(vmem_limit_bytes=VMEM_LIMIT),
        name="finish",
    )(*args.values())
    return tuple(v.T if s is tall else v for v, s in zip(final, results.values()))


def solution(mesh):
    wide = P("img", "ch")
    deep = P("img", "ch", None)
    table = P(None, "ch")
    return jax.shard_map(
        per_device,
        mesh=mesh,
        in_specs=(deep, P("img"), P("img"), P()) + (wide,) * 9 + (table,) * 3 + (deep,),
        out_specs=(deep, deep) + (wide,) * 9 + (table,) * 3 + (P(),),
        check_vma=False,
    )
```

```python
import functools
import math
from types import SimpleNamespace

import jax
import jax.numpy as jnp
from jax import lax
from jax.experimental import pallas as pl
from jax.experimental.pallas import tpu as pltpu
from jax.sharding import PartitionSpec as P

LEVELS = 4
STEP = 5
NORM_EPSILON = 1e-05
ADAM_EPSILON = 1e-06
MOMENT_DECAY = 0.9
SQUARE_DECAY = 0.999
WEIGHT_DECAY = 0.01
MATRIX_RATE = 0.3
AFFINE_RATE = 0.2

OUTER = 8
VMEM_LIMIT = 56 * 1024 * 1024
BF16 = jnp.bfloat16
F32 = jnp.float32
MESH = pl.DeviceIdType.MESH
PARTS = ("s1", "r1", "s2", "r2", "s3", "r3")


def nn(left, right):
    return lax.dot_general(left, right, (((1,), (0,)), ((), ())), preferred_element_type=F32)


def nt(left, right):
    return lax.dot_general(left, right, (((1,), (1,)), ((), ())), preferred_element_type=F32)


def tn(left, right):
    return lax.dot_general(left, right, (((0,), (0,)), ((), ())), preferred_element_type=F32)


def flip(index, mask):
    result = index
    for bit in range(3):
        if (mask >> bit) & 1:
            digit = lax.rem(lax.div(index, 1 << bit), 2)
            result = result + (1 - 2 * digit) * (1 << bit)
    return result


def sigmoid(value):
    return 0.5 * jnp.tanh(0.5 * value) + 0.5


def iota(shape, axis):
    return lax.broadcasted_iota(jnp.int32, shape, axis)


def to_bf16(condition):
    return jnp.where(condition, 1.0, 0.0).astype(BF16)


def pick_row(table, index):
    hit = iota(table.shape, 0) == index
    return jnp.sum(jnp.where(hit, table, 0.0), axis=0, keepdims=True)


def place_row(row, index, rows):
    hit = iota((rows, row.shape[1]), 0) == index
    return jnp.where(hit, row, 0.0)


def colsum(value):
    return jnp.sum(value, axis=0, keepdims=True)


def adam_update(grad, moment, square):
    moment_new = MOMENT_DECAY * moment + (1.0 - MOMENT_DECAY) * grad
    square_new = SQUARE_DECAY * square + (1.0 - SQUARE_DECAY) * grad * grad
    direction = (
        moment_new
        / (1.0 - MOMENT_DECAY**STEP)
        / (jnp.sqrt(square_new / (1.0 - SQUARE_DECAY**STEP)) + ADAM_EPSILON)
    )
    return (moment_new, square_new, direction)


def total(value):
    return jnp.sum(jnp.sum(value, axis=1, keepdims=True), axis=0, keepdims=True)


def main_kernel(cfg, *refs):
    r = SimpleNamespace(**dict(zip(cfg.names, refs)))
    inner, n_ch, batch, local = cfg.inner, cfg.n_ch, cfg.batch, cfg.local
    classes, count = cfg.classes, cfg.count
    per = batch // n_ch
    chans = local * n_ch
    rows, small = cfg.rows, cfg.small
    tail = (rows - 256) // 2
    hw, hs = rows // 2, small // 2
    slots = SimpleNamespace(remote=0, local=0)

    img = lax.axis_index("img")
    me = lax.axis_index("ch")
    block = lax.div(img, inner)
    within = lax.rem(img, inner)
    core = lax.rem(block, 2)
    plane = lax.div(block, 2)
    partner = flip(block, 1)

    def dev(block_id, within_id, ch_id):
        return (block_id * inner + within_id, ch_id)

    pending = []

    def post(src, dst, landed, peer):
        slot = slots.remote
        slots.remote = slot + 1
        copy = pltpu.make_async_remote_copy(
            src_ref=src,
            dst_ref=dst,
            send_sem=r.send.at[slot],
            recv_sem=r.recv.at[slot],
            device_id=peer,
            device_id_type=MESH,
        )
        copy.start()
        pending.append(copy.wait_send)
        arrival = pltpu.make_async_remote_copy(
            src_ref=landed,
            dst_ref=landed,
            send_sem=r.send.at[slot],
            recv_sem=r.recv.at[slot],
            device_id=peer,
            device_id_type=MESH,
        )
        return arrival.wait_recv

    def here(src, dst):
        slot = slots.local
        slots.local = slot + 1
        copy = pltpu.make_async_copy(src, dst, r.lsem.at[slot])
        copy.start()
        return copy.wait

    outer_peers = [flip(block, mask) for mask in range(1, OUTER)]
    ch_peers = [flip(me, mask) for mask in range(1, n_ch)]
    inner_pairs = [
        (lax.rem(within + step, inner), lax.rem(within + inner - step, inner))
        for step in range(1, inner)
    ]
    up, down, far = (lax.rem(me + step, n_ch) for step in (1, 3, 2))
    up_peer, down_peer = dev(block, within, up), dev(block, within, down)

    class Ring:
        def __init__(self, source, target, passing):
            self.target, self.passing = target, passing
            self.waits = []
            self.early = [
                post(source(far, 0), passing.at[0], passing.at[0], up_peer),
                post(source(far, 1), passing.at[1], passing.at[1], down_peer),
            ]
            for im in range(per):
                self.waits += [
                    post(source(up, im), target(me, im), target(down, im), up_peer),
                    post(source(down, im), target(me, im), target(up, im), down_peer),
                ]

        def forward(self):
            self.early[0]()
            self.waits.append(
                post(self.passing.at[0], self.target(down, 0), self.target(far, 0), up_peer)
            )
            self.early[1]()
            self.waits.append(
                post(self.passing.at[1], self.target(up, 1), self.target(far, 1), down_peer)
            )

        def settle(self):
            for wait in self.waits:
                wait()

    barrier = pltpu.get_barrier_semaphore()
    everyone = [dev(peer, within, me) for peer in outer_peers]
    everyone += [dev(block, within, peer) for peer in ch_peers]
    everyone += [dev(block, peer, me) for peer, _ in inner_pairs]
    for peer in everyone:
        pl.semaphore_signal(barrier, inc=1, device_id=peer, device_id_type=MESH)

    got_entry = here(r.entry, r.entry_v)
    got_features = here(r.features, r.fown)
    got_exit = here(r.exit, r.exit_v)
    got_bypass = here(r.bypass, r.bypass_v)
    got_affine = here(r.affine, r.affine_v)
    got_cot = here(r.cotangent, r.cown)
    states = ((r.entry_m, r.entry_q), (r.exit_m, r.exit_q), (r.bypass_m, r.bypass_q)) if inner == 1 else ()
    held = [
        (here(m, getattr(r, v + "m")), here(q, getattr(r, v + "q")))
        for (m, q), v in zip(states, ("v1", "v2", "vs"))
    ]

    s_row, s_col = iota((hw, 384), 0), iota((hw, 384), 1)
    pick_first = to_bf16(s_col == jnp.where(s_row < 128, s_row, s_row + 128))
    pick_second = to_bf16(s_col == jnp.where(s_row < 128, s_row + 128, s_row + 128 + tail))
    r.padded[...] = jnp.zeros(r.padded.shape, BF16)

    def pack_own(value):
        r.padded[local : 2 * local, 0:rows] = value.astype(BF16)
        packed = nt(pick_first, r.padded[local : 3 * local, :])
        return (packed + nt(pick_second, r.padded[0 : 2 * local, :])).astype(BF16)

    got_entry()
    r.wz1[me] = pack_own(r.entry_v[...])
    pl.semaphore_wait(barrier, len(everyone))

    def to_channels(buffer):
        return [
            post(buffer.at[me], buffer.at[me], buffer.at[peer], dev(block, within, peer))
            for peer in ch_peers
        ]

    entry_waits = to_channels(r.wz1)
    got_features()
    feature_waits = [
        post(
            r.fown.at[pl.ds(per * peer, per)],
            r.fbuf.at[me],
            r.fbuf.at[peer],
            dev(block, within, peer),
        )
        for peer in ch_peers
    ]
    r.fbuf[me] = r.fown[pl.ds(per * me, per)]
    flat = jnp.concatenate([r.fown[b] for b in range(batch)], axis=1)
    wide = flat.astype(F32)
    square = wide * wide
    square_hi = square.astype(BF16)
    square_lo = (square - square_hi.astype(F32)).astype(BF16)
    level = iota((16, 256), 0)
    first_mask = jnp.concatenate([to_bf16(level == r.groups[b]) for b in range(batch)], axis=1)
    second_mask = jnp.concatenate([to_bf16(level == r.groups[b] + 4) for b in range(batch)], axis=1)
    sums = nt(first_mask, flat) + nt(second_mask, square_hi) + nt(second_mask, square_lo)

    got_affine()
    r.aff_z[me] = jnp.zeros((32, 128), F32)
    r.aff_z[me, 0 : 2 * classes + 3, 0:local] = r.affine_v[...]
    r.aff_z[me, 24:32, 0:local] = sums[0:8]
    affine_waits = to_channels(r.aff_z)

    got_exit()
    got_bypass()
    r.wz2[me, 0:hw, :] = pack_own(r.exit_v[...])
    e_row, e_col = iota((local, 128), 0), iota((local, 128), 1)
    value = r.bypass_v[...].astype(BF16)
    r.wz2[me, hw : hw + hs, :] = (
        nn(value[:hs], to_bf16(e_col == e_row)) + nn(value[hs:], to_bf16(e_col == e_row + local))
    ).astype(BF16)

    exit_waits = to_channels(r.wz2)
    got_cot()
    cotangent = Ring(
        lambda c, im: r.cown.at[per * c + im], lambda c, im: r.cbuf.at[c, im], r.pass_c
    )

    lane = iota((512, 512), 0)
    column = iota((512, 512), 1)
    spot = 256 * ((lane >> 6) & 1) + 64 * (lane >> 7) + (lane & 63)
    r.unpack[...] = to_bf16(column == spot)

    def ordered_sum(ref, size):
        result = ref[0]
        for slot in range(1, size):
            result = result + ref[slot]
        return result

    class AllReduce:
        def __init__(self, number):
            self.over_outer, self.over_inner, self.over_ch = (
                getattr(r, axis + str(number), None) for axis in "abc"
            )

        def begin(self, value):
            ref = self.over_outer
            ref[block] = value
            self.waits = [
                post(ref.at[block], ref.at[block], ref.at[peer], dev(peer, within, me))
                for peer in outer_peers
            ]

        def plane(self):
            for wait in self.waits:
                wait()
            value = ordered_sum(self.over_outer, OUTER)
            if inner > 1:
                ref = self.over_inner
                ref[within] = value
                waits = [
                    post(ref.at[within], ref.at[within], ref.at[back], dev(block, peer, me))
                    for peer, back in inner_pairs
                ]
                for wait in waits:
                    wait()
                value = ordered_sum(ref, inner)
            return value

        def middle(self):
            self.over_ch[me] = self.plane()
            self.waits = to_channels(self.over_ch)

        def end(self):
            for wait in self.waits:
                wait()
            return ordered_sum(self.over_ch, n_ch)

    def rows_of(ref, index):
        size = ref.shape[0] // OUTER
        return ref.at[pl.ds(pl.multiple_of(size * index, 16), size)]

    def unpack_own(ref, full):
        own = rows_of(ref, block)
        if full.shape[0] == hw:
            own[0:128, :] = full[0:128, 0:256]
            own[128:256, :] = full[0:128, 256:512]
            own[256 : 256 + tail, :] = full[128:, 0:256]
            own[256 + tail :, :] = full[128:, 256:512]
        else:
            own[0:hs, :] = full[:, 0:256]
            own[hs:, :] = full[:, 256:512]

    def spread(ref):
        own = rows_of(ref, block)
        return {
            mask: post(own, own, rows_of(ref, flip(block, mask)), dev(flip(block, mask), within, me))
            for mask in (2, 4, 6, 1)
        }

    def forward(ref, waits):
        rest = [waits[1]]
        for mask in (2, 4, 6):
            waits[mask]()
            mine = rows_of(ref, flip(block, mask))
            theirs = rows_of(ref, flip(partner, mask))
            rest.append(post(mine, mine, theirs, dev(partner, within, me)))
        return rest

    def widen(buffer):
        packed = jnp.concatenate([buffer[c] for c in range(n_ch)], axis=1)
        return nn(packed, r.unpack[...]).astype(BF16)

    def wide_lanes(ref):
        parts = [
            ref[c] + pltpu.roll(ref[c + 1], local, axis=1) for c in range(0, n_ch, 2)
        ]
        return jnp.concatenate(parts, axis=1)

    for wait in affine_waits:
        wait()
    affine = wide_lanes(r.aff_z)
    input_sums = AllReduce(1)
    input_sums.begin(affine[24:32])
    for wait in entry_waits:
        wait()
    unpack_own(r.w1, widen(r.wz1))
    gather1 = spread(r.w1)

    ident = to_bf16(iota((256, 256), 0) == iota((256, 256), 1))
    r.ident[...] = ident
    q_out, q_in = iota((256, 256), 0), iota((256, 256), 1)
    r.shift[0] = to_bf16((q_in == q_out + 1) & ((q_out & 15) < 15))
    r.shift[1] = to_bf16((q_in == q_out - 1) & ((q_out & 15) > 0))

    for wait in exit_waits:
        wait()
    full = widen(r.wz2)
    unpack_own(r.w2, full[0:hw])
    unpack_own(r.ws, full[hw:])
    gather2 = spread(r.w2)
    gather3 = spread(r.ws)

    rho, px = iota((512, 256), 0), iota((512, 256), 1)
    version, a, b_ = rho >> 8, (rho >> 7) & 1, (rho >> 6) & 1
    col = (rho & 15) + version * (1 - 2 * b_)
    target = (2 * ((rho & 63) >> 4) + a) * 32 + 2 * col + b_
    r.gridder[...] = to_bf16((px == target) & (col >= 0) & (col < 16))
    zeros = jnp.zeros((16, 256), BF16)
    for im in range(per):
        for ver in range(3):
            r.h1s[ver, im, 0:16, :] = zeros
            r.h1s[ver, im, 272:288, :] = zeros
        for ver in range(2):
            for ph in range(4):
                for ref in (r.h2s, r.dzs):
                    ref[ver, ph, im, 0:16, :] = zeros
                    ref[ver, ph, im, 272:288, :] = zeros

    def channel_major(ref, im, lanes):
        return jnp.concatenate([ref[c, im, :, lanes] for c in range(n_ch)], axis=0)

    for wait in feature_waits:
        wait()
    for im in range(per):
        r.fpm[256 * im : 256 * im + 256, :] = nt(
            ident, channel_major(r.fbuf, im, slice(0, 256))
        ).astype(BF16)

    stats = input_sums.plane()
    mean1 = stats[0:4] / count
    inv1 = lax.rsqrt(stats[4:8] / count - mean1 * mean1 + NORM_EPSILON)
    gain = affine[2 * classes : 2 * classes + 1]
    shift = affine[2 * classes + 1 : 2 * classes + 2]
    out_bias = affine[2 * classes + 2 : 2 * classes + 3]
    group, label, mean1_b, inv1_b, gamma_b, beta_b, mask_b = [], [], [], [], [], [], []
    for im in range(per):
        group.append(r.groups[per * me + im])
        label.append(r.labels[per * me + im])
        mean1_b.append(pick_row(mean1, group[im]))
        inv1_b.append(pick_row(inv1, group[im]))
        gamma_b.append(pick_row(affine, label[im]))
        beta_b.append(pick_row(affine, label[im] + classes))
        width = r.widths[group[im]]
        mask_b.append(
            jnp.where(iota((1, chans), 1) < width * (chans // LEVELS), 1.0, 0.0)
        )

    for im in range(per):
        normal = (r.fpm[256 * im : 256 * im + 256, :].astype(F32) - mean1_b[im]) * inv1_b[im]
        pre = gamma_b[im] * normal + beta_b[im]
        hidden = (pre * sigmoid(pre)).astype(BF16)
        r.h1s[1, im, 16:272, :] = hidden
        r.h1s[0, im, 16:272, :] = nn(r.shift[1], hidden).astype(BF16)
        r.h1s[2, im, 16:272, :] = nn(r.shift[0], hidden).astype(BF16)
        r.h1cm[:, 256 * im : 256 * im + 256] = nt(ident, hidden).astype(BF16)

    rest = forward(r.w1, gather1)
    cotangent.forward()
    for wait in rest:
        wait()

    def back_product(parts, ref):
        result = nt(parts[0], ref[0:256, :])
        for tap in range(1, 9):
            result = result + nt(parts[tap], ref[256 * tap : 256 * tap + 256, :])
        return result

    def taps():
        return [(dy, dx) for dy in range(3) for dx in range(3)]

    def stack(pieces):
        return jnp.concatenate(pieces, axis=0)

    def conv1(phase, carry):
        a, c = lax.div(phase, 2), lax.rem(phase, 2)
        parts = []
        for dy, dx in taps():
            first = pl.multiple_of(16 * lax.div(a + dy + 1, 2), 16)
            ver = lax.div(c + dx + 1, 2)
            parts.append(
                stack([r.h1s[ver, im, pl.ds(first, 256), :] for im in range(per)])
            )
        y = nn(jnp.concatenate(parts, axis=1), r.w1[...])
        r.y1[phase] = y
        out = []
        for im in range(per):
            piece = y[256 * im : 256 * im + 256]
            out.append(carry[2 * im] + colsum(piece))
            out.append(carry[2 * im + 1] + colsum(piece * piece))
        return tuple(out)

    nought = jnp.zeros((1, chans), F32)
    mid = lax.fori_loop(0, 4, conv1, (nought,) * (2 * per))
    payload = jnp.zeros((8, chans), F32)
    for im in range(per):
        payload = payload + place_row(mid[2 * im], group[im], 8)
        payload = payload + place_row(mid[2 * im + 1], group[im] + 4, 8)
    mid_sums = AllReduce(2)
    mid_sums.begin(payload)

    rest = forward(r.w2, gather2) + forward(r.ws, gather3)
    mid_sums.middle()

    r.cbuf[me] = r.cown[pl.ds(per * me, per)]
    cotangent.settle()
    for im in range(per):
        for n in range(4):
            piece = channel_major(r.cbuf, im, slice(256 * n, 256 * n + 256))
            grid = nt(r.gridder[...], piece).astype(BF16)
            for ver in range(2):
                for ph in range(4):
                    at = 256 * ver + 64 * ph
                    r.dzs[ver, ph, im, 16 + 64 * n : 80 + 64 * n, :] = grid[at : at + 64]

    coarse = jnp.zeros((256 * per, chans), F32)
    for ph in range(4):
        coarse = coarse + stack([r.dzs[0, ph, im, 16:272, :] for im in range(per)]).astype(F32)
    bias_sum = colsum(coarse)
    r.dzc[...] = coarse.astype(BF16)

    def tap_slice(ref, a, c, dy, dx, im):
        row, colm = a + dy + 1, c + dx + 1
        first = pl.multiple_of(16 * lax.div(row, 2), 16)
        ph = 2 * lax.rem(row, 2) + lax.rem(colm, 2)
        side_step = lax.div(colm, 2) - 1
        return ref[side_step * side_step, ph, im, pl.ds(first, 256), :]

    for wait in rest:
        wait()

    def back2(phase, carry):
        a, c = lax.div(phase, 2), lax.rem(phase, 2)
        parts = [
            stack([tap_slice(r.dzs, a, c, 2 - dy, 2 - dx, im) for im in range(per)])
            for dy, dx in taps()
        ]
        r.act[phase] = back_product(parts, r.w2)
        return carry

    lax.fori_loop(0, 4, back2, 0)

    stats = mid_sums.end()
    mean2 = stats[0:4] / (4.0 * count)
    inv2 = lax.rsqrt(stats[4:8] / (4.0 * count) - mean2 * mean2 + NORM_EPSILON)
    mean2_b = [pick_row(mean2, group[im]) for im in range(per)]
    inv2_b = [pick_row(inv2, group[im]) for im in range(per)]

    def hidden2(phase, carry):
        c = lax.rem(phase, 2)
        out = []
        for im in range(per):
            span = slice(256 * im, 256 * im + 256)
            normal = (r.y1[phase, span, :] - mean2_b[im]) * inv2_b[im]
            r.y1[phase, span, :] = normal
            pre = gain * normal + shift
            sig = sigmoid(pre)
            hidden = (pre * sig * mask_b[im]).astype(BF16)
            act = r.act[phase, span, :] * (sig * (1.0 + pre * (1.0 - sig)) * mask_b[im])
            r.act[phase, span, :] = act
            out.append(carry[2 * im] + colsum(act))
            out.append(carry[2 * im + 1] + colsum(act * normal))
            r.h2s[0, phase, im, 16:272, :] = hidden
            r.h2s[1, phase, im, 16:272, :] = nn(r.shift[c], hidden).astype(BF16)
            lanes = pl.ds(pl.multiple_of(512 * phase + 256 * im, 256), 256)
            r.h2cm[:, lanes] = nt(r.ident[...], hidden).astype(BF16)
        return tuple(out)

    mid = lax.fori_loop(0, 4, hidden2, (nought,) * (2 * per))
    payload = place_row(bias_sum, 8, 16)
    for im in range(per):
        payload = payload + place_row(mid[2 * im], group[im], 16)
        payload = payload + place_row(mid[2 * im + 1], group[im] + 4, 16)
    back_sums = AllReduce(3)
    back_sums.begin(payload)

    r.short[...] = nn(r.fpm[...], r.ws[...]) + out_bias
    def conv2(phase, carry):
        a, c = lax.div(phase, 2), lax.rem(phase, 2)
        parts = [
            stack([tap_slice(r.h2s, a, c, dy, dx, im) for im in range(per)]) for dy, dx in taps()
        ]
        y = nn(jnp.concatenate(parts, axis=1), r.w2[...]) + r.short[...]
        r.rc[phase] = y.astype(BF16)
        return carry

    lax.fori_loop(0, 4, conv2, 0)
    for im in range(per):
        for n in range(4):
            first = 256 * im + 64 * n
            piece = stack([r.rc[ph, first : first + 64, :] for ph in range(4)])
            r.ocm[im, :, 256 * n : 256 * n + 256] = tn(piece, r.gridder[0:256, :]).astype(BF16)

    def own_channels(ref, index, im):
        return ref.at[im, pl.ds(pl.multiple_of(local * index, local), local), :]

    def give_back(ref, out, passing):
        for im in range(per):
            out[per * me + im] = own_channels(ref, me, im)[...]
        return Ring(
            lambda c, im: own_channels(ref, c, im), lambda c, im: out.at[per * c + im], passing
        )

    back_sums.middle()
    block_output = give_back(r.ocm, r.out_v, r.pass_o)

    def grad2(tap, carry):
        dy, dx = lax.div(tap, 3), lax.rem(tap, 3)
        pieces = []
        for ph in range(4):
            a, c = ph // 2, ph % 2
            for im in range(per):
                pieces.append(tap_slice(r.dzs, a, c, 2 - dy, 2 - dx, im))
        first = pl.multiple_of(256 * tap, 256)
        r.dw2[pl.ds(first, 256), :] = nn(r.h2cm[...], stack(pieces))
        return carry

    lax.fori_loop(0, 9, grad2, 0)
    for im in range(per):
        piece = channel_major(r.fbuf, im, slice(0, 256))
        grad = nn(piece, r.dzc[256 * im : 256 * im + 256, :])
        if im == 0:
            r.dws[...] = grad
        else:
            r.dws[...] = r.dws[...] + grad

    class GradSum:
        def __init__(self, number, fetch):
            self.fetch = fetch
            self.waits = []
            for part in PARTS:
                setattr(self, part, getattr(r, part + str(number)))

        def begin(self, parts=range(4)):
            for u in parts:
                self.s1[u] = self.fetch(2 * u + 1 - core).astype(BF16)
                self.waits.append(
                    post(self.s1.at[u], self.r1.at[u], self.r1.at[u], dev(partner, within, me))
                )

        def settle(self):
            for wait in self.waits:
                wait()

        def first(self):
            for u in range(4):
                self.waits[u]()
                value = self.fetch(2 * u + core) + self.r1[u].astype(F32)
                self.s2[u] = value.astype(BF16)
            self.waits = [
                post(
                    self.s2.at[lax.div(flip(block, mask), 2)],
                    self.r2.at[plane],
                    self.r2.at[lax.div(flip(block, mask), 2)],
                    dev(flip(block, mask), within, me),
                )
                for mask in (2, 4, 6)
            ]
            self.r2[plane] = self.s2[plane]

        def second(self):
            self.settle()
            value = self.r2[0].astype(F32)
            for u in range(1, 4):
                value = value + self.r2[u].astype(F32)
            value = value.astype(BF16)
            left = [value[0:128], value[256 : 256 + tail]]
            right = [value[128:256], value[256 + tail : rows]]
            if value.shape[0] > rows:
                left.append(value[rows : rows + hs])
                right.append(value[rows + hs :])
            pair = jnp.concatenate([stack(left), stack(right)], axis=1)
            packed = nt(pair, r.unpack[...]).astype(BF16)
            for c in range(n_ch):
                self.s3[c] = packed[:, 128 * c : 128 * c + 128]
            self.r3[me] = self.s3[me]
            self.waits = [
                post(self.s3.at[peer], self.r3.at[me], self.r3.at[peer], dev(block, within, peer))
                for peer in ch_peers
            ]

        def end(self, out, out_small=None):
            self.settle()
            done = self.r3[0].astype(F32)
            for c in range(1, n_ch):
                done = done + self.r3[c].astype(F32)
            turned = done[0:128].T
            out[:, 0:128] = turned[0:local]
            out[:, 128:256] = turned[local:]
            gap = jnp.zeros((128 - tail, 128), F32)
            turned = stack([done[128 : 128 + tail], gap]).T
            ends = turned[0:local] + pltpu.roll(turned[local:], tail, axis=1)
            out[:, 256:rows] = ends[:, 0 : rows - 256]
            if out_small is not None:
                last = done[hw:]
                out_small[0:hs, :] = last[:, 0:local]
                out_small[hs:, :] = pltpu.roll(last, local, axis=1)[:, 0:local]

    def block_rows(ref, size, index):
        return ref[pl.ds(pl.multiple_of(size * index, 8), size), :]

    second = GradSum(2, lambda k: stack([block_rows(r.dw2, rows, k), block_rows(r.dws, small, k)]))
    entry = GradSum(1, lambda k: block_rows(r.dw1, rows, k))
    second.begin()
    r.dshort[...] = nt(r.dzc[...], r.ws[...])

    stats = back_sums.end()
    affine_grad2 = stats
    p1_b = [pick_row(stats[0:4], group[im]) / (4.0 * count) for im in range(per)]
    p2_b = [pick_row(stats[4:8], group[im]) / (4.0 * count) for im in range(per)]

    for im in range(per):
        span = slice(256 * im, 256 * im + 256)
        scale = gain * inv2_b[im]
        combos = []
        for a in range(2):
            grads = []
            for c in range(2):
                ph = 2 * a + c
                d = scale * (r.act[ph, span, :] - (p1_b[im] + r.y1[ph, span, :] * p2_b[im]))
                grads.append(d.astype(BF16))
            right = nn(r.shift[0], grads[0])
            left = nn(r.shift[1], grads[1])
            even, odd = grads[0].astype(F32), grads[1].astype(F32)
            combos.append((odd + right, even + odd, left + even))
        gap = jnp.zeros((16, chans), F32)
        if im == 0:
            second.first()
        for dx in range(3):
            upper, lower = combos[0][dx], combos[1][dx]
            r.field[dx, im] = (lower + stack([upper[16:], gap])).astype(BF16)
            r.field[3 + dx, im] = (upper + lower).astype(BF16)
            r.field[6 + dx, im] = (stack([gap, lower[:-16]]) + upper).astype(BF16)

    block_output.forward()

    def grad1(tap, carry):
        first = pl.multiple_of(256 * tap, 256)
        r.dw1[pl.ds(first, 256), :] = nn(
            r.h1cm[...], stack([r.field[tap, im] for im in range(per)])
        )
        return carry

    for u, (first, last) in enumerate(((0, 3), (3, 5), (5, 7), (7, 9))):
        lax.fori_loop(first, last, grad1, 0)
        entry.begin([u])
    second.second()

    parts = [stack([r.field[tap, im] for im in range(per)]) for tap in range(9)]
    dh1 = back_product(parts, r.w1)
    payload = jnp.zeros((8, chans), F32)
    class_rows = jnp.zeros((24, chans), F32)
    for im in range(per):
        span = slice(256 * im, 256 * im + 256)
        normal = (r.fpm[span, :].astype(F32) - mean1_b[im]) * inv1_b[im]
        pre = gamma_b[im] * normal + beta_b[im]
        sig = sigmoid(pre)
        act = dh1[span] * (sig * (1.0 + pre * (1.0 - sig)))
        r.act1[span, :] = act
        q1, q2 = colsum(act), colsum(act * normal)
        class_rows = class_rows + place_row(q2, label[im], 24)
        class_rows = class_rows + place_row(q1, label[im] + classes, 24)
        payload = payload + place_row(gamma_b[im] * q1, group[im], 8)
        payload = payload + place_row(gamma_b[im] * q2, group[im] + 4, 8)
    last_sums, class_sums = AllReduce(4), AllReduce(6)
    last_sums.begin(payload)
    entry.first()
    class_sums.begin(class_rows)
    last_sums.middle()
    second.end(r.grad2, r.grad3)

    row = iota((8, 128), 0)

    def norm_rows(index, weight, grad, v):
        for wait in held[index]:
            wait()
        master = weight[...]
        _, _, direction = adam_update(
            grad[...], getattr(r, v + "m")[...], getattr(r, v + "q")[...]
        )
        update = direction + WEIGHT_DECAY * master
        rows_w = jnp.where(row == index, total(master * master), 0.0)
        return rows_w + jnp.where(row == index + 3, total(update * update), 0.0)

    if inner == 1:
        norms = norm_rows(1, r.exit_v, r.grad2, "v2") + norm_rows(2, r.bypass_v, r.grad3, "vs")
    stats = last_sums.end()
    for im in range(per):
        span = slice(256 * im, 256 * im + 256)
        normal = (r.fpm[span, :].astype(F32) - mean1_b[im]) * inv1_b[im]
        r1 = pick_row(stats[0:4], group[im]) / count
        r2 = pick_row(stats[4:8], group[im]) / count
        grad = inv1_b[im] * (gamma_b[im] * r.act1[span, :] - (r1 + normal * r2))
        grad = (grad + r.dshort[span, :]).astype(BF16)
        r.dcm[im] = nt(r.ident[...], grad).astype(BF16)
    entry.second()
    input_gradient = give_back(r.dcm, r.dx_v, r.pass_x)
    class_sums.middle()

    if inner == 1:
        entry.end(r.grad1)
        norms = norms + norm_rows(0, r.entry_v, r.grad1, "v1")
        norm_sums = AllReduce(5)
        norm_sums.begin(norms)
        input_gradient.forward()
        norm_sums.middle()
    else:
        entry.end(r.grad1)
        input_gradient.forward()
        r.norms[...] = jnp.zeros((8, 128), F32)

    table = jnp.zeros((24, chans), F32)
    table = table + jnp.where(iota((24, chans), 0) < 2 * classes, class_sums.end(), 0.0)
    table = table + place_row(colsum(affine_grad2[4:8]), 2 * classes, 24)
    table = table + place_row(colsum(affine_grad2[0:4]), 2 * classes + 1, 24)
    table = table + place_row(affine_grad2[8:9], 2 * classes + 2, 24)
    mine = jnp.zeros((24, 128), F32)
    for c in range(n_ch):
        piece = table[:, 128 * (c // 2) : 128 * (c // 2) + 128]
        if c % 2:
            piece = pltpu.roll(piece, local, axis=1)
        mine = mine + jnp.where(me == c, piece, 0.0)
    r.affine_grad[...] = mine

    block_output.settle()
    written = [here(r.out_v, r.out)]
    input_gradient.settle()
    written.append(here(r.dx_v, r.dx))
    if inner == 1:
        r.norms[...] = norm_sums.end()
    for wait in written:
        wait()
    for wait in pending:
        wait()
    cfg.used.append((slots.remote, slots.local))


def final_kernel(cfg, *refs):
    r = SimpleNamespace(**dict(zip(cfg.names, refs)))
    classes = cfg.classes
    local = cfg.local
    r.block_output[...] = r.out[...]
    r.input_gradient[...] = r.dx[...].astype(F32)
    norms = jnp.sqrt(r.norms[...])
    weight_norm, update_norm = norms[0:3, 0:1], norms[3:6, 0:1]
    ratio = weight_norm / update_norm
    at = iota((3, 3), 1)
    r.trust_norms[...] = jnp.where(
        at == 0, weight_norm, jnp.where(at == 1, update_norm, ratio)
    )
    sets = (
        (r.entry, r.entry_m, r.entry_q, r.entry_g, r.entry_1, r.entry_2, r.entry_w),
        (r.exit, r.exit_m, r.exit_q, r.exit_g, r.exit_1, r.exit_2, r.exit_w),
        (r.bypass, r.bypass_m, r.bypass_q, r.bypass_g, r.bypass_1, r.bypass_2, r.bypass_w),
    )
    for index, (weight, m, q, g, first, second, result) in enumerate(sets):
        master = weight[...]
        moment, square, direction = adam_update(g[...], m[...], q[...])
        update = direction + WEIGHT_DECAY * master
        first[...] = moment
        second[...] = square
        result[...] = master - MATRIX_RATE * ratio[index : index + 1] * update
    grad = r.affine_grad[0 : 2 * classes + 3, 0:local]
    moment, square, direction = adam_update(grad, r.affine_m[...], r.affine_q[...])
    r.affine_1[...] = moment
    r.affine_2[...] = square
    r.affine_w[...] = r.affine[...] - AFFINE_RATE * direction


def per_device(
    features,
    labels,
    groups,
    widths,
    entry_conv,
    entry_moment,
    entry_square,
    exit_conv,
    exit_moment,
    exit_square,
    bypass_conv,
    bypass_moment,
    bypass_square,
    norm_affine,
    norm_moment,
    norm_square,
    cotangent,
):
    n_img, n_ch = lax.axis_size("img"), lax.axis_size("ch")
    batch, local, pixels = features.shape
    chans = local * n_ch
    side = math.isqrt(pixels)
    inner = n_img // OUTER
    classes = (norm_affine.shape[0] - 3) // 2
    per = batch // n_ch
    assert (side, chans, n_ch, local, batch % n_ch) == (16, 256, 4, 64, 0) and per == 2
    rows, small = entry_conv.shape[0] * inner, bypass_conv.shape[0] * inner
    masters = (entry_conv, exit_conv, bypass_conv)
    if inner == 1:
        blocks = masters
    else:
        sets = [[o * inner + i for i in range(inner)] for o in range(OUTER)]
        blocks = tuple(
            lax.all_gather(w.astype(BF16), "img", axis=0, tiled=True, axis_index_groups=sets)
            for w in masters
        )

    vmem = pl.BlockSpec(memory_space=pltpu.VMEM)
    smem = pl.BlockSpec(memory_space=pltpu.SMEM)
    anywhere = pl.BlockSpec(memory_space=pl.ANY)
    states = dict(
        entry_m=entry_moment.T,
        entry_q=entry_square.T,
        exit_m=exit_moment.T,
        exit_q=exit_square.T,
        bypass_m=bypass_moment,
        bypass_q=bypass_square,
    )
    inputs = dict(
        labels=(labels, smem),
        groups=(groups, smem),
        widths=(widths, smem),
        features=(features, anywhere),
        cotangent=(cotangent, anywhere),
        entry=(blocks[0].T, anywhere),
        exit=(blocks[1].T, anywhere),
        bypass=(blocks[2], anywhere),
        affine=(norm_affine, anywhere),
    )
    if inner == 1:
        inputs.update({name: (value, anywhere) for name, value in states.items()})
    sds = jax.ShapeDtypeStruct
    outputs = dict(
        out=(sds(cotangent.shape, BF16), anywhere),
        dx=(sds(features.shape, BF16), anywhere),
        grad1=(sds((local, rows), F32), vmem),
        grad2=(sds((local, rows), F32), vmem),
        grad3=(sds((small, local), F32), vmem),
        affine_grad=(sds((24, 128), F32), vmem),
        norms=(sds((8, 128), F32), vmem),
    )
    pix = pixels * per
    taps9 = 9 * chans
    held = lambda shape, dtype=BF16: pltpu.VMEM(shape, dtype)
    scratch = dict(
        fown=held((batch, local, pixels)),
        cown=held((batch, local, 4 * pixels)),
        pass_c=held((2, local, 4 * pixels)),
        pass_o=held((2, local, 4 * pixels)),
        pass_x=held((2, local, pixels)),
        out_v=held(cotangent.shape),
        dx_v=held(features.shape),
        fbuf=held((n_ch, per, local, pixels)),
        cbuf=held((n_ch, per, local, 4 * pixels)),
        entry_v=held((local, rows), blocks[0].dtype),
        exit_v=held((local, rows), blocks[1].dtype),
        bypass_v=held((small, local), blocks[2].dtype),
        affine_v=held(norm_affine.shape, F32),
        padded=held((3 * local, 384)),
        wz1=held((n_ch, rows // 2, 128)),
        wz2=held((n_ch, (rows + small) // 2, 128)),
        aff_z=held((n_ch, 32, 128), F32),
        w1=held((taps9, chans)),
        w2=held((taps9, chans)),
        ws=held((chans, chans)),
        unpack=held((512, 512)),
        ident=held((256, 256)),
        shift=held((2, 256, 256)),
        gridder=held((512, 256)),
        fpm=held((pix, chans)),
        h1s=held((3, per, pixels + 32, chans)),
        h1cm=held((chans, pix)),
        y1=held((4, pix, chans), F32),
        act=held((4, pix, chans), F32),
        h2s=held((2, 4, per, pixels + 32, chans)),
        dzs=held((2, 4, per, pixels + 32, chans)),
        h2cm=held((chans, 4 * pix)),
        short=held((pix, chans), F32),
        dshort=held((pix, chans), F32),
        dzc=held((pix, chans)),
        act1=held((pix, chans), F32),
        rc=held((4, pix, chans)),
        ocm=held((per, chans, 4 * pixels)),
        dcm=held((per, chans, pixels)),
        field=held((9, per, pixels, chans)),
        dw1=held((taps9, chans), F32),
        dw2=held((taps9, chans), F32),
        dws=held((chans, chans), F32),
    )
    for number, size in ((1, rows), (2, rows + small)):
        shapes = ((4, size, chans),) * 4 + ((n_ch, size // 2, 128),) * 2
        for part, shape in zip(PARTS, shapes):
            scratch[part + str(number)] = held(shape)
    exchanges = [(8, chans), (8, chans), (16, chans), (8, chans), (8, 128), (24, chans)]
    if inner == 1:
        for v, shape in (("v1", (local, rows)), ("v2", (local, rows)), ("vs", (small, local))):
            scratch[v + "m"] = held(shape, F32)
            scratch[v + "q"] = held(shape, F32)
    for number, shape in enumerate(exchanges, 1):
        for axis, size in zip("abc", (OUTER, inner, n_ch)):
            if size > 1:
                scratch[axis + str(number)] = held((size,) + shape, F32)
    remote_count = 3 * 3 + 4 * 4 * per + 3 * 7 + 2 * 13 + len(exchanges) * (7 + 3 + inner - 1)
    scratch.update(
        send=pltpu.SemaphoreType.DMA((remote_count,)),
        recv=pltpu.SemaphoreType.DMA((remote_count,)),
        lsem=pltpu.SemaphoreType.DMA((20,)),
    )
    cfg = SimpleNamespace(
        names=[*inputs, *outputs, *scratch],
        inner=inner,
        n_ch=n_ch,
        batch=batch,
        local=local,
        classes=classes,
        count=float(batch * n_img // widths.shape[0] * pixels),
        rows=rows,
        small=small,
        used=[],
    )
    out, dx, grad1, grad2, grad3, affine_grad, norms = pl.pallas_call(
        functools.partial(main_kernel, cfg),
        out_shape=[s for s, _ in outputs.values()],
        in_specs=[s for _, s in inputs.values()],
        out_specs=[s for _, s in outputs.values()],
        scratch_shapes=list(scratch.values()),
        compiler_params=pltpu.CompilerParams(
            collective_id=0, has_side_effects=True, vmem_limit_bytes=VMEM_LIMIT
        ),
        name="block_step",
    )(*[v for v, _ in inputs.values()])
    assert max(n for n, _ in cfg.used) <= remote_count and max(n for _, n in cfg.used) <= 20

    grads = [grad1, grad2, grad3]
    if inner > 1:
        grads = [
            lax.psum_scatter(g, "img", scatter_dimension=0, axis_index_groups=sets, tiled=True)
            for g in (grad1.T, grad2.T, grad3)
        ]
        updates = []
        for w, g, m, s in zip(
            masters,
            grads,
            (entry_moment, exit_moment, bypass_moment),
            (entry_square, exit_square, bypass_square),
        ):
            updates.append(adam_update(g, m, s)[2] + WEIGHT_DECAY * w)
        sums = lax.psum(
            jnp.stack([jnp.sum(w * w) for w in masters] + [jnp.sum(u * u) for u in updates]),
            ("img", "ch"),
        )
        norms = jnp.broadcast_to(jnp.pad(sums, (0, 2))[:, None], (8, 128))
        grads = [grads[0].T, grads[1].T, grads[2]]

    args = dict(
        out=out,
        dx=dx,
        norms=norms,
        affine_grad=affine_grad,
        entry_g=grads[0],
        exit_g=grads[1],
        bypass_g=grads[2],
        entry=entry_conv.T,
        exit=exit_conv.T,
        bypass=bypass_conv,
        **states,
        affine=norm_affine,
        affine_m=norm_moment,
        affine_q=norm_square,
    )
    tall = sds(entry_conv.shape[::-1], F32)
    short, wide = (sds(w.shape, F32) for w in (bypass_conv, norm_affine))
    results = dict(
        block_output=sds(cotangent.shape, BF16),
        input_gradient=sds(features.shape, F32),
        entry_1=tall,
        entry_2=tall,
        entry_w=tall,
        exit_1=tall,
        exit_2=tall,
        exit_w=tall,
        bypass_1=short,
        bypass_2=short,
        bypass_w=short,
        affine_1=wide,
        affine_2=wide,
        affine_w=wide,
        trust_norms=sds((3, 3), F32),
    )
    end_cfg = SimpleNamespace(names=[*args, *results], classes=classes, local=local)
    final = pl.pallas_call(
        functools.partial(final_kernel, end_cfg),
        out_shape=list(results.values()),
        in_specs=[vmem] * len(args),
        out_specs=[vmem] * len(results),
        compiler_params=pltpu.CompilerParams(vmem_limit_bytes=VMEM_LIMIT),
        name="finish",
    )(*args.values())
    return tuple(v.T if s is tall else v for v, s in zip(final, results.values()))


def solution(mesh):
    wide = P("img", "ch")
    deep = P("img", "ch", None)
    table = P(None, "ch")
    return jax.shard_map(
        per_device,
        mesh=mesh,
        in_specs=(deep, P("img"), P("img"), P()) + (wide,) * 9 + (table,) * 3 + (deep,),
        out_specs=(deep, deep) + (wide,) * 9 + (table,) * 3 + (P(),),
        check_vma=False,
    )
```

```python
import functools
import math
from types import SimpleNamespace

import jax
import jax.numpy as jnp
from jax import lax
from jax.experimental import pallas as pl
from jax.experimental.pallas import tpu as pltpu
from jax.sharding import PartitionSpec as P

LEVELS = 4
STEP = 5
NORM_EPSILON = 1e-05
ADAM_EPSILON = 1e-06
MOMENT_DECAY = 0.9
SQUARE_DECAY = 0.999
WEIGHT_DECAY = 0.01
MATRIX_RATE = 0.3
AFFINE_RATE = 0.2

OUTER = 8
VMEM_LIMIT = 56 * 1024 * 1024
BF16 = jnp.bfloat16
F32 = jnp.float32
MESH = pl.DeviceIdType.MESH
PARTS = ("s1", "r1", "s2", "r2", "s3", "r3")


def nn(left, right):
    return lax.dot_general(left, right, (((1,), (0,)), ((), ())), preferred_element_type=F32)


def nt(left, right):
    return lax.dot_general(left, right, (((1,), (1,)), ((), ())), preferred_element_type=F32)


def tn(left, right):
    return lax.dot_general(left, right, (((0,), (0,)), ((), ())), preferred_element_type=F32)


def flip(index, mask):
    result = index
    for bit in range(3):
        if (mask >> bit) & 1:
            digit = lax.rem(lax.div(index, 1 << bit), 2)
            result = result + (1 - 2 * digit) * (1 << bit)
    return result


def sigmoid(value):
    return 0.5 * jnp.tanh(0.5 * value) + 0.5


def iota(shape, axis):
    return lax.broadcasted_iota(jnp.int32, shape, axis)


def to_bf16(condition):
    return jnp.where(condition, 1.0, 0.0).astype(BF16)


def pick_row(table, index):
    hit = iota(table.shape, 0) == index
    return jnp.sum(jnp.where(hit, table, 0.0), axis=0, keepdims=True)


def place_row(row, index, rows):
    hit = iota((rows, row.shape[1]), 0) == index
    return jnp.where(hit, row, 0.0)


def colsum(value):
    return jnp.sum(value, axis=0, keepdims=True)


def adam_update(grad, moment, square):
    moment_new = MOMENT_DECAY * moment + (1.0 - MOMENT_DECAY) * grad
    square_new = SQUARE_DECAY * square + (1.0 - SQUARE_DECAY) * grad * grad
    direction = (
        moment_new
        / (1.0 - MOMENT_DECAY**STEP)
        / (jnp.sqrt(square_new / (1.0 - SQUARE_DECAY**STEP)) + ADAM_EPSILON)
    )
    return (moment_new, square_new, direction)


def total(value):
    return jnp.sum(jnp.sum(value, axis=1, keepdims=True), axis=0, keepdims=True)


def main_kernel(cfg, *refs):
    r = SimpleNamespace(**dict(zip(cfg.names, refs)))
    inner, n_ch, batch, local = cfg.inner, cfg.n_ch, cfg.batch, cfg.local
    classes, count = cfg.classes, cfg.count
    per = batch // n_ch
    chans = local * n_ch
    rows, small = cfg.rows, cfg.small
    tail = (rows - 256) // 2
    hw, hs = rows // 2, small // 2
    slots = SimpleNamespace(remote=0, local=0)

    img = lax.axis_index("img")
    me = lax.axis_index("ch")
    block = lax.div(img, inner)
    within = lax.rem(img, inner)
    core = lax.rem(block, 2)
    plane = lax.div(block, 2)
    partner = flip(block, 1)

    def dev(block_id, within_id, ch_id):
        return (block_id * inner + within_id, ch_id)

    pending = []

    def post(src, dst, landed, peer):
        slot = slots.remote
        slots.remote = slot + 1
        copy = pltpu.make_async_remote_copy(
            src_ref=src,
            dst_ref=dst,
            send_sem=r.send.at[slot],
            recv_sem=r.recv.at[slot],
            device_id=peer,
            device_id_type=MESH,
        )
        copy.start()
        pending.append(copy.wait_send)
        arrival = pltpu.make_async_remote_copy(
            src_ref=landed,
            dst_ref=landed,
            send_sem=r.send.at[slot],
            recv_sem=r.recv.at[slot],
            device_id=peer,
            device_id_type=MESH,
        )
        return arrival.wait_recv

    def here(src, dst):
        slot = slots.local
        slots.local = slot + 1
        copy = pltpu.make_async_copy(src, dst, r.lsem.at[slot])
        copy.start()
        return copy.wait

    outer_peers = [flip(block, mask) for mask in range(1, OUTER)]
    ch_peers = [flip(me, mask) for mask in range(1, n_ch)]
    inner_pairs = [
        (lax.rem(within + step, inner), lax.rem(within + inner - step, inner))
        for step in range(1, inner)
    ]
    up, down, far = (lax.rem(me + step, n_ch) for step in (1, 3, 2))
    up_peer, down_peer = dev(block, within, up), dev(block, within, down)

    class Ring:
        def __init__(self, source, target, passing):
            self.target, self.passing = target, passing
            self.waits = []
            self.early = [
                post(source(far, 0), passing.at[0], passing.at[0], up_peer),
                post(source(far, 1), passing.at[1], passing.at[1], down_peer),
            ]
            for im in range(per):
                self.waits += [
                    post(source(up, im), target(me, im), target(down, im), up_peer),
                    post(source(down, im), target(me, im), target(up, im), down_peer),
                ]

        def forward(self):
            self.early[0]()
            self.waits.append(
                post(self.passing.at[0], self.target(down, 0), self.target(far, 0), up_peer)
            )
            self.early[1]()
            self.waits.append(
                post(self.passing.at[1], self.target(up, 1), self.target(far, 1), down_peer)
            )

        def settle(self):
            for wait in self.waits:
                wait()

    barrier = pltpu.get_barrier_semaphore()
    everyone = [dev(peer, within, me) for peer in outer_peers]
    everyone += [dev(block, within, peer) for peer in ch_peers]
    everyone += [dev(block, peer, me) for peer, _ in inner_pairs]
    for peer in everyone:
        pl.semaphore_signal(barrier, inc=1, device_id=peer, device_id_type=MESH)

    got_entry = here(r.entry, r.entry_v)
    got_features = here(r.features, r.fown)
    got_exit = here(r.exit, r.exit_v)
    got_bypass = here(r.bypass, r.bypass_v)
    got_affine = here(r.affine, r.affine_v)
    got_cot = here(r.cotangent, r.cown)
    states = ((r.entry_m, r.entry_q), (r.exit_m, r.exit_q), (r.bypass_m, r.bypass_q)) if inner == 1 else ()
    held = [
        (here(m, getattr(r, v + "m")), here(q, getattr(r, v + "q")))
        for (m, q), v in zip(states, ("v1", "v2", "vs"))
    ]

    s_row, s_col = iota((hw, 384), 0), iota((hw, 384), 1)
    pick_first = to_bf16(s_col == jnp.where(s_row < 128, s_row, s_row + 128))
    pick_second = to_bf16(s_col == jnp.where(s_row < 128, s_row + 128, s_row + 128 + tail))
    r.padded[...] = jnp.zeros(r.padded.shape, BF16)

    def pack_own(value):
        r.padded[local : 2 * local, 0:rows] = value.astype(BF16)
        packed = nt(pick_first, r.padded[local : 3 * local, :])
        return (packed + nt(pick_second, r.padded[0 : 2 * local, :])).astype(BF16)

    got_entry()
    r.wz1[me] = pack_own(r.entry_v[...])
    pl.semaphore_wait(barrier, len(everyone))

    def to_channels(buffer):
        return [
            post(buffer.at[me], buffer.at[me], buffer.at[peer], dev(block, within, peer))
            for peer in ch_peers
        ]

    entry_waits = to_channels(r.wz1)
    got_features()
    feature_waits = [
        post(
            r.fown.at[pl.ds(per * peer, per)],
            r.fbuf.at[me],
            r.fbuf.at[peer],
            dev(block, within, peer),
        )
        for peer in ch_peers
    ]
    r.fbuf[me] = r.fown[pl.ds(per * me, per)]
    flat = jnp.concatenate([r.fown[b] for b in range(batch)], axis=1)
    wide = flat.astype(F32)
    square = wide * wide
    square_hi = square.astype(BF16)
    square_lo = (square - square_hi.astype(F32)).astype(BF16)
    level = iota((16, 256), 0)
    first_mask = jnp.concatenate([to_bf16(level == r.groups[b]) for b in range(batch)], axis=1)
    second_mask = jnp.concatenate([to_bf16(level == r.groups[b] + 4) for b in range(batch)], axis=1)
    sums = nt(first_mask, flat) + nt(second_mask, square_hi) + nt(second_mask, square_lo)

    got_affine()
    r.aff_z[me] = jnp.zeros((32, 128), F32)
    r.aff_z[me, 0 : 2 * classes + 3, 0:local] = r.affine_v[...]
    r.aff_z[me, 24:32, 0:local] = sums[0:8]
    affine_waits = to_channels(r.aff_z)

    got_exit()
    got_bypass()
    r.wz2[me, 0:hw, :] = pack_own(r.exit_v[...])
    e_row, e_col = iota((local, 128), 0), iota((local, 128), 1)
    value = r.bypass_v[...].astype(BF16)
    r.wz2[me, hw : hw + hs, :] = (
        nn(value[:hs], to_bf16(e_col == e_row)) + nn(value[hs:], to_bf16(e_col == e_row + local))
    ).astype(BF16)

    exit_waits = to_channels(r.wz2)
    got_cot()
    cotangent = Ring(
        lambda c, im: r.cown.at[per * c + im], lambda c, im: r.cbuf.at[c, im], r.pass_c
    )

    lane = iota((512, 512), 0)
    column = iota((512, 512), 1)
    spot = 256 * ((lane >> 6) & 1) + 64 * (lane >> 7) + (lane & 63)
    r.unpack[...] = to_bf16(column == spot)

    def ordered_sum(ref, size):
        result = ref[0]
        for slot in range(1, size):
            result = result + ref[slot]
        return result

    class AllReduce:
        def __init__(self, number):
            self.over_outer, self.over_inner, self.over_ch = (
                getattr(r, axis + str(number), None) for axis in "abc"
            )

        def begin(self, value):
            ref = self.over_outer
            ref[block] = value
            self.waits = [
                post(ref.at[block], ref.at[block], ref.at[peer], dev(peer, within, me))
                for peer in outer_peers
            ]

        def plane(self):
            for wait in self.waits:
                wait()
            value = ordered_sum(self.over_outer, OUTER)
            if inner > 1:
                ref = self.over_inner
                ref[within] = value
                waits = [
                    post(ref.at[within], ref.at[within], ref.at[back], dev(block, peer, me))
                    for peer, back in inner_pairs
                ]
                for wait in waits:
                    wait()
                value = ordered_sum(ref, inner)
            return value

        def middle(self):
            self.over_ch[me] = self.plane()
            self.waits = to_channels(self.over_ch)

        def end(self):
            for wait in self.waits:
                wait()
            return ordered_sum(self.over_ch, n_ch)

    def rows_of(ref, index):
        size = ref.shape[0] // OUTER
        return ref.at[pl.ds(pl.multiple_of(size * index, 16), size)]

    def unpack_own(ref, full):
        own = rows_of(ref, block)
        if full.shape[0] == hw:
            own[0:128, :] = full[0:128, 0:256]
            own[128:256, :] = full[0:128, 256:512]
            own[256 : 256 + tail, :] = full[128:, 0:256]
            own[256 + tail :, :] = full[128:, 256:512]
        else:
            own[0:hs, :] = full[:, 0:256]
            own[hs:, :] = full[:, 256:512]

    def spread(ref):
        own = rows_of(ref, block)
        return {
            mask: post(own, own, rows_of(ref, flip(block, mask)), dev(flip(block, mask), within, me))
            for mask in (2, 4, 6, 1)
        }

    def forward(ref, waits):
        rest = [waits[1]]
        for mask in (2, 4, 6):
            waits[mask]()
            mine = rows_of(ref, flip(block, mask))
            theirs = rows_of(ref, flip(partner, mask))
            rest.append(post(mine, mine, theirs, dev(partner, within, me)))
        return rest

    def widen(buffer):
        packed = jnp.concatenate([buffer[c] for c in range(n_ch)], axis=1)
        return nn(packed, r.unpack[...]).astype(BF16)

    def wide_lanes(ref):
        parts = [
            ref[c] + pltpu.roll(ref[c + 1], local, axis=1) for c in range(0, n_ch, 2)
        ]
        return jnp.concatenate(parts, axis=1)

    for wait in affine_waits:
        wait()
    affine = wide_lanes(r.aff_z)
    input_sums = AllReduce(1)
    input_sums.begin(affine[24:32])
    for wait in entry_waits:
        wait()
    unpack_own(r.w1, widen(r.wz1))
    gather1 = spread(r.w1)

    ident = to_bf16(iota((256, 256), 0) == iota((256, 256), 1))
    r.ident[...] = ident
    q_out, q_in = iota((256, 256), 0), iota((256, 256), 1)
    r.shift[0] = to_bf16((q_in == q_out + 1) & ((q_out & 15) < 15))
    r.shift[1] = to_bf16((q_in == q_out - 1) & ((q_out & 15) > 0))

    for wait in exit_waits:
        wait()
    full = widen(r.wz2)
    unpack_own(r.w2, full[0:hw])
    unpack_own(r.ws, full[hw:])
    gather2 = spread(r.w2)
    gather3 = spread(r.ws)

    rho, px = iota((512, 256), 0), iota((512, 256), 1)
    version, a, b_ = rho >> 8, (rho >> 7) & 1, (rho >> 6) & 1
    col = (rho & 15) + version * (1 - 2 * b_)
    target = (2 * ((rho & 63) >> 4) + a) * 32 + 2 * col + b_
    r.gridder[...] = to_bf16((px == target) & (col >= 0) & (col < 16))
    zeros = jnp.zeros((16, 256), BF16)
    for im in range(per):
        for ver in range(3):
            r.h1s[ver, im, 0:16, :] = zeros
            r.h1s[ver, im, 272:288, :] = zeros
        for ver in range(2):
            for ph in range(4):
                for ref in (r.h2s, r.dzs):
                    ref[ver, ph, im, 0:16, :] = zeros
                    ref[ver, ph, im, 272:288, :] = zeros

    def channel_major(ref, im, lanes):
        return jnp.concatenate([ref[c, im, :, lanes] for c in range(n_ch)], axis=0)

    for wait in feature_waits:
        wait()
    for im in range(per):
        r.fpm[256 * im : 256 * im + 256, :] = nt(
            ident, channel_major(r.fbuf, im, slice(0, 256))
        ).astype(BF16)

    stats = input_sums.plane()
    mean1 = stats[0:4] / count
    inv1 = lax.rsqrt(stats[4:8] / count - mean1 * mean1 + NORM_EPSILON)
    gain = affine[2 * classes : 2 * classes + 1]
    shift = affine[2 * classes + 1 : 2 * classes + 2]
    out_bias = affine[2 * classes + 2 : 2 * classes + 3]
    group, label, mean1_b, inv1_b, gamma_b, beta_b, mask_b = [], [], [], [], [], [], []
    for im in range(per):
        group.append(r.groups[per * me + im])
        label.append(r.labels[per * me + im])
        mean1_b.append(pick_row(mean1, group[im]))
        inv1_b.append(pick_row(inv1, group[im]))
        gamma_b.append(pick_row(affine, label[im]))
        beta_b.append(pick_row(affine, label[im] + classes))
        width = r.widths[group[im]]
        mask_b.append(
            jnp.where(iota((1, chans), 1) < width * (chans // LEVELS), 1.0, 0.0)
        )

    for im in range(per):
        normal = (r.fpm[256 * im : 256 * im + 256, :].astype(F32) - mean1_b[im]) * inv1_b[im]
        pre = gamma_b[im] * normal + beta_b[im]
        hidden = (pre * sigmoid(pre)).astype(BF16)
        r.h1s[1, im, 16:272, :] = hidden
        r.h1s[0, im, 16:272, :] = nn(r.shift[1], hidden).astype(BF16)
        r.h1s[2, im, 16:272, :] = nn(r.shift[0], hidden).astype(BF16)
        r.h1cm[:, 256 * im : 256 * im + 256] = nt(ident, hidden).astype(BF16)

    rest = forward(r.w1, gather1)
    cotangent.forward()
    for wait in rest:
        wait()

    def back_product(parts, ref):
        result = nt(parts[0], ref[0:256, :])
        for tap in range(1, 9):
            result = result + nt(parts[tap], ref[256 * tap : 256 * tap + 256, :])
        return result

    def taps():
        return [(dy, dx) for dy in range(3) for dx in range(3)]

    def stack(pieces):
        return jnp.concatenate(pieces, axis=0)

    def conv1(phase, carry):
        a, c = lax.div(phase, 2), lax.rem(phase, 2)
        parts = []
        for dy, dx in taps():
            first = pl.multiple_of(16 * lax.div(a + dy + 1, 2), 16)
            ver = lax.div(c + dx + 1, 2)
            parts.append(
                stack([r.h1s[ver, im, pl.ds(first, 256), :] for im in range(per)])
            )
        y = nn(jnp.concatenate(parts, axis=1), r.w1[...])
        r.y1[phase] = y
        out = []
        for im in range(per):
            piece = y[256 * im : 256 * im + 256]
            out.append(carry[2 * im] + colsum(piece))
            out.append(carry[2 * im + 1] + colsum(piece * piece))
        return tuple(out)

    nought = jnp.zeros((1, chans), F32)
    mid = lax.fori_loop(0, 4, conv1, (nought,) * (2 * per))
    payload = jnp.zeros((8, chans), F32)
    for im in range(per):
        payload = payload + place_row(mid[2 * im], group[im], 8)
        payload = payload + place_row(mid[2 * im + 1], group[im] + 4, 8)
    mid_sums = AllReduce(2)
    mid_sums.begin(payload)

    rest = forward(r.w2, gather2) + forward(r.ws, gather3)
    mid_sums.middle()

    r.cbuf[me] = r.cown[pl.ds(per * me, per)]
    cotangent.settle()
    for im in range(per):
        for n in range(4):
            piece = channel_major(r.cbuf, im, slice(256 * n, 256 * n + 256))
            grid = nt(r.gridder[...], piece).astype(BF16)
            for ver in range(2):
                for ph in range(4):
                    at = 256 * ver + 64 * ph
                    r.dzs[ver, ph, im, 16 + 64 * n : 80 + 64 * n, :] = grid[at : at + 64]

    coarse = jnp.zeros((256 * per, chans), F32)
    for ph in range(4):
        coarse = coarse + stack([r.dzs[0, ph, im, 16:272, :] for im in range(per)]).astype(F32)
    bias_sum = colsum(coarse)
    r.dzc[...] = coarse.astype(BF16)

    def tap_slice(ref, a, c, dy, dx, im):
        row, colm = a + dy + 1, c + dx + 1
        first = pl.multiple_of(16 * lax.div(row, 2), 16)
        ph = 2 * lax.rem(row, 2) + lax.rem(colm, 2)
        side_step = lax.div(colm, 2) - 1
        return ref[side_step * side_step, ph, im, pl.ds(first, 256), :]

    for wait in rest:
        wait()

    def back2(phase, carry):
        a, c = lax.div(phase, 2), lax.rem(phase, 2)
        parts = [
            stack([tap_slice(r.dzs, a, c, 2 - dy, 2 - dx, im) for im in range(per)])
            for dy, dx in taps()
        ]
        r.act[phase] = back_product(parts, r.w2)
        return carry

    lax.fori_loop(0, 4, back2, 0)

    stats = mid_sums.end()
    mean2 = stats[0:4] / (4.0 * count)
    inv2 = lax.rsqrt(stats[4:8] / (4.0 * count) - mean2 * mean2 + NORM_EPSILON)
    mean2_b = [pick_row(mean2, group[im]) for im in range(per)]
    inv2_b = [pick_row(inv2, group[im]) for im in range(per)]

    def hidden2(phase, carry):
        c = lax.rem(phase, 2)
        out = []
        for im in range(per):
            span = slice(256 * im, 256 * im + 256)
            normal = (r.y1[phase, span, :] - mean2_b[im]) * inv2_b[im]
            r.y1[phase, span, :] = normal
            pre = gain * normal + shift
            sig = sigmoid(pre)
            hidden = (pre * sig * mask_b[im]).astype(BF16)
            act = r.act[phase, span, :] * (sig * (1.0 + pre * (1.0 - sig)) * mask_b[im])
            r.act[phase, span, :] = act
            out.append(carry[2 * im] + colsum(act))
            out.append(carry[2 * im + 1] + colsum(act * normal))
            r.h2s[0, phase, im, 16:272, :] = hidden
            r.h2s[1, phase, im, 16:272, :] = nn(r.shift[c], hidden).astype(BF16)
            lanes = pl.ds(pl.multiple_of(512 * phase + 256 * im, 256), 256)
            r.h2cm[:, lanes] = nt(r.ident[...], hidden).astype(BF16)
        return tuple(out)

    mid = lax.fori_loop(0, 4, hidden2, (nought,) * (2 * per))
    payload = place_row(bias_sum, 8, 16)
    for im in range(per):
        payload = payload + place_row(mid[2 * im], group[im], 16)
        payload = payload + place_row(mid[2 * im + 1], group[im] + 4, 16)
    back_sums = AllReduce(3)
    back_sums.begin(payload)

    r.short[...] = nn(r.fpm[...], r.ws[...]) + out_bias
    def conv2(phase, carry):
        a, c = lax.div(phase, 2), lax.rem(phase, 2)
        parts = [
            stack([tap_slice(r.h2s, a, c, dy, dx, im) for im in range(per)]) for dy, dx in taps()
        ]
        y = nn(jnp.concatenate(parts, axis=1), r.w2[...]) + r.short[...]
        r.rc[phase] = y.astype(BF16)
        return carry

    lax.fori_loop(0, 4, conv2, 0)
    for im in range(per):
        for n in range(4):
            first = 256 * im + 64 * n
            piece = stack([r.rc[ph, first : first + 64, :] for ph in range(4)])
            r.ocm[im, :, 256 * n : 256 * n + 256] = tn(piece, r.gridder[0:256, :]).astype(BF16)

    def own_channels(ref, index, im):
        return ref.at[im, pl.ds(pl.multiple_of(local * index, local), local), :]

    def give_back(ref, out, passing):
        for im in range(per):
            out[per * me + im] = own_channels(ref, me, im)[...]
        return Ring(
            lambda c, im: own_channels(ref, c, im), lambda c, im: out.at[per * c + im], passing
        )

    back_sums.middle()
    block_output = give_back(r.ocm, r.out_v, r.pass_o)

    def grad2(tap, carry):
        dy, dx = lax.div(tap, 3), lax.rem(tap, 3)
        pieces = []
        for ph in range(4):
            a, c = ph // 2, ph % 2
            for im in range(per):
                pieces.append(tap_slice(r.dzs, a, c, 2 - dy, 2 - dx, im))
        first = pl.multiple_of(256 * tap, 256)
        r.dw2[pl.ds(first, 256), :] = nn(r.h2cm[...], stack(pieces))
        return carry

    lax.fori_loop(0, 9, grad2, 0)
    for im in range(per):
        piece = channel_major(r.fbuf, im, slice(0, 256))
        grad = nn(piece, r.dzc[256 * im : 256 * im + 256, :])
        if im == 0:
            r.dws[...] = grad
        else:
            r.dws[...] = r.dws[...] + grad

    class GradSum:
        def __init__(self, number, fetch):
            self.fetch = fetch
            self.waits = []
            for part in PARTS:
                setattr(self, part, getattr(r, part + str(number)))

        def begin(self, parts=range(4)):
            for u in parts:
                self.s1[u] = self.fetch(2 * u + 1 - core).astype(BF16)
                self.waits.append(
                    post(self.s1.at[u], self.r1.at[u], self.r1.at[u], dev(partner, within, me))
                )

        def settle(self):
            for wait in self.waits:
                wait()

        def first(self):
            self.settle()
            self.waits = []
            for mask in (6, 2, 4, 0):
                peer = flip(block, mask)
                u = lax.div(peer, 2)
                value = self.fetch(peer) + self.r1[u].astype(F32)
                if mask == 0:
                    self.r2[plane] = value.astype(BF16)
                    continue
                self.s2[u] = value.astype(BF16)
                self.waits.append(
                    post(self.s2.at[u], self.r2.at[plane], self.r2.at[u], dev(peer, within, me))
                )

        def second(self):
            self.settle()
            value = self.r2[0].astype(F32)
            for u in range(1, 4):
                value = value + self.r2[u].astype(F32)
            value = value.astype(BF16)
            left = [value[0:128], value[256 : 256 + tail]]
            right = [value[128:256], value[256 + tail : rows]]
            if value.shape[0] > rows:
                left.append(value[rows : rows + hs])
                right.append(value[rows + hs :])
            pair = jnp.concatenate([stack(left), stack(right)], axis=1)
            packed = nt(pair, r.unpack[...]).astype(BF16)
            for c in range(n_ch):
                self.s3[c] = packed[:, 128 * c : 128 * c + 128]
            self.r3[me] = self.s3[me]
            self.waits = [
                post(self.s3.at[peer], self.r3.at[me], self.r3.at[peer], dev(block, within, peer))
                for peer in ch_peers
            ]

        def end(self, out, out_small=None):
            self.settle()
            done = self.r3[0].astype(F32)
            for c in range(1, n_ch):
                done = done + self.r3[c].astype(F32)
            turned = done[0:128].T
            out[:, 0:128] = turned[0:local]
            out[:, 128:256] = turned[local:]
            gap = jnp.zeros((128 - tail, 128), F32)
            turned = stack([done[128 : 128 + tail], gap]).T
            ends = turned[0:local] + pltpu.roll(turned[local:], tail, axis=1)
            out[:, 256:rows] = ends[:, 0 : rows - 256]
            if out_small is not None:
                last = done[hw:]
                out_small[0:hs, :] = last[:, 0:local]
                out_small[hs:, :] = pltpu.roll(last, local, axis=1)[:, 0:local]

    def block_rows(ref, size, index):
        return ref[pl.ds(pl.multiple_of(size * index, 8), size), :]

    second = GradSum(2, lambda k: stack([block_rows(r.dw2, rows, k), block_rows(r.dws, small, k)]))
    entry = GradSum(1, lambda k: block_rows(r.dw1, rows, k))
    second.begin()
    r.dshort[...] = nt(r.dzc[...], r.ws[...])

    stats = back_sums.end()
    affine_grad2 = stats
    p1_b = [pick_row(stats[0:4], group[im]) / (4.0 * count) for im in range(per)]
    p2_b = [pick_row(stats[4:8], group[im]) / (4.0 * count) for im in range(per)]

    for im in range(per):
        span = slice(256 * im, 256 * im + 256)
        scale = gain * inv2_b[im]
        combos = []
        for a in range(2):
            grads = []
            for c in range(2):
                ph = 2 * a + c
                d = scale * (r.act[ph, span, :] - (p1_b[im] + r.y1[ph, span, :] * p2_b[im]))
                grads.append(d.astype(BF16))
            right = nn(r.shift[0], grads[0])
            left = nn(r.shift[1], grads[1])
            even, odd = grads[0].astype(F32), grads[1].astype(F32)
            combos.append((odd + right, even + odd, left + even))
        gap = jnp.zeros((16, chans), F32)
        for dx in range(3):
            upper, lower = combos[0][dx], combos[1][dx]
            r.field[dx, im] = (lower + stack([upper[16:], gap])).astype(BF16)
            r.field[3 + dx, im] = (upper + lower).astype(BF16)
            r.field[6 + dx, im] = (stack([gap, lower[:-16]]) + upper).astype(BF16)

    second.first()
    block_output.forward()

    def grad1(tap, carry):
        first = pl.multiple_of(256 * tap, 256)
        r.dw1[pl.ds(first, 256), :] = nn(
            r.h1cm[...], stack([r.field[tap, im] for im in range(per)])
        )
        return carry

    for u, (first, last) in enumerate(((0, 3), (3, 5), (5, 7), (7, 9))):
        lax.fori_loop(first, last, grad1, 0)
        entry.begin([u])

    parts = [stack([r.field[tap, im] for im in range(per)]) for tap in range(9)]
    dh1 = back_product(parts, r.w1)
    payload = jnp.zeros((8, chans), F32)
    class_rows = jnp.zeros((24, chans), F32)
    for im in range(per):
        span = slice(256 * im, 256 * im + 256)
        normal = (r.fpm[span, :].astype(F32) - mean1_b[im]) * inv1_b[im]
        pre = gamma_b[im] * normal + beta_b[im]
        sig = sigmoid(pre)
        act = dh1[span] * (sig * (1.0 + pre * (1.0 - sig)))
        r.act1[span, :] = act
        q1, q2 = colsum(act), colsum(act * normal)
        class_rows = class_rows + place_row(q2, label[im], 24)
        class_rows = class_rows + place_row(q1, label[im] + classes, 24)
        payload = payload + place_row(gamma_b[im] * q1, group[im], 8)
        payload = payload + place_row(gamma_b[im] * q2, group[im] + 4, 8)
    last_sums, class_sums = AllReduce(4), AllReduce(6)
    last_sums.begin(payload)
    entry.first()
    class_sums.begin(class_rows)
    last_sums.middle()
    second.second()
    stats = last_sums.end()
    for im in range(per):
        span = slice(256 * im, 256 * im + 256)
        normal = (r.fpm[span, :].astype(F32) - mean1_b[im]) * inv1_b[im]
        r1 = pick_row(stats[0:4], group[im]) / count
        r2 = pick_row(stats[4:8], group[im]) / count
        grad = inv1_b[im] * (gamma_b[im] * r.act1[span, :] - (r1 + normal * r2))
        grad = (grad + r.dshort[span, :]).astype(BF16)
        r.dcm[im] = nt(r.ident[...], grad).astype(BF16)
    entry.second()
    input_gradient = give_back(r.dcm, r.dx_v, r.pass_x)
    class_sums.middle()
    second.end(r.grad2, r.grad3)

    row = iota((8, 128), 0)

    def norm_rows(index, weight, grad, v):
        for wait in held[index]:
            wait()
        master = weight[...]
        _, _, direction = adam_update(
            grad[...], getattr(r, v + "m")[...], getattr(r, v + "q")[...]
        )
        update = direction + WEIGHT_DECAY * master
        rows_w = jnp.where(row == index, total(master * master), 0.0)
        return rows_w + jnp.where(row == index + 3, total(update * update), 0.0)

    if inner == 1:
        norms = norm_rows(1, r.exit_v, r.grad2, "v2") + norm_rows(2, r.bypass_v, r.grad3, "vs")

    if inner == 1:
        entry.end(r.grad1)
        norms = norms + norm_rows(0, r.entry_v, r.grad1, "v1")
        norm_sums = AllReduce(5)
        norm_sums.begin(norms)
        input_gradient.forward()
        norm_sums.middle()
    else:
        entry.end(r.grad1)
        input_gradient.forward()
        r.norms[...] = jnp.zeros((8, 128), F32)

    table = jnp.zeros((24, chans), F32)
    table = table + jnp.where(iota((24, chans), 0) < 2 * classes, class_sums.end(), 0.0)
    table = table + place_row(colsum(affine_grad2[4:8]), 2 * classes, 24)
    table = table + place_row(colsum(affine_grad2[0:4]), 2 * classes + 1, 24)
    table = table + place_row(affine_grad2[8:9], 2 * classes + 2, 24)
    mine = jnp.zeros((24, 128), F32)
    for c in range(n_ch):
        piece = table[:, 128 * (c // 2) : 128 * (c // 2) + 128]
        if c % 2:
            piece = pltpu.roll(piece, local, axis=1)
        mine = mine + jnp.where(me == c, piece, 0.0)
    r.affine_grad[...] = mine

    block_output.settle()
    written = [here(r.out_v, r.out)]
    input_gradient.settle()
    written.append(here(r.dx_v, r.dx))
    if inner == 1:
        r.norms[...] = norm_sums.end()
    for wait in written:
        wait()
    for wait in pending:
        wait()
    cfg.used.append((slots.remote, slots.local))


def final_kernel(cfg, *refs):
    r = SimpleNamespace(**dict(zip(cfg.names, refs)))
    classes = cfg.classes
    local = cfg.local
    r.block_output[...] = r.out[...]
    r.input_gradient[...] = r.dx[...].astype(F32)
    norms = jnp.sqrt(r.norms[...])
    weight_norm, update_norm = norms[0:3, 0:1], norms[3:6, 0:1]
    ratio = weight_norm / update_norm
    at = iota((3, 3), 1)
    r.trust_norms[...] = jnp.where(
        at == 0, weight_norm, jnp.where(at == 1, update_norm, ratio)
    )
    sets = (
        (r.entry, r.entry_m, r.entry_q, r.entry_g, r.entry_1, r.entry_2, r.entry_w),
        (r.exit, r.exit_m, r.exit_q, r.exit_g, r.exit_1, r.exit_2, r.exit_w),
        (r.bypass, r.bypass_m, r.bypass_q, r.bypass_g, r.bypass_1, r.bypass_2, r.bypass_w),
    )
    for index, (weight, m, q, g, first, second, result) in enumerate(sets):
        master = weight[...]
        moment, square, direction = adam_update(g[...], m[...], q[...])
        update = direction + WEIGHT_DECAY * master
        first[...] = moment
        second[...] = square
        result[...] = master - MATRIX_RATE * ratio[index : index + 1] * update
    grad = r.affine_grad[0 : 2 * classes + 3, 0:local]
    moment, square, direction = adam_update(grad, r.affine_m[...], r.affine_q[...])
    r.affine_1[...] = moment
    r.affine_2[...] = square
    r.affine_w[...] = r.affine[...] - AFFINE_RATE * direction


def per_device(
    features,
    labels,
    groups,
    widths,
    entry_conv,
    entry_moment,
    entry_square,
    exit_conv,
    exit_moment,
    exit_square,
    bypass_conv,
    bypass_moment,
    bypass_square,
    norm_affine,
    norm_moment,
    norm_square,
    cotangent,
):
    n_img, n_ch = lax.axis_size("img"), lax.axis_size("ch")
    batch, local, pixels = features.shape
    chans = local * n_ch
    side = math.isqrt(pixels)
    inner = n_img // OUTER
    classes = (norm_affine.shape[0] - 3) // 2
    per = batch // n_ch
    assert (side, chans, n_ch, local, batch % n_ch) == (16, 256, 4, 64, 0) and per == 2
    rows, small = entry_conv.shape[0] * inner, bypass_conv.shape[0] * inner
    masters = (entry_conv, exit_conv, bypass_conv)
    if inner == 1:
        blocks = masters
    else:
        sets = [[o * inner + i for i in range(inner)] for o in range(OUTER)]
        blocks = tuple(
            lax.all_gather(w.astype(BF16), "img", axis=0, tiled=True, axis_index_groups=sets)
            for w in masters
        )

    vmem = pl.BlockSpec(memory_space=pltpu.VMEM)
    smem = pl.BlockSpec(memory_space=pltpu.SMEM)
    anywhere = pl.BlockSpec(memory_space=pl.ANY)
    states = dict(
        entry_m=entry_moment.T,
        entry_q=entry_square.T,
        exit_m=exit_moment.T,
        exit_q=exit_square.T,
        bypass_m=bypass_moment,
        bypass_q=bypass_square,
    )
    inputs = dict(
        labels=(labels, smem),
        groups=(groups, smem),
        widths=(widths, smem),
        features=(features, anywhere),
        cotangent=(cotangent, anywhere),
        entry=(blocks[0].T, anywhere),
        exit=(blocks[1].T, anywhere),
        bypass=(blocks[2], anywhere),
        affine=(norm_affine, anywhere),
    )
    if inner == 1:
        inputs.update({name: (value, anywhere) for name, value in states.items()})
    sds = jax.ShapeDtypeStruct
    outputs = dict(
        out=(sds(cotangent.shape, BF16), anywhere),
        dx=(sds(features.shape, BF16), anywhere),
        grad1=(sds((local, rows), F32), vmem),
        grad2=(sds((local, rows), F32), vmem),
        grad3=(sds((small, local), F32), vmem),
        affine_grad=(sds((24, 128), F32), vmem),
        norms=(sds((8, 128), F32), vmem),
    )
    pix = pixels * per
    taps9 = 9 * chans
    held = lambda shape, dtype=BF16: pltpu.VMEM(shape, dtype)
    scratch = dict(
        fown=held((batch, local, pixels)),
        cown=held((batch, local, 4 * pixels)),
        pass_c=held((2, local, 4 * pixels)),
        pass_o=held((2, local, 4 * pixels)),
        pass_x=held((2, local, pixels)),
        out_v=held(cotangent.shape),
        dx_v=held(features.shape),
        fbuf=held((n_ch, per, local, pixels)),
        cbuf=held((n_ch, per, local, 4 * pixels)),
        entry_v=held((local, rows), blocks[0].dtype),
        exit_v=held((local, rows), blocks[1].dtype),
        bypass_v=held((small, local), blocks[2].dtype),
        affine_v=held(norm_affine.shape, F32),
        padded=held((3 * local, 384)),
        wz1=held((n_ch, rows // 2, 128)),
        wz2=held((n_ch, (rows + small) // 2, 128)),
        aff_z=held((n_ch, 32, 128), F32),
        w1=held((taps9, chans)),
        w2=held((taps9, chans)),
        ws=held((chans, chans)),
        unpack=held((512, 512)),
        ident=held((256, 256)),
        shift=held((2, 256, 256)),
        gridder=held((512, 256)),
        fpm=held((pix, chans)),
        h1s=held((3, per, pixels + 32, chans)),
        h1cm=held((chans, pix)),
        y1=held((4, pix, chans), F32),
        act=held((4, pix, chans), F32),
        h2s=held((2, 4, per, pixels + 32, chans)),
        dzs=held((2, 4, per, pixels + 32, chans)),
        h2cm=held((chans, 4 * pix)),
        short=held((pix, chans), F32),
        dshort=held((pix, chans), F32),
        dzc=held((pix, chans)),
        act1=held((pix, chans), F32),
        rc=held((4, pix, chans)),
        ocm=held((per, chans, 4 * pixels)),
        dcm=held((per, chans, pixels)),
        field=held((9, per, pixels, chans)),
        dw1=held((taps9, chans), F32),
        dw2=held((taps9, chans), F32),
        dws=held((chans, chans), F32),
    )
    for number, size in ((1, rows), (2, rows + small)):
        shapes = ((4, size, chans),) * 4 + ((n_ch, size // 2, 128),) * 2
        for part, shape in zip(PARTS, shapes):
            scratch[part + str(number)] = held(shape)
    exchanges = [(8, chans), (8, chans), (16, chans), (8, chans), (8, 128), (24, chans)]
    if inner == 1:
        for v, shape in (("v1", (local, rows)), ("v2", (local, rows)), ("vs", (small, local))):
            scratch[v + "m"] = held(shape, F32)
            scratch[v + "q"] = held(shape, F32)
    for number, shape in enumerate(exchanges, 1):
        for axis, size in zip("abc", (OUTER, inner, n_ch)):
            if size > 1:
                scratch[axis + str(number)] = held((size,) + shape, F32)
    remote_count = 3 * 3 + 4 * 4 * per + 3 * 7 + 2 * 13 + len(exchanges) * (7 + 3 + inner - 1)
    scratch.update(
        send=pltpu.SemaphoreType.DMA((remote_count,)),
        recv=pltpu.SemaphoreType.DMA((remote_count,)),
        lsem=pltpu.SemaphoreType.DMA((20,)),
    )
    cfg = SimpleNamespace(
        names=[*inputs, *outputs, *scratch],
        inner=inner,
        n_ch=n_ch,
        batch=batch,
        local=local,
        classes=classes,
        count=float(batch * n_img // widths.shape[0] * pixels),
        rows=rows,
        small=small,
        used=[],
    )
    out, dx, grad1, grad2, grad3, affine_grad, norms = pl.pallas_call(
        functools.partial(main_kernel, cfg),
        out_shape=[s for s, _ in outputs.values()],
        in_specs=[s for _, s in inputs.values()],
        out_specs=[s for _, s in outputs.values()],
        scratch_shapes=list(scratch.values()),
        compiler_params=pltpu.CompilerParams(
            collective_id=0, has_side_effects=True, vmem_limit_bytes=VMEM_LIMIT
        ),
        name="block_step",
    )(*[v for v, _ in inputs.values()])
    assert max(n for n, _ in cfg.used) <= remote_count and max(n for _, n in cfg.used) <= 20

    grads = [grad1, grad2, grad3]
    if inner > 1:
        grads = [
            lax.psum_scatter(g, "img", scatter_dimension=0, axis_index_groups=sets, tiled=True)
            for g in (grad1.T, grad2.T, grad3)
        ]
        updates = []
        for w, g, m, s in zip(
            masters,
            grads,
            (entry_moment, exit_moment, bypass_moment),
            (entry_square, exit_square, bypass_square),
        ):
            updates.append(adam_update(g, m, s)[2] + WEIGHT_DECAY * w)
        sums = lax.psum(
            jnp.stack([jnp.sum(w * w) for w in masters] + [jnp.sum(u * u) for u in updates]),
            ("img", "ch"),
        )
        norms = jnp.broadcast_to(jnp.pad(sums, (0, 2))[:, None], (8, 128))
        grads = [grads[0].T, grads[1].T, grads[2]]

    args = dict(
        out=out,
        dx=dx,
        norms=norms,
        affine_grad=affine_grad,
        entry_g=grads[0],
        exit_g=grads[1],
        bypass_g=grads[2],
        entry=entry_conv.T,
        exit=exit_conv.T,
        bypass=bypass_conv,
        **states,
        affine=norm_affine,
        affine_m=norm_moment,
        affine_q=norm_square,
    )
    tall = sds(entry_conv.shape[::-1], F32)
    short, wide = (sds(w.shape, F32) for w in (bypass_conv, norm_affine))
    results = dict(
        block_output=sds(cotangent.shape, BF16),
        input_gradient=sds(features.shape, F32),
        entry_1=tall,
        entry_2=tall,
        entry_w=tall,
        exit_1=tall,
        exit_2=tall,
        exit_w=tall,
        bypass_1=short,
        bypass_2=short,
        bypass_w=short,
        affine_1=wide,
        affine_2=wide,
        affine_w=wide,
        trust_norms=sds((3, 3), F32),
    )
    end_cfg = SimpleNamespace(names=[*args, *results], classes=classes, local=local)
    final = pl.pallas_call(
        functools.partial(final_kernel, end_cfg),
        out_shape=list(results.values()),
        in_specs=[vmem] * len(args),
        out_specs=[vmem] * len(results),
        compiler_params=pltpu.CompilerParams(vmem_limit_bytes=VMEM_LIMIT),
        name="finish",
    )(*args.values())
    return tuple(v.T if s is tall else v for v, s in zip(final, results.values()))


def solution(mesh):
    wide = P("img", "ch")
    deep = P("img", "ch", None)
    table = P(None, "ch")
    return jax.shard_map(
        per_device,
        mesh=mesh,
        in_specs=(deep, P("img"), P("img"), P()) + (wide,) * 9 + (table,) * 3 + (deep,),
        out_specs=(deep, deep) + (wide,) * 9 + (table,) * 3 + (P(),),
        check_vma=False,
    )
```

```python
import functools
import math
from types import SimpleNamespace

import jax
import jax.numpy as jnp
from jax import lax
from jax.experimental import pallas as pl
from jax.experimental.pallas import tpu as pltpu
from jax.sharding import PartitionSpec as P

LEVELS = 4
STEP = 5
NORM_EPSILON = 1e-05
ADAM_EPSILON = 1e-06
MOMENT_DECAY = 0.9
SQUARE_DECAY = 0.999
WEIGHT_DECAY = 0.01
MATRIX_RATE = 0.3
AFFINE_RATE = 0.2

OUTER = 8
VMEM_LIMIT = 56 * 1024 * 1024
BF16 = jnp.bfloat16
F32 = jnp.float32
MESH = pl.DeviceIdType.MESH
PARTS = ("s1", "r1", "s2", "r2", "s3", "r3")


def nn(left, right):
    return lax.dot_general(left, right, (((1,), (0,)), ((), ())), preferred_element_type=F32)


def nt(left, right):
    return lax.dot_general(left, right, (((1,), (1,)), ((), ())), preferred_element_type=F32)


def tn(left, right):
    return lax.dot_general(left, right, (((0,), (0,)), ((), ())), preferred_element_type=F32)


def flip(index, mask):
    result = index
    for bit in range(3):
        if (mask >> bit) & 1:
            digit = lax.rem(lax.div(index, 1 << bit), 2)
            result = result + (1 - 2 * digit) * (1 << bit)
    return result


def sigmoid(value):
    return 0.5 * jnp.tanh(0.5 * value) + 0.5


def iota(shape, axis):
    return lax.broadcasted_iota(jnp.int32, shape, axis)


def to_bf16(condition):
    return jnp.where(condition, 1.0, 0.0).astype(BF16)


def pick_row(table, index):
    hit = iota(table.shape, 0) == index
    return jnp.sum(jnp.where(hit, table, 0.0), axis=0, keepdims=True)


def place_row(row, index, rows):
    hit = iota((rows, row.shape[1]), 0) == index
    return jnp.where(hit, row, 0.0)


def colsum(value):
    return jnp.sum(value, axis=0, keepdims=True)


def adam_update(grad, moment, square):
    moment_new = MOMENT_DECAY * moment + (1.0 - MOMENT_DECAY) * grad
    square_new = SQUARE_DECAY * square + (1.0 - SQUARE_DECAY) * grad * grad
    direction = (
        moment_new
        / (1.0 - MOMENT_DECAY**STEP)
        / (jnp.sqrt(square_new / (1.0 - SQUARE_DECAY**STEP)) + ADAM_EPSILON)
    )
    return (moment_new, square_new, direction)


def total(value):
    return jnp.sum(jnp.sum(value, axis=1, keepdims=True), axis=0, keepdims=True)


def main_kernel(cfg, *refs):
    r = SimpleNamespace(**dict(zip(cfg.names, refs)))
    inner, n_ch, batch, local = cfg.inner, cfg.n_ch, cfg.batch, cfg.local
    classes, count = cfg.classes, cfg.count
    per = batch // n_ch
    chans = local * n_ch
    rows, small = cfg.rows, cfg.small
    tail = (rows - 256) // 2
    hw, hs = rows // 2, small // 2
    slots = SimpleNamespace(remote=0, local=0)

    img = lax.axis_index("img")
    me = lax.axis_index("ch")
    block = lax.div(img, inner)
    within = lax.rem(img, inner)
    core = lax.rem(block, 2)
    plane = lax.div(block, 2)
    partner = flip(block, 1)

    def dev(block_id, within_id, ch_id):
        return (block_id * inner + within_id, ch_id)

    pending = []

    def post(src, dst, landed, peer):
        slot = slots.remote
        slots.remote = slot + 1
        copy = pltpu.make_async_remote_copy(
            src_ref=src,
            dst_ref=dst,
            send_sem=r.send.at[slot],
            recv_sem=r.recv.at[slot],
            device_id=peer,
            device_id_type=MESH,
        )
        copy.start()
        pending.append(copy.wait_send)
        arrival = pltpu.make_async_remote_copy(
            src_ref=landed,
            dst_ref=landed,
            send_sem=r.send.at[slot],
            recv_sem=r.recv.at[slot],
            device_id=peer,
            device_id_type=MESH,
        )
        return arrival.wait_recv

    def here(src, dst):
        slot = slots.local
        slots.local = slot + 1
        copy = pltpu.make_async_copy(src, dst, r.lsem.at[slot])
        copy.start()
        return copy.wait

    outer_peers = [flip(block, mask) for mask in range(1, OUTER)]
    ch_peers = [flip(me, mask) for mask in range(1, n_ch)]
    inner_pairs = [
        (lax.rem(within + step, inner), lax.rem(within + inner - step, inner))
        for step in range(1, inner)
    ]
    up, down, far = (lax.rem(me + step, n_ch) for step in (1, 3, 2))
    up_peer, down_peer = dev(block, within, up), dev(block, within, down)

    class Ring:
        def __init__(self, source, target, passing):
            self.target, self.passing = target, passing
            self.waits = []
            self.early = [
                post(source(far, 0), passing.at[0], passing.at[0], up_peer),
                post(source(far, 1), passing.at[1], passing.at[1], down_peer),
            ]
            for im in range(per):
                self.waits += [
                    post(source(up, im), target(me, im), target(down, im), up_peer),
                    post(source(down, im), target(me, im), target(up, im), down_peer),
                ]

        def forward(self):
            self.early[0]()
            self.waits.append(
                post(self.passing.at[0], self.target(down, 0), self.target(far, 0), up_peer)
            )
            self.early[1]()
            self.waits.append(
                post(self.passing.at[1], self.target(up, 1), self.target(far, 1), down_peer)
            )

        def settle(self):
            for wait in self.waits:
                wait()

    barrier = pltpu.get_barrier_semaphore()
    everyone = [dev(peer, within, me) for peer in outer_peers]
    everyone += [dev(block, within, peer) for peer in ch_peers]
    everyone += [dev(block, peer, me) for peer, _ in inner_pairs]
    for peer in everyone:
        pl.semaphore_signal(barrier, inc=1, device_id=peer, device_id_type=MESH)

    got_entry = here(r.entry, r.entry_v)
    got_features = here(r.features, r.fown)
    got_exit = here(r.exit, r.exit_v)
    got_bypass = here(r.bypass, r.bypass_v)
    got_affine = here(r.affine, r.affine_v)
    got_cot = here(r.cotangent, r.cown)
    states = ((r.entry_m, r.entry_q), (r.exit_m, r.exit_q), (r.bypass_m, r.bypass_q)) if inner == 1 else ()
    held = [
        (here(m, getattr(r, v + "m")), here(q, getattr(r, v + "q")))
        for (m, q), v in zip(states, ("v1", "v2", "vs"))
    ]

    s_row, s_col = iota((hw, 384), 0), iota((hw, 384), 1)
    pick_first = to_bf16(s_col == jnp.where(s_row < 128, s_row, s_row + 128))
    pick_second = to_bf16(s_col == jnp.where(s_row < 128, s_row + 128, s_row + 128 + tail))
    r.padded[...] = jnp.zeros(r.padded.shape, BF16)

    def pack_own(value):
        r.padded[local : 2 * local, 0:rows] = value.astype(BF16)
        packed = nt(pick_first, r.padded[local : 3 * local, :])
        return (packed + nt(pick_second, r.padded[0 : 2 * local, :])).astype(BF16)

    got_entry()
    r.wz1[me] = pack_own(r.entry_v[...])
    pl.semaphore_wait(barrier, len(everyone))

    def to_channels(buffer):
        return [
            post(buffer.at[me], buffer.at[me], buffer.at[peer], dev(block, within, peer))
            for peer in ch_peers
        ]

    entry_waits = to_channels(r.wz1)
    got_features()
    feature_waits = [
        post(
            r.fown.at[pl.ds(per * peer, per)],
            r.fbuf.at[me],
            r.fbuf.at[peer],
            dev(block, within, peer),
        )
        for peer in ch_peers
    ]
    r.fbuf[me] = r.fown[pl.ds(per * me, per)]
    flat = jnp.concatenate([r.fown[b] for b in range(batch)], axis=1)
    wide = flat.astype(F32)
    square = wide * wide
    square_hi = square.astype(BF16)
    square_lo = (square - square_hi.astype(F32)).astype(BF16)
    level = iota((16, 256), 0)
    first_mask = jnp.concatenate([to_bf16(level == r.groups[b]) for b in range(batch)], axis=1)
    second_mask = jnp.concatenate([to_bf16(level == r.groups[b] + 4) for b in range(batch)], axis=1)
    sums = nt(first_mask, flat) + nt(second_mask, square_hi) + nt(second_mask, square_lo)

    got_affine()
    r.aff_z[me] = jnp.zeros((32, 128), F32)
    r.aff_z[me, 0 : 2 * classes + 3, 0:local] = r.affine_v[...]
    r.aff_z[me, 24:32, 0:local] = sums[0:8]
    affine_waits = to_channels(r.aff_z)

    got_exit()
    got_bypass()
    r.wz2[me, 0:hw, :] = pack_own(r.exit_v[...])
    e_row, e_col = iota((local, 128), 0), iota((local, 128), 1)
    value = r.bypass_v[...].astype(BF16)
    r.wz2[me, hw : hw + hs, :] = (
        nn(value[:hs], to_bf16(e_col == e_row)) + nn(value[hs:], to_bf16(e_col == e_row + local))
    ).astype(BF16)

    exit_waits = to_channels(r.wz2)
    got_cot()
    cotangent = Ring(
        lambda c, im: r.cown.at[per * c + im], lambda c, im: r.cbuf.at[c, im], r.pass_c
    )

    lane = iota((512, 512), 0)
    column = iota((512, 512), 1)
    spot = 256 * ((lane >> 6) & 1) + 64 * (lane >> 7) + (lane & 63)
    r.unpack[...] = to_bf16(column == spot)

    def ordered_sum(ref, size):
        result = ref[0]
        for slot in range(1, size):
            result = result + ref[slot]
        return result

    class AllReduce:
        def __init__(self, number):
            self.over_outer, self.over_inner, self.over_ch = (
                getattr(r, axis + str(number), None) for axis in "abc"
            )

        def begin(self, value):
            ref = self.over_outer
            ref[block] = value
            self.waits = [
                post(ref.at[block], ref.at[block], ref.at[peer], dev(peer, within, me))
                for peer in outer_peers
            ]

        def plane(self):
            for wait in self.waits:
                wait()
            value = ordered_sum(self.over_outer, OUTER)
            if inner > 1:
                ref = self.over_inner
                ref[within] = value
                waits = [
                    post(ref.at[within], ref.at[within], ref.at[back], dev(block, peer, me))
                    for peer, back in inner_pairs
                ]
                for wait in waits:
                    wait()
                value = ordered_sum(ref, inner)
            return value

        def middle(self):
            self.over_ch[me] = self.plane()
            self.waits = to_channels(self.over_ch)

        def end(self):
            for wait in self.waits:
                wait()
            return ordered_sum(self.over_ch, n_ch)

    def rows_of(ref, index):
        size = ref.shape[0] // OUTER
        return ref.at[pl.ds(pl.multiple_of(size * index, 16), size)]

    def unpack_own(ref, full):
        own = rows_of(ref, block)
        if full.shape[0] == hw:
            own[0:128, :] = full[0:128, 0:256]
            own[128:256, :] = full[0:128, 256:512]
            own[256 : 256 + tail, :] = full[128:, 0:256]
            own[256 + tail :, :] = full[128:, 256:512]
        else:
            own[0:hs, :] = full[:, 0:256]
            own[hs:, :] = full[:, 256:512]

    def spread(ref):
        own = rows_of(ref, block)
        return {
            mask: post(own, own, rows_of(ref, flip(block, mask)), dev(flip(block, mask), within, me))
            for mask in (2, 4, 6, 1)
        }

    def forward(ref, waits):
        rest = [waits[1]]
        for mask in (2, 4, 6):
            waits[mask]()
            mine = rows_of(ref, flip(block, mask))
            theirs = rows_of(ref, flip(partner, mask))
            rest.append(post(mine, mine, theirs, dev(partner, within, me)))
        return rest

    def widen(buffer):
        packed = jnp.concatenate([buffer[c] for c in range(n_ch)], axis=1)
        return nn(packed, r.unpack[...]).astype(BF16)

    def wide_lanes(ref):
        parts = [
            ref[c] + pltpu.roll(ref[c + 1], local, axis=1) for c in range(0, n_ch, 2)
        ]
        return jnp.concatenate(parts, axis=1)

    for wait in affine_waits:
        wait()
    affine = wide_lanes(r.aff_z)
    input_sums = AllReduce(1)
    input_sums.begin(affine[24:32])
    for wait in entry_waits:
        wait()
    unpack_own(r.w1, widen(r.wz1))
    gather1 = spread(r.w1)

    ident = to_bf16(iota((256, 256), 0) == iota((256, 256), 1))
    r.ident[...] = ident
    q_out, q_in = iota((256, 256), 0), iota((256, 256), 1)
    r.shift[0] = to_bf16((q_in == q_out + 1) & ((q_out & 15) < 15))
    r.shift[1] = to_bf16((q_in == q_out - 1) & ((q_out & 15) > 0))

    for wait in exit_waits:
        wait()
    full = widen(r.wz2)
    unpack_own(r.w2, full[0:hw])
    unpack_own(r.ws, full[hw:])
    gather2 = spread(r.w2)
    gather3 = spread(r.ws)

    rho, px = iota((512, 256), 0), iota((512, 256), 1)
    version, a, b_ = rho >> 8, (rho >> 7) & 1, (rho >> 6) & 1
    col = (rho & 15) + version * (1 - 2 * b_)
    target = (2 * ((rho & 63) >> 4) + a) * 32 + 2 * col + b_
    r.gridder[...] = to_bf16((px == target) & (col >= 0) & (col < 16))
    zeros = jnp.zeros((16, 256), BF16)
    for im in range(per):
        for ver in range(3):
            r.h1s[ver, im, 0:16, :] = zeros
            r.h1s[ver, im, 272:288, :] = zeros
        for ver in range(2):
            for ph in range(4):
                for ref in (r.h2s, r.dzs):
                    ref[ver, ph, im, 0:16, :] = zeros
                    ref[ver, ph, im, 272:288, :] = zeros

    def channel_major(ref, im, lanes):
        return jnp.concatenate([ref[c, im, :, lanes] for c in range(n_ch)], axis=0)

    for wait in feature_waits:
        wait()
    for im in range(per):
        r.fpm[256 * im : 256 * im + 256, :] = nt(
            ident, channel_major(r.fbuf, im, slice(0, 256))
        ).astype(BF16)

    stats = input_sums.plane()
    mean1 = stats[0:4] / count
    inv1 = lax.rsqrt(stats[4:8] / count - mean1 * mean1 + NORM_EPSILON)
    gain = affine[2 * classes : 2 * classes + 1]
    shift = affine[2 * classes + 1 : 2 * classes + 2]
    out_bias = affine[2 * classes + 2 : 2 * classes + 3]
    group, label, mean1_b, inv1_b, gamma_b, beta_b, mask_b = [], [], [], [], [], [], []
    for im in range(per):
        group.append(r.groups[per * me + im])
        label.append(r.labels[per * me + im])
        mean1_b.append(pick_row(mean1, group[im]))
        inv1_b.append(pick_row(inv1, group[im]))
        gamma_b.append(pick_row(affine, label[im]))
        beta_b.append(pick_row(affine, label[im] + classes))
        width = r.widths[group[im]]
        mask_b.append(
            jnp.where(iota((1, chans), 1) < width * (chans // LEVELS), 1.0, 0.0)
        )

    for im in range(per):
        normal = (r.fpm[256 * im : 256 * im + 256, :].astype(F32) - mean1_b[im]) * inv1_b[im]
        pre = gamma_b[im] * normal + beta_b[im]
        hidden = (pre * sigmoid(pre)).astype(BF16)
        r.h1s[1, im, 16:272, :] = hidden
        r.h1s[0, im, 16:272, :] = nn(r.shift[1], hidden).astype(BF16)
        r.h1s[2, im, 16:272, :] = nn(r.shift[0], hidden).astype(BF16)
        r.h1cm[:, 256 * im : 256 * im + 256] = nt(ident, hidden).astype(BF16)
        if im == 0:
            rest = forward(r.w1, gather1)

    cotangent.forward()
    for wait in rest:
        wait()

    def back_product(parts, ref):
        result = nt(parts[0], ref[0:256, :])
        for tap in range(1, 9):
            result = result + nt(parts[tap], ref[256 * tap : 256 * tap + 256, :])
        return result

    def taps():
        return [(dy, dx) for dy in range(3) for dx in range(3)]

    def stack(pieces):
        return jnp.concatenate(pieces, axis=0)

    def conv1(phase, carry):
        a, c = lax.div(phase, 2), lax.rem(phase, 2)
        parts = []
        for dy, dx in taps():
            first = pl.multiple_of(16 * lax.div(a + dy + 1, 2), 16)
            ver = lax.div(c + dx + 1, 2)
            parts.append(
                stack([r.h1s[ver, im, pl.ds(first, 256), :] for im in range(per)])
            )
        y = nn(jnp.concatenate(parts, axis=1), r.w1[...])
        r.y1[phase] = y
        out = []
        for im in range(per):
            piece = y[256 * im : 256 * im + 256]
            out.append(carry[2 * im] + colsum(piece))
            out.append(carry[2 * im + 1] + colsum(piece * piece))
        return tuple(out)

    nought = jnp.zeros((1, chans), F32)
    mid = lax.fori_loop(0, 4, conv1, (nought,) * (2 * per))
    payload = jnp.zeros((8, chans), F32)
    for im in range(per):
        payload = payload + place_row(mid[2 * im], group[im], 8)
        payload = payload + place_row(mid[2 * im + 1], group[im] + 4, 8)
    mid_sums = AllReduce(2)
    mid_sums.begin(payload)

    rest = forward(r.w2, gather2) + forward(r.ws, gather3)
    mid_sums.middle()

    r.cbuf[me] = r.cown[pl.ds(per * me, per)]
    cotangent.settle()
    for im in range(per):
        for n in range(4):
            piece = channel_major(r.cbuf, im, slice(256 * n, 256 * n + 256))
            grid = nt(r.gridder[...], piece).astype(BF16)
            for ver in range(2):
                for ph in range(4):
                    at = 256 * ver + 64 * ph
                    r.dzs[ver, ph, im, 16 + 64 * n : 80 + 64 * n, :] = grid[at : at + 64]

    coarse = jnp.zeros((256 * per, chans), F32)
    for ph in range(4):
        coarse = coarse + stack([r.dzs[0, ph, im, 16:272, :] for im in range(per)]).astype(F32)
    bias_sum = colsum(coarse)
    r.dzc[...] = coarse.astype(BF16)

    def tap_slice(ref, a, c, dy, dx, im):
        row, colm = a + dy + 1, c + dx + 1
        first = pl.multiple_of(16 * lax.div(row, 2), 16)
        ph = 2 * lax.rem(row, 2) + lax.rem(colm, 2)
        side_step = lax.div(colm, 2) - 1
        return ref[side_step * side_step, ph, im, pl.ds(first, 256), :]

    for wait in rest:
        wait()

    def back2(phase, carry):
        a, c = lax.div(phase, 2), lax.rem(phase, 2)
        parts = [
            stack([tap_slice(r.dzs, a, c, 2 - dy, 2 - dx, im) for im in range(per)])
            for dy, dx in taps()
        ]
        r.act[phase] = back_product(parts, r.w2)
        return carry

    lax.fori_loop(0, 4, back2, 0)

    stats = mid_sums.end()
    mean2 = stats[0:4] / (4.0 * count)
    inv2 = lax.rsqrt(stats[4:8] / (4.0 * count) - mean2 * mean2 + NORM_EPSILON)
    mean2_b = [pick_row(mean2, group[im]) for im in range(per)]
    inv2_b = [pick_row(inv2, group[im]) for im in range(per)]

    def hidden2(phase, carry):
        c = lax.rem(phase, 2)
        out = []
        for im in range(per):
            span = slice(256 * im, 256 * im + 256)
            normal = (r.y1[phase, span, :] - mean2_b[im]) * inv2_b[im]
            r.y1[phase, span, :] = normal
            pre = gain * normal + shift
            sig = sigmoid(pre)
            hidden = (pre * sig * mask_b[im]).astype(BF16)
            act = r.act[phase, span, :] * (sig * (1.0 + pre * (1.0 - sig)) * mask_b[im])
            r.act[phase, span, :] = act
            out.append(carry[2 * im] + colsum(act))
            out.append(carry[2 * im + 1] + colsum(act * normal))
            r.h2s[0, phase, im, 16:272, :] = hidden
            r.h2s[1, phase, im, 16:272, :] = nn(r.shift[c], hidden).astype(BF16)
            lanes = pl.ds(pl.multiple_of(512 * phase + 256 * im, 256), 256)
            r.h2cm[:, lanes] = nt(r.ident[...], hidden).astype(BF16)
        return tuple(out)

    mid = lax.fori_loop(0, 4, hidden2, (nought,) * (2 * per))
    payload = place_row(bias_sum, 8, 16)
    for im in range(per):
        payload = payload + place_row(mid[2 * im], group[im], 16)
        payload = payload + place_row(mid[2 * im + 1], group[im] + 4, 16)
    back_sums = AllReduce(3)
    back_sums.begin(payload)

    r.short[...] = nn(r.fpm[...], r.ws[...]) + out_bias
    def conv2(phase, carry):
        a, c = lax.div(phase, 2), lax.rem(phase, 2)
        parts = [
            stack([tap_slice(r.h2s, a, c, dy, dx, im) for im in range(per)]) for dy, dx in taps()
        ]
        y = nn(jnp.concatenate(parts, axis=1), r.w2[...]) + r.short[...]
        r.rc[phase] = y.astype(BF16)
        return carry

    lax.fori_loop(0, 4, conv2, 0)
    for im in range(per):
        for n in range(4):
            first = 256 * im + 64 * n
            piece = stack([r.rc[ph, first : first + 64, :] for ph in range(4)])
            r.ocm[im, :, 256 * n : 256 * n + 256] = tn(piece, r.gridder[0:256, :]).astype(BF16)

    def own_channels(ref, index, im):
        return ref.at[im, pl.ds(pl.multiple_of(local * index, local), local), :]

    def give_back(ref, out, passing):
        for im in range(per):
            out[per * me + im] = own_channels(ref, me, im)[...]
        return Ring(
            lambda c, im: own_channels(ref, c, im), lambda c, im: out.at[per * c + im], passing
        )

    back_sums.middle()
    block_output = give_back(r.ocm, r.out_v, r.pass_o)

    def grad2(tap, carry):
        dy, dx = lax.div(tap, 3), lax.rem(tap, 3)
        pieces = []
        for ph in range(4):
            a, c = ph // 2, ph % 2
            for im in range(per):
                pieces.append(tap_slice(r.dzs, a, c, 2 - dy, 2 - dx, im))
        first = pl.multiple_of(256 * tap, 256)
        r.dw2[pl.ds(first, 256), :] = nn(r.h2cm[...], stack(pieces))
        return carry

    for im in range(per):
        piece = channel_major(r.fbuf, im, slice(0, 256))
        grad = nn(piece, r.dzc[256 * im : 256 * im + 256, :])
        if im == 0:
            r.dws[...] = grad
        else:
            r.dws[...] = r.dws[...] + grad

    class GradSum:
        def __init__(self, number, fetch):
            self.fetch = fetch
            self.waits = []
            for part in PARTS:
                setattr(self, part, getattr(r, part + str(number)))

        def begin(self, parts=range(4)):
            for u in parts:
                self.s1[u] = self.fetch(2 * u + 1 - core).astype(BF16)
                self.waits.append(
                    post(self.s1.at[u], self.r1.at[u], self.r1.at[u], dev(partner, within, me))
                )

        def settle(self):
            for wait in self.waits:
                wait()

        def first(self):
            self.settle()
            self.waits = []
            for mask in (6, 2, 4, 0):
                peer = flip(block, mask)
                u = lax.div(peer, 2)
                value = self.fetch(peer) + self.r1[u].astype(F32)
                if mask == 0:
                    self.r2[plane] = value.astype(BF16)
                    continue
                self.s2[u] = value.astype(BF16)
                self.waits.append(
                    post(self.s2.at[u], self.r2.at[plane], self.r2.at[u], dev(peer, within, me))
                )

        def second(self):
            self.settle()
            value = self.r2[0].astype(F32)
            for u in range(1, 4):
                value = value + self.r2[u].astype(F32)
            value = value.astype(BF16)
            left = [value[0:128], value[256 : 256 + tail]]
            right = [value[128:256], value[256 + tail : rows]]
            if value.shape[0] > rows:
                left.append(value[rows : rows + hs])
                right.append(value[rows + hs :])
            pair = jnp.concatenate([stack(left), stack(right)], axis=1)
            packed = nt(pair, r.unpack[...]).astype(BF16)
            for c in range(n_ch):
                self.s3[c] = packed[:, 128 * c : 128 * c + 128]
            self.r3[me] = self.s3[me]
            self.waits = [
                post(self.s3.at[peer], self.r3.at[me], self.r3.at[peer], dev(block, within, peer))
                for peer in ch_peers
            ]

        def end(self, out, out_small=None):
            self.settle()
            done = self.r3[0].astype(F32)
            for c in range(1, n_ch):
                done = done + self.r3[c].astype(F32)
            turned = done[0:128].T
            out[:, 0:128] = turned[0:local]
            out[:, 128:256] = turned[local:]
            gap = jnp.zeros((128 - tail, 128), F32)
            turned = stack([done[128 : 128 + tail], gap]).T
            ends = turned[0:local] + pltpu.roll(turned[local:], tail, axis=1)
            out[:, 256:rows] = ends[:, 0 : rows - 256]
            if out_small is not None:
                last = done[hw:]
                out_small[0:hs, :] = last[:, 0:local]
                out_small[hs:, :] = pltpu.roll(last, local, axis=1)[:, 0:local]

    def block_rows(ref, size, index):
        return ref[pl.ds(pl.multiple_of(size * index, 8), size), :]

    second = GradSum(2, lambda k: stack([block_rows(r.dw2, rows, k), block_rows(r.dws, small, k)]))
    entry = GradSum(1, lambda k: block_rows(r.dw1, rows, k))
    for u, (first, last) in enumerate(((0, 3), (3, 5), (5, 7), (7, 9))):
        lax.fori_loop(first, last, grad2, 0)
        second.begin([u])
    stats = back_sums.end()
    affine_grad2 = stats
    p1_b = [pick_row(stats[0:4], group[im]) / (4.0 * count) for im in range(per)]
    p2_b = [pick_row(stats[4:8], group[im]) / (4.0 * count) for im in range(per)]

    for im in range(per):
        span = slice(256 * im, 256 * im + 256)
        scale = gain * inv2_b[im]
        combos = []
        for a in range(2):
            grads = []
            for c in range(2):
                ph = 2 * a + c
                d = scale * (r.act[ph, span, :] - (p1_b[im] + r.y1[ph, span, :] * p2_b[im]))
                grads.append(d.astype(BF16))
            right = nn(r.shift[0], grads[0])
            left = nn(r.shift[1], grads[1])
            even, odd = grads[0].astype(F32), grads[1].astype(F32)
            combos.append((odd + right, even + odd, left + even))
        gap = jnp.zeros((16, chans), F32)
        for dx in range(3):
            upper, lower = combos[0][dx], combos[1][dx]
            r.field[dx, im] = (lower + stack([upper[16:], gap])).astype(BF16)
            r.field[3 + dx, im] = (upper + lower).astype(BF16)
            r.field[6 + dx, im] = (stack([gap, lower[:-16]]) + upper).astype(BF16)

    second.first()
    block_output.forward()

    def grad1(tap, carry):
        first = pl.multiple_of(256 * tap, 256)
        r.dw1[pl.ds(first, 256), :] = nn(
            r.h1cm[...], stack([r.field[tap, im] for im in range(per)])
        )
        return carry

    for u, (first, last) in enumerate(((0, 3), (3, 5), (5, 7), (7, 9))):
        lax.fori_loop(first, last, grad1, 0)
        entry.begin([u])

    parts = [stack([r.field[tap, im] for im in range(per)]) for tap in range(9)]
    dh1 = back_product(parts, r.w1)
    payload = jnp.zeros((8, chans), F32)
    class_rows = jnp.zeros((24, chans), F32)
    for im in range(per):
        span = slice(256 * im, 256 * im + 256)
        normal = (r.fpm[span, :].astype(F32) - mean1_b[im]) * inv1_b[im]
        pre = gamma_b[im] * normal + beta_b[im]
        sig = sigmoid(pre)
        act = dh1[span] * (sig * (1.0 + pre * (1.0 - sig)))
        r.act1[span, :] = act
        q1, q2 = colsum(act), colsum(act * normal)
        class_rows = class_rows + place_row(q2, label[im], 24)
        class_rows = class_rows + place_row(q1, label[im] + classes, 24)
        payload = payload + place_row(gamma_b[im] * q1, group[im], 8)
        payload = payload + place_row(gamma_b[im] * q2, group[im] + 4, 8)
    last_sums, class_sums = AllReduce(4), AllReduce(6)
    last_sums.begin(payload)
    entry.first()
    class_sums.begin(class_rows)
    last_sums.middle()
    second.second()
    r.dshort[...] = nt(r.dzc[...], r.ws[...])
    stats = last_sums.end()
    for im in range(per):
        span = slice(256 * im, 256 * im + 256)
        normal = (r.fpm[span, :].astype(F32) - mean1_b[im]) * inv1_b[im]
        r1 = pick_row(stats[0:4], group[im]) / count
        r2 = pick_row(stats[4:8], group[im]) / count
        grad = inv1_b[im] * (gamma_b[im] * r.act1[span, :] - (r1 + normal * r2))
        grad = (grad + r.dshort[span, :]).astype(BF16)
        r.dcm[im] = nt(r.ident[...], grad).astype(BF16)
    entry.second()
    input_gradient = give_back(r.dcm, r.dx_v, r.pass_x)
    class_sums.middle()
    second.end(r.grad2, r.grad3)

    row = iota((8, 128), 0)

    def norm_rows(index, weight, grad, v):
        for wait in held[index]:
            wait()
        master = weight[...]
        _, _, direction = adam_update(
            grad[...], getattr(r, v + "m")[...], getattr(r, v + "q")[...]
        )
        update = direction + WEIGHT_DECAY * master
        rows_w = jnp.where(row == index, total(master * master), 0.0)
        return rows_w + jnp.where(row == index + 3, total(update * update), 0.0)

    if inner == 1:
        norms = norm_rows(1, r.exit_v, r.grad2, "v2") + norm_rows(2, r.bypass_v, r.grad3, "vs")

    if inner == 1:
        entry.end(r.grad1)
        norms = norms + norm_rows(0, r.entry_v, r.grad1, "v1")
        norm_sums = AllReduce(5)
        norm_sums.begin(norms)
        input_gradient.forward()
        norm_sums.middle()
    else:
        entry.end(r.grad1)
        input_gradient.forward()
        r.norms[...] = jnp.zeros((8, 128), F32)

    table = jnp.zeros((24, chans), F32)
    table = table + jnp.where(iota((24, chans), 0) < 2 * classes, class_sums.end(), 0.0)
    table = table + place_row(colsum(affine_grad2[4:8]), 2 * classes, 24)
    table = table + place_row(colsum(affine_grad2[0:4]), 2 * classes + 1, 24)
    table = table + place_row(affine_grad2[8:9], 2 * classes + 2, 24)
    mine = jnp.zeros((24, 128), F32)
    for c in range(n_ch):
        piece = table[:, 128 * (c // 2) : 128 * (c // 2) + 128]
        if c % 2:
            piece = pltpu.roll(piece, local, axis=1)
        mine = mine + jnp.where(me == c, piece, 0.0)
    r.affine_grad[...] = mine

    block_output.settle()
    written = [here(r.out_v, r.out)]
    input_gradient.settle()
    written.append(here(r.dx_v, r.dx))
    if inner == 1:
        r.norms[...] = norm_sums.end()
    for wait in written:
        wait()
    for wait in pending:
        wait()
    cfg.used.append((slots.remote, slots.local))


def final_kernel(cfg, *refs):
    r = SimpleNamespace(**dict(zip(cfg.names, refs)))
    classes = cfg.classes
    local = cfg.local
    r.block_output[...] = r.out[...]
    r.input_gradient[...] = r.dx[...].astype(F32)
    norms = jnp.sqrt(r.norms[...])
    weight_norm, update_norm = norms[0:3, 0:1], norms[3:6, 0:1]
    ratio = weight_norm / update_norm
    at = iota((3, 3), 1)
    r.trust_norms[...] = jnp.where(
        at == 0, weight_norm, jnp.where(at == 1, update_norm, ratio)
    )
    sets = (
        (r.entry, r.entry_m, r.entry_q, r.entry_g, r.entry_1, r.entry_2, r.entry_w),
        (r.exit, r.exit_m, r.exit_q, r.exit_g, r.exit_1, r.exit_2, r.exit_w),
        (r.bypass, r.bypass_m, r.bypass_q, r.bypass_g, r.bypass_1, r.bypass_2, r.bypass_w),
    )
    for index, (weight, m, q, g, first, second, result) in enumerate(sets):
        master = weight[...]
        moment, square, direction = adam_update(g[...], m[...], q[...])
        update = direction + WEIGHT_DECAY * master
        first[...] = moment
        second[...] = square
        result[...] = master - MATRIX_RATE * ratio[index : index + 1] * update
    grad = r.affine_grad[0 : 2 * classes + 3, 0:local]
    moment, square, direction = adam_update(grad, r.affine_m[...], r.affine_q[...])
    r.affine_1[...] = moment
    r.affine_2[...] = square
    r.affine_w[...] = r.affine[...] - AFFINE_RATE * direction


def per_device(
    features,
    labels,
    groups,
    widths,
    entry_conv,
    entry_moment,
    entry_square,
    exit_conv,
    exit_moment,
    exit_square,
    bypass_conv,
    bypass_moment,
    bypass_square,
    norm_affine,
    norm_moment,
    norm_square,
    cotangent,
):
    n_img, n_ch = lax.axis_size("img"), lax.axis_size("ch")
    batch, local, pixels = features.shape
    chans = local * n_ch
    side = math.isqrt(pixels)
    inner = n_img // OUTER
    classes = (norm_affine.shape[0] - 3) // 2
    per = batch // n_ch
    assert (side, chans, n_ch, local, batch % n_ch) == (16, 256, 4, 64, 0) and per == 2
    rows, small = entry_conv.shape[0] * inner, bypass_conv.shape[0] * inner
    masters = (entry_conv, exit_conv, bypass_conv)
    if inner == 1:
        blocks = masters
    else:
        sets = [[o * inner + i for i in range(inner)] for o in range(OUTER)]
        blocks = tuple(
            lax.all_gather(w.astype(BF16), "img", axis=0, tiled=True, axis_index_groups=sets)
            for w in masters
        )

    vmem = pl.BlockSpec(memory_space=pltpu.VMEM)
    smem = pl.BlockSpec(memory_space=pltpu.SMEM)
    anywhere = pl.BlockSpec(memory_space=pl.ANY)
    states = dict(
        entry_m=entry_moment.T,
        entry_q=entry_square.T,
        exit_m=exit_moment.T,
        exit_q=exit_square.T,
        bypass_m=bypass_moment,
        bypass_q=bypass_square,
    )
    inputs = dict(
        labels=(labels, smem),
        groups=(groups, smem),
        widths=(widths, smem),
        features=(features, anywhere),
        cotangent=(cotangent, anywhere),
        entry=(blocks[0].T, anywhere),
        exit=(blocks[1].T, anywhere),
        bypass=(blocks[2], anywhere),
        affine=(norm_affine, anywhere),
    )
    if inner == 1:
        inputs.update({name: (value, anywhere) for name, value in states.items()})
    sds = jax.ShapeDtypeStruct
    outputs = dict(
        out=(sds(cotangent.shape, BF16), anywhere),
        dx=(sds(features.shape, BF16), anywhere),
        grad1=(sds((local, rows), F32), vmem),
        grad2=(sds((local, rows), F32), vmem),
        grad3=(sds((small, local), F32), vmem),
        affine_grad=(sds((24, 128), F32), vmem),
        norms=(sds((8, 128), F32), vmem),
    )
    pix = pixels * per
    taps9 = 9 * chans
    held = lambda shape, dtype=BF16: pltpu.VMEM(shape, dtype)
    scratch = dict(
        fown=held((batch, local, pixels)),
        cown=held((batch, local, 4 * pixels)),
        pass_c=held((2, local, 4 * pixels)),
        pass_o=held((2, local, 4 * pixels)),
        pass_x=held((2, local, pixels)),
        out_v=held(cotangent.shape),
        dx_v=held(features.shape),
        fbuf=held((n_ch, per, local, pixels)),
        cbuf=held((n_ch, per, local, 4 * pixels)),
        entry_v=held((local, rows), blocks[0].dtype),
        exit_v=held((local, rows), blocks[1].dtype),
        bypass_v=held((small, local), blocks[2].dtype),
        affine_v=held(norm_affine.shape, F32),
        padded=held((3 * local, 384)),
        wz1=held((n_ch, rows // 2, 128)),
        wz2=held((n_ch, (rows + small) // 2, 128)),
        aff_z=held((n_ch, 32, 128), F32),
        w1=held((taps9, chans)),
        w2=held((taps9, chans)),
        ws=held((chans, chans)),
        unpack=held((512, 512)),
        ident=held((256, 256)),
        shift=held((2, 256, 256)),
        gridder=held((512, 256)),
        fpm=held((pix, chans)),
        h1s=held((3, per, pixels + 32, chans)),
        h1cm=held((chans, pix)),
        y1=held((4, pix, chans), F32),
        act=held((4, pix, chans), F32),
        h2s=held((2, 4, per, pixels + 32, chans)),
        dzs=held((2, 4, per, pixels + 32, chans)),
        h2cm=held((chans, 4 * pix)),
        short=held((pix, chans), F32),
        dshort=held((pix, chans), F32),
        dzc=held((pix, chans)),
        act1=held((pix, chans), F32),
        rc=held((4, pix, chans)),
        ocm=held((per, chans, 4 * pixels)),
        dcm=held((per, chans, pixels)),
        field=held((9, per, pixels, chans)),
        dw1=held((taps9, chans), F32),
        dw2=held((taps9, chans), F32),
        dws=held((chans, chans), F32),
    )
    for number, size in ((1, rows), (2, rows + small)):
        shapes = ((4, size, chans),) * 4 + ((n_ch, size // 2, 128),) * 2
        for part, shape in zip(PARTS, shapes):
            scratch[part + str(number)] = held(shape)
    exchanges = [(8, chans), (8, chans), (16, chans), (8, chans), (8, 128), (24, chans)]
    if inner == 1:
        for v, shape in (("v1", (local, rows)), ("v2", (local, rows)), ("vs", (small, local))):
            scratch[v + "m"] = held(shape, F32)
            scratch[v + "q"] = held(shape, F32)
    for number, shape in enumerate(exchanges, 1):
        for axis, size in zip("abc", (OUTER, inner, n_ch)):
            if size > 1:
                scratch[axis + str(number)] = held((size,) + shape, F32)
    remote_count = 3 * 3 + 4 * 4 * per + 3 * 7 + 2 * 13 + len(exchanges) * (7 + 3 + inner - 1)
    scratch.update(
        send=pltpu.SemaphoreType.DMA((remote_count,)),
        recv=pltpu.SemaphoreType.DMA((remote_count,)),
        lsem=pltpu.SemaphoreType.DMA((20,)),
    )
    cfg = SimpleNamespace(
        names=[*inputs, *outputs, *scratch],
        inner=inner,
        n_ch=n_ch,
        batch=batch,
        local=local,
        classes=classes,
        count=float(batch * n_img // widths.shape[0] * pixels),
        rows=rows,
        small=small,
        used=[],
    )
    out, dx, grad1, grad2, grad3, affine_grad, norms = pl.pallas_call(
        functools.partial(main_kernel, cfg),
        out_shape=[s for s, _ in outputs.values()],
        in_specs=[s for _, s in inputs.values()],
        out_specs=[s for _, s in outputs.values()],
        scratch_shapes=list(scratch.values()),
        compiler_params=pltpu.CompilerParams(
            collective_id=0, has_side_effects=True, vmem_limit_bytes=VMEM_LIMIT
        ),
        name="block_step",
    )(*[v for v, _ in inputs.values()])
    assert max(n for n, _ in cfg.used) <= remote_count and max(n for _, n in cfg.used) <= 20

    grads = [grad1, grad2, grad3]
    if inner > 1:
        grads = [
            lax.psum_scatter(g, "img", scatter_dimension=0, axis_index_groups=sets, tiled=True)
            for g in (grad1.T, grad2.T, grad3)
        ]
        updates = []
        for w, g, m, s in zip(
            masters,
            grads,
            (entry_moment, exit_moment, bypass_moment),
            (entry_square, exit_square, bypass_square),
        ):
            updates.append(adam_update(g, m, s)[2] + WEIGHT_DECAY * w)
        sums = lax.psum(
            jnp.stack([jnp.sum(w * w) for w in masters] + [jnp.sum(u * u) for u in updates]),
            ("img", "ch"),
        )
        norms = jnp.broadcast_to(jnp.pad(sums, (0, 2))[:, None], (8, 128))
        grads = [grads[0].T, grads[1].T, grads[2]]

    args = dict(
        out=out,
        dx=dx,
        norms=norms,
        affine_grad=affine_grad,
        entry_g=grads[0],
        exit_g=grads[1],
        bypass_g=grads[2],
        entry=entry_conv.T,
        exit=exit_conv.T,
        bypass=bypass_conv,
        **states,
        affine=norm_affine,
        affine_m=norm_moment,
        affine_q=norm_square,
    )
    tall = sds(entry_conv.shape[::-1], F32)
    short, wide = (sds(w.shape, F32) for w in (bypass_conv, norm_affine))
    results = dict(
        block_output=sds(cotangent.shape, BF16),
        input_gradient=sds(features.shape, F32),
        entry_1=tall,
        entry_2=tall,
        entry_w=tall,
        exit_1=tall,
        exit_2=tall,
        exit_w=tall,
        bypass_1=short,
        bypass_2=short,
        bypass_w=short,
        affine_1=wide,
        affine_2=wide,
        affine_w=wide,
        trust_norms=sds((3, 3), F32),
    )
    end_cfg = SimpleNamespace(names=[*args, *results], classes=classes, local=local)
    final = pl.pallas_call(
        functools.partial(final_kernel, end_cfg),
        out_shape=list(results.values()),
        in_specs=[vmem] * len(args),
        out_specs=[vmem] * len(results),
        compiler_params=pltpu.CompilerParams(vmem_limit_bytes=VMEM_LIMIT),
        name="finish",
    )(*args.values())
    return tuple(v.T if s is tall else v for v, s in zip(final, results.values()))


def solution(mesh):
    wide = P("img", "ch")
    deep = P("img", "ch", None)
    table = P(None, "ch")
    return jax.shard_map(
        per_device,
        mesh=mesh,
        in_specs=(deep, P("img"), P("img"), P()) + (wide,) * 9 + (table,) * 3 + (deep,),
        out_specs=(deep, deep) + (wide,) * 9 + (table,) * 3 + (P(),),
        check_vma=False,
    )
```

```python
import functools
import math
from types import SimpleNamespace

import jax
import jax.numpy as jnp
from jax import lax
from jax.experimental import pallas as pl
from jax.experimental.pallas import tpu as pltpu
from jax.sharding import PartitionSpec as P

LEVELS = 4
STEP = 5
NORM_EPSILON = 1e-05
ADAM_EPSILON = 1e-06
MOMENT_DECAY = 0.9
SQUARE_DECAY = 0.999
WEIGHT_DECAY = 0.01
MATRIX_RATE = 0.3
AFFINE_RATE = 0.2

OUTER = 8
VMEM_LIMIT = 56 * 1024 * 1024
BF16 = jnp.bfloat16
F32 = jnp.float32
MESH = pl.DeviceIdType.MESH
PARTS = ("s1", "r1", "s2", "r2", "s3", "r3")


def nn(left, right):
    return lax.dot_general(left, right, (((1,), (0,)), ((), ())), preferred_element_type=F32)


def nt(left, right):
    return lax.dot_general(left, right, (((1,), (1,)), ((), ())), preferred_element_type=F32)


def tn(left, right):
    return lax.dot_general(left, right, (((0,), (0,)), ((), ())), preferred_element_type=F32)


def flip(index, mask):
    result = index
    for bit in range(3):
        if (mask >> bit) & 1:
            digit = lax.rem(lax.div(index, 1 << bit), 2)
            result = result + (1 - 2 * digit) * (1 << bit)
    return result


def sigmoid(value):
    return 0.5 * jnp.tanh(0.5 * value) + 0.5


def iota(shape, axis):
    return lax.broadcasted_iota(jnp.int32, shape, axis)


def to_bf16(condition):
    return jnp.where(condition, 1.0, 0.0).astype(BF16)


def pick_row(table, index):
    hit = iota(table.shape, 0) == index
    return jnp.sum(jnp.where(hit, table, 0.0), axis=0, keepdims=True)


def place_row(row, index, rows):
    hit = iota((rows, row.shape[1]), 0) == index
    return jnp.where(hit, row, 0.0)


def colsum(value):
    return jnp.sum(value, axis=0, keepdims=True)


def adam_update(grad, moment, square):
    moment_new = MOMENT_DECAY * moment + (1.0 - MOMENT_DECAY) * grad
    square_new = SQUARE_DECAY * square + (1.0 - SQUARE_DECAY) * grad * grad
    direction = (
        moment_new
        / (1.0 - MOMENT_DECAY**STEP)
        / (jnp.sqrt(square_new / (1.0 - SQUARE_DECAY**STEP)) + ADAM_EPSILON)
    )
    return (moment_new, square_new, direction)


def total(value):
    return jnp.sum(jnp.sum(value, axis=1, keepdims=True), axis=0, keepdims=True)


def main_kernel(cfg, *refs):
    r = SimpleNamespace(**dict(zip(cfg.names, refs)))
    inner, n_ch, batch, local = cfg.inner, cfg.n_ch, cfg.batch, cfg.local
    classes, count = cfg.classes, cfg.count
    per = batch // n_ch
    chans = local * n_ch
    rows, small = cfg.rows, cfg.small
    tail = (rows - 256) // 2
    hw, hs = rows // 2, small // 2
    slots = SimpleNamespace(remote=0, local=0)

    img = lax.axis_index("img")
    me = lax.axis_index("ch")
    block = lax.div(img, inner)
    within = lax.rem(img, inner)
    core = lax.rem(block, 2)
    plane = lax.div(block, 2)
    partner = flip(block, 1)

    def dev(block_id, within_id, ch_id):
        return (block_id * inner + within_id, ch_id)

    pending = []

    def post(src, dst, landed, peer):
        slot = slots.remote
        slots.remote = slot + 1
        copy = pltpu.make_async_remote_copy(
            src_ref=src,
            dst_ref=dst,
            send_sem=r.send.at[slot],
            recv_sem=r.recv.at[slot],
            device_id=peer,
            device_id_type=MESH,
        )
        copy.start()
        pending.append(copy.wait_send)
        arrival = pltpu.make_async_remote_copy(
            src_ref=landed,
            dst_ref=landed,
            send_sem=r.send.at[slot],
            recv_sem=r.recv.at[slot],
            device_id=peer,
            device_id_type=MESH,
        )
        return arrival.wait_recv

    def here(src, dst):
        slot = slots.local
        slots.local = slot + 1
        copy = pltpu.make_async_copy(src, dst, r.lsem.at[slot])
        copy.start()
        return copy.wait

    outer_peers = [flip(block, mask) for mask in range(1, OUTER)]
    ch_peers = [flip(me, mask) for mask in range(1, n_ch)]
    inner_pairs = [
        (lax.rem(within + step, inner), lax.rem(within + inner - step, inner))
        for step in range(1, inner)
    ]
    up, down, far = (lax.rem(me + step, n_ch) for step in (1, 3, 2))
    up_peer, down_peer = dev(block, within, up), dev(block, within, down)

    class Ring:
        def __init__(self, source, target, passing):
            self.target, self.passing = target, passing
            self.waits = []
            self.early = [
                post(source(far, 0), passing.at[0], passing.at[0], up_peer),
                post(source(far, 1), passing.at[1], passing.at[1], down_peer),
            ]
            for im in range(per):
                self.waits += [
                    post(source(up, im), target(me, im), target(down, im), up_peer),
                    post(source(down, im), target(me, im), target(up, im), down_peer),
                ]

        def forward(self):
            self.early[0]()
            self.waits.append(
                post(self.passing.at[0], self.target(down, 0), self.target(far, 0), up_peer)
            )
            self.early[1]()
            self.waits.append(
                post(self.passing.at[1], self.target(up, 1), self.target(far, 1), down_peer)
            )

        def settle(self):
            for wait in self.waits:
                wait()

    barrier = pltpu.get_barrier_semaphore()
    everyone = [dev(peer, within, me) for peer in outer_peers]
    everyone += [dev(block, within, peer) for peer in ch_peers]
    everyone += [dev(block, peer, me) for peer, _ in inner_pairs]
    for peer in everyone:
        pl.semaphore_signal(barrier, inc=1, device_id=peer, device_id_type=MESH)

    got_entry = here(r.entry, r.entry_v)
    got_features = here(r.features, r.fown)
    got_exit = here(r.exit, r.exit_v)
    got_bypass = here(r.bypass, r.bypass_v)
    got_affine = here(r.affine, r.affine_v)
    got_cot = here(r.cotangent, r.cown)
    states = ((r.entry_m, r.entry_q), (r.exit_m, r.exit_q), (r.bypass_m, r.bypass_q)) if inner == 1 else ()
    held = [
        (here(m, getattr(r, v + "m")), here(q, getattr(r, v + "q")))
        for (m, q), v in zip(states, ("v1", "v2", "vs"))
    ]

    s_row, s_col = iota((hw, 384), 0), iota((hw, 384), 1)
    pick_first = to_bf16(s_col == jnp.where(s_row < 128, s_row, s_row + 128))
    pick_second = to_bf16(s_col == jnp.where(s_row < 128, s_row + 128, s_row + 128 + tail))
    r.padded[...] = jnp.zeros(r.padded.shape, BF16)

    def pack_own(value):
        r.padded[local : 2 * local, 0:rows] = value.astype(BF16)
        packed = nt(pick_first, r.padded[local : 3 * local, :])
        return (packed + nt(pick_second, r.padded[0 : 2 * local, :])).astype(BF16)

    got_entry()
    r.wz1[me] = pack_own(r.entry_v[...])
    pl.semaphore_wait(barrier, len(everyone))

    def to_channels(buffer):
        return [
            post(buffer.at[me], buffer.at[me], buffer.at[peer], dev(block, within, peer))
            for peer in ch_peers
        ]

    entry_waits = to_channels(r.wz1)
    got_features()
    r.fbuf[me] = r.fown[pl.ds(per * me, per)]
    flat = jnp.concatenate([r.fown[b] for b in range(batch)], axis=1)
    wide = flat.astype(F32)
    square = wide * wide
    square_hi = square.astype(BF16)
    square_lo = (square - square_hi.astype(F32)).astype(BF16)
    level = iota((16, 256), 0)
    first_mask = jnp.concatenate([to_bf16(level == r.groups[b]) for b in range(batch)], axis=1)
    second_mask = jnp.concatenate([to_bf16(level == r.groups[b] + 4) for b in range(batch)], axis=1)
    sums = nt(first_mask, flat) + nt(second_mask, square_hi) + nt(second_mask, square_lo)

    got_affine()
    r.aff_z[me] = jnp.zeros((32, 128), F32)
    r.aff_z[me, 0 : 2 * classes + 3, 0:local] = r.affine_v[...]
    r.aff_z[me, 24:32, 0:local] = sums[0:8]
    affine_waits = to_channels(r.aff_z)
    feature_waits = [
        post(
            r.fown.at[pl.ds(per * peer, per)],
            r.fbuf.at[me],
            r.fbuf.at[peer],
            dev(block, within, peer),
        )
        for peer in ch_peers
    ]

    got_exit()
    got_bypass()
    r.wz2[me, 0:hw, :] = pack_own(r.exit_v[...])
    e_row, e_col = iota((local, 128), 0), iota((local, 128), 1)
    value = r.bypass_v[...].astype(BF16)
    r.wz2[me, hw : hw + hs, :] = (
        nn(value[:hs], to_bf16(e_col == e_row)) + nn(value[hs:], to_bf16(e_col == e_row + local))
    ).astype(BF16)

    exit_waits = to_channels(r.wz2)
    got_cot()
    cotangent = Ring(
        lambda c, im: r.cown.at[per * c + im], lambda c, im: r.cbuf.at[c, im], r.pass_c
    )

    lane = iota((512, 512), 0)
    column = iota((512, 512), 1)
    spot = 256 * ((lane >> 6) & 1) + 64 * (lane >> 7) + (lane & 63)
    r.unpack[...] = to_bf16(column == spot)

    def ordered_sum(ref, size):
        result = ref[0]
        for slot in range(1, size):
            result = result + ref[slot]
        return result

    class AllReduce:
        def __init__(self, number):
            self.over_outer, self.over_inner, self.over_ch = (
                getattr(r, axis + str(number), None) for axis in "abc"
            )

        def begin(self, value):
            ref = self.over_outer
            ref[block] = value
            self.waits = [
                post(ref.at[block], ref.at[block], ref.at[peer], dev(peer, within, me))
                for peer in outer_peers
            ]

        def plane(self):
            for wait in self.waits:
                wait()
            value = ordered_sum(self.over_outer, OUTER)
            if inner > 1:
                ref = self.over_inner
                ref[within] = value
                waits = [
                    post(ref.at[within], ref.at[within], ref.at[back], dev(block, peer, me))
                    for peer, back in inner_pairs
                ]
                for wait in waits:
                    wait()
                value = ordered_sum(ref, inner)
            return value

        def middle(self):
            self.over_ch[me] = self.plane()
            self.waits = to_channels(self.over_ch)

        def end(self):
            for wait in self.waits:
                wait()
            return ordered_sum(self.over_ch, n_ch)

    def rows_of(ref, index):
        size = ref.shape[0] // OUTER
        return ref.at[pl.ds(pl.multiple_of(size * index, 16), size)]

    def unpack_own(ref, full):
        own = rows_of(ref, block)
        if full.shape[0] == hw:
            own[0:128, :] = full[0:128, 0:256]
            own[128:256, :] = full[0:128, 256:512]
            own[256 : 256 + tail, :] = full[128:, 0:256]
            own[256 + tail :, :] = full[128:, 256:512]
        else:
            own[0:hs, :] = full[:, 0:256]
            own[hs:, :] = full[:, 256:512]

    def spread(ref):
        own = rows_of(ref, block)
        return {
            mask: post(own, own, rows_of(ref, flip(block, mask)), dev(flip(block, mask), within, me))
            for mask in (2, 4, 6, 1)
        }

    def forward(ref, waits):
        rest = [waits[1]]
        for mask in (2, 4, 6):
            waits[mask]()
            mine = rows_of(ref, flip(block, mask))
            theirs = rows_of(ref, flip(partner, mask))
            rest.append(post(mine, mine, theirs, dev(partner, within, me)))
        return rest

    def widen(buffer):
        packed = jnp.concatenate([buffer[c] for c in range(n_ch)], axis=1)
        return nn(packed, r.unpack[...]).astype(BF16)

    def wide_lanes(ref):
        parts = [
            ref[c] + pltpu.roll(ref[c + 1], local, axis=1) for c in range(0, n_ch, 2)
        ]
        return jnp.concatenate(parts, axis=1)

    for wait in affine_waits:
        wait()
    affine = wide_lanes(r.aff_z)
    input_sums = AllReduce(1)
    input_sums.begin(affine[24:32])
    for wait in entry_waits:
        wait()
    unpack_own(r.w1, widen(r.wz1))
    gather1 = spread(r.w1)

    ident = to_bf16(iota((256, 256), 0) == iota((256, 256), 1))
    r.ident[...] = ident
    q_out, q_in = iota((256, 256), 0), iota((256, 256), 1)
    r.shift[0] = to_bf16((q_in == q_out + 1) & ((q_out & 15) < 15))
    r.shift[1] = to_bf16((q_in == q_out - 1) & ((q_out & 15) > 0))

    for wait in exit_waits:
        wait()
    full = widen(r.wz2)
    unpack_own(r.w2, full[0:hw])
    unpack_own(r.ws, full[hw:])
    gather2 = spread(r.w2)
    gather3 = spread(r.ws)

    rho, px = iota((512, 256), 0), iota((512, 256), 1)
    version, a, b_ = rho >> 8, (rho >> 7) & 1, (rho >> 6) & 1
    col = (rho & 15) + version * (1 - 2 * b_)
    target = (2 * ((rho & 63) >> 4) + a) * 32 + 2 * col + b_
    r.gridder[...] = to_bf16((px == target) & (col >= 0) & (col < 16))
    zeros = jnp.zeros((16, 256), BF16)
    for im in range(per):
        for ver in range(3):
            r.h1s[ver, im, 0:16, :] = zeros
            r.h1s[ver, im, 272:288, :] = zeros
        for ver in range(2):
            for ph in range(4):
                for ref in (r.h2s, r.dzs):
                    ref[ver, ph, im, 0:16, :] = zeros
                    ref[ver, ph, im, 272:288, :] = zeros

    def channel_major(ref, im, lanes):
        return jnp.concatenate([ref[c, im, :, lanes] for c in range(n_ch)], axis=0)

    for wait in feature_waits:
        wait()
    for im in range(per):
        r.fpm[256 * im : 256 * im + 256, :] = nt(
            ident, channel_major(r.fbuf, im, slice(0, 256))
        ).astype(BF16)

    stats = input_sums.plane()
    mean1 = stats[0:4] / count
    inv1 = lax.rsqrt(stats[4:8] / count - mean1 * mean1 + NORM_EPSILON)
    gain = affine[2 * classes : 2 * classes + 1]
    shift = affine[2 * classes + 1 : 2 * classes + 2]
    out_bias = affine[2 * classes + 2 : 2 * classes + 3]
    group, label, mean1_b, inv1_b, gamma_b, beta_b, mask_b = [], [], [], [], [], [], []
    for im in range(per):
        group.append(r.groups[per * me + im])
        label.append(r.labels[per * me + im])
        mean1_b.append(pick_row(mean1, group[im]))
        inv1_b.append(pick_row(inv1, group[im]))
        gamma_b.append(pick_row(affine, label[im]))
        beta_b.append(pick_row(affine, label[im] + classes))
        width = r.widths[group[im]]
        mask_b.append(
            jnp.where(iota((1, chans), 1) < width * (chans // LEVELS), 1.0, 0.0)
        )

    for im in range(per):
        normal = (r.fpm[256 * im : 256 * im + 256, :].astype(F32) - mean1_b[im]) * inv1_b[im]
        pre = gamma_b[im] * normal + beta_b[im]
        hidden = (pre * sigmoid(pre)).astype(BF16)
        r.h1s[1, im, 16:272, :] = hidden
        r.h1s[0, im, 16:272, :] = nn(r.shift[1], hidden).astype(BF16)
        r.h1s[2, im, 16:272, :] = nn(r.shift[0], hidden).astype(BF16)
        r.h1cm[:, 256 * im : 256 * im + 256] = nt(ident, hidden).astype(BF16)
        if im == 0:
            rest = forward(r.w1, gather1)

    cotangent.forward()
    for wait in rest:
        wait()

    def back_product(parts, ref):
        result = nt(parts[0], ref[0:256, :])
        for tap in range(1, 9):
            result = result + nt(parts[tap], ref[256 * tap : 256 * tap + 256, :])
        return result

    def taps():
        return [(dy, dx) for dy in range(3) for dx in range(3)]

    def stack(pieces):
        return jnp.concatenate(pieces, axis=0)

    def conv1(phase, carry):
        a, c = lax.div(phase, 2), lax.rem(phase, 2)
        parts = []
        for dy, dx in taps():
            first = pl.multiple_of(16 * lax.div(a + dy + 1, 2), 16)
            ver = lax.div(c + dx + 1, 2)
            parts.append(
                stack([r.h1s[ver, im, pl.ds(first, 256), :] for im in range(per)])
            )
        y = nn(jnp.concatenate(parts, axis=1), r.w1[...])
        r.y1[phase] = y
        out = []
        for im in range(per):
            piece = y[256 * im : 256 * im + 256]
            out.append(carry[2 * im] + colsum(piece))
            out.append(carry[2 * im + 1] + colsum(piece * piece))
        return tuple(out)

    nought = jnp.zeros((1, chans), F32)
    mid = lax.fori_loop(0, 4, conv1, (nought,) * (2 * per))
    payload = jnp.zeros((8, chans), F32)
    for im in range(per):
        payload = payload + place_row(mid[2 * im], group[im], 8)
        payload = payload + place_row(mid[2 * im + 1], group[im] + 4, 8)
    mid_sums = AllReduce(2)
    mid_sums.begin(payload)

    rest = forward(r.w2, gather2) + forward(r.ws, gather3)
    mid_sums.middle()

    r.cbuf[me] = r.cown[pl.ds(per * me, per)]
    cotangent.settle()
    for im in range(per):
        for n in range(4):
            piece = channel_major(r.cbuf, im, slice(256 * n, 256 * n + 256))
            grid = nt(r.gridder[...], piece).astype(BF16)
            for ver in range(2):
                for ph in range(4):
                    at = 256 * ver + 64 * ph
                    r.dzs[ver, ph, im, 16 + 64 * n : 80 + 64 * n, :] = grid[at : at + 64]

    coarse = jnp.zeros((256 * per, chans), F32)
    for ph in range(4):
        coarse = coarse + stack([r.dzs[0, ph, im, 16:272, :] for im in range(per)]).astype(F32)
    bias_sum = colsum(coarse)
    r.dzc[...] = coarse.astype(BF16)

    def tap_slice(ref, a, c, dy, dx, im):
        row, colm = a + dy + 1, c + dx + 1
        first = pl.multiple_of(16 * lax.div(row, 2), 16)
        ph = 2 * lax.rem(row, 2) + lax.rem(colm, 2)
        side_step = lax.div(colm, 2) - 1
        return ref[side_step * side_step, ph, im, pl.ds(first, 256), :]

    for wait in rest:
        wait()

    def back2(phase, carry):
        a, c = lax.div(phase, 2), lax.rem(phase, 2)
        parts = [
            stack([tap_slice(r.dzs, a, c, 2 - dy, 2 - dx, im) for im in range(per)])
            for dy, dx in taps()
        ]
        r.act[phase] = back_product(parts, r.w2)
        return carry

    lax.fori_loop(0, 4, back2, 0)

    stats = mid_sums.end()
    mean2 = stats[0:4] / (4.0 * count)
    inv2 = lax.rsqrt(stats[4:8] / (4.0 * count) - mean2 * mean2 + NORM_EPSILON)
    mean2_b = [pick_row(mean2, group[im]) for im in range(per)]
    inv2_b = [pick_row(inv2, group[im]) for im in range(per)]

    def hidden2(phase, carry):
        c = lax.rem(phase, 2)
        out = []
        for im in range(per):
            span = slice(256 * im, 256 * im + 256)
            normal = (r.y1[phase, span, :] - mean2_b[im]) * inv2_b[im]
            r.y1[phase, span, :] = normal
            pre = gain * normal + shift
            sig = sigmoid(pre)
            hidden = (pre * sig * mask_b[im]).astype(BF16)
            act = r.act[phase, span, :] * (sig * (1.0 + pre * (1.0 - sig)) * mask_b[im])
            r.act[phase, span, :] = act
            out.append(carry[2 * im] + colsum(act))
            out.append(carry[2 * im + 1] + colsum(act * normal))
            r.h2s[0, phase, im, 16:272, :] = hidden
            r.h2s[1, phase, im, 16:272, :] = nn(r.shift[c], hidden).astype(BF16)
            lanes = pl.ds(pl.multiple_of(512 * phase + 256 * im, 256), 256)
            r.h2cm[:, lanes] = nt(r.ident[...], hidden).astype(BF16)
        return tuple(out)

    mid = lax.fori_loop(0, 4, hidden2, (nought,) * (2 * per))
    payload = place_row(bias_sum, 8, 16)
    for im in range(per):
        payload = payload + place_row(mid[2 * im], group[im], 16)
        payload = payload + place_row(mid[2 * im + 1], group[im] + 4, 16)
    back_sums = AllReduce(3)
    back_sums.begin(payload)

    r.short[...] = nn(r.fpm[...], r.ws[...]) + out_bias
    def conv2(phase, carry):
        a, c = lax.div(phase, 2), lax.rem(phase, 2)
        parts = [
            stack([tap_slice(r.h2s, a, c, dy, dx, im) for im in range(per)]) for dy, dx in taps()
        ]
        y = nn(jnp.concatenate(parts, axis=1), r.w2[...]) + r.short[...]
        r.rc[phase] = y.astype(BF16)
        return carry

    lax.fori_loop(0, 4, conv2, 0)
    for im in range(per):
        for n in range(4):
            first = 256 * im + 64 * n
            piece = stack([r.rc[ph, first : first + 64, :] for ph in range(4)])
            r.ocm[im, :, 256 * n : 256 * n + 256] = tn(piece, r.gridder[0:256, :]).astype(BF16)

    def own_channels(ref, index, im):
        return ref.at[im, pl.ds(pl.multiple_of(local * index, local), local), :]

    def give_back(ref, out, passing):
        for im in range(per):
            out[per * me + im] = own_channels(ref, me, im)[...]
        return Ring(
            lambda c, im: own_channels(ref, c, im), lambda c, im: out.at[per * c + im], passing
        )

    back_sums.middle()
    block_output = give_back(r.ocm, r.out_v, r.pass_o)

    def grad2(tap, carry):
        dy, dx = lax.div(tap, 3), lax.rem(tap, 3)
        pieces = []
        for ph in range(4):
            a, c = ph // 2, ph % 2
            for im in range(per):
                pieces.append(tap_slice(r.dzs, a, c, 2 - dy, 2 - dx, im))
        first = pl.multiple_of(256 * tap, 256)
        r.dw2[pl.ds(first, 256), :] = nn(r.h2cm[...], stack(pieces))
        return carry

    for im in range(per):
        piece = channel_major(r.fbuf, im, slice(0, 256))
        grad = nn(piece, r.dzc[256 * im : 256 * im + 256, :])
        if im == 0:
            r.dws[...] = grad
        else:
            r.dws[...] = r.dws[...] + grad

    class GradSum:
        def __init__(self, number, fetch):
            self.fetch = fetch
            self.waits = []
            for part in PARTS:
                setattr(self, part, getattr(r, part + str(number)))

        def begin(self, parts=range(4)):
            for u in parts:
                self.s1[u] = self.fetch(2 * u + 1 - core).astype(BF16)
                self.waits.append(
                    post(self.s1.at[u], self.r1.at[u], self.r1.at[u], dev(partner, within, me))
                )

        def settle(self):
            for wait in self.waits:
                wait()

        def first(self):
            self.settle()
            self.waits = []
            for mask in (6, 2, 4, 0):
                peer = flip(block, mask)
                u = lax.div(peer, 2)
                value = self.fetch(peer) + self.r1[u].astype(F32)
                if mask == 0:
                    self.r2[plane] = value.astype(BF16)
                    continue
                self.s2[u] = value.astype(BF16)
                self.waits.append(
                    post(self.s2.at[u], self.r2.at[plane], self.r2.at[u], dev(peer, within, me))
                )

        def second(self):
            self.settle()
            value = self.r2[0].astype(F32)
            for u in range(1, 4):
                value = value + self.r2[u].astype(F32)
            value = value.astype(BF16)
            left = [value[0:128], value[256 : 256 + tail]]
            right = [value[128:256], value[256 + tail : rows]]
            if value.shape[0] > rows:
                left.append(value[rows : rows + hs])
                right.append(value[rows + hs :])
            pair = jnp.concatenate([stack(left), stack(right)], axis=1)
            packed = nt(pair, r.unpack[...]).astype(BF16)
            for c in range(n_ch):
                self.s3[c] = packed[:, 128 * c : 128 * c + 128]
            self.r3[me] = self.s3[me]
            self.waits = [
                post(self.s3.at[peer], self.r3.at[me], self.r3.at[peer], dev(block, within, peer))
                for peer in ch_peers
            ]

        def end(self, out, out_small=None):
            self.settle()
            done = self.r3[0].astype(F32)
            for c in range(1, n_ch):
                done = done + self.r3[c].astype(F32)
            turned = done[0:128].T
            out[:, 0:128] = turned[0:local]
            out[:, 128:256] = turned[local:]
            gap = jnp.zeros((128 - tail, 128), F32)
            turned = stack([done[128 : 128 + tail], gap]).T
            ends = turned[0:local] + pltpu.roll(turned[local:], tail, axis=1)
            out[:, 256:rows] = ends[:, 0 : rows - 256]
            if out_small is not None:
                last = done[hw:]
                out_small[0:hs, :] = last[:, 0:local]
                out_small[hs:, :] = pltpu.roll(last, local, axis=1)[:, 0:local]

    def block_rows(ref, size, index):
        return ref[pl.ds(pl.multiple_of(size * index, 8), size), :]

    second = GradSum(2, lambda k: stack([block_rows(r.dw2, rows, k), block_rows(r.dws, small, k)]))
    entry = GradSum(1, lambda k: block_rows(r.dw1, rows, k))
    for u, (first, last) in enumerate(((0, 3), (3, 5), (5, 7), (7, 9))):
        lax.fori_loop(first, last, grad2, 0)
        second.begin([u])
    stats = back_sums.end()
    affine_grad2 = stats
    p1_b = [pick_row(stats[0:4], group[im]) / (4.0 * count) for im in range(per)]
    p2_b = [pick_row(stats[4:8], group[im]) / (4.0 * count) for im in range(per)]

    for im in range(per):
        span = slice(256 * im, 256 * im + 256)
        scale = gain * inv2_b[im]
        combos = []
        for a in range(2):
            grads = []
            for c in range(2):
                ph = 2 * a + c
                d = scale * (r.act[ph, span, :] - (p1_b[im] + r.y1[ph, span, :] * p2_b[im]))
                grads.append(d.astype(BF16))
            right = nn(r.shift[0], grads[0])
            left = nn(r.shift[1], grads[1])
            even, odd = grads[0].astype(F32), grads[1].astype(F32)
            combos.append((odd + right, even + odd, left + even))
        gap = jnp.zeros((16, chans), F32)
        for dx in range(3):
            upper, lower = combos[0][dx], combos[1][dx]
            r.field[dx, im] = (lower + stack([upper[16:], gap])).astype(BF16)
            r.field[3 + dx, im] = (upper + lower).astype(BF16)
            r.field[6 + dx, im] = (stack([gap, lower[:-16]]) + upper).astype(BF16)

    second.first()
    block_output.forward()

    def grad1(tap, carry):
        first = pl.multiple_of(256 * tap, 256)
        r.dw1[pl.ds(first, 256), :] = nn(
            r.h1cm[...], stack([r.field[tap, im] for im in range(per)])
        )
        return carry

    for u, (first, last) in enumerate(((0, 3), (3, 5), (5, 7), (7, 9))):
        lax.fori_loop(first, last, grad1, 0)
        entry.begin([u])

    parts = [stack([r.field[tap, im] for im in range(per)]) for tap in range(9)]
    dh1 = back_product(parts, r.w1)
    payload = jnp.zeros((8, chans), F32)
    class_rows = jnp.zeros((24, chans), F32)
    for im in range(per):
        span = slice(256 * im, 256 * im + 256)
        normal = (r.fpm[span, :].astype(F32) - mean1_b[im]) * inv1_b[im]
        pre = gamma_b[im] * normal + beta_b[im]
        sig = sigmoid(pre)
        act = dh1[span] * (sig * (1.0 + pre * (1.0 - sig)))
        r.act1[span, :] = act
        q1, q2 = colsum(act), colsum(act * normal)
        class_rows = class_rows + place_row(q2, label[im], 24)
        class_rows = class_rows + place_row(q1, label[im] + classes, 24)
        payload = payload + place_row(gamma_b[im] * q1, group[im], 8)
        payload = payload + place_row(gamma_b[im] * q2, group[im] + 4, 8)
    last_sums, class_sums = AllReduce(4), AllReduce(6)
    last_sums.begin(payload)
    entry.first()
    class_sums.begin(class_rows)
    last_sums.middle()
    second.second()
    r.dshort[...] = nt(r.dzc[...], r.ws[...])
    entry.second()
    stats = last_sums.end()
    for im in range(per):
        span = slice(256 * im, 256 * im + 256)
        normal = (r.fpm[span, :].astype(F32) - mean1_b[im]) * inv1_b[im]
        r1 = pick_row(stats[0:4], group[im]) / count
        r2 = pick_row(stats[4:8], group[im]) / count
        grad = inv1_b[im] * (gamma_b[im] * r.act1[span, :] - (r1 + normal * r2))
        grad = (grad + r.dshort[span, :]).astype(BF16)
        r.dcm[im] = nt(r.ident[...], grad).astype(BF16)
    input_gradient = give_back(r.dcm, r.dx_v, r.pass_x)
    class_sums.middle()
    second.end(r.grad2, r.grad3)

    row = iota((8, 128), 0)

    def norm_rows(index, weight, grad, v):
        for wait in held[index]:
            wait()
        master = weight[...]
        _, _, direction = adam_update(
            grad[...], getattr(r, v + "m")[...], getattr(r, v + "q")[...]
        )
        update = direction + WEIGHT_DECAY * master
        rows_w = jnp.where(row == index, total(master * master), 0.0)
        return rows_w + jnp.where(row == index + 3, total(update * update), 0.0)

    if inner == 1:
        norms = norm_rows(1, r.exit_v, r.grad2, "v2") + norm_rows(2, r.bypass_v, r.grad3, "vs")

    if inner == 1:
        entry.end(r.grad1)
        norms = norms + norm_rows(0, r.entry_v, r.grad1, "v1")
        norm_sums = AllReduce(5)
        norm_sums.begin(norms)
        input_gradient.forward()
        norm_sums.middle()
    else:
        entry.end(r.grad1)
        input_gradient.forward()
        r.norms[...] = jnp.zeros((8, 128), F32)

    table = jnp.zeros((24, chans), F32)
    table = table + jnp.where(iota((24, chans), 0) < 2 * classes, class_sums.end(), 0.0)
    table = table + place_row(colsum(affine_grad2[4:8]), 2 * classes, 24)
    table = table + place_row(colsum(affine_grad2[0:4]), 2 * classes + 1, 24)
    table = table + place_row(affine_grad2[8:9], 2 * classes + 2, 24)
    mine = jnp.zeros((24, 128), F32)
    for c in range(n_ch):
        piece = table[:, 128 * (c // 2) : 128 * (c // 2) + 128]
        if c % 2:
            piece = pltpu.roll(piece, local, axis=1)
        mine = mine + jnp.where(me == c, piece, 0.0)
    r.affine_grad[...] = mine

    block_output.settle()
    written = [here(r.out_v, r.out)]
    input_gradient.settle()
    written.append(here(r.dx_v, r.dx))
    if inner == 1:
        r.norms[...] = norm_sums.end()
    for wait in written:
        wait()
    for wait in pending:
        wait()
    cfg.used.append((slots.remote, slots.local))


def final_kernel(cfg, *refs):
    r = SimpleNamespace(**dict(zip(cfg.names, refs)))
    classes = cfg.classes
    local = cfg.local
    r.block_output[...] = r.out[...]
    r.input_gradient[...] = r.dx[...].astype(F32)
    norms = jnp.sqrt(r.norms[...])
    weight_norm, update_norm = norms[0:3, 0:1], norms[3:6, 0:1]
    ratio = weight_norm / update_norm
    at = iota((3, 3), 1)
    r.trust_norms[...] = jnp.where(
        at == 0, weight_norm, jnp.where(at == 1, update_norm, ratio)
    )
    sets = (
        (r.entry, r.entry_m, r.entry_q, r.entry_g, r.entry_1, r.entry_2, r.entry_w),
        (r.exit, r.exit_m, r.exit_q, r.exit_g, r.exit_1, r.exit_2, r.exit_w),
        (r.bypass, r.bypass_m, r.bypass_q, r.bypass_g, r.bypass_1, r.bypass_2, r.bypass_w),
    )
    for index, (weight, m, q, g, first, second, result) in enumerate(sets):
        master = weight[...]
        moment, square, direction = adam_update(g[...], m[...], q[...])
        update = direction + WEIGHT_DECAY * master
        first[...] = moment
        second[...] = square
        result[...] = master - MATRIX_RATE * ratio[index : index + 1] * update
    grad = r.affine_grad[0 : 2 * classes + 3, 0:local]
    moment, square, direction = adam_update(grad, r.affine_m[...], r.affine_q[...])
    r.affine_1[...] = moment
    r.affine_2[...] = square
    r.affine_w[...] = r.affine[...] - AFFINE_RATE * direction


def per_device(
    features,
    labels,
    groups,
    widths,
    entry_conv,
    entry_moment,
    entry_square,
    exit_conv,
    exit_moment,
    exit_square,
    bypass_conv,
    bypass_moment,
    bypass_square,
    norm_affine,
    norm_moment,
    norm_square,
    cotangent,
):
    n_img, n_ch = lax.axis_size("img"), lax.axis_size("ch")
    batch, local, pixels = features.shape
    chans = local * n_ch
    side = math.isqrt(pixels)
    inner = n_img // OUTER
    classes = (norm_affine.shape[0] - 3) // 2
    per = batch // n_ch
    assert (side, chans, n_ch, local, batch % n_ch) == (16, 256, 4, 64, 0) and per == 2
    rows, small = entry_conv.shape[0] * inner, bypass_conv.shape[0] * inner
    masters = (entry_conv, exit_conv, bypass_conv)
    if inner == 1:
        blocks = masters
    else:
        sets = [[o * inner + i for i in range(inner)] for o in range(OUTER)]
        blocks = tuple(
            lax.all_gather(w.astype(BF16), "img", axis=0, tiled=True, axis_index_groups=sets)
            for w in masters
        )

    vmem = pl.BlockSpec(memory_space=pltpu.VMEM)
    smem = pl.BlockSpec(memory_space=pltpu.SMEM)
    anywhere = pl.BlockSpec(memory_space=pl.ANY)
    states = dict(
        entry_m=entry_moment.T,
        entry_q=entry_square.T,
        exit_m=exit_moment.T,
        exit_q=exit_square.T,
        bypass_m=bypass_moment,
        bypass_q=bypass_square,
    )
    inputs = dict(
        labels=(labels, smem),
        groups=(groups, smem),
        widths=(widths, smem),
        features=(features, anywhere),
        cotangent=(cotangent, anywhere),
        entry=(blocks[0].T, anywhere),
        exit=(blocks[1].T, anywhere),
        bypass=(blocks[2], anywhere),
        affine=(norm_affine, anywhere),
    )
    if inner == 1:
        inputs.update({name: (value, anywhere) for name, value in states.items()})
    sds = jax.ShapeDtypeStruct
    outputs = dict(
        out=(sds(cotangent.shape, BF16), anywhere),
        dx=(sds(features.shape, BF16), anywhere),
        grad1=(sds((local, rows), F32), vmem),
        grad2=(sds((local, rows), F32), vmem),
        grad3=(sds((small, local), F32), vmem),
        affine_grad=(sds((24, 128), F32), vmem),
        norms=(sds((8, 128), F32), vmem),
    )
    pix = pixels * per
    taps9 = 9 * chans
    held = lambda shape, dtype=BF16: pltpu.VMEM(shape, dtype)
    scratch = dict(
        fown=held((batch, local, pixels)),
        cown=held((batch, local, 4 * pixels)),
        pass_c=held((2, local, 4 * pixels)),
        pass_o=held((2, local, 4 * pixels)),
        pass_x=held((2, local, pixels)),
        out_v=held(cotangent.shape),
        dx_v=held(features.shape),
        fbuf=held((n_ch, per, local, pixels)),
        cbuf=held((n_ch, per, local, 4 * pixels)),
        entry_v=held((local, rows), blocks[0].dtype),
        exit_v=held((local, rows), blocks[1].dtype),
        bypass_v=held((small, local), blocks[2].dtype),
        affine_v=held(norm_affine.shape, F32),
        padded=held((3 * local, 384)),
        wz1=held((n_ch, rows // 2, 128)),
        wz2=held((n_ch, (rows + small) // 2, 128)),
        aff_z=held((n_ch, 32, 128), F32),
        w1=held((taps9, chans)),
        w2=held((taps9, chans)),
        ws=held((chans, chans)),
        unpack=held((512, 512)),
        ident=held((256, 256)),
        shift=held((2, 256, 256)),
        gridder=held((512, 256)),
        fpm=held((pix, chans)),
        h1s=held((3, per, pixels + 32, chans)),
        h1cm=held((chans, pix)),
        y1=held((4, pix, chans), F32),
        act=held((4, pix, chans), F32),
        h2s=held((2, 4, per, pixels + 32, chans)),
        dzs=held((2, 4, per, pixels + 32, chans)),
        h2cm=held((chans, 4 * pix)),
        short=held((pix, chans), F32),
        dshort=held((pix, chans), F32),
        dzc=held((pix, chans)),
        act1=held((pix, chans), F32),
        rc=held((4, pix, chans)),
        ocm=held((per, chans, 4 * pixels)),
        dcm=held((per, chans, pixels)),
        field=held((9, per, pixels, chans)),
        dw1=held((taps9, chans), F32),
        dw2=held((taps9, chans), F32),
        dws=held((chans, chans), F32),
    )
    for number, size in ((1, rows), (2, rows + small)):
        shapes = ((4, size, chans),) * 4 + ((n_ch, size // 2, 128),) * 2
        for part, shape in zip(PARTS, shapes):
            scratch[part + str(number)] = held(shape)
    exchanges = [(8, chans), (8, chans), (16, chans), (8, chans), (8, 128), (24, chans)]
    if inner == 1:
        for v, shape in (("v1", (local, rows)), ("v2", (local, rows)), ("vs", (small, local))):
            scratch[v + "m"] = held(shape, F32)
            scratch[v + "q"] = held(shape, F32)
    for number, shape in enumerate(exchanges, 1):
        for axis, size in zip("abc", (OUTER, inner, n_ch)):
            if size > 1:
                scratch[axis + str(number)] = held((size,) + shape, F32)
    remote_count = 3 * 3 + 4 * 4 * per + 3 * 7 + 2 * 13 + len(exchanges) * (7 + 3 + inner - 1)
    scratch.update(
        send=pltpu.SemaphoreType.DMA((remote_count,)),
        recv=pltpu.SemaphoreType.DMA((remote_count,)),
        lsem=pltpu.SemaphoreType.DMA((20,)),
    )
    cfg = SimpleNamespace(
        names=[*inputs, *outputs, *scratch],
        inner=inner,
        n_ch=n_ch,
        batch=batch,
        local=local,
        classes=classes,
        count=float(batch * n_img // widths.shape[0] * pixels),
        rows=rows,
        small=small,
        used=[],
    )
    out, dx, grad1, grad2, grad3, affine_grad, norms = pl.pallas_call(
        functools.partial(main_kernel, cfg),
        out_shape=[s for s, _ in outputs.values()],
        in_specs=[s for _, s in inputs.values()],
        out_specs=[s for _, s in outputs.values()],
        scratch_shapes=list(scratch.values()),
        compiler_params=pltpu.CompilerParams(
            collective_id=0, has_side_effects=True, vmem_limit_bytes=VMEM_LIMIT
        ),
        name="block_step",
    )(*[v for v, _ in inputs.values()])
    assert max(n for n, _ in cfg.used) <= remote_count and max(n for _, n in cfg.used) <= 20

    grads = [grad1, grad2, grad3]
    if inner > 1:
        grads = [
            lax.psum_scatter(g, "img", scatter_dimension=0, axis_index_groups=sets, tiled=True)
            for g in (grad1.T, grad2.T, grad3)
        ]
        updates = []
        for w, g, m, s in zip(
            masters,
            grads,
            (entry_moment, exit_moment, bypass_moment),
            (entry_square, exit_square, bypass_square),
        ):
            updates.append(adam_update(g, m, s)[2] + WEIGHT_DECAY * w)
        sums = lax.psum(
            jnp.stack([jnp.sum(w * w) for w in masters] + [jnp.sum(u * u) for u in updates]),
            ("img", "ch"),
        )
        norms = jnp.broadcast_to(jnp.pad(sums, (0, 2))[:, None], (8, 128))
        grads = [grads[0].T, grads[1].T, grads[2]]

    args = dict(
        out=out,
        dx=dx,
        norms=norms,
        affine_grad=affine_grad,
        entry_g=grads[0],
        exit_g=grads[1],
        bypass_g=grads[2],
        entry=entry_conv.T,
        exit=exit_conv.T,
        bypass=bypass_conv,
        **states,
        affine=norm_affine,
        affine_m=norm_moment,
        affine_q=norm_square,
    )
    tall = sds(entry_conv.shape[::-1], F32)
    short, wide = (sds(w.shape, F32) for w in (bypass_conv, norm_affine))
    results = dict(
        block_output=sds(cotangent.shape, BF16),
        input_gradient=sds(features.shape, F32),
        entry_1=tall,
        entry_2=tall,
        entry_w=tall,
        exit_1=tall,
        exit_2=tall,
        exit_w=tall,
        bypass_1=short,
        bypass_2=short,
        bypass_w=short,
        affine_1=wide,
        affine_2=wide,
        affine_w=wide,
        trust_norms=sds((3, 3), F32),
    )
    end_cfg = SimpleNamespace(names=[*args, *results], classes=classes, local=local)
    final = pl.pallas_call(
        functools.partial(final_kernel, end_cfg),
        out_shape=list(results.values()),
        in_specs=[vmem] * len(args),
        out_specs=[vmem] * len(results),
        compiler_params=pltpu.CompilerParams(vmem_limit_bytes=VMEM_LIMIT),
        name="finish",
    )(*args.values())
    return tuple(v.T if s is tall else v for v, s in zip(final, results.values()))


def solution(mesh):
    wide = P("img", "ch")
    deep = P("img", "ch", None)
    table = P(None, "ch")
    return jax.shard_map(
        per_device,
        mesh=mesh,
        in_specs=(deep, P("img"), P("img"), P()) + (wide,) * 9 + (table,) * 3 + (deep,),
        out_specs=(deep, deep) + (wide,) * 9 + (table,) * 3 + (P(),),
        check_vma=False,
    )
```

```python
import functools
import math
from types import SimpleNamespace

import jax
import jax.numpy as jnp
from jax import lax
from jax.experimental import pallas as pl
from jax.experimental.pallas import tpu as pltpu
from jax.sharding import PartitionSpec as P

LEVELS = 4
STEP = 5
NORM_EPSILON = 1e-05
ADAM_EPSILON = 1e-06
MOMENT_DECAY = 0.9
SQUARE_DECAY = 0.999
WEIGHT_DECAY = 0.01
MATRIX_RATE = 0.3
AFFINE_RATE = 0.2

OUTER = 8
VMEM_LIMIT = 56 * 1024 * 1024
BF16 = jnp.bfloat16
F32 = jnp.float32
MESH = pl.DeviceIdType.MESH
PARTS = ("s1", "r1", "s2", "r2", "s3", "r3")


def nn(left, right):
    return lax.dot_general(left, right, (((1,), (0,)), ((), ())), preferred_element_type=F32)


def nt(left, right):
    return lax.dot_general(left, right, (((1,), (1,)), ((), ())), preferred_element_type=F32)


def tn(left, right):
    return lax.dot_general(left, right, (((0,), (0,)), ((), ())), preferred_element_type=F32)


def flip(index, mask):
    result = index
    for bit in range(3):
        if (mask >> bit) & 1:
            digit = lax.rem(lax.div(index, 1 << bit), 2)
            result = result + (1 - 2 * digit) * (1 << bit)
    return result


def sigmoid(value):
    return 0.5 * jnp.tanh(0.5 * value) + 0.5


def iota(shape, axis):
    return lax.broadcasted_iota(jnp.int32, shape, axis)


def to_bf16(condition):
    return jnp.where(condition, 1.0, 0.0).astype(BF16)


def pick_row(table, index):
    hit = iota(table.shape, 0) == index
    return jnp.sum(jnp.where(hit, table, 0.0), axis=0, keepdims=True)


def place_row(row, index, rows):
    hit = iota((rows, row.shape[1]), 0) == index
    return jnp.where(hit, row, 0.0)


def colsum(value):
    return jnp.sum(value, axis=0, keepdims=True)


def adam_update(grad, moment, square):
    moment_new = MOMENT_DECAY * moment + (1.0 - MOMENT_DECAY) * grad
    square_new = SQUARE_DECAY * square + (1.0 - SQUARE_DECAY) * grad * grad
    direction = (
        moment_new
        / (1.0 - MOMENT_DECAY**STEP)
        / (jnp.sqrt(square_new / (1.0 - SQUARE_DECAY**STEP)) + ADAM_EPSILON)
    )
    return (moment_new, square_new, direction)


def total(value):
    return jnp.sum(jnp.sum(value, axis=1, keepdims=True), axis=0, keepdims=True)


def main_kernel(cfg, *refs):
    r = SimpleNamespace(**dict(zip(cfg.names, refs)))
    inner, n_ch, batch, local = cfg.inner, cfg.n_ch, cfg.batch, cfg.local
    classes, count = cfg.classes, cfg.count
    per = batch // n_ch
    chans = local * n_ch
    rows, small = cfg.rows, cfg.small
    tail = (rows - 256) // 2
    hw, hs = rows // 2, small // 2
    slots = SimpleNamespace(remote=0, local=0)

    img = lax.axis_index("img")
    me = lax.axis_index("ch")
    block = lax.div(img, inner)
    within = lax.rem(img, inner)
    core = lax.rem(block, 2)
    plane = lax.div(block, 2)
    partner = flip(block, 1)

    def dev(block_id, within_id, ch_id):
        return (block_id * inner + within_id, ch_id)

    pending = []

    def post(src, dst, landed, peer):
        slot = slots.remote
        slots.remote = slot + 1
        copy = pltpu.make_async_remote_copy(
            src_ref=src,
            dst_ref=dst,
            send_sem=r.send.at[slot],
            recv_sem=r.recv.at[slot],
            device_id=peer,
            device_id_type=MESH,
        )
        copy.start()
        pending.append(copy.wait_send)
        arrival = pltpu.make_async_remote_copy(
            src_ref=landed,
            dst_ref=landed,
            send_sem=r.send.at[slot],
            recv_sem=r.recv.at[slot],
            device_id=peer,
            device_id_type=MESH,
        )
        return arrival.wait_recv

    def here(src, dst):
        slot = slots.local
        slots.local = slot + 1
        copy = pltpu.make_async_copy(src, dst, r.lsem.at[slot])
        copy.start()
        return copy.wait

    outer_peers = [flip(block, mask) for mask in range(1, OUTER)]
    ch_peers = [flip(me, mask) for mask in range(1, n_ch)]
    inner_pairs = [
        (lax.rem(within + step, inner), lax.rem(within + inner - step, inner))
        for step in range(1, inner)
    ]
    up, down, far = (lax.rem(me + step, n_ch) for step in (1, 3, 2))
    up_peer, down_peer = dev(block, within, up), dev(block, within, down)

    class Ring:
        def __init__(self, source, target, passing):
            self.target, self.passing = target, passing
            self.waits = []
            self.early = [
                post(source(far, 0), passing.at[0], passing.at[0], up_peer),
                post(source(far, 1), passing.at[1], passing.at[1], down_peer),
            ]
            for im in range(per):
                self.waits += [
                    post(source(up, im), target(me, im), target(down, im), up_peer),
                    post(source(down, im), target(me, im), target(up, im), down_peer),
                ]

        def forward(self):
            self.early[0]()
            self.waits.append(
                post(self.passing.at[0], self.target(down, 0), self.target(far, 0), up_peer)
            )
            self.early[1]()
            self.waits.append(
                post(self.passing.at[1], self.target(up, 1), self.target(far, 1), down_peer)
            )

        def settle(self):
            for wait in self.waits:
                wait()

    barrier = pltpu.get_barrier_semaphore()
    everyone = [dev(peer, within, me) for peer in outer_peers]
    everyone += [dev(block, within, peer) for peer in ch_peers]
    everyone += [dev(block, peer, me) for peer, _ in inner_pairs]
    for peer in everyone:
        pl.semaphore_signal(barrier, inc=1, device_id=peer, device_id_type=MESH)

    got_entry = here(r.entry, r.entry_v)
    got_features = here(r.features, r.fown)
    got_exit = here(r.exit, r.exit_v)
    got_bypass = here(r.bypass, r.bypass_v)
    got_affine = here(r.affine, r.affine_v)
    got_cot = here(r.cotangent, r.cown)
    states = ((r.entry_m, r.entry_q), (r.exit_m, r.exit_q), (r.bypass_m, r.bypass_q)) if inner == 1 else ()
    held = [
        (here(m, getattr(r, v + "m")), here(q, getattr(r, v + "q")))
        for (m, q), v in zip(states, ("v1", "v2", "vs"))
    ]

    s_row, s_col = iota((hw, 384), 0), iota((hw, 384), 1)
    pick_first = to_bf16(s_col == jnp.where(s_row < 128, s_row, s_row + 128))
    pick_second = to_bf16(s_col == jnp.where(s_row < 128, s_row + 128, s_row + 128 + tail))
    r.padded[...] = jnp.zeros(r.padded.shape, BF16)

    def pack_own(value):
        r.padded[local : 2 * local, 0:rows] = value.astype(BF16)
        packed = nt(pick_first, r.padded[local : 3 * local, :])
        return (packed + nt(pick_second, r.padded[0 : 2 * local, :])).astype(BF16)

    got_entry()
    r.wz1[me] = pack_own(r.entry_v[...])
    pl.semaphore_wait(barrier, len(everyone))

    def to_channels(buffer):
        return [
            post(buffer.at[me], buffer.at[me], buffer.at[peer], dev(block, within, peer))
            for peer in ch_peers
        ]

    entry_waits = to_channels(r.wz1)
    got_features()
    r.fbuf[me] = r.fown[pl.ds(per * me, per)]
    flat = jnp.concatenate([r.fown[b] for b in range(batch)], axis=1)
    wide = flat.astype(F32)
    square = wide * wide
    square_hi = square.astype(BF16)
    square_lo = (square - square_hi.astype(F32)).astype(BF16)
    level = iota((16, 256), 0)
    first_mask = jnp.concatenate([to_bf16(level == r.groups[b]) for b in range(batch)], axis=1)
    second_mask = jnp.concatenate([to_bf16(level == r.groups[b] + 4) for b in range(batch)], axis=1)
    sums = nt(first_mask, flat) + nt(second_mask, square_hi) + nt(second_mask, square_lo)

    got_affine()
    r.aff_z[me] = jnp.zeros((32, 128), F32)
    r.aff_z[me, 0 : 2 * classes + 3, 0:local] = r.affine_v[...]
    r.aff_z[me, 24:32, 0:local] = sums[0:8]
    affine_waits = to_channels(r.aff_z)
    feature_waits = [
        post(
            r.fown.at[pl.ds(per * peer, per)],
            r.fbuf.at[me],
            r.fbuf.at[peer],
            dev(block, within, peer),
        )
        for peer in ch_peers
    ]

    got_exit()
    got_bypass()
    r.wz2[me, 0:hw, :] = pack_own(r.exit_v[...])
    e_row, e_col = iota((local, 128), 0), iota((local, 128), 1)
    value = r.bypass_v[...].astype(BF16)
    r.wz2[me, hw : hw + hs, :] = (
        nn(value[:hs], to_bf16(e_col == e_row)) + nn(value[hs:], to_bf16(e_col == e_row + local))
    ).astype(BF16)

    exit_waits = to_channels(r.wz2)
    got_cot()
    cotangent = Ring(
        lambda c, im: r.cown.at[per * c + im], lambda c, im: r.cbuf.at[c, im], r.pass_c
    )

    lane = iota((512, 512), 0)
    column = iota((512, 512), 1)
    spot = 256 * ((lane >> 6) & 1) + 64 * (lane >> 7) + (lane & 63)
    r.unpack[...] = to_bf16(column == spot)

    def ordered_sum(ref, size):
        result = ref[0]
        for slot in range(1, size):
            result = result + ref[slot]
        return result

    class AllReduce:
        def __init__(self, number):
            self.over_outer, self.over_inner, self.over_ch = (
                getattr(r, axis + str(number), None) for axis in "abc"
            )

        def begin(self, value):
            ref = self.over_outer
            ref[block] = value
            self.waits = [
                post(ref.at[block], ref.at[block], ref.at[peer], dev(peer, within, me))
                for peer in outer_peers
            ]

        def plane(self):
            for wait in self.waits:
                wait()
            value = ordered_sum(self.over_outer, OUTER)
            if inner > 1:
                ref = self.over_inner
                ref[within] = value
                waits = [
                    post(ref.at[within], ref.at[within], ref.at[back], dev(block, peer, me))
                    for peer, back in inner_pairs
                ]
                for wait in waits:
                    wait()
                value = ordered_sum(ref, inner)
            return value

        def middle(self):
            self.over_ch[me] = self.plane()
            self.waits = to_channels(self.over_ch)

        def end(self):
            for wait in self.waits:
                wait()
            return ordered_sum(self.over_ch, n_ch)

    def rows_of(ref, index):
        size = ref.shape[0] // OUTER
        return ref.at[pl.ds(pl.multiple_of(size * index, 16), size)]

    def unpack_own(ref, full):
        own = rows_of(ref, block)
        if full.shape[0] == hw:
            own[0:128, :] = full[0:128, 0:256]
            own[128:256, :] = full[0:128, 256:512]
            own[256 : 256 + tail, :] = full[128:, 0:256]
            own[256 + tail :, :] = full[128:, 256:512]
        else:
            own[0:hs, :] = full[:, 0:256]
            own[hs:, :] = full[:, 256:512]

    def spread(ref):
        own = rows_of(ref, block)
        return {
            mask: post(own, own, rows_of(ref, flip(block, mask)), dev(flip(block, mask), within, me))
            for mask in (2, 4, 6, 1)
        }

    def forward(ref, waits):
        rest = [waits[1]]
        for mask in (2, 4, 6):
            waits[mask]()
            mine = rows_of(ref, flip(block, mask))
            theirs = rows_of(ref, flip(partner, mask))
            rest.append(post(mine, mine, theirs, dev(partner, within, me)))
        return rest

    def widen(buffer):
        packed = jnp.concatenate([buffer[c] for c in range(n_ch)], axis=1)
        return nn(packed, r.unpack[...]).astype(BF16)

    def wide_lanes(ref):
        parts = [
            ref[c] + pltpu.roll(ref[c + 1], local, axis=1) for c in range(0, n_ch, 2)
        ]
        return jnp.concatenate(parts, axis=1)

    for wait in affine_waits:
        wait()
    affine = wide_lanes(r.aff_z)
    input_sums = AllReduce(1)
    input_sums.begin(affine[24:32])
    for wait in entry_waits:
        wait()
    unpack_own(r.w1, widen(r.wz1))
    gather1 = spread(r.w1)

    ident = to_bf16(iota((256, 256), 0) == iota((256, 256), 1))
    r.ident[...] = ident
    q_out, q_in = iota((256, 256), 0), iota((256, 256), 1)
    r.shift[0] = to_bf16((q_in == q_out + 1) & ((q_out & 15) < 15))
    r.shift[1] = to_bf16((q_in == q_out - 1) & ((q_out & 15) > 0))

    for wait in exit_waits:
        wait()
    full = widen(r.wz2)
    unpack_own(r.w2, full[0:hw])
    unpack_own(r.ws, full[hw:])
    gather2 = spread(r.w2)
    gather3 = spread(r.ws)

    rho, px = iota((512, 256), 0), iota((512, 256), 1)
    version, a, b_ = rho >> 8, (rho >> 7) & 1, (rho >> 6) & 1
    col = (rho & 15) + version * (1 - 2 * b_)
    target = (2 * ((rho & 63) >> 4) + a) * 32 + 2 * col + b_
    r.gridder[...] = to_bf16((px == target) & (col >= 0) & (col < 16))
    zeros = jnp.zeros((16, 256), BF16)
    for im in range(per):
        for ver in range(3):
            r.h1s[ver, im, 0:16, :] = zeros
            r.h1s[ver, im, 272:288, :] = zeros
        for ver in range(2):
            for ph in range(4):
                for ref in (r.h2s, r.dzs):
                    ref[ver, ph, im, 0:16, :] = zeros
                    ref[ver, ph, im, 272:288, :] = zeros

    def channel_major(ref, im, lanes):
        return jnp.concatenate([ref[c, im, :, lanes] for c in range(n_ch)], axis=0)

    for wait in feature_waits:
        wait()
    for im in range(per):
        r.fpm[256 * im : 256 * im + 256, :] = nt(
            ident, channel_major(r.fbuf, im, slice(0, 256))
        ).astype(BF16)

    stats = input_sums.plane()
    mean1 = stats[0:4] / count
    inv1 = lax.rsqrt(stats[4:8] / count - mean1 * mean1 + NORM_EPSILON)
    gain = affine[2 * classes : 2 * classes + 1]
    shift = affine[2 * classes + 1 : 2 * classes + 2]
    out_bias = affine[2 * classes + 2 : 2 * classes + 3]
    group, label, mean1_b, inv1_b, gamma_b, beta_b, mask_b = [], [], [], [], [], [], []
    for im in range(per):
        group.append(r.groups[per * me + im])
        label.append(r.labels[per * me + im])
        mean1_b.append(pick_row(mean1, group[im]))
        inv1_b.append(pick_row(inv1, group[im]))
        gamma_b.append(pick_row(affine, label[im]))
        beta_b.append(pick_row(affine, label[im] + classes))
        width = r.widths[group[im]]
        mask_b.append(
            jnp.where(iota((1, chans), 1) < width * (chans // LEVELS), 1.0, 0.0)
        )

    for im in range(per):
        normal = (r.fpm[256 * im : 256 * im + 256, :].astype(F32) - mean1_b[im]) * inv1_b[im]
        pre = gamma_b[im] * normal + beta_b[im]
        hidden = (pre * sigmoid(pre)).astype(BF16)
        r.h1s[1, im, 16:272, :] = hidden
        r.h1s[0, im, 16:272, :] = nn(r.shift[1], hidden).astype(BF16)
        r.h1s[2, im, 16:272, :] = nn(r.shift[0], hidden).astype(BF16)
        r.h1cm[:, 256 * im : 256 * im + 256] = nt(ident, hidden).astype(BF16)
        if im == 0:
            rest = forward(r.w1, gather1)

    cotangent.forward()
    for wait in rest:
        wait()

    def back_product(parts, ref):
        result = nt(parts[0], ref[0:256, :])
        for tap in range(1, 9):
            result = result + nt(parts[tap], ref[256 * tap : 256 * tap + 256, :])
        return result

    def taps():
        return [(dy, dx) for dy in range(3) for dx in range(3)]

    def stack(pieces):
        return jnp.concatenate(pieces, axis=0)

    def conv1(phase, carry):
        a, c = lax.div(phase, 2), lax.rem(phase, 2)
        parts = []
        for dy, dx in taps():
            first = pl.multiple_of(16 * lax.div(a + dy + 1, 2), 16)
            ver = lax.div(c + dx + 1, 2)
            parts.append(
                stack([r.h1s[ver, im, pl.ds(first, 256), :] for im in range(per)])
            )
        y = nn(jnp.concatenate(parts, axis=1), r.w1[...])
        r.y1[phase] = y
        out = []
        for im in range(per):
            piece = y[256 * im : 256 * im + 256]
            out.append(carry[2 * im] + colsum(piece))
            out.append(carry[2 * im + 1] + colsum(piece * piece))
        return tuple(out)

    nought = jnp.zeros((1, chans), F32)
    mid = lax.fori_loop(0, 4, conv1, (nought,) * (2 * per))
    payload = jnp.zeros((8, chans), F32)
    for im in range(per):
        payload = payload + place_row(mid[2 * im], group[im], 8)
        payload = payload + place_row(mid[2 * im + 1], group[im] + 4, 8)
    mid_sums = AllReduce(2)
    mid_sums.begin(payload)

    rest = forward(r.w2, gather2) + forward(r.ws, gather3)
    mid_sums.middle()

    r.cbuf[me] = r.cown[pl.ds(per * me, per)]
    cotangent.settle()
    for im in range(per):
        for n in range(4):
            piece = channel_major(r.cbuf, im, slice(256 * n, 256 * n + 256))
            grid = nt(r.gridder[...], piece).astype(BF16)
            for ver in range(2):
                for ph in range(4):
                    at = 256 * ver + 64 * ph
                    r.dzs[ver, ph, im, 16 + 64 * n : 80 + 64 * n, :] = grid[at : at + 64]

    coarse = jnp.zeros((256 * per, chans), F32)
    for ph in range(4):
        coarse = coarse + stack([r.dzs[0, ph, im, 16:272, :] for im in range(per)]).astype(F32)
    bias_sum = colsum(coarse)
    r.dzc[...] = coarse.astype(BF16)

    def tap_slice(ref, a, c, dy, dx, im):
        row, colm = a + dy + 1, c + dx + 1
        first = pl.multiple_of(16 * lax.div(row, 2), 16)
        ph = 2 * lax.rem(row, 2) + lax.rem(colm, 2)
        side_step = lax.div(colm, 2) - 1
        return ref[side_step * side_step, ph, im, pl.ds(first, 256), :]

    for wait in rest:
        wait()

    def back2(phase, carry):
        a, c = lax.div(phase, 2), lax.rem(phase, 2)
        parts = [
            stack([tap_slice(r.dzs, a, c, 2 - dy, 2 - dx, im) for im in range(per)])
            for dy, dx in taps()
        ]
        r.act[phase] = back_product(parts, r.w2)
        return carry

    lax.fori_loop(0, 4, back2, 0)

    stats = mid_sums.end()
    mean2 = stats[0:4] / (4.0 * count)
    inv2 = lax.rsqrt(stats[4:8] / (4.0 * count) - mean2 * mean2 + NORM_EPSILON)
    mean2_b = [pick_row(mean2, group[im]) for im in range(per)]
    inv2_b = [pick_row(inv2, group[im]) for im in range(per)]

    def hidden2(phase, carry):
        c = lax.rem(phase, 2)
        out = []
        for im in range(per):
            span = slice(256 * im, 256 * im + 256)
            normal = (r.y1[phase, span, :] - mean2_b[im]) * inv2_b[im]
            r.y1[phase, span, :] = normal
            pre = gain * normal + shift
            sig = sigmoid(pre)
            hidden = (pre * sig * mask_b[im]).astype(BF16)
            act = r.act[phase, span, :] * (sig * (1.0 + pre * (1.0 - sig)) * mask_b[im])
            r.act[phase, span, :] = act
            out.append(carry[2 * im] + colsum(act))
            out.append(carry[2 * im + 1] + colsum(act * normal))
            r.h2s[0, phase, im, 16:272, :] = hidden
            r.h2s[1, phase, im, 16:272, :] = nn(r.shift[c], hidden).astype(BF16)
            lanes = pl.ds(pl.multiple_of(512 * phase + 256 * im, 256), 256)
            r.h2cm[:, lanes] = nt(r.ident[...], hidden).astype(BF16)
        return tuple(out)

    mid = lax.fori_loop(0, 4, hidden2, (nought,) * (2 * per))
    payload = place_row(bias_sum, 8, 16)
    for im in range(per):
        payload = payload + place_row(mid[2 * im], group[im], 16)
        payload = payload + place_row(mid[2 * im + 1], group[im] + 4, 16)
    back_sums = AllReduce(3)
    back_sums.begin(payload)

    r.short[...] = nn(r.fpm[...], r.ws[...]) + out_bias
    def conv2(phase, carry):
        a, c = lax.div(phase, 2), lax.rem(phase, 2)
        parts = [
            stack([tap_slice(r.h2s, a, c, dy, dx, im) for im in range(per)]) for dy, dx in taps()
        ]
        y = nn(jnp.concatenate(parts, axis=1), r.w2[...]) + r.short[...]
        r.rc[phase] = y.astype(BF16)
        return carry

    lax.fori_loop(0, 4, conv2, 0)
    for im in range(per):
        for n in range(4):
            first = 256 * im + 64 * n
            piece = stack([r.rc[ph, first : first + 64, :] for ph in range(4)])
            r.ocm[im, :, 256 * n : 256 * n + 256] = tn(piece, r.gridder[0:256, :]).astype(BF16)

    def own_channels(ref, index, im):
        return ref.at[im, pl.ds(pl.multiple_of(local * index, local), local), :]

    def give_back(ref, out, passing):
        for im in range(per):
            out[per * me + im] = own_channels(ref, me, im)[...]
        return Ring(
            lambda c, im: own_channels(ref, c, im), lambda c, im: out.at[per * c + im], passing
        )

    back_sums.middle()
    block_output = give_back(r.ocm, r.out_v, r.pass_o)

    def grad2(tap, carry):
        dy, dx = lax.div(tap, 3), lax.rem(tap, 3)
        pieces = []
        for ph in range(4):
            a, c = ph // 2, ph % 2
            for im in range(per):
                pieces.append(tap_slice(r.dzs, a, c, 2 - dy, 2 - dx, im))
        first = pl.multiple_of(256 * tap, 256)
        r.dw2[pl.ds(first, 256), :] = nn(r.h2cm[...], stack(pieces))
        return carry

    for im in range(per):
        piece = channel_major(r.fbuf, im, slice(0, 256))
        grad = nn(piece, r.dzc[256 * im : 256 * im + 256, :])
        if im == 0:
            r.dws[...] = grad
        else:
            r.dws[...] = r.dws[...] + grad

    class GradSum:
        def __init__(self, number, fetch):
            self.fetch = fetch
            self.waits = []
            for part in PARTS:
                setattr(self, part, getattr(r, part + str(number)))

        def begin(self, parts=range(4)):
            for u in parts:
                self.s1[u] = self.fetch(2 * u + 1 - core).astype(BF16)
                self.waits.append(
                    post(self.s1.at[u], self.r1.at[u], self.r1.at[u], dev(partner, within, me))
                )

        def settle(self):
            for wait in self.waits:
                wait()

        def first(self):
            self.settle()
            self.waits = []
            for mask in (6, 2, 4, 0):
                peer = flip(block, mask)
                u = lax.div(peer, 2)
                value = self.fetch(peer) + self.r1[u].astype(F32)
                if mask == 0:
                    self.r2[plane] = value.astype(BF16)
                    continue
                self.s2[u] = value.astype(BF16)
                self.waits.append(
                    post(self.s2.at[u], self.r2.at[plane], self.r2.at[u], dev(peer, within, me))
                )

        def second(self):
            self.settle()
            value = self.r2[0].astype(F32)
            for u in range(1, 4):
                value = value + self.r2[u].astype(F32)
            value = value.astype(BF16)
            left = [value[0:128], value[256 : 256 + tail]]
            right = [value[128:256], value[256 + tail : rows]]
            if value.shape[0] > rows:
                left.append(value[rows : rows + hs])
                right.append(value[rows + hs :])
            pair = jnp.concatenate([stack(left), stack(right)], axis=1)
            packed = nt(pair, r.unpack[...]).astype(BF16)
            for c in range(n_ch):
                self.s3[c] = packed[:, 128 * c : 128 * c + 128]
            self.r3[me] = self.s3[me]
            self.waits = [
                post(self.s3.at[peer], self.r3.at[me], self.r3.at[peer], dev(block, within, peer))
                for peer in ch_peers
            ]

        def end(self, out, out_small=None):
            self.settle()
            done = self.r3[0].astype(F32)
            for c in range(1, n_ch):
                done = done + self.r3[c].astype(F32)
            turned = done[0:128].T
            out[:, 0:128] = turned[0:local]
            out[:, 128:256] = turned[local:]
            gap = jnp.zeros((128 - tail, 128), F32)
            turned = stack([done[128 : 128 + tail], gap]).T
            ends = turned[0:local] + pltpu.roll(turned[local:], tail, axis=1)
            out[:, 256:rows] = ends[:, 0 : rows - 256]
            if out_small is not None:
                last = done[hw:]
                out_small[0:hs, :] = last[:, 0:local]
                out_small[hs:, :] = pltpu.roll(last, local, axis=1)[:, 0:local]

    def block_rows(ref, size, index):
        return ref[pl.ds(pl.multiple_of(size * index, 8), size), :]

    second = GradSum(2, lambda k: stack([block_rows(r.dw2, rows, k), block_rows(r.dws, small, k)]))
    entry = GradSum(1, lambda k: block_rows(r.dw1, rows, k))
    for u, (first, last) in enumerate(((0, 3), (3, 5), (5, 7), (7, 9))):
        lax.fori_loop(first, last, grad2, 0)
        second.begin([u])
    stats = back_sums.end()
    affine_grad2 = stats
    p1_b = [pick_row(stats[0:4], group[im]) / (4.0 * count) for im in range(per)]
    p2_b = [pick_row(stats[4:8], group[im]) / (4.0 * count) for im in range(per)]

    for im in range(per):
        span = slice(256 * im, 256 * im + 256)
        scale = gain * inv2_b[im]
        combos = []
        for a in range(2):
            grads = []
            for c in range(2):
                ph = 2 * a + c
                d = scale * (r.act[ph, span, :] - (p1_b[im] + r.y1[ph, span, :] * p2_b[im]))
                grads.append(d.astype(BF16))
            right = nn(r.shift[0], grads[0])
            left = nn(r.shift[1], grads[1])
            even, odd = grads[0].astype(F32), grads[1].astype(F32)
            combos.append((odd + right, even + odd, left + even))
        gap = jnp.zeros((16, chans), F32)
        for dx in range(3):
            upper, lower = combos[0][dx], combos[1][dx]
            r.field[dx, im] = (lower + stack([upper[16:], gap])).astype(BF16)
            r.field[3 + dx, im] = (upper + lower).astype(BF16)
            r.field[6 + dx, im] = (stack([gap, lower[:-16]]) + upper).astype(BF16)

    second.first()
    block_output.forward()

    def grad1(tap, carry):
        first = pl.multiple_of(256 * tap, 256)
        r.dw1[pl.ds(first, 256), :] = nn(
            r.h1cm[...], stack([r.field[tap, im] for im in range(per)])
        )
        return carry

    for u, (first, last) in enumerate(((0, 3), (3, 5), (5, 7), (7, 9))):
        lax.fori_loop(first, last, grad1, 0)
        entry.begin([u])

    parts = [stack([r.field[tap, im] for im in range(per)]) for tap in range(9)]
    dh1 = back_product(parts, r.w1)
    payload = jnp.zeros((8, chans), F32)
    class_rows = jnp.zeros((24, chans), F32)
    for im in range(per):
        span = slice(256 * im, 256 * im + 256)
        normal = (r.fpm[span, :].astype(F32) - mean1_b[im]) * inv1_b[im]
        pre = gamma_b[im] * normal + beta_b[im]
        sig = sigmoid(pre)
        act = dh1[span] * (sig * (1.0 + pre * (1.0 - sig)))
        r.act1[span, :] = act
        q1, q2 = colsum(act), colsum(act * normal)
        class_rows = class_rows + place_row(q2, label[im], 24)
        class_rows = class_rows + place_row(q1, label[im] + classes, 24)
        payload = payload + place_row(gamma_b[im] * q1, group[im], 8)
        payload = payload + place_row(gamma_b[im] * q2, group[im] + 4, 8)
    last_sums, class_sums = AllReduce(4), AllReduce(6)
    last_sums.begin(payload)
    entry.first()
    class_sums.begin(class_rows)
    last_sums.middle()
    second.second()
    r.dshort[...] = nt(r.dzc[...], r.ws[...])
    stats = last_sums.end()
    for im in range(per):
        span = slice(256 * im, 256 * im + 256)
        normal = (r.fpm[span, :].astype(F32) - mean1_b[im]) * inv1_b[im]
        r1 = pick_row(stats[0:4], group[im]) / count
        r2 = pick_row(stats[4:8], group[im]) / count
        grad = inv1_b[im] * (gamma_b[im] * r.act1[span, :] - (r1 + normal * r2))
        grad = (grad + r.dshort[span, :]).astype(BF16)
        r.dcm[im] = nt(r.ident[...], grad).astype(BF16)
    input_gradient = give_back(r.dcm, r.dx_v, r.pass_x)
    entry.second()
    class_sums.middle()
    second.end(r.grad2, r.grad3)

    row = iota((8, 128), 0)

    def norm_rows(index, weight, grad, v):
        for wait in held[index]:
            wait()
        master = weight[...]
        _, _, direction = adam_update(
            grad[...], getattr(r, v + "m")[...], getattr(r, v + "q")[...]
        )
        update = direction + WEIGHT_DECAY * master
        rows_w = jnp.where(row == index, total(master * master), 0.0)
        return rows_w + jnp.where(row == index + 3, total(update * update), 0.0)

    if inner == 1:
        norms = norm_rows(1, r.exit_v, r.grad2, "v2") + norm_rows(2, r.bypass_v, r.grad3, "vs")

    input_gradient.forward()
    if inner == 1:
        entry.end(r.grad1)
        norms = norms + norm_rows(0, r.entry_v, r.grad1, "v1")
        norm_sums = AllReduce(5)
        norm_sums.begin(norms)
        norm_sums.middle()
    else:
        entry.end(r.grad1)
        r.norms[...] = jnp.zeros((8, 128), F32)

    table = jnp.zeros((24, chans), F32)
    table = table + jnp.where(iota((24, chans), 0) < 2 * classes, class_sums.end(), 0.0)
    table = table + place_row(colsum(affine_grad2[4:8]), 2 * classes, 24)
    table = table + place_row(colsum(affine_grad2[0:4]), 2 * classes + 1, 24)
    table = table + place_row(affine_grad2[8:9], 2 * classes + 2, 24)
    mine = jnp.zeros((24, 128), F32)
    for c in range(n_ch):
        piece = table[:, 128 * (c // 2) : 128 * (c // 2) + 128]
        if c % 2:
            piece = pltpu.roll(piece, local, axis=1)
        mine = mine + jnp.where(me == c, piece, 0.0)
    r.affine_grad[...] = mine

    block_output.settle()
    written = [here(r.out_v, r.out)]
    input_gradient.settle()
    written.append(here(r.dx_v, r.dx))
    if inner == 1:
        r.norms[...] = norm_sums.end()
    for wait in written:
        wait()
    for wait in pending:
        wait()
    cfg.used.append((slots.remote, slots.local))


def final_kernel(cfg, *refs):
    r = SimpleNamespace(**dict(zip(cfg.names, refs)))
    classes = cfg.classes
    local = cfg.local
    r.block_output[...] = r.out[...]
    r.input_gradient[...] = r.dx[...].astype(F32)
    norms = jnp.sqrt(r.norms[...])
    weight_norm, update_norm = norms[0:3, 0:1], norms[3:6, 0:1]
    ratio = weight_norm / update_norm
    at = iota((3, 3), 1)
    r.trust_norms[...] = jnp.where(
        at == 0, weight_norm, jnp.where(at == 1, update_norm, ratio)
    )
    sets = (
        (r.entry, r.entry_m, r.entry_q, r.entry_g, r.entry_1, r.entry_2, r.entry_w),
        (r.exit, r.exit_m, r.exit_q, r.exit_g, r.exit_1, r.exit_2, r.exit_w),
        (r.bypass, r.bypass_m, r.bypass_q, r.bypass_g, r.bypass_1, r.bypass_2, r.bypass_w),
    )
    for index, (weight, m, q, g, first, second, result) in enumerate(sets):
        master = weight[...]
        moment, square, direction = adam_update(g[...], m[...], q[...])
        update = direction + WEIGHT_DECAY * master
        first[...] = moment
        second[...] = square
        result[...] = master - MATRIX_RATE * ratio[index : index + 1] * update
    grad = r.affine_grad[0 : 2 * classes + 3, 0:local]
    moment, square, direction = adam_update(grad, r.affine_m[...], r.affine_q[...])
    r.affine_1[...] = moment
    r.affine_2[...] = square
    r.affine_w[...] = r.affine[...] - AFFINE_RATE * direction


def per_device(
    features,
    labels,
    groups,
    widths,
    entry_conv,
    entry_moment,
    entry_square,
    exit_conv,
    exit_moment,
    exit_square,
    bypass_conv,
    bypass_moment,
    bypass_square,
    norm_affine,
    norm_moment,
    norm_square,
    cotangent,
):
    n_img, n_ch = lax.axis_size("img"), lax.axis_size("ch")
    batch, local, pixels = features.shape
    chans = local * n_ch
    side = math.isqrt(pixels)
    inner = n_img // OUTER
    classes = (norm_affine.shape[0] - 3) // 2
    per = batch // n_ch
    assert (side, chans, n_ch, local, batch % n_ch) == (16, 256, 4, 64, 0) and per == 2
    rows, small = entry_conv.shape[0] * inner, bypass_conv.shape[0] * inner
    masters = (entry_conv, exit_conv, bypass_conv)
    if inner == 1:
        blocks = masters
    else:
        sets = [[o * inner + i for i in range(inner)] for o in range(OUTER)]
        blocks = tuple(
            lax.all_gather(w.astype(BF16), "img", axis=0, tiled=True, axis_index_groups=sets)
            for w in masters
        )

    vmem = pl.BlockSpec(memory_space=pltpu.VMEM)
    smem = pl.BlockSpec(memory_space=pltpu.SMEM)
    anywhere = pl.BlockSpec(memory_space=pl.ANY)
    states = dict(
        entry_m=entry_moment.T,
        entry_q=entry_square.T,
        exit_m=exit_moment.T,
        exit_q=exit_square.T,
        bypass_m=bypass_moment,
        bypass_q=bypass_square,
    )
    inputs = dict(
        labels=(labels, smem),
        groups=(groups, smem),
        widths=(widths, smem),
        features=(features, anywhere),
        cotangent=(cotangent, anywhere),
        entry=(blocks[0].T, anywhere),
        exit=(blocks[1].T, anywhere),
        bypass=(blocks[2], anywhere),
        affine=(norm_affine, anywhere),
    )
    if inner == 1:
        inputs.update({name: (value, anywhere) for name, value in states.items()})
    sds = jax.ShapeDtypeStruct
    outputs = dict(
        out=(sds(cotangent.shape, BF16), anywhere),
        dx=(sds(features.shape, BF16), anywhere),
        grad1=(sds((local, rows), F32), vmem),
        grad2=(sds((local, rows), F32), vmem),
        grad3=(sds((small, local), F32), vmem),
        affine_grad=(sds((24, 128), F32), vmem),
        norms=(sds((8, 128), F32), vmem),
    )
    pix = pixels * per
    taps9 = 9 * chans
    held = lambda shape, dtype=BF16: pltpu.VMEM(shape, dtype)
    scratch = dict(
        fown=held((batch, local, pixels)),
        cown=held((batch, local, 4 * pixels)),
        pass_c=held((2, local, 4 * pixels)),
        pass_o=held((2, local, 4 * pixels)),
        pass_x=held((2, local, pixels)),
        out_v=held(cotangent.shape),
        dx_v=held(features.shape),
        fbuf=held((n_ch, per, local, pixels)),
        cbuf=held((n_ch, per, local, 4 * pixels)),
        entry_v=held((local, rows), blocks[0].dtype),
        exit_v=held((local, rows), blocks[1].dtype),
        bypass_v=held((small, local), blocks[2].dtype),
        affine_v=held(norm_affine.shape, F32),
        padded=held((3 * local, 384)),
        wz1=held((n_ch, rows // 2, 128)),
        wz2=held((n_ch, (rows + small) // 2, 128)),
        aff_z=held((n_ch, 32, 128), F32),
        w1=held((taps9, chans)),
        w2=held((taps9, chans)),
        ws=held((chans, chans)),
        unpack=held((512, 512)),
        ident=held((256, 256)),
        shift=held((2, 256, 256)),
        gridder=held((512, 256)),
        fpm=held((pix, chans)),
        h1s=held((3, per, pixels + 32, chans)),
        h1cm=held((chans, pix)),
        y1=held((4, pix, chans), F32),
        act=held((4, pix, chans), F32),
        h2s=held((2, 4, per, pixels + 32, chans)),
        dzs=held((2, 4, per, pixels + 32, chans)),
        h2cm=held((chans, 4 * pix)),
        short=held((pix, chans), F32),
        dshort=held((pix, chans), F32),
        dzc=held((pix, chans)),
        act1=held((pix, chans), F32),
        rc=held((4, pix, chans)),
        ocm=held((per, chans, 4 * pixels)),
        dcm=held((per, chans, pixels)),
        field=held((9, per, pixels, chans)),
        dw1=held((taps9, chans), F32),
        dw2=held((taps9, chans), F32),
        dws=held((chans, chans), F32),
    )
    for number, size in ((1, rows), (2, rows + small)):
        shapes = ((4, size, chans),) * 4 + ((n_ch, size // 2, 128),) * 2
        for part, shape in zip(PARTS, shapes):
            scratch[part + str(number)] = held(shape)
    exchanges = [(8, chans), (8, chans), (16, chans), (8, chans), (8, 128), (24, chans)]
    if inner == 1:
        for v, shape in (("v1", (local, rows)), ("v2", (local, rows)), ("vs", (small, local))):
            scratch[v + "m"] = held(shape, F32)
            scratch[v + "q"] = held(shape, F32)
    for number, shape in enumerate(exchanges, 1):
        for axis, size in zip("abc", (OUTER, inner, n_ch)):
            if size > 1:
                scratch[axis + str(number)] = held((size,) + shape, F32)
    remote_count = 3 * 3 + 4 * 4 * per + 3 * 7 + 2 * 13 + len(exchanges) * (7 + 3 + inner - 1)
    scratch.update(
        send=pltpu.SemaphoreType.DMA((remote_count,)),
        recv=pltpu.SemaphoreType.DMA((remote_count,)),
        lsem=pltpu.SemaphoreType.DMA((20,)),
    )
    cfg = SimpleNamespace(
        names=[*inputs, *outputs, *scratch],
        inner=inner,
        n_ch=n_ch,
        batch=batch,
        local=local,
        classes=classes,
        count=float(batch * n_img // widths.shape[0] * pixels),
        rows=rows,
        small=small,
        used=[],
    )
    out, dx, grad1, grad2, grad3, affine_grad, norms = pl.pallas_call(
        functools.partial(main_kernel, cfg),
        out_shape=[s for s, _ in outputs.values()],
        in_specs=[s for _, s in inputs.values()],
        out_specs=[s for _, s in outputs.values()],
        scratch_shapes=list(scratch.values()),
        compiler_params=pltpu.CompilerParams(
            collective_id=0, has_side_effects=True, vmem_limit_bytes=VMEM_LIMIT
        ),
        name="block_step",
    )(*[v for v, _ in inputs.values()])
    assert max(n for n, _ in cfg.used) <= remote_count and max(n for _, n in cfg.used) <= 20

    grads = [grad1, grad2, grad3]
    if inner > 1:
        grads = [
            lax.psum_scatter(g, "img", scatter_dimension=0, axis_index_groups=sets, tiled=True)
            for g in (grad1.T, grad2.T, grad3)
        ]
        updates = []
        for w, g, m, s in zip(
            masters,
            grads,
            (entry_moment, exit_moment, bypass_moment),
            (entry_square, exit_square, bypass_square),
        ):
            updates.append(adam_update(g, m, s)[2] + WEIGHT_DECAY * w)
        sums = lax.psum(
            jnp.stack([jnp.sum(w * w) for w in masters] + [jnp.sum(u * u) for u in updates]),
            ("img", "ch"),
        )
        norms = jnp.broadcast_to(jnp.pad(sums, (0, 2))[:, None], (8, 128))
        grads = [grads[0].T, grads[1].T, grads[2]]

    args = dict(
        out=out,
        dx=dx,
        norms=norms,
        affine_grad=affine_grad,
        entry_g=grads[0],
        exit_g=grads[1],
        bypass_g=grads[2],
        entry=entry_conv.T,
        exit=exit_conv.T,
        bypass=bypass_conv,
        **states,
        affine=norm_affine,
        affine_m=norm_moment,
        affine_q=norm_square,
    )
    tall = sds(entry_conv.shape[::-1], F32)
    short, wide = (sds(w.shape, F32) for w in (bypass_conv, norm_affine))
    results = dict(
        block_output=sds(cotangent.shape, BF16),
        input_gradient=sds(features.shape, F32),
        entry_1=tall,
        entry_2=tall,
        entry_w=tall,
        exit_1=tall,
        exit_2=tall,
        exit_w=tall,
        bypass_1=short,
        bypass_2=short,
        bypass_w=short,
        affine_1=wide,
        affine_2=wide,
        affine_w=wide,
        trust_norms=sds((3, 3), F32),
    )
    end_cfg = SimpleNamespace(names=[*args, *results], classes=classes, local=local)
    final = pl.pallas_call(
        functools.partial(final_kernel, end_cfg),
        out_shape=list(results.values()),
        in_specs=[vmem] * len(args),
        out_specs=[vmem] * len(results),
        compiler_params=pltpu.CompilerParams(vmem_limit_bytes=VMEM_LIMIT),
        name="finish",
    )(*args.values())
    return tuple(v.T if s is tall else v for v, s in zip(final, results.values()))


def solution(mesh):
    wide = P("img", "ch")
    deep = P("img", "ch", None)
    table = P(None, "ch")
    return jax.shard_map(
        per_device,
        mesh=mesh,
        in_specs=(deep, P("img"), P("img"), P()) + (wide,) * 9 + (table,) * 3 + (deep,),
        out_specs=(deep, deep) + (wide,) * 9 + (table,) * 3 + (P(),),
        check_vma=False,
    )
```

```python
import functools
import math
from types import SimpleNamespace

import jax
import jax.numpy as jnp
from jax import lax
from jax.experimental import pallas as pl
from jax.experimental.pallas import tpu as pltpu
from jax.sharding import PartitionSpec as P

LEVELS = 4
STEP = 5
NORM_EPSILON = 1e-05
ADAM_EPSILON = 1e-06
MOMENT_DECAY = 0.9
SQUARE_DECAY = 0.999
WEIGHT_DECAY = 0.01
MATRIX_RATE = 0.3
AFFINE_RATE = 0.2

OUTER = 8
VMEM_LIMIT = 56 * 1024 * 1024
BF16 = jnp.bfloat16
F32 = jnp.float32
MESH = pl.DeviceIdType.MESH
PARTS = ("s1", "r1", "s2", "r2", "s3", "r3")


def nn(left, right):
    return lax.dot_general(left, right, (((1,), (0,)), ((), ())), preferred_element_type=F32)


def nt(left, right):
    return lax.dot_general(left, right, (((1,), (1,)), ((), ())), preferred_element_type=F32)


def tn(left, right):
    return lax.dot_general(left, right, (((0,), (0,)), ((), ())), preferred_element_type=F32)


def flip(index, mask):
    result = index
    for bit in range(3):
        if (mask >> bit) & 1:
            digit = lax.rem(lax.div(index, 1 << bit), 2)
            result = result + (1 - 2 * digit) * (1 << bit)
    return result


def sigmoid(value):
    return 0.5 * jnp.tanh(0.5 * value) + 0.5


def iota(shape, axis):
    return lax.broadcasted_iota(jnp.int32, shape, axis)


def to_bf16(condition):
    return jnp.where(condition, 1.0, 0.0).astype(BF16)


def pick_row(table, index):
    hit = iota(table.shape, 0) == index
    return jnp.sum(jnp.where(hit, table, 0.0), axis=0, keepdims=True)


def place_row(row, index, rows):
    hit = iota((rows, row.shape[1]), 0) == index
    return jnp.where(hit, row, 0.0)


def colsum(value):
    return jnp.sum(value, axis=0, keepdims=True)


def adam_update(grad, moment, square):
    moment_new = MOMENT_DECAY * moment + (1.0 - MOMENT_DECAY) * grad
    square_new = SQUARE_DECAY * square + (1.0 - SQUARE_DECAY) * grad * grad
    direction = (
        moment_new
        / (1.0 - MOMENT_DECAY**STEP)
        / (jnp.sqrt(square_new / (1.0 - SQUARE_DECAY**STEP)) + ADAM_EPSILON)
    )
    return (moment_new, square_new, direction)


def total(value):
    return jnp.sum(jnp.sum(value, axis=1, keepdims=True), axis=0, keepdims=True)


def main_kernel(cfg, *refs):
    r = SimpleNamespace(**dict(zip(cfg.names, refs)))
    inner, n_ch, batch, local = cfg.inner, cfg.n_ch, cfg.batch, cfg.local
    classes, count = cfg.classes, cfg.count
    per = batch // n_ch
    chans = local * n_ch
    rows, small = cfg.rows, cfg.small
    tail = (rows - 256) // 2
    hw, hs = rows // 2, small // 2
    slots = SimpleNamespace(remote=0, local=0)

    img = lax.axis_index("img")
    me = lax.axis_index("ch")
    block = lax.div(img, inner)
    within = lax.rem(img, inner)
    core = lax.rem(block, 2)
    plane = lax.div(block, 2)
    partner = flip(block, 1)

    def dev(block_id, within_id, ch_id):
        return (block_id * inner + within_id, ch_id)

    pending = []

    def post(src, dst, landed, peer):
        slot = slots.remote
        slots.remote = slot + 1
        copy = pltpu.make_async_remote_copy(
            src_ref=src,
            dst_ref=dst,
            send_sem=r.send.at[slot],
            recv_sem=r.recv.at[slot],
            device_id=peer,
            device_id_type=MESH,
        )
        copy.start()
        pending.append(copy.wait_send)
        arrival = pltpu.make_async_remote_copy(
            src_ref=landed,
            dst_ref=landed,
            send_sem=r.send.at[slot],
            recv_sem=r.recv.at[slot],
            device_id=peer,
            device_id_type=MESH,
        )
        return arrival.wait_recv

    def here(src, dst):
        slot = slots.local
        slots.local = slot + 1
        copy = pltpu.make_async_copy(src, dst, r.lsem.at[slot])
        copy.start()
        return copy.wait

    outer_peers = [flip(block, mask) for mask in range(1, OUTER)]
    ch_peers = [flip(me, mask) for mask in range(1, n_ch)]
    inner_pairs = [
        (lax.rem(within + step, inner), lax.rem(within + inner - step, inner))
        for step in range(1, inner)
    ]
    up, down, far = (lax.rem(me + step, n_ch) for step in (1, 3, 2))
    up_peer, down_peer = dev(block, within, up), dev(block, within, down)

    class Ring:
        def __init__(self, source, target, passing):
            self.target, self.passing = target, passing
            self.waits = []
            self.early = [
                post(source(far, 0), passing.at[0], passing.at[0], up_peer),
                post(source(far, 1), passing.at[1], passing.at[1], down_peer),
            ]
            for im in range(per):
                self.waits += [
                    post(source(up, im), target(me, im), target(down, im), up_peer),
                    post(source(down, im), target(me, im), target(up, im), down_peer),
                ]

        def forward(self):
            self.early[0]()
            self.waits.append(
                post(self.passing.at[0], self.target(down, 0), self.target(far, 0), up_peer)
            )
            self.early[1]()
            self.waits.append(
                post(self.passing.at[1], self.target(up, 1), self.target(far, 1), down_peer)
            )

        def settle(self):
            for wait in self.waits:
                wait()

    barrier = pltpu.get_barrier_semaphore()
    everyone = [dev(peer, within, me) for peer in outer_peers]
    everyone += [dev(block, within, peer) for peer in ch_peers]
    everyone += [dev(block, peer, me) for peer, _ in inner_pairs]
    for peer in everyone:
        pl.semaphore_signal(barrier, inc=1, device_id=peer, device_id_type=MESH)

    got_entry = here(r.entry, r.entry_v)
    got_features = here(r.features, r.fown)
    got_exit = here(r.exit, r.exit_v)
    got_bypass = here(r.bypass, r.bypass_v)
    got_affine = here(r.affine, r.affine_v)
    got_cot = here(r.cotangent, r.cown)
    states = ((r.entry_m, r.entry_q), (r.exit_m, r.exit_q), (r.bypass_m, r.bypass_q)) if inner == 1 else ()
    held = [
        (here(m, getattr(r, v + "m")), here(q, getattr(r, v + "q")))
        for (m, q), v in zip(states, ("v1", "v2", "vs"))
    ]

    s_row, s_col = iota((hw, 384), 0), iota((hw, 384), 1)
    pick_first = to_bf16(s_col == jnp.where(s_row < 128, s_row, s_row + 128))
    pick_second = to_bf16(s_col == jnp.where(s_row < 128, s_row + 128, s_row + 128 + tail))
    r.padded[...] = jnp.zeros(r.padded.shape, BF16)

    def pack_own(value):
        r.padded[local : 2 * local, 0:rows] = value.astype(BF16)
        packed = nt(pick_first, r.padded[local : 3 * local, :])
        return (packed + nt(pick_second, r.padded[0 : 2 * local, :])).astype(BF16)

    got_entry()
    r.wz1[me] = pack_own(r.entry_v[...])
    pl.semaphore_wait(barrier, len(everyone))

    def to_channels(buffer):
        return [
            post(buffer.at[me], buffer.at[me], buffer.at[peer], dev(block, within, peer))
            for peer in ch_peers
        ]

    entry_waits = to_channels(r.wz1)
    got_features()
    feature_waits = [
        post(
            r.fown.at[pl.ds(per * peer, per)],
            r.fbuf.at[me],
            r.fbuf.at[peer],
            dev(block, within, peer),
        )
        for peer in ch_peers
    ]
    r.fbuf[me] = r.fown[pl.ds(per * me, per)]
    flat = jnp.concatenate([r.fown[b] for b in range(batch)], axis=1)
    wide = flat.astype(F32)
    square = wide * wide
    square_hi = square.astype(BF16)
    square_lo = (square - square_hi.astype(F32)).astype(BF16)
    level = iota((16, 256), 0)
    first_mask = jnp.concatenate([to_bf16(level == r.groups[b]) for b in range(batch)], axis=1)
    second_mask = jnp.concatenate([to_bf16(level == r.groups[b] + 4) for b in range(batch)], axis=1)
    sums = nt(first_mask, flat) + nt(second_mask, square_hi) + nt(second_mask, square_lo)

    got_affine()
    r.aff_z[me] = jnp.zeros((32, 128), F32)
    r.aff_z[me, 0 : 2 * classes + 3, 0:local] = r.affine_v[...]
    r.aff_z[me, 24:32, 0:local] = sums[0:8]
    affine_waits = to_channels(r.aff_z)

    got_exit()
    got_bypass()
    r.wz2[me, 0:hw, :] = pack_own(r.exit_v[...])
    e_row, e_col = iota((local, 128), 0), iota((local, 128), 1)
    value = r.bypass_v[...].astype(BF16)
    r.wz2[me, hw : hw + hs, :] = (
        nn(value[:hs], to_bf16(e_col == e_row)) + nn(value[hs:], to_bf16(e_col == e_row + local))
    ).astype(BF16)

    exit_waits = to_channels(r.wz2)
    got_cot()
    cotangent = Ring(
        lambda c, im: r.cown.at[per * c + im], lambda c, im: r.cbuf.at[c, im], r.pass_c
    )

    lane = iota((512, 512), 0)
    column = iota((512, 512), 1)
    spot = 256 * ((lane >> 6) & 1) + 64 * (lane >> 7) + (lane & 63)
    r.unpack[...] = to_bf16(column == spot)

    def ordered_sum(ref, size):
        result = ref[0]
        for slot in range(1, size):
            result = result + ref[slot]
        return result

    class AllReduce:
        def __init__(self, number):
            self.over_outer, self.over_inner, self.over_ch = (
                getattr(r, axis + str(number), None) for axis in "abc"
            )

        def begin(self, value):
            ref = self.over_outer
            ref[block] = value
            self.waits = [
                post(ref.at[block], ref.at[block], ref.at[peer], dev(peer, within, me))
                for peer in outer_peers
            ]

        def plane(self):
            for wait in self.waits:
                wait()
            value = ordered_sum(self.over_outer, OUTER)
            if inner > 1:
                ref = self.over_inner
                ref[within] = value
                waits = [
                    post(ref.at[within], ref.at[within], ref.at[back], dev(block, peer, me))
                    for peer, back in inner_pairs
                ]
                for wait in waits:
                    wait()
                value = ordered_sum(ref, inner)
            return value

        def middle(self):
            self.over_ch[me] = self.plane()
            self.waits = to_channels(self.over_ch)

        def end(self):
            for wait in self.waits:
                wait()
            return ordered_sum(self.over_ch, n_ch)

    def rows_of(ref, index):
        size = ref.shape[0] // OUTER
        return ref.at[pl.ds(pl.multiple_of(size * index, 16), size)]

    def unpack_own(ref, full):
        own = rows_of(ref, block)
        if full.shape[0] == hw:
            own[0:128, :] = full[0:128, 0:256]
            own[128:256, :] = full[0:128, 256:512]
            own[256 : 256 + tail, :] = full[128:, 0:256]
            own[256 + tail :, :] = full[128:, 256:512]
        else:
            own[0:hs, :] = full[:, 0:256]
            own[hs:, :] = full[:, 256:512]

    def spread(ref):
        own = rows_of(ref, block)
        return {
            mask: post(own, own, rows_of(ref, flip(block, mask)), dev(flip(block, mask), within, me))
            for mask in (2, 4, 6, 1)
        }

    def forward(ref, waits):
        rest = [waits[1]]
        for mask in (2, 4, 6):
            waits[mask]()
            mine = rows_of(ref, flip(block, mask))
            theirs = rows_of(ref, flip(partner, mask))
            rest.append(post(mine, mine, theirs, dev(partner, within, me)))
        return rest

    def widen(buffer):
        packed = jnp.concatenate([buffer[c] for c in range(n_ch)], axis=1)
        return nn(packed, r.unpack[...]).astype(BF16)

    def wide_lanes(ref):
        parts = [
            ref[c] + pltpu.roll(ref[c + 1], local, axis=1) for c in range(0, n_ch, 2)
        ]
        return jnp.concatenate(parts, axis=1)

    for wait in affine_waits:
        wait()
    affine = wide_lanes(r.aff_z)
    input_sums = AllReduce(1)
    input_sums.begin(affine[24:32])
    for wait in entry_waits:
        wait()
    unpack_own(r.w1, widen(r.wz1))
    gather1 = spread(r.w1)

    ident = to_bf16(iota((256, 256), 0) == iota((256, 256), 1))
    r.ident[...] = ident
    q_out, q_in = iota((256, 256), 0), iota((256, 256), 1)
    r.shift[0] = to_bf16((q_in == q_out + 1) & ((q_out & 15) < 15))
    r.shift[1] = to_bf16((q_in == q_out - 1) & ((q_out & 15) > 0))

    for wait in exit_waits:
        wait()
    full = widen(r.wz2)
    unpack_own(r.w2, full[0:hw])
    unpack_own(r.ws, full[hw:])
    gather2 = spread(r.w2)
    gather3 = spread(r.ws)

    rho, px = iota((512, 256), 0), iota((512, 256), 1)
    version, a, b_ = rho >> 8, (rho >> 7) & 1, (rho >> 6) & 1
    col = (rho & 15) + version * (1 - 2 * b_)
    target = (2 * ((rho & 63) >> 4) + a) * 32 + 2 * col + b_
    r.gridder[...] = to_bf16((px == target) & (col >= 0) & (col < 16))
    zeros = jnp.zeros((16, 256), BF16)
    for im in range(per):
        for ver in range(3):
            r.h1s[ver, im, 0:16, :] = zeros
            r.h1s[ver, im, 272:288, :] = zeros
        for ver in range(2):
            for ph in range(4):
                for ref in (r.h2s, r.dzs):
                    ref[ver, ph, im, 0:16, :] = zeros
                    ref[ver, ph, im, 272:288, :] = zeros

    def channel_major(ref, im, lanes):
        return jnp.concatenate([ref[c, im, :, lanes] for c in range(n_ch)], axis=0)

    for wait in feature_waits:
        wait()
    for im in range(per):
        r.fpm[256 * im : 256 * im + 256, :] = nt(
            ident, channel_major(r.fbuf, im, slice(0, 256))
        ).astype(BF16)

    stats = input_sums.plane()
    mean1 = stats[0:4] / count
    inv1 = lax.rsqrt(stats[4:8] / count - mean1 * mean1 + NORM_EPSILON)
    gain = affine[2 * classes : 2 * classes + 1]
    shift = affine[2 * classes + 1 : 2 * classes + 2]
    out_bias = affine[2 * classes + 2 : 2 * classes + 3]
    group, label, mean1_b, inv1_b, gamma_b, beta_b, mask_b = [], [], [], [], [], [], []
    for im in range(per):
        group.append(r.groups[per * me + im])
        label.append(r.labels[per * me + im])
        mean1_b.append(pick_row(mean1, group[im]))
        inv1_b.append(pick_row(inv1, group[im]))
        gamma_b.append(pick_row(affine, label[im]))
        beta_b.append(pick_row(affine, label[im] + classes))
        width = r.widths[group[im]]
        mask_b.append(
            jnp.where(iota((1, chans), 1) < width * (chans // LEVELS), 1.0, 0.0)
        )

    for im in range(per):
        normal = (r.fpm[256 * im : 256 * im + 256, :].astype(F32) - mean1_b[im]) * inv1_b[im]
        pre = gamma_b[im] * normal + beta_b[im]
        hidden = (pre * sigmoid(pre)).astype(BF16)
        r.h1s[1, im, 16:272, :] = hidden
        r.h1s[0, im, 16:272, :] = nn(r.shift[1], hidden).astype(BF16)
        r.h1s[2, im, 16:272, :] = nn(r.shift[0], hidden).astype(BF16)
        r.h1cm[:, 256 * im : 256 * im + 256] = nt(ident, hidden).astype(BF16)
        if im == 0:
            rest = forward(r.w1, gather1)

    cotangent.forward()
    for wait in rest:
        wait()

    def back_product(parts, ref):
        result = nt(parts[0], ref[0:256, :])
        for tap in range(1, 9):
            result = result + nt(parts[tap], ref[256 * tap : 256 * tap + 256, :])
        return result

    def taps():
        return [(dy, dx) for dy in range(3) for dx in range(3)]

    def stack(pieces):
        return jnp.concatenate(pieces, axis=0)

    def conv1(phase, carry):
        a, c = lax.div(phase, 2), lax.rem(phase, 2)
        parts = []
        for dy, dx in taps():
            first = pl.multiple_of(16 * lax.div(a + dy + 1, 2), 16)
            ver = lax.div(c + dx + 1, 2)
            parts.append(
                stack([r.h1s[ver, im, pl.ds(first, 256), :] for im in range(per)])
            )
        y = nn(jnp.concatenate(parts, axis=1), r.w1[...])
        r.y1[phase] = y
        out = []
        for im in range(per):
            piece = y[256 * im : 256 * im + 256]
            out.append(carry[2 * im] + colsum(piece))
            out.append(carry[2 * im + 1] + colsum(piece * piece))
        return tuple(out)

    nought = jnp.zeros((1, chans), F32)
    mid = lax.fori_loop(0, 4, conv1, (nought,) * (2 * per))
    payload = jnp.zeros((8, chans), F32)
    for im in range(per):
        payload = payload + place_row(mid[2 * im], group[im], 8)
        payload = payload + place_row(mid[2 * im + 1], group[im] + 4, 8)
    mid_sums = AllReduce(2)
    mid_sums.begin(payload)

    rest = forward(r.w2, gather2) + forward(r.ws, gather3)
    mid_sums.middle()

    r.cbuf[me] = r.cown[pl.ds(per * me, per)]
    cotangent.settle()
    for im in range(per):
        for n in range(4):
            piece = channel_major(r.cbuf, im, slice(256 * n, 256 * n + 256))
            grid = nt(r.gridder[...], piece).astype(BF16)
            for ver in range(2):
                for ph in range(4):
                    at = 256 * ver + 64 * ph
                    r.dzs[ver, ph, im, 16 + 64 * n : 80 + 64 * n, :] = grid[at : at + 64]

    coarse = jnp.zeros((256 * per, chans), F32)
    for ph in range(4):
        coarse = coarse + stack([r.dzs[0, ph, im, 16:272, :] for im in range(per)]).astype(F32)
    bias_sum = colsum(coarse)
    r.dzc[...] = coarse.astype(BF16)

    def tap_slice(ref, a, c, dy, dx, im):
        row, colm = a + dy + 1, c + dx + 1
        first = pl.multiple_of(16 * lax.div(row, 2), 16)
        ph = 2 * lax.rem(row, 2) + lax.rem(colm, 2)
        side_step = lax.div(colm, 2) - 1
        return ref[side_step * side_step, ph, im, pl.ds(first, 256), :]

    for wait in rest:
        wait()

    def back2(phase, carry):
        a, c = lax.div(phase, 2), lax.rem(phase, 2)
        parts = [
            stack([tap_slice(r.dzs, a, c, 2 - dy, 2 - dx, im) for im in range(per)])
            for dy, dx in taps()
        ]
        r.act[phase] = back_product(parts, r.w2)
        return carry

    lax.fori_loop(0, 4, back2, 0)

    stats = mid_sums.end()
    mean2 = stats[0:4] / (4.0 * count)
    inv2 = lax.rsqrt(stats[4:8] / (4.0 * count) - mean2 * mean2 + NORM_EPSILON)
    mean2_b = [pick_row(mean2, group[im]) for im in range(per)]
    inv2_b = [pick_row(inv2, group[im]) for im in range(per)]

    def hidden2(phase, carry):
        c = lax.rem(phase, 2)
        out = []
        for im in range(per):
            span = slice(256 * im, 256 * im + 256)
            normal = (r.y1[phase, span, :] - mean2_b[im]) * inv2_b[im]
            r.y1[phase, span, :] = normal
            pre = gain * normal + shift
            sig = sigmoid(pre)
            hidden = (pre * sig * mask_b[im]).astype(BF16)
            act = r.act[phase, span, :] * (sig * (1.0 + pre * (1.0 - sig)) * mask_b[im])
            r.act[phase, span, :] = act
            out.append(carry[2 * im] + colsum(act))
            out.append(carry[2 * im + 1] + colsum(act * normal))
            r.h2s[0, phase, im, 16:272, :] = hidden
            r.h2s[1, phase, im, 16:272, :] = nn(r.shift[c], hidden).astype(BF16)
            lanes = pl.ds(pl.multiple_of(512 * phase + 256 * im, 256), 256)
            r.h2cm[:, lanes] = nt(r.ident[...], hidden).astype(BF16)
        return tuple(out)

    mid = lax.fori_loop(0, 4, hidden2, (nought,) * (2 * per))
    payload = place_row(bias_sum, 8, 16)
    for im in range(per):
        payload = payload + place_row(mid[2 * im], group[im], 16)
        payload = payload + place_row(mid[2 * im + 1], group[im] + 4, 16)
    back_sums = AllReduce(3)
    back_sums.begin(payload)

    r.short[...] = nn(r.fpm[...], r.ws[...]) + out_bias
    def conv2(phase, carry):
        a, c = lax.div(phase, 2), lax.rem(phase, 2)
        parts = [
            stack([tap_slice(r.h2s, a, c, dy, dx, im) for im in range(per)]) for dy, dx in taps()
        ]
        y = nn(jnp.concatenate(parts, axis=1), r.w2[...]) + r.short[...]
        r.rc[phase] = y.astype(BF16)
        return carry

    lax.fori_loop(0, 4, conv2, 0)
    for im in range(per):
        for n in range(4):
            first = 256 * im + 64 * n
            piece = stack([r.rc[ph, first : first + 64, :] for ph in range(4)])
            r.ocm[im, :, 256 * n : 256 * n + 256] = tn(piece, r.gridder[0:256, :]).astype(BF16)

    def own_channels(ref, index, im):
        return ref.at[im, pl.ds(pl.multiple_of(local * index, local), local), :]

    def give_back(ref, out, passing):
        for im in range(per):
            out[per * me + im] = own_channels(ref, me, im)[...]
        return Ring(
            lambda c, im: own_channels(ref, c, im), lambda c, im: out.at[per * c + im], passing
        )

    back_sums.middle()
    block_output = give_back(r.ocm, r.out_v, r.pass_o)

    def grad2(tap, carry):
        dy, dx = lax.div(tap, 3), lax.rem(tap, 3)
        pieces = []
        for ph in range(4):
            a, c = ph // 2, ph % 2
            for im in range(per):
                pieces.append(tap_slice(r.dzs, a, c, 2 - dy, 2 - dx, im))
        first = pl.multiple_of(256 * tap, 256)
        r.dw2[pl.ds(first, 256), :] = nn(r.h2cm[...], stack(pieces))
        return carry

    for im in range(per):
        piece = channel_major(r.fbuf, im, slice(0, 256))
        grad = nn(piece, r.dzc[256 * im : 256 * im + 256, :])
        if im == 0:
            r.dws[...] = grad
        else:
            r.dws[...] = r.dws[...] + grad

    class GradSum:
        def __init__(self, number, fetch):
            self.fetch = fetch
            self.waits = []
            for part in PARTS:
                setattr(self, part, getattr(r, part + str(number)))

        def begin(self, parts=range(4)):
            for u in parts:
                self.s1[u] = self.fetch(2 * u + 1 - core).astype(BF16)
                self.waits.append(
                    post(self.s1.at[u], self.r1.at[u], self.r1.at[u], dev(partner, within, me))
                )

        def settle(self):
            for wait in self.waits:
                wait()

        def first(self):
            self.settle()
            self.waits = []
            for mask in (6, 2, 4, 0):
                peer = flip(block, mask)
                u = lax.div(peer, 2)
                value = self.fetch(peer) + self.r1[u].astype(F32)
                if mask == 0:
                    self.r2[plane] = value.astype(BF16)
                    continue
                self.s2[u] = value.astype(BF16)
                self.waits.append(
                    post(self.s2.at[u], self.r2.at[plane], self.r2.at[u], dev(peer, within, me))
                )

        def second(self):
            self.settle()
            value = self.r2[0].astype(F32)
            for u in range(1, 4):
                value = value + self.r2[u].astype(F32)
            value = value.astype(BF16)
            left = [value[0:128], value[256 : 256 + tail]]
            right = [value[128:256], value[256 + tail : rows]]
            if value.shape[0] > rows:
                left.append(value[rows : rows + hs])
                right.append(value[rows + hs :])
            pair = jnp.concatenate([stack(left), stack(right)], axis=1)
            packed = nt(pair, r.unpack[...]).astype(BF16)
            for c in range(n_ch):
                self.s3[c] = packed[:, 128 * c : 128 * c + 128]
            self.r3[me] = self.s3[me]
            self.waits = [
                post(self.s3.at[peer], self.r3.at[me], self.r3.at[peer], dev(block, within, peer))
                for peer in ch_peers
            ]

        def end(self, out, out_small=None):
            self.settle()
            done = self.r3[0].astype(F32)
            for c in range(1, n_ch):
                done = done + self.r3[c].astype(F32)
            turned = done[0:128].T
            out[:, 0:128] = turned[0:local]
            out[:, 128:256] = turned[local:]
            gap = jnp.zeros((128 - tail, 128), F32)
            turned = stack([done[128 : 128 + tail], gap]).T
            ends = turned[0:local] + pltpu.roll(turned[local:], tail, axis=1)
            out[:, 256:rows] = ends[:, 0 : rows - 256]
            if out_small is not None:
                last = done[hw:]
                out_small[0:hs, :] = last[:, 0:local]
                out_small[hs:, :] = pltpu.roll(last, local, axis=1)[:, 0:local]

    def block_rows(ref, size, index):
        return ref[pl.ds(pl.multiple_of(size * index, 8), size), :]

    second = GradSum(2, lambda k: stack([block_rows(r.dw2, rows, k), block_rows(r.dws, small, k)]))
    entry = GradSum(1, lambda k: block_rows(r.dw1, rows, k))
    for u, (first, last) in enumerate(((0, 3), (3, 5), (5, 7), (7, 9))):
        lax.fori_loop(first, last, grad2, 0)
        second.begin([u])
    stats = back_sums.end()
    affine_grad2 = stats
    p1_b = [pick_row(stats[0:4], group[im]) / (4.0 * count) for im in range(per)]
    p2_b = [pick_row(stats[4:8], group[im]) / (4.0 * count) for im in range(per)]

    for im in range(per):
        span = slice(256 * im, 256 * im + 256)
        scale = gain * inv2_b[im]
        combos = []
        for a in range(2):
            grads = []
            for c in range(2):
                ph = 2 * a + c
                d = scale * (r.act[ph, span, :] - (p1_b[im] + r.y1[ph, span, :] * p2_b[im]))
                grads.append(d.astype(BF16))
            right = nn(r.shift[0], grads[0])
            left = nn(r.shift[1], grads[1])
            even, odd = grads[0].astype(F32), grads[1].astype(F32)
            combos.append((odd + right, even + odd, left + even))
        gap = jnp.zeros((16, chans), F32)
        for dx in range(3):
            upper, lower = combos[0][dx], combos[1][dx]
            r.field[dx, im] = (lower + stack([upper[16:], gap])).astype(BF16)
            r.field[3 + dx, im] = (upper + lower).astype(BF16)
            r.field[6 + dx, im] = (stack([gap, lower[:-16]]) + upper).astype(BF16)

    second.first()
    block_output.forward()

    def grad1(tap, carry):
        first = pl.multiple_of(256 * tap, 256)
        r.dw1[pl.ds(first, 256), :] = nn(
            r.h1cm[...], stack([r.field[tap, im] for im in range(per)])
        )
        return carry

    for u, (first, last) in enumerate(((0, 3), (3, 5), (5, 7), (7, 9))):
        lax.fori_loop(first, last, grad1, 0)
        entry.begin([u])

    parts = [stack([r.field[tap, im] for im in range(per)]) for tap in range(9)]
    dh1 = back_product(parts, r.w1)
    payload = jnp.zeros((8, chans), F32)
    class_rows = jnp.zeros((24, chans), F32)
    for im in range(per):
        span = slice(256 * im, 256 * im + 256)
        normal = (r.fpm[span, :].astype(F32) - mean1_b[im]) * inv1_b[im]
        pre = gamma_b[im] * normal + beta_b[im]
        sig = sigmoid(pre)
        act = dh1[span] * (sig * (1.0 + pre * (1.0 - sig)))
        r.act1[span, :] = act
        q1, q2 = colsum(act), colsum(act * normal)
        class_rows = class_rows + place_row(q2, label[im], 24)
        class_rows = class_rows + place_row(q1, label[im] + classes, 24)
        payload = payload + place_row(gamma_b[im] * q1, group[im], 8)
        payload = payload + place_row(gamma_b[im] * q2, group[im] + 4, 8)
    last_sums, class_sums = AllReduce(4), AllReduce(6)
    last_sums.begin(payload)
    entry.first()
    class_sums.begin(class_rows)
    last_sums.middle()
    second.second()
    r.dshort[...] = nt(r.dzc[...], r.ws[...])
    entry.second()
    stats = last_sums.end()
    for im in range(per):
        span = slice(256 * im, 256 * im + 256)
        normal = (r.fpm[span, :].astype(F32) - mean1_b[im]) * inv1_b[im]
        r1 = pick_row(stats[0:4], group[im]) / count
        r2 = pick_row(stats[4:8], group[im]) / count
        grad = inv1_b[im] * (gamma_b[im] * r.act1[span, :] - (r1 + normal * r2))
        grad = (grad + r.dshort[span, :]).astype(BF16)
        r.dcm[im] = nt(r.ident[...], grad).astype(BF16)
    input_gradient = give_back(r.dcm, r.dx_v, r.pass_x)
    class_sums.middle()
    second.end(r.grad2, r.grad3)

    row = iota((8, 128), 0)

    def norm_rows(index, weight, grad, v):
        for wait in held[index]:
            wait()
        master = weight[...]
        _, _, direction = adam_update(
            grad[...], getattr(r, v + "m")[...], getattr(r, v + "q")[...]
        )
        update = direction + WEIGHT_DECAY * master
        rows_w = jnp.where(row == index, total(master * master), 0.0)
        return rows_w + jnp.where(row == index + 3, total(update * update), 0.0)

    if inner == 1:
        norms = norm_rows(1, r.exit_v, r.grad2, "v2") + norm_rows(2, r.bypass_v, r.grad3, "vs")

    if inner == 1:
        entry.end(r.grad1)
        norms = norms + norm_rows(0, r.entry_v, r.grad1, "v1")
        norm_sums = AllReduce(5)
        norm_sums.begin(norms)
        input_gradient.forward()
        norm_sums.middle()
    else:
        entry.end(r.grad1)
        input_gradient.forward()
        r.norms[...] = jnp.zeros((8, 128), F32)

    table = jnp.zeros((24, chans), F32)
    table = table + jnp.where(iota((24, chans), 0) < 2 * classes, class_sums.end(), 0.0)
    table = table + place_row(colsum(affine_grad2[4:8]), 2 * classes, 24)
    table = table + place_row(colsum(affine_grad2[0:4]), 2 * classes + 1, 24)
    table = table + place_row(affine_grad2[8:9], 2 * classes + 2, 24)
    mine = jnp.zeros((24, 128), F32)
    for c in range(n_ch):
        piece = table[:, 128 * (c // 2) : 128 * (c // 2) + 128]
        if c % 2:
            piece = pltpu.roll(piece, local, axis=1)
        mine = mine + jnp.where(me == c, piece, 0.0)
    r.affine_grad[...] = mine

    block_output.settle()
    written = [here(r.out_v, r.out)]
    input_gradient.settle()
    written.append(here(r.dx_v, r.dx))
    if inner == 1:
        r.norms[...] = norm_sums.end()
    for wait in written:
        wait()
    for wait in pending:
        wait()
    cfg.used.append((slots.remote, slots.local))


def final_kernel(cfg, *refs):
    r = SimpleNamespace(**dict(zip(cfg.names, refs)))
    classes = cfg.classes
    local = cfg.local
    r.block_output[...] = r.out[...]
    r.input_gradient[...] = r.dx[...].astype(F32)
    norms = jnp.sqrt(r.norms[...])
    weight_norm, update_norm = norms[0:3, 0:1], norms[3:6, 0:1]
    ratio = weight_norm / update_norm
    at = iota((3, 3), 1)
    r.trust_norms[...] = jnp.where(
        at == 0, weight_norm, jnp.where(at == 1, update_norm, ratio)
    )
    sets = (
        (r.entry, r.entry_m, r.entry_q, r.entry_g, r.entry_1, r.entry_2, r.entry_w),
        (r.exit, r.exit_m, r.exit_q, r.exit_g, r.exit_1, r.exit_2, r.exit_w),
        (r.bypass, r.bypass_m, r.bypass_q, r.bypass_g, r.bypass_1, r.bypass_2, r.bypass_w),
    )
    for index, (weight, m, q, g, first, second, result) in enumerate(sets):
        master = weight[...]
        moment, square, direction = adam_update(g[...], m[...], q[...])
        update = direction + WEIGHT_DECAY * master
        first[...] = moment
        second[...] = square
        result[...] = master - MATRIX_RATE * ratio[index : index + 1] * update
    grad = r.affine_grad[0 : 2 * classes + 3, 0:local]
    moment, square, direction = adam_update(grad, r.affine_m[...], r.affine_q[...])
    r.affine_1[...] = moment
    r.affine_2[...] = square
    r.affine_w[...] = r.affine[...] - AFFINE_RATE * direction


def per_device(
    features,
    labels,
    groups,
    widths,
    entry_conv,
    entry_moment,
    entry_square,
    exit_conv,
    exit_moment,
    exit_square,
    bypass_conv,
    bypass_moment,
    bypass_square,
    norm_affine,
    norm_moment,
    norm_square,
    cotangent,
):
    n_img, n_ch = lax.axis_size("img"), lax.axis_size("ch")
    batch, local, pixels = features.shape
    chans = local * n_ch
    side = math.isqrt(pixels)
    inner = n_img // OUTER
    classes = (norm_affine.shape[0] - 3) // 2
    per = batch // n_ch
    assert (side, chans, n_ch, local, batch % n_ch) == (16, 256, 4, 64, 0) and per == 2
    rows, small = entry_conv.shape[0] * inner, bypass_conv.shape[0] * inner
    masters = (entry_conv, exit_conv, bypass_conv)
    if inner == 1:
        blocks = masters
    else:
        sets = [[o * inner + i for i in range(inner)] for o in range(OUTER)]
        blocks = tuple(
            lax.all_gather(w.astype(BF16), "img", axis=0, tiled=True, axis_index_groups=sets)
            for w in masters
        )

    vmem = pl.BlockSpec(memory_space=pltpu.VMEM)
    smem = pl.BlockSpec(memory_space=pltpu.SMEM)
    anywhere = pl.BlockSpec(memory_space=pl.ANY)
    states = dict(
        entry_m=entry_moment.T,
        entry_q=entry_square.T,
        exit_m=exit_moment.T,
        exit_q=exit_square.T,
        bypass_m=bypass_moment,
        bypass_q=bypass_square,
    )
    inputs = dict(
        labels=(labels, smem),
        groups=(groups, smem),
        widths=(widths, smem),
        features=(features, anywhere),
        cotangent=(cotangent, anywhere),
        entry=(blocks[0].T, anywhere),
        exit=(blocks[1].T, anywhere),
        bypass=(blocks[2], anywhere),
        affine=(norm_affine, anywhere),
    )
    if inner == 1:
        inputs.update({name: (value, anywhere) for name, value in states.items()})
    sds = jax.ShapeDtypeStruct
    outputs = dict(
        out=(sds(cotangent.shape, BF16), anywhere),
        dx=(sds(features.shape, BF16), anywhere),
        grad1=(sds((local, rows), F32), vmem),
        grad2=(sds((local, rows), F32), vmem),
        grad3=(sds((small, local), F32), vmem),
        affine_grad=(sds((24, 128), F32), vmem),
        norms=(sds((8, 128), F32), vmem),
    )
    pix = pixels * per
    taps9 = 9 * chans
    held = lambda shape, dtype=BF16: pltpu.VMEM(shape, dtype)
    scratch = dict(
        fown=held((batch, local, pixels)),
        cown=held((batch, local, 4 * pixels)),
        pass_c=held((2, local, 4 * pixels)),
        pass_o=held((2, local, 4 * pixels)),
        pass_x=held((2, local, pixels)),
        out_v=held(cotangent.shape),
        dx_v=held(features.shape),
        fbuf=held((n_ch, per, local, pixels)),
        cbuf=held((n_ch, per, local, 4 * pixels)),
        entry_v=held((local, rows), blocks[0].dtype),
        exit_v=held((local, rows), blocks[1].dtype),
        bypass_v=held((small, local), blocks[2].dtype),
        affine_v=held(norm_affine.shape, F32),
        padded=held((3 * local, 384)),
        wz1=held((n_ch, rows // 2, 128)),
        wz2=held((n_ch, (rows + small) // 2, 128)),
        aff_z=held((n_ch, 32, 128), F32),
        w1=held((taps9, chans)),
        w2=held((taps9, chans)),
        ws=held((chans, chans)),
        unpack=held((512, 512)),
        ident=held((256, 256)),
        shift=held((2, 256, 256)),
        gridder=held((512, 256)),
        fpm=held((pix, chans)),
        h1s=held((3, per, pixels + 32, chans)),
        h1cm=held((chans, pix)),
        y1=held((4, pix, chans), F32),
        act=held((4, pix, chans), F32),
        h2s=held((2, 4, per, pixels + 32, chans)),
        dzs=held((2, 4, per, pixels + 32, chans)),
        h2cm=held((chans, 4 * pix)),
        short=held((pix, chans), F32),
        dshort=held((pix, chans), F32),
        dzc=held((pix, chans)),
        act1=held((pix, chans), F32),
        rc=held((4, pix, chans)),
        ocm=held((per, chans, 4 * pixels)),
        dcm=held((per, chans, pixels)),
        field=held((9, per, pixels, chans)),
        dw1=held((taps9, chans), F32),
        dw2=held((taps9, chans), F32),
        dws=held((chans, chans), F32),
    )
    for number, size in ((1, rows), (2, rows + small)):
        shapes = ((4, size, chans),) * 4 + ((n_ch, size // 2, 128),) * 2
        for part, shape in zip(PARTS, shapes):
            scratch[part + str(number)] = held(shape)
    exchanges = [(8, chans), (8, chans), (16, chans), (8, chans), (8, 128), (24, chans)]
    if inner == 1:
        for v, shape in (("v1", (local, rows)), ("v2", (local, rows)), ("vs", (small, local))):
            scratch[v + "m"] = held(shape, F32)
            scratch[v + "q"] = held(shape, F32)
    for number, shape in enumerate(exchanges, 1):
        for axis, size in zip("abc", (OUTER, inner, n_ch)):
            if size > 1:
                scratch[axis + str(number)] = held((size,) + shape, F32)
    remote_count = 3 * 3 + 4 * 4 * per + 3 * 7 + 2 * 13 + len(exchanges) * (7 + 3 + inner - 1)
    scratch.update(
        send=pltpu.SemaphoreType.DMA((remote_count,)),
        recv=pltpu.SemaphoreType.DMA((remote_count,)),
        lsem=pltpu.SemaphoreType.DMA((20,)),
    )
    cfg = SimpleNamespace(
        names=[*inputs, *outputs, *scratch],
        inner=inner,
        n_ch=n_ch,
        batch=batch,
        local=local,
        classes=classes,
        count=float(batch * n_img // widths.shape[0] * pixels),
        rows=rows,
        small=small,
        used=[],
    )
    out, dx, grad1, grad2, grad3, affine_grad, norms = pl.pallas_call(
        functools.partial(main_kernel, cfg),
        out_shape=[s for s, _ in outputs.values()],
        in_specs=[s for _, s in inputs.values()],
        out_specs=[s for _, s in outputs.values()],
        scratch_shapes=list(scratch.values()),
        compiler_params=pltpu.CompilerParams(
            collective_id=0, has_side_effects=True, vmem_limit_bytes=VMEM_LIMIT
        ),
        name="block_step",
    )(*[v for v, _ in inputs.values()])
    assert max(n for n, _ in cfg.used) <= remote_count and max(n for _, n in cfg.used) <= 20

    grads = [grad1, grad2, grad3]
    if inner > 1:
        grads = [
            lax.psum_scatter(g, "img", scatter_dimension=0, axis_index_groups=sets, tiled=True)
            for g in (grad1.T, grad2.T, grad3)
        ]
        updates = []
        for w, g, m, s in zip(
            masters,
            grads,
            (entry_moment, exit_moment, bypass_moment),
            (entry_square, exit_square, bypass_square),
        ):
            updates.append(adam_update(g, m, s)[2] + WEIGHT_DECAY * w)
        sums = lax.psum(
            jnp.stack([jnp.sum(w * w) for w in masters] + [jnp.sum(u * u) for u in updates]),
            ("img", "ch"),
        )
        norms = jnp.broadcast_to(jnp.pad(sums, (0, 2))[:, None], (8, 128))
        grads = [grads[0].T, grads[1].T, grads[2]]

    args = dict(
        out=out,
        dx=dx,
        norms=norms,
        affine_grad=affine_grad,
        entry_g=grads[0],
        exit_g=grads[1],
        bypass_g=grads[2],
        entry=entry_conv.T,
        exit=exit_conv.T,
        bypass=bypass_conv,
        **states,
        affine=norm_affine,
        affine_m=norm_moment,
        affine_q=norm_square,
    )
    tall = sds(entry_conv.shape[::-1], F32)
    short, wide = (sds(w.shape, F32) for w in (bypass_conv, norm_affine))
    results = dict(
        block_output=sds(cotangent.shape, BF16),
        input_gradient=sds(features.shape, F32),
        entry_1=tall,
        entry_2=tall,
        entry_w=tall,
        exit_1=tall,
        exit_2=tall,
        exit_w=tall,
        bypass_1=short,
        bypass_2=short,
        bypass_w=short,
        affine_1=wide,
        affine_2=wide,
        affine_w=wide,
        trust_norms=sds((3, 3), F32),
    )
    end_cfg = SimpleNamespace(names=[*args, *results], classes=classes, local=local)
    final = pl.pallas_call(
        functools.partial(final_kernel, end_cfg),
        out_shape=list(results.values()),
        in_specs=[vmem] * len(args),
        out_specs=[vmem] * len(results),
        compiler_params=pltpu.CompilerParams(vmem_limit_bytes=VMEM_LIMIT),
        name="finish",
    )(*args.values())
    return tuple(v.T if s is tall else v for v, s in zip(final, results.values()))


def solution(mesh):
    wide = P("img", "ch")
    deep = P("img", "ch", None)
    table = P(None, "ch")
    return jax.shard_map(
        per_device,
        mesh=mesh,
        in_specs=(deep, P("img"), P("img"), P()) + (wide,) * 9 + (table,) * 3 + (deep,),
        out_specs=(deep, deep) + (wide,) * 9 + (table,) * 3 + (P(),),
        check_vma=False,
    )
```
